32 devices in a mesh: section: 2 (over y), dp: 16 (over z, x, core).
Axes of the slice: x: 2, y: 2, z: 4, core: 2. Of those that a mesh axis runs over, the one named last changes fastest.
Arguments:
- token_ids: int32 [48, 128], P('dp'), may hold values from 0 to 31999
- target_ids: int32 [48, 128], P('dp'), may hold values from 0 to 31999
- time_bins: int32 [48], P('dp'), may hold values from 0 to 127
- sigma_table: float32 [128], replicated, may hold values from 0.2 to 8
- noise: float32 [48, 128, 256], P('dp'), may hold values from -6 to 6
- embed: bfloat16 [32000, 256], P('dp'), may hold values from -6 to 6
- w_in: bfloat16 [256, 1024], replicated, may hold values from -0.375 to 0.375
- w_time: bfloat16 [2, 256, 2048], P('section'), may hold values from -0.375 to 0.375
- norm_gain: float32 [2, 2048], P('section'), may hold values from 0.5 to 1.5
- w_qkv: bfloat16 [2, 1024, 3072], P('section'), may hold values from -0.1875 to 0.1875
- w_out: bfloat16 [2, 1024, 1024], P('section'), may hold values from -0.375 to 0.375
- w_up: bfloat16 [2, 1024, 4096], P('section'), may hold values from -0.1875 to 0.1875
- b_hidden: float32 [2, 4096], P('section'), may hold values from -3 to 3
- w_down: bfloat16 [2, 4096, 1024], P('section'), may hold values from -0.09375 to 0.09375
- out_gain: float32 [1024], replicated, may hold values from 0.5 to 1.5
- head: bfloat16 [32000, 1024], P(('section', 'dp')), may hold values from -0.375 to 0.375
Outputs:
- loss: float32 [], replicated
- grad_embed: float32 [32000, 256], P(('section', 'dp'))
- grad_w_in: float32 [256, 1024], P(('section', 'dp'))
- grad_w_time: float32 [2, 256, 2048], P('section', 'dp')
- grad_norm_gain: float32 [2, 2048], P('section', 'dp')
- grad_w_qkv: float32 [2, 1024, 3072], P('section', 'dp')
- grad_w_out: float32 [2, 1024, 1024], P('section', 'dp')
- grad_w_up: float32 [2, 1024, 4096], P('section', 'dp')
- grad_b_hidden: float32 [2, 4096], P('section', 'dp')
- grad_w_down: float32 [2, 4096, 1024], P('section', 'dp')
- grad_out_gain: float32 [1024], P('dp')
- grad_head: float32 [32000, 1024], P(('section', 'dp'))
The draws below stay inside these ranges and needn't reach their ends.
All inputs are finite; a program needn't handle non-finite values.
Results may differ from the reference program's by a relative error of at most 0.035.
Values may be sent and summed in bfloat16 or wider, within the bound.
A program may use at most 384 MiB of HBM per device.

```python
import math
import jax
import jax.numpy as jnp
import numpy as np
from jax import lax

D = 1024
HEADS = 16
HEAD_DIM = 64
FF = 4096
EMB = 256
VOCAB = 32000
TFEAT = 256
BINS = 128
SEQ = 128
SEQ_DEV = 3
SEQS = 48


def place_ends(array, stream_key, smallest, high):
    spot = [jax.random.randint(jax.random.fold_in(stream_key, axis), (), 0, length) for axis, length in enumerate(array.shape)]
    longest = array.shape.index(max(array.shape))
    next_to = spot[:longest] + [(spot[longest] + 1) % array.shape[longest]] + spot[longest + 1:]
    return array.at[tuple(spot)].set(smallest).at[tuple(next_to)].set(high)


def shard_levels(stream_key, shape, shards, least, top_value):
    loudness = 1.0
    for axis_at, blocks in shards:
        steps = jax.random.uniform(jax.random.fold_in(jax.random.fold_in(stream_key, 6), axis_at), (blocks,), jnp.float32, least / len(shards), top_value / len(shards))
        loudness = loudness * jnp.repeat(jnp.exp(steps), shape[axis_at] // blocks).reshape((-1,) + (1,) * (len(shape) - 1 - axis_at))
    return loudness


def cumulative_ranks(amount, skew):
    portions = [(1 << 20) // math.isqrt(rank ** skew) + 1 for rank in range(1, amount + 1)]
    width = 1 + sum(portions) // (1 << 30)
    return np.cumsum(np.array([max(1, weight // width) for weight in portions]))


def skewed_ids(stream_key, extent, number_of, skew):
    table = cumulative_ranks(number_of, skew)
    pick = jax.random.randint(jax.random.fold_in(stream_key, 1), extent, 0, int(table[number_of - 1]))
    grade = jnp.searchsorted(jnp.asarray(table, jnp.int32), pick, side="right")
    return jax.random.permutation(jax.random.fold_in(stream_key, 2), number_of)[grade].astype(jnp.int32)


def normal_values(own_key, extent, scale, limit, shards=(), held_as=jnp.bfloat16):
    entries = scale * jax.random.normal(own_key, extent, jnp.float32)
    if shards:
        entries = entries * shard_levels(own_key, extent, shards, -0.22, 0.18)
    return jnp.clip(entries, -limit, limit).astype(held_as)


def setup_inputs(seed: int = 0) -> dict:
    streams_of = jax.random.split(jax.random.key(seed), 17)
    token_ids = place_ends(skewed_ids(streams_of[0], (SEQS, SEQ), VOCAB, 2), jax.random.fold_in(streams_of[0], 3), 0, VOCAB - 1).astype(jnp.int32)
    target_ids = place_ends(skewed_ids(streams_of[1], (SEQS, SEQ), VOCAB, 2), jax.random.fold_in(streams_of[1], 3), 0, VOCAB - 1).astype(jnp.int32)
    time_bins = place_ends(jax.random.randint(streams_of[2], (SEQS,), 0, BINS), jax.random.fold_in(streams_of[2], 1), 0, BINS - 1).astype(jnp.int32)
    sigma_table = jnp.clip(jnp.exp(jax.random.uniform(streams_of[3], (BINS,), jnp.float32, math.log(0.2), math.log(8.0))), 0.2, 8.0)
    noise = normal_values(streams_of[4], (SEQS, SEQ, EMB), 1.0, 6.0, ((0, 16),), jnp.float32)
    embed = normal_values(streams_of[5], (VOCAB, EMB), 1.0, 6.0, ((0, 16),))
    w_in = normal_values(streams_of[6], (EMB, D), EMB ** -0.5, 0.375)
    w_time = normal_values(streams_of[7], (2, TFEAT, 2 * D), TFEAT ** -0.5, 0.375, ((0, 2),))
    norm_gain = jnp.clip(1.0 + 0.1 * jax.random.normal(streams_of[8], (2, 2 * D), jnp.float32), 0.5, 1.5)
    w_qkv = normal_values(streams_of[9], (2, D, 3 * D), D ** -0.5, 0.1875, ((0, 2),))
    w_out = normal_values(streams_of[10], (2, D, D), (D // 4) ** -0.5, 0.375, ((0, 2),))
    w_up = normal_values(streams_of[11], (2, D, FF), D ** -0.5, 0.1875, ((0, 2),))
    b_hidden = normal_values(streams_of[12], (2, FF), 0.5, 3.0, ((0, 2),), jnp.float32)
    w_down = normal_values(streams_of[13], (2, FF, D), FF ** -0.5, 0.09375, ((0, 2),))
    out_gain = jnp.clip(1.0 + 0.1 * jax.random.normal(streams_of[14], (D,), jnp.float32), 0.5, 1.5)
    head = normal_values(streams_of[15], (VOCAB, D), (D // 4) ** -0.5, 0.375, ((0, 32),))
    return dict(token_ids=token_ids, target_ids=target_ids, time_bins=time_bins, sigma_table=sigma_table, noise=noise, embed=embed, w_in=w_in, w_time=w_time, norm_gain=norm_gain, w_qkv=w_qkv, w_out=w_out, w_up=w_up, b_hidden=b_hidden, w_down=w_down, out_gain=out_gain, head=head)


@jax.custom_vjp
def low(v):
    return lax.optimization_barrier(v.astype(jnp.bfloat16)).astype(jnp.float32)

@jax.custom_vjp
def low_back(v):
    return v

def low_keep(v):
    return (low(v), None)

def low_pass(kept, grad):
    return (grad,)

def back_keep(v):
    return (v, None)

def back_low(kept, grad):
    return (low(grad),)
low.defvjp(low_keep, low_pass)
low_back.defvjp(back_keep, back_low)
epsilon = 1e-05
highest = lax.Precision.HIGHEST

def norm_rows(values):
    centred = values - lax.optimization_barrier(jnp.mean(values, -1, keepdims=True))
    return centred * lax.rsqrt(lax.optimization_barrier(jnp.mean(centred * centred, -1, keepdims=True)) + epsilon)

def time_features(noise_level):
    half_width = TFEAT // 2
    rates = jnp.exp(jnp.arange(half_width, dtype=jnp.float32) * (math.log(1000.0) / half_width))
    angles = (jnp.log(noise_level) / 4.0)[:, None] * rates[None, :]
    return jnp.concatenate([jnp.cos(angles), jnp.sin(angles)], -1)

def block(stream, time_feats, w_time, gain, w_qkv, w_out, w_up, b_hidden, w_down):
    seq_count, length, model_width = stream.shape
    conditioned = jnp.dot(time_feats, w_time, precision=highest) + gain
    scale_attn = conditioned[:, None, :model_width]
    scale_mlp = conditioned[:, None, model_width:]
    attn_entry = low(norm_rows(stream) * scale_attn)
    joined = low(low_back(jnp.einsum('nsd,de->nse', attn_entry, w_qkv, precision=highest)))
    qkv_parts = joined.reshape(seq_count, length, 3, HEADS, HEAD_DIM)
    query_rows = qkv_parts[:, :, 0]
    key_rows = qkv_parts[:, :, 1]
    value_rows = qkv_parts[:, :, 2]
    scores = low_back(jnp.einsum('nqhe,nkhe->nhqk', query_rows, key_rows, precision=highest) / math.sqrt(HEAD_DIM))
    largest = lax.optimization_barrier(jnp.max(scores, -1, keepdims=True))
    exp_scores = jnp.exp(scores - largest)
    attn_probs = exp_scores / lax.optimization_barrier(jnp.sum(exp_scores, -1, keepdims=True))
    attn_mixed = low(low_back(jnp.einsum('nhqk,nkhe->nqhe', low(attn_probs), value_rows, precision=highest)))
    attn_mixed = attn_mixed.reshape(seq_count, length, model_width)
    middle = stream + low_back(jnp.einsum('nsd,de->nse', attn_mixed, w_out, precision=highest))
    mlp_entry = low(norm_rows(middle) * scale_mlp)
    up_proj = low_back(jnp.einsum('nsd,df->nsf', mlp_entry, w_up, precision=highest) + b_hidden)
    hidden = low(jax.nn.gelu(up_proj, approximate=False))
    return middle + low_back(jnp.einsum('nsf,fd->nsd', hidden, w_down, precision=highest))

def objective(params, token_rows, target_rows, noise_level, noise_rows):
    embed, w_in, w_time, norm_gain, w_qkv, w_out, w_up, b_hidden, w_down, out_gain, head = params
    embedded = jnp.take(embed, token_rows, axis=0)
    unit_rows = embedded * lax.rsqrt(lax.optimization_barrier(jnp.mean(embedded * embedded, -1, keepdims=True)) + epsilon)
    level_col = noise_level[:, None, None]
    noisy_rows = low((unit_rows + level_col * noise_rows) * lax.rsqrt(level_col * level_col + 1.0))
    stream = low_back(jnp.einsum('nse,ed->nsd', noisy_rows, w_in, precision=highest))
    time_feats = time_features(noise_level)
    stream = block(stream, time_feats, w_time[0], norm_gain[0], w_qkv[0], w_out[0], w_up[0], b_hidden[0], w_down[0])
    stream = low(low_back(stream))
    stream = block(stream, time_feats, w_time[1], norm_gain[1], w_qkv[1], w_out[1], w_up[1], b_hidden[1], w_down[1])
    stream = low(stream)
    final_rows = low(norm_rows(stream) * out_gain)
    logits = low_back(jnp.einsum('nsd,vd->nsv', final_rows, head, precision=highest))
    picked = jnp.take_along_axis(logits, target_rows[..., None], -1)[..., 0]
    return jnp.sum(jax.nn.logsumexp(logits, -1) - picked) / SEQ

def reference(token_ids, target_ids, time_bins, sigma_table, noise, embed, w_in, w_time, norm_gain, w_qkv, w_out, w_up, b_hidden, w_down, out_gain, head):
    params = tuple((member.astype(jnp.float32) for member in (embed, w_in, w_time, norm_gain, w_qkv, w_out, w_up, b_hidden, w_down, out_gain, head)))
    groups = token_ids.shape[0] // SEQ_DEV
    blocks = (token_ids.reshape(groups, SEQ_DEV, SEQ), target_ids.reshape(groups, SEQ_DEV, SEQ), jnp.take(sigma_table, time_bins).reshape(groups, SEQ_DEV), noise.astype(jnp.float32).reshape(groups, SEQ_DEV, SEQ, EMB))

    def scan_step(running, block_data):
        token_rows, target_rows, noise_level, noise_rows = block_data

        def local_objective(*params_now):
            return objective(params_now, token_rows, target_rows, noise_level, noise_rows)
        objective_value, pullback = jax.vjp(local_objective, *params)
        gradients = pullback(jnp.ones_like(objective_value))
        summed = tuple((before + fresh for before, fresh in zip(running[1], gradients)))
        return ((running[0] + objective_value, summed), None)
    start_state = (jnp.zeros((), jnp.float32), tuple((jnp.zeros_like(member) for member in params)))
    (grand_total, gradients), _ = lax.scan(scan_step, start_state, blocks)
    grad_embed, grad_w_in, grad_w_time, grad_norm_gain, grad_w_qkv, grad_w_out, grad_w_up, grad_b_hidden, grad_w_down, grad_out_gain, grad_head = gradients
    loss = grand_total / token_ids.shape[0]
    return (loss, grad_embed, grad_w_in, grad_w_time, grad_norm_gain, grad_w_qkv, grad_w_out, grad_w_up, grad_b_hidden, grad_w_down, grad_out_gain, grad_head)
```

```python
from functools import partial
import math

import jax
import jax.numpy as jnp
from jax import lax
from jax.sharding import Mesh, PartitionSpec as P

HEADS = 16
HEAD_DIM = 64
TFEAT = 256

epsilon = 1e-05
highest = lax.Precision.HIGHEST
f32 = jnp.float32
bf16 = jnp.bfloat16
DP = ("chip", "core")


def norm_rows(values):
    centred = values - jnp.mean(values, -1, keepdims=True)
    factor = lax.rsqrt(jnp.mean(centred * centred, -1, keepdims=True) + epsilon)
    return (centred * factor, factor)


def norm_back(gradient, normed, factor):
    return factor * (
        gradient
        - jnp.mean(gradient, -1, keepdims=True)
        - normed * jnp.mean(gradient * normed, -1, keepdims=True)
    )


def time_features(noise_level):
    half_width = TFEAT // 2
    rates = jnp.exp(jnp.arange(half_width, dtype=f32) * (math.log(1000.0) / half_width))
    angles = (jnp.log(noise_level) / 4.0)[:, None] * rates[None, :]
    return jnp.concatenate([jnp.cos(angles), jnp.sin(angles)], -1)


def levels_of(bins, table):
    hits = bins[:, None] == jnp.arange(table.shape[0])[None, :]
    return jnp.sum(jnp.where(hits, table[None, :], 0.0), -1)


def over_dp(part):
    cores = lax.axis_size("core")
    part = part.reshape((part.shape[0] // cores, cores) + part.shape[1:])
    part = lax.psum_scatter(part, "core", scatter_dimension=1)
    return lax.psum_scatter(part, "chip", scatter_dimension=0)


def rows_over_dp(part):
    count = lax.axis_size("chip") * lax.axis_size("core")
    rows = part.shape[0]
    return over_dp(part.astype(bf16).reshape((count, rows // count) + part.shape[1:])).astype(f32)


def mm(spec, left, right):
    return jnp.einsum(spec, left, right, preferred_element_type=f32)


def layer_forward(stream, scale_attn, scale_mlp, weights):
    w_qkv, w_out, w_up, b_hidden, w_down = weights
    seq_count, length, model_width = stream.shape
    normed_attn, factor_attn = norm_rows(stream)
    attn_entry = (normed_attn * scale_attn).astype(bf16)
    joined = mm("nsd,de->nse", attn_entry, w_qkv).astype(bf16)
    qkv_parts = joined.reshape(seq_count, length, 3, HEADS, HEAD_DIM)
    query_rows = qkv_parts[:, :, 0]
    key_rows = qkv_parts[:, :, 1]
    value_rows = qkv_parts[:, :, 2]
    scores = mm("nqhe,nkhe->nhqk", query_rows, key_rows) / math.sqrt(HEAD_DIM)
    exp_scores = jnp.exp(scores - jnp.max(scores, -1, keepdims=True))
    attn_probs = exp_scores / jnp.sum(exp_scores, -1, keepdims=True)
    probs_low = attn_probs.astype(bf16)
    attn_mixed = mm("nhqk,nkhe->nqhe", probs_low, value_rows).astype(bf16)
    attn_mixed = attn_mixed.reshape(seq_count, length, model_width)
    middle = stream + mm("nsd,de->nse", attn_mixed, w_out)
    normed_mlp, factor_mlp = norm_rows(middle)
    mlp_entry = (normed_mlp * scale_mlp).astype(bf16)
    up_proj = mm("nsd,df->nsf", mlp_entry, w_up) + b_hidden
    hidden = jax.nn.gelu(up_proj, approximate=False).astype(bf16)
    block_out = middle + mm("nsf,fd->nsd", hidden, w_down)
    kept = (
        normed_attn,
        factor_attn,
        attn_entry,
        query_rows,
        key_rows,
        value_rows,
        attn_probs,
        probs_low,
        attn_mixed,
        normed_mlp,
        factor_mlp,
        mlp_entry,
        up_proj,
        hidden,
    )
    return (block_out, kept)


def layer_backward(grad_out, kept, scale_attn, scale_mlp, weights, whole):
    w_qkv, w_out, w_up, b_hidden, w_down = weights
    (
        normed_attn,
        factor_attn,
        attn_entry,
        query_rows,
        key_rows,
        value_rows,
        attn_probs,
        probs_low,
        attn_mixed,
        normed_mlp,
        factor_mlp,
        mlp_entry,
        up_proj,
        hidden,
    ) = kept
    seq_count, length, model_width = grad_out.shape
    grads = {}
    grad_branch = grad_out.astype(bf16)
    if whole:
        grads["down"] = rows_over_dp(mm("nsf,nsd->fd", hidden, grad_branch))
    grad_hidden = mm("nsd,fd->nsf", grad_branch, w_down)
    _, gelu_pull = jax.vjp(partial(jax.nn.gelu, approximate=False), up_proj)
    grad_up_proj = gelu_pull(grad_hidden)[0].astype(bf16)
    if whole:
        grads["bias"] = jnp.sum(grad_up_proj.astype(f32), (0, 1))
        grads["up"] = rows_over_dp(mm("nsd,nsf->df", mlp_entry, grad_up_proj))
    grad_entry = mm("nsf,df->nsd", grad_up_proj, w_up)
    grad_middle = grad_out + norm_back(grad_entry * scale_mlp, normed_mlp, factor_mlp)
    grad_attn = grad_middle.astype(bf16)
    if whole:
        grads["out"] = rows_over_dp(mm("nsd,nse->de", attn_mixed, grad_attn))
    grad_mixed = mm("nse,de->nsd", grad_attn, w_out)
    grad_mixed = grad_mixed.astype(bf16).reshape(seq_count, length, HEADS, HEAD_DIM)
    grad_probs = mm("nqhe,nkhe->nhqk", grad_mixed, value_rows)
    grad_values = mm("nhqk,nqhe->nkhe", probs_low, grad_mixed)
    grad_scores = (
        attn_probs * (grad_probs - jnp.sum(grad_probs * attn_probs, -1, keepdims=True))
    ).astype(bf16)
    grad_query = mm("nhqk,nkhe->nqhe", grad_scores, key_rows) / math.sqrt(HEAD_DIM)
    grad_keys = mm("nhqk,nqhe->nkhe", grad_scores, query_rows) / math.sqrt(HEAD_DIM)
    grad_joined = jnp.stack([grad_query, grad_keys, grad_values], 2).astype(bf16)
    grad_joined = grad_joined.reshape(seq_count, length, 3 * model_width)
    if whole:
        grads["qkv"] = rows_over_dp(mm("nsd,nse->de", attn_entry, grad_joined))
    grad_attn_entry = mm("nse,de->nsd", grad_joined, w_qkv)
    grad_stream = grad_middle + norm_back(grad_attn_entry * scale_attn, normed_attn, factor_attn)
    if whole:
        grads["cond"] = jnp.concatenate(
            [jnp.sum(grad_attn_entry * normed_attn, 1), jnp.sum(grad_entry * normed_mlp, 1)], -1
        )
    return (grad_stream, grads)


def local(
    token_ids,
    target_ids,
    time_bins,
    sigma_table,
    noise,
    embed,
    w_in,
    w_time,
    norm_gain,
    w_qkv,
    w_out,
    w_up,
    b_hidden,
    w_down,
    out_gain,
    head,
):
    section = lax.axis_index("section")
    chip = lax.axis_index("chip")
    core = lax.axis_index("core")
    sections = lax.axis_size("section")
    chips = lax.axis_size("chip")
    cores = lax.axis_size("core")
    dp_count = chips * cores
    dp_index = chip * cores + core
    is_first = section == 0
    seqs, length = token_ids.shape
    tokens = seqs * length
    half = tokens // sections
    model_width = w_out.shape[-1]
    emb_rows, emb_width = embed.shape

    own_ids = jnp.concatenate([token_ids.reshape(-1), target_ids.reshape(-1), time_bins])
    all_ids = lax.all_gather(own_ids, DP)
    all_tokens = all_ids[:, :tokens]
    all_targets = all_ids[:, tokens : 2 * tokens]
    all_bins = all_ids[:, 2 * tokens :].reshape(-1)

    own_rows = dp_index * emb_rows + jnp.arange(emb_rows)
    picked = (all_tokens.reshape(-1)[:, None] == own_rows[None, :]).astype(bf16)
    found = jnp.dot(picked, embed, preferred_element_type=f32).astype(bf16)
    embedded = over_dp(found.reshape(dp_count, tokens, emb_width)).astype(f32)
    embedded = embedded.reshape(seqs, length, emb_width)

    head_rows = head.shape[0]
    head_group = lax.all_gather(lax.all_gather(head, "core"), "section")
    vocab_base = (
        (jnp.arange(sections)[:, None] * chips + chip) * cores + jnp.arange(cores)[None, :]
    ) * head_rows
    columns = (vocab_base[:, :, None] + jnp.arange(head_rows)[None, None, :]).reshape(-1)
    head_group = head_group.reshape(-1, model_width)

    noise_level = levels_of(time_bins, sigma_table)
    unit_factor = lax.rsqrt(jnp.mean(embedded * embedded, -1, keepdims=True) + epsilon)
    level_col = noise_level[:, None, None]
    noise_scale = lax.rsqrt(level_col * level_col + 1.0)
    noisy_rows = ((embedded * unit_factor + level_col * noise) * noise_scale).astype(bf16)
    time_feats = time_features(noise_level)
    conditioned = jnp.dot(time_feats, w_time[0].astype(f32), precision=highest) + norm_gain[0]
    scale_attn = conditioned[:, None, :model_width]
    scale_mlp = conditioned[:, None, model_width:]
    weights = (w_qkv[0], w_out[0], w_up[0], b_hidden[0], w_down[0])

    stream0 = mm("nse,ed->nsd", noisy_rows, w_in)
    first_out, _ = layer_forward(stream0, scale_attn, scale_mlp, weights)
    arrived = lax.ppermute(first_out.astype(bf16), "section", [(0, 1), (1, 0)])
    stream = jnp.where(is_first, stream0, arrived.astype(f32))
    block_out, kept = layer_forward(stream, scale_attn, scale_mlp, weights)

    top_stream = block_out.astype(bf16).astype(f32)
    final_normed, final_factor = norm_rows(top_stream)
    final_rows = (final_normed * out_gain).astype(bf16).reshape(tokens, model_width)
    handed = lax.ppermute(final_rows[:half], "section", [(1, 0), (0, 1)])
    own_final = jnp.where(is_first, handed, final_rows[half:])
    group_final = lax.all_gather(own_final, "chip", tiled=True)
    targets_group = lax.dynamic_slice_in_dim(
        all_targets.reshape(chips, cores, tokens), core, 1, 1
    )[:, 0]
    targets_group = lax.dynamic_slice_in_dim(targets_group, section * half, half, 1).reshape(-1)
    logits = mm("td,vd->tv", group_final, head_group)
    local_top = jnp.max(logits, -1)
    local_total = jnp.sum(jnp.exp(logits - local_top[:, None]), -1)
    mark = columns[None, :] == targets_group[:, None]
    local_pick = jnp.sum(jnp.where(mark, logits, 0.0))
    stats = lax.all_gather(jnp.stack([local_top, local_total]), "chip")
    all_top = jnp.max(stats[:, 0], 0)
    all_total = jnp.sum(stats[:, 1] * jnp.exp(stats[:, 0] - all_top), 0)
    log_total = all_top + jnp.log(all_total)
    soft_rows = jnp.exp(logits - log_total[:, None])
    logit_grads = ((soft_rows - jnp.where(mark, 1.0, 0.0)) / length).astype(bf16)
    grad_final = jnp.dot(logit_grads, head_group, preferred_element_type=f32).astype(bf16)
    grad_final = lax.psum_scatter(grad_final, "chip", scatter_dimension=0, tiled=True)
    handed = lax.ppermute(grad_final, "section", [(0, 1), (1, 0)])
    grad_final = jnp.concatenate([handed, grad_final], 0).astype(f32)
    grad_final = grad_final.reshape(seqs, length, model_width)
    grad_head = mm("tv,td->vd", logit_grads, group_final).astype(bf16)
    grad_head = grad_head.reshape(sections, cores, head_rows, model_width)
    grad_head = lax.psum_scatter(grad_head, "core", scatter_dimension=1)
    grad_head = lax.psum_scatter(grad_head, "section", scatter_dimension=0).astype(f32)

    out_part = jnp.where(is_first, 0.0, jnp.sum(grad_final * final_normed, (0, 1)))
    ce_part = jnp.sum(log_total) / chips - local_pick
    early = lax.psum(jnp.concatenate([out_part, ce_part[None]]), ("section",) + DP)
    loss = early[model_width] / (tokens * dp_count)
    gain_rows = model_width // dp_count
    grad_out_gain = lax.dynamic_slice_in_dim(early, dp_index * gain_rows, gain_rows)

    grad_top = norm_back(grad_final * out_gain, final_normed, final_factor)
    grad_second, _ = layer_backward(grad_top, kept, scale_attn, scale_mlp, weights, False)
    returned = lax.ppermute(grad_second.astype(bf16), "section", [(0, 1), (1, 0)])
    grad_cot = jnp.where(is_first, returned.astype(f32), grad_top)
    grad_stream, grads = layer_backward(grad_cot, kept, scale_attn, scale_mlp, weights, True)
    grad_first = grad_stream.astype(bf16)

    in_part = mm("nse,nsd->ed", noisy_rows, grad_first).astype(bf16)
    in_part = in_part.reshape(sections, dp_count, -1, model_width).swapaxes(0, 1)
    in_part = over_dp(in_part)
    in_handed = lax.ppermute(in_part[1], "section", [(0, 1), (1, 0)])
    grad_w_in = jnp.where(is_first, in_part[0], in_handed).astype(f32)
    grad_noisy = mm("nsd,ed->nse", grad_first, w_in)
    grad_unit = grad_noisy * noise_scale
    cubed = unit_factor * unit_factor * unit_factor
    grad_embedded = unit_factor * grad_unit - cubed * embedded * jnp.mean(
        grad_unit * embedded, -1, keepdims=True
    )
    grad_flat = grad_embedded.reshape(tokens, emb_width).astype(bf16)
    handed = lax.ppermute(grad_flat, "section", [(0, 1), (1, 0)])
    grad_flat = jnp.where(is_first, grad_flat, handed)
    grad_all = lax.all_gather(grad_flat, DP, tiled=True)
    out_rows = emb_rows // sections
    target_rows = (section * dp_count + dp_index) * out_rows + jnp.arange(out_rows)
    place = (target_rows[:, None] == all_tokens.reshape(-1)[None, :]).astype(bf16)
    grad_embed = jnp.dot(place, grad_all, preferred_element_type=f32)

    late = lax.all_gather(jnp.concatenate([grads["cond"].reshape(-1), grads["bias"]]), DP)
    cond_size = grads["cond"].size
    cond_all = late[:, :cond_size].reshape(dp_count * seqs, 2 * model_width)
    hidden_rows = grads["bias"].shape[0] // dp_count
    grad_bias = jnp.sum(
        lax.dynamic_slice_in_dim(late, cond_size + dp_index * hidden_rows, hidden_rows, 1), 0
    )
    norm_cols = 2 * model_width // dp_count
    grad_gain = jnp.sum(lax.dynamic_slice_in_dim(cond_all, dp_index * norm_cols, norm_cols, 1), 0)
    feats_all = time_features(levels_of(all_bins, sigma_table))
    feat_rows = TFEAT // dp_count
    feats_own = lax.dynamic_slice_in_dim(feats_all, dp_index * feat_rows, feat_rows, 1)
    grad_time = jnp.dot(feats_own.T, cond_all, precision=highest)
    return (
        loss,
        grad_embed,
        grad_w_in,
        grad_time[None],
        grad_gain[None],
        grads["qkv"][None],
        grads["out"][None],
        grads["up"][None],
        grad_bias[None],
        grads["down"][None],
        grad_out_gain,
        grad_head,
    )


def solution(mesh):
    sections, dp_count = mesh.shape["section"], mesh.shape["dp"]
    fine = Mesh(mesh.devices.reshape(sections, dp_count // 2, 2), ("section",) + DP)
    everywhere = ("section",) + DP
    in_specs = (
        P(DP, None),
        P(DP, None),
        P(DP),
        P(),
        P(DP, None, None),
        P(DP, None),
        P(),
        P("section", None, None),
        P("section", None),
        P("section", None, None),
        P("section", None, None),
        P("section", None, None),
        P("section", None),
        P("section", None, None),
        P(),
        P(everywhere, None),
    )
    out_specs = (
        P(),
        P(everywhere, None),
        P(everywhere, None),
        P("section", DP, None),
        P("section", DP),
        P("section", DP, None),
        P("section", DP, None),
        P("section", DP, None),
        P("section", DP),
        P("section", DP, None),
        P(DP),
        P(everywhere, None),
    )
    return jax.shard_map(local, mesh=fine, in_specs=in_specs, out_specs=out_specs, check_vma=False)
```

```python
from functools import partial
import math

import jax
import jax.numpy as jnp
from jax import lax
from jax.experimental import pallas as pl
from jax.experimental.pallas import tpu as pltpu
from jax.sharding import Mesh, PartitionSpec as P

HEADS = 16
HEAD_DIM = 64
TFEAT = 256

epsilon = 1e-05
highest = lax.Precision.HIGHEST
f32 = jnp.float32
bf16 = jnp.bfloat16
DP = ("line", "pair", "core")


MESH = pl.DeviceIdType.MESH


def greet(peers):
    barrier = pltpu.get_barrier_semaphore()
    for peer in peers:
        pl.semaphore_signal(barrier, inc=1, device_id=peer, device_id_type=MESH)
    pl.semaphore_wait(barrier, len(peers))


def remote(source, target, send, recv, peer):
    return pltpu.make_async_remote_copy(
        src_ref=source,
        dst_ref=target,
        send_sem=send,
        recv_sem=recv,
        device_id=peer,
        device_id_type=MESH,
    )


def sum_pieces(shapes, splits):
    pieces = []
    for index, (shape, parts) in enumerate(zip(shapes, splits)):
        wide = shape[-1] // parts
        pieces += [(index, part * wide, wide) for part in range(parts)]
    return pieces


def sum_kernel(shapes, splits, line, packet_rows, swap, *refs):
    count = len(shapes)
    pieces = sum_pieces(shapes, splits)
    refs = list(refs)
    parts = [refs.pop(0) for _ in range(count)]
    packet = refs.pop(0) if packet_rows else None
    outs = [refs.pop(0) for _ in range(count)]
    packets = refs.pop(0) if packet_rows else None
    own = [refs.pop(0) for _ in range(count)]
    from_core = [refs.pop(0) for _ in range(count)]
    from_pair = [refs.pop(0) for _ in range(count)]
    from_line = [refs.pop(0) for _ in range(count)]
    load_sem, core_send, core_recv, pair_send, pair_recv, line_send, line_recv = refs[:7]
    refs = refs[7:]
    me_section = lax.axis_index("section")
    me_line = lax.axis_index("line")
    me_pair = lax.axis_index("pair")
    me_core = lax.axis_index("core")
    section_peer = {"section": 1 - me_section}
    core_peer = {"core": 1 - me_core}
    pair_peer = {"pair": 1 - me_pair}
    line_at = [lax.rem(me_line + step, line) for step in range(1, line)]
    line_peers = [{"line": place} for place in line_at]
    greet([core_peer, pair_peer] + line_peers + ([section_peer] if swap else []))

    started = []
    if packet_rows:
        own_sem, packet_send, packet_recv, wide_send, wide_recv = refs
        mine = packets.at[me_line, me_pair, me_core]
        keep = pltpu.make_async_copy(packet, mine, own_sem)
        keep.start()
        along = [
            remote(packet, mine, packet_send.at[n], packet_recv.at[n], peer)
            for n, peer in enumerate(line_peers)
        ]
        for copy in along:
            copy.start()

    def columns(piece):
        _, first, wide = pieces[piece]
        return pl.ds(first, wide)

    loads, core_copies, pair_copies, line_copies = {}, {}, {}, {}
    for piece, (index, _, _) in enumerate(pieces):
        cols = columns(piece)
        for turn, side in enumerate((1 - me_pair, me_pair)):
            load = pltpu.make_async_copy(
                parts[index].at[:, side, me_core, :, cols],
                own[index].at[:, side, :, cols],
                load_sem.at[piece, turn],
            )
            load.start()
            loads[piece, turn] = load
            copy = remote(
                parts[index].at[:, side, 1 - me_core, :, cols],
                from_core[index].at[:, side, :, cols],
                core_send.at[piece, turn],
                core_recv.at[piece, turn],
                core_peer,
            )
            copy.start()
            core_copies[piece, turn] = copy

    def tiles(piece, body):
        index, first, wide = pieces[piece]
        rows = shapes[index][-2]
        step = min(wide, 512)

        @pl.loop(0, rows // 16)
        def _(block):
            row = pl.ds(pl.multiple_of(block * 16, 16), 16)
            for col in range(first, first + wide, step):
                body(index, row, pl.ds(col, step))

    def over_cores(piece):
        loads[piece, 0].wait()
        core_copies[piece, 0].wait_recv()
        side = 1 - me_pair

        def add(index, row, cols):
            for place in range(line):
                total = from_core[index][place, side, row, cols].astype(f32) + own[index][
                    place, side, row, cols
                ].astype(f32)
                from_core[index][place, side, row, cols] = total.astype(bf16)

        tiles(piece, add)
        index = pieces[piece][0]
        cols = columns(piece)
        copy = remote(
            from_core[index].at[:, side, :, cols],
            from_pair[index].at[:, :, cols],
            pair_send.at[piece],
            pair_recv.at[piece],
            pair_peer,
        )
        copy.start()
        pair_copies[piece] = copy

    def over_pair(piece):
        loads[piece, 1].wait()
        core_copies[piece, 1].wait_recv()
        pair_copies[piece].wait_recv()

        def add(index, row, cols):
            for place in range(line):
                total = (
                    from_core[index][place, me_pair, row, cols].astype(f32)
                    + own[index][place, me_pair, row, cols].astype(f32)
                    + from_pair[index][place, row, cols].astype(f32)
                )
                from_core[index][place, me_pair, row, cols] = total.astype(bf16)

        tiles(piece, add)
        index = pieces[piece][0]
        cols = columns(piece)
        for n, peer in enumerate(line_peers):
            copy = remote(
                from_core[index].at[line_at[n], me_pair, :, cols],
                from_line[index].at[n, :, cols],
                line_send.at[piece, n],
                line_recv.at[piece, n],
                peer,
            )
            copy.start()
            line_copies[piece, n] = copy

    def over_line(piece):
        for n in range(line - 1):
            line_copies[piece, n].wait_recv()

        def add(index, row, cols):
            total = from_core[index][me_line, me_pair, row, cols].astype(f32)
            for n in range(line - 1):
                total = total + from_line[index][n, row, cols].astype(f32)
            if swap:
                outs[index][me_section, row, cols] = total.astype(outs[index].dtype)
            else:
                outs[index][row, cols] = total.astype(outs[index].dtype)

        tiles(piece, add)

    total = len(pieces)
    lead = 2
    for piece in range(min(lead, total)):
        over_cores(piece)
    if packet_rows:
        keep.wait()
        for copy in along:
            copy.wait()
        sideways = remote(
            packets.at[:, me_pair, me_core],
            packets.at[:, me_pair, me_core],
            wide_send.at[0],
            wide_recv.at[0],
            pair_peer,
        )
        sideways.start()
    for piece in range(total + 1):
        if piece + lead < total:
            over_cores(piece + lead)
        if piece < total:
            over_pair(piece)
        if packet_rows and piece == 1:
            sideways.wait()
            across = remote(
                packets.at[:, :, me_core],
                packets.at[:, :, me_core],
                wide_send.at[1],
                wide_recv.at[1],
                core_peer,
            )
            across.start()
        if piece >= 1:
            over_line(piece - 1)
    if packet_rows:
        across.wait()
    for copy in list(core_copies.values()) + list(pair_copies.values()) + list(line_copies.values()):
        copy.wait_send()
    if swap:
        swap_send, swap_recv = refs[-2:]
        copy = remote(
            outs[0].at[me_section], outs[0].at[me_section], swap_send, swap_recv, section_peer
        )
        copy.start()
        copy.wait()


def summed_over_dp(parts, splits, collective_id, packet=None, swap=False):
    shapes = [part.shape for part in parts]
    line = shapes[0][0]
    total = len(sum_pieces(shapes, splits))
    packet_rows = 0 if packet is None else packet.shape[0]
    vmem = pl.BlockSpec(memory_space=pltpu.VMEM)
    anywhere = pl.BlockSpec(memory_space=pl.ANY)
    if swap:
        out_shape = [jax.ShapeDtypeStruct((2,) + shapes[0][-2:], bf16)]
    else:
        out_shape = [jax.ShapeDtypeStruct(shape[-2:], f32) for shape in shapes]
    out_specs = [vmem] * len(parts)
    operands = list(parts)
    in_specs = [anywhere] * len(parts)
    dma = pltpu.SemaphoreType.DMA
    scratch = [pltpu.VMEM((line, 2) + shape[-2:], bf16) for shape in shapes]
    scratch += [pltpu.VMEM((line, 2) + shape[-2:], bf16) for shape in shapes]
    scratch += [pltpu.VMEM((line,) + shape[-2:], bf16) for shape in shapes]
    scratch += [pltpu.VMEM((line - 1,) + shape[-2:], bf16) for shape in shapes]
    scratch += [dma((total, 2))] * 3 + [dma((total,))] * 2 + [dma((total, line - 1))] * 2
    if packet_rows:
        operands.append(packet)
        in_specs.append(anywhere)
        out_shape.append(jax.ShapeDtypeStruct((line, 2, 2) + packet.shape, packet.dtype))
        out_specs.append(anywhere)
        scratch += [dma, dma((line - 1,)), dma((line - 1,)), dma((2,)), dma((2,))]
    if swap:
        scratch += [dma, dma]
    return pl.pallas_call(
        partial(sum_kernel, shapes, splits, line, packet_rows, swap),
        out_shape=out_shape,
        in_specs=in_specs,
        out_specs=out_specs,
        scratch_shapes=scratch,
        compiler_params=pltpu.CompilerParams(
            collective_id=collective_id, has_side_effects=True, vmem_limit_bytes=60 * 2**20
        ),
    )(*operands)


def gather_kernel(line, mine, out, send, recv, own_sem):
    me_line = lax.axis_index("line")
    me_pair = lax.axis_index("pair")
    me_core = lax.axis_index("core")
    peers = []
    for step in range(1, line * 4):
        peers.append(
            {
                "line": lax.rem(me_line + step // 4, line),
                "pair": lax.rem(me_pair + step // 2 % 2, 2),
                "core": lax.rem(me_core + step % 2, 2),
            }
        )
    greet(peers)
    place = out.at[me_line, me_pair, me_core]
    keep = pltpu.make_async_copy(mine, place, own_sem)
    keep.start()
    copies = [remote(mine, place, send.at[n], recv.at[n], peer) for n, peer in enumerate(peers)]
    for copy in copies:
        copy.start()
    keep.wait()
    for copy in copies:
        copy.wait()


def gathered_small(block, line, collective_id):
    count = line * 4 - 1
    vmem = pl.BlockSpec(memory_space=pltpu.VMEM)
    return pl.pallas_call(
        partial(gather_kernel, line),
        out_shape=jax.ShapeDtypeStruct((line, 2, 2) + block.shape, block.dtype),
        in_specs=[vmem],
        out_specs=vmem,
        scratch_shapes=[
            pltpu.SemaphoreType.DMA((count,)),
            pltpu.SemaphoreType.DMA((count,)),
            pltpu.SemaphoreType.DMA,
        ],
        compiler_params=pltpu.CompilerParams(collective_id=collective_id, has_side_effects=True),
    )(block)


def norm_rows(values):
    centred = values - jnp.mean(values, -1, keepdims=True)
    factor = lax.rsqrt(jnp.mean(centred * centred, -1, keepdims=True) + epsilon)
    return (centred * factor, factor)


def norm_back(gradient, normed, factor):
    return factor * (
        gradient
        - jnp.mean(gradient, -1, keepdims=True)
        - normed * jnp.mean(gradient * normed, -1, keepdims=True)
    )


def time_features(noise_level):
    half_width = TFEAT // 2
    rates = jnp.exp(jnp.arange(half_width, dtype=f32) * (math.log(1000.0) / half_width))
    angles = (jnp.log(noise_level) / 4.0)[:, None] * rates[None, :]
    return jnp.concatenate([jnp.cos(angles), jnp.sin(angles)], -1)


def levels_of(bins, table):
    hits = bins[:, None] == jnp.arange(table.shape[0])[None, :]
    return jnp.sum(jnp.where(hits, table[None, :], 0.0), -1)


def over_dp(part):
    part = part.reshape((part.shape[0] // 4, 2, 2) + part.shape[1:])
    part = lax.psum_scatter(part, "core", scatter_dimension=2)
    part = lax.psum_scatter(part, "pair", scatter_dimension=1)
    return lax.psum_scatter(part, "line", scatter_dimension=0)


def by_owner(part):
    line = lax.axis_size("line")
    return part.astype(bf16).reshape((line, 2, 2, part.shape[0] // (line * 4)) + part.shape[1:])


def mm(spec, left, right):
    return jnp.einsum(spec, left, right, preferred_element_type=f32)


def layer_forward(stream, scale_attn, scale_mlp, weights):
    w_qkv, w_out, w_up, b_hidden, w_down = weights
    seq_count, length, model_width = stream.shape
    normed_attn, factor_attn = norm_rows(stream)
    attn_entry = (normed_attn * scale_attn).astype(bf16)
    joined = mm("nsd,de->nse", attn_entry, w_qkv).astype(bf16)
    qkv_parts = joined.reshape(seq_count, length, 3, HEADS, HEAD_DIM)
    query_rows = qkv_parts[:, :, 0]
    key_rows = qkv_parts[:, :, 1]
    value_rows = qkv_parts[:, :, 2]
    scores = mm("nqhe,nkhe->nhqk", query_rows, key_rows) / math.sqrt(HEAD_DIM)
    exp_scores = jnp.exp(scores - jnp.max(scores, -1, keepdims=True))
    attn_probs = exp_scores / jnp.sum(exp_scores, -1, keepdims=True)
    probs_low = attn_probs.astype(bf16)
    attn_mixed = mm("nhqk,nkhe->nqhe", probs_low, value_rows).astype(bf16)
    attn_mixed = attn_mixed.reshape(seq_count, length, model_width)
    middle = stream + mm("nsd,de->nse", attn_mixed, w_out)
    normed_mlp, factor_mlp = norm_rows(middle)
    mlp_entry = (normed_mlp * scale_mlp).astype(bf16)
    up_proj = mm("nsd,df->nsf", mlp_entry, w_up) + b_hidden
    hidden = jax.nn.gelu(up_proj, approximate=False).astype(bf16)
    block_out = middle + mm("nsf,fd->nsd", hidden, w_down)
    kept = (
        normed_attn,
        factor_attn,
        attn_entry,
        query_rows,
        key_rows,
        value_rows,
        attn_probs,
        probs_low,
        attn_mixed,
        normed_mlp,
        factor_mlp,
        mlp_entry,
        up_proj,
        hidden,
    )
    return (block_out, kept)


def layer_backward(grad_out, kept, scale_attn, scale_mlp, weights, whole):
    w_qkv, w_out, w_up, b_hidden, w_down = weights
    (
        normed_attn,
        factor_attn,
        attn_entry,
        query_rows,
        key_rows,
        value_rows,
        attn_probs,
        probs_low,
        attn_mixed,
        normed_mlp,
        factor_mlp,
        mlp_entry,
        up_proj,
        hidden,
    ) = kept
    seq_count, length, model_width = grad_out.shape
    grads = {}
    grad_branch = grad_out.astype(bf16)
    if whole:
        grads["down"] = by_owner(mm("nsf,nsd->fd", hidden, grad_branch))
    grad_hidden = mm("nsd,fd->nsf", grad_branch, w_down)
    _, gelu_pull = jax.vjp(partial(jax.nn.gelu, approximate=False), up_proj)
    grad_up_proj = gelu_pull(grad_hidden)[0].astype(bf16)
    if whole:
        grads["bias"] = jnp.sum(grad_up_proj.astype(f32), (0, 1))
        grads["up"] = by_owner(mm("nsd,nsf->df", mlp_entry, grad_up_proj))
    grad_entry = mm("nsf,df->nsd", grad_up_proj, w_up)
    grad_middle = grad_out + norm_back(grad_entry * scale_mlp, normed_mlp, factor_mlp)
    grad_attn = grad_middle.astype(bf16)
    if whole:
        grads["out"] = by_owner(mm("nsd,nse->de", attn_mixed, grad_attn))
    grad_mixed = mm("nse,de->nsd", grad_attn, w_out)
    grad_mixed = grad_mixed.astype(bf16).reshape(seq_count, length, HEADS, HEAD_DIM)
    grad_probs = mm("nqhe,nkhe->nhqk", grad_mixed, value_rows)
    grad_values = mm("nhqk,nqhe->nkhe", probs_low, grad_mixed)
    grad_scores = (
        attn_probs * (grad_probs - jnp.sum(grad_probs * attn_probs, -1, keepdims=True))
    ).astype(bf16)
    grad_query = mm("nhqk,nkhe->nqhe", grad_scores, key_rows) / math.sqrt(HEAD_DIM)
    grad_keys = mm("nhqk,nqhe->nkhe", grad_scores, query_rows) / math.sqrt(HEAD_DIM)
    grad_joined = jnp.stack([grad_query, grad_keys, grad_values], 2).astype(bf16)
    grad_joined = grad_joined.reshape(seq_count, length, 3 * model_width)
    if whole:
        grads["qkv"] = by_owner(mm("nsd,nse->de", attn_entry, grad_joined))
    grad_attn_entry = mm("nse,de->nsd", grad_joined, w_qkv)
    grad_stream = grad_middle + norm_back(grad_attn_entry * scale_attn, normed_attn, factor_attn)
    if whole:
        grads["cond"] = jnp.concatenate(
            [jnp.sum(grad_attn_entry * normed_attn, 1), jnp.sum(grad_entry * normed_mlp, 1)], -1
        )
    return (grad_stream, grads)


def local(
    token_ids,
    target_ids,
    time_bins,
    sigma_table,
    noise,
    embed,
    w_in,
    w_time,
    norm_gain,
    w_qkv,
    w_out,
    w_up,
    b_hidden,
    w_down,
    out_gain,
    head,
):
    section = lax.axis_index("section")
    line_at = lax.axis_index("line")
    pair_at = lax.axis_index("pair")
    core = lax.axis_index("core")
    sections = lax.axis_size("section")
    line = lax.axis_size("line")
    chip = line_at * 2 + pair_at
    chips = line * 2
    cores = 2
    dp_count = chips * cores
    dp_index = chip * cores + core
    is_first = section == 0
    seqs, length = token_ids.shape
    tokens = seqs * length
    half = tokens // sections
    model_width = w_out.shape[-1]
    emb_rows, emb_width = embed.shape
    straight = line <= 4 and half % 16 == 0 and model_width // dp_count % 16 == 0

    own_ids = jnp.concatenate([token_ids.reshape(-1), target_ids.reshape(-1), time_bins])
    if straight:
        padded = jnp.pad(own_ids, (0, -own_ids.shape[0] % 1024)).reshape(-1, 128)
        all_ids = gathered_small(padded, line, 0).reshape(dp_count, -1)[:, : own_ids.shape[0]]
    else:
        all_ids = lax.all_gather(own_ids, DP)
    all_tokens = all_ids[:, :tokens]
    all_targets = all_ids[:, tokens : 2 * tokens]
    all_bins = all_ids[:, 2 * tokens :].reshape(-1)

    own_rows = dp_index * emb_rows + jnp.arange(emb_rows)
    half_tokens = lax.dynamic_slice_in_dim(all_tokens, section * half, half, 1)
    picked = (half_tokens.reshape(-1)[:, None] == own_rows[None, :]).astype(bf16)
    found = jnp.dot(picked, embed, preferred_element_type=f32).astype(bf16)
    if straight:
        found = found.reshape(line, 2, 2, half, emb_width)
        (embedded,) = summed_over_dp([found], [2], 1, swap=True)
    else:
        embedded = lax.all_gather(over_dp(found.reshape(dp_count, half, emb_width)), "section")
    embedded = embedded.astype(f32).reshape(seqs, length, emb_width)

    head_rows = head.shape[0]
    head_group = lax.all_gather(lax.all_gather(head, "core"), "section")
    vocab_base = (
        (jnp.arange(sections)[:, None] * chips + chip) * cores + jnp.arange(cores)[None, :]
    ) * head_rows
    columns = (vocab_base[:, :, None] + jnp.arange(head_rows)[None, None, :]).reshape(-1)
    head_group = head_group.reshape(-1, model_width)

    noise_level = levels_of(time_bins, sigma_table)
    unit_factor = lax.rsqrt(jnp.mean(embedded * embedded, -1, keepdims=True) + epsilon)
    level_col = noise_level[:, None, None]
    noise_scale = lax.rsqrt(level_col * level_col + 1.0)
    noisy_rows = ((embedded * unit_factor + level_col * noise) * noise_scale).astype(bf16)
    time_feats = time_features(noise_level)
    conditioned = jnp.dot(time_feats, w_time[0].astype(f32), precision=highest) + norm_gain[0]
    scale_attn = conditioned[:, None, :model_width]
    scale_mlp = conditioned[:, None, model_width:]
    weights = (w_qkv[0], w_out[0], w_up[0], b_hidden[0], w_down[0])

    stream0 = mm("nse,ed->nsd", noisy_rows, w_in)
    first_out, _ = layer_forward(stream0, scale_attn, scale_mlp, weights)
    arrived = lax.ppermute(first_out.astype(bf16), "section", [(0, 1), (1, 0)])
    stream = jnp.where(is_first, stream0, arrived.astype(f32))
    block_out, kept = layer_forward(stream, scale_attn, scale_mlp, weights)

    top_stream = block_out.astype(bf16).astype(f32)
    final_normed, final_factor = norm_rows(top_stream)
    final_rows = (final_normed * out_gain).astype(bf16).reshape(tokens, model_width)
    handed = lax.ppermute(final_rows[:half], "section", [(1, 0), (0, 1)])
    own_final = jnp.where(is_first, handed, final_rows[half:])
    group_final = lax.all_gather(own_final, ("line", "pair"), tiled=True)
    targets_group = lax.dynamic_slice_in_dim(
        all_targets.reshape(chips, cores, tokens), core, 1, 1
    )[:, 0]
    targets_group = lax.dynamic_slice_in_dim(targets_group, section * half, half, 1).reshape(-1)
    logits = mm("td,vd->tv", group_final, head_group)
    local_top = jnp.max(logits, -1)
    local_total = jnp.sum(jnp.exp(logits - local_top[:, None]), -1)
    mark = columns[None, :] == targets_group[:, None]
    local_pick = jnp.sum(jnp.where(mark, logits, 0.0))
    stats = lax.all_gather(jnp.stack([local_top, local_total]), ("line", "pair"))
    all_top = jnp.max(stats[:, 0], 0)
    all_total = jnp.sum(stats[:, 1] * jnp.exp(stats[:, 0] - all_top), 0)
    log_total = all_top + jnp.log(all_total)
    soft_rows = jnp.exp(logits - log_total[:, None])
    logit_grads = ((soft_rows - jnp.where(mark, 1.0, 0.0)) / length).astype(bf16)
    grad_final = jnp.dot(logit_grads, head_group, preferred_element_type=f32).astype(bf16)
    grad_final = lax.psum_scatter(grad_final, ("line", "pair"), scatter_dimension=0, tiled=True)
    handed = lax.ppermute(grad_final, "section", [(0, 1), (1, 0)])
    grad_final = jnp.concatenate([handed, grad_final], 0).astype(f32)
    grad_final = grad_final.reshape(seqs, length, model_width)
    grad_head = mm("tv,td->vd", logit_grads, group_final).astype(bf16)
    grad_head = grad_head.reshape(sections, cores, head_rows, model_width)
    grad_head = lax.psum_scatter(grad_head, "core", scatter_dimension=1)
    grad_head = lax.psum_scatter(grad_head, "section", scatter_dimension=0).astype(f32)

    out_part = jnp.where(is_first, 0.0, jnp.sum(grad_final * final_normed, (0, 1)))
    ce_part = jnp.sum(log_total) / chips - local_pick
    grad_top = norm_back(grad_final * out_gain, final_normed, final_factor)
    grad_second, _ = layer_backward(grad_top, kept, scale_attn, scale_mlp, weights, False)
    returned = lax.ppermute(grad_second.astype(bf16), "section", [(0, 1), (1, 0)])
    grad_cot = jnp.where(is_first, returned.astype(f32), grad_top)
    grad_stream, grads = layer_backward(grad_cot, kept, scale_attn, scale_mlp, weights, True)
    grad_first = grad_stream.astype(bf16)

    in_part = mm("nse,nsd->ed", noisy_rows, grad_first).astype(bf16)
    in_part = in_part.reshape(sections, line, 2, 2, -1, model_width)
    in_part = jnp.moveaxis(in_part, 0, 3).reshape(line, 2, 2, -1, model_width)
    grad_noisy = mm("nsd,ed->nse", grad_first, w_in)
    grad_unit = grad_noisy * noise_scale
    cubed = unit_factor * unit_factor * unit_factor
    grad_embedded = unit_factor * grad_unit - cubed * embedded * jnp.mean(
        grad_unit * embedded, -1, keepdims=True
    )
    grad_flat = grad_embedded.reshape(tokens, emb_width)

    ce_high = ce_part.astype(bf16).astype(f32)
    ce_mid = (ce_part - ce_high).astype(bf16).astype(f32)
    ce_low = ce_part - ce_high - ce_mid
    shared = jnp.concatenate([out_part, jnp.stack([ce_high, ce_mid, ce_low])])
    shared_rows = -(-shared.shape[0] // emb_width)
    shared = jnp.pad(shared, (0, shared_rows * emb_width - shared.shape[0]))
    handing = jnp.concatenate([grad_flat, shared.reshape(-1, emb_width)], 0).astype(bf16)
    handed = lax.ppermute(handing, "section", [(0, 1), (1, 0)])
    kept_rows = jnp.where(is_first, handing[:tokens], handed[:tokens])
    layer_small = jnp.concatenate([grads["cond"].reshape(-1), grads["bias"]])
    layer_rows = layer_small.shape[0] // emb_width
    packet = jnp.concatenate(
        [
            kept_rows,
            layer_small.astype(bf16).reshape(layer_rows, emb_width),
            handing[tokens:],
            handed[tokens:],
        ],
        0,
    )
    packet = jnp.pad(packet, ((0, -packet.shape[0] % 16), (0, 0)))
    parts = [grads["down"], grads["up"], grads["qkv"], grads["out"], in_part]
    if straight:
        *sums, packets = summed_over_dp(parts, [2, 2, 2, 1, 1], 2, packet=packet)
        packets = packets.reshape((dp_count,) + packet.shape)
    else:
        sums = [over_dp(part.reshape((dp_count,) + part.shape[3:])).astype(f32) for part in parts]
        packets = lax.all_gather(packet, DP)
    grad_down, grad_up, grad_qkv, grad_wout, in_sum = sums
    in_sum = in_sum.reshape(sections, -1, model_width)
    in_handed = lax.ppermute(in_sum[1], "section", [(0, 1), (1, 0)])
    grad_w_in = jnp.where(is_first, in_sum[0], in_handed)

    grad_all = packets[:, :tokens].reshape(-1, emb_width)
    out_rows = emb_rows // sections
    target_rows = (section * dp_count + dp_index) * out_rows + jnp.arange(out_rows)
    place = (target_rows[:, None] == all_tokens.reshape(-1)[None, :]).astype(bf16)
    grad_embed = jnp.dot(place, grad_all, preferred_element_type=f32)

    small = packets[:, tokens : tokens + layer_rows].astype(f32).reshape(dp_count, -1)
    cond_size = grads["cond"].size
    cond_all = small[:, :cond_size].reshape(dp_count * seqs, 2 * model_width)
    hidden_rows = grads["bias"].shape[0] // dp_count
    grad_bias = jnp.sum(
        lax.dynamic_slice_in_dim(small, cond_size + dp_index * hidden_rows, hidden_rows, 1), 0
    )
    norm_cols = 2 * model_width // dp_count
    grad_gain = jnp.sum(lax.dynamic_slice_in_dim(cond_all, dp_index * norm_cols, norm_cols, 1), 0)
    feats_all = time_features(levels_of(all_bins, sigma_table))
    feat_rows = TFEAT // dp_count
    feats_own = lax.dynamic_slice_in_dim(feats_all, dp_index * feat_rows, feat_rows, 1)
    grad_time = jnp.dot(feats_own.T, cond_all, precision=highest)
    both = packets[:, tokens + layer_rows : tokens + layer_rows + 2 * shared_rows].astype(f32)
    both = jnp.sum(both.reshape(dp_count, 2, -1), (0, 1))
    loss = jnp.sum(both[model_width : model_width + 3]) / (tokens * dp_count)
    gain_rows = model_width // dp_count
    grad_out_gain = lax.dynamic_slice_in_dim(both, dp_index * gain_rows, gain_rows)
    return (
        loss,
        grad_embed,
        grad_w_in,
        grad_time[None],
        grad_gain[None],
        grad_qkv[None],
        grad_wout[None],
        grad_up[None],
        grad_bias[None],
        grad_down[None],
        grad_out_gain,
        grad_head,
    )


def solution(mesh):
    sections, dp_count = mesh.shape["section"], mesh.shape["dp"]
    fine = Mesh(mesh.devices.reshape(sections, dp_count // 4, 2, 2), ("section",) + DP)
    everywhere = ("section",) + DP
    in_specs = (
        P(DP, None),
        P(DP, None),
        P(DP),
        P(),
        P(DP, None, None),
        P(DP, None),
        P(),
        P("section", None, None),
        P("section", None),
        P("section", None, None),
        P("section", None, None),
        P("section", None, None),
        P("section", None),
        P("section", None, None),
        P(),
        P(everywhere, None),
    )
    out_specs = (
        P(),
        P(everywhere, None),
        P(everywhere, None),
        P("section", DP, None),
        P("section", DP),
        P("section", DP, None),
        P("section", DP, None),
        P("section", DP, None),
        P("section", DP),
        P("section", DP, None),
        P(DP),
        P(everywhere, None),
    )
    return jax.shard_map(local, mesh=fine, in_specs=in_specs, out_specs=out_specs, check_vma=False)
```

```python
from functools import partial
import math

import jax
import jax.numpy as jnp
from jax import lax
from jax.experimental import pallas as pl
from jax.experimental.pallas import tpu as pltpu
from jax.sharding import Mesh, PartitionSpec as P

HEADS = 16
HEAD_DIM = 64
TFEAT = 256

epsilon = 1e-05
highest = lax.Precision.HIGHEST
f32 = jnp.float32
bf16 = jnp.bfloat16
DP = ("line", "pair", "core")


MESH = pl.DeviceIdType.MESH


def greet(peers):
    barrier = pltpu.get_barrier_semaphore()
    for peer in peers:
        pl.semaphore_signal(barrier, inc=1, device_id=peer, device_id_type=MESH)
    pl.semaphore_wait(barrier, len(peers))


def remote(source, target, send, recv, peer):
    return pltpu.make_async_remote_copy(
        src_ref=source,
        dst_ref=target,
        send_sem=send,
        recv_sem=recv,
        device_id=peer,
        device_id_type=MESH,
    )


def sum_pieces(shapes, splits):
    pieces = []
    for index, (shape, parts) in enumerate(zip(shapes, splits)):
        wide = shape[-1] // parts
        pieces += [(index, part * wide, wide) for part in range(parts)]
    return pieces


def sum_kernel(shapes, splits, line, packet_rows, swap, with_head, *refs):
    count = len(shapes)
    pieces = sum_pieces(shapes, splits)
    refs = list(refs)
    parts = [refs.pop(0) for _ in range(count)]
    packet = refs.pop(0) if packet_rows else None
    head_part = refs.pop(0) if with_head else None
    outs = [refs.pop(0) for _ in range(count)]
    packets = refs.pop(0) if packet_rows else None
    head_out = refs.pop(0) if with_head else None
    own = [refs.pop(0) for _ in range(count)]
    from_core = [refs.pop(0) for _ in range(count)]
    from_pair = [refs.pop(0) for _ in range(count)]
    from_line = [refs.pop(0) for _ in range(count)]
    load_sem, core_send, core_recv, pair_send, pair_recv, line_send, line_recv = refs[:7]
    refs = refs[7:]
    if with_head:
        head_own, head_core, head_section = refs[-6:-3]
    me_section = lax.axis_index("section")
    me_line = lax.axis_index("line")
    me_pair = lax.axis_index("pair")
    me_core = lax.axis_index("core")
    section_peer = {"section": 1 - me_section}
    core_peer = {"core": 1 - me_core}
    pair_peer = {"pair": 1 - me_pair}
    line_at = [lax.rem(me_line + step, line) for step in range(1, line)]
    line_peers = [{"line": place} for place in line_at]
    greet([core_peer, pair_peer] + line_peers + ([section_peer] if swap or with_head else []))

    started = []
    if packet_rows:
        own_sem, packet_send, packet_recv, wide_send, wide_recv = refs[:5]
        mine = packets.at[me_line, me_pair, me_core]
        keep = pltpu.make_async_copy(packet, mine, own_sem)
        keep.start()
        along = [
            remote(packet, mine, packet_send.at[n], packet_recv.at[n], peer)
            for n, peer in enumerate(line_peers)
        ]
        for copy in along:
            copy.start()

    def columns(piece):
        _, first, wide = pieces[piece]
        return pl.ds(first, wide)

    loads, core_copies, pair_copies, line_copies = {}, {}, {}, {}

    if head_part is not None:
        head_sem, head_send, head_recv = refs[-3:]
        high = head_out.shape[0]

        def shard(n):
            return head_part.at[pl.ds(n * high, high)]

        head_loads = [
            pltpu.make_async_copy(shard(2 * n), head_own.at[n], head_sem.at[n]) for n in range(2)
        ]
        head_copies = [
            remote(shard(2 * n + 1), head_core.at[n], head_send.at[n], head_recv.at[n], core_peer)
            for n in range(2)
        ]
        head_copies.append(
            remote(head_core.at[1], head_section, head_send.at[2], head_recv.at[2], section_peer)
        )

        def head_to_core():
            for copy in head_loads + head_copies[:2]:
                copy.start()

        def head_rows(body):
            @pl.loop(0, high // 16)
            def _(block):
                body(pl.ds(pl.multiple_of(block * 16, 16), 16))

        def head_over_cores():
            for copy in head_loads:
                copy.wait()
            for copy in head_copies[:2]:
                copy.wait_recv()

            def add(rows):
                value = head_core[1, rows, :].astype(f32) + head_own[1, rows, :].astype(f32)
                head_core[1, rows, :] = value.astype(bf16)

            head_rows(add)
            head_copies[2].start()

        def head_over_sections():
            head_copies[2].wait_recv()

            def add(rows):
                head_out[rows, :] = (
                    head_core[0, rows, :].astype(f32)
                    + head_own[0, rows, :].astype(f32)
                    + head_section[rows, :].astype(f32)
                )

            head_rows(add)
            for copy in head_copies:
                copy.wait_send()

    def to_core(piece):
        index = pieces[piece][0]
        cols = columns(piece)
        for turn, side in enumerate((1 - me_pair, me_pair)):
            load = pltpu.make_async_copy(
                parts[index].at[:, side, me_core, :, cols],
                own[index].at[:, side, :, cols],
                load_sem.at[piece, turn],
            )
            load.start()
            loads[piece, turn] = load
            copy = remote(
                parts[index].at[:, side, 1 - me_core, :, cols],
                from_core[index].at[:, side, :, cols],
                core_send.at[piece, turn],
                core_recv.at[piece, turn],
                core_peer,
            )
            copy.start()
            core_copies[piece, turn] = copy

    def tiles(piece, body):
        index, first, wide = pieces[piece]
        rows = shapes[index][-2]
        step = min(wide, 512)

        @pl.loop(0, rows // 16)
        def _(block):
            row = pl.ds(pl.multiple_of(block * 16, 16), 16)
            for col in range(first, first + wide, step):
                body(index, row, pl.ds(col, step))

    def over_cores(piece):
        loads[piece, 0].wait()
        core_copies[piece, 0].wait_recv()
        side = 1 - me_pair

        def add(index, row, cols):
            for place in range(line):
                total = from_core[index][place, side, row, cols].astype(f32) + own[index][
                    place, side, row, cols
                ].astype(f32)
                from_core[index][place, side, row, cols] = total.astype(bf16)

        tiles(piece, add)
        index = pieces[piece][0]
        cols = columns(piece)
        copy = remote(
            from_core[index].at[:, side, :, cols],
            from_pair[index].at[:, :, cols],
            pair_send.at[piece],
            pair_recv.at[piece],
            pair_peer,
        )
        copy.start()
        pair_copies[piece] = copy

    def over_pair(piece):
        loads[piece, 1].wait()
        core_copies[piece, 1].wait_recv()
        pair_copies[piece].wait_recv()

        def add(index, row, cols):
            for place in range(line):
                total = (
                    from_core[index][place, me_pair, row, cols].astype(f32)
                    + own[index][place, me_pair, row, cols].astype(f32)
                    + from_pair[index][place, row, cols].astype(f32)
                )
                from_core[index][place, me_pair, row, cols] = total.astype(bf16)

        tiles(piece, add)
        index = pieces[piece][0]
        cols = columns(piece)
        for n, peer in enumerate(line_peers):
            copy = remote(
                from_core[index].at[line_at[n], me_pair, :, cols],
                from_line[index].at[n, :, cols],
                line_send.at[piece, n],
                line_recv.at[piece, n],
                peer,
            )
            copy.start()
            line_copies[piece, n] = copy

    def over_line(piece):
        for n in range(line - 1):
            line_copies[piece, n].wait_recv()

        def add(index, row, cols):
            total = from_core[index][me_line, me_pair, row, cols].astype(f32)
            for n in range(line - 1):
                total = total + from_line[index][n, row, cols].astype(f32)
            if swap:
                outs[index][me_section, row, cols] = total.astype(outs[index].dtype)
            else:
                outs[index][row, cols] = total.astype(outs[index].dtype)

        tiles(piece, add)

    total = len(pieces)
    lead = 2
    ahead = 2
    for piece in range(min(ahead, total)):
        to_core(piece)

    def first_step(piece):
        if piece + ahead < total:
            to_core(piece + ahead)
        elif piece + ahead == total and head_part is not None:
            head_to_core()
        over_cores(piece)

    for piece in range(min(lead, total)):
        first_step(piece)
    if packet_rows:
        keep.wait()
        for copy in along:
            copy.wait()
        sideways = remote(
            packets.at[:, me_pair, me_core],
            packets.at[:, me_pair, me_core],
            wide_send.at[0],
            wide_recv.at[0],
            pair_peer,
        )
        sideways.start()
    for piece in range(total + 1):
        if piece + lead < total:
            first_step(piece + lead)
        if head_part is not None and piece + lead == total:
            head_over_cores()
        if piece < total:
            over_pair(piece)
        if packet_rows and piece == 1:
            sideways.wait()
            across = remote(
                packets.at[:, :, me_core],
                packets.at[:, :, me_core],
                wide_send.at[1],
                wide_recv.at[1],
                core_peer,
            )
            across.start()
        if piece >= 1:
            over_line(piece - 1)
    if packet_rows:
        across.wait()
    if head_part is not None:
        head_over_sections()
    for copy in list(core_copies.values()) + list(pair_copies.values()) + list(line_copies.values()):
        copy.wait_send()
    if swap:
        swap_send, swap_recv = refs[-2:]
        copy = remote(
            outs[0].at[me_section], outs[0].at[me_section], swap_send, swap_recv, section_peer
        )
        copy.start()
        copy.wait()


def summed_over_dp(parts, splits, collective_id, packet=None, swap=False, head_part=None):
    shapes = [part.shape for part in parts]
    line = shapes[0][0]
    total = len(sum_pieces(shapes, splits))
    packet_rows = 0 if packet is None else packet.shape[0]
    vmem = pl.BlockSpec(memory_space=pltpu.VMEM)
    anywhere = pl.BlockSpec(memory_space=pl.ANY)
    if swap:
        out_shape = [jax.ShapeDtypeStruct((2,) + shapes[0][-2:], bf16)]
    else:
        out_shape = [jax.ShapeDtypeStruct(shape[-2:], f32) for shape in shapes]
    out_specs = [vmem] * len(parts)
    operands = list(parts)
    in_specs = [anywhere] * len(parts)
    dma = pltpu.SemaphoreType.DMA
    scratch = [pltpu.VMEM((line, 2) + shape[-2:], bf16) for shape in shapes]
    scratch += [pltpu.VMEM((line, 2) + shape[-2:], bf16) for shape in shapes]
    scratch += [pltpu.VMEM((line,) + shape[-2:], bf16) for shape in shapes]
    scratch += [pltpu.VMEM((line - 1,) + shape[-2:], bf16) for shape in shapes]
    scratch += [dma((total, 2))] * 3 + [dma((total,))] * 2 + [dma((total, line - 1))] * 2
    if packet_rows:
        operands.append(packet)
        in_specs.append(anywhere)
        out_shape.append(jax.ShapeDtypeStruct((line, 2, 2) + packet.shape, packet.dtype))
        out_specs.append(anywhere)
        scratch += [dma, dma((line - 1,)), dma((line - 1,)), dma((2,)), dma((2,))]
    if head_part is not None:
        high, deep = head_part.shape[0] // 4, head_part.shape[1]
        operands.append(head_part)
        in_specs.append(anywhere)
        out_shape.append(jax.ShapeDtypeStruct((high, deep), f32))
        out_specs.append(vmem)
        scratch += [pltpu.VMEM((2, high, deep), bf16)] * 2 + [pltpu.VMEM((high, deep), bf16)]
        scratch += [dma((2,)), dma((3,)), dma((3,))]
    if swap:
        scratch += [dma, dma]
    return pl.pallas_call(
        partial(sum_kernel, shapes, splits, line, packet_rows, swap, head_part is not None),
        out_shape=out_shape,
        in_specs=in_specs,
        out_specs=out_specs,
        scratch_shapes=scratch,
        compiler_params=pltpu.CompilerParams(
            collective_id=collective_id, has_side_effects=True, vmem_limit_bytes=60 * 2**20
        ),
    )(*operands)


def gather_kernel(line, mine, out, send, recv, own_sem):
    me_line = lax.axis_index("line")
    me_pair = lax.axis_index("pair")
    me_core = lax.axis_index("core")
    peers = []
    for step in range(1, line * 4):
        peers.append(
            {
                "line": lax.rem(me_line + step // 4, line),
                "pair": lax.rem(me_pair + step // 2 % 2, 2),
                "core": lax.rem(me_core + step % 2, 2),
            }
        )
    greet(peers)
    place = out.at[me_line, me_pair, me_core]
    keep = pltpu.make_async_copy(mine, place, own_sem)
    keep.start()
    copies = [remote(mine, place, send.at[n], recv.at[n], peer) for n, peer in enumerate(peers)]
    for copy in copies:
        copy.start()
    keep.wait()
    for copy in copies:
        copy.wait()


def gathered_small(block, line, collective_id):
    count = line * 4 - 1
    vmem = pl.BlockSpec(memory_space=pltpu.VMEM)
    return pl.pallas_call(
        partial(gather_kernel, line),
        out_shape=jax.ShapeDtypeStruct((line, 2, 2) + block.shape, block.dtype),
        in_specs=[vmem],
        out_specs=vmem,
        scratch_shapes=[
            pltpu.SemaphoreType.DMA((count,)),
            pltpu.SemaphoreType.DMA((count,)),
            pltpu.SemaphoreType.DMA,
        ],
        compiler_params=pltpu.CompilerParams(collective_id=collective_id, has_side_effects=True),
    )(block)


def head_kernel(line, head_rows, length, *refs):
    final, targets, *heads = refs[:6]
    out, grads, lse_out, pick_out = refs[6:10]
    (table, rows_all, logits, probs, acc, parts, from_pair, from_line, stats, done) = refs[10:20]
    (head_sem, own_sem, give_send, give_recv, along_send, along_recv, pair_send, pair_recv) = refs[20:28]
    (stat_send, stat_recv, sum_send, sum_recv, line_send, line_recv, back_send, back_recv) = refs[28:]
    half = final.shape[0] // 2
    width = 2 * half
    padded = heads[0].shape[0]
    me_section = lax.axis_index("section")
    me_line = lax.axis_index("line")
    me_pair = lax.axis_index("pair")
    me_core = lax.axis_index("core")
    section_peer = {"section": 1 - me_section}
    pair_peer = {"pair": 1 - me_pair}
    chip_peers = []
    for step in range(1, 2 * line):
        chip_peers.append(
            {"line": lax.rem(me_line + step // 2, line), "pair": lax.rem(me_pair + step % 2, 2)}
        )
    greet(chip_peers + [section_peer])

    def side(pair):
        return pl.ds(pl.multiple_of(pair * half, 16), half)

    loads = [
        pltpu.make_async_copy(part, table.at[pl.ds(n * padded, padded)], head_sem.at[n])
        for n, part in enumerate(heads)
    ]
    for load in loads:
        load.start()

    mine = rows_all.at[me_line, side(me_pair)]
    give = remote(final.at[pl.ds(0, half)], mine, give_send, give_recv, section_peer)

    @pl.when(me_section == 1)
    def _():
        give.start()
        keep = pltpu.make_async_copy(final.at[pl.ds(half, half)], mine, own_sem)
        keep.start()
        keep.wait()

    @pl.when(me_section == 0)
    def _():
        give.wait_recv()

    def column_block(place):
        return rows_all.at[place, side(me_pair)]

    def along(step, way):
        block = column_block(me_line - way * step)
        turn = (way + 1) // 2
        return remote(
            block,
            block,
            along_send.at[turn, step],
            along_recv.at[turn, step],
            {"line": me_line + way},
        )

    def inside(place):
        return (place >= 0) & (place < line)

    def sends_along(step, way):
        return inside(me_line - way * step) & inside(me_line + way)

    def sideways(place):
        block = column_block(place)
        return remote(block, block, pair_send.at[place], pair_recv.at[place], pair_peer)

    def arrived_sideways(place):
        block = rows_all.at[place, side(1 - me_pair)]
        return remote(block, block, pair_send.at[place], pair_recv.at[place], pair_peer)

    for way in (1, -1):

        @pl.when(sends_along(0, way))
        def _():
            along(0, way).start()

    sideways(me_line).start()

    def pass_on(step):
        for way in (1, -1):
            place = me_line - way * step

            @pl.when(inside(place))
            def _():
                block = column_block(place)
                turn = (way + 1) // 2
                remote(
                    block,
                    block,
                    along_send.at[turn, step - 1],
                    along_recv.at[turn, step - 1],
                    {"line": me_line - way},
                ).wait_recv()

                @pl.when(inside(me_line + way))
                def _():
                    along(step, way).start()

                sideways(place).start()

    nearest = []
    for own in range(line):
        near = [own]
        for step in range(1, line):
            near += [place for place in (own - step, own + step) if 0 <= place < line]
        nearest.append(near)

    def by_distance(turn):
        place = 0
        for own in range(line):
            for n in range(line):
                hit = ((me_line == own) & (turn == n)).astype(jnp.int32)
                place = place + hit * nearest[own][n]
        return place

    def vocabulary(tile, rows):
        shard = tile * rows // padded
        first = lax.rem(tile * rows, padded)
        shard_section = lax.rem(me_section + shard // 2, 2)
        shard_core = lax.rem(me_core + lax.rem(shard, 2), 2)
        base = (((shard_section * line + me_line) * 2 + me_pair) * 2 + shard_core) * head_rows
        row = lax.broadcasted_iota(jnp.int32, (rows, 1), 0) + first
        return jnp.where(row < head_rows, row + base, -1)

    tile_rows = 512
    tiles = 4 * padded // tile_rows
    lowest = -1e30

    def score(place):
        tokens = rows_all.at[place]
        wanted = targets[place]

        def one(tile, carry):
            top, pick = carry
            rows = pl.ds(pl.multiple_of(tile * tile_rows, tile_rows), tile_rows)
            entry = vocabulary(tile, tile_rows)
            part = lax.dot_general(
                table[rows, :], tokens[...], (((1,), (1,)), ((), ())), preferred_element_type=f32
            )
            part = jnp.where(entry >= 0, part, lowest)
            logits[rows, :] = part
            top = jnp.maximum(top, jnp.max(part, 0, keepdims=True))
            pick = pick + jnp.sum(jnp.where(entry == wanted, part, 0.0), 0, keepdims=True)
            return top, pick

        start = (jnp.full((1, width), lowest, f32), jnp.zeros((1, width), f32))
        top, pick = lax.fori_loop(0, tiles, one, start)
        pick_out[place] = pick

        def two(tile, total):
            rows = pl.ds(pl.multiple_of(tile * tile_rows, tile_rows), tile_rows)
            value = jnp.exp(logits[rows, :] - top)
            probs[place, rows, :] = value.astype(bf16)
            return total + jnp.sum(value, 0, keepdims=True)

        total = lax.fori_loop(0, tiles, two, jnp.zeros((1, width), f32))
        own = stats.at[me_line, me_pair, place]
        own[0:1, :] = top
        own[1:2, :] = total

    def stat_copy(n, place):
        own = stats.at[me_line, me_pair, place]
        return remote(own, own, stat_send.at[n, place], stat_recv.at[n, place], chip_peers[n])

    def stat_wait(n, place):
        peer = chip_peers[n]
        source_line = lax.rem(2 * me_line + line - peer["line"], line)
        source_pair = peer["pair"]
        block = stats.at[source_line, source_pair, place]
        remote(block, block, stat_send.at[n, place], stat_recv.at[n, place], peer).wait_recv()

    for load in loads:
        load.wait()

    @pl.loop(0, line)
    def _(turn):
        pass_on(turn + 1)
        place = by_distance(turn)
        arrived_sideways(place).wait_recv()
        score(place)
        for n in range(len(chip_peers)):
            stat_copy(n, place).start()

    def sum_copy(turn):
        place = lax.rem(me_line + turn + 1, line)
        return remote(
            parts.at[place, side(1 - me_pair)],
            from_pair.at[turn],
            sum_send.at[turn],
            sum_recv.at[turn],
            pair_peer,
        )

    def line_copy(turn):
        place = lax.rem(me_line + turn + 1, line)
        return remote(
            parts.at[place, side(me_pair)],
            from_line.at[turn],
            line_send.at[turn],
            line_recv.at[turn],
            {"line": place},
        )

    def finish(turn):
        place = lax.rem(me_line + turn + 1, line)
        sum_copy(turn).wait_recv()
        own = parts.at[place, side(me_pair)]

        @pl.loop(0, half // 16)
        def _(block):
            rows = pl.ds(pl.multiple_of(block * 16, 16), 16)
            value = own[rows, :].astype(f32) + from_pair[turn, rows, :].astype(f32)
            own[rows, :] = value.astype(bf16)

    @pl.loop(0, line)
    def _(turn):
        place = lax.rem(me_line + turn + 1, line)
        for n in range(len(chip_peers)):
            stat_wait(n, place)
        tops = [stats[a, b, place, 0:1, :] for a in range(line) for b in range(2)]
        totals = [stats[a, b, place, 1:2, :] for a in range(line) for b in range(2)]
        top = tops[0]
        for value in tops[1:]:
            top = jnp.maximum(top, value)
        total = jnp.zeros_like(top)
        for peak, part in zip(tops, totals):
            total = total + part * jnp.exp(peak - top)
        lse = top + jnp.log(total)
        lse_out[place] = lse
        factor = jnp.exp(stats[me_line, me_pair, place, 0:1, :] - lse) / length
        wanted = targets[place]

        @pl.loop(0, 4)
        def _(tile):
            rows = pl.ds(pl.multiple_of(tile * padded, padded), padded)
            entry = vocabulary(tile, padded)
            grad = probs[place, rows, :].astype(f32) * factor
            grad = (grad - jnp.where(entry == wanted, 1.0 / length, 0.0)).astype(bf16)
            probs[place, rows, :] = grad
            product = lax.dot_general(
                grad, table[rows, :], (((0,), (0,)), ((), ())), preferred_element_type=f32
            )

            @pl.when(tile == 0)
            def _():
                acc[...] = product

            @pl.when((tile > 0) & (tile < 3))
            def _():
                acc[...] += product

            @pl.when(tile == 3)
            def _():
                parts[place] = (acc[...] + product).astype(bf16)

        sum_copy(turn).start()

        @pl.when(turn > 0)
        def _():
            finish(turn - 1)
            line_copy(turn - 1).start()

    gh_rows = 256
    gh_tiles = 4 * padded // gh_rows

    def head_grads(first, last):
        @pl.loop(first, last)
        def _(tile):
            rows = pl.ds(pl.multiple_of(tile * gh_rows, gh_rows), gh_rows)
            value = jnp.zeros((gh_rows, table.shape[1]), f32)
            for place in range(line):
                value = value + jnp.dot(
                    probs[place, rows, :], rows_all[place], preferred_element_type=f32
                )
            grads[rows, :] = value.astype(bf16)

    head_grads(0, gh_tiles // 2)
    finish(line - 1)
    for turn in range(line - 1):
        line_copy(turn).wait_recv()
    own = parts.at[me_line, side(me_pair)]

    @pl.loop(0, half // 16)
    def _(block):
        rows = pl.ds(pl.multiple_of(block * 16, 16), 16)
        value = own[rows, :].astype(f32)
        for turn in range(line - 1):
            value = value + from_line[turn, rows, :].astype(f32)
        done[rows, :] = value.astype(bf16)

    back = remote(done, out.at[pl.ds(0, half)], back_send, back_recv, section_peer)

    @pl.when(me_section == 0)
    def _():
        back.start()
        out[...] = jnp.zeros_like(out)

    @pl.when(me_section == 1)
    def _():
        out[pl.ds(half, half), :] = done[...]

    head_grads(gh_tiles // 2, gh_tiles)

    @pl.when(me_section == 0)
    def _():
        back.wait_send()

    @pl.when(me_section == 1)
    def _():
        back.wait_recv()
        give.wait_send()

    for way in (1, -1):
        for step in range(line - 1):

            @pl.when(sends_along(step, way))
            def _():
                along(step, way).wait_send()

    for place in range(line):
        sideways(place).wait_send()
        for n in range(len(chip_peers)):
            stat_copy(n, place).wait_send()
    for turn in range(line):
        sum_copy(turn).wait_send()
    for turn in range(line - 1):
        line_copy(turn).wait_send()


def head_pass(final, targets, heads, line, head_rows, length, collective_id):
    tokens, deep = final.shape
    half = tokens // 2
    padded = heads[0].shape[0]
    vmem = pl.BlockSpec(memory_space=pltpu.VMEM)
    anywhere = pl.BlockSpec(memory_space=pl.ANY)
    dma = pltpu.SemaphoreType.DMA
    peers = 2 * line - 1
    return pl.pallas_call(
        partial(head_kernel, line, head_rows, length),
        out_shape=[
            jax.ShapeDtypeStruct((tokens, deep), bf16),
            jax.ShapeDtypeStruct((4 * padded, deep), bf16),
            jax.ShapeDtypeStruct((line, 1, tokens), f32),
            jax.ShapeDtypeStruct((line, 1, tokens), f32),
        ],
        in_specs=[vmem, vmem] + [anywhere] * 4,
        out_specs=[vmem] * 4,
        scratch_shapes=[
            pltpu.VMEM((4 * padded, deep), bf16),
            pltpu.VMEM((line, tokens, deep), bf16),
            pltpu.VMEM((4 * padded, tokens), f32),
            pltpu.VMEM((line, 4 * padded, tokens), bf16),
            pltpu.VMEM((tokens, deep), f32),
            pltpu.VMEM((line, tokens, deep), bf16),
            pltpu.VMEM((line, half, deep), bf16),
            pltpu.VMEM((line - 1, half, deep), bf16),
            pltpu.VMEM((line, 2, line, 8, tokens), f32),
            pltpu.VMEM((half, deep), bf16),
            dma((4,)),
            dma,
            dma,
            dma,
            dma((2, line)),
            dma((2, line)),
            dma((line,)),
            dma((line,)),
            dma((peers, line)),
            dma((peers, line)),
            dma((line,)),
            dma((line,)),
            dma((line,)),
            dma((line,)),
            dma,
            dma,
        ],
        compiler_params=pltpu.CompilerParams(
            collective_id=collective_id, has_side_effects=True, vmem_limit_bytes=60 * 2**20
        ),
    )(final, targets, *heads)


def norm_rows(values):
    centred = values - jnp.mean(values, -1, keepdims=True)
    factor = lax.rsqrt(jnp.mean(centred * centred, -1, keepdims=True) + epsilon)
    return (centred * factor, factor)


def norm_back(gradient, normed, factor):
    return factor * (
        gradient
        - jnp.mean(gradient, -1, keepdims=True)
        - normed * jnp.mean(gradient * normed, -1, keepdims=True)
    )


def time_features(noise_level):
    half_width = TFEAT // 2
    rates = jnp.exp(jnp.arange(half_width, dtype=f32) * (math.log(1000.0) / half_width))
    angles = (jnp.log(noise_level) / 4.0)[:, None] * rates[None, :]
    return jnp.concatenate([jnp.cos(angles), jnp.sin(angles)], -1)


def levels_of(bins, table):
    hits = bins[:, None] == jnp.arange(table.shape[0])[None, :]
    return jnp.sum(jnp.where(hits, table[None, :], 0.0), -1)


def over_dp(part):
    part = part.reshape((part.shape[0] // 4, 2, 2) + part.shape[1:])
    part = lax.psum_scatter(part, "core", scatter_dimension=2)
    part = lax.psum_scatter(part, "pair", scatter_dimension=1)
    return lax.psum_scatter(part, "line", scatter_dimension=0)


def by_owner(part):
    line = lax.axis_size("line")
    return part.astype(bf16).reshape((line, 2, 2, part.shape[0] // (line * 4)) + part.shape[1:])


def mm(spec, left, right):
    return jnp.einsum(spec, left, right, preferred_element_type=f32)


def layer_forward(stream, scale_attn, scale_mlp, weights):
    w_qkv, w_out, w_up, b_hidden, w_down = weights
    seq_count, length, model_width = stream.shape
    normed_attn, factor_attn = norm_rows(stream)
    attn_entry = (normed_attn * scale_attn).astype(bf16)
    joined = mm("nsd,de->nse", attn_entry, w_qkv).astype(bf16)
    qkv_parts = joined.reshape(seq_count, length, 3, HEADS, HEAD_DIM)
    query_rows = qkv_parts[:, :, 0]
    key_rows = qkv_parts[:, :, 1]
    value_rows = qkv_parts[:, :, 2]
    scores = mm("nqhe,nkhe->nhqk", query_rows, key_rows) / math.sqrt(HEAD_DIM)
    exp_scores = jnp.exp(scores - jnp.max(scores, -1, keepdims=True))
    attn_probs = exp_scores / jnp.sum(exp_scores, -1, keepdims=True)
    probs_low = attn_probs.astype(bf16)
    attn_mixed = mm("nhqk,nkhe->nqhe", probs_low, value_rows).astype(bf16)
    attn_mixed = attn_mixed.reshape(seq_count, length, model_width)
    middle = stream + mm("nsd,de->nse", attn_mixed, w_out)
    normed_mlp, factor_mlp = norm_rows(middle)
    mlp_entry = (normed_mlp * scale_mlp).astype(bf16)
    up_proj = mm("nsd,df->nsf", mlp_entry, w_up) + b_hidden
    hidden = jax.nn.gelu(up_proj, approximate=False).astype(bf16)
    block_out = middle + mm("nsf,fd->nsd", hidden, w_down)
    kept = (
        normed_attn,
        factor_attn,
        attn_entry,
        query_rows,
        key_rows,
        value_rows,
        attn_probs,
        probs_low,
        attn_mixed,
        normed_mlp,
        factor_mlp,
        mlp_entry,
        up_proj,
        hidden,
    )
    return (block_out, kept)


def layer_backward(grad_out, kept, scale_attn, scale_mlp, weights, whole):
    w_qkv, w_out, w_up, b_hidden, w_down = weights
    (
        normed_attn,
        factor_attn,
        attn_entry,
        query_rows,
        key_rows,
        value_rows,
        attn_probs,
        probs_low,
        attn_mixed,
        normed_mlp,
        factor_mlp,
        mlp_entry,
        up_proj,
        hidden,
    ) = kept
    seq_count, length, model_width = grad_out.shape
    grads = {}
    grad_branch = grad_out.astype(bf16)
    if whole:
        grads["down"] = by_owner(mm("nsf,nsd->fd", hidden, grad_branch))
    grad_hidden = mm("nsd,fd->nsf", grad_branch, w_down)
    _, gelu_pull = jax.vjp(partial(jax.nn.gelu, approximate=False), up_proj)
    grad_up_proj = gelu_pull(grad_hidden)[0].astype(bf16)
    if whole:
        grads["bias"] = jnp.sum(grad_up_proj.astype(f32), (0, 1))
        grads["up"] = by_owner(mm("nsd,nsf->df", mlp_entry, grad_up_proj))
    grad_entry = mm("nsf,df->nsd", grad_up_proj, w_up)
    grad_middle = grad_out + norm_back(grad_entry * scale_mlp, normed_mlp, factor_mlp)
    grad_attn = grad_middle.astype(bf16)
    if whole:
        grads["out"] = by_owner(mm("nsd,nse->de", attn_mixed, grad_attn))
    grad_mixed = mm("nse,de->nsd", grad_attn, w_out)
    grad_mixed = grad_mixed.astype(bf16).reshape(seq_count, length, HEADS, HEAD_DIM)
    grad_probs = mm("nqhe,nkhe->nhqk", grad_mixed, value_rows)
    grad_values = mm("nhqk,nqhe->nkhe", probs_low, grad_mixed)
    grad_scores = (
        attn_probs * (grad_probs - jnp.sum(grad_probs * attn_probs, -1, keepdims=True))
    ).astype(bf16)
    grad_query = mm("nhqk,nkhe->nqhe", grad_scores, key_rows) / math.sqrt(HEAD_DIM)
    grad_keys = mm("nhqk,nqhe->nkhe", grad_scores, query_rows) / math.sqrt(HEAD_DIM)
    grad_joined = jnp.stack([grad_query, grad_keys, grad_values], 2).astype(bf16)
    grad_joined = grad_joined.reshape(seq_count, length, 3 * model_width)
    if whole:
        grads["qkv"] = by_owner(mm("nsd,nse->de", attn_entry, grad_joined))
    grad_attn_entry = mm("nse,de->nsd", grad_joined, w_qkv)
    grad_stream = grad_middle + norm_back(grad_attn_entry * scale_attn, normed_attn, factor_attn)
    if whole:
        grads["cond"] = jnp.concatenate(
            [jnp.sum(grad_attn_entry * normed_attn, 1), jnp.sum(grad_entry * normed_mlp, 1)], -1
        )
    return (grad_stream, grads)


def local(
    token_ids,
    target_ids,
    time_bins,
    sigma_table,
    noise,
    embed,
    w_in,
    w_time,
    norm_gain,
    w_qkv,
    w_out,
    w_up,
    b_hidden,
    w_down,
    out_gain,
    head,
):
    section = lax.axis_index("section")
    line_at = lax.axis_index("line")
    pair_at = lax.axis_index("pair")
    core = lax.axis_index("core")
    sections = lax.axis_size("section")
    line = lax.axis_size("line")
    chip = line_at * 2 + pair_at
    chips = line * 2
    cores = 2
    dp_count = chips * cores
    dp_index = chip * cores + core
    is_first = section == 0
    seqs, length = token_ids.shape
    tokens = seqs * length
    half = tokens // sections
    model_width = w_out.shape[-1]
    emb_rows, emb_width = embed.shape
    straight = line <= 4 and half % 16 == 0 and model_width // dp_count % 16 == 0

    own_ids = jnp.concatenate([token_ids.reshape(-1), target_ids.reshape(-1), time_bins])
    if straight:
        padded = jnp.pad(own_ids, (0, -own_ids.shape[0] % 1024)).reshape(-1, 128)
        all_ids = gathered_small(padded, line, 0).reshape(dp_count, -1)[:, : own_ids.shape[0]]
    else:
        all_ids = lax.all_gather(own_ids, DP)
    all_tokens = all_ids[:, :tokens]
    all_targets = all_ids[:, tokens : 2 * tokens]
    all_bins = all_ids[:, 2 * tokens :].reshape(-1)

    own_rows = dp_index * emb_rows + jnp.arange(emb_rows)
    half_tokens = lax.dynamic_slice_in_dim(all_tokens, section * half, half, 1)
    picked = (half_tokens.reshape(-1)[:, None] == own_rows[None, :]).astype(bf16)
    found = jnp.dot(picked, embed, preferred_element_type=f32).astype(bf16)
    if straight:
        found = found.reshape(line, 2, 2, half, emb_width)
        (embedded,) = summed_over_dp([found], [2], 1, swap=True)
    else:
        embedded = lax.all_gather(over_dp(found.reshape(dp_count, half, emb_width)), "section")
    embedded = embedded.astype(f32).reshape(seqs, length, emb_width)

    head_rows = head.shape[0]
    swapped = [(0, 1), (1, 0)]
    if straight:
        head_own = jnp.pad(head, ((0, -head_rows % 512), (0, 0)))
        head_core = lax.ppermute(head_own, "core", swapped)
        head_section = lax.ppermute(head_own, "section", swapped)
        heads = [head_own, head_core, head_section, lax.ppermute(head_section, "core", swapped)]
    else:
        head_group = lax.all_gather(lax.all_gather(head, "core"), "section")
        head_group = head_group.reshape(-1, model_width)
        vocab_base = (
            (jnp.arange(sections)[:, None] * chips + chip) * cores + jnp.arange(cores)[None, :]
        ) * head_rows
        columns = (vocab_base[:, :, None] + jnp.arange(head_rows)[None, None, :]).reshape(-1)

    noise_level = levels_of(time_bins, sigma_table)
    unit_factor = lax.rsqrt(jnp.mean(embedded * embedded, -1, keepdims=True) + epsilon)
    level_col = noise_level[:, None, None]
    noise_scale = lax.rsqrt(level_col * level_col + 1.0)
    noisy_rows = ((embedded * unit_factor + level_col * noise) * noise_scale).astype(bf16)
    time_feats = time_features(noise_level)
    conditioned = jnp.dot(time_feats, w_time[0].astype(f32), precision=highest) + norm_gain[0]
    scale_attn = conditioned[:, None, :model_width]
    scale_mlp = conditioned[:, None, model_width:]
    weights = (w_qkv[0], w_out[0], w_up[0], b_hidden[0], w_down[0])

    stream0 = mm("nse,ed->nsd", noisy_rows, w_in)
    first_out, _ = layer_forward(stream0, scale_attn, scale_mlp, weights)
    arrived = lax.ppermute(first_out.astype(bf16), "section", swapped)
    stream = jnp.where(is_first, stream0, arrived.astype(f32))
    block_out, kept = layer_forward(stream, scale_attn, scale_mlp, weights)

    top_stream = block_out.astype(bf16).astype(f32)
    final_normed, final_factor = norm_rows(top_stream)
    final_rows = (final_normed * out_gain).astype(bf16).reshape(tokens, model_width)
    targets_group = lax.dynamic_slice_in_dim(
        all_targets.reshape(chips, cores, tokens), core, 1, 1
    )[:, 0]
    targets_group = lax.dynamic_slice_in_dim(targets_group, section * half, half, 1)
    if straight:
        grad_final, grad_head, lse, picks = head_pass(
            final_rows, targets_group.reshape(line, 1, tokens), heads, line, head_rows, length, 3
        )
        ce_part = jnp.sum(lse) / chips - jnp.sum(picks)
    else:
        targets_group = targets_group.reshape(-1)
        handed = lax.ppermute(final_rows[:half], "section", [(1, 0), (0, 1)])
        own_final = jnp.where(is_first, handed, final_rows[half:])
        group_final = lax.all_gather(own_final, ("line", "pair"), tiled=True)
        logits = mm("td,vd->tv", group_final, head_group)
        local_top = jnp.max(logits, -1)
        local_total = jnp.sum(jnp.exp(logits - local_top[:, None]), -1)
        mark = columns[None, :] == targets_group[:, None]
        local_pick = jnp.sum(jnp.where(mark, logits, 0.0))
        stats = lax.all_gather(jnp.stack([local_top, local_total]), ("line", "pair"))
        all_top = jnp.max(stats[:, 0], 0)
        all_total = jnp.sum(stats[:, 1] * jnp.exp(stats[:, 0] - all_top), 0)
        log_total = all_top + jnp.log(all_total)
        soft_rows = jnp.exp(logits - log_total[:, None])
        logit_grads = ((soft_rows - jnp.where(mark, 1.0, 0.0)) / length).astype(bf16)
        grad_final = jnp.dot(logit_grads, head_group, preferred_element_type=f32).astype(bf16)
        grad_final = lax.psum_scatter(grad_final, ("line", "pair"), scatter_dimension=0, tiled=True)
        handed = lax.ppermute(grad_final, "section", swapped)
        grad_final = jnp.concatenate([handed, grad_final], 0)
        grad_head = mm("tv,td->vd", logit_grads, group_final).astype(bf16)
        grad_head = grad_head.reshape(sections, cores, head_rows, model_width)
        grad_head = lax.psum_scatter(grad_head, "core", scatter_dimension=1)
        grad_head = lax.psum_scatter(grad_head, "section", scatter_dimension=0).astype(f32)

        ce_part = jnp.sum(log_total) / chips - local_pick
    grad_final = grad_final.astype(f32).reshape(seqs, length, model_width)
    out_part = jnp.where(is_first, 0.0, jnp.sum(grad_final * final_normed, (0, 1)))

    grad_top = norm_back(grad_final * out_gain, final_normed, final_factor)
    grad_second, _ = layer_backward(grad_top, kept, scale_attn, scale_mlp, weights, False)
    returned = lax.ppermute(grad_second.astype(bf16), "section", swapped)
    grad_cot = jnp.where(is_first, returned.astype(f32), grad_top)
    grad_stream, grads = layer_backward(grad_cot, kept, scale_attn, scale_mlp, weights, True)
    grad_first = grad_stream.astype(bf16)

    in_part = mm("nse,nsd->ed", noisy_rows, grad_first).astype(bf16)
    in_part = in_part.reshape(sections, line, 2, 2, -1, model_width)
    in_part = jnp.moveaxis(in_part, 0, 3).reshape(line, 2, 2, -1, model_width)
    grad_noisy = mm("nsd,ed->nse", grad_first, w_in)
    grad_unit = grad_noisy * noise_scale
    cubed = unit_factor * unit_factor * unit_factor
    grad_embedded = unit_factor * grad_unit - cubed * embedded * jnp.mean(
        grad_unit * embedded, -1, keepdims=True
    )
    grad_flat = grad_embedded.reshape(tokens, emb_width)

    ce_high = ce_part.astype(bf16).astype(f32)
    ce_mid = (ce_part - ce_high).astype(bf16).astype(f32)
    ce_low = ce_part - ce_high - ce_mid
    shared = jnp.concatenate([out_part, jnp.stack([ce_high, ce_mid, ce_low])])
    shared_rows = -(-shared.shape[0] // emb_width)
    shared = jnp.pad(shared, (0, shared_rows * emb_width - shared.shape[0]))
    handing = jnp.concatenate([grad_flat, shared.reshape(-1, emb_width)], 0).astype(bf16)
    handed = lax.ppermute(handing, "section", swapped)
    kept_rows = jnp.where(is_first, handing[:tokens], handed[:tokens])
    layer_small = jnp.concatenate([grads["cond"].reshape(-1), grads["bias"]])
    layer_rows = layer_small.shape[0] // emb_width
    packet = jnp.concatenate(
        [
            kept_rows,
            layer_small.astype(bf16).reshape(layer_rows, emb_width),
            handing[tokens:],
            handed[tokens:],
        ],
        0,
    )
    packet = jnp.pad(packet, ((0, -packet.shape[0] % 16), (0, 0)))
    parts = [grads["down"], grads["up"], grads["qkv"], grads["out"], in_part]
    if straight:
        *sums, packets, grad_head = summed_over_dp(
            parts, [2, 2, 2, 1, 1], 2, packet=packet, head_part=grad_head
        )
        grad_head = grad_head[:head_rows]
        packets = packets.reshape((dp_count,) + packet.shape)
    else:
        sums = [over_dp(part.reshape((dp_count,) + part.shape[3:])).astype(f32) for part in parts]
        packets = lax.all_gather(packet, DP)
    grad_down, grad_up, grad_qkv, grad_wout, in_sum = sums
    in_sum = in_sum.reshape(sections, -1, model_width)
    in_handed = lax.ppermute(in_sum[1], "section", swapped)
    grad_w_in = jnp.where(is_first, in_sum[0], in_handed)

    grad_all = packets[:, :tokens].reshape(-1, emb_width)
    out_rows = emb_rows // sections
    target_rows = (section * dp_count + dp_index) * out_rows + jnp.arange(out_rows)
    place = (target_rows[:, None] == all_tokens.reshape(-1)[None, :]).astype(bf16)
    grad_embed = jnp.dot(place, grad_all, preferred_element_type=f32)

    small = packets[:, tokens : tokens + layer_rows].astype(f32).reshape(dp_count, -1)
    cond_size = grads["cond"].size
    cond_all = small[:, :cond_size].reshape(dp_count * seqs, 2 * model_width)
    hidden_rows = grads["bias"].shape[0] // dp_count
    grad_bias = jnp.sum(
        lax.dynamic_slice_in_dim(small, cond_size + dp_index * hidden_rows, hidden_rows, 1), 0
    )
    norm_cols = 2 * model_width // dp_count
    grad_gain = jnp.sum(lax.dynamic_slice_in_dim(cond_all, dp_index * norm_cols, norm_cols, 1), 0)
    feats_all = time_features(levels_of(all_bins, sigma_table))
    feat_rows = TFEAT // dp_count
    feats_own = lax.dynamic_slice_in_dim(feats_all, dp_index * feat_rows, feat_rows, 1)
    grad_time = jnp.dot(feats_own.T, cond_all, precision=highest)
    both = packets[:, tokens + layer_rows : tokens + layer_rows + 2 * shared_rows].astype(f32)
    both = jnp.sum(both.reshape(dp_count, 2, -1), (0, 1))
    loss = jnp.sum(both[model_width : model_width + 3]) / (tokens * dp_count)
    gain_rows = model_width // dp_count
    grad_out_gain = lax.dynamic_slice_in_dim(both, dp_index * gain_rows, gain_rows)
    return (
        loss,
        grad_embed,
        grad_w_in,
        grad_time[None],
        grad_gain[None],
        grad_qkv[None],
        grad_wout[None],
        grad_up[None],
        grad_bias[None],
        grad_down[None],
        grad_out_gain,
        grad_head,
    )


def solution(mesh):
    sections, dp_count = mesh.shape["section"], mesh.shape["dp"]
    fine = Mesh(mesh.devices.reshape(sections, dp_count // 4, 2, 2), ("section",) + DP)
    everywhere = ("section",) + DP
    in_specs = (
        P(DP, None),
        P(DP, None),
        P(DP),
        P(),
        P(DP, None, None),
        P(DP, None),
        P(),
        P("section", None, None),
        P("section", None),
        P("section", None, None),
        P("section", None, None),
        P("section", None, None),
        P("section", None),
        P("section", None, None),
        P(),
        P(everywhere, None),
    )
    out_specs = (
        P(),
        P(everywhere, None),
        P(everywhere, None),
        P("section", DP, None),
        P("section", DP),
        P("section", DP, None),
        P("section", DP, None),
        P("section", DP, None),
        P("section", DP),
        P("section", DP, None),
        P(DP),
        P(everywhere, None),
    )
    return jax.shard_map(local, mesh=fine, in_specs=in_specs, out_specs=out_specs, check_vma=False)
```

```python
from functools import partial
import math

import jax
import jax.numpy as jnp
from jax import lax
from jax.experimental import pallas as pl
from jax.experimental.pallas import tpu as pltpu
from jax.sharding import Mesh, PartitionSpec as P

HEADS = 16
HEAD_DIM = 64
TFEAT = 256

epsilon = 1e-05
highest = lax.Precision.HIGHEST
f32 = jnp.float32
bf16 = jnp.bfloat16
DP = ("line", "pair", "core")


MESH = pl.DeviceIdType.MESH


def greet(peers):
    barrier = pltpu.get_barrier_semaphore()
    for peer in peers:
        pl.semaphore_signal(barrier, inc=1, device_id=peer, device_id_type=MESH)
    pl.semaphore_wait(barrier, len(peers))


def remote(source, target, send, recv, peer):
    return pltpu.make_async_remote_copy(
        src_ref=source,
        dst_ref=target,
        send_sem=send,
        recv_sem=recv,
        device_id=peer,
        device_id_type=MESH,
    )


def ring_place(position, line):
    turned = position // line
    return position * (1 - turned) + (2 * line - 1 - position) * turned, turned


def sum_kernel(shapes, line, with_packet, with_head, swap, *refs):
    count = len(shapes)
    refs = list(refs)

    def take(number):
        return [refs.pop(0) for _ in range(number)]

    parts = take(count)
    packet = take(1)[0] if with_packet else None
    head_part = take(1)[0] if with_head else None
    outs = take(count)
    packets = take(1)[0] if with_packet else None
    head_out = take(1)[0] if with_head else None
    own, from_core, slots = take(count), take(count), take(count)
    load_sem, core_send, core_recv, ring_send, ring_recv = take(5)
    if with_packet:
        own_sem, packet_send, packet_recv, wide_send, wide_recv = take(5)
    if with_head:
        head_own, head_core, head_section, head_sem, head_send, head_recv = take(6)
    if swap:
        swap_send, swap_recv = take(2)

    chips = 2 * line
    me_section = lax.axis_index("section")
    me_line = lax.axis_index("line")
    me_pair = lax.axis_index("pair")
    me_core = lax.axis_index("core")
    position = me_line + me_pair * (chips - 1 - 2 * me_line)
    section_peer = {"section": 1 - me_section}
    core_peer = {"core": 1 - me_core}
    ways = (1, -1)
    ring_peers = []
    for way in ways:
        peer_line, peer_pair = ring_place(lax.rem(position + way + chips, chips), line)
        ring_peers.append({"line": peer_line, "pair": peer_pair})
    greet([core_peer] + ring_peers + ([section_peer] if swap or with_head else []))

    def block_of(turn, step):
        ahead = lax.rem(position - ways[turn] * (1 + step) + 2 * chips, chips)
        return ring_place(ahead, line)

    def columns(index, turn):
        wide = shapes[index][-1] // 2
        return pl.ds(turn * wide, wide)

    def load(index, turn, step):
        place, pair = block_of(turn, step)
        cols = columns(index, turn)
        return pltpu.make_async_copy(
            parts[index].at[place, pair, me_core, :, cols],
            own[index].at[step, :, cols],
            load_sem.at[index, turn, step],
        )

    def core_copy(index, turn, step):
        place, pair = block_of(turn, step)
        cols = columns(index, turn)
        return remote(
            parts[index].at[place, pair, 1 - me_core, :, cols],
            from_core[index].at[step, :, cols],
            core_send.at[index, turn, step],
            core_recv.at[index, turn, step],
            core_peer,
        )

    def ring_copy(index, turn, step):
        cols = columns(index, turn)
        if isinstance(step, int) and step == 0:
            source = from_core[index].at[0, :, cols]
        else:
            source = slots[index].at[step - 1, :, cols]
        return remote(
            source,
            slots[index].at[step, :, cols],
            ring_send.at[index, turn, step],
            ring_recv.at[index, turn, step],
            ring_peers[turn],
        )

    def to_core(step):
        for index in range(count):
            for turn in range(2):
                load(index, turn, step).start()
                core_copy(index, turn, step).start()

    def stop(step):
        first = isinstance(step, int) and step == 0
        last = isinstance(step, int) and step == chips - 1
        for index in range(count):
            rows = shapes[index][-2]
            wide = shapes[index][-1] // 2
            tile = min(wide, 512)
            for turn in range(2):
                load(index, turn, step).wait()
                core_copy(index, turn, step).wait_recv()
                if not first:
                    ring_copy(index, turn, step - 1).wait_recv()

                @pl.loop(0, rows // 16)
                def _(block):
                    row = pl.ds(pl.multiple_of(block * 16, 16), 16)
                    for col in range(turn * wide, (turn + 1) * wide, tile):
                        cols = pl.ds(col, tile)
                        total = from_core[index][step, row, cols].astype(f32)
                        total = total + own[index][step, row, cols].astype(f32)
                        if not first:
                            total = total + slots[index][step - 1, row, cols].astype(f32)
                        if last and swap:
                            outs[index][me_section, row, cols] = total.astype(outs[index].dtype)
                        elif last:
                            outs[index][row, cols] = total.astype(outs[index].dtype)
                        elif first:
                            from_core[index][0, row, cols] = total.astype(bf16)
                        else:
                            slots[index][step - 1, row, cols] = total.astype(bf16)

                if not last:
                    ring_copy(index, turn, step).start()

    hops = (line, line - 1)

    def packet_copy(turn, hop):
        place, pair = ring_place(lax.rem(position - ways[turn] * hop + 2 * chips, chips), line)
        block = packets.at[place, pair, me_core]
        return remote(
            block, block, packet_send.at[turn, hop], packet_recv.at[turn, hop], ring_peers[turn]
        )

    def packet_arrived(turn, hop):
        place, pair = ring_place(lax.rem(position - ways[turn] * (hop + 1) + 2 * chips, chips), line)
        block = packets.at[place, pair, me_core]
        return remote(
            block, block, packet_send.at[turn, hop], packet_recv.at[turn, hop], ring_peers[turn]
        )

    def pass_packets(hop):
        for turn in range(2):
            if 0 < hop <= hops[turn]:
                packet_arrived(turn, hop - 1).wait_recv()
            if hop < hops[turn]:
                packet_copy(turn, hop).start()

    if with_packet:
        keep = pltpu.make_async_copy(packet, packets.at[me_line, me_pair, me_core], own_sem)
        keep.start()
        across = remote(
            packets.at[:, :, me_core],
            packets.at[:, :, me_core],
            wide_send,
            wide_recv,
            core_peer,
        )

    if with_head:
        high = head_part.shape[0] // 4

        def shard(n):
            return head_part.at[pl.ds(n * high, high)]

        head_loads = [
            pltpu.make_async_copy(shard(2 * n), head_own.at[n], head_sem.at[n]) for n in range(2)
        ]
        head_copies = [
            remote(shard(2 * n + 1), head_core.at[n], head_send.at[n], head_recv.at[n], core_peer)
            for n in range(2)
        ]
        head_copies.append(
            remote(head_core.at[1], head_section, head_send.at[2], head_recv.at[2], section_peer)
        )

        def head_rows(body):
            @pl.loop(0, high // 16)
            def _(block):
                body(pl.ds(pl.multiple_of(block * 16, 16), 16))

        def head_over_cores():
            for copy in head_loads:
                copy.wait()
            for copy in head_copies[:2]:
                copy.wait_recv()

            def add(rows):
                value = head_core[1, rows, :].astype(f32) + head_own[1, rows, :].astype(f32)
                head_core[1, rows, :] = value.astype(bf16)

            head_rows(add)
            head_copies[2].start()

        def head_over_sections():
            head_copies[2].wait_recv()

            def total(rows):
                return (
                    head_core[0, rows, :].astype(f32)
                    + head_own[0, rows, :].astype(f32)
                    + head_section[rows, :].astype(f32)
                )

            whole = head_out.shape[0] // 16
            rest = head_out.shape[0] % 16

            @pl.loop(0, whole)
            def _(block):
                rows = pl.ds(pl.multiple_of(block * 16, 16), 16)
                head_out[rows, :] = total(rows)

            if rest:
                value = total(pl.ds(whole * 16, 16))
                head_out[pl.ds(whole * 16, rest), :] = value[:rest]

    to_core(0)
    to_core(1)
    stop(0)
    if with_packet:
        keep.wait()
        pass_packets(0)
    for step in range(1, chips - 1):
        to_core(step + 1)
        if with_head and step == 1:
            for copy in head_loads + head_copies[:2]:
                copy.start()
        stop(step)
        if with_packet and step <= line:
            pass_packets(step)
            if step == line:
                across.start()
        if with_head and step == 2:
            head_over_cores()
    stop(chips - 1)
    if swap:
        give = remote(
            outs[0].at[me_section], outs[0].at[me_section], swap_send, swap_recv, section_peer
        )
        give.start()
    if with_head:
        head_over_sections()
        for copy in head_copies:
            copy.wait_send()
    if with_packet:
        across.wait()
        for turn in range(2):
            for hop in range(hops[turn]):
                packet_copy(turn, hop).wait_send()
    for index in range(count):
        for turn in range(2):
            for step in range(chips):
                core_copy(index, turn, step).wait_send()
                if step < chips - 1:
                    ring_copy(index, turn, step).wait_send()
    if swap:
        give.wait()


def summed_over_dp(parts, collective_id, packet=None, head_part=None, head_rows=0, swap=False):
    shapes = [part.shape for part in parts]
    line = shapes[0][0]
    chips = 2 * line
    count = len(parts)
    vmem = pl.BlockSpec(memory_space=pltpu.VMEM)
    anywhere = pl.BlockSpec(memory_space=pl.ANY)
    if swap:
        out_shape = [jax.ShapeDtypeStruct((2,) + shapes[0][-2:], bf16)]
    else:
        out_shape = [jax.ShapeDtypeStruct(shape[-2:], f32) for shape in shapes]
    out_specs = [vmem] * count
    operands = list(parts)
    dma = pltpu.SemaphoreType.DMA
    scratch = [pltpu.VMEM((chips,) + shape[-2:], bf16) for shape in shapes]
    scratch += [pltpu.VMEM((chips,) + shape[-2:], bf16) for shape in shapes]
    scratch += [pltpu.VMEM((chips - 1,) + shape[-2:], bf16) for shape in shapes]
    scratch += [dma((count, 2, chips))] * 3 + [dma((count, 2, chips - 1))] * 2
    if packet is not None:
        operands.append(packet)
        out_shape.append(jax.ShapeDtypeStruct((line, 2, 2) + packet.shape, packet.dtype))
        out_specs.append(anywhere)
        scratch += [dma, dma((2, line)), dma((2, line)), dma, dma]
    if head_part is not None:
        high, deep = head_part.shape[0] // 4, head_part.shape[1]
        operands.append(head_part)
        out_shape.append(jax.ShapeDtypeStruct((head_rows, deep), f32))
        out_specs.append(vmem)
        scratch += [pltpu.VMEM((2, high, deep), bf16)] * 2 + [pltpu.VMEM((high, deep), bf16)]
        scratch += [dma((2,)), dma((3,)), dma((3,))]
    if swap:
        scratch += [dma, dma]
    return pl.pallas_call(
        partial(sum_kernel, shapes, line, packet is not None, head_part is not None, swap),
        out_shape=out_shape,
        in_specs=[anywhere] * len(operands),
        out_specs=out_specs,
        scratch_shapes=scratch,
        compiler_params=pltpu.CompilerParams(
            collective_id=collective_id, has_side_effects=True, vmem_limit_bytes=60 * 2**20
        ),
    )(*operands)


def gather_kernel(line, mine, out, send, recv, own_sem):
    me_line = lax.axis_index("line")
    me_pair = lax.axis_index("pair")
    me_core = lax.axis_index("core")
    peers = []
    for step in range(1, line * 4):
        peers.append(
            {
                "line": lax.rem(me_line + step // 4, line),
                "pair": lax.rem(me_pair + step // 2 % 2, 2),
                "core": lax.rem(me_core + step % 2, 2),
            }
        )
    greet(peers)
    place = out.at[me_line, me_pair, me_core]
    keep = pltpu.make_async_copy(mine, place, own_sem)
    keep.start()
    copies = [remote(mine, place, send.at[n], recv.at[n], peer) for n, peer in enumerate(peers)]
    for copy in copies:
        copy.start()
    keep.wait()
    for copy in copies:
        copy.wait()


def gathered_small(block, line, collective_id):
    count = line * 4 - 1
    vmem = pl.BlockSpec(memory_space=pltpu.VMEM)
    return pl.pallas_call(
        partial(gather_kernel, line),
        out_shape=jax.ShapeDtypeStruct((line, 2, 2) + block.shape, block.dtype),
        in_specs=[vmem],
        out_specs=vmem,
        scratch_shapes=[
            pltpu.SemaphoreType.DMA((count,)),
            pltpu.SemaphoreType.DMA((count,)),
            pltpu.SemaphoreType.DMA,
        ],
        compiler_params=pltpu.CompilerParams(collective_id=collective_id, has_side_effects=True),
    )(block)


def head_kernel(line, head_rows, length, *refs):
    final, targets, *heads = refs[:6]
    out, grads, lse_out, pick_out = refs[6:10]
    (table, rows_all, logits, probs, acc, parts, from_pair, from_line, stats, done) = refs[10:20]
    (head_sem, own_sem, give_send, give_recv, along_send, along_recv, pair_send, pair_recv) = refs[20:28]
    (stat_send, stat_recv, sum_send, sum_recv, line_send, line_recv, back_send, back_recv) = refs[28:]
    half = final.shape[0] // 2
    width = 2 * half
    padded = heads[0].shape[0]
    me_section = lax.axis_index("section")
    me_line = lax.axis_index("line")
    me_pair = lax.axis_index("pair")
    me_core = lax.axis_index("core")
    section_peer = {"section": 1 - me_section}
    pair_peer = {"pair": 1 - me_pair}
    chip_peers = []
    for step in range(1, 2 * line):
        chip_peers.append(
            {"line": lax.rem(me_line + step // 2, line), "pair": lax.rem(me_pair + step % 2, 2)}
        )
    greet(chip_peers + [section_peer])

    def side(pair):
        return pl.ds(pl.multiple_of(pair * half, 16), half)

    loads = [
        pltpu.make_async_copy(part, table.at[pl.ds(n * padded, padded)], head_sem.at[n])
        for n, part in enumerate(heads)
    ]
    for load in loads:
        load.start()

    mine = rows_all.at[me_line, side(me_pair)]
    give = remote(final.at[pl.ds(0, half)], mine, give_send, give_recv, section_peer)

    @pl.when(me_section == 1)
    def _():
        give.start()
        keep = pltpu.make_async_copy(final.at[pl.ds(half, half)], mine, own_sem)
        keep.start()
        keep.wait()

    @pl.when(me_section == 0)
    def _():
        give.wait_recv()

    def column_block(place):
        return rows_all.at[place, side(me_pair)]

    def along(step, way):
        block = column_block(me_line - way * step)
        turn = (way + 1) // 2
        return remote(
            block,
            block,
            along_send.at[turn, step],
            along_recv.at[turn, step],
            {"line": me_line + way},
        )

    def inside(place):
        return (place >= 0) & (place < line)

    def sends_along(step, way):
        return inside(me_line - way * step) & inside(me_line + way)

    def sideways(place):
        block = column_block(place)
        return remote(block, block, pair_send.at[place], pair_recv.at[place], pair_peer)

    def arrived_sideways(place):
        block = rows_all.at[place, side(1 - me_pair)]
        return remote(block, block, pair_send.at[place], pair_recv.at[place], pair_peer)

    for way in (1, -1):

        @pl.when(sends_along(0, way))
        def _():
            along(0, way).start()

    sideways(me_line).start()

    def pass_on(step):
        for way in (1, -1):
            place = me_line - way * step

            @pl.when(inside(place))
            def _():
                block = column_block(place)
                turn = (way + 1) // 2
                remote(
                    block,
                    block,
                    along_send.at[turn, step - 1],
                    along_recv.at[turn, step - 1],
                    {"line": me_line - way},
                ).wait_recv()

                @pl.when(inside(me_line + way))
                def _():
                    along(step, way).start()

                sideways(place).start()

    nearest = []
    for own in range(line):
        near = [own]
        for step in range(1, line):
            near += [place for place in (own - step, own + step) if 0 <= place < line]
        nearest.append(near)

    def by_distance(turn):
        place = 0
        for own in range(line):
            for n in range(line):
                hit = ((me_line == own) & (turn == n)).astype(jnp.int32)
                place = place + hit * nearest[own][n]
        return place

    def vocabulary(tile, rows):
        shard = tile * rows // padded
        first = lax.rem(tile * rows, padded)
        shard_section = lax.rem(me_section + shard // 2, 2)
        shard_core = lax.rem(me_core + lax.rem(shard, 2), 2)
        base = (((shard_section * line + me_line) * 2 + me_pair) * 2 + shard_core) * head_rows
        row = lax.broadcasted_iota(jnp.int32, (rows, 1), 0) + first
        return jnp.where(row < head_rows, row + base, -1)

    tile_rows = 512
    tiles = 4 * padded // tile_rows
    lowest = -1e30

    def score(place):
        tokens = rows_all.at[place]
        wanted = targets[place]

        def one(tile, carry):
            top, pick = carry
            rows = pl.ds(pl.multiple_of(tile * tile_rows, tile_rows), tile_rows)
            entry = vocabulary(tile, tile_rows)
            part = lax.dot_general(
                table[rows, :], tokens[...], (((1,), (1,)), ((), ())), preferred_element_type=f32
            )
            part = jnp.where(entry >= 0, part, lowest)
            logits[rows, :] = part
            top = jnp.maximum(top, jnp.max(part, 0, keepdims=True))
            pick = pick + jnp.sum(jnp.where(entry == wanted, part, 0.0), 0, keepdims=True)
            return top, pick

        start = (jnp.full((1, width), lowest, f32), jnp.zeros((1, width), f32))
        top, pick = lax.fori_loop(0, tiles, one, start)
        pick_out[place] = pick

        def two(tile, total):
            rows = pl.ds(pl.multiple_of(tile * tile_rows, tile_rows), tile_rows)
            value = jnp.exp(logits[rows, :] - top)
            probs[place, rows, :] = value.astype(bf16)
            return total + jnp.sum(value, 0, keepdims=True)

        total = lax.fori_loop(0, tiles, two, jnp.zeros((1, width), f32))
        own = stats.at[me_line, me_pair, place]
        own[0:1, :] = top
        own[1:2, :] = total

    def stat_copy(n, place):
        own = stats.at[me_line, me_pair, place]
        return remote(own, own, stat_send.at[n, place], stat_recv.at[n, place], chip_peers[n])

    def stat_wait(n, place):
        peer = chip_peers[n]
        source_line = lax.rem(2 * me_line + line - peer["line"], line)
        source_pair = peer["pair"]
        block = stats.at[source_line, source_pair, place]
        remote(block, block, stat_send.at[n, place], stat_recv.at[n, place], peer).wait_recv()

    for load in loads:
        load.wait()

    @pl.loop(0, line)
    def _(turn):
        pass_on(turn + 1)
        place = by_distance(turn)
        arrived_sideways(place).wait_recv()
        score(place)
        for n in range(len(chip_peers)):
            stat_copy(n, place).start()

    def sum_copy(turn):
        place = lax.rem(me_line + turn + 1, line)
        return remote(
            parts.at[place, side(1 - me_pair)],
            from_pair.at[turn],
            sum_send.at[turn],
            sum_recv.at[turn],
            pair_peer,
        )

    def line_copy(turn):
        place = lax.rem(me_line + turn + 1, line)
        return remote(
            parts.at[place, side(me_pair)],
            from_line.at[turn],
            line_send.at[turn],
            line_recv.at[turn],
            {"line": place},
        )

    def finish(turn):
        place = lax.rem(me_line + turn + 1, line)
        sum_copy(turn).wait_recv()
        own = parts.at[place, side(me_pair)]

        @pl.loop(0, half // 16)
        def _(block):
            rows = pl.ds(pl.multiple_of(block * 16, 16), 16)
            value = own[rows, :].astype(f32) + from_pair[turn, rows, :].astype(f32)
            own[rows, :] = value.astype(bf16)

    @pl.loop(0, line)
    def _(turn):
        place = lax.rem(me_line + turn + 1, line)
        for n in range(len(chip_peers)):
            stat_wait(n, place)
        tops = [stats[a, b, place, 0:1, :] for a in range(line) for b in range(2)]
        totals = [stats[a, b, place, 1:2, :] for a in range(line) for b in range(2)]
        top = tops[0]
        for value in tops[1:]:
            top = jnp.maximum(top, value)
        total = jnp.zeros_like(top)
        for peak, part in zip(tops, totals):
            total = total + part * jnp.exp(peak - top)
        lse = top + jnp.log(total)
        lse_out[place] = lse
        factor = jnp.exp(stats[me_line, me_pair, place, 0:1, :] - lse) / length
        wanted = targets[place]

        @pl.loop(0, 4)
        def _(tile):
            rows = pl.ds(pl.multiple_of(tile * padded, padded), padded)
            entry = vocabulary(tile, padded)
            grad = probs[place, rows, :].astype(f32) * factor
            grad = (grad - jnp.where(entry == wanted, 1.0 / length, 0.0)).astype(bf16)
            probs[place, rows, :] = grad
            product = lax.dot_general(
                grad, table[rows, :], (((0,), (0,)), ((), ())), preferred_element_type=f32
            )

            @pl.when(tile == 0)
            def _():
                acc[...] = product

            @pl.when((tile > 0) & (tile < 3))
            def _():
                acc[...] += product

            @pl.when(tile == 3)
            def _():
                parts[place] = (acc[...] + product).astype(bf16)

        sum_copy(turn).start()

        @pl.when(turn > 0)
        def _():
            finish(turn - 1)
            line_copy(turn - 1).start()

    gh_rows = 256
    gh_tiles = 4 * padded // gh_rows

    def head_grads(first, last):
        @pl.loop(first, last)
        def _(tile):
            rows = pl.ds(pl.multiple_of(tile * gh_rows, gh_rows), gh_rows)
            value = jnp.zeros((gh_rows, table.shape[1]), f32)
            for place in range(line):
                value = value + jnp.dot(
                    probs[place, rows, :], rows_all[place], preferred_element_type=f32
                )
            grads[rows, :] = value.astype(bf16)

    head_grads(0, gh_tiles // 2)
    finish(line - 1)
    for turn in range(line - 1):
        line_copy(turn).wait_recv()
    own = parts.at[me_line, side(me_pair)]

    @pl.loop(0, half // 16)
    def _(block):
        rows = pl.ds(pl.multiple_of(block * 16, 16), 16)
        value = own[rows, :].astype(f32)
        for turn in range(line - 1):
            value = value + from_line[turn, rows, :].astype(f32)
        done[rows, :] = value.astype(bf16)

    back = remote(done, out.at[pl.ds(0, half)], back_send, back_recv, section_peer)

    @pl.when(me_section == 0)
    def _():
        back.start()
        out[...] = jnp.zeros_like(out)

    @pl.when(me_section == 1)
    def _():
        out[pl.ds(half, half), :] = done[...]

    head_grads(gh_tiles // 2, gh_tiles)

    @pl.when(me_section == 0)
    def _():
        back.wait_send()

    @pl.when(me_section == 1)
    def _():
        back.wait_recv()
        give.wait_send()

    for way in (1, -1):
        for step in range(line - 1):

            @pl.when(sends_along(step, way))
            def _():
                along(step, way).wait_send()

    for place in range(line):
        sideways(place).wait_send()
        for n in range(len(chip_peers)):
            stat_copy(n, place).wait_send()
    for turn in range(line):
        sum_copy(turn).wait_send()
    for turn in range(line - 1):
        line_copy(turn).wait_send()


def head_pass(final, targets, heads, line, head_rows, length, collective_id):
    tokens, deep = final.shape
    half = tokens // 2
    padded = heads[0].shape[0]
    vmem = pl.BlockSpec(memory_space=pltpu.VMEM)
    anywhere = pl.BlockSpec(memory_space=pl.ANY)
    dma = pltpu.SemaphoreType.DMA
    peers = 2 * line - 1
    return pl.pallas_call(
        partial(head_kernel, line, head_rows, length),
        out_shape=[
            jax.ShapeDtypeStruct((tokens, deep), bf16),
            jax.ShapeDtypeStruct((4 * padded, deep), bf16),
            jax.ShapeDtypeStruct((line, 1, tokens), f32),
            jax.ShapeDtypeStruct((line, 1, tokens), f32),
        ],
        in_specs=[vmem, vmem] + [anywhere] * 4,
        out_specs=[vmem] * 4,
        scratch_shapes=[
            pltpu.VMEM((4 * padded, deep), bf16),
            pltpu.VMEM((line, tokens, deep), bf16),
            pltpu.VMEM((4 * padded, tokens), f32),
            pltpu.VMEM((line, 4 * padded, tokens), bf16),
            pltpu.VMEM((tokens, deep), f32),
            pltpu.VMEM((line, tokens, deep), bf16),
            pltpu.VMEM((line, half, deep), bf16),
            pltpu.VMEM((line - 1, half, deep), bf16),
            pltpu.VMEM((line, 2, line, 8, tokens), f32),
            pltpu.VMEM((half, deep), bf16),
            dma((4,)),
            dma,
            dma,
            dma,
            dma((2, line)),
            dma((2, line)),
            dma((line,)),
            dma((line,)),
            dma((peers, line)),
            dma((peers, line)),
            dma((line,)),
            dma((line,)),
            dma((line,)),
            dma((line,)),
            dma,
            dma,
        ],
        compiler_params=pltpu.CompilerParams(
            collective_id=collective_id, has_side_effects=True, vmem_limit_bytes=60 * 2**20
        ),
    )(final, targets, *heads)


def norm_rows(values):
    centred = values - jnp.mean(values, -1, keepdims=True)
    factor = lax.rsqrt(jnp.mean(centred * centred, -1, keepdims=True) + epsilon)
    return (centred * factor, factor)


def norm_back(gradient, normed, factor):
    return factor * (
        gradient
        - jnp.mean(gradient, -1, keepdims=True)
        - normed * jnp.mean(gradient * normed, -1, keepdims=True)
    )


def time_features(noise_level):
    half_width = TFEAT // 2
    rates = jnp.exp(jnp.arange(half_width, dtype=f32) * (math.log(1000.0) / half_width))
    angles = (jnp.log(noise_level) / 4.0)[:, None] * rates[None, :]
    return jnp.concatenate([jnp.cos(angles), jnp.sin(angles)], -1)


def levels_of(bins, table):
    hits = bins[:, None] == jnp.arange(table.shape[0])[None, :]
    return jnp.sum(jnp.where(hits, table[None, :], 0.0), -1)


def over_dp(part):
    part = part.reshape((part.shape[0] // 4, 2, 2) + part.shape[1:])
    part = lax.psum_scatter(part, "core", scatter_dimension=2)
    part = lax.psum_scatter(part, "pair", scatter_dimension=1)
    return lax.psum_scatter(part, "line", scatter_dimension=0)


def by_owner(part):
    line = lax.axis_size("line")
    return part.astype(bf16).reshape((line, 2, 2, part.shape[0] // (line * 4)) + part.shape[1:])


def mm(spec, left, right):
    return jnp.einsum(spec, left, right, preferred_element_type=f32)


def layer_forward(stream, scale_attn, scale_mlp, weights):
    w_qkv, w_out, w_up, b_hidden, w_down = weights
    seq_count, length, model_width = stream.shape
    normed_attn, factor_attn = norm_rows(stream)
    attn_entry = (normed_attn * scale_attn).astype(bf16)
    joined = mm("nsd,de->nse", attn_entry, w_qkv).astype(bf16)
    qkv_parts = joined.reshape(seq_count, length, 3, HEADS, HEAD_DIM)
    query_rows = qkv_parts[:, :, 0]
    key_rows = qkv_parts[:, :, 1]
    value_rows = qkv_parts[:, :, 2]
    scores = mm("nqhe,nkhe->nhqk", query_rows, key_rows) / math.sqrt(HEAD_DIM)
    exp_scores = jnp.exp(scores - jnp.max(scores, -1, keepdims=True))
    attn_probs = exp_scores / jnp.sum(exp_scores, -1, keepdims=True)
    probs_low = attn_probs.astype(bf16)
    attn_mixed = mm("nhqk,nkhe->nqhe", probs_low, value_rows).astype(bf16)
    attn_mixed = attn_mixed.reshape(seq_count, length, model_width)
    middle = stream + mm("nsd,de->nse", attn_mixed, w_out)
    normed_mlp, factor_mlp = norm_rows(middle)
    mlp_entry = (normed_mlp * scale_mlp).astype(bf16)
    up_proj = mm("nsd,df->nsf", mlp_entry, w_up) + b_hidden
    below = 0.5 + 0.5 * lax.erf(up_proj * math.sqrt(0.5))
    hidden = (up_proj * below).astype(bf16)
    density = jnp.exp(-0.5 * up_proj * up_proj) * (1.0 / math.sqrt(2.0 * math.pi))
    slope = (below + up_proj * density).astype(bf16)
    block_out = middle + mm("nsf,fd->nsd", hidden, w_down)
    kept = (
        normed_attn,
        factor_attn,
        attn_entry,
        query_rows,
        key_rows,
        value_rows,
        attn_probs,
        probs_low,
        attn_mixed,
        normed_mlp,
        factor_mlp,
        mlp_entry,
        slope,
        hidden,
    )
    return (block_out, kept)


def layer_backward(grad_out, kept, scale_attn, scale_mlp, weights, whole):
    w_qkv, w_out, w_up, b_hidden, w_down = weights
    (
        normed_attn,
        factor_attn,
        attn_entry,
        query_rows,
        key_rows,
        value_rows,
        attn_probs,
        probs_low,
        attn_mixed,
        normed_mlp,
        factor_mlp,
        mlp_entry,
        slope,
        hidden,
    ) = kept
    seq_count, length, model_width = grad_out.shape
    grads = {}
    grad_branch = grad_out.astype(bf16)
    if whole:
        grads["down"] = by_owner(mm("nsf,nsd->fd", hidden, grad_branch))
    grad_hidden = mm("nsd,fd->nsf", grad_branch, w_down)
    grad_up_proj = (grad_hidden * slope.astype(f32)).astype(bf16)
    if whole:
        grads["bias"] = jnp.sum(grad_up_proj.astype(f32), (0, 1))
        grads["up"] = by_owner(mm("nsd,nsf->df", mlp_entry, grad_up_proj))
    grad_entry = mm("nsf,df->nsd", grad_up_proj, w_up)
    grad_middle = grad_out + norm_back(grad_entry * scale_mlp, normed_mlp, factor_mlp)
    grad_attn = grad_middle.astype(bf16)
    if whole:
        grads["out"] = by_owner(mm("nsd,nse->de", attn_mixed, grad_attn))
    grad_mixed = mm("nse,de->nsd", grad_attn, w_out)
    grad_mixed = grad_mixed.astype(bf16).reshape(seq_count, length, HEADS, HEAD_DIM)
    grad_probs = mm("nqhe,nkhe->nhqk", grad_mixed, value_rows)
    grad_values = mm("nhqk,nqhe->nkhe", probs_low, grad_mixed)
    grad_scores = (
        attn_probs * (grad_probs - jnp.sum(grad_probs * attn_probs, -1, keepdims=True))
    ).astype(bf16)
    grad_query = mm("nhqk,nkhe->nqhe", grad_scores, key_rows) / math.sqrt(HEAD_DIM)
    grad_keys = mm("nhqk,nqhe->nkhe", grad_scores, query_rows) / math.sqrt(HEAD_DIM)
    grad_joined = jnp.stack([grad_query, grad_keys, grad_values], 2).astype(bf16)
    grad_joined = grad_joined.reshape(seq_count, length, 3 * model_width)
    if whole:
        grads["qkv"] = by_owner(mm("nsd,nse->de", attn_entry, grad_joined))
    grad_attn_entry = mm("nse,de->nsd", grad_joined, w_qkv)
    grad_stream = grad_middle + norm_back(grad_attn_entry * scale_attn, normed_attn, factor_attn)
    if whole:
        grads["cond"] = jnp.concatenate(
            [jnp.sum(grad_attn_entry * normed_attn, 1), jnp.sum(grad_entry * normed_mlp, 1)], -1
        )
    return (grad_stream, grads)


def local(
    token_ids,
    target_ids,
    time_bins,
    sigma_table,
    noise,
    embed,
    w_in,
    w_time,
    norm_gain,
    w_qkv,
    w_out,
    w_up,
    b_hidden,
    w_down,
    out_gain,
    head,
):
    section = lax.axis_index("section")
    line_at = lax.axis_index("line")
    pair_at = lax.axis_index("pair")
    core = lax.axis_index("core")
    sections = lax.axis_size("section")
    line = lax.axis_size("line")
    chip = line_at * 2 + pair_at
    chips = line * 2
    cores = 2
    dp_count = chips * cores
    dp_index = chip * cores + core
    is_first = section == 0
    seqs, length = token_ids.shape
    tokens = seqs * length
    half = tokens // sections
    model_width = w_out.shape[-1]
    emb_rows, emb_width = embed.shape
    straight = line <= 4 and half % 16 == 0 and model_width // dp_count % 16 == 0

    own_ids = jnp.concatenate([token_ids.reshape(-1), target_ids.reshape(-1), time_bins])
    if straight:
        padded = jnp.pad(own_ids, (0, -own_ids.shape[0] % 1024)).reshape(-1, 128)
        all_ids = gathered_small(padded, line, 0).reshape(dp_count, -1)[:, : own_ids.shape[0]]
    else:
        all_ids = lax.all_gather(own_ids, DP)
    all_tokens = all_ids[:, :tokens]
    all_targets = all_ids[:, tokens : 2 * tokens]
    all_bins = all_ids[:, 2 * tokens :].reshape(-1)

    own_rows = dp_index * emb_rows + jnp.arange(emb_rows)
    half_tokens = lax.dynamic_slice_in_dim(all_tokens, section * half, half, 1)
    picked = (half_tokens.reshape(-1)[:, None] == own_rows[None, :]).astype(bf16)
    found = jnp.dot(picked, embed, preferred_element_type=f32).astype(bf16)
    if straight:
        found = found.reshape(line, 2, 2, half, emb_width)
        (embedded,) = summed_over_dp([found], 1, swap=True)
    else:
        embedded = lax.all_gather(over_dp(found.reshape(dp_count, half, emb_width)), "section")
    embedded = embedded.astype(f32).reshape(seqs, length, emb_width)

    head_rows = head.shape[0]
    swapped = [(0, 1), (1, 0)]
    if straight:
        head_own = jnp.pad(head, ((0, -head_rows % 512), (0, 0)))
        head_core = lax.ppermute(head_own, "core", swapped)
        head_section = lax.ppermute(head_own, "section", swapped)
        heads = [head_own, head_core, head_section, lax.ppermute(head_section, "core", swapped)]
    else:
        head_group = lax.all_gather(lax.all_gather(head, "core"), "section")
        head_group = head_group.reshape(-1, model_width)
        vocab_base = (
            (jnp.arange(sections)[:, None] * chips + chip) * cores + jnp.arange(cores)[None, :]
        ) * head_rows
        columns = (vocab_base[:, :, None] + jnp.arange(head_rows)[None, None, :]).reshape(-1)

    noise_level = levels_of(time_bins, sigma_table)
    unit_factor = lax.rsqrt(jnp.mean(embedded * embedded, -1, keepdims=True) + epsilon)
    level_col = noise_level[:, None, None]
    noise_scale = lax.rsqrt(level_col * level_col + 1.0)
    noisy_rows = ((embedded * unit_factor + level_col * noise) * noise_scale).astype(bf16)
    time_feats = time_features(noise_level)
    conditioned = jnp.dot(time_feats, w_time[0].astype(f32), precision=highest) + norm_gain[0]
    scale_attn = conditioned[:, None, :model_width]
    scale_mlp = conditioned[:, None, model_width:]
    weights = (w_qkv[0], w_out[0], w_up[0], b_hidden[0], w_down[0])

    stream0 = mm("nse,ed->nsd", noisy_rows, w_in)
    first_out, _ = layer_forward(stream0, scale_attn, scale_mlp, weights)
    arrived = lax.ppermute(first_out.astype(bf16), "section", swapped)
    stream = jnp.where(is_first, stream0, arrived.astype(f32))
    block_out, kept = layer_forward(stream, scale_attn, scale_mlp, weights)

    top_stream = block_out.astype(bf16).astype(f32)
    final_normed, final_factor = norm_rows(top_stream)
    final_rows = (final_normed * out_gain).astype(bf16).reshape(tokens, model_width)
    targets_group = lax.dynamic_slice_in_dim(
        all_targets.reshape(chips, cores, tokens), core, 1, 1
    )[:, 0]
    targets_group = lax.dynamic_slice_in_dim(targets_group, section * half, half, 1)
    if straight:
        grad_final, grad_head, lse, picks = head_pass(
            final_rows, targets_group.reshape(line, 1, tokens), heads, line, head_rows, length, 3
        )
        ce_part = jnp.sum(lse) / chips - jnp.sum(picks)
    else:
        targets_group = targets_group.reshape(-1)
        handed = lax.ppermute(final_rows[:half], "section", [(1, 0), (0, 1)])
        own_final = jnp.where(is_first, handed, final_rows[half:])
        group_final = lax.all_gather(own_final, ("line", "pair"), tiled=True)
        logits = mm("td,vd->tv", group_final, head_group)
        local_top = jnp.max(logits, -1)
        local_total = jnp.sum(jnp.exp(logits - local_top[:, None]), -1)
        mark = columns[None, :] == targets_group[:, None]
        local_pick = jnp.sum(jnp.where(mark, logits, 0.0))
        stats = lax.all_gather(jnp.stack([local_top, local_total]), ("line", "pair"))
        all_top = jnp.max(stats[:, 0], 0)
        all_total = jnp.sum(stats[:, 1] * jnp.exp(stats[:, 0] - all_top), 0)
        log_total = all_top + jnp.log(all_total)
        soft_rows = jnp.exp(logits - log_total[:, None])
        logit_grads = ((soft_rows - jnp.where(mark, 1.0, 0.0)) / length).astype(bf16)
        grad_final = jnp.dot(logit_grads, head_group, preferred_element_type=f32).astype(bf16)
        grad_final = lax.psum_scatter(grad_final, ("line", "pair"), scatter_dimension=0, tiled=True)
        handed = lax.ppermute(grad_final, "section", swapped)
        grad_final = jnp.concatenate([handed, grad_final], 0)
        grad_head = mm("tv,td->vd", logit_grads, group_final).astype(bf16)
        grad_head = grad_head.reshape(sections, cores, head_rows, model_width)
        grad_head = lax.psum_scatter(grad_head, "core", scatter_dimension=1)
        grad_head = lax.psum_scatter(grad_head, "section", scatter_dimension=0).astype(f32)

        ce_part = jnp.sum(log_total) / chips - local_pick
    grad_final = grad_final.astype(f32).reshape(seqs, length, model_width)
    out_part = jnp.where(is_first, 0.0, jnp.sum(grad_final * final_normed, (0, 1)))

    grad_top = norm_back(grad_final * out_gain, final_normed, final_factor)
    grad_second, _ = layer_backward(grad_top, kept, scale_attn, scale_mlp, weights, False)
    returned = lax.ppermute(grad_second.astype(bf16), "section", swapped)
    grad_cot = jnp.where(is_first, returned.astype(f32), grad_top)
    grad_stream, grads = layer_backward(grad_cot, kept, scale_attn, scale_mlp, weights, True)
    grad_first = grad_stream.astype(bf16)

    in_part = mm("nse,nsd->ed", noisy_rows, grad_first).astype(bf16)
    in_part = in_part.reshape(sections, line, 2, 2, -1, model_width)
    in_part = jnp.moveaxis(in_part, 0, 3).reshape(line, 2, 2, -1, model_width)
    grad_noisy = mm("nsd,ed->nse", grad_first, w_in)
    grad_unit = grad_noisy * noise_scale
    cubed = unit_factor * unit_factor * unit_factor
    grad_embedded = unit_factor * grad_unit - cubed * embedded * jnp.mean(
        grad_unit * embedded, -1, keepdims=True
    )
    grad_flat = grad_embedded.reshape(tokens, emb_width)

    ce_high = ce_part.astype(bf16).astype(f32)
    ce_mid = (ce_part - ce_high).astype(bf16).astype(f32)
    ce_low = ce_part - ce_high - ce_mid
    shared = jnp.concatenate([out_part, jnp.stack([ce_high, ce_mid, ce_low])])
    shared_rows = -(-shared.shape[0] // emb_width)
    shared = jnp.pad(shared, (0, shared_rows * emb_width - shared.shape[0]))
    handing = jnp.concatenate([grad_flat, shared.reshape(-1, emb_width)], 0).astype(bf16)
    handed = lax.ppermute(handing, "section", swapped)
    kept_rows = jnp.where(is_first, handing[:tokens], handed[:tokens])
    layer_small = jnp.concatenate([grads["cond"].reshape(-1), grads["bias"]])
    layer_rows = layer_small.shape[0] // emb_width
    packet = jnp.concatenate(
        [
            kept_rows,
            layer_small.astype(bf16).reshape(layer_rows, emb_width),
            handing[tokens:],
            handed[tokens:],
        ],
        0,
    )
    packet = jnp.pad(packet, ((0, -packet.shape[0] % 16), (0, 0)))
    parts = [grads["down"], grads["up"], grads["qkv"], grads["out"], in_part]
    if straight:
        *sums, packets, grad_head = summed_over_dp(
            parts, 2, packet=packet, head_part=grad_head, head_rows=head_rows
        )
        packets = packets.reshape((dp_count,) + packet.shape)
    else:
        sums = [over_dp(part.reshape((dp_count,) + part.shape[3:])).astype(f32) for part in parts]
        packets = lax.all_gather(packet, DP)
    grad_down, grad_up, grad_qkv, grad_wout, in_sum = sums
    in_sum = in_sum.reshape(sections, -1, model_width)
    in_handed = lax.ppermute(in_sum[1], "section", swapped)
    grad_w_in = jnp.where(is_first, in_sum[0], in_handed)

    grad_all = packets[:, :tokens].reshape(-1, emb_width)
    out_rows = emb_rows // sections
    target_rows = (section * dp_count + dp_index) * out_rows + jnp.arange(out_rows)
    place = (target_rows[:, None] == all_tokens.reshape(-1)[None, :]).astype(bf16)
    grad_embed = jnp.dot(place, grad_all, preferred_element_type=f32)

    small = packets[:, tokens : tokens + layer_rows].astype(f32).reshape(dp_count, -1)
    cond_size = grads["cond"].size
    cond_all = small[:, :cond_size].reshape(dp_count * seqs, 2 * model_width)
    hidden_rows = grads["bias"].shape[0] // dp_count
    grad_bias = jnp.sum(
        lax.dynamic_slice_in_dim(small, cond_size + dp_index * hidden_rows, hidden_rows, 1), 0
    )
    norm_cols = 2 * model_width // dp_count
    grad_gain = jnp.sum(lax.dynamic_slice_in_dim(cond_all, dp_index * norm_cols, norm_cols, 1), 0)
    feats_all = time_features(levels_of(all_bins, sigma_table))
    feat_rows = TFEAT // dp_count
    feats_own = lax.dynamic_slice_in_dim(feats_all, dp_index * feat_rows, feat_rows, 1)
    grad_time = jnp.dot(feats_own.T, cond_all, precision=highest)
    both = packets[:, tokens + layer_rows : tokens + layer_rows + 2 * shared_rows].astype(f32)
    both = jnp.sum(both.reshape(dp_count, 2, -1), (0, 1))
    loss = jnp.sum(both[model_width : model_width + 3]) / (tokens * dp_count)
    gain_rows = model_width // dp_count
    grad_out_gain = lax.dynamic_slice_in_dim(both, dp_index * gain_rows, gain_rows)
    return (
        loss,
        grad_embed,
        grad_w_in,
        grad_time[None],
        grad_gain[None],
        grad_qkv[None],
        grad_wout[None],
        grad_up[None],
        grad_bias[None],
        grad_down[None],
        grad_out_gain,
        grad_head,
    )


def solution(mesh):
    sections, dp_count = mesh.shape["section"], mesh.shape["dp"]
    fine = Mesh(mesh.devices.reshape(sections, dp_count // 4, 2, 2), ("section",) + DP)
    everywhere = ("section",) + DP
    in_specs = (
        P(DP, None),
        P(DP, None),
        P(DP),
        P(),
        P(DP, None, None),
        P(DP, None),
        P(),
        P("section", None, None),
        P("section", None),
        P("section", None, None),
        P("section", None, None),
        P("section", None, None),
        P("section", None),
        P("section", None, None),
        P(),
        P(everywhere, None),
    )
    out_specs = (
        P(),
        P(everywhere, None),
        P(everywhere, None),
        P("section", DP, None),
        P("section", DP),
        P("section", DP, None),
        P("section", DP, None),
        P("section", DP, None),
        P("section", DP),
        P("section", DP, None),
        P(DP),
        P(everywhere, None),
    )
    return jax.shard_map(local, mesh=fine, in_specs=in_specs, out_specs=out_specs, check_vma=False)
```

```python
from functools import partial
import math

import jax
import jax.numpy as jnp
from jax import lax
from jax.experimental import pallas as pl
from jax.experimental.pallas import tpu as pltpu
from jax.sharding import Mesh, PartitionSpec as P

HEADS = 16
HEAD_DIM = 64
TFEAT = 256

epsilon = 1e-05
highest = lax.Precision.HIGHEST
f32 = jnp.float32
bf16 = jnp.bfloat16
DP = ("line", "pair", "core")


MESH = pl.DeviceIdType.MESH


def greet(peers):
    barrier = pltpu.get_barrier_semaphore()
    for peer in peers:
        pl.semaphore_signal(barrier, inc=1, device_id=peer, device_id_type=MESH)
    pl.semaphore_wait(barrier, len(peers))


def remote(source, target, send, recv, peer):
    return pltpu.make_async_remote_copy(
        src_ref=source,
        dst_ref=target,
        send_sem=send,
        recv_sem=recv,
        device_id=peer,
        device_id_type=MESH,
    )


def ring_place(position, line):
    turned = position // line
    return position * (1 - turned) + (2 * line - 1 - position) * turned, turned


def sum_kernel(shapes, line, half_rows, with_head, swap, *refs):
    count = len(shapes)
    with_packet = half_rows > 0
    refs = list(refs)

    def take(number):
        return [refs.pop(0) for _ in range(number)]

    parts = take(count)
    sent = take(2) if with_packet else []
    head_part = take(1)[0] if with_head else None
    outs = take(count)
    smalls, halves = take(2) if with_packet else (None, None)
    head_out = take(1)[0] if with_head else None
    own, from_core, slots = take(count), take(count), take(count)
    load_sem, core_send, core_recv, ring_send, ring_recv = take(5)
    if with_packet:
        own_sem, packet_send, packet_recv, wide_send, wide_recv, half_send, half_recv = take(7)
    if with_head:
        head_own, head_core, head_section, head_sem, head_send, head_recv = take(6)
    if swap:
        swap_send, swap_recv = take(2)

    chips = 2 * line
    me_section = lax.axis_index("section")
    me_line = lax.axis_index("line")
    me_pair = lax.axis_index("pair")
    me_core = lax.axis_index("core")
    position = me_line + me_pair * (chips - 1 - 2 * me_line)
    section_peer = {"section": 1 - me_section}
    core_peer = {"core": 1 - me_core}
    ways = (1, -1)
    ring_peers = []
    for way in ways:
        peer_line, peer_pair = ring_place(lax.rem(position + way + chips, chips), line)
        ring_peers.append({"line": peer_line, "pair": peer_pair})
    greet([core_peer, section_peer] + ring_peers)

    def block_of(turn, step):
        ahead = lax.rem(position - ways[turn] * (1 + step) + 2 * chips, chips)
        return ring_place(ahead, line)

    def columns(index, turn):
        wide = shapes[index][-1] // 2
        return pl.ds(turn * wide, wide)

    def load(index, turn, step):
        place, pair = block_of(turn, step)
        cols = columns(index, turn)
        return pltpu.make_async_copy(
            parts[index].at[place, pair, me_core, :, cols],
            own[index].at[step, :, cols],
            load_sem.at[index, turn, step],
        )

    def core_copy(index, turn, step):
        place, pair = block_of(turn, step)
        cols = columns(index, turn)
        return remote(
            parts[index].at[place, pair, 1 - me_core, :, cols],
            from_core[index].at[step, :, cols],
            core_send.at[index, turn, step],
            core_recv.at[index, turn, step],
            core_peer,
        )

    def ring_copy(index, turn, step):
        cols = columns(index, turn)
        if isinstance(step, int) and step == 0:
            source = from_core[index].at[0, :, cols]
        else:
            source = slots[index].at[step - 1, :, cols]
        return remote(
            source,
            slots[index].at[step, :, cols],
            ring_send.at[index, turn, step],
            ring_recv.at[index, turn, step],
            ring_peers[turn],
        )

    def to_core(step):
        for index in range(count):
            for turn in range(2):
                load(index, turn, step).start()
                core_copy(index, turn, step).start()

    def stop(step):
        first = isinstance(step, int) and step == 0
        last = isinstance(step, int) and step == chips - 1
        for index in range(count):
            rows = shapes[index][-2]
            wide = shapes[index][-1] // 2
            tile = min(wide, 512)
            for turn in range(2):
                load(index, turn, step).wait()
                core_copy(index, turn, step).wait_recv()
                if not first:
                    ring_copy(index, turn, step - 1).wait_recv()

                @pl.loop(0, rows // 16)
                def _(block):
                    row = pl.ds(pl.multiple_of(block * 16, 16), 16)
                    for col in range(turn * wide, (turn + 1) * wide, tile):
                        cols = pl.ds(col, tile)
                        total = from_core[index][step, row, cols].astype(f32)
                        total = total + own[index][step, row, cols].astype(f32)
                        if not first:
                            total = total + slots[index][step - 1, row, cols].astype(f32)
                        if last and swap:
                            outs[index][me_section, row, cols] = total.astype(outs[index].dtype)
                        elif last:
                            outs[index][row, cols] = total.astype(outs[index].dtype)
                        elif first:
                            from_core[index][0, row, cols] = total.astype(bf16)
                        else:
                            slots[index][step - 1, row, cols] = total.astype(bf16)

                if not last:
                    ring_copy(index, turn, step).start()

    hops = (line, line - 1)

    def packet_blocks(place, pair):
        return [smalls.at[place, pair, me_core], halves.at[me_section, place, pair, me_core]]

    def packet_hops(turn, hop, away):
        place, pair = ring_place(
            lax.rem(position - ways[turn] * (hop + away) + 2 * chips, chips), line
        )
        return [
            remote(
                block,
                block,
                packet_send.at[n, turn, hop],
                packet_recv.at[n, turn, hop],
                ring_peers[turn],
            )
            for n, block in enumerate(packet_blocks(place, pair))
        ]

    def pass_packets(hop):
        for turn in range(2):
            if 0 < hop <= hops[turn]:
                for copy in packet_hops(turn, hop - 1, 1):
                    copy.wait_recv()
            if hop < hops[turn]:
                for copy in packet_hops(turn, hop, 0):
                    copy.start()

    if with_packet:
        keeps = [
            pltpu.make_async_copy(block, target, own_sem.at[n])
            for n, (block, target) in enumerate(zip(sent, packet_blocks(me_line, me_pair)))
        ]
        for keep in keeps:
            keep.start()
        columns_of = [smalls.at[:, :, me_core], halves.at[me_section, :, :, me_core]]
        across = [
            remote(block, block, wide_send.at[n], wide_recv.at[n], core_peer)
            for n, block in enumerate(columns_of)
        ]
        half_swap = remote(
            halves.at[me_section], halves.at[me_section], half_send, half_recv, section_peer
        )

    if with_head:
        high = head_part.shape[0] // 4

        def shard(n):
            return head_part.at[pl.ds(n * high, high)]

        head_loads = [
            pltpu.make_async_copy(shard(2 * n), head_own.at[n], head_sem.at[n]) for n in range(2)
        ]
        head_copies = [
            remote(shard(2 * n + 1), head_core.at[n], head_send.at[n], head_recv.at[n], core_peer)
            for n in range(2)
        ]
        head_copies.append(
            remote(head_core.at[1], head_section, head_send.at[2], head_recv.at[2], section_peer)
        )

        def head_rows(body):
            @pl.loop(0, high // 16)
            def _(block):
                body(pl.ds(pl.multiple_of(block * 16, 16), 16))

        def head_over_cores():
            for copy in head_loads:
                copy.wait()
            for copy in head_copies[:2]:
                copy.wait_recv()

            def add(rows):
                value = head_core[1, rows, :].astype(f32) + head_own[1, rows, :].astype(f32)
                head_core[1, rows, :] = value.astype(bf16)

            head_rows(add)
            head_copies[2].start()

        def head_over_sections():
            head_copies[2].wait_recv()

            def total(rows):
                return (
                    head_core[0, rows, :].astype(f32)
                    + head_own[0, rows, :].astype(f32)
                    + head_section[rows, :].astype(f32)
                )

            whole = head_out.shape[0] // 16
            rest = head_out.shape[0] % 16

            @pl.loop(0, whole)
            def _(block):
                rows = pl.ds(pl.multiple_of(block * 16, 16), 16)
                head_out[rows, :] = total(rows)

            if rest:
                value = total(pl.ds(whole * 16, 16))
                head_out[pl.ds(whole * 16, rest), :] = value[:rest]

    to_core(0)
    to_core(1)
    stop(0)
    if with_packet:
        for keep in keeps:
            keep.wait()
        pass_packets(0)
    for step in range(1, chips - 1):
        to_core(step + 1)
        if with_head and step == 1:
            for copy in head_loads + head_copies[:2]:
                copy.start()
        stop(step)
        if with_packet and step <= line:
            pass_packets(step)
            if step == line:
                for copy in across:
                    copy.start()
        if with_packet and step == line + 1:
            for copy in across:
                copy.wait_recv()
            half_swap.start()
        if with_head and step == 2:
            head_over_cores()
    stop(chips - 1)
    if swap:
        give = remote(
            outs[0].at[me_section], outs[0].at[me_section], swap_send, swap_recv, section_peer
        )
        give.start()
    if with_head:
        head_over_sections()
        for copy in head_copies:
            copy.wait_send()
    if with_packet:
        half_swap.wait()
        for copy in across:
            copy.wait_send()
        for turn in range(2):
            for hop in range(hops[turn]):
                for copy in packet_hops(turn, hop, 0):
                    copy.wait_send()
    for index in range(count):
        for turn in range(2):
            for step in range(chips):
                core_copy(index, turn, step).wait_send()
                if step < chips - 1:
                    ring_copy(index, turn, step).wait_send()
    if swap:
        give.wait()


def summed_over_dp(parts, collective_id, packets=(), head_part=None, head_rows=0, swap=False):
    shapes = [part.shape for part in parts]
    line = shapes[0][0]
    chips = 2 * line
    count = len(parts)
    vmem = pl.BlockSpec(memory_space=pltpu.VMEM)
    anywhere = pl.BlockSpec(memory_space=pl.ANY)
    if swap:
        out_shape = [jax.ShapeDtypeStruct((2,) + shapes[0][-2:], bf16)]
    else:
        out_shape = [jax.ShapeDtypeStruct(shape[-2:], f32) for shape in shapes]
    out_specs = [vmem] * count
    operands = list(parts)
    dma = pltpu.SemaphoreType.DMA
    scratch = [pltpu.VMEM((chips,) + shape[-2:], bf16) for shape in shapes]
    scratch += [pltpu.VMEM((chips,) + shape[-2:], bf16) for shape in shapes]
    scratch += [pltpu.VMEM((chips - 1,) + shape[-2:], bf16) for shape in shapes]
    scratch += [dma((count, 2, chips))] * 3 + [dma((count, 2, chips - 1))] * 2
    cost = 5 * sum(math.prod(shape) for shape in shapes) + 2**26
    half_rows = 0
    if packets:
        small, half = packets
        half_rows = half.shape[0]
        operands += [small, half]
        out_shape.append(jax.ShapeDtypeStruct((line, 2, 2) + small.shape, small.dtype))
        out_shape.append(jax.ShapeDtypeStruct((2, line, 2, 2) + half.shape, half.dtype))
        out_specs += [anywhere, anywhere]
        scratch += [dma((2,)), dma((2, 2, line)), dma((2, 2, line)), dma((2,)), dma((2,)), dma, dma]
    if head_part is not None:
        high, deep = head_part.shape[0] // 4, head_part.shape[1]
        operands.append(head_part)
        out_shape.append(jax.ShapeDtypeStruct((head_rows, deep), f32))
        out_specs.append(vmem)
        scratch += [pltpu.VMEM((2, high, deep), bf16)] * 2 + [pltpu.VMEM((high, deep), bf16)]
        scratch += [dma((2,)), dma((3,)), dma((3,))]
    if swap:
        scratch += [dma, dma]
    return pl.pallas_call(
        partial(sum_kernel, shapes, line, half_rows, head_part is not None, swap),
        out_shape=out_shape,
        in_specs=[anywhere] * len(operands),
        out_specs=out_specs,
        scratch_shapes=scratch,
        compiler_params=pltpu.CompilerParams(
            collective_id=collective_id, has_side_effects=True, vmem_limit_bytes=60 * 2**20
        ),
        cost_estimate=pl.CostEstimate(flops=0, bytes_accessed=cost, transcendentals=0),
    )(*operands)


def gather_kernel(line, mine, out, send, recv, own_sem):
    me_line = lax.axis_index("line")
    me_pair = lax.axis_index("pair")
    me_core = lax.axis_index("core")
    peers = []
    for step in range(1, line * 4):
        peers.append(
            {
                "line": lax.rem(me_line + step // 4, line),
                "pair": lax.rem(me_pair + step // 2 % 2, 2),
                "core": lax.rem(me_core + step % 2, 2),
            }
        )
    greet(peers)
    place = out.at[me_line, me_pair, me_core]
    keep = pltpu.make_async_copy(mine, place, own_sem)
    keep.start()
    copies = [remote(mine, place, send.at[n], recv.at[n], peer) for n, peer in enumerate(peers)]
    for copy in copies:
        copy.start()
    keep.wait()
    for copy in copies:
        copy.wait()


def gathered_small(block, line, collective_id):
    count = line * 4 - 1
    vmem = pl.BlockSpec(memory_space=pltpu.VMEM)
    return pl.pallas_call(
        partial(gather_kernel, line),
        out_shape=jax.ShapeDtypeStruct((line, 2, 2) + block.shape, block.dtype),
        in_specs=[vmem],
        out_specs=vmem,
        scratch_shapes=[
            pltpu.SemaphoreType.DMA((count,)),
            pltpu.SemaphoreType.DMA((count,)),
            pltpu.SemaphoreType.DMA,
        ],
        compiler_params=pltpu.CompilerParams(collective_id=collective_id, has_side_effects=True),
        cost_estimate=pl.CostEstimate(flops=0, bytes_accessed=2**25, transcendentals=0),
    )(block)


def head_kernel(line, head_rows, length, *refs):
    final, targets, *heads = refs[:6]
    out, grads, lse_out, pick_out = refs[6:10]
    (table, rows_all, logits, probs, acc, parts, from_pair, from_line, stats, done) = refs[10:20]
    (head_sem, own_sem, give_send, give_recv, along_send, along_recv, pair_send, pair_recv) = refs[20:28]
    (stat_send, stat_recv, sum_send, sum_recv, line_send, line_recv, back_send, back_recv) = refs[28:]
    half = final.shape[0] // 2
    width = 2 * half
    padded = heads[0].shape[0]
    me_section = lax.axis_index("section")
    me_line = lax.axis_index("line")
    me_pair = lax.axis_index("pair")
    me_core = lax.axis_index("core")
    section_peer = {"section": 1 - me_section}
    pair_peer = {"pair": 1 - me_pair}
    chip_peers = []
    for step in range(1, 2 * line):
        chip_peers.append(
            {"line": lax.rem(me_line + step // 2, line), "pair": lax.rem(me_pair + step % 2, 2)}
        )
    greet(chip_peers + [section_peer])

    def side(pair):
        return pl.ds(pl.multiple_of(pair * half, 16), half)

    loads = [
        pltpu.make_async_copy(part, table.at[pl.ds(n * padded, padded)], head_sem.at[n])
        for n, part in enumerate(heads)
    ]
    for load in loads:
        load.start()

    def token_rows(place, pair):
        return pl.ds(pl.multiple_of(place * width + pair * half, 16), half)

    def group(place):
        return pl.ds(pl.multiple_of(place * width, 128), width)

    mine = rows_all.at[token_rows(me_line, me_pair)]
    give = remote(final.at[pl.ds(0, half)], mine, give_send, give_recv, section_peer)

    @pl.when(me_section == 1)
    def _():
        give.start()
        keep = pltpu.make_async_copy(final.at[pl.ds(half, half)], mine, own_sem)
        keep.start()
        keep.wait()

    @pl.when(me_section == 0)
    def _():
        give.wait_recv()

    def column_block(place):
        return rows_all.at[token_rows(place, me_pair)]

    def along(step, way):
        block = column_block(me_line - way * step)
        turn = (way + 1) // 2
        return remote(
            block,
            block,
            along_send.at[turn, step],
            along_recv.at[turn, step],
            {"line": me_line + way},
        )

    def inside(place):
        return (place >= 0) & (place < line)

    def sends_along(step, way):
        return inside(me_line - way * step) & inside(me_line + way)

    def sideways(place):
        block = column_block(place)
        return remote(block, block, pair_send.at[place], pair_recv.at[place], pair_peer)

    def arrived_sideways(place):
        block = rows_all.at[token_rows(place, 1 - me_pair)]
        return remote(block, block, pair_send.at[place], pair_recv.at[place], pair_peer)

    for way in (1, -1):

        @pl.when(sends_along(0, way))
        def _():
            along(0, way).start()

    sideways(me_line).start()

    def pass_on(step):
        for way in (1, -1):
            place = me_line - way * step

            @pl.when(inside(place))
            def _():
                block = column_block(place)
                turn = (way + 1) // 2
                remote(
                    block,
                    block,
                    along_send.at[turn, step - 1],
                    along_recv.at[turn, step - 1],
                    {"line": me_line - way},
                ).wait_recv()

                @pl.when(inside(me_line + way))
                def _():
                    along(step, way).start()

                sideways(place).start()

    nearest = []
    for own in range(line):
        near = [own]
        for step in range(1, line):
            near += [place for place in (own - step, own + step) if 0 <= place < line]
        nearest.append(near)

    def by_distance(turn):
        place = 0
        for own in range(line):
            for n in range(line):
                hit = ((me_line == own) & (turn == n)).astype(jnp.int32)
                place = place + hit * nearest[own][n]
        return place

    def vocabulary(tile, rows):
        shard = tile * rows // padded
        first = lax.rem(tile * rows, padded)
        shard_section = lax.rem(me_section + shard // 2, 2)
        shard_core = lax.rem(me_core + lax.rem(shard, 2), 2)
        base = (((shard_section * line + me_line) * 2 + me_pair) * 2 + shard_core) * head_rows
        row = lax.broadcasted_iota(jnp.int32, (rows, 1), 0) + first
        return jnp.where(row < head_rows, row + base, -1)

    tile_rows = 512
    tiles = 4 * padded // tile_rows
    lowest = -1e30

    def score(place):
        tokens = rows_all[group(place), :]
        wanted = targets[place]

        def one(tile, carry):
            top, pick = carry
            rows = pl.ds(pl.multiple_of(tile * tile_rows, tile_rows), tile_rows)
            entry = vocabulary(tile, tile_rows)
            part = lax.dot_general(
                table[rows, :], tokens, (((1,), (1,)), ((), ())), preferred_element_type=f32
            )
            part = jnp.where(entry >= 0, part, lowest)
            logits[rows, :] = part
            top = jnp.maximum(top, jnp.max(part, 0, keepdims=True))
            pick = pick + jnp.sum(jnp.where(entry == wanted, part, 0.0), 0, keepdims=True)
            return top, pick

        start = (jnp.full((1, width), lowest, f32), jnp.zeros((1, width), f32))
        top, pick = lax.fori_loop(0, tiles, one, start)
        pick_out[place] = pick

        def two(tile, total):
            rows = pl.ds(pl.multiple_of(tile * tile_rows, tile_rows), tile_rows)
            value = jnp.exp(logits[rows, :] - top)
            probs[rows, group(place)] = value.astype(bf16)
            return total + jnp.sum(value, 0, keepdims=True)

        total = lax.fori_loop(0, tiles, two, jnp.zeros((1, width), f32))
        own = stats.at[me_line, me_pair, place]
        own[0:1, :] = top
        own[1:2, :] = total

    def stat_copy(n, place):
        own = stats.at[me_line, me_pair, place]
        return remote(own, own, stat_send.at[n, place], stat_recv.at[n, place], chip_peers[n])

    def stat_wait(n, place):
        peer = chip_peers[n]
        source_line = lax.rem(2 * me_line + line - peer["line"], line)
        source_pair = peer["pair"]
        block = stats.at[source_line, source_pair, place]
        remote(block, block, stat_send.at[n, place], stat_recv.at[n, place], peer).wait_recv()

    for load in loads:
        load.wait()

    @pl.loop(0, line)
    def _(turn):
        pass_on(turn + 1)
        place = by_distance(turn)
        arrived_sideways(place).wait_recv()
        score(place)
        for n in range(len(chip_peers)):
            stat_copy(n, place).start()

    def sum_copy(turn):
        place = lax.rem(me_line + turn + 1, line)
        return remote(
            parts.at[place, side(1 - me_pair)],
            from_pair.at[turn],
            sum_send.at[turn],
            sum_recv.at[turn],
            pair_peer,
        )

    def line_copy(turn):
        place = lax.rem(me_line + turn + 1, line)
        return remote(
            parts.at[place, side(me_pair)],
            from_line.at[turn],
            line_send.at[turn],
            line_recv.at[turn],
            {"line": place},
        )

    def finish(turn):
        place = lax.rem(me_line + turn + 1, line)
        sum_copy(turn).wait_recv()
        own = parts.at[place, side(me_pair)]

        @pl.loop(0, half // 16)
        def _(block):
            rows = pl.ds(pl.multiple_of(block * 16, 16), 16)
            value = own[rows, :].astype(f32) + from_pair[turn, rows, :].astype(f32)
            own[rows, :] = value.astype(bf16)

    @pl.loop(0, line)
    def _(turn):
        place = lax.rem(me_line + turn + 1, line)
        for n in range(len(chip_peers)):
            stat_wait(n, place)
        tops = [stats[a, b, place, 0:1, :] for a in range(line) for b in range(2)]
        totals = [stats[a, b, place, 1:2, :] for a in range(line) for b in range(2)]
        top = tops[0]
        for value in tops[1:]:
            top = jnp.maximum(top, value)
        total = jnp.zeros_like(top)
        for peak, part in zip(tops, totals):
            total = total + part * jnp.exp(peak - top)
        lse = top + jnp.log(total)
        lse_out[place] = lse
        factor = jnp.exp(stats[me_line, me_pair, place, 0:1, :] - lse) / length
        wanted = targets[place]

        @pl.loop(0, 4)
        def _(tile):
            rows = pl.ds(pl.multiple_of(tile * padded, padded), padded)
            entry = vocabulary(tile, padded)
            grad = probs[rows, group(place)].astype(f32) * factor
            grad = (grad - jnp.where(entry == wanted, 1.0 / length, 0.0)).astype(bf16)
            probs[rows, group(place)] = grad
            product = lax.dot_general(
                grad, table[rows, :], (((0,), (0,)), ((), ())), preferred_element_type=f32
            )

            @pl.when(tile == 0)
            def _():
                acc[...] = product

            @pl.when((tile > 0) & (tile < 3))
            def _():
                acc[...] += product

            @pl.when(tile == 3)
            def _():
                parts[place] = (acc[...] + product).astype(bf16)

        sum_copy(turn).start()

        @pl.when(turn > 0)
        def _():
            finish(turn - 1)
            line_copy(turn - 1).start()

    gh_rows = 256
    gh_tiles = 4 * padded // gh_rows

    def head_grads(first, last):
        @pl.loop(first, last)
        def _(tile):
            rows = pl.ds(pl.multiple_of(tile * gh_rows, gh_rows), gh_rows)
            value = jnp.dot(probs[rows, :], rows_all[...], preferred_element_type=f32)
            grads[rows, :] = value.astype(bf16)

    head_grads(0, gh_tiles // 2)
    finish(line - 1)
    for turn in range(line - 1):
        line_copy(turn).wait_recv()
    own = parts.at[me_line, side(me_pair)]

    @pl.loop(0, half // 16)
    def _(block):
        rows = pl.ds(pl.multiple_of(block * 16, 16), 16)
        value = own[rows, :].astype(f32)
        for turn in range(line - 1):
            value = value + from_line[turn, rows, :].astype(f32)
        done[rows, :] = value.astype(bf16)

    back = remote(done, out.at[pl.ds(0, half)], back_send, back_recv, section_peer)

    @pl.when(me_section == 0)
    def _():
        back.start()
        out[...] = jnp.zeros_like(out)

    @pl.when(me_section == 1)
    def _():
        out[pl.ds(half, half), :] = done[...]

    head_grads(gh_tiles // 2, gh_tiles)

    @pl.when(me_section == 0)
    def _():
        back.wait_send()

    @pl.when(me_section == 1)
    def _():
        back.wait_recv()
        give.wait_send()

    for way in (1, -1):
        for step in range(line - 1):

            @pl.when(sends_along(step, way))
            def _():
                along(step, way).wait_send()

    for place in range(line):
        sideways(place).wait_send()
        for n in range(len(chip_peers)):
            stat_copy(n, place).wait_send()
    for turn in range(line):
        sum_copy(turn).wait_send()
    for turn in range(line - 1):
        line_copy(turn).wait_send()


def head_pass(final, targets, heads, line, head_rows, length, collective_id):
    tokens, deep = final.shape
    half = tokens // 2
    padded = heads[0].shape[0]
    vmem = pl.BlockSpec(memory_space=pltpu.VMEM)
    anywhere = pl.BlockSpec(memory_space=pl.ANY)
    dma = pltpu.SemaphoreType.DMA
    peers = 2 * line - 1
    return pl.pallas_call(
        partial(head_kernel, line, head_rows, length),
        out_shape=[
            jax.ShapeDtypeStruct((tokens, deep), bf16),
            jax.ShapeDtypeStruct((4 * padded, deep), bf16),
            jax.ShapeDtypeStruct((line, 1, tokens), f32),
            jax.ShapeDtypeStruct((line, 1, tokens), f32),
        ],
        in_specs=[vmem, vmem] + [anywhere] * 4,
        out_specs=[vmem] * 4,
        scratch_shapes=[
            pltpu.VMEM((4 * padded, deep), bf16),
            pltpu.VMEM((line * tokens, deep), bf16),
            pltpu.VMEM((4 * padded, tokens), f32),
            pltpu.VMEM((4 * padded, line * tokens), bf16),
            pltpu.VMEM((tokens, deep), f32),
            pltpu.VMEM((line, tokens, deep), bf16),
            pltpu.VMEM((line, half, deep), bf16),
            pltpu.VMEM((line - 1, half, deep), bf16),
            pltpu.VMEM((line, 2, line, 8, tokens), f32),
            pltpu.VMEM((half, deep), bf16),
            dma((4,)),
            dma,
            dma,
            dma,
            dma((2, line)),
            dma((2, line)),
            dma((line,)),
            dma((line,)),
            dma((peers, line)),
            dma((peers, line)),
            dma((line,)),
            dma((line,)),
            dma((line,)),
            dma((line,)),
            dma,
            dma,
        ],
        compiler_params=pltpu.CompilerParams(
            collective_id=collective_id, has_side_effects=True, vmem_limit_bytes=60 * 2**20
        ),
        cost_estimate=pl.CostEstimate(
            flops=24 * line * padded * tokens * deep, bytes_accessed=2**28, transcendentals=0
        ),
    )(final, targets, *heads)


def row_stats(values):
    centred = values - jnp.mean(values, -1, keepdims=True)
    factor = lax.rsqrt(jnp.mean(centred * centred, -1, keepdims=True) + epsilon)
    return centred * factor, factor


def nt(left, right):
    return lax.dot_general(left, right, (((1,), (1,)), ((), ())), preferred_element_type=f32)


def tn(left, right):
    return lax.dot_general(left, right, (((0,), (0,)), ((), ())), preferred_element_type=f32)


def two_heads(block):
    first = lax.broadcasted_iota(jnp.int32, block.shape, 1) < HEAD_DIM
    zero = jnp.zeros_like(block)
    return jnp.concatenate([jnp.where(first, block, zero), jnp.where(first, zero, block)], 0)


def one_block(stacked):
    rows = stacked.shape[0] // 2
    first = lax.broadcasted_iota(jnp.int32, (rows, stacked.shape[1]), 1) < HEAD_DIM
    return jnp.where(first, stacked[:rows], stacked[rows:])


def attention_weights(queries, keys):
    scores = nt(queries, keys) * (1.0 / math.sqrt(HEAD_DIM))
    exped = jnp.exp(scores - jnp.max(scores, -1, keepdims=True))
    return exped * (1.0 / jnp.sum(exped, -1, keepdims=True))


def loaded(sources, targets, sems):
    copies = [
        pltpu.make_async_copy(source.at[0], target, sems.at[n])
        for n, (source, target) in enumerate(zip(sources, targets))
    ]
    for copy in copies:
        copy.start()
    return copies


def tile_of(index, size):
    return pl.ds(pl.multiple_of(index * size, size), size)


def forward_kernel(full, seqs, *refs):
    x, scale, bias, *weights = refs[:7]
    refs = refs[7:]
    if full:
        out, joined, mixed, middle, entry_attn, entry_mlp, slope, hidden = refs[:8]
        refs = refs[8:]
    else:
        out, joined, mixed, middle, entry_attn, hidden = (refs[0],) + tuple(refs[-5:])
        entry_mlp = entry_attn
        refs = refs[1:]
    w_qkv, w_out, w_up, w_down, total, sems = refs[:6]
    width = x.shape[1]
    length = x.shape[0] // seqs
    load_qkv, load_out, load_up, load_down = loaded(weights, (w_qkv, w_out, w_up, w_down), sems)

    for seq in range(seqs):
        rows = pl.ds(seq * length, length)
        normed, _ = row_stats(x[rows, :])
        entry_attn[rows, :] = (normed * scale[seq, :, :width]).astype(bf16)

    load_qkv.wait()
    tile = 512

    @pl.loop(0, 3 * width // tile)
    def _(index):
        cols = tile_of(index, tile)
        joined[:, cols] = jnp.dot(
            entry_attn[...], w_qkv[:, cols], preferred_element_type=f32
        ).astype(bf16)

    pairs = width // 128

    @pl.loop(0, pairs)
    def _(pair):
        cols = tile_of(pair, 128)
        for seq in range(seqs):
            rows = pl.ds(seq * length, length)
            queries = two_heads(joined[rows, cols])
            keys = joined[rows, tile_of(pair + pairs, 128)]
            values = joined[rows, tile_of(pair + 2 * pairs, 128)]
            probs = attention_weights(queries, keys).astype(bf16)
            mixed[rows, cols] = one_block(
                jnp.dot(probs, values, preferred_element_type=f32)
            ).astype(bf16)

    load_out.wait()

    @pl.loop(0, width // tile)
    def _(index):
        cols = tile_of(index, tile)
        middle[:, cols] = x[:, cols] + jnp.dot(
            mixed[...], w_out[:, cols], preferred_element_type=f32
        )

    for seq in range(seqs):
        rows = pl.ds(seq * length, length)
        normed, _ = row_stats(middle[rows, :])
        entry_mlp[rows, :] = (normed * scale[seq, :, width:]).astype(bf16)

    load_up.wait()
    load_down.wait()
    total[...] = middle[...]

    def gelu_of(up, cols):
        below = 0.5 + 0.5 * lax.erf(up * math.sqrt(0.5))
        if full:
            density = jnp.exp(-0.5 * up * up) * (1.0 / math.sqrt(2.0 * math.pi))
            slope[:, cols] = (below + up * density).astype(bf16)
        value = (up * below).astype(bf16)
        if full:
            hidden[:, cols] = value
        return value

    @pl.loop(0, w_up.shape[1] // (2 * tile))
    def _(index):
        ups = []
        for side in range(2):
            cols = tile_of(2 * index + side, tile)
            ups.append(
                jnp.dot(entry_mlp[...], w_up[:, cols], preferred_element_type=f32) + bias[:, cols]
            )
        gelus = [gelu_of(up, tile_of(2 * index + side, tile)) for side, up in enumerate(ups)]
        both = jnp.concatenate(gelus, 1)
        total[...] += jnp.dot(both, w_down[tile_of(index, 2 * tile), :], preferred_element_type=f32)

    out[...] = total[...].astype(bf16)


def layer_scratch(width, hidden):
    return [
        pltpu.VMEM((width, 3 * width), bf16),
        pltpu.VMEM((width, width), bf16),
        pltpu.VMEM((width, hidden), bf16),
        pltpu.VMEM((hidden, width), bf16),
    ]


def forward_pass(stream, scale, weights, full):
    w_qkv, w_out, w_up, b_hidden, w_down = weights
    tokens, width = stream.shape
    wide = w_up.shape[-1]
    vmem = pl.BlockSpec(memory_space=pltpu.VMEM)
    anywhere = pl.BlockSpec(memory_space=pl.ANY)

    def low(columns):
        return (tokens, columns), bf16

    kept = [
        low(3 * width),
        low(width),
        ((tokens, width), f32),
        low(width),
        low(width),
        low(wide),
        low(wide),
    ]
    out_shape = [jax.ShapeDtypeStruct((tokens, width), bf16)]
    scratch = layer_scratch(width, wide)
    scratch += [pltpu.VMEM((tokens, width), f32), pltpu.SemaphoreType.DMA((4,))]
    if full:
        out_shape += [jax.ShapeDtypeStruct(*item) for item in kept]
    else:
        scratch += [pltpu.VMEM(*kept[n]) for n in (0, 1, 2, 3, 6)]
    flops = 2 * tokens * (4 * width * width + 2 * width * wide)
    return pl.pallas_call(
        partial(forward_kernel, full, scale.shape[0]),
        out_shape=out_shape,
        in_specs=[vmem] * 3 + [anywhere] * 4,
        out_specs=[vmem] * len(out_shape),
        scratch_shapes=scratch,
        compiler_params=pltpu.CompilerParams(vmem_limit_bytes=60 * 2**20),
        cost_estimate=pl.CostEstimate(flops=2 * flops, bytes_accessed=2**25, transcendentals=0),
    )(stream, scale, b_hidden, w_qkv, w_out, w_up, w_down)


def backward_kernel(full, seqs, *refs):
    grad_out, x, scale, joined, middle, slope, *weights = refs[:10]
    refs = refs[10:]
    if full:
        out, grad_low, grad_up, grad_attn, grad_joined, grad_cond, grad_bias = refs[:7]
        refs = refs[7:]
    else:
        out, grad_low, grad_up, grad_attn, grad_joined = (refs[0],) + tuple(refs[-4:])
        refs = refs[1:]
    w_qkv, w_out, w_up, w_down, total, grad_middle, grad_mixed, sems = refs[:8]
    width = x.shape[1]
    length = x.shape[0] // seqs
    load_down, load_up, load_out, load_qkv = loaded(
        (weights[3], weights[2], weights[1], weights[0]), (w_down, w_up, w_out, w_qkv), sems
    )
    grad_low[...] = grad_out[...].astype(bf16)
    load_down.wait()
    load_up.wait()
    tile = 1024

    @pl.loop(0, w_up.shape[1] // tile)
    def _(index):
        cols = tile_of(index, tile)
        grad_hidden = nt(grad_low[...], w_down[cols, :])
        value = (grad_hidden * slope[:, cols].astype(f32)).astype(bf16)
        grad_up[:, cols] = value
        if full:
            grad_bias[:, cols] = jnp.sum(value.astype(f32), 0, keepdims=True)
        product = nt(value, w_up[:, cols])

        @pl.when(index == 0)
        def _():
            total[...] = product

        @pl.when(index > 0)
        def _():
            total[...] += product

    def norm_grads(source, half, onto, store):
        for seq in range(seqs):
            rows = pl.ds(seq * length, length)
            normed, factor = row_stats(source[rows, :])
            gradient = total[rows, :]
            cols = pl.ds(half * width, width)
            if full:
                grad_cond[seq, :, cols] = jnp.sum(gradient * normed, 0, keepdims=True)
            scaled = gradient * scale[seq, :, cols]
            back = factor * (
                scaled
                - jnp.mean(scaled, -1, keepdims=True)
                - normed * jnp.mean(scaled * normed, -1, keepdims=True)
            )
            store(rows, onto[rows, :] + back)

    def store_middle(rows, value):
        grad_middle[rows, :] = value
        grad_attn[rows, :] = value.astype(bf16)

    norm_grads(middle, 1, grad_out, store_middle)
    load_out.wait()
    grad_mixed[...] = nt(grad_attn[...], w_out[...]).astype(bf16)
    pairs = width // 128
    shrink = 1.0 / math.sqrt(HEAD_DIM)

    @pl.loop(0, pairs)
    def _(pair):
        cols = tile_of(pair, 128)
        key_cols = tile_of(pair + pairs, 128)
        value_cols = tile_of(pair + 2 * pairs, 128)
        for seq in range(seqs):
            rows = pl.ds(seq * length, length)
            queries = two_heads(joined[rows, cols])
            keys = joined[rows, key_cols]
            values = joined[rows, value_cols]
            probs = attention_weights(queries, keys)
            grads = two_heads(grad_mixed[rows, cols])
            grad_probs = nt(grads, values)
            inner = jnp.sum(grad_probs * probs, -1, keepdims=True)
            grad_scores = (probs * (grad_probs - inner)).astype(bf16)
            grad_query = one_block(jnp.dot(grad_scores, keys, preferred_element_type=f32))
            grad_joined[rows, cols] = (grad_query * shrink).astype(bf16)
            grad_joined[rows, key_cols] = (tn(grad_scores, queries) * shrink).astype(bf16)
            grad_joined[rows, value_cols] = tn(probs.astype(bf16), grads).astype(bf16)

    load_qkv.wait()
    part = 256

    @pl.loop(0, width // part)
    def _(index):
        total[:, tile_of(index, part)] = nt(grad_joined[...], w_qkv[tile_of(index, part), :])

    def store_out(rows, value):
        out[rows, :] = value.astype(bf16)

    norm_grads(x, 0, grad_middle, store_out)


def backward_pass(grad_out, stream, scale, kept, weights, full):
    w_qkv, w_out, w_up, _, w_down = weights
    joined, _, middle, _, _, slope, _ = kept
    tokens, width = stream.shape
    wide = w_up.shape[-1]
    seqs = scale.shape[0]
    vmem = pl.BlockSpec(memory_space=pltpu.VMEM)
    anywhere = pl.BlockSpec(memory_space=pl.ANY)
    lows = [
        ((tokens, width), bf16),
        ((tokens, wide), bf16),
        ((tokens, width), bf16),
        ((tokens, 3 * width), bf16),
    ]
    out_shape = [jax.ShapeDtypeStruct((tokens, width), bf16)]
    scratch = layer_scratch(width, wide)
    scratch += [
        pltpu.VMEM((tokens, width), f32),
        pltpu.VMEM((tokens, width), f32),
        pltpu.VMEM((tokens, width), bf16),
        pltpu.SemaphoreType.DMA((4,)),
    ]
    if full:
        out_shape += [jax.ShapeDtypeStruct(*item) for item in lows]
        out_shape.append(jax.ShapeDtypeStruct((seqs, 1, 2 * width), f32))
        out_shape.append(jax.ShapeDtypeStruct((1, wide), f32))
    else:
        scratch += [pltpu.VMEM(*item) for item in lows]
    flops = 2 * tokens * (4 * width * width + 2 * width * wide)
    return pl.pallas_call(
        partial(backward_kernel, full, seqs),
        out_shape=out_shape,
        in_specs=[vmem] * 6 + [anywhere] * 4,
        out_specs=[vmem] * len(out_shape),
        scratch_shapes=scratch,
        compiler_params=pltpu.CompilerParams(vmem_limit_bytes=60 * 2**20),
        cost_estimate=pl.CostEstimate(flops=2 * flops, bytes_accessed=2**25, transcendentals=0),
    )(grad_out, stream, scale, joined, middle, slope, w_qkv, w_out, w_up, w_down)


def norm_rows(values):
    centred = values - jnp.mean(values, -1, keepdims=True)
    factor = lax.rsqrt(jnp.mean(centred * centred, -1, keepdims=True) + epsilon)
    return (centred * factor, factor)


def norm_back(gradient, normed, factor):
    return factor * (
        gradient
        - jnp.mean(gradient, -1, keepdims=True)
        - normed * jnp.mean(gradient * normed, -1, keepdims=True)
    )


def time_features(noise_level):
    half_width = TFEAT // 2
    rates = jnp.exp(jnp.arange(half_width, dtype=f32) * (math.log(1000.0) / half_width))
    angles = (jnp.log(noise_level) / 4.0)[:, None] * rates[None, :]
    return jnp.concatenate([jnp.cos(angles), jnp.sin(angles)], -1)


def levels_of(bins, table):
    hits = bins[:, None] == jnp.arange(table.shape[0])[None, :]
    return jnp.sum(jnp.where(hits, table[None, :], 0.0), -1)


def over_dp(part):
    part = part.reshape((part.shape[0] // 4, 2, 2) + part.shape[1:])
    part = lax.psum_scatter(part, "core", scatter_dimension=2)
    part = lax.psum_scatter(part, "pair", scatter_dimension=1)
    return lax.psum_scatter(part, "line", scatter_dimension=0)


def by_owner(part):
    line = lax.axis_size("line")
    return part.astype(bf16).reshape((line, 2, 2, part.shape[0] // (line * 4)) + part.shape[1:])


def mm(spec, left, right):
    return jnp.einsum(spec, left, right, preferred_element_type=f32)


def layer_forward(stream, scale_attn, scale_mlp, weights):
    w_qkv, w_out, w_up, b_hidden, w_down = weights
    seq_count, length, model_width = stream.shape
    normed_attn, factor_attn = norm_rows(stream)
    attn_entry = (normed_attn * scale_attn).astype(bf16)
    joined = mm("nsd,de->nse", attn_entry, w_qkv).astype(bf16)
    qkv_parts = joined.reshape(seq_count, length, 3, HEADS, HEAD_DIM)
    query_rows = qkv_parts[:, :, 0]
    key_rows = qkv_parts[:, :, 1]
    value_rows = qkv_parts[:, :, 2]
    scores = mm("nqhe,nkhe->nhqk", query_rows, key_rows) / math.sqrt(HEAD_DIM)
    exp_scores = jnp.exp(scores - jnp.max(scores, -1, keepdims=True))
    attn_probs = exp_scores / jnp.sum(exp_scores, -1, keepdims=True)
    probs_low = attn_probs.astype(bf16)
    attn_mixed = mm("nhqk,nkhe->nqhe", probs_low, value_rows).astype(bf16)
    attn_mixed = attn_mixed.reshape(seq_count, length, model_width)
    middle = stream + mm("nsd,de->nse", attn_mixed, w_out)
    normed_mlp, factor_mlp = norm_rows(middle)
    mlp_entry = (normed_mlp * scale_mlp).astype(bf16)
    up_proj = mm("nsd,df->nsf", mlp_entry, w_up) + b_hidden
    below = 0.5 + 0.5 * lax.erf(up_proj * math.sqrt(0.5))
    hidden = (up_proj * below).astype(bf16)
    density = jnp.exp(-0.5 * up_proj * up_proj) * (1.0 / math.sqrt(2.0 * math.pi))
    slope = (below + up_proj * density).astype(bf16)
    block_out = middle + mm("nsf,fd->nsd", hidden, w_down)
    kept = (
        normed_attn,
        factor_attn,
        attn_entry,
        query_rows,
        key_rows,
        value_rows,
        attn_probs,
        probs_low,
        attn_mixed,
        normed_mlp,
        factor_mlp,
        mlp_entry,
        slope,
        hidden,
    )
    return (block_out, kept)


def layer_backward(grad_out, kept, scale_attn, scale_mlp, weights, whole):
    w_qkv, w_out, w_up, b_hidden, w_down = weights
    (
        normed_attn,
        factor_attn,
        attn_entry,
        query_rows,
        key_rows,
        value_rows,
        attn_probs,
        probs_low,
        attn_mixed,
        normed_mlp,
        factor_mlp,
        mlp_entry,
        slope,
        hidden,
    ) = kept
    seq_count, length, model_width = grad_out.shape
    grads = {}
    grad_branch = grad_out.astype(bf16)
    if whole:
        grads["down"] = by_owner(mm("nsf,nsd->fd", hidden, grad_branch))
    grad_hidden = mm("nsd,fd->nsf", grad_branch, w_down)
    grad_up_proj = (grad_hidden * slope.astype(f32)).astype(bf16)
    if whole:
        grads["bias"] = jnp.sum(grad_up_proj.astype(f32), (0, 1))
        grads["up"] = by_owner(mm("nsd,nsf->df", mlp_entry, grad_up_proj))
    grad_entry = mm("nsf,df->nsd", grad_up_proj, w_up)
    grad_middle = grad_out + norm_back(grad_entry * scale_mlp, normed_mlp, factor_mlp)
    grad_attn = grad_middle.astype(bf16)
    if whole:
        grads["out"] = by_owner(mm("nsd,nse->de", attn_mixed, grad_attn))
    grad_mixed = mm("nse,de->nsd", grad_attn, w_out)
    grad_mixed = grad_mixed.astype(bf16).reshape(seq_count, length, HEADS, HEAD_DIM)
    grad_probs = mm("nqhe,nkhe->nhqk", grad_mixed, value_rows)
    grad_values = mm("nhqk,nqhe->nkhe", probs_low, grad_mixed)
    grad_scores = (
        attn_probs * (grad_probs - jnp.sum(grad_probs * attn_probs, -1, keepdims=True))
    ).astype(bf16)
    grad_query = mm("nhqk,nkhe->nqhe", grad_scores, key_rows) / math.sqrt(HEAD_DIM)
    grad_keys = mm("nhqk,nqhe->nkhe", grad_scores, query_rows) / math.sqrt(HEAD_DIM)
    grad_joined = jnp.stack([grad_query, grad_keys, grad_values], 2).astype(bf16)
    grad_joined = grad_joined.reshape(seq_count, length, 3 * model_width)
    if whole:
        grads["qkv"] = by_owner(mm("nsd,nse->de", attn_entry, grad_joined))
    grad_attn_entry = mm("nse,de->nsd", grad_joined, w_qkv)
    grad_stream = grad_middle + norm_back(grad_attn_entry * scale_attn, normed_attn, factor_attn)
    if whole:
        grads["cond"] = jnp.concatenate(
            [jnp.sum(grad_attn_entry * normed_attn, 1), jnp.sum(grad_entry * normed_mlp, 1)], -1
        )
    return (grad_stream, grads)


def local(
    token_ids,
    target_ids,
    time_bins,
    sigma_table,
    noise,
    embed,
    w_in,
    w_time,
    norm_gain,
    w_qkv,
    w_out,
    w_up,
    b_hidden,
    w_down,
    out_gain,
    head,
):
    section = lax.axis_index("section")
    line_at = lax.axis_index("line")
    pair_at = lax.axis_index("pair")
    core = lax.axis_index("core")
    sections = lax.axis_size("section")
    line = lax.axis_size("line")
    chip = line_at * 2 + pair_at
    chips = line * 2
    cores = 2
    dp_count = chips * cores
    dp_index = chip * cores + core
    is_first = section == 0
    seqs, length = token_ids.shape
    tokens = seqs * length
    half = tokens // sections
    model_width = w_out.shape[-1]
    emb_rows, emb_width = embed.shape
    straight = line <= 4 and half % 16 == 0 and model_width // dp_count % 16 == 0

    own_ids = jnp.concatenate([token_ids.reshape(-1), target_ids.reshape(-1), time_bins])
    if straight:
        padded = jnp.pad(own_ids, (0, -own_ids.shape[0] % 1024)).reshape(-1, 128)
        all_ids = gathered_small(padded, line, 0).reshape(dp_count, -1)[:, : own_ids.shape[0]]
    else:
        all_ids = lax.all_gather(own_ids, DP)
    all_tokens = all_ids[:, :tokens]
    all_targets = all_ids[:, tokens : 2 * tokens]
    all_bins = all_ids[:, 2 * tokens :].reshape(-1)

    own_rows = dp_index * emb_rows + jnp.arange(emb_rows)
    half_tokens = lax.dynamic_slice_in_dim(all_tokens, section * half, half, 1)
    picked = (half_tokens.reshape(-1)[:, None] == own_rows[None, :]).astype(bf16)
    found = jnp.dot(picked, embed, preferred_element_type=f32).astype(bf16)
    if straight:
        found = found.reshape(line, 2, 2, half, emb_width)
        (embedded,) = summed_over_dp([found], 1, swap=True)
    else:
        embedded = lax.all_gather(over_dp(found.reshape(dp_count, half, emb_width)), "section")
    embedded = embedded.astype(f32).reshape(seqs, length, emb_width)

    head_rows = head.shape[0]
    swapped = [(0, 1), (1, 0)]
    if straight:
        head_own = jnp.pad(head, ((0, -head_rows % 512), (0, 0)))
        head_core = lax.ppermute(head_own, "core", swapped)
        head_section = lax.ppermute(head_own, "section", swapped)
    else:
        head_group = lax.all_gather(lax.all_gather(head, "core"), "section")
        head_group = head_group.reshape(-1, model_width)
        vocab_base = (
            (jnp.arange(sections)[:, None] * chips + chip) * cores + jnp.arange(cores)[None, :]
        ) * head_rows
        columns = (vocab_base[:, :, None] + jnp.arange(head_rows)[None, None, :]).reshape(-1)

    noise_level = levels_of(time_bins, sigma_table)
    unit_factor = lax.rsqrt(jnp.mean(embedded * embedded, -1, keepdims=True) + epsilon)
    level_col = noise_level[:, None, None]
    noise_scale = lax.rsqrt(level_col * level_col + 1.0)
    noisy_rows = ((embedded * unit_factor + level_col * noise) * noise_scale).astype(bf16)
    time_feats = time_features(noise_level)
    conditioned = jnp.dot(time_feats, w_time[0].astype(f32), precision=highest) + norm_gain[0]
    scale_attn = conditioned[:, None, :model_width]
    scale_mlp = conditioned[:, None, model_width:]
    scale = conditioned[:, None, :]
    weights = (w_qkv[0], w_out[0], w_up[0], b_hidden[0], w_down[0])
    stacked = (w_qkv, w_out, w_up, b_hidden, w_down)
    if straight:
        noisy_rows, head_core, head_section = lax.optimization_barrier(
            (noisy_rows, head_core, head_section)
        )
        heads = [head_own, head_core, head_section, lax.ppermute(head_section, "core", swapped)]

    stream0 = mm("nse,ed->nsd", noisy_rows, w_in)
    if straight:
        (first_out,) = forward_pass(stream0.reshape(tokens, model_width), scale, stacked, False)
        first_out = first_out.reshape(stream0.shape)
    else:
        first_out = layer_forward(stream0, scale_attn, scale_mlp, weights)[0].astype(bf16)
    arrived = lax.ppermute(first_out, "section", swapped)
    stream = jnp.where(is_first, stream0, arrived.astype(f32))
    if straight:
        flat_stream = stream.reshape(tokens, model_width)
        block_out, *kept = forward_pass(flat_stream, scale, stacked, True)
        block_out = block_out.reshape(stream0.shape)
    else:
        block_out, kept = layer_forward(stream, scale_attn, scale_mlp, weights)
        block_out = block_out.astype(bf16)

    top_stream = block_out.astype(f32)
    final_normed, final_factor = norm_rows(top_stream)
    final_rows = (final_normed * out_gain).astype(bf16).reshape(tokens, model_width)
    targets_group = lax.dynamic_slice_in_dim(
        all_targets.reshape(chips, cores, tokens), core, 1, 1
    )[:, 0]
    targets_group = lax.dynamic_slice_in_dim(targets_group, section * half, half, 1)
    if straight:
        grad_final, grad_head, lse, picks = head_pass(
            final_rows, targets_group.reshape(line, 1, tokens), heads, line, head_rows, length, 3
        )
        ce_part = jnp.sum(lse) / chips - jnp.sum(picks)
    else:
        targets_group = targets_group.reshape(-1)
        handed = lax.ppermute(final_rows[:half], "section", [(1, 0), (0, 1)])
        own_final = jnp.where(is_first, handed, final_rows[half:])
        group_final = lax.all_gather(own_final, ("line", "pair"), tiled=True)
        logits = mm("td,vd->tv", group_final, head_group)
        local_top = jnp.max(logits, -1)
        local_total = jnp.sum(jnp.exp(logits - local_top[:, None]), -1)
        mark = columns[None, :] == targets_group[:, None]
        local_pick = jnp.sum(jnp.where(mark, logits, 0.0))
        stats = lax.all_gather(jnp.stack([local_top, local_total]), ("line", "pair"))
        all_top = jnp.max(stats[:, 0], 0)
        all_total = jnp.sum(stats[:, 1] * jnp.exp(stats[:, 0] - all_top), 0)
        log_total = all_top + jnp.log(all_total)
        soft_rows = jnp.exp(logits - log_total[:, None])
        logit_grads = ((soft_rows - jnp.where(mark, 1.0, 0.0)) / length).astype(bf16)
        grad_final = jnp.dot(logit_grads, head_group, preferred_element_type=f32).astype(bf16)
        grad_final = lax.psum_scatter(grad_final, ("line", "pair"), scatter_dimension=0, tiled=True)
        handed = lax.ppermute(grad_final, "section", swapped)
        grad_final = jnp.concatenate([handed, grad_final], 0)
        grad_head = mm("tv,td->vd", logit_grads, group_final).astype(bf16)
        grad_head = grad_head.reshape(sections, cores, head_rows, model_width)
        grad_head = lax.psum_scatter(grad_head, "core", scatter_dimension=1)
        grad_head = lax.psum_scatter(grad_head, "section", scatter_dimension=0).astype(f32)

        ce_part = jnp.sum(log_total) / chips - local_pick
    grad_final = grad_final.astype(f32).reshape(seqs, length, model_width)
    out_part = jnp.where(is_first, 0.0, jnp.sum(grad_final * final_normed, (0, 1)))

    grad_top = norm_back(grad_final * out_gain, final_normed, final_factor)
    if straight:
        (grad_second,) = backward_pass(
            grad_top.reshape(tokens, model_width), flat_stream, scale, kept, stacked, False
        )
        grad_second = grad_second.reshape(stream0.shape)
    else:
        grad_second = layer_backward(grad_top, kept, scale_attn, scale_mlp, weights, False)[0]
        grad_second = grad_second.astype(bf16)
    returned = lax.ppermute(grad_second, "section", swapped)
    grad_cot = jnp.where(is_first, returned.astype(f32), grad_top)
    if straight:
        grad_first, grad_branch, grad_up, grad_attn, grad_joined, grad_cond, grad_bias = (
            backward_pass(
                grad_cot.reshape(tokens, model_width), flat_stream, scale, kept, stacked, True
            )
        )
        grad_first = grad_first.reshape(stream0.shape)
        _, mixed, _, entry_attn, entry_mlp, _, hidden = kept
        grads = {
            "down": by_owner(mm("tf,td->fd", hidden, grad_branch)),
            "up": by_owner(mm("td,tf->df", entry_mlp, grad_up)),
            "qkv": by_owner(mm("td,te->de", entry_attn, grad_joined)),
            "out": by_owner(mm("td,te->de", mixed, grad_attn)),
            "cond": grad_cond,
            "bias": grad_bias.reshape(-1),
        }
    else:
        grad_stream, grads = layer_backward(grad_cot, kept, scale_attn, scale_mlp, weights, True)
        grad_first = grad_stream.astype(bf16)

    in_part = mm("nse,nsd->ed", noisy_rows, grad_first).astype(bf16)
    in_part = in_part.reshape(sections, line, 2, 2, -1, model_width)
    in_part = jnp.moveaxis(in_part, 0, 3).reshape(line, 2, 2, -1, model_width)
    grad_noisy = mm("nsd,ed->nse", grad_first, w_in)
    grad_unit = grad_noisy * noise_scale
    cubed = unit_factor * unit_factor * unit_factor
    grad_embedded = unit_factor * grad_unit - cubed * embedded * jnp.mean(
        grad_unit * embedded, -1, keepdims=True
    )
    grad_flat = grad_embedded.reshape(tokens, emb_width)

    ce_high = ce_part.astype(bf16).astype(f32)
    ce_mid = (ce_part - ce_high).astype(bf16).astype(f32)
    ce_low = ce_part - ce_high - ce_mid
    shared = jnp.concatenate([out_part, jnp.stack([ce_high, ce_mid, ce_low])])
    shared_rows = -(-shared.shape[0] // emb_width)
    shared = jnp.pad(shared, (0, shared_rows * emb_width - shared.shape[0]))
    handing = jnp.concatenate([grad_flat, shared.reshape(-1, emb_width)], 0).astype(bf16)
    handed = lax.ppermute(handing, "section", swapped)
    kept_rows = jnp.where(is_first, handing[:half], handed[half:tokens])
    layer_small = jnp.concatenate([grads["cond"].reshape(-1), grads["bias"]])
    layer_rows = layer_small.shape[0] // emb_width
    small = jnp.concatenate(
        [
            layer_small.astype(bf16).reshape(layer_rows, emb_width),
            handing[tokens:],
            handed[tokens:],
        ],
        0,
    )
    small = jnp.pad(small, ((0, -small.shape[0] % 16), (0, 0)))
    parts = [grads["down"], grads["up"], grads["qkv"], grads["out"], in_part]
    if straight:
        *sums, smalls, halves, grad_head = summed_over_dp(
            parts, 2, packets=(small, kept_rows), head_part=grad_head, head_rows=head_rows
        )
    else:
        sums = [over_dp(part.reshape((dp_count,) + part.shape[3:])).astype(f32) for part in parts]
        smalls = lax.all_gather(small, DP)
        halves = lax.all_gather(kept_rows, ("section",) + DP)
    grad_down, grad_up, grad_qkv, grad_wout, in_sum = sums
    in_sum = in_sum.reshape(sections, -1, model_width)
    in_handed = lax.ppermute(in_sum[1], "section", swapped)
    grad_w_in = jnp.where(is_first, in_sum[0], in_handed)

    grad_all = halves.reshape(-1, emb_width)
    tokens_all = all_tokens.reshape(dp_count, sections, half).swapaxes(0, 1).reshape(-1)
    out_rows = emb_rows // sections
    target_rows = (section * dp_count + dp_index) * out_rows + jnp.arange(out_rows)
    place = (target_rows[:, None] == tokens_all[None, :]).astype(bf16)
    grad_embed = jnp.dot(place, grad_all, preferred_element_type=f32)

    smalls = smalls.reshape(dp_count, -1, emb_width).astype(f32)
    layer_small = smalls[:, :layer_rows].reshape(dp_count, -1)
    cond_size = grads["cond"].size
    cond_all = layer_small[:, :cond_size].reshape(dp_count * seqs, 2 * model_width)
    hidden_rows = grads["bias"].shape[0] // dp_count
    grad_bias = jnp.sum(
        lax.dynamic_slice_in_dim(layer_small, cond_size + dp_index * hidden_rows, hidden_rows, 1), 0
    )
    norm_cols = 2 * model_width // dp_count
    grad_gain = jnp.sum(lax.dynamic_slice_in_dim(cond_all, dp_index * norm_cols, norm_cols, 1), 0)
    feats_all = time_features(levels_of(all_bins, sigma_table))
    feat_rows = TFEAT // dp_count
    feats_own = lax.dynamic_slice_in_dim(feats_all, dp_index * feat_rows, feat_rows, 1)
    grad_time = jnp.dot(feats_own.T, cond_all, precision=highest)
    both = smalls[:, layer_rows : layer_rows + 2 * shared_rows]
    both = jnp.sum(both.reshape(dp_count, 2, -1), (0, 1))
    loss = jnp.sum(both[model_width : model_width + 3]) / (tokens * dp_count)
    gain_rows = model_width // dp_count
    grad_out_gain = lax.dynamic_slice_in_dim(both, dp_index * gain_rows, gain_rows)
    return (
        loss,
        grad_embed,
        grad_w_in,
        grad_time[None],
        grad_gain[None],
        grad_qkv[None],
        grad_wout[None],
        grad_up[None],
        grad_bias[None],
        grad_down[None],
        grad_out_gain,
        grad_head,
    )


def solution(mesh):
    sections, dp_count = mesh.shape["section"], mesh.shape["dp"]
    fine = Mesh(mesh.devices.reshape(sections, dp_count // 4, 2, 2), ("section",) + DP)
    everywhere = ("section",) + DP
    in_specs = (
        P(DP, None),
        P(DP, None),
        P(DP),
        P(),
        P(DP, None, None),
        P(DP, None),
        P(),
        P("section", None, None),
        P("section", None),
        P("section", None, None),
        P("section", None, None),
        P("section", None, None),
        P("section", None),
        P("section", None, None),
        P(),
        P(everywhere, None),
    )
    out_specs = (
        P(),
        P(everywhere, None),
        P(everywhere, None),
        P("section", DP, None),
        P("section", DP),
        P("section", DP, None),
        P("section", DP, None),
        P("section", DP, None),
        P("section", DP),
        P("section", DP, None),
        P(DP),
        P(everywhere, None),
    )
    return jax.shard_map(local, mesh=fine, in_specs=in_specs, out_specs=out_specs, check_vma=False)
```

```python
from functools import partial
import math

import jax
import jax.numpy as jnp
from jax import lax
from jax.experimental import pallas as pl
from jax.experimental.pallas import tpu as pltpu
from jax.sharding import Mesh, PartitionSpec as P

HEADS = 16
HEAD_DIM = 64
TFEAT = 256

epsilon = 1e-05
highest = lax.Precision.HIGHEST
f32 = jnp.float32
bf16 = jnp.bfloat16
DP = ("line", "pair", "core")


MESH = pl.DeviceIdType.MESH


def nt(left, right):
    return lax.dot_general(left, right, (((1,), (1,)), ((), ())), preferred_element_type=f32)


def tn(left, right):
    return lax.dot_general(left, right, (((0,), (0,)), ((), ())), preferred_element_type=f32)


def nn(left, right):
    return jnp.dot(left, right, preferred_element_type=f32)


def greet(peers):
    barrier = pltpu.get_barrier_semaphore()
    for peer in peers:
        pl.semaphore_signal(barrier, inc=1, device_id=peer, device_id_type=MESH)
    pl.semaphore_wait(barrier, len(peers))


def remote(source, target, send, recv, peer):
    return pltpu.make_async_remote_copy(
        src_ref=source,
        dst_ref=target,
        send_sem=send,
        recv_sem=recv,
        device_id=peer,
        device_id_type=MESH,
    )


def ring_place(position, line):
    turned = position // line
    return position * (1 - turned) + (2 * line - 1 - position) * turned, turned


def sum_kernel(shapes, line, half_rows, with_head, *refs):
    count = len(shapes)
    with_packet = half_rows > 0
    refs = list(refs)

    def take(number):
        return [refs.pop(0) for _ in range(number)]

    parts = take(count)
    sent = take(2) if with_packet else []
    head_part = take(1)[0] if with_head else None
    outs = take(count)
    smalls, halves = take(2) if with_packet else (None, None)
    head_out = take(1)[0] if with_head else None
    own, from_core, slots = take(count), take(count), take(count)
    load_sem, core_send, core_recv, ring_send, ring_recv = take(5)
    if with_packet:
        own_sem, packet_send, packet_recv, wide_send, wide_recv, half_send, half_recv = take(7)
    if with_head:
        head_own, head_core, head_section, head_sem, head_send, head_recv = take(6)
    last_total, cross_send, cross_recv = take(3)

    chips = 2 * line
    me_section = lax.axis_index("section")
    me_line = lax.axis_index("line")
    me_pair = lax.axis_index("pair")
    me_core = lax.axis_index("core")
    position = me_line + me_pair * (chips - 1 - 2 * me_line)
    section_peer = {"section": 1 - me_section}
    core_peer = {"core": 1 - me_core}
    ways = (1, -1)
    ring_peers = []
    for way in ways:
        peer_line, peer_pair = ring_place(lax.rem(position + way + chips, chips), line)
        ring_peers.append({"line": peer_line, "pair": peer_pair})
    greet([core_peer, section_peer] + ring_peers)

    def block_of(turn, step):
        ahead = lax.rem(position - ways[turn] * (1 + step) + 2 * chips, chips)
        return ring_place(ahead, line)

    def columns(index, turn):
        wide = shapes[index][-1] // 2
        return pl.ds(turn * wide, wide)

    def load(index, turn, step):
        place, pair = block_of(turn, step)
        cols = columns(index, turn)
        return pltpu.make_async_copy(
            parts[index].at[place, pair, me_core, :, cols],
            own[index].at[step, :, cols],
            load_sem.at[index, turn, step],
        )

    def core_copy(index, turn, step):
        place, pair = block_of(turn, step)
        cols = columns(index, turn)
        return remote(
            parts[index].at[place, pair, 1 - me_core, :, cols],
            from_core[index].at[step, :, cols],
            core_send.at[index, turn, step],
            core_recv.at[index, turn, step],
            core_peer,
        )

    def ring_copy(index, turn, step):
        cols = columns(index, turn)
        if isinstance(step, int) and step == 0:
            source = from_core[index].at[0, :, cols]
        else:
            source = slots[index].at[step - 1, :, cols]
        return remote(
            source,
            slots[index].at[step, :, cols],
            ring_send.at[index, turn, step],
            ring_recv.at[index, turn, step],
            ring_peers[turn],
        )

    def to_core(step):
        for index in range(count):
            for turn in range(2):
                load(index, turn, step).start()
                core_copy(index, turn, step).start()

    def stop(step):
        first = isinstance(step, int) and step == 0
        last = isinstance(step, int) and step == chips - 1
        for index in range(count):
            rows = shapes[index][-2]
            wide = shapes[index][-1] // 2
            tile = min(wide, 512)
            for turn in range(2):
                load(index, turn, step).wait()
                core_copy(index, turn, step).wait_recv()
                if not first:
                    ring_copy(index, turn, step - 1).wait_recv()

                @pl.loop(0, rows // 16)
                def _(block):
                    row = pl.ds(pl.multiple_of(block * 16, 16), 16)
                    for col in range(turn * wide, (turn + 1) * wide, tile):
                        cols = pl.ds(col, tile)
                        total = from_core[index][step, row, cols].astype(f32)
                        total = total + own[index][step, row, cols].astype(f32)
                        if not first:
                            total = total + slots[index][step - 1, row, cols].astype(f32)
                        if last and index == count - 1:
                            last_total[row, cols] = total
                        elif last:
                            outs[index][row, cols] = total
                        elif first:
                            from_core[index][0, row, cols] = total.astype(bf16)
                        else:
                            slots[index][step - 1, row, cols] = total.astype(bf16)

                if not last:
                    ring_copy(index, turn, step).start()

    hops = (line, line - 1)

    def packet_blocks(place, pair):
        return [smalls.at[place, pair, me_core], halves.at[me_section, place, pair, me_core]]

    def packet_hops(turn, hop, away):
        place, pair = ring_place(
            lax.rem(position - ways[turn] * (hop + away) + 2 * chips, chips), line
        )
        return [
            remote(
                block,
                block,
                packet_send.at[n, turn, hop],
                packet_recv.at[n, turn, hop],
                ring_peers[turn],
            )
            for n, block in enumerate(packet_blocks(place, pair))
        ]

    def pass_packets(hop):
        for turn in range(2):
            if 0 < hop <= hops[turn]:
                for copy in packet_hops(turn, hop - 1, 1):
                    copy.wait_recv()
            if hop < hops[turn]:
                for copy in packet_hops(turn, hop, 0):
                    copy.start()

    if with_packet:
        keeps = [
            pltpu.make_async_copy(block, target, own_sem.at[n])
            for n, (block, target) in enumerate(zip(sent, packet_blocks(me_line, me_pair)))
        ]
        for keep in keeps:
            keep.start()
        columns_of = [smalls.at[:, :, me_core], halves.at[me_section, :, :, me_core]]
        across = [
            remote(block, block, wide_send.at[n], wide_recv.at[n], core_peer)
            for n, block in enumerate(columns_of)
        ]
        half_swap = remote(
            halves.at[me_section], halves.at[me_section], half_send, half_recv, section_peer
        )

    if with_head:
        high = head_part.shape[0] // 4

        def shard(n):
            return head_part.at[pl.ds(n * high, high)]

        head_loads = [
            pltpu.make_async_copy(shard(2 * n), head_own.at[n], head_sem.at[n]) for n in range(2)
        ]
        head_copies = [
            remote(shard(2 * n + 1), head_core.at[n], head_send.at[n], head_recv.at[n], core_peer)
            for n in range(2)
        ]
        head_copies.append(
            remote(head_core.at[1], head_section, head_send.at[2], head_recv.at[2], section_peer)
        )

        def head_rows(body):
            @pl.loop(0, high // 16)
            def _(block):
                body(pl.ds(pl.multiple_of(block * 16, 16), 16))

        def head_over_cores():
            for copy in head_loads:
                copy.wait()
            for copy in head_copies[:2]:
                copy.wait_recv()

            def add(rows):
                value = head_core[1, rows, :].astype(f32) + head_own[1, rows, :].astype(f32)
                head_core[1, rows, :] = value.astype(bf16)

            head_rows(add)
            head_copies[2].start()

        def head_over_sections():
            head_copies[2].wait_recv()

            def total(rows):
                return (
                    head_core[0, rows, :].astype(f32)
                    + head_own[0, rows, :].astype(f32)
                    + head_section[rows, :].astype(f32)
                )

            whole = head_out.shape[0] // 16
            rest = head_out.shape[0] % 16

            @pl.loop(0, whole)
            def _(block):
                rows = pl.ds(pl.multiple_of(block * 16, 16), 16)
                head_out[rows, :] = total(rows)

            if rest:
                value = total(pl.ds(whole * 16, 16))
                head_out[pl.ds(whole * 16, rest), :] = value[:rest]

    to_core(0)
    to_core(1)
    stop(0)
    if with_packet:
        for keep in keeps:
            keep.wait()
        pass_packets(0)
    for step in range(1, chips - 1):
        to_core(step + 1)
        if with_head and step == 1:
            for copy in head_loads + head_copies[:2]:
                copy.start()
        stop(step)
        if with_packet and step <= line:
            pass_packets(step)
            if step == line:
                for copy in across:
                    copy.start()
        if with_packet and step == line + 1:
            for copy in across:
                copy.wait_recv()
            half_swap.start()
        if with_head and step == 2:
            head_over_cores()
    stop(chips - 1)
    each = outs[-1].shape[0]
    give = remote(
        last_total.at[pl.ds(each, each)], outs[-1], cross_send, cross_recv, section_peer
    )

    @pl.when(me_section == 0)
    def _():
        give.start()
        outs[-1][...] = last_total[pl.ds(0, each), :]

    if with_head:
        head_over_sections()
        for copy in head_copies:
            copy.wait_send()
    if with_packet:
        half_swap.wait()
        for copy in across:
            copy.wait_send()
        for turn in range(2):
            for hop in range(hops[turn]):
                for copy in packet_hops(turn, hop, 0):
                    copy.wait_send()
    for index in range(count):
        for turn in range(2):
            for step in range(chips):
                core_copy(index, turn, step).wait_send()
                if step < chips - 1:
                    ring_copy(index, turn, step).wait_send()

    @pl.when(me_section == 0)
    def _():
        give.wait_send()

    @pl.when(me_section == 1)
    def _():
        give.wait_recv()


def summed_over_dp(parts, collective_id, packets=(), head_part=None, head_rows=0):
    shapes = [part.shape for part in parts]
    line = shapes[0][0]
    chips = 2 * line
    count = len(parts)
    vmem = pl.BlockSpec(memory_space=pltpu.VMEM)
    anywhere = pl.BlockSpec(memory_space=pl.ANY)
    out_shape = [jax.ShapeDtypeStruct(shape[-2:], f32) for shape in shapes]
    high, deep = shapes[-1][-2:]
    out_shape[-1] = jax.ShapeDtypeStruct((high // 2, deep), f32)
    out_specs = [vmem] * count
    operands = list(parts)
    dma = pltpu.SemaphoreType.DMA
    scratch = [pltpu.VMEM((chips,) + shape[-2:], bf16) for shape in shapes]
    scratch += [pltpu.VMEM((chips,) + shape[-2:], bf16) for shape in shapes]
    scratch += [pltpu.VMEM((chips - 1,) + shape[-2:], bf16) for shape in shapes]
    scratch += [dma((count, 2, chips))] * 3 + [dma((count, 2, chips - 1))] * 2
    cost = 5 * sum(math.prod(shape) for shape in shapes) + 2**26
    half_rows = 0
    if packets:
        small, half = packets
        half_rows = half.shape[0]
        operands += [small, half]
        out_shape.append(jax.ShapeDtypeStruct((line, 2, 2) + small.shape, small.dtype))
        out_shape.append(jax.ShapeDtypeStruct((2, line, 2, 2) + half.shape, half.dtype))
        out_specs += [anywhere, anywhere]
        scratch += [dma((2,)), dma((2, 2, line)), dma((2, 2, line)), dma((2,)), dma((2,)), dma, dma]
    if head_part is not None:
        high, deep = head_part.shape[0] // 4, head_part.shape[1]
        operands.append(head_part)
        out_shape.append(jax.ShapeDtypeStruct((head_rows, deep), f32))
        out_specs.append(vmem)
        scratch += [pltpu.VMEM((2, high, deep), bf16)] * 2 + [pltpu.VMEM((high, deep), bf16)]
        scratch += [dma((2,)), dma((3,)), dma((3,))]
    scratch += [pltpu.VMEM(shapes[-1][-2:], f32), dma, dma]
    return pl.pallas_call(
        partial(sum_kernel, shapes, line, half_rows, head_part is not None),
        out_shape=out_shape,
        in_specs=[anywhere] * len(operands),
        out_specs=out_specs,
        scratch_shapes=scratch,
        compiler_params=pltpu.CompilerParams(
            collective_id=collective_id, has_side_effects=True, vmem_limit_bytes=60 * 2**20
        ),
        cost_estimate=pl.CostEstimate(flops=0, bytes_accessed=cost, transcendentals=0),
    )(*operands)


def rows_kernel(line, found, out, own, from_core, from_pair, from_line, *sems):
    load_sem, core_send, core_recv, pair_send, pair_recv, line_send, line_recv, swap_send, swap_recv = (
        sems
    )
    me_section = lax.axis_index("section")
    me_line = lax.axis_index("line")
    me_pair = lax.axis_index("pair")
    me_core = lax.axis_index("core")
    section_peer = {"section": 1 - me_section}
    core_peer = {"core": 1 - me_core}
    pair_peer = {"pair": 1 - me_pair}
    line_at = [lax.rem(me_line + step, line) for step in range(1, line)]
    greet([section_peer, core_peer, pair_peer] + [{"line": place} for place in line_at])
    rows, width = out.shape[-2:]
    wide = width // 2
    sides = (1 - me_pair, me_pair)
    loads, core_copies, pair_copies, line_copies = {}, {}, {}, {}
    for turn, side in enumerate(sides):
        for piece in range(2):
            cols = pl.ds(piece * wide, wide)
            loads[piece, turn] = pltpu.make_async_copy(
                found.at[:, side, me_core, :, cols],
                own.at[:, side, :, cols],
                load_sem.at[piece, turn],
            )
            core_copies[piece, turn] = remote(
                found.at[:, side, 1 - me_core, :, cols],
                from_core.at[:, side, :, cols],
                core_send.at[piece, turn],
                core_recv.at[piece, turn],
                core_peer,
            )
            loads[piece, turn].start()
            core_copies[piece, turn].start()

    def tiles(body):
        @pl.loop(0, rows // 16)
        def _(block):
            body(pl.ds(pl.multiple_of(block * 16, 16), 16))

    for piece in range(2):
        cols = pl.ds(piece * wide, wide)
        side = sides[0]
        loads[piece, 0].wait()
        core_copies[piece, 0].wait_recv()

        def add(row):
            for place in range(line):
                total = from_core[place, side, row, cols] + own[place, side, row, cols]
                from_core[place, side, row, cols] = total

        tiles(add)
        pair_copies[piece] = remote(
            from_core.at[:, side, :, cols],
            from_pair.at[:, :, cols],
            pair_send.at[piece],
            pair_recv.at[piece],
            pair_peer,
        )
        pair_copies[piece].start()
    for piece in range(2):
        cols = pl.ds(piece * wide, wide)
        loads[piece, 1].wait()
        core_copies[piece, 1].wait_recv()
        pair_copies[piece].wait_recv()

        def add(row):
            for place in range(line):
                total = from_core[place, me_pair, row, cols] + own[place, me_pair, row, cols]
                from_core[place, me_pair, row, cols] = total + from_pair[place, row, cols]

        tiles(add)
        for n in range(line - 1):
            line_copies[piece, n] = remote(
                from_core.at[line_at[n], me_pair, :, cols],
                from_line.at[n, :, cols],
                line_send.at[piece, n],
                line_recv.at[piece, n],
                {"line": line_at[n]},
            )
            line_copies[piece, n].start()
    for piece in range(2):
        cols = pl.ds(piece * wide, wide)
        for n in range(line - 1):
            line_copies[piece, n].wait_recv()

        def add(row):
            total = from_core[me_line, me_pair, row, cols]
            for n in range(line - 1):
                total = total + from_line[n, row, cols]
            out[me_section, row, cols] = total

        tiles(add)
    swap = remote(out.at[me_section], out.at[me_section], swap_send, swap_recv, section_peer)
    swap.start()
    for copy in list(core_copies.values()) + list(pair_copies.values()) + list(line_copies.values()):
        copy.wait_send()
    swap.wait()


def rows_over_dp(found, collective_id):
    line = found.shape[0]
    shape = found.shape[-2:]
    dma = pltpu.SemaphoreType.DMA
    return pl.pallas_call(
        partial(rows_kernel, line),
        out_shape=jax.ShapeDtypeStruct((2,) + shape, bf16),
        in_specs=[pl.BlockSpec(memory_space=pl.ANY)],
        out_specs=pl.BlockSpec(memory_space=pltpu.VMEM),
        scratch_shapes=[
            pltpu.VMEM((line, 2) + shape, bf16),
            pltpu.VMEM((line, 2) + shape, bf16),
            pltpu.VMEM((line,) + shape, bf16),
            pltpu.VMEM((line - 1,) + shape, bf16),
        ]
        + [dma((2, 2))] * 3
        + [dma((2,))] * 2
        + [dma((2, line - 1))] * 2
        + [dma, dma],
        compiler_params=pltpu.CompilerParams(
            collective_id=collective_id, has_side_effects=True, vmem_limit_bytes=32 * 2**20
        ),
        cost_estimate=pl.CostEstimate(flops=0, bytes_accessed=2**26, transcendentals=0),
    )(found)


def gather_kernel(line, mine, out, send, recv, own_sem):
    me_line = lax.axis_index("line")
    me_pair = lax.axis_index("pair")
    me_core = lax.axis_index("core")
    peers = []
    for step in range(1, line * 4):
        peers.append(
            {
                "line": lax.rem(me_line + step // 4, line),
                "pair": lax.rem(me_pair + step // 2 % 2, 2),
                "core": lax.rem(me_core + step % 2, 2),
            }
        )
    greet(peers)
    place = out.at[me_line, me_pair, me_core]
    keep = pltpu.make_async_copy(mine, place, own_sem)
    keep.start()
    copies = [remote(mine, place, send.at[n], recv.at[n], peer) for n, peer in enumerate(peers)]
    for copy in copies:
        copy.start()
    keep.wait()
    for copy in copies:
        copy.wait()


def gathered_small(block, line, collective_id):
    count = line * 4 - 1
    vmem = pl.BlockSpec(memory_space=pltpu.VMEM)
    return pl.pallas_call(
        partial(gather_kernel, line),
        out_shape=jax.ShapeDtypeStruct((line, 2, 2) + block.shape, block.dtype),
        in_specs=[vmem],
        out_specs=vmem,
        scratch_shapes=[
            pltpu.SemaphoreType.DMA((count,)),
            pltpu.SemaphoreType.DMA((count,)),
            pltpu.SemaphoreType.DMA,
        ],
        compiler_params=pltpu.CompilerParams(collective_id=collective_id, has_side_effects=True),
        cost_estimate=pl.CostEstimate(flops=0, bytes_accessed=2**25, transcendentals=0),
    )(block)


def head_kernel(line, head_rows, length, *refs):
    final, targets, *heads = refs[:6]
    out, grads, lse_out, pick_out = refs[6:10]
    (table, rows_all, logits, probs, acc, parts, from_pair, from_line, stats, done) = refs[10:20]
    (head_sem, own_sem, give_send, give_recv, along_send, along_recv, pair_send, pair_recv) = refs[20:28]
    (stat_send, stat_recv, sum_send, sum_recv, line_send, line_recv, back_send, back_recv) = refs[28:]
    half = final.shape[0] // 2
    width = 2 * half
    padded = heads[0].shape[0]
    me_section = lax.axis_index("section")
    me_line = lax.axis_index("line")
    me_pair = lax.axis_index("pair")
    me_core = lax.axis_index("core")
    section_peer = {"section": 1 - me_section}
    pair_peer = {"pair": 1 - me_pair}
    chip_peers = []
    for step in range(1, 2 * line):
        chip_peers.append(
            {"line": lax.rem(me_line + step // 2, line), "pair": lax.rem(me_pair + step % 2, 2)}
        )
    greet(chip_peers + [section_peer])

    def side(pair):
        return pl.ds(pl.multiple_of(pair * half, 16), half)

    loads = [
        pltpu.make_async_copy(part, table.at[pl.ds(n * padded, padded)], head_sem.at[n])
        for n, part in enumerate(heads)
    ]
    for load in loads:
        load.start()

    def token_rows(place, pair):
        return pl.ds(pl.multiple_of(place * width + pair * half, 16), half)

    def group(place):
        return pl.ds(pl.multiple_of(place * width, 128), width)

    mine = rows_all.at[token_rows(me_line, me_pair)]
    give = remote(final.at[pl.ds(0, half)], mine, give_send, give_recv, section_peer)

    @pl.when(me_section == 1)
    def _():
        give.start()
        keep = pltpu.make_async_copy(final.at[pl.ds(half, half)], mine, own_sem)
        keep.start()
        keep.wait()

    @pl.when(me_section == 0)
    def _():
        give.wait_recv()

    def column_block(place):
        return rows_all.at[token_rows(place, me_pair)]

    def along(step, way):
        block = column_block(me_line - way * step)
        turn = (way + 1) // 2
        return remote(
            block,
            block,
            along_send.at[turn, step],
            along_recv.at[turn, step],
            {"line": me_line + way},
        )

    def inside(place):
        return (place >= 0) & (place < line)

    def sends_along(step, way):
        return inside(me_line - way * step) & inside(me_line + way)

    def sideways(place):
        block = column_block(place)
        return remote(block, block, pair_send.at[place], pair_recv.at[place], pair_peer)

    def arrived_sideways(place):
        block = rows_all.at[token_rows(place, 1 - me_pair)]
        return remote(block, block, pair_send.at[place], pair_recv.at[place], pair_peer)

    for way in (1, -1):

        @pl.when(sends_along(0, way))
        def _():
            along(0, way).start()

    sideways(me_line).start()

    def pass_on(step):
        for way in (1, -1):
            place = me_line - way * step

            @pl.when(inside(place))
            def _():
                block = column_block(place)
                turn = (way + 1) // 2
                remote(
                    block,
                    block,
                    along_send.at[turn, step - 1],
                    along_recv.at[turn, step - 1],
                    {"line": me_line - way},
                ).wait_recv()

                @pl.when(inside(me_line + way))
                def _():
                    along(step, way).start()

                sideways(place).start()

    nearest = []
    for own in range(line):
        near = [own]
        for step in range(1, line):
            near += [place for place in (own - step, own + step) if 0 <= place < line]
        nearest.append(near)

    def by_distance(turn):
        place = 0
        for own in range(line):
            for n in range(line):
                hit = ((me_line == own) & (turn == n)).astype(jnp.int32)
                place = place + hit * nearest[own][n]
        return place

    def vocabulary(tile, rows):
        shard = tile * rows // padded
        first = lax.rem(tile * rows, padded)
        shard_section = lax.rem(me_section + shard // 2, 2)
        shard_core = lax.rem(me_core + lax.rem(shard, 2), 2)
        base = (((shard_section * line + me_line) * 2 + me_pair) * 2 + shard_core) * head_rows
        row = lax.broadcasted_iota(jnp.int32, (rows, 1), 0) + first
        return jnp.where(row < head_rows, row + base, -1)

    tile_rows = 512
    tiles = 4 * padded // tile_rows
    lowest = -1e30

    def score(turn, tops):
        place = by_distance(turn) if turn < line else None
        before = by_distance(turn - 1) if turn > 0 else None
        wanted = None if place is None else targets[place]

        def one(tile, carry):
            rows = pl.ds(pl.multiple_of(tile * tile_rows, tile_rows), tile_rows)
            out = []
            if place is not None:
                top, pick = carry[:2]
                entry = vocabulary(tile, tile_rows)
                part = nt(table[rows, :], rows_all[group(place), :])
                part = jnp.where(entry >= 0, part, lowest)
                logits[turn % 2, rows, :] = part
                out.append(jnp.maximum(top, jnp.max(part, 0, keepdims=True)))
                out.append(
                    pick + jnp.sum(jnp.where(entry == wanted, part, 0.0), 0, keepdims=True)
                )
            if before is not None:
                value = jnp.exp(logits[(turn - 1) % 2, rows, :] - tops)
                probs[rows, group(before)] = value.astype(bf16)
                out.append(carry[-1] + jnp.sum(value, 0, keepdims=True))
            return tuple(out)

        none = jnp.zeros((1, width), f32)
        start = () if place is None else (jnp.full((1, width), lowest, f32), none)
        start += () if before is None else (none,)
        result = lax.fori_loop(0, tiles, one, start)
        if place is not None:
            pick_out[place] = result[1]
        if before is not None:
            own = stats.at[me_line, me_pair, before]
            own[0:1, :] = tops
            own[1:2, :] = result[-1]
            for n in range(len(chip_peers)):
                stat_copy(n, before).start()
        return None if place is None else result[0]

    def stat_copy(n, place):
        own = stats.at[me_line, me_pair, place]
        return remote(own, own, stat_send.at[n, place], stat_recv.at[n, place], chip_peers[n])

    def stat_wait(n, place):
        peer = chip_peers[n]
        source_line = lax.rem(2 * me_line + line - peer["line"], line)
        source_pair = peer["pair"]
        block = stats.at[source_line, source_pair, place]
        remote(block, block, stat_send.at[n, place], stat_recv.at[n, place], peer).wait_recv()

    for load in loads:
        load.wait()

    tops = None
    for turn in range(line + 1):
        if turn + 1 < line:
            pass_on(turn + 1)
        if turn < line:
            arrived_sideways(by_distance(turn)).wait_recv()
        tops = score(turn, tops)

    def sum_copy(turn):
        place = lax.rem(me_line + turn + 1, line)
        return remote(
            parts.at[place, side(1 - me_pair)],
            from_pair.at[turn],
            sum_send.at[turn],
            sum_recv.at[turn],
            pair_peer,
        )

    def line_copy(turn):
        place = lax.rem(me_line + turn + 1, line)
        return remote(
            parts.at[place, side(me_pair)],
            from_line.at[turn],
            line_send.at[turn],
            line_recv.at[turn],
            {"line": place},
        )

    def finish(turn):
        place = lax.rem(me_line + turn + 1, line)
        sum_copy(turn).wait_recv()
        own = parts.at[place, side(me_pair)]

        @pl.loop(0, half // 16)
        def _(block):
            rows = pl.ds(pl.multiple_of(block * 16, 16), 16)
            value = own[rows, :].astype(f32) + from_pair[turn, rows, :].astype(f32)
            own[rows, :] = value.astype(bf16)

    @pl.loop(0, line)
    def _(turn):
        place = lax.rem(me_line + turn + 1, line)
        for n in range(len(chip_peers)):
            stat_wait(n, place)
        tops = [stats[a, b, place, 0:1, :] for a in range(line) for b in range(2)]
        totals = [stats[a, b, place, 1:2, :] for a in range(line) for b in range(2)]
        top = tops[0]
        for value in tops[1:]:
            top = jnp.maximum(top, value)
        total = jnp.zeros_like(top)
        for peak, part in zip(tops, totals):
            total = total + part * jnp.exp(peak - top)
        lse = top + jnp.log(total)
        lse_out[place] = lse
        factor = jnp.exp(stats[me_line, me_pair, place, 0:1, :] - lse) / length
        wanted = targets[place]

        def scaled(tile):
            rows = pl.ds(tile * padded, padded)
            entry = vocabulary(tile, padded)
            grad = probs[rows, group(place)].astype(f32) * factor
            grad = (grad - jnp.where(entry == wanted, 1.0 / length, 0.0)).astype(bf16)
            probs[rows, group(place)] = grad
            return grad

        grad = scaled(0)
        for tile in range(4):
            product = tn(grad, table[pl.ds(tile * padded, padded), :])
            if tile < 3:
                grad = scaled(tile + 1)
                acc[...] = product if tile == 0 else acc[...] + product
            else:
                parts[place] = (acc[...] + product).astype(bf16)

        sum_copy(turn).start()

        @pl.when(turn > 0)
        def _():
            finish(turn - 1)
            line_copy(turn - 1).start()

    gh_rows = 256
    gh_tiles = 4 * padded // gh_rows

    def head_grads(first, last):
        @pl.loop(first, last)
        def _(tile):
            rows = pl.ds(pl.multiple_of(tile * gh_rows, gh_rows), gh_rows)
            value = jnp.dot(probs[rows, :], rows_all[...], preferred_element_type=f32)
            grads[rows, :] = value.astype(bf16)

    head_grads(0, gh_tiles // 2)
    finish(line - 1)
    for turn in range(line - 1):
        line_copy(turn).wait_recv()
    own = parts.at[me_line, side(me_pair)]

    @pl.loop(0, half // 16)
    def _(block):
        rows = pl.ds(pl.multiple_of(block * 16, 16), 16)
        value = own[rows, :].astype(f32)
        for turn in range(line - 1):
            value = value + from_line[turn, rows, :].astype(f32)
        done[rows, :] = value.astype(bf16)

    back = remote(done, out.at[pl.ds(0, half)], back_send, back_recv, section_peer)

    @pl.when(me_section == 0)
    def _():
        back.start()
        out[...] = jnp.zeros_like(out)

    @pl.when(me_section == 1)
    def _():
        out[pl.ds(half, half), :] = done[...]

    head_grads(gh_tiles // 2, gh_tiles)

    @pl.when(me_section == 0)
    def _():
        back.wait_send()

    @pl.when(me_section == 1)
    def _():
        back.wait_recv()
        give.wait_send()

    for way in (1, -1):
        for step in range(line - 1):

            @pl.when(sends_along(step, way))
            def _():
                along(step, way).wait_send()

    for place in range(line):
        sideways(place).wait_send()
        for n in range(len(chip_peers)):
            stat_copy(n, place).wait_send()
    for turn in range(line):
        sum_copy(turn).wait_send()
    for turn in range(line - 1):
        line_copy(turn).wait_send()


def head_pass(final, targets, heads, line, head_rows, length, collective_id):
    tokens, deep = final.shape
    half = tokens // 2
    padded = heads[0].shape[0]
    vmem = pl.BlockSpec(memory_space=pltpu.VMEM)
    anywhere = pl.BlockSpec(memory_space=pl.ANY)
    dma = pltpu.SemaphoreType.DMA
    peers = 2 * line - 1
    return pl.pallas_call(
        partial(head_kernel, line, head_rows, length),
        out_shape=[
            jax.ShapeDtypeStruct((tokens, deep), bf16),
            jax.ShapeDtypeStruct((4 * padded, deep), bf16),
            jax.ShapeDtypeStruct((line, 1, tokens), f32),
            jax.ShapeDtypeStruct((line, 1, tokens), f32),
        ],
        in_specs=[vmem, vmem] + [anywhere] * 4,
        out_specs=[vmem] * 4,
        scratch_shapes=[
            pltpu.VMEM((4 * padded, deep), bf16),
            pltpu.VMEM((line * tokens, deep), bf16),
            pltpu.VMEM((2, 4 * padded, tokens), f32),
            pltpu.VMEM((4 * padded, line * tokens), bf16),
            pltpu.VMEM((tokens, deep), f32),
            pltpu.VMEM((line, tokens, deep), bf16),
            pltpu.VMEM((line, half, deep), bf16),
            pltpu.VMEM((line - 1, half, deep), bf16),
            pltpu.VMEM((line, 2, line, 8, tokens), f32),
            pltpu.VMEM((half, deep), bf16),
            dma((4,)),
            dma,
            dma,
            dma,
            dma((2, line)),
            dma((2, line)),
            dma((line,)),
            dma((line,)),
            dma((peers, line)),
            dma((peers, line)),
            dma((line,)),
            dma((line,)),
            dma((line,)),
            dma((line,)),
            dma,
            dma,
        ],
        compiler_params=pltpu.CompilerParams(
            collective_id=collective_id, has_side_effects=True, vmem_limit_bytes=60 * 2**20
        ),
        cost_estimate=pl.CostEstimate(
            flops=24 * line * padded * tokens * deep, bytes_accessed=2**28, transcendentals=0
        ),
    )(final, targets, *heads)


def row_stats(values):
    centred = values - jnp.mean(values, -1, keepdims=True)
    factor = lax.rsqrt(jnp.mean(centred * centred, -1, keepdims=True) + epsilon)
    return centred * factor, factor


def two_heads(block):
    first = lax.broadcasted_iota(jnp.int32, block.shape, 1) < HEAD_DIM
    zero = jnp.zeros_like(block)
    return jnp.concatenate([jnp.where(first, block, zero), jnp.where(first, zero, block)], 0)


def one_block(stacked):
    rows = stacked.shape[0] // 2
    first = lax.broadcasted_iota(jnp.int32, (rows, stacked.shape[1]), 1) < HEAD_DIM
    return jnp.where(first, stacked[:rows], stacked[rows:])


def attention_weights(queries, keys):
    scores = nt(keys, queries) * (1.0 / math.sqrt(HEAD_DIM))
    exped = jnp.exp(scores - jnp.max(scores, 0, keepdims=True))
    return exped * (1.0 / jnp.sum(exped, 0, keepdims=True))


def tile_of(index, size):
    return pl.ds(pl.multiple_of(index * size, size), size)


def forward_kernel(full, seqs, *refs):
    refs = list(refs)

    def take(number):
        return [refs.pop(0) for _ in range(number)]

    start, scale, bias = take(3)
    arrived, gain = take(2) if full else (None, None)
    weights = take(4)
    if full:
        out, final, x, joined, mixed, middle, entry_attn, entry_mlp, slope, hidden = take(10)
    else:
        (out,) = take(1)
        x = start
        joined, mixed, middle, entry_attn = take(4)
        entry_mlp = entry_attn
    w_qkv, w_out, w_up, w_down, total, sems = refs
    width = start.shape[1]
    length = start.shape[0] // seqs
    load_qkv, load_out, load_up, load_down = [
        pltpu.make_async_copy(source.at[0], target, sems.at[n])
        for n, (source, target) in enumerate(zip(weights, (w_qkv, w_out, w_up, w_down)))
    ]
    load_qkv.start()

    for seq in range(seqs):
        rows = pl.ds(seq * length, length)
        if full:
            first = (lax.axis_index("section") == 0).astype(f32)
            x[rows, :] = start[rows, :] * first + arrived[rows, :].astype(f32) * (1.0 - first)
        normed, _ = row_stats(x[rows, :])
        entry_attn[rows, :] = (normed * scale[seq, :, :width]).astype(bf16)

    load_qkv.wait()
    load_out.start()
    load_up.start()
    tile = 512

    @pl.loop(0, 3 * width // tile)
    def _(index):
        cols = tile_of(index, tile)
        joined[:, cols] = nn(entry_attn[...], w_qkv[:, cols]).astype(bf16)

    load_out.wait()
    load_down.start()
    pairs = width // 128

    @pl.loop(0, pairs)
    def _(pair):
        cols = tile_of(pair, 128)
        for seq in range(seqs):
            rows = pl.ds(seq * length, length)
            queries = two_heads(joined[rows, cols])
            keys = joined[rows, tile_of(pair + pairs, 128)]
            values = joined[rows, tile_of(pair + 2 * pairs, 128)]
            probs = attention_weights(queries, keys).astype(bf16)
            mixed[rows, cols] = one_block(tn(probs, values)).astype(bf16)

    @pl.loop(0, width // tile)
    def _(index):
        cols = tile_of(index, tile)
        middle[:, cols] = x[:, cols] + nn(mixed[...], w_out[:, cols])

    for seq in range(seqs):
        rows = pl.ds(seq * length, length)
        normed, _ = row_stats(middle[rows, :])
        entry_mlp[rows, :] = (normed * scale[seq, :, width:]).astype(bf16)

    load_up.wait()
    load_down.wait()
    total[...] = middle[...]

    def gelu_of(up, cols):
        below = 0.5 + 0.5 * lax.erf(up * math.sqrt(0.5))
        value = (up * below).astype(bf16)
        if full:
            density = jnp.exp(-0.5 * up * up) * (1.0 / math.sqrt(2.0 * math.pi))
            slope[:, cols] = (below + up * density).astype(bf16)
            hidden[:, cols] = value
        return value

    @pl.loop(0, w_up.shape[1] // (2 * tile))
    def _(index):
        sides = [tile_of(2 * index + side, tile) for side in range(2)]
        ups = [nn(entry_mlp[...], w_up[:, cols]) + bias[:, cols] for cols in sides]
        both = jnp.concatenate([gelu_of(up, cols) for up, cols in zip(ups, sides)], 1)
        total[...] += nn(both, w_down[tile_of(index, 2 * tile), :])

    for seq in range(seqs):
        rows = pl.ds(seq * length, length)
        value = total[rows, :].astype(bf16)
        out[rows, :] = value
        if full:
            normed, _ = row_stats(value.astype(f32))
            final[rows, :] = (normed * gain[...]).astype(bf16)


def layer_scratch(width, hidden):
    return [
        pltpu.VMEM((width, 3 * width), bf16),
        pltpu.VMEM((width, width), bf16),
        pltpu.VMEM((width, hidden), bf16),
        pltpu.VMEM((hidden, width), bf16),
    ]


def forward_pass(start, scale, weights, arrived=None, gain=None):
    w_qkv, w_out, w_up, b_hidden, w_down = weights
    tokens, width = start.shape
    wide = w_up.shape[-1]
    full = arrived is not None
    vmem = pl.BlockSpec(memory_space=pltpu.VMEM)
    anywhere = pl.BlockSpec(memory_space=pl.ANY)

    def low(columns):
        return (tokens, columns), bf16

    exact = ((tokens, width), f32)
    out_shape = [jax.ShapeDtypeStruct((tokens, width), bf16)]
    scratch = layer_scratch(width, wide)
    scratch += [pltpu.VMEM(*exact), pltpu.SemaphoreType.DMA((4,))]
    operands = [start, scale, b_hidden]
    if full:
        operands += [arrived, gain]
        kept = [low(width), exact, low(3 * width), low(width), exact, low(width), low(width)]
        out_shape += [jax.ShapeDtypeStruct(*item) for item in kept + [low(wide), low(wide)]]
    else:
        inside = [low(3 * width), low(width), exact, low(width)]
        scratch = [pltpu.VMEM(*item) for item in inside] + scratch
    flops = 2 * tokens * (4 * width * width + 2 * width * wide)
    return pl.pallas_call(
        partial(forward_kernel, full, scale.shape[0]),
        out_shape=out_shape,
        in_specs=[vmem] * len(operands) + [anywhere] * 4,
        out_specs=[vmem] * len(out_shape),
        scratch_shapes=scratch,
        compiler_params=pltpu.CompilerParams(vmem_limit_bytes=60 * 2**20),
        cost_estimate=pl.CostEstimate(flops=2 * flops, bytes_accessed=2**25, transcendentals=0),
    )(*operands, w_qkv, w_out, w_up, w_down)


def backward_kernel(full, seqs, *refs):
    refs = list(refs)

    def take(number):
        return [refs.pop(0) for _ in range(number)]

    scale, incoming, other = take(3)
    gain = None if full else take(1)[0]
    far = take(8)
    if full:
        out, grad_low, grad_up, grad_attn, grad_joined, grad_cond, grad_bias = take(7)
    else:
        out, grad_top, grad_gain = take(3)
        grad_low, grad_up, grad_attn, grad_joined = take(4)
    near = take(8)
    total, grad_middle, grad_mixed, sems = refs
    x, middle, joined, slope, w_qkv, w_out, w_up, w_down = near
    width = x.shape[1]
    length = x.shape[0] // seqs
    copies = [
        pltpu.make_async_copy(source, target, sems.at[n])
        for n, (source, target) in enumerate(
            zip(list(far[:4]) + [weight.at[0] for weight in far[4:]], near)
        )
    ]
    load_x, load_middle, load_joined, load_slope, load_qkv, load_out, load_up, load_down = copies
    load_down.start()
    load_slope.start()

    grad_out = total
    for seq in range(seqs):
        rows = pl.ds(seq * length, length)
        if full:
            first = (lax.axis_index("section") == 0).astype(f32)
            value = incoming[rows, :].astype(f32) * first + other[rows, :] * (1.0 - first)
        else:
            normed, factor = row_stats(other[rows, :].astype(f32))
            gradient = incoming[rows, :].astype(f32)
            part = jnp.sum(gradient * normed, 0, keepdims=True)
            grad_gain[...] = part if seq == 0 else grad_gain[...] + part
            scaled = gradient * gain[...]
            value = factor * (
                scaled
                - jnp.mean(scaled, -1, keepdims=True)
                - normed * jnp.mean(scaled * normed, -1, keepdims=True)
            )
            grad_top[rows, :] = value
        grad_middle[rows, :] = value
        grad_low[rows, :] = value.astype(bf16)

    load_down.wait()
    load_slope.wait()
    load_up.start()
    load_middle.start()
    load_out.start()
    load_joined.start()
    tile = 1024

    @pl.loop(0, w_up.shape[1] // tile)
    def _(index):
        cols = tile_of(index, tile)
        grad_hidden = nt(grad_low[...], w_down[cols, :])
        value = (grad_hidden * slope[:, cols].astype(f32)).astype(bf16)
        grad_up[:, cols] = value
        if full:
            grad_bias[:, cols] = jnp.sum(value.astype(f32), 0, keepdims=True)

    load_up.wait()
    load_middle.wait()
    load_out.wait()
    load_joined.wait()
    load_qkv.start()
    load_x.start()

    @pl.loop(0, width // 256)
    def _(index):
        total[:, tile_of(index, 256)] = nt(grad_up[...], w_up[tile_of(index, 256), :])

    def norm_grads(source, half, store):
        for seq in range(seqs):
            rows = pl.ds(seq * length, length)
            normed, factor = row_stats(source[rows, :])
            gradient = total[rows, :]
            cols = pl.ds(half * width, width)
            if full:
                grad_cond[seq, :, cols] = jnp.sum(gradient * normed, 0, keepdims=True)
            scaled = gradient * scale[seq, :, cols]
            back = factor * (
                scaled
                - jnp.mean(scaled, -1, keepdims=True)
                - normed * jnp.mean(scaled * normed, -1, keepdims=True)
            )
            store(rows, grad_middle[rows, :] + back)

    def store_middle(rows, value):
        grad_middle[rows, :] = value
        grad_attn[rows, :] = value.astype(bf16)

    norm_grads(middle, 1, store_middle)

    @pl.loop(0, width // 512)
    def _(index):
        part = tile_of(index, 512)
        grad_mixed[:, part] = nt(grad_attn[...], w_out[part, :]).astype(bf16)

    pairs = width // 128
    shrink = 1.0 / math.sqrt(HEAD_DIM)

    @pl.loop(0, pairs)
    def _(pair):
        cols = tile_of(pair, 128)
        key_cols = tile_of(pair + pairs, 128)
        value_cols = tile_of(pair + 2 * pairs, 128)
        for seq in range(seqs):
            rows = pl.ds(seq * length, length)
            queries = two_heads(joined[rows, cols])
            keys = joined[rows, key_cols]
            probs = attention_weights(queries, keys)
            grads = two_heads(grad_mixed[rows, cols])
            grad_probs = nt(joined[rows, value_cols], grads)
            inner = jnp.sum(grad_probs * probs, 0, keepdims=True)
            grad_scores = (probs * (grad_probs - inner)).astype(bf16)
            grad_joined[rows, cols] = (one_block(tn(grad_scores, keys)) * shrink).astype(bf16)
            grad_joined[rows, key_cols] = (nn(grad_scores, queries) * shrink).astype(bf16)
            grad_joined[rows, value_cols] = nn(probs.astype(bf16), grads).astype(bf16)

    load_qkv.wait()
    load_x.wait()

    @pl.loop(0, width // 256)
    def _(index):
        total[:, tile_of(index, 256)] = nt(grad_joined[...], w_qkv[tile_of(index, 256), :])

    def store_out(rows, value):
        out[rows, :] = value.astype(bf16)

    norm_grads(x, 0, store_out)


def backward_pass(incoming, other, scale, kept, weights, gain=None):
    w_qkv, w_out, w_up, _, w_down = weights
    x, joined, _, middle, _, _, slope, _ = kept
    tokens, width = x.shape
    wide = w_up.shape[-1]
    seqs = scale.shape[0]
    full = gain is None
    vmem = pl.BlockSpec(memory_space=pltpu.VMEM)
    anywhere = pl.BlockSpec(memory_space=pl.ANY)
    exact = ((tokens, width), f32)
    lows = [
        ((tokens, width), bf16),
        ((tokens, wide), bf16),
        ((tokens, width), bf16),
        ((tokens, 3 * width), bf16),
    ]
    out_shape = [jax.ShapeDtypeStruct((tokens, width), bf16)]
    scratch = [
        pltpu.VMEM(*exact),
        pltpu.VMEM(*exact),
        pltpu.VMEM((tokens, 3 * width), bf16),
        pltpu.VMEM((tokens, wide), bf16),
    ]
    scratch += layer_scratch(width, wide)
    scratch += [
        pltpu.VMEM(*exact),
        pltpu.VMEM(*exact),
        pltpu.VMEM((tokens, width), bf16),
        pltpu.SemaphoreType.DMA((8,)),
    ]
    operands = [scale, incoming, other]
    if full:
        out_shape += [jax.ShapeDtypeStruct(*item) for item in lows]
        out_shape.append(jax.ShapeDtypeStruct((seqs, 1, 2 * width), f32))
        out_shape.append(jax.ShapeDtypeStruct((1, wide), f32))
    else:
        operands.append(gain)
        out_shape.append(jax.ShapeDtypeStruct(*exact))
        out_shape.append(jax.ShapeDtypeStruct((1, width), f32))
        scratch = [pltpu.VMEM(*item) for item in lows] + scratch
    flops = 2 * tokens * (4 * width * width + 2 * width * wide)
    return pl.pallas_call(
        partial(backward_kernel, full, seqs),
        out_shape=out_shape,
        in_specs=[vmem] * len(operands) + [anywhere] * 8,
        out_specs=[vmem] * len(out_shape),
        scratch_shapes=scratch,
        compiler_params=pltpu.CompilerParams(vmem_limit_bytes=60 * 2**20),
        cost_estimate=pl.CostEstimate(flops=2 * flops, bytes_accessed=2**25, transcendentals=0),
    )(*operands, x, middle, joined, slope, w_qkv, w_out, w_up, w_down)


def norm_rows(values):
    centred = values - jnp.mean(values, -1, keepdims=True)
    factor = lax.rsqrt(jnp.mean(centred * centred, -1, keepdims=True) + epsilon)
    return (centred * factor, factor)


def norm_back(gradient, normed, factor):
    return factor * (
        gradient
        - jnp.mean(gradient, -1, keepdims=True)
        - normed * jnp.mean(gradient * normed, -1, keepdims=True)
    )


def time_features(noise_level):
    half_width = TFEAT // 2
    rates = jnp.exp(jnp.arange(half_width, dtype=f32) * (math.log(1000.0) / half_width))
    angles = (jnp.log(noise_level) / 4.0)[:, None] * rates[None, :]
    return jnp.concatenate([jnp.cos(angles), jnp.sin(angles)], -1)


def levels_of(bins, table):
    hits = bins[:, None] == jnp.arange(table.shape[0])[None, :]
    return jnp.sum(jnp.where(hits, table[None, :], 0.0), -1)


def over_dp(part):
    part = part.reshape((part.shape[0] // 4, 2, 2) + part.shape[1:])
    part = lax.psum_scatter(part, "core", scatter_dimension=2)
    part = lax.psum_scatter(part, "pair", scatter_dimension=1)
    return lax.psum_scatter(part, "line", scatter_dimension=0)


def by_owner(part):
    line = lax.axis_size("line")
    return part.astype(bf16).reshape((line, 2, 2, part.shape[0] // (line * 4)) + part.shape[1:])


def mm(spec, left, right):
    return jnp.einsum(spec, left, right, preferred_element_type=f32)


def layer_forward(stream, scale_attn, scale_mlp, weights):
    w_qkv, w_out, w_up, b_hidden, w_down = weights
    seq_count, length, model_width = stream.shape
    normed_attn, factor_attn = norm_rows(stream)
    attn_entry = (normed_attn * scale_attn).astype(bf16)
    joined = mm("nsd,de->nse", attn_entry, w_qkv).astype(bf16)
    qkv_parts = joined.reshape(seq_count, length, 3, HEADS, HEAD_DIM)
    query_rows = qkv_parts[:, :, 0]
    key_rows = qkv_parts[:, :, 1]
    value_rows = qkv_parts[:, :, 2]
    scores = mm("nqhe,nkhe->nhqk", query_rows, key_rows) / math.sqrt(HEAD_DIM)
    exp_scores = jnp.exp(scores - jnp.max(scores, -1, keepdims=True))
    attn_probs = exp_scores / jnp.sum(exp_scores, -1, keepdims=True)
    probs_low = attn_probs.astype(bf16)
    attn_mixed = mm("nhqk,nkhe->nqhe", probs_low, value_rows).astype(bf16)
    attn_mixed = attn_mixed.reshape(seq_count, length, model_width)
    middle = stream + mm("nsd,de->nse", attn_mixed, w_out)
    normed_mlp, factor_mlp = norm_rows(middle)
    mlp_entry = (normed_mlp * scale_mlp).astype(bf16)
    up_proj = mm("nsd,df->nsf", mlp_entry, w_up) + b_hidden
    below = 0.5 + 0.5 * lax.erf(up_proj * math.sqrt(0.5))
    hidden = (up_proj * below).astype(bf16)
    density = jnp.exp(-0.5 * up_proj * up_proj) * (1.0 / math.sqrt(2.0 * math.pi))
    slope = (below + up_proj * density).astype(bf16)
    block_out = middle + mm("nsf,fd->nsd", hidden, w_down)
    kept = (
        normed_attn,
        factor_attn,
        attn_entry,
        query_rows,
        key_rows,
        value_rows,
        attn_probs,
        probs_low,
        attn_mixed,
        normed_mlp,
        factor_mlp,
        mlp_entry,
        slope,
        hidden,
    )
    return (block_out, kept)


def layer_backward(grad_out, kept, scale_attn, scale_mlp, weights, whole):
    w_qkv, w_out, w_up, b_hidden, w_down = weights
    (
        normed_attn,
        factor_attn,
        attn_entry,
        query_rows,
        key_rows,
        value_rows,
        attn_probs,
        probs_low,
        attn_mixed,
        normed_mlp,
        factor_mlp,
        mlp_entry,
        slope,
        hidden,
    ) = kept
    seq_count, length, model_width = grad_out.shape
    grads = {}
    grad_branch = grad_out.astype(bf16)
    if whole:
        grads["down"] = by_owner(mm("nsf,nsd->fd", hidden, grad_branch))
    grad_hidden = mm("nsd,fd->nsf", grad_branch, w_down)
    grad_up_proj = (grad_hidden * slope.astype(f32)).astype(bf16)
    if whole:
        grads["bias"] = jnp.sum(grad_up_proj.astype(f32), (0, 1))
        grads["up"] = by_owner(mm("nsd,nsf->df", mlp_entry, grad_up_proj))
    grad_entry = mm("nsf,df->nsd", grad_up_proj, w_up)
    grad_middle = grad_out + norm_back(grad_entry * scale_mlp, normed_mlp, factor_mlp)
    grad_attn = grad_middle.astype(bf16)
    if whole:
        grads["out"] = by_owner(mm("nsd,nse->de", attn_mixed, grad_attn))
    grad_mixed = mm("nse,de->nsd", grad_attn, w_out)
    grad_mixed = grad_mixed.astype(bf16).reshape(seq_count, length, HEADS, HEAD_DIM)
    grad_probs = mm("nqhe,nkhe->nhqk", grad_mixed, value_rows)
    grad_values = mm("nhqk,nqhe->nkhe", probs_low, grad_mixed)
    grad_scores = (
        attn_probs * (grad_probs - jnp.sum(grad_probs * attn_probs, -1, keepdims=True))
    ).astype(bf16)
    grad_query = mm("nhqk,nkhe->nqhe", grad_scores, key_rows) / math.sqrt(HEAD_DIM)
    grad_keys = mm("nhqk,nqhe->nkhe", grad_scores, query_rows) / math.sqrt(HEAD_DIM)
    grad_joined = jnp.stack([grad_query, grad_keys, grad_values], 2).astype(bf16)
    grad_joined = grad_joined.reshape(seq_count, length, 3 * model_width)
    if whole:
        grads["qkv"] = by_owner(mm("nsd,nse->de", attn_entry, grad_joined))
    grad_attn_entry = mm("nse,de->nsd", grad_joined, w_qkv)
    grad_stream = grad_middle + norm_back(grad_attn_entry * scale_attn, normed_attn, factor_attn)
    if whole:
        grads["cond"] = jnp.concatenate(
            [jnp.sum(grad_attn_entry * normed_attn, 1), jnp.sum(grad_entry * normed_mlp, 1)], -1
        )
    return (grad_stream, grads)


def local(
    token_ids,
    target_ids,
    time_bins,
    sigma_table,
    noise,
    embed,
    w_in,
    w_time,
    norm_gain,
    w_qkv,
    w_out,
    w_up,
    b_hidden,
    w_down,
    out_gain,
    head,
):
    section = lax.axis_index("section")
    line_at = lax.axis_index("line")
    pair_at = lax.axis_index("pair")
    core = lax.axis_index("core")
    sections = lax.axis_size("section")
    line = lax.axis_size("line")
    chip = line_at * 2 + pair_at
    chips = line * 2
    cores = 2
    dp_count = chips * cores
    dp_index = chip * cores + core
    is_first = section == 0
    seqs, length = token_ids.shape
    tokens = seqs * length
    half = tokens // sections
    model_width = w_out.shape[-1]
    emb_rows, emb_width = embed.shape
    straight = line <= 4 and half % 16 == 0 and model_width // dp_count % 16 == 0

    own_ids = jnp.concatenate([token_ids.reshape(-1), target_ids.reshape(-1), time_bins])
    if straight:
        padded = jnp.pad(own_ids, (0, -own_ids.shape[0] % 1024)).reshape(-1, 128)
        all_ids = gathered_small(padded, line, 0).reshape(dp_count, -1)[:, : own_ids.shape[0]]
    else:
        all_ids = lax.all_gather(own_ids, DP)
    all_tokens = all_ids[:, :tokens]
    all_targets = all_ids[:, tokens : 2 * tokens]
    all_bins = all_ids[:, 2 * tokens :].reshape(-1)

    own_rows = dp_index * emb_rows + jnp.arange(emb_rows)
    half_tokens = lax.dynamic_slice_in_dim(all_tokens, section * half, half, 1)
    picked = (half_tokens.reshape(-1)[:, None] == own_rows[None, :]).astype(bf16)
    found = jnp.dot(picked, embed, preferred_element_type=f32).astype(bf16)
    if straight:
        found = found.reshape(line, 2, 2, half, emb_width)
        embedded = rows_over_dp(found, 1)
    else:
        embedded = lax.all_gather(over_dp(found.reshape(dp_count, half, emb_width)), "section")
    embedded = embedded.astype(f32).reshape(seqs, length, emb_width)

    head_rows = head.shape[0]
    swapped = [(0, 1), (1, 0)]
    if straight:
        head_own = jnp.pad(head, ((0, -head_rows % 512), (0, 0)))
        head_core = lax.ppermute(head_own, "core", swapped)
        head_section = lax.ppermute(head_own, "section", swapped)
    else:
        head_group = lax.all_gather(lax.all_gather(head, "core"), "section")
        head_group = head_group.reshape(-1, model_width)
        vocab_base = (
            (jnp.arange(sections)[:, None] * chips + chip) * cores + jnp.arange(cores)[None, :]
        ) * head_rows
        columns = (vocab_base[:, :, None] + jnp.arange(head_rows)[None, None, :]).reshape(-1)

    noise_level = levels_of(time_bins, sigma_table)
    unit_factor = lax.rsqrt(jnp.mean(embedded * embedded, -1, keepdims=True) + epsilon)
    level_col = noise_level[:, None, None]
    noise_scale = lax.rsqrt(level_col * level_col + 1.0)
    noisy_rows = ((embedded * unit_factor + level_col * noise) * noise_scale).astype(bf16)
    time_feats = time_features(noise_level)
    conditioned = jnp.dot(time_feats, w_time[0].astype(f32), precision=highest) + norm_gain[0]
    scale_attn = conditioned[:, None, :model_width]
    scale_mlp = conditioned[:, None, model_width:]
    scale = conditioned[:, None, :]
    weights = (w_qkv[0], w_out[0], w_up[0], b_hidden[0], w_down[0])
    stacked = (w_qkv, w_out, w_up, b_hidden, w_down)
    if straight:
        noisy_rows, head_core, head_section = lax.optimization_barrier(
            (noisy_rows, head_core, head_section)
        )
        heads = [head_own, head_core, head_section, lax.ppermute(head_section, "core", swapped)]

    stream0 = mm("nse,ed->nsd", noisy_rows, w_in)
    flat = (tokens, model_width)
    if straight:
        start = stream0.reshape(flat)
        (first_out,) = forward_pass(start, scale, stacked)
        arrived = lax.ppermute(first_out, "section", swapped)
        block_out, final_rows, *kept = forward_pass(
            start, scale, stacked, arrived, out_gain[None, :]
        )
    else:
        first_out = layer_forward(stream0, scale_attn, scale_mlp, weights)[0].astype(bf16)
        arrived = lax.ppermute(first_out, "section", swapped)
        stream = jnp.where(is_first, stream0, arrived.astype(f32))
        block_out, kept = layer_forward(stream, scale_attn, scale_mlp, weights)
        final_normed, final_factor = norm_rows(block_out.astype(bf16).astype(f32))
        final_rows = (final_normed * out_gain).astype(bf16).reshape(flat)

    targets_group = lax.dynamic_slice_in_dim(
        all_targets.reshape(chips, cores, tokens), core, 1, 1
    )[:, 0]
    targets_group = lax.dynamic_slice_in_dim(targets_group, section * half, half, 1)
    if straight:
        grad_final, grad_head, lse, picks = head_pass(
            final_rows, targets_group.reshape(line, 1, tokens), heads, line, head_rows, length, 3
        )
        ce_part = jnp.sum(lse) / chips - jnp.sum(picks)
    else:
        targets_group = targets_group.reshape(-1)
        handed = lax.ppermute(final_rows[:half], "section", [(1, 0), (0, 1)])
        own_final = jnp.where(is_first, handed, final_rows[half:])
        group_final = lax.all_gather(own_final, ("line", "pair"), tiled=True)
        logits = mm("td,vd->tv", group_final, head_group)
        local_top = jnp.max(logits, -1)
        local_total = jnp.sum(jnp.exp(logits - local_top[:, None]), -1)
        mark = columns[None, :] == targets_group[:, None]
        local_pick = jnp.sum(jnp.where(mark, logits, 0.0))
        stats = lax.all_gather(jnp.stack([local_top, local_total]), ("line", "pair"))
        all_top = jnp.max(stats[:, 0], 0)
        all_total = jnp.sum(stats[:, 1] * jnp.exp(stats[:, 0] - all_top), 0)
        log_total = all_top + jnp.log(all_total)
        soft_rows = jnp.exp(logits - log_total[:, None])
        logit_grads = ((soft_rows - jnp.where(mark, 1.0, 0.0)) / length).astype(bf16)
        grad_final = jnp.dot(logit_grads, head_group, preferred_element_type=f32).astype(bf16)
        grad_final = lax.psum_scatter(grad_final, ("line", "pair"), scatter_dimension=0, tiled=True)
        handed = lax.ppermute(grad_final, "section", swapped)
        grad_final = jnp.concatenate([handed, grad_final], 0)
        grad_head = mm("tv,td->vd", logit_grads, group_final).astype(bf16)
        grad_head = grad_head.reshape(sections, cores, head_rows, model_width)
        grad_head = lax.psum_scatter(grad_head, "core", scatter_dimension=1)
        grad_head = lax.psum_scatter(grad_head, "section", scatter_dimension=0).astype(f32)

        ce_part = jnp.sum(log_total) / chips - local_pick
    if straight:
        grad_second, grad_top, out_part = backward_pass(
            grad_final, block_out, scale, kept, stacked, out_gain[None, :]
        )
        returned = lax.ppermute(grad_second, "section", swapped)
        grad_first, grad_branch, grad_up, grad_attn, grad_joined, grad_cond, grad_bias = (
            backward_pass(returned, grad_top, scale, kept, stacked)
        )
        grad_first = grad_first.reshape(stream0.shape)
        out_part = out_part.reshape(-1)
        _, _, mixed, _, entry_attn, entry_mlp, _, hidden = kept
        grads = {
            "down": by_owner(mm("tf,td->fd", hidden, grad_branch)),
            "up": by_owner(mm("td,tf->df", entry_mlp, grad_up)),
            "qkv": by_owner(mm("td,te->de", entry_attn, grad_joined)),
            "out": by_owner(mm("td,te->de", mixed, grad_attn)),
            "cond": grad_cond,
            "bias": grad_bias.reshape(-1),
        }
    else:
        grad_final = grad_final.astype(f32).reshape(stream0.shape)
        out_part = jnp.sum(grad_final * final_normed, (0, 1))
        grad_top = norm_back(grad_final * out_gain, final_normed, final_factor)
        grad_second = layer_backward(grad_top, kept, scale_attn, scale_mlp, weights, False)[0]
        returned = lax.ppermute(grad_second.astype(bf16), "section", swapped)
        grad_cot = jnp.where(is_first, returned.astype(f32), grad_top)
        grad_stream, grads = layer_backward(grad_cot, kept, scale_attn, scale_mlp, weights, True)
        grad_first = grad_stream.astype(bf16)
    out_part = jnp.where(is_first, 0.0, out_part)

    in_part = mm("nse,nsd->ed", noisy_rows, grad_first).astype(bf16)
    in_part = in_part.reshape(sections, line, 2, 2, -1, model_width)
    in_part = jnp.moveaxis(in_part, 0, 3).reshape(line, 2, 2, -1, model_width)
    grad_noisy = mm("nsd,ed->nse", grad_first, w_in)
    grad_unit = grad_noisy * noise_scale
    cubed = unit_factor * unit_factor * unit_factor
    grad_embedded = unit_factor * grad_unit - cubed * embedded * jnp.mean(
        grad_unit * embedded, -1, keepdims=True
    )
    grad_flat = grad_embedded.reshape(tokens, emb_width)

    ce_high = ce_part.astype(bf16).astype(f32)
    ce_mid = (ce_part - ce_high).astype(bf16).astype(f32)
    ce_low = ce_part - ce_high - ce_mid
    shared = jnp.concatenate([out_part, jnp.stack([ce_high, ce_mid, ce_low])])
    shared_rows = -(-shared.shape[0] // emb_width)
    shared = jnp.pad(shared, (0, shared_rows * emb_width - shared.shape[0]))
    handing = jnp.concatenate([grad_flat, shared.reshape(-1, emb_width)], 0).astype(bf16)
    handed = lax.ppermute(handing, "section", swapped)
    kept_rows = jnp.where(is_first, handing[:half], handed[half:tokens])
    layer_small = jnp.concatenate([grads["cond"].reshape(-1), grads["bias"]])
    layer_rows = layer_small.shape[0] // emb_width
    small = jnp.concatenate(
        [
            layer_small.astype(bf16).reshape(layer_rows, emb_width),
            handing[tokens:],
            handed[tokens:],
        ],
        0,
    )
    small = jnp.pad(small, ((0, -small.shape[0] % 16), (0, 0)))
    parts = [grads["down"], grads["up"], grads["qkv"], grads["out"], in_part]
    if straight:
        *sums, smalls, halves, grad_head = summed_over_dp(
            parts, 2, packets=(small, kept_rows), head_part=grad_head, head_rows=head_rows
        )
    else:
        sums = [over_dp(part.reshape((dp_count,) + part.shape[3:])).astype(f32) for part in parts]
        smalls = lax.all_gather(small, DP)
        halves = lax.all_gather(kept_rows, ("section",) + DP)
        in_sum = sums[-1].reshape(sections, -1, model_width)
        in_handed = lax.ppermute(in_sum[1], "section", swapped)
        sums[-1] = jnp.where(is_first, in_sum[0], in_handed)
    grad_down, grad_up, grad_qkv, grad_wout, grad_w_in = sums

    grad_all = halves.reshape(-1, emb_width)
    tokens_all = all_tokens.reshape(dp_count, sections, half).swapaxes(0, 1).reshape(-1)
    out_rows = emb_rows // sections
    target_rows = (section * dp_count + dp_index) * out_rows + jnp.arange(out_rows)
    place = (target_rows[:, None] == tokens_all[None, :]).astype(bf16)
    grad_embed = jnp.dot(place, grad_all, preferred_element_type=f32)

    smalls = smalls.reshape(dp_count, -1, emb_width).astype(f32)
    layer_small = smalls[:, :layer_rows].reshape(dp_count, -1)
    cond_size = grads["cond"].size
    cond_all = layer_small[:, :cond_size].reshape(dp_count * seqs, 2 * model_width)
    hidden_rows = grads["bias"].shape[0] // dp_count
    grad_bias = jnp.sum(
        lax.dynamic_slice_in_dim(layer_small, cond_size + dp_index * hidden_rows, hidden_rows, 1), 0
    )
    norm_cols = 2 * model_width // dp_count
    grad_gain = jnp.sum(lax.dynamic_slice_in_dim(cond_all, dp_index * norm_cols, norm_cols, 1), 0)
    feats_all = time_features(levels_of(all_bins, sigma_table))
    feat_rows = TFEAT // dp_count
    feats_own = lax.dynamic_slice_in_dim(feats_all, dp_index * feat_rows, feat_rows, 1)
    grad_time = jnp.dot(feats_own.T, cond_all, precision=highest)
    both = smalls[:, layer_rows : layer_rows + 2 * shared_rows]
    both = jnp.sum(both.reshape(dp_count, 2, -1), (0, 1))
    loss = jnp.sum(both[model_width : model_width + 3]) / (tokens * dp_count)
    gain_rows = model_width // dp_count
    grad_out_gain = lax.dynamic_slice_in_dim(both, dp_index * gain_rows, gain_rows)
    return (
        loss,
        grad_embed,
        grad_w_in,
        grad_time[None],
        grad_gain[None],
        grad_qkv[None],
        grad_wout[None],
        grad_up[None],
        grad_bias[None],
        grad_down[None],
        grad_out_gain,
        grad_head,
    )


def solution(mesh):
    sections, dp_count = mesh.shape["section"], mesh.shape["dp"]
    fine = Mesh(mesh.devices.reshape(sections, dp_count // 4, 2, 2), ("section",) + DP)
    everywhere = ("section",) + DP
    in_specs = (
        P(DP, None),
        P(DP, None),
        P(DP),
        P(),
        P(DP, None, None),
        P(DP, None),
        P(),
        P("section", None, None),
        P("section", None),
        P("section", None, None),
        P("section", None, None),
        P("section", None, None),
        P("section", None),
        P("section", None, None),
        P(),
        P(everywhere, None),
    )
    out_specs = (
        P(),
        P(everywhere, None),
        P(everywhere, None),
        P("section", DP, None),
        P("section", DP),
        P("section", DP, None),
        P("section", DP, None),
        P("section", DP, None),
        P("section", DP),
        P("section", DP, None),
        P(DP),
        P(everywhere, None),
    )
    return jax.shard_map(local, mesh=fine, in_specs=in_specs, out_specs=out_specs, check_vma=False)
```

```python
from functools import partial
import math

import jax
import jax.numpy as jnp
from jax import lax
from jax.experimental import pallas as pl
from jax.experimental.pallas import tpu as pltpu
from jax.sharding import Mesh, PartitionSpec as P

HEADS = 16
HEAD_DIM = 64
TFEAT = 256

epsilon = 1e-05
highest = lax.Precision.HIGHEST
f32 = jnp.float32
bf16 = jnp.bfloat16
DP = ("line", "pair", "core")


MESH = pl.DeviceIdType.MESH


def nt(left, right):
    return lax.dot_general(left, right, (((1,), (1,)), ((), ())), preferred_element_type=f32)


def tn(left, right):
    return lax.dot_general(left, right, (((0,), (0,)), ((), ())), preferred_element_type=f32)


def nn(left, right):
    return jnp.dot(left, right, preferred_element_type=f32)


def greet(peers):
    barrier = pltpu.get_barrier_semaphore()
    for peer in peers:
        pl.semaphore_signal(barrier, inc=1, device_id=peer, device_id_type=MESH)
    pl.semaphore_wait(barrier, len(peers))


def remote(source, target, send, recv, peer):
    return pltpu.make_async_remote_copy(
        src_ref=source,
        dst_ref=target,
        send_sem=send,
        recv_sem=recv,
        device_id=peer,
        device_id_type=MESH,
    )


def ring_place(position, line):
    turned = position // line
    return position * (1 - turned) + (2 * line - 1 - position) * turned, turned


def sum_kernel(shapes, line, half_rows, with_head, cross, work, *refs):
    count = len(shapes)
    with_packet = half_rows > 0
    refs = list(refs)
    extra_ins, extra_outs, extra_scratch = work[1:] if work else (0, 0, 0)

    def take(number):
        return [refs.pop(0) for _ in range(number)]

    parts = take(count)
    sent = take(2) if with_packet else []
    head_part = take(1)[0] if with_head else None
    extra = take(extra_ins)
    outs = take(count)
    smalls, halves = take(2) if with_packet else (None, None)
    head_out = take(1)[0] if with_head else None
    extra += take(extra_outs)
    own, from_core, slots = take(count), take(count), take(count)
    load_sem, core_send, core_recv, ring_send, ring_recv = take(5)
    if with_packet:
        own_sem, packet_send, packet_recv, wide_send, wide_recv, half_send, half_recv = take(7)
    if with_head:
        head_own, head_core, head_section, head_sem, head_send, head_recv = take(6)
    if cross:
        last_total, cross_send, cross_recv = take(3)
    slices = work[0](extra + take(extra_scratch)) if work else []

    chips = 2 * line
    me_section = lax.axis_index("section")
    me_line = lax.axis_index("line")
    me_pair = lax.axis_index("pair")
    me_core = lax.axis_index("core")
    position = me_line + me_pair * (chips - 1 - 2 * me_line)
    section_peer = {"section": 1 - me_section}
    core_peer = {"core": 1 - me_core}
    ways = (1, -1)
    ring_peers = []
    for way in ways:
        peer_line, peer_pair = ring_place(lax.rem(position + way + chips, chips), line)
        ring_peers.append({"line": peer_line, "pair": peer_pair})
    greet([core_peer] + ring_peers + ([section_peer] if with_packet or with_head or cross else []))

    def block_of(turn, step):
        ahead = lax.rem(position - ways[turn] * (1 + step) + 2 * chips, chips)
        return ring_place(ahead, line)

    def columns(index, turn):
        wide = shapes[index][-1] // 2
        return pl.ds(turn * wide, wide)

    def load(index, turn, step):
        place, pair = block_of(turn, step)
        cols = columns(index, turn)
        return pltpu.make_async_copy(
            parts[index].at[place, pair, me_core, :, cols],
            own[index].at[step % 2, :, cols],
            load_sem.at[index, turn, step],
        )

    def core_copy(index, turn, step):
        place, pair = block_of(turn, step)
        cols = columns(index, turn)
        return remote(
            parts[index].at[place, pair, 1 - me_core, :, cols],
            from_core[index].at[step, :, cols],
            core_send.at[index, turn, step],
            core_recv.at[index, turn, step],
            core_peer,
        )

    def ring_copy(index, turn, step):
        cols = columns(index, turn)
        if isinstance(step, int) and step == 0:
            source = from_core[index].at[0, :, cols]
        else:
            source = slots[index].at[step - 1, :, cols]
        return remote(
            source,
            slots[index].at[step, :, cols],
            ring_send.at[index, turn, step],
            ring_recv.at[index, turn, step],
            ring_peers[turn],
        )

    def to_core(step):
        for index in range(count):
            for turn in range(2):
                load(index, turn, step).start()
                core_copy(index, turn, step).start()

    def stop(step):
        first = isinstance(step, int) and step == 0
        last = isinstance(step, int) and step == chips - 1
        for index in range(count):
            rows = shapes[index][-2]
            wide = shapes[index][-1] // 2
            tile = min(wide, 512)
            for turn in range(2):
                load(index, turn, step).wait()
                core_copy(index, turn, step).wait_recv()
                if not first:
                    ring_copy(index, turn, step - 1).wait_recv()

                @pl.loop(0, rows // 16)
                def _(block):
                    row = pl.ds(pl.multiple_of(block * 16, 16), 16)
                    for col in range(turn * wide, (turn + 1) * wide, tile):
                        cols = pl.ds(col, tile)
                        total = from_core[index][step, row, cols].astype(f32)
                        total = total + own[index][step % 2, row, cols].astype(f32)
                        if not first:
                            total = total + slots[index][step - 1, row, cols].astype(f32)
                        if last and cross and index == count - 1:
                            last_total[row, cols] = total
                        elif last:
                            outs[index][row, cols] = total
                        elif first:
                            from_core[index][0, row, cols] = total.astype(bf16)
                        else:
                            slots[index][step - 1, row, cols] = total.astype(bf16)

                if not last:
                    ring_copy(index, turn, step).start()
                if slices:
                    slices.pop(0)()

    hops = (line, line - 1)

    def packet_blocks(place, pair):
        return [smalls.at[place, pair, me_core], halves.at[me_section, place, pair, me_core]]

    def packet_hops(turn, hop, away):
        place, pair = ring_place(
            lax.rem(position - ways[turn] * (hop + away) + 2 * chips, chips), line
        )
        return [
            remote(
                block,
                block,
                packet_send.at[n, turn, hop],
                packet_recv.at[n, turn, hop],
                ring_peers[turn],
            )
            for n, block in enumerate(packet_blocks(place, pair))
        ]

    def pass_packets(hop):
        for turn in range(2):
            if 0 < hop <= hops[turn]:
                for copy in packet_hops(turn, hop - 1, 1):
                    copy.wait_recv()
            if hop < hops[turn]:
                for copy in packet_hops(turn, hop, 0):
                    copy.start()

    if with_packet:
        keeps = [
            pltpu.make_async_copy(block, target, own_sem.at[n])
            for n, (block, target) in enumerate(zip(sent, packet_blocks(me_line, me_pair)))
        ]
        for keep in keeps:
            keep.start()
        columns_of = [smalls.at[:, :, me_core], halves.at[me_section, :, :, me_core]]
        across = [
            remote(block, block, wide_send.at[n], wide_recv.at[n], core_peer)
            for n, block in enumerate(columns_of)
        ]
        half_swap = remote(
            halves.at[me_section], halves.at[me_section], half_send, half_recv, section_peer
        )

    if with_head:
        high = head_part.shape[0] // 4

        def shard(n):
            return head_part.at[pl.ds(n * high, high)]

        head_loads = [
            pltpu.make_async_copy(shard(2 * n), head_own.at[n], head_sem.at[n]) for n in range(2)
        ]
        head_copies = [
            remote(shard(2 * n + 1), head_core.at[n], head_send.at[n], head_recv.at[n], core_peer)
            for n in range(2)
        ]
        head_copies.append(
            remote(head_core.at[1], head_section, head_send.at[2], head_recv.at[2], section_peer)
        )

        def head_rows(body):
            @pl.loop(0, high // 16)
            def _(block):
                body(pl.ds(pl.multiple_of(block * 16, 16), 16))

        def head_over_cores():
            for copy in head_loads:
                copy.wait()
            for copy in head_copies[:2]:
                copy.wait_recv()

            def add(rows):
                value = head_core[1, rows, :].astype(f32) + head_own[1, rows, :].astype(f32)
                head_core[1, rows, :] = value.astype(bf16)

            head_rows(add)
            head_copies[2].start()

        def head_over_sections():
            head_copies[2].wait_recv()

            def total(rows):
                return (
                    head_core[0, rows, :].astype(f32)
                    + head_own[0, rows, :].astype(f32)
                    + head_section[rows, :].astype(f32)
                )

            whole = head_out.shape[0] // 16
            rest = head_out.shape[0] % 16

            @pl.loop(0, whole)
            def _(block):
                rows = pl.ds(pl.multiple_of(block * 16, 16), 16)
                head_out[rows, :] = total(rows)

            if rest:
                value = total(pl.ds(whole * 16, 16))
                head_out[pl.ds(whole * 16, rest), :] = value[:rest]

    to_core(0)
    to_core(1)
    stop(0)
    if with_packet:
        for keep in keeps:
            keep.wait()
        pass_packets(0)
    for step in range(1, chips - 1):
        to_core(step + 1)
        if with_head and step == 1:
            for copy in head_loads + head_copies[:2]:
                copy.start()
        stop(step)
        if with_packet and step <= line:
            pass_packets(step)
            if step == line:
                for copy in across:
                    copy.start()
        if with_packet and step == line + 1:
            for copy in across:
                copy.wait_recv()
            half_swap.start()
        if with_head and step == 2:
            head_over_cores()
    stop(chips - 1)
    while slices:
        slices.pop(0)()
    if cross:
        each = outs[-1].shape[0]
        give = remote(
            last_total.at[pl.ds(each, each)], outs[-1], cross_send, cross_recv, section_peer
        )

        @pl.when(me_section == 0)
        def _():
            give.start()
            outs[-1][...] = last_total[pl.ds(0, each), :]

    if with_head:
        head_over_sections()
        for copy in head_copies:
            copy.wait_send()
    if with_packet:
        half_swap.wait()
        for copy in across:
            copy.wait_send()
        for turn in range(2):
            for hop in range(hops[turn]):
                for copy in packet_hops(turn, hop, 0):
                    copy.wait_send()
    for index in range(count):
        for turn in range(2):
            for step in range(chips):
                core_copy(index, turn, step).wait_send()
                if step < chips - 1:
                    ring_copy(index, turn, step).wait_send()

    if cross:

        @pl.when(me_section == 0)
        def _():
            give.wait_send()

        @pl.when(me_section == 1)
        def _():
            give.wait_recv()


def summed_over_dp(
    parts, collective_id, packets=(), head_part=None, head_rows=0, cross=False, work=None
):
    shapes = [part.shape for part in parts]
    line = shapes[0][0]
    chips = 2 * line
    count = len(parts)
    vmem = pl.BlockSpec(memory_space=pltpu.VMEM)
    anywhere = pl.BlockSpec(memory_space=pl.ANY)
    out_shape = [jax.ShapeDtypeStruct(shape[-2:], f32) for shape in shapes]
    if cross:
        high, deep = shapes[-1][-2:]
        out_shape[-1] = jax.ShapeDtypeStruct((high // 2, deep), f32)
    out_specs = [vmem] * count
    operands = list(parts)
    dma = pltpu.SemaphoreType.DMA
    scratch = [pltpu.VMEM((2,) + shape[-2:], bf16) for shape in shapes]
    scratch += [pltpu.VMEM((chips,) + shape[-2:], bf16) for shape in shapes]
    scratch += [pltpu.VMEM((chips - 1,) + shape[-2:], bf16) for shape in shapes]
    scratch += [dma((count, 2, chips))] * 3 + [dma((count, 2, chips - 1))] * 2
    cost = 5 * sum(math.prod(shape) for shape in shapes) + 2**26
    half_rows = 0
    if packets:
        small, half = packets
        half_rows = half.shape[0]
        operands += [small, half]
        out_shape.append(jax.ShapeDtypeStruct((line, 2, 2) + small.shape, small.dtype))
        out_shape.append(jax.ShapeDtypeStruct((2, line, 2, 2) + half.shape, half.dtype))
        out_specs += [anywhere, anywhere]
        scratch += [dma((2,)), dma((2, 2, line)), dma((2, 2, line)), dma((2,)), dma((2,)), dma, dma]
    if head_part is not None:
        high, deep = head_part.shape[0] // 4, head_part.shape[1]
        operands.append(head_part)
        out_shape.append(jax.ShapeDtypeStruct((head_rows, deep), f32))
        out_specs.append(vmem)
        scratch += [pltpu.VMEM((2, high, deep), bf16)] * 2 + [pltpu.VMEM((high, deep), bf16)]
        scratch += [dma((2,)), dma((3,)), dma((3,))]
    if cross:
        scratch += [pltpu.VMEM(shapes[-1][-2:], f32), dma, dma]
    in_specs = [anywhere] * len(operands)
    slices = None
    if work:
        make, ins, results, room = work
        operands += ins
        in_specs += [vmem] + [anywhere] * (len(ins) - 1)
        out_shape += results
        out_specs += [vmem] * len(results)
        scratch += room
        slices = (make, len(ins), len(results), len(room))
    return pl.pallas_call(
        partial(sum_kernel, shapes, line, half_rows, head_part is not None, cross, slices),
        out_shape=out_shape,
        in_specs=in_specs,
        out_specs=out_specs,
        scratch_shapes=scratch,
        compiler_params=pltpu.CompilerParams(
            collective_id=collective_id, has_side_effects=True, vmem_limit_bytes=60 * 2**20
        ),
        cost_estimate=pl.CostEstimate(flops=0, bytes_accessed=cost, transcendentals=0),
    )(*operands)


def rows_kernel(line, found, out, own, from_core, from_pair, from_line, *sems):
    load_sem, core_send, core_recv, pair_send, pair_recv, line_send, line_recv, swap_send, swap_recv = (
        sems
    )
    me_section = lax.axis_index("section")
    me_line = lax.axis_index("line")
    me_pair = lax.axis_index("pair")
    me_core = lax.axis_index("core")
    section_peer = {"section": 1 - me_section}
    core_peer = {"core": 1 - me_core}
    pair_peer = {"pair": 1 - me_pair}
    line_at = [lax.rem(me_line + step, line) for step in range(1, line)]
    greet([section_peer, core_peer, pair_peer] + [{"line": place} for place in line_at])
    rows, width = out.shape[-2:]
    wide = width // 2
    sides = (1 - me_pair, me_pair)
    loads, core_copies, pair_copies, line_copies = {}, {}, {}, {}
    for turn, side in enumerate(sides):
        for piece in range(2):
            cols = pl.ds(piece * wide, wide)
            loads[piece, turn] = pltpu.make_async_copy(
                found.at[:, side, me_core, :, cols],
                own.at[:, side, :, cols],
                load_sem.at[piece, turn],
            )
            core_copies[piece, turn] = remote(
                found.at[:, side, 1 - me_core, :, cols],
                from_core.at[:, side, :, cols],
                core_send.at[piece, turn],
                core_recv.at[piece, turn],
                core_peer,
            )
            loads[piece, turn].start()
            core_copies[piece, turn].start()

    def tiles(body):
        @pl.loop(0, rows // 16)
        def _(block):
            body(pl.ds(pl.multiple_of(block * 16, 16), 16))

    for piece in range(2):
        cols = pl.ds(piece * wide, wide)
        side = sides[0]
        loads[piece, 0].wait()
        core_copies[piece, 0].wait_recv()

        def add(row):
            for place in range(line):
                total = from_core[place, side, row, cols] + own[place, side, row, cols]
                from_core[place, side, row, cols] = total

        tiles(add)
        pair_copies[piece] = remote(
            from_core.at[:, side, :, cols],
            from_pair.at[:, :, cols],
            pair_send.at[piece],
            pair_recv.at[piece],
            pair_peer,
        )
        pair_copies[piece].start()
    for piece in range(2):
        cols = pl.ds(piece * wide, wide)
        loads[piece, 1].wait()
        core_copies[piece, 1].wait_recv()
        pair_copies[piece].wait_recv()

        def add(row):
            for place in range(line):
                total = from_core[place, me_pair, row, cols] + own[place, me_pair, row, cols]
                from_core[place, me_pair, row, cols] = total + from_pair[place, row, cols]

        tiles(add)
        for n in range(line - 1):
            line_copies[piece, n] = remote(
                from_core.at[line_at[n], me_pair, :, cols],
                from_line.at[n, :, cols],
                line_send.at[piece, n],
                line_recv.at[piece, n],
                {"line": line_at[n]},
            )
            line_copies[piece, n].start()
    for piece in range(2):
        cols = pl.ds(piece * wide, wide)
        for n in range(line - 1):
            line_copies[piece, n].wait_recv()

        def add(row):
            total = from_core[me_line, me_pair, row, cols]
            for n in range(line - 1):
                total = total + from_line[n, row, cols]
            out[me_section, row, cols] = total

        tiles(add)
    swap = remote(out.at[me_section], out.at[me_section], swap_send, swap_recv, section_peer)
    swap.start()
    for copy in list(core_copies.values()) + list(pair_copies.values()) + list(line_copies.values()):
        copy.wait_send()
    swap.wait()


def rows_over_dp(found, collective_id):
    line = found.shape[0]
    shape = found.shape[-2:]
    dma = pltpu.SemaphoreType.DMA
    return pl.pallas_call(
        partial(rows_kernel, line),
        out_shape=jax.ShapeDtypeStruct((2,) + shape, bf16),
        in_specs=[pl.BlockSpec(memory_space=pl.ANY)],
        out_specs=pl.BlockSpec(memory_space=pltpu.VMEM),
        scratch_shapes=[
            pltpu.VMEM((line, 2) + shape, bf16),
            pltpu.VMEM((line, 2) + shape, bf16),
            pltpu.VMEM((line,) + shape, bf16),
            pltpu.VMEM((line - 1,) + shape, bf16),
        ]
        + [dma((2, 2))] * 3
        + [dma((2,))] * 2
        + [dma((2, line - 1))] * 2
        + [dma, dma],
        compiler_params=pltpu.CompilerParams(
            collective_id=collective_id, has_side_effects=True, vmem_limit_bytes=32 * 2**20
        ),
        cost_estimate=pl.CostEstimate(flops=0, bytes_accessed=2**26, transcendentals=0),
    )(found)


def gather_kernel(line, mine, out, send, recv, own_sem):
    me_line = lax.axis_index("line")
    me_pair = lax.axis_index("pair")
    me_core = lax.axis_index("core")
    peers = []
    for step in range(1, line * 4):
        peers.append(
            {
                "line": lax.rem(me_line + step // 4, line),
                "pair": lax.rem(me_pair + step // 2 % 2, 2),
                "core": lax.rem(me_core + step % 2, 2),
            }
        )
    greet(peers)
    place = out.at[me_line, me_pair, me_core]
    keep = pltpu.make_async_copy(mine, place, own_sem)
    keep.start()
    copies = [remote(mine, place, send.at[n], recv.at[n], peer) for n, peer in enumerate(peers)]
    for copy in copies:
        copy.start()
    keep.wait()
    for copy in copies:
        copy.wait()


def gathered_small(block, line, collective_id):
    count = line * 4 - 1
    vmem = pl.BlockSpec(memory_space=pltpu.VMEM)
    return pl.pallas_call(
        partial(gather_kernel, line),
        out_shape=jax.ShapeDtypeStruct((line, 2, 2) + block.shape, block.dtype),
        in_specs=[vmem],
        out_specs=vmem,
        scratch_shapes=[
            pltpu.SemaphoreType.DMA((count,)),
            pltpu.SemaphoreType.DMA((count,)),
            pltpu.SemaphoreType.DMA,
        ],
        compiler_params=pltpu.CompilerParams(collective_id=collective_id, has_side_effects=True),
        cost_estimate=pl.CostEstimate(flops=0, bytes_accessed=2**25, transcendentals=0),
    )(block)


def head_kernel(line, head_rows, length, *refs):
    final, targets, *heads = refs[:6]
    out, grads, lse_out, pick_out = refs[6:10]
    (table, rows_all, logits, probs, acc, parts, from_pair, from_line, stats, done) = refs[10:20]
    (head_sem, own_sem, give_send, give_recv, along_send, along_recv, pair_send, pair_recv) = refs[20:28]
    (stat_send, stat_recv, sum_send, sum_recv, line_send, line_recv, back_send, back_recv) = refs[28:]
    half = final.shape[0] // 2
    width = 2 * half
    padded = heads[0].shape[0]
    me_section = lax.axis_index("section")
    me_line = lax.axis_index("line")
    me_pair = lax.axis_index("pair")
    me_core = lax.axis_index("core")
    section_peer = {"section": 1 - me_section}
    pair_peer = {"pair": 1 - me_pair}
    chip_peers = []
    for step in range(1, 2 * line):
        chip_peers.append(
            {"line": lax.rem(me_line + step // 2, line), "pair": lax.rem(me_pair + step % 2, 2)}
        )
    greet(chip_peers + [section_peer])

    def side(pair):
        return pl.ds(pl.multiple_of(pair * half, 16), half)

    loads = [
        pltpu.make_async_copy(part, table.at[pl.ds(n * padded, padded)], head_sem.at[n])
        for n, part in enumerate(heads)
    ]
    for load in loads:
        load.start()

    def token_rows(place, pair):
        return pl.ds(pl.multiple_of(place * width + pair * half, 16), half)

    def group(place):
        return pl.ds(pl.multiple_of(place * width, 128), width)

    mine = rows_all.at[token_rows(me_line, me_pair)]
    give = remote(final.at[pl.ds(0, half)], mine, give_send, give_recv, section_peer)

    @pl.when(me_section == 1)
    def _():
        give.start()
        keep = pltpu.make_async_copy(final.at[pl.ds(half, half)], mine, own_sem)
        keep.start()
        keep.wait()

    @pl.when(me_section == 0)
    def _():
        give.wait_recv()

    def column_block(place):
        return rows_all.at[token_rows(place, me_pair)]

    def along(step, way):
        block = column_block(me_line - way * step)
        turn = (way + 1) // 2
        return remote(
            block,
            block,
            along_send.at[turn, step],
            along_recv.at[turn, step],
            {"line": me_line + way},
        )

    def inside(place):
        return (place >= 0) & (place < line)

    def sends_along(step, way):
        return inside(me_line - way * step) & inside(me_line + way)

    def sideways(place):
        block = column_block(place)
        return remote(block, block, pair_send.at[place], pair_recv.at[place], pair_peer)

    def arrived_sideways(place):
        block = rows_all.at[token_rows(place, 1 - me_pair)]
        return remote(block, block, pair_send.at[place], pair_recv.at[place], pair_peer)

    for way in (1, -1):

        @pl.when(sends_along(0, way))
        def _():
            along(0, way).start()

    sideways(me_line).start()

    def pass_on(step):
        for way in (1, -1):
            place = me_line - way * step

            @pl.when(inside(place))
            def _():
                block = column_block(place)
                turn = (way + 1) // 2
                remote(
                    block,
                    block,
                    along_send.at[turn, step - 1],
                    along_recv.at[turn, step - 1],
                    {"line": me_line - way},
                ).wait_recv()

                @pl.when(inside(me_line + way))
                def _():
                    along(step, way).start()

                sideways(place).start()

    nearest = []
    for own in range(line):
        near = [own]
        for step in range(1, line):
            near += [place for place in (own - step, own + step) if 0 <= place < line]
        nearest.append(near)

    def by_distance(turn):
        place = 0
        for own in range(line):
            for n in range(line):
                hit = ((me_line == own) & (turn == n)).astype(jnp.int32)
                place = place + hit * nearest[own][n]
        return place

    def vocabulary(tile, rows):
        shard = tile * rows // padded
        first = lax.rem(tile * rows, padded)
        shard_section = lax.rem(me_section + shard // 2, 2)
        shard_core = lax.rem(me_core + lax.rem(shard, 2), 2)
        base = (((shard_section * line + me_line) * 2 + me_pair) * 2 + shard_core) * head_rows
        row = lax.broadcasted_iota(jnp.int32, (rows, 1), 0) + first
        return jnp.where(row < head_rows, row + base, -1)

    tile_rows = 512
    tiles = 4 * padded // tile_rows
    lowest = -1e30

    def score(turn, tops):
        place = by_distance(turn) if turn < line else None
        before = by_distance(turn - 1) if turn > 0 else None
        wanted = None if place is None else targets[place]

        def one(tile, carry):
            rows = pl.ds(pl.multiple_of(tile * tile_rows, tile_rows), tile_rows)
            out = []
            if place is not None:
                top, pick = carry[:2]
                entry = vocabulary(tile, tile_rows)
                part = nt(table[rows, :], rows_all[group(place), :])
                part = jnp.where(entry >= 0, part, lowest)
                logits[turn % 2, rows, :] = part
                out.append(jnp.maximum(top, jnp.max(part, 0, keepdims=True)))
                out.append(
                    pick + jnp.sum(jnp.where(entry == wanted, part, 0.0), 0, keepdims=True)
                )
            if before is not None:
                value = jnp.exp(logits[(turn - 1) % 2, rows, :] - tops)
                probs[rows, group(before)] = value.astype(bf16)
                out.append(carry[-1] + jnp.sum(value, 0, keepdims=True))
            return tuple(out)

        none = jnp.zeros((1, width), f32)
        start = () if place is None else (jnp.full((1, width), lowest, f32), none)
        start += () if before is None else (none,)
        result = lax.fori_loop(0, tiles, one, start)
        if place is not None:
            pick_out[place] = result[1]
        if before is not None:
            own = stats.at[me_line, me_pair, before]
            own[0:1, :] = tops
            own[1:2, :] = result[-1]
            for n in range(len(chip_peers)):
                stat_copy(n, before).start()
        return None if place is None else result[0]

    def stat_copy(n, place):
        own = stats.at[me_line, me_pair, place]
        return remote(own, own, stat_send.at[n, place], stat_recv.at[n, place], chip_peers[n])

    def stat_wait(n, place):
        peer = chip_peers[n]
        source_line = lax.rem(2 * me_line + line - peer["line"], line)
        source_pair = peer["pair"]
        block = stats.at[source_line, source_pair, place]
        remote(block, block, stat_send.at[n, place], stat_recv.at[n, place], peer).wait_recv()

    for load in loads:
        load.wait()

    tops = None
    for turn in range(line + 1):
        if turn + 1 < line:
            pass_on(turn + 1)
        if turn < line:
            arrived_sideways(by_distance(turn)).wait_recv()
        tops = score(turn, tops)

    def sum_copy(turn):
        place = lax.rem(me_line + turn + 1, line)
        return remote(
            parts.at[place, side(1 - me_pair)],
            from_pair.at[turn],
            sum_send.at[turn],
            sum_recv.at[turn],
            pair_peer,
        )

    def line_copy(turn):
        place = lax.rem(me_line + turn + 1, line)
        return remote(
            parts.at[place, side(me_pair)],
            from_line.at[turn],
            line_send.at[turn],
            line_recv.at[turn],
            {"line": place},
        )

    def finish(turn):
        place = lax.rem(me_line + turn + 1, line)
        sum_copy(turn).wait_recv()
        own = parts.at[place, side(me_pair)]

        @pl.loop(0, half // 16)
        def _(block):
            rows = pl.ds(pl.multiple_of(block * 16, 16), 16)
            value = own[rows, :].astype(f32) + from_pair[turn, rows, :].astype(f32)
            own[rows, :] = value.astype(bf16)

    @pl.loop(0, line)
    def _(turn):
        place = lax.rem(me_line + turn + 1, line)
        for n in range(len(chip_peers)):
            stat_wait(n, place)
        tops = [stats[a, b, place, 0:1, :] for a in range(line) for b in range(2)]
        totals = [stats[a, b, place, 1:2, :] for a in range(line) for b in range(2)]
        top = tops[0]
        for value in tops[1:]:
            top = jnp.maximum(top, value)
        total = jnp.zeros_like(top)
        for peak, part in zip(tops, totals):
            total = total + part * jnp.exp(peak - top)
        lse = top + jnp.log(total)
        lse_out[place] = lse
        factor = jnp.exp(stats[me_line, me_pair, place, 0:1, :] - lse) / length
        wanted = targets[place]

        def scaled(tile):
            rows = pl.ds(tile * padded, padded)
            entry = vocabulary(tile, padded)
            grad = probs[rows, group(place)].astype(f32) * factor
            grad = (grad - jnp.where(entry == wanted, 1.0 / length, 0.0)).astype(bf16)
            probs[rows, group(place)] = grad
            return grad

        grad = scaled(0)
        for tile in range(4):
            product = tn(grad, table[pl.ds(tile * padded, padded), :])
            if tile < 3:
                grad = scaled(tile + 1)
                acc[...] = product if tile == 0 else acc[...] + product
            else:
                parts[place] = (acc[...] + product).astype(bf16)

        sum_copy(turn).start()

        @pl.when(turn > 0)
        def _():
            finish(turn - 1)
            line_copy(turn - 1).start()

    gh_rows = 256
    gh_tiles = 4 * padded // gh_rows

    def head_grads(first, last):
        @pl.loop(first, last)
        def _(tile):
            rows = pl.ds(pl.multiple_of(tile * gh_rows, gh_rows), gh_rows)
            value = jnp.dot(probs[rows, :], rows_all[...], preferred_element_type=f32)
            grads[rows, :] = value.astype(bf16)

    head_grads(0, gh_tiles // 2)
    finish(line - 1)
    for turn in range(line - 1):
        line_copy(turn).wait_recv()
    own = parts.at[me_line, side(me_pair)]

    @pl.loop(0, half // 16)
    def _(block):
        rows = pl.ds(pl.multiple_of(block * 16, 16), 16)
        value = own[rows, :].astype(f32)
        for turn in range(line - 1):
            value = value + from_line[turn, rows, :].astype(f32)
        done[rows, :] = value.astype(bf16)

    back = remote(done, out.at[pl.ds(0, half)], back_send, back_recv, section_peer)

    @pl.when(me_section == 0)
    def _():
        back.start()
        out[...] = jnp.zeros_like(out)

    @pl.when(me_section == 1)
    def _():
        out[pl.ds(half, half), :] = done[...]

    head_grads(gh_tiles // 2, gh_tiles)

    @pl.when(me_section == 0)
    def _():
        back.wait_send()

    @pl.when(me_section == 1)
    def _():
        back.wait_recv()
        give.wait_send()

    for way in (1, -1):
        for step in range(line - 1):

            @pl.when(sends_along(step, way))
            def _():
                along(step, way).wait_send()

    for place in range(line):
        sideways(place).wait_send()
        for n in range(len(chip_peers)):
            stat_copy(n, place).wait_send()
    for turn in range(line):
        sum_copy(turn).wait_send()
    for turn in range(line - 1):
        line_copy(turn).wait_send()


def head_pass(final, targets, heads, line, head_rows, length, collective_id):
    tokens, deep = final.shape
    half = tokens // 2
    padded = heads[0].shape[0]
    vmem = pl.BlockSpec(memory_space=pltpu.VMEM)
    anywhere = pl.BlockSpec(memory_space=pl.ANY)
    dma = pltpu.SemaphoreType.DMA
    peers = 2 * line - 1
    return pl.pallas_call(
        partial(head_kernel, line, head_rows, length),
        out_shape=[
            jax.ShapeDtypeStruct((tokens, deep), bf16),
            jax.ShapeDtypeStruct((4 * padded, deep), bf16),
            jax.ShapeDtypeStruct((line, 1, tokens), f32),
            jax.ShapeDtypeStruct((line, 1, tokens), f32),
        ],
        in_specs=[vmem, vmem] + [anywhere] * 4,
        out_specs=[vmem] * 4,
        scratch_shapes=[
            pltpu.VMEM((4 * padded, deep), bf16),
            pltpu.VMEM((line * tokens, deep), bf16),
            pltpu.VMEM((2, 4 * padded, tokens), f32),
            pltpu.VMEM((4 * padded, line * tokens), bf16),
            pltpu.VMEM((tokens, deep), f32),
            pltpu.VMEM((line, tokens, deep), bf16),
            pltpu.VMEM((line, half, deep), bf16),
            pltpu.VMEM((line - 1, half, deep), bf16),
            pltpu.VMEM((line, 2, line, 8, tokens), f32),
            pltpu.VMEM((half, deep), bf16),
            dma((4,)),
            dma,
            dma,
            dma,
            dma((2, line)),
            dma((2, line)),
            dma((line,)),
            dma((line,)),
            dma((peers, line)),
            dma((peers, line)),
            dma((line,)),
            dma((line,)),
            dma((line,)),
            dma((line,)),
            dma,
            dma,
        ],
        compiler_params=pltpu.CompilerParams(
            collective_id=collective_id, has_side_effects=True, vmem_limit_bytes=60 * 2**20
        ),
        cost_estimate=pl.CostEstimate(
            flops=24 * line * padded * tokens * deep, bytes_accessed=2**28, transcendentals=0
        ),
    )(final, targets, *heads)


def row_stats(values):
    centred = values - jnp.mean(values, -1, keepdims=True)
    factor = lax.rsqrt(jnp.mean(centred * centred, -1, keepdims=True) + epsilon)
    return centred * factor, factor


def two_heads(block):
    first = lax.broadcasted_iota(jnp.int32, block.shape, 1) < HEAD_DIM
    zero = jnp.zeros_like(block)
    return jnp.concatenate([jnp.where(first, block, zero), jnp.where(first, zero, block)], 0)


def one_block(stacked):
    rows = stacked.shape[0] // 2
    first = lax.broadcasted_iota(jnp.int32, (rows, stacked.shape[1]), 1) < HEAD_DIM
    return jnp.where(first, stacked[:rows], stacked[rows:])


def attention_weights(queries, keys):
    scores = nt(keys, queries) * (1.0 / math.sqrt(HEAD_DIM))
    exped = jnp.exp(scores - jnp.max(scores, 0, keepdims=True))
    return exped * (1.0 / jnp.sum(exped, 0, keepdims=True))


def tile_of(index, size):
    return pl.ds(pl.multiple_of(index * size, size), size)


def forward_kernel(full, seqs, *refs):
    refs = list(refs)

    def take(number):
        return [refs.pop(0) for _ in range(number)]

    start, scale, bias = take(3)
    arrived, gain = take(2) if full else (None, None)
    weights = take(4)
    if full:
        out, final, x, joined, mixed, middle, entry_attn, entry_mlp, slope, hidden = take(10)
    else:
        (out,) = take(1)
        x = start
        joined, mixed, middle, entry_attn = take(4)
        entry_mlp = entry_attn
    w_qkv, w_out, w_up, w_down, total, sems = refs
    width = start.shape[1]
    length = start.shape[0] // seqs
    load_qkv, load_out, load_up, load_down = [
        pltpu.make_async_copy(source.at[0], target, sems.at[n])
        for n, (source, target) in enumerate(zip(weights, (w_qkv, w_out, w_up, w_down)))
    ]
    load_qkv.start()

    for seq in range(seqs):
        rows = pl.ds(seq * length, length)
        if full:
            first = (lax.axis_index("section") == 0).astype(f32)
            x[rows, :] = start[rows, :] * first + arrived[rows, :].astype(f32) * (1.0 - first)
        normed, _ = row_stats(x[rows, :])
        entry_attn[rows, :] = (normed * scale[seq, :, :width]).astype(bf16)

    load_qkv.wait()
    load_out.start()
    load_up.start()
    tile = 512

    @pl.loop(0, 3 * width // tile)
    def _(index):
        cols = tile_of(index, tile)
        joined[:, cols] = nn(entry_attn[...], w_qkv[:, cols]).astype(bf16)

    load_out.wait()
    load_down.start()
    pairs = width // 128

    @pl.loop(0, pairs)
    def _(pair):
        cols = tile_of(pair, 128)
        for seq in range(seqs):
            rows = pl.ds(seq * length, length)
            queries = two_heads(joined[rows, cols])
            keys = joined[rows, tile_of(pair + pairs, 128)]
            values = joined[rows, tile_of(pair + 2 * pairs, 128)]
            probs = attention_weights(queries, keys).astype(bf16)
            mixed[rows, cols] = one_block(tn(probs, values)).astype(bf16)

    @pl.loop(0, width // tile)
    def _(index):
        cols = tile_of(index, tile)
        middle[:, cols] = x[:, cols] + nn(mixed[...], w_out[:, cols])

    for seq in range(seqs):
        rows = pl.ds(seq * length, length)
        normed, _ = row_stats(middle[rows, :])
        entry_mlp[rows, :] = (normed * scale[seq, :, width:]).astype(bf16)

    load_up.wait()
    load_down.wait()
    total[...] = middle[...]

    def gelu_of(up, cols):
        below = 0.5 + 0.5 * lax.erf(up * math.sqrt(0.5))
        value = (up * below).astype(bf16)
        if full:
            density = jnp.exp(-0.5 * up * up) * (1.0 / math.sqrt(2.0 * math.pi))
            slope[:, cols] = (below + up * density).astype(bf16)
            hidden[:, cols] = value
        return value

    @pl.loop(0, w_up.shape[1] // (2 * tile))
    def _(index):
        sides = [tile_of(2 * index + side, tile) for side in range(2)]
        ups = [nn(entry_mlp[...], w_up[:, cols]) + bias[:, cols] for cols in sides]
        both = jnp.concatenate([gelu_of(up, cols) for up, cols in zip(ups, sides)], 1)
        total[...] += nn(both, w_down[tile_of(index, 2 * tile), :])

    for seq in range(seqs):
        rows = pl.ds(seq * length, length)
        value = total[rows, :].astype(bf16)
        out[rows, :] = value
        if full:
            normed, _ = row_stats(value.astype(f32))
            final[rows, :] = (normed * gain[...]).astype(bf16)


def layer_scratch(width, hidden):
    return [
        pltpu.VMEM((width, 3 * width), bf16),
        pltpu.VMEM((width, width), bf16),
        pltpu.VMEM((width, hidden), bf16),
        pltpu.VMEM((hidden, width), bf16),
    ]


def forward_pass(start, scale, weights, arrived=None, gain=None):
    w_qkv, w_out, w_up, b_hidden, w_down = weights
    tokens, width = start.shape
    wide = w_up.shape[-1]
    full = arrived is not None
    vmem = pl.BlockSpec(memory_space=pltpu.VMEM)
    anywhere = pl.BlockSpec(memory_space=pl.ANY)

    def low(columns):
        return (tokens, columns), bf16

    exact = ((tokens, width), f32)
    out_shape = [jax.ShapeDtypeStruct((tokens, width), bf16)]
    scratch = layer_scratch(width, wide)
    scratch += [pltpu.VMEM(*exact), pltpu.SemaphoreType.DMA((4,))]
    operands = [start, scale, b_hidden]
    if full:
        operands += [arrived, gain]
        kept = [low(width), exact, low(3 * width), low(width), exact, low(width), low(width)]
        out_shape += [jax.ShapeDtypeStruct(*item) for item in kept + [low(wide), low(wide)]]
    else:
        inside = [low(3 * width), low(width), exact, low(width)]
        scratch = [pltpu.VMEM(*item) for item in inside] + scratch
    flops = 2 * tokens * (4 * width * width + 2 * width * wide)
    return pl.pallas_call(
        partial(forward_kernel, full, scale.shape[0]),
        out_shape=out_shape,
        in_specs=[vmem] * len(operands) + [anywhere] * 4,
        out_specs=[vmem] * len(out_shape),
        scratch_shapes=scratch,
        compiler_params=pltpu.CompilerParams(vmem_limit_bytes=60 * 2**20),
        cost_estimate=pl.CostEstimate(flops=2 * flops, bytes_accessed=2**25, transcendentals=0),
    )(*operands, w_qkv, w_out, w_up, w_down)


def norm_grads(source, total, grad_middle, scale, grad_cond, half, seq, store):
    width = total.shape[1]
    length = total.shape[0] // scale.shape[0]
    rows = pl.ds(seq * length, length)
    cols = pl.ds(half * width, width)
    normed, factor = row_stats(source[rows, :])
    gradient = total[rows, :]
    if grad_cond is not None:
        grad_cond[seq, :, cols] = jnp.sum(gradient * normed, 0, keepdims=True)
    scaled = gradient * scale[seq, :, cols]
    back = factor * (
        scaled
        - jnp.mean(scaled, -1, keepdims=True)
        - normed * jnp.mean(scaled * normed, -1, keepdims=True)
    )
    store(rows, grad_middle[rows, :] + back)


def attention_grads(joined, grad_mixed, grad_joined, pair, seqs):
    pairs = grad_mixed.shape[1] // 128
    length = grad_mixed.shape[0] // seqs
    shrink = 1.0 / math.sqrt(HEAD_DIM)
    cols = tile_of(pair, 128)
    key_cols = tile_of(pair + pairs, 128)
    value_cols = tile_of(pair + 2 * pairs, 128)
    for seq in range(seqs):
        rows = pl.ds(seq * length, length)
        queries = two_heads(joined[rows, cols])
        keys = joined[rows, key_cols]
        probs = attention_weights(queries, keys)
        grads = two_heads(grad_mixed[rows, cols])
        grad_probs = nt(joined[rows, value_cols], grads)
        inner = jnp.sum(grad_probs * probs, 0, keepdims=True)
        grad_scores = (probs * (grad_probs - inner)).astype(bf16)
        grad_joined[rows, cols] = (one_block(tn(grad_scores, keys)) * shrink).astype(bf16)
        grad_joined[rows, key_cols] = (nn(grad_scores, queries) * shrink).astype(bf16)
        grad_joined[rows, value_cols] = nn(probs.astype(bf16), grads).astype(bf16)


def backward_kernel(begin, seqs, *refs):
    refs = list(refs)

    def take(number):
        return [refs.pop(0) for _ in range(number)]

    if begin:
        incoming, other = take(2)
        far = take(3)
        grad_middle, total, grad_low, grad_up, grad_bias = take(5)
        near = take(3)
    else:
        scale, incoming, other, gain = take(4)
        far = take(8)
        out, grad_top, grad_gain = take(3)
        grad_low, grad_up, grad_attn, grad_joined = take(4)
        near = take(8)
        total, grad_middle, grad_mixed = take(3)
    (sems,) = refs
    if begin:
        slope, w_up, w_down = near
        load_slope = pltpu.make_async_copy(far[0], slope, sems.at[0])
        load_up = pltpu.make_async_copy(far[1].at[0], w_up, sems.at[1])
        load_down = pltpu.make_async_copy(far[2].at[0], w_down, sems.at[2])
    else:
        slope, w_up, w_down, x, middle, joined, w_qkv, w_out = near
        load_slope = pltpu.make_async_copy(far[0], slope, sems.at[0])
        load_up = pltpu.make_async_copy(far[1].at[0], w_up, sems.at[1])
        load_down = pltpu.make_async_copy(far[2].at[0], w_down, sems.at[2])
        load_x = pltpu.make_async_copy(far[3], x, sems.at[3])
        load_middle = pltpu.make_async_copy(far[4], middle, sems.at[4])
        load_joined = pltpu.make_async_copy(far[5], joined, sems.at[5])
        load_qkv = pltpu.make_async_copy(far[6].at[0], w_qkv, sems.at[6])
        load_out = pltpu.make_async_copy(far[7].at[0], w_out, sems.at[7])
    width = incoming.shape[1]
    length = incoming.shape[0] // seqs
    load_down.start()
    load_slope.start()

    for seq in range(seqs):
        rows = pl.ds(seq * length, length)
        if begin:
            first = (lax.axis_index("section") == 0).astype(f32)
            value = incoming[rows, :].astype(f32) * first + other[rows, :] * (1.0 - first)
        else:
            normed, factor = row_stats(other[rows, :].astype(f32))
            gradient = incoming[rows, :].astype(f32)
            part = jnp.sum(gradient * normed, 0, keepdims=True)
            grad_gain[...] = part if seq == 0 else grad_gain[...] + part
            scaled = gradient * gain[...]
            value = factor * (
                scaled
                - jnp.mean(scaled, -1, keepdims=True)
                - normed * jnp.mean(scaled * normed, -1, keepdims=True)
            )
            grad_top[rows, :] = value
        grad_middle[rows, :] = value
        grad_low[rows, :] = value.astype(bf16)

    load_down.wait()
    load_slope.wait()
    load_up.start()
    if not begin:
        load_middle.start()
        load_out.start()
        load_joined.start()
    tile = 1024

    @pl.loop(0, w_up.shape[1] // tile)
    def _(index):
        cols = tile_of(index, tile)
        grad_hidden = nt(grad_low[...], w_down[cols, :])
        value = (grad_hidden * slope[:, cols].astype(f32)).astype(bf16)
        grad_up[:, cols] = value
        if begin:
            grad_bias[:, cols] = jnp.sum(value.astype(f32), 0, keepdims=True)

    load_up.wait()
    if not begin:
        load_middle.wait()
        load_out.wait()
        load_joined.wait()
        load_qkv.start()
        load_x.start()

    @pl.loop(0, width // 256)
    def _(index):
        total[:, tile_of(index, 256)] = nt(grad_up[...], w_up[tile_of(index, 256), :])

    if begin:
        return

    def store_middle(rows, value):
        grad_middle[rows, :] = value
        grad_attn[rows, :] = value.astype(bf16)

    for seq in range(seqs):
        norm_grads(middle, total, grad_middle, scale, None, 1, seq, store_middle)

    @pl.loop(0, width // 512)
    def _(index):
        part = tile_of(index, 512)
        grad_mixed[:, part] = nt(grad_attn[...], w_out[part, :]).astype(bf16)

    @pl.loop(0, width // 128)
    def _(pair):
        attention_grads(joined, grad_mixed, grad_joined, pair, seqs)

    load_qkv.wait()
    load_x.wait()

    @pl.loop(0, width // 256)
    def _(index):
        total[:, tile_of(index, 256)] = nt(grad_joined[...], w_qkv[tile_of(index, 256), :])

    def store_out(rows, value):
        out[rows, :] = value.astype(bf16)

    for seq in range(seqs):
        norm_grads(x, total, grad_middle, scale, None, 0, seq, store_out)


def backward_pass(grad_final, block_out, gain, scale, kept, weights):
    w_qkv, w_out, w_up, _, w_down = weights
    x, joined, _, middle, _, _, slope, _ = kept
    tokens, width = x.shape
    wide = w_up.shape[-1]
    vmem = pl.BlockSpec(memory_space=pltpu.VMEM)
    anywhere = pl.BlockSpec(memory_space=pl.ANY)
    exact = ((tokens, width), f32)
    low = ((tokens, width), bf16)
    lows = [low, ((tokens, wide), bf16), low, ((tokens, 3 * width), bf16)]
    near = [
        ((tokens, wide), bf16),
        ((width, wide), bf16),
        ((wide, width), bf16),
        exact,
        exact,
        ((tokens, 3 * width), bf16),
        ((width, 3 * width), bf16),
        ((width, width), bf16),
    ]
    flops = 4 * tokens * (4 * width * width + 2 * width * wide)
    return pl.pallas_call(
        partial(backward_kernel, False, scale.shape[0]),
        out_shape=[jax.ShapeDtypeStruct(*item) for item in [low, exact, ((1, width), f32)]],
        in_specs=[vmem] * 4 + [anywhere] * 8,
        out_specs=[vmem] * 3,
        scratch_shapes=[pltpu.VMEM(*item) for item in lows + near + [exact, exact, low]]
        + [pltpu.SemaphoreType.DMA((8,))],
        compiler_params=pltpu.CompilerParams(vmem_limit_bytes=60 * 2**20),
        cost_estimate=pl.CostEstimate(flops=flops, bytes_accessed=2**25, transcendentals=0),
    )(scale, grad_final, block_out, gain, slope, w_up, w_down, x, middle, joined, w_qkv, w_out)


def backward_begin(returned, grad_top, seqs, slope, w_up, w_down):
    tokens, width = grad_top.shape
    wide = w_up.shape[-1]
    vmem = pl.BlockSpec(memory_space=pltpu.VMEM)
    anywhere = pl.BlockSpec(memory_space=pl.ANY)
    exact = ((tokens, width), f32)
    results = [exact, exact, ((tokens, width), bf16), ((tokens, wide), bf16), ((1, wide), f32)]
    near = [((tokens, wide), bf16), ((width, wide), bf16), ((wide, width), bf16)]
    return pl.pallas_call(
        partial(backward_kernel, True, seqs),
        out_shape=[jax.ShapeDtypeStruct(*item) for item in results],
        in_specs=[vmem] * 2 + [anywhere] * 3,
        out_specs=[vmem] * 5,
        scratch_shapes=[pltpu.VMEM(*item) for item in near] + [pltpu.SemaphoreType.DMA((3,))],
        compiler_params=pltpu.CompilerParams(vmem_limit_bytes=60 * 2**20),
        cost_estimate=pl.CostEstimate(
            flops=8 * tokens * width * wide, bytes_accessed=2**25, transcendentals=0
        ),
    )(returned, grad_top, slope, w_up, w_down)


def backward_rest(seqs, refs):
    scale, *far = refs[:10]
    out, grad_cond, grad_out_weight, grad_qkv_weight = refs[10:14]
    near = refs[14:23]
    total, grad_attn, grad_mixed, grad_joined, sems = refs[23:]
    grad_middle, grad_entry, middle, x, joined, mixed, entry_attn, w_out, w_qkv = near
    width = x.shape[1]
    copies = []
    for n, (source, target) in enumerate(zip(far, near)):
        source = source.at[0] if n >= 7 else source
        copies.append(pltpu.make_async_copy(source, target, sems.at[n]))
    for copy in copies:
        copy.start()
    steps = []

    def waits(*numbers):
        for n in numbers:
            copies[n].wait()

    def store_middle(rows, value):
        grad_middle[rows, :] = value
        grad_attn[rows, :] = value.astype(bf16)

    def store_out(rows, value):
        out[rows, :] = value.astype(bf16)

    def second_norm(seq):
        if seq == 0:
            waits(0, 1, 2)
        norm_grads(middle, grad_entry, grad_middle, scale, grad_cond, 1, seq, store_middle)

    def mixed_grads(index):
        if index == 0:
            waits(7)
        part = pl.ds(index * 512, 512)
        grad_mixed[:, part] = nt(grad_attn[...], w_out[part, :]).astype(bf16)

    def heads_grads(pair):
        if pair == 0:
            waits(4)
        attention_grads(joined, grad_mixed, grad_joined, pair, seqs)

    def entry_grads(index):
        if index == 0:
            waits(8)
        part = pl.ds(index * 256, 256)
        total[:, part] = nt(grad_joined[...], w_qkv[part, :])

    def first_norm(seq):
        if seq == 0:
            waits(3)
        norm_grads(x, total, grad_middle, scale, grad_cond, 0, seq, store_out)

    def out_weight(index):
        if index == 0:
            waits(5)
        part = pl.ds(index * 512, 512)
        grad_out_weight[part, :] = tn(mixed[:, part], grad_attn[...]).astype(bf16)

    def qkv_weight(index):
        if index == 0:
            waits(6)
        part = pl.ds(index * 256, 256)
        grad_qkv_weight[part, :] = tn(entry_attn[:, part], grad_joined[...]).astype(bf16)

    for step, number in (
        (second_norm, seqs),
        (mixed_grads, width // 512),
        (heads_grads, width // 128),
        (entry_grads, width // 256),
        (first_norm, seqs),
        (qkv_weight, width // 256),
        (out_weight, width // 512),
    ):
        steps += [partial(step, n) for n in range(number)]
    return steps


def rest_work(scale, grad_middle, grad_entry, kept, w_out, w_qkv):
    x, joined, mixed, middle, entry_attn = kept[:5]
    tokens, width = x.shape
    seqs = scale.shape[0]
    exact = ((tokens, width), f32)
    low = ((tokens, width), bf16)
    three = ((tokens, 3 * width), bf16)
    ins = [scale, grad_middle, grad_entry, middle, x, joined, mixed, entry_attn, w_out, w_qkv]
    results = [
        low,
        ((seqs, 1, 2 * width), f32),
        ((width, width), bf16),
        ((width, 3 * width), bf16),
    ]
    near = [exact, exact, exact, exact, three, low, low, results[2], results[3]]
    room = [pltpu.VMEM(*item) for item in near + [exact, low, low, three]]
    room.append(pltpu.SemaphoreType.DMA((9,)))
    return (
        partial(backward_rest, seqs),
        ins,
        [jax.ShapeDtypeStruct(*item) for item in results],
        room,
    )


def norm_rows(values):
    centred = values - jnp.mean(values, -1, keepdims=True)
    factor = lax.rsqrt(jnp.mean(centred * centred, -1, keepdims=True) + epsilon)
    return (centred * factor, factor)


def norm_back(gradient, normed, factor):
    return factor * (
        gradient
        - jnp.mean(gradient, -1, keepdims=True)
        - normed * jnp.mean(gradient * normed, -1, keepdims=True)
    )


def time_features(noise_level):
    half_width = TFEAT // 2
    rates = jnp.exp(jnp.arange(half_width, dtype=f32) * (math.log(1000.0) / half_width))
    angles = (jnp.log(noise_level) / 4.0)[:, None] * rates[None, :]
    return jnp.concatenate([jnp.cos(angles), jnp.sin(angles)], -1)


def levels_of(bins, table):
    hits = bins[:, None] == jnp.arange(table.shape[0])[None, :]
    return jnp.sum(jnp.where(hits, table[None, :], 0.0), -1)


def over_dp(part):
    part = part.reshape((part.shape[0] // 4, 2, 2) + part.shape[1:])
    part = lax.psum_scatter(part, "core", scatter_dimension=2)
    part = lax.psum_scatter(part, "pair", scatter_dimension=1)
    return lax.psum_scatter(part, "line", scatter_dimension=0)


def by_owner(part):
    line = lax.axis_size("line")
    return part.astype(bf16).reshape((line, 2, 2, part.shape[0] // (line * 4)) + part.shape[1:])


def mm(spec, left, right):
    return jnp.einsum(spec, left, right, preferred_element_type=f32)


def layer_forward(stream, scale_attn, scale_mlp, weights):
    w_qkv, w_out, w_up, b_hidden, w_down = weights
    seq_count, length, model_width = stream.shape
    normed_attn, factor_attn = norm_rows(stream)
    attn_entry = (normed_attn * scale_attn).astype(bf16)
    joined = mm("nsd,de->nse", attn_entry, w_qkv).astype(bf16)
    qkv_parts = joined.reshape(seq_count, length, 3, HEADS, HEAD_DIM)
    query_rows = qkv_parts[:, :, 0]
    key_rows = qkv_parts[:, :, 1]
    value_rows = qkv_parts[:, :, 2]
    scores = mm("nqhe,nkhe->nhqk", query_rows, key_rows) / math.sqrt(HEAD_DIM)
    exp_scores = jnp.exp(scores - jnp.max(scores, -1, keepdims=True))
    attn_probs = exp_scores / jnp.sum(exp_scores, -1, keepdims=True)
    probs_low = attn_probs.astype(bf16)
    attn_mixed = mm("nhqk,nkhe->nqhe", probs_low, value_rows).astype(bf16)
    attn_mixed = attn_mixed.reshape(seq_count, length, model_width)
    middle = stream + mm("nsd,de->nse", attn_mixed, w_out)
    normed_mlp, factor_mlp = norm_rows(middle)
    mlp_entry = (normed_mlp * scale_mlp).astype(bf16)
    up_proj = mm("nsd,df->nsf", mlp_entry, w_up) + b_hidden
    below = 0.5 + 0.5 * lax.erf(up_proj * math.sqrt(0.5))
    hidden = (up_proj * below).astype(bf16)
    density = jnp.exp(-0.5 * up_proj * up_proj) * (1.0 / math.sqrt(2.0 * math.pi))
    slope = (below + up_proj * density).astype(bf16)
    block_out = middle + mm("nsf,fd->nsd", hidden, w_down)
    kept = (
        normed_attn,
        factor_attn,
        attn_entry,
        query_rows,
        key_rows,
        value_rows,
        attn_probs,
        probs_low,
        attn_mixed,
        normed_mlp,
        factor_mlp,
        mlp_entry,
        slope,
        hidden,
    )
    return (block_out, kept)


def layer_backward(grad_out, kept, scale_attn, scale_mlp, weights, whole):
    w_qkv, w_out, w_up, b_hidden, w_down = weights
    (
        normed_attn,
        factor_attn,
        attn_entry,
        query_rows,
        key_rows,
        value_rows,
        attn_probs,
        probs_low,
        attn_mixed,
        normed_mlp,
        factor_mlp,
        mlp_entry,
        slope,
        hidden,
    ) = kept
    seq_count, length, model_width = grad_out.shape
    grads = {}
    grad_branch = grad_out.astype(bf16)
    if whole:
        grads["down"] = by_owner(mm("nsf,nsd->fd", hidden, grad_branch))
    grad_hidden = mm("nsd,fd->nsf", grad_branch, w_down)
    grad_up_proj = (grad_hidden * slope.astype(f32)).astype(bf16)
    if whole:
        grads["bias"] = jnp.sum(grad_up_proj.astype(f32), (0, 1))
        grads["up"] = by_owner(mm("nsd,nsf->df", mlp_entry, grad_up_proj))
    grad_entry = mm("nsf,df->nsd", grad_up_proj, w_up)
    grad_middle = grad_out + norm_back(grad_entry * scale_mlp, normed_mlp, factor_mlp)
    grad_attn = grad_middle.astype(bf16)
    if whole:
        grads["out"] = by_owner(mm("nsd,nse->de", attn_mixed, grad_attn))
    grad_mixed = mm("nse,de->nsd", grad_attn, w_out)
    grad_mixed = grad_mixed.astype(bf16).reshape(seq_count, length, HEADS, HEAD_DIM)
    grad_probs = mm("nqhe,nkhe->nhqk", grad_mixed, value_rows)
    grad_values = mm("nhqk,nqhe->nkhe", probs_low, grad_mixed)
    grad_scores = (
        attn_probs * (grad_probs - jnp.sum(grad_probs * attn_probs, -1, keepdims=True))
    ).astype(bf16)
    grad_query = mm("nhqk,nkhe->nqhe", grad_scores, key_rows) / math.sqrt(HEAD_DIM)
    grad_keys = mm("nhqk,nqhe->nkhe", grad_scores, query_rows) / math.sqrt(HEAD_DIM)
    grad_joined = jnp.stack([grad_query, grad_keys, grad_values], 2).astype(bf16)
    grad_joined = grad_joined.reshape(seq_count, length, 3 * model_width)
    if whole:
        grads["qkv"] = by_owner(mm("nsd,nse->de", attn_entry, grad_joined))
    grad_attn_entry = mm("nse,de->nsd", grad_joined, w_qkv)
    grad_stream = grad_middle + norm_back(grad_attn_entry * scale_attn, normed_attn, factor_attn)
    if whole:
        grads["cond"] = jnp.concatenate(
            [jnp.sum(grad_attn_entry * normed_attn, 1), jnp.sum(grad_entry * normed_mlp, 1)], -1
        )
    return (grad_stream, grads)


def local(
    token_ids,
    target_ids,
    time_bins,
    sigma_table,
    noise,
    embed,
    w_in,
    w_time,
    norm_gain,
    w_qkv,
    w_out,
    w_up,
    b_hidden,
    w_down,
    out_gain,
    head,
):
    section = lax.axis_index("section")
    line_at = lax.axis_index("line")
    pair_at = lax.axis_index("pair")
    core = lax.axis_index("core")
    sections = lax.axis_size("section")
    line = lax.axis_size("line")
    chip = line_at * 2 + pair_at
    chips = line * 2
    cores = 2
    dp_count = chips * cores
    dp_index = chip * cores + core
    is_first = section == 0
    seqs, length = token_ids.shape
    tokens = seqs * length
    half = tokens // sections
    model_width = w_out.shape[-1]
    emb_rows, emb_width = embed.shape
    straight = line <= 4 and half % 16 == 0 and model_width // dp_count % 16 == 0

    own_ids = jnp.concatenate([token_ids.reshape(-1), target_ids.reshape(-1), time_bins])
    if straight:
        padded = jnp.pad(own_ids, (0, -own_ids.shape[0] % 1024)).reshape(-1, 128)
        all_ids = gathered_small(padded, line, 0).reshape(dp_count, -1)[:, : own_ids.shape[0]]
    else:
        all_ids = lax.all_gather(own_ids, DP)
    all_tokens = all_ids[:, :tokens]
    all_targets = all_ids[:, tokens : 2 * tokens]
    all_bins = all_ids[:, 2 * tokens :].reshape(-1)

    own_rows = dp_index * emb_rows + jnp.arange(emb_rows)
    half_tokens = lax.dynamic_slice_in_dim(all_tokens, section * half, half, 1)
    picked = (half_tokens.reshape(-1)[:, None] == own_rows[None, :]).astype(bf16)
    found = jnp.dot(picked, embed, preferred_element_type=f32).astype(bf16)
    if straight:
        found = found.reshape(line, 2, 2, half, emb_width)
        embedded = rows_over_dp(found, 1)
    else:
        embedded = lax.all_gather(over_dp(found.reshape(dp_count, half, emb_width)), "section")
    embedded = embedded.astype(f32).reshape(seqs, length, emb_width)

    head_rows = head.shape[0]
    swapped = [(0, 1), (1, 0)]
    if straight:
        head_own = jnp.pad(head, ((0, -head_rows % 512), (0, 0)))
        head_section = lax.ppermute(head_own, "section", swapped)
    else:
        head_group = lax.all_gather(lax.all_gather(head, "core"), "section")
        head_group = head_group.reshape(-1, model_width)
        vocab_base = (
            (jnp.arange(sections)[:, None] * chips + chip) * cores + jnp.arange(cores)[None, :]
        ) * head_rows
        columns = (vocab_base[:, :, None] + jnp.arange(head_rows)[None, None, :]).reshape(-1)

    noise_level = levels_of(time_bins, sigma_table)
    unit_factor = lax.rsqrt(jnp.mean(embedded * embedded, -1, keepdims=True) + epsilon)
    level_col = noise_level[:, None, None]
    noise_scale = lax.rsqrt(level_col * level_col + 1.0)
    noisy_rows = ((embedded * unit_factor + level_col * noise) * noise_scale).astype(bf16)
    time_feats = time_features(noise_level)
    conditioned = jnp.dot(time_feats, w_time[0].astype(f32), precision=highest) + norm_gain[0]
    scale_attn = conditioned[:, None, :model_width]
    scale_mlp = conditioned[:, None, model_width:]
    scale = conditioned[:, None, :]
    weights = (w_qkv[0], w_out[0], w_up[0], b_hidden[0], w_down[0])
    stacked = (w_qkv, w_out, w_up, b_hidden, w_down)
    if straight:
        noisy_rows, head_own, head_section = lax.optimization_barrier(
            (noisy_rows, head_own, head_section)
        )
        heads = [head_own, lax.ppermute(head_own, "core", swapped)]
        heads += [head_section, lax.ppermute(head_section, "core", swapped)]

    stream0 = mm("nse,ed->nsd", noisy_rows, w_in)
    flat = (tokens, model_width)
    if straight:
        start = stream0.reshape(flat)
        (first_out,) = forward_pass(start, scale, stacked)
        arrived = lax.ppermute(first_out, "section", swapped)
        block_out, final_rows, *kept = forward_pass(
            start, scale, stacked, arrived, out_gain[None, :]
        )
    else:
        first_out = layer_forward(stream0, scale_attn, scale_mlp, weights)[0].astype(bf16)
        arrived = lax.ppermute(first_out, "section", swapped)
        stream = jnp.where(is_first, stream0, arrived.astype(f32))
        block_out, kept = layer_forward(stream, scale_attn, scale_mlp, weights)
        final_normed, final_factor = norm_rows(block_out.astype(bf16).astype(f32))
        final_rows = (final_normed * out_gain).astype(bf16).reshape(flat)

    targets_group = lax.dynamic_slice_in_dim(
        all_targets.reshape(chips, cores, tokens), core, 1, 1
    )[:, 0]
    targets_group = lax.dynamic_slice_in_dim(targets_group, section * half, half, 1)
    if straight:
        grad_final, grad_head, lse, picks = head_pass(
            final_rows, targets_group.reshape(line, 1, tokens), heads, line, head_rows, length, 3
        )
        ce_part = jnp.sum(lse) / chips - jnp.sum(picks)
    else:
        targets_group = targets_group.reshape(-1)
        handed = lax.ppermute(final_rows[:half], "section", [(1, 0), (0, 1)])
        own_final = jnp.where(is_first, handed, final_rows[half:])
        group_final = lax.all_gather(own_final, ("line", "pair"), tiled=True)
        logits = mm("td,vd->tv", group_final, head_group)
        local_top = jnp.max(logits, -1)
        local_total = jnp.sum(jnp.exp(logits - local_top[:, None]), -1)
        mark = columns[None, :] == targets_group[:, None]
        local_pick = jnp.sum(jnp.where(mark, logits, 0.0))
        stats = lax.all_gather(jnp.stack([local_top, local_total]), ("line", "pair"))
        all_top = jnp.max(stats[:, 0], 0)
        all_total = jnp.sum(stats[:, 1] * jnp.exp(stats[:, 0] - all_top), 0)
        log_total = all_top + jnp.log(all_total)
        soft_rows = jnp.exp(logits - log_total[:, None])
        logit_grads = ((soft_rows - jnp.where(mark, 1.0, 0.0)) / length).astype(bf16)
        grad_final = jnp.dot(logit_grads, head_group, preferred_element_type=f32).astype(bf16)
        grad_final = lax.psum_scatter(grad_final, ("line", "pair"), scatter_dimension=0, tiled=True)
        handed = lax.ppermute(grad_final, "section", swapped)
        grad_final = jnp.concatenate([handed, grad_final], 0)
        grad_head = mm("tv,td->vd", logit_grads, group_final).astype(bf16)
        grad_head = grad_head.reshape(sections, cores, head_rows, model_width)
        grad_head = lax.psum_scatter(grad_head, "core", scatter_dimension=1)
        grad_head = lax.psum_scatter(grad_head, "section", scatter_dimension=0).astype(f32)

        ce_part = jnp.sum(log_total) / chips - local_pick
    if straight:
        grad_second, grad_top, out_part = backward_pass(
            grad_final, block_out, out_gain[None, :], scale, kept, stacked
        )
        returned = lax.ppermute(grad_second, "section", swapped)
        out_part = out_part.reshape(-1)
        _, _, _, _, _, entry_mlp, slope, hidden = kept
        grad_middle, grad_entry, grad_branch, grad_up, grad_bias = backward_begin(
            returned, grad_top, seqs, slope, w_up, w_down
        )
        parts = [
            by_owner(mm("tf,td->fd", hidden, grad_branch)),
            by_owner(mm("td,tf->df", entry_mlp, grad_up)),
        ]
        grad_down, grad_up, grad_first, grad_cond, grad_wout, grad_qkv = summed_over_dp(
            parts, 4, work=rest_work(scale, grad_middle, grad_entry, kept, w_out, w_qkv)
        )
        grad_first = grad_first.reshape(stream0.shape)
        grads = {
            "qkv": by_owner(grad_qkv),
            "out": by_owner(grad_wout),
            "cond": grad_cond,
            "bias": grad_bias.reshape(-1),
        }
    else:
        grad_final = grad_final.astype(f32).reshape(stream0.shape)
        out_part = jnp.sum(grad_final * final_normed, (0, 1))
        grad_top = norm_back(grad_final * out_gain, final_normed, final_factor)
        grad_second = layer_backward(grad_top, kept, scale_attn, scale_mlp, weights, False)[0]
        returned = lax.ppermute(grad_second.astype(bf16), "section", swapped)
        grad_cot = jnp.where(is_first, returned.astype(f32), grad_top)
        grad_stream, grads = layer_backward(grad_cot, kept, scale_attn, scale_mlp, weights, True)
        grad_first = grad_stream.astype(bf16)
    out_part = jnp.where(is_first, 0.0, out_part)

    in_part = mm("nse,nsd->ed", noisy_rows, grad_first).astype(bf16)
    in_part = in_part.reshape(sections, line, 2, 2, -1, model_width)
    in_part = jnp.moveaxis(in_part, 0, 3).reshape(line, 2, 2, -1, model_width)
    grad_noisy = mm("nsd,ed->nse", grad_first, w_in)
    grad_unit = grad_noisy * noise_scale
    cubed = unit_factor * unit_factor * unit_factor
    grad_embedded = unit_factor * grad_unit - cubed * embedded * jnp.mean(
        grad_unit * embedded, -1, keepdims=True
    )
    grad_flat = grad_embedded.reshape(tokens, emb_width)

    ce_high = ce_part.astype(bf16).astype(f32)
    ce_mid = (ce_part - ce_high).astype(bf16).astype(f32)
    ce_low = ce_part - ce_high - ce_mid
    shared = jnp.concatenate([out_part, jnp.stack([ce_high, ce_mid, ce_low])])
    shared_rows = -(-shared.shape[0] // emb_width)
    shared = jnp.pad(shared, (0, shared_rows * emb_width - shared.shape[0]))
    handing = jnp.concatenate([grad_flat, shared.reshape(-1, emb_width)], 0).astype(bf16)
    handed = lax.ppermute(handing, "section", swapped)
    kept_rows = jnp.where(is_first, handing[:half], handed[half:tokens])
    layer_small = jnp.concatenate([grads["cond"].reshape(-1), grads["bias"]])
    layer_rows = layer_small.shape[0] // emb_width
    small = jnp.concatenate(
        [
            layer_small.astype(bf16).reshape(layer_rows, emb_width),
            handing[tokens:],
            handed[tokens:],
        ],
        0,
    )
    small = jnp.pad(small, ((0, -small.shape[0] % 16), (0, 0)))
    parts = [grads["qkv"], grads["out"], in_part]
    if straight:
        grad_qkv, grad_wout, grad_w_in, smalls, halves, grad_head = summed_over_dp(
            parts,
            2,
            packets=(small, kept_rows),
            head_part=grad_head,
            head_rows=head_rows,
            cross=True,
        )
    else:
        parts += [grads["down"], grads["up"]]
        sums = [over_dp(part.reshape((dp_count,) + part.shape[3:])).astype(f32) for part in parts]
        smalls = lax.all_gather(small, DP)
        halves = lax.all_gather(kept_rows, ("section",) + DP)
        grad_qkv, grad_wout, in_sum, grad_down, grad_up = sums
        in_sum = in_sum.reshape(sections, -1, model_width)
        in_handed = lax.ppermute(in_sum[1], "section", swapped)
        grad_w_in = jnp.where(is_first, in_sum[0], in_handed)

    grad_all = halves.reshape(-1, emb_width)
    tokens_all = all_tokens.reshape(dp_count, sections, half).swapaxes(0, 1).reshape(-1)
    out_rows = emb_rows // sections
    target_rows = (section * dp_count + dp_index) * out_rows + jnp.arange(out_rows)
    place = (target_rows[:, None] == tokens_all[None, :]).astype(bf16)
    grad_embed = jnp.dot(place, grad_all, preferred_element_type=f32)

    smalls = smalls.reshape(dp_count, -1, emb_width).astype(f32)
    layer_small = smalls[:, :layer_rows].reshape(dp_count, -1)
    cond_size = grads["cond"].size
    cond_all = layer_small[:, :cond_size].reshape(dp_count * seqs, 2 * model_width)
    hidden_rows = grads["bias"].shape[0] // dp_count
    grad_bias = jnp.sum(
        lax.dynamic_slice_in_dim(layer_small, cond_size + dp_index * hidden_rows, hidden_rows, 1), 0
    )
    norm_cols = 2 * model_width // dp_count
    grad_gain = jnp.sum(lax.dynamic_slice_in_dim(cond_all, dp_index * norm_cols, norm_cols, 1), 0)
    feats_all = time_features(levels_of(all_bins, sigma_table))
    feat_rows = TFEAT // dp_count
    feats_own = lax.dynamic_slice_in_dim(feats_all, dp_index * feat_rows, feat_rows, 1)
    grad_time = jnp.dot(feats_own.T, cond_all, precision=highest)
    both = smalls[:, layer_rows : layer_rows + 2 * shared_rows]
    both = jnp.sum(both.reshape(dp_count, 2, -1), (0, 1))
    loss = jnp.sum(both[model_width : model_width + 3]) / (tokens * dp_count)
    gain_rows = model_width // dp_count
    grad_out_gain = lax.dynamic_slice_in_dim(both, dp_index * gain_rows, gain_rows)
    return (
        loss,
        grad_embed,
        grad_w_in,
        grad_time[None],
        grad_gain[None],
        grad_qkv[None],
        grad_wout[None],
        grad_up[None],
        grad_bias[None],
        grad_down[None],
        grad_out_gain,
        grad_head,
    )


def solution(mesh):
    sections, dp_count = mesh.shape["section"], mesh.shape["dp"]
    fine = Mesh(mesh.devices.reshape(sections, dp_count // 4, 2, 2), ("section",) + DP)
    everywhere = ("section",) + DP
    in_specs = (
        P(DP, None),
        P(DP, None),
        P(DP),
        P(),
        P(DP, None, None),
        P(DP, None),
        P(),
        P("section", None, None),
        P("section", None),
        P("section", None, None),
        P("section", None, None),
        P("section", None, None),
        P("section", None),
        P("section", None, None),
        P(),
        P(everywhere, None),
    )
    out_specs = (
        P(),
        P(everywhere, None),
        P(everywhere, None),
        P("section", DP, None),
        P("section", DP),
        P("section", DP, None),
        P("section", DP, None),
        P("section", DP, None),
        P("section", DP),
        P("section", DP, None),
        P(DP),
        P(everywhere, None),
    )
    return jax.shard_map(local, mesh=fine, in_specs=in_specs, out_specs=out_specs, check_vma=False)
```

```python
from functools import partial
import math

import jax
import jax.numpy as jnp
from jax import lax
from jax.experimental import pallas as pl
from jax.experimental.pallas import tpu as pltpu
from jax.sharding import Mesh, PartitionSpec as P

HEADS = 16
HEAD_DIM = 64
TFEAT = 256

epsilon = 1e-05
highest = lax.Precision.HIGHEST
f32 = jnp.float32
bf16 = jnp.bfloat16
DP = ("line", "pair", "core")


MESH = pl.DeviceIdType.MESH


def nt(left, right):
    return lax.dot_general(left, right, (((1,), (1,)), ((), ())), preferred_element_type=f32)


def tn(left, right):
    return lax.dot_general(left, right, (((0,), (0,)), ((), ())), preferred_element_type=f32)


def nn(left, right):
    return jnp.dot(left, right, preferred_element_type=f32)


def greet(peers):
    barrier = pltpu.get_barrier_semaphore()
    for peer in peers:
        pl.semaphore_signal(barrier, inc=1, device_id=peer, device_id_type=MESH)
    pl.semaphore_wait(barrier, len(peers))


def remote(source, target, send, recv, peer):
    return pltpu.make_async_remote_copy(
        src_ref=source,
        dst_ref=target,
        send_sem=send,
        recv_sem=recv,
        device_id=peer,
        device_id_type=MESH,
    )


def ring_place(position, line):
    turned = position // line
    return position * (1 - turned) + (2 * line - 1 - position) * turned, turned


def rows_kernel(line, found, out, own, from_core, from_pair, from_line, *sems):
    load_sem, core_send, core_recv, pair_send, pair_recv, line_send, line_recv, swap_send, swap_recv = (
        sems
    )
    me_section = lax.axis_index("section")
    me_line = lax.axis_index("line")
    me_pair = lax.axis_index("pair")
    me_core = lax.axis_index("core")
    section_peer = {"section": 1 - me_section}
    core_peer = {"core": 1 - me_core}
    pair_peer = {"pair": 1 - me_pair}
    line_at = [lax.rem(me_line + step, line) for step in range(1, line)]
    greet([section_peer, core_peer, pair_peer] + [{"line": place} for place in line_at])
    rows, width = out.shape[-2:]
    wide = width // 2
    sides = (1 - me_pair, me_pair)
    loads, core_copies, pair_copies, line_copies = {}, {}, {}, {}
    for turn, side in enumerate(sides):
        for piece in range(2):
            cols = pl.ds(piece * wide, wide)
            loads[piece, turn] = pltpu.make_async_copy(
                found.at[:, side, me_core, :, cols],
                own.at[:, side, :, cols],
                load_sem.at[piece, turn],
            )
            core_copies[piece, turn] = remote(
                found.at[:, side, 1 - me_core, :, cols],
                from_core.at[:, side, :, cols],
                core_send.at[piece, turn],
                core_recv.at[piece, turn],
                core_peer,
            )
            loads[piece, turn].start()
            core_copies[piece, turn].start()

    def tiles(body):
        @pl.loop(0, rows // 16)
        def _(block):
            body(pl.ds(pl.multiple_of(block * 16, 16), 16))

    for piece in range(2):
        cols = pl.ds(piece * wide, wide)
        side = sides[0]
        loads[piece, 0].wait()
        core_copies[piece, 0].wait_recv()

        def add(row):
            for place in range(line):
                total = from_core[place, side, row, cols] + own[place, side, row, cols]
                from_core[place, side, row, cols] = total

        tiles(add)
        pair_copies[piece] = remote(
            from_core.at[:, side, :, cols],
            from_pair.at[:, :, cols],
            pair_send.at[piece],
            pair_recv.at[piece],
            pair_peer,
        )
        pair_copies[piece].start()
    for piece in range(2):
        cols = pl.ds(piece * wide, wide)
        loads[piece, 1].wait()
        core_copies[piece, 1].wait_recv()
        pair_copies[piece].wait_recv()

        def add(row):
            for place in range(line):
                total = from_core[place, me_pair, row, cols] + own[place, me_pair, row, cols]
                from_core[place, me_pair, row, cols] = total + from_pair[place, row, cols]

        tiles(add)
        for n in range(line - 1):
            line_copies[piece, n] = remote(
                from_core.at[line_at[n], me_pair, :, cols],
                from_line.at[n, :, cols],
                line_send.at[piece, n],
                line_recv.at[piece, n],
                {"line": line_at[n]},
            )
            line_copies[piece, n].start()
    for piece in range(2):
        cols = pl.ds(piece * wide, wide)
        for n in range(line - 1):
            line_copies[piece, n].wait_recv()

        def add(row):
            total = from_core[me_line, me_pair, row, cols]
            for n in range(line - 1):
                total = total + from_line[n, row, cols]
            out[me_section, row, cols] = total

        tiles(add)
    swap = remote(out.at[me_section], out.at[me_section], swap_send, swap_recv, section_peer)
    swap.start()
    for copy in list(core_copies.values()) + list(pair_copies.values()) + list(line_copies.values()):
        copy.wait_send()
    swap.wait()


def rows_over_dp(found, collective_id):
    line = found.shape[0]
    shape = found.shape[-2:]
    dma = pltpu.SemaphoreType.DMA
    return pl.pallas_call(
        partial(rows_kernel, line),
        out_shape=jax.ShapeDtypeStruct((2,) + shape, bf16),
        in_specs=[pl.BlockSpec(memory_space=pl.ANY)],
        out_specs=pl.BlockSpec(memory_space=pltpu.VMEM),
        scratch_shapes=[
            pltpu.VMEM((line, 2) + shape, bf16),
            pltpu.VMEM((line, 2) + shape, bf16),
            pltpu.VMEM((line,) + shape, bf16),
            pltpu.VMEM((line - 1,) + shape, bf16),
        ]
        + [dma((2, 2))] * 3
        + [dma((2,))] * 2
        + [dma((2, line - 1))] * 2
        + [dma, dma],
        compiler_params=pltpu.CompilerParams(
            collective_id=collective_id, has_side_effects=True, vmem_limit_bytes=32 * 2**20
        ),
        cost_estimate=pl.CostEstimate(flops=0, bytes_accessed=2**26, transcendentals=0),
    )(found)


def gather_kernel(line, mine, out, send, recv, own_sem):
    me_line = lax.axis_index("line")
    me_pair = lax.axis_index("pair")
    me_core = lax.axis_index("core")
    peers = []
    for step in range(1, line * 4):
        peers.append(
            {
                "line": lax.rem(me_line + step // 4, line),
                "pair": lax.rem(me_pair + step // 2 % 2, 2),
                "core": lax.rem(me_core + step % 2, 2),
            }
        )
    greet(peers)
    place = out.at[me_line, me_pair, me_core]
    keep = pltpu.make_async_copy(mine, place, own_sem)
    keep.start()
    copies = [remote(mine, place, send.at[n], recv.at[n], peer) for n, peer in enumerate(peers)]
    for copy in copies:
        copy.start()
    keep.wait()
    for copy in copies:
        copy.wait()


def gathered_small(block, line, collective_id):
    count = line * 4 - 1
    vmem = pl.BlockSpec(memory_space=pltpu.VMEM)
    return pl.pallas_call(
        partial(gather_kernel, line),
        out_shape=jax.ShapeDtypeStruct((line, 2, 2) + block.shape, block.dtype),
        in_specs=[vmem],
        out_specs=vmem,
        scratch_shapes=[
            pltpu.SemaphoreType.DMA((count,)),
            pltpu.SemaphoreType.DMA((count,)),
            pltpu.SemaphoreType.DMA,
        ],
        compiler_params=pltpu.CompilerParams(collective_id=collective_id, has_side_effects=True),
        cost_estimate=pl.CostEstimate(flops=0, bytes_accessed=2**25, transcendentals=0),
    )(block)


def head_kernel(line, head_rows, length, *refs):
    final, targets, *heads = refs[:6]
    out, grads, lse_out, pick_out = refs[6:10]
    (table, rows_all, logits, probs, acc, parts, from_pair, from_line, stats, done) = refs[10:20]
    (head_sem, own_sem, give_send, give_recv, along_send, along_recv, pair_send, pair_recv) = refs[20:28]
    (stat_send, stat_recv, sum_send, sum_recv, line_send, line_recv, back_send, back_recv) = refs[28:]
    half = final.shape[0] // 2
    width = 2 * half
    padded = heads[0].shape[0]
    me_section = lax.axis_index("section")
    me_line = lax.axis_index("line")
    me_pair = lax.axis_index("pair")
    me_core = lax.axis_index("core")
    section_peer = {"section": 1 - me_section}
    pair_peer = {"pair": 1 - me_pair}
    chip_peers = []
    for step in range(1, 2 * line):
        chip_peers.append(
            {"line": lax.rem(me_line + step // 2, line), "pair": lax.rem(me_pair + step % 2, 2)}
        )
    greet(chip_peers + [section_peer])

    def side(pair):
        return pl.ds(pl.multiple_of(pair * half, 16), half)

    loads = [
        pltpu.make_async_copy(part, table.at[pl.ds(n * padded, padded)], head_sem.at[n])
        for n, part in enumerate(heads)
    ]
    for load in loads:
        load.start()

    def token_rows(place, pair):
        return pl.ds(pl.multiple_of(place * width + pair * half, 16), half)

    def group(place):
        return pl.ds(pl.multiple_of(place * width, 128), width)

    mine = rows_all.at[token_rows(me_line, me_pair)]
    give = remote(final.at[pl.ds(0, half)], mine, give_send, give_recv, section_peer)

    @pl.when(me_section == 1)
    def _():
        give.start()
        keep = pltpu.make_async_copy(final.at[pl.ds(half, half)], mine, own_sem)
        keep.start()
        keep.wait()

    @pl.when(me_section == 0)
    def _():
        give.wait_recv()

    def column_block(place):
        return rows_all.at[token_rows(place, me_pair)]

    def along(step, way):
        block = column_block(me_line - way * step)
        turn = (way + 1) // 2
        return remote(
            block,
            block,
            along_send.at[turn, step],
            along_recv.at[turn, step],
            {"line": me_line + way},
        )

    def inside(place):
        return (place >= 0) & (place < line)

    def sends_along(step, way):
        return inside(me_line - way * step) & inside(me_line + way)

    def sideways(place):
        block = column_block(place)
        return remote(block, block, pair_send.at[place], pair_recv.at[place], pair_peer)

    def arrived_sideways(place):
        block = rows_all.at[token_rows(place, 1 - me_pair)]
        return remote(block, block, pair_send.at[place], pair_recv.at[place], pair_peer)

    for way in (1, -1):

        @pl.when(sends_along(0, way))
        def _():
            along(0, way).start()

    sideways(me_line).start()

    def pass_on(step):
        for way in (1, -1):
            place = me_line - way * step

            @pl.when(inside(place))
            def _():
                block = column_block(place)
                turn = (way + 1) // 2
                remote(
                    block,
                    block,
                    along_send.at[turn, step - 1],
                    along_recv.at[turn, step - 1],
                    {"line": me_line - way},
                ).wait_recv()

                @pl.when(inside(me_line + way))
                def _():
                    along(step, way).start()

                sideways(place).start()

    nearest = []
    for own in range(line):
        near = [own]
        for step in range(1, line):
            near += [place for place in (own - step, own + step) if 0 <= place < line]
        nearest.append(near)

    def by_distance(turn):
        place = 0
        for own in range(line):
            for n in range(line):
                hit = ((me_line == own) & (turn == n)).astype(jnp.int32)
                place = place + hit * nearest[own][n]
        return place

    def vocabulary(tile, rows):
        shard = tile * rows // padded
        first = lax.rem(tile * rows, padded)
        shard_section = lax.rem(me_section + shard // 2, 2)
        shard_core = lax.rem(me_core + lax.rem(shard, 2), 2)
        base = (((shard_section * line + me_line) * 2 + me_pair) * 2 + shard_core) * head_rows
        row = lax.broadcasted_iota(jnp.int32, (rows, 1), 0) + first
        return jnp.where(row < head_rows, row + base, -1)

    tile_rows = 512
    tiles = 4 * padded // tile_rows
    lowest = -1e30

    def score(turn, tops):
        place = by_distance(turn) if turn < line else None
        before = by_distance(turn - 1) if turn > 0 else None
        wanted = None if place is None else targets[place]

        def one(tile, carry):
            rows = pl.ds(pl.multiple_of(tile * tile_rows, tile_rows), tile_rows)
            out = []
            if place is not None:
                top, pick = carry[:2]
                entry = vocabulary(tile, tile_rows)
                part = nt(table[rows, :], rows_all[group(place), :])
                part = jnp.where(entry >= 0, part, lowest)
                logits[turn % 2, rows, :] = part
                out.append(jnp.maximum(top, jnp.max(part, 0, keepdims=True)))
                out.append(
                    pick + jnp.sum(jnp.where(entry == wanted, part, 0.0), 0, keepdims=True)
                )
            if before is not None:
                value = jnp.exp(logits[(turn - 1) % 2, rows, :] - tops)
                probs[rows, group(before)] = value.astype(bf16)
                out.append(carry[-1] + jnp.sum(value, 0, keepdims=True))
            return tuple(out)

        none = jnp.zeros((1, width), f32)
        start = () if place is None else (jnp.full((1, width), lowest, f32), none)
        start += () if before is None else (none,)
        result = lax.fori_loop(0, tiles, one, start)
        if place is not None:
            pick_out[place] = result[1]
        if before is not None:
            own = stats.at[me_line, me_pair, before]
            own[0:1, :] = tops
            own[1:2, :] = result[-1]
            for n in range(len(chip_peers)):
                stat_copy(n, before).start()
        return None if place is None else result[0]

    def stat_copy(n, place):
        own = stats.at[me_line, me_pair, place]
        return remote(own, own, stat_send.at[n, place], stat_recv.at[n, place], chip_peers[n])

    def stat_wait(n, place):
        peer = chip_peers[n]
        source_line = lax.rem(2 * me_line + line - peer["line"], line)
        source_pair = peer["pair"]
        block = stats.at[source_line, source_pair, place]
        remote(block, block, stat_send.at[n, place], stat_recv.at[n, place], peer).wait_recv()

    for load in loads:
        load.wait()

    tops = None
    for turn in range(line + 1):
        if turn + 1 < line:
            pass_on(turn + 1)
        if turn < line:
            arrived_sideways(by_distance(turn)).wait_recv()
        tops = score(turn, tops)

    def sum_copy(turn):
        place = lax.rem(me_line + turn + 1, line)
        return remote(
            parts.at[place, side(1 - me_pair)],
            from_pair.at[turn],
            sum_send.at[turn],
            sum_recv.at[turn],
            pair_peer,
        )

    def line_copy(turn):
        place = lax.rem(me_line + turn + 1, line)
        return remote(
            parts.at[place, side(me_pair)],
            from_line.at[turn],
            line_send.at[turn],
            line_recv.at[turn],
            {"line": place},
        )

    def finish(turn):
        place = lax.rem(me_line + turn + 1, line)
        sum_copy(turn).wait_recv()
        own = parts.at[place, side(me_pair)]

        @pl.loop(0, half // 16)
        def _(block):
            rows = pl.ds(pl.multiple_of(block * 16, 16), 16)
            value = own[rows, :].astype(f32) + from_pair[turn, rows, :].astype(f32)
            own[rows, :] = value.astype(bf16)

    @pl.loop(0, line)
    def _(turn):
        place = lax.rem(me_line + turn + 1, line)
        for n in range(len(chip_peers)):
            stat_wait(n, place)
        tops = [stats[a, b, place, 0:1, :] for a in range(line) for b in range(2)]
        totals = [stats[a, b, place, 1:2, :] for a in range(line) for b in range(2)]
        top = tops[0]
        for value in tops[1:]:
            top = jnp.maximum(top, value)
        total = jnp.zeros_like(top)
        for peak, part in zip(tops, totals):
            total = total + part * jnp.exp(peak - top)
        lse = top + jnp.log(total)
        lse_out[place] = lse
        factor = jnp.exp(stats[me_line, me_pair, place, 0:1, :] - lse) / length
        wanted = targets[place]

        def scaled(tile):
            rows = pl.ds(tile * padded, padded)
            entry = vocabulary(tile, padded)
            grad = probs[rows, group(place)].astype(f32) * factor
            grad = (grad - jnp.where(entry == wanted, 1.0 / length, 0.0)).astype(bf16)
            probs[rows, group(place)] = grad
            return grad

        grad = scaled(0)
        for tile in range(4):
            product = tn(grad, table[pl.ds(tile * padded, padded), :])
            if tile < 3:
                grad = scaled(tile + 1)
                acc[...] = product if tile == 0 else acc[...] + product
            else:
                parts[place] = (acc[...] + product).astype(bf16)

        sum_copy(turn).start()

        @pl.when(turn > 0)
        def _():
            finish(turn - 1)
            line_copy(turn - 1).start()

    gh_rows = 256
    gh_tiles = 4 * padded // gh_rows

    def head_grads(first, last):
        @pl.loop(first, last)
        def _(tile):
            rows = pl.ds(pl.multiple_of(tile * gh_rows, gh_rows), gh_rows)
            value = jnp.dot(probs[rows, :], rows_all[...], preferred_element_type=f32)
            grads[rows, :] = value.astype(bf16)

    head_grads(0, gh_tiles // 2)
    finish(line - 1)
    for turn in range(line - 1):
        line_copy(turn).wait_recv()
    own = parts.at[me_line, side(me_pair)]

    @pl.loop(0, half // 16)
    def _(block):
        rows = pl.ds(pl.multiple_of(block * 16, 16), 16)
        value = own[rows, :].astype(f32)
        for turn in range(line - 1):
            value = value + from_line[turn, rows, :].astype(f32)
        done[rows, :] = value.astype(bf16)

    back = remote(done, out.at[pl.ds(0, half)], back_send, back_recv, section_peer)

    @pl.when(me_section == 0)
    def _():
        back.start()
        out[...] = jnp.zeros_like(out)

    @pl.when(me_section == 1)
    def _():
        out[pl.ds(half, half), :] = done[...]

    head_grads(gh_tiles // 2, gh_tiles)

    @pl.when(me_section == 0)
    def _():
        back.wait_send()

    @pl.when(me_section == 1)
    def _():
        back.wait_recv()
        give.wait_send()

    for way in (1, -1):
        for step in range(line - 1):

            @pl.when(sends_along(step, way))
            def _():
                along(step, way).wait_send()

    for place in range(line):
        sideways(place).wait_send()
        for n in range(len(chip_peers)):
            stat_copy(n, place).wait_send()
    for turn in range(line):
        sum_copy(turn).wait_send()
    for turn in range(line - 1):
        line_copy(turn).wait_send()


def head_pass(final, targets, heads, line, head_rows, length, collective_id):
    tokens, deep = final.shape
    half = tokens // 2
    padded = heads[0].shape[0]
    vmem = pl.BlockSpec(memory_space=pltpu.VMEM)
    anywhere = pl.BlockSpec(memory_space=pl.ANY)
    dma = pltpu.SemaphoreType.DMA
    peers = 2 * line - 1
    return pl.pallas_call(
        partial(head_kernel, line, head_rows, length),
        out_shape=[
            jax.ShapeDtypeStruct((tokens, deep), bf16),
            jax.ShapeDtypeStruct((4 * padded, deep), bf16),
            jax.ShapeDtypeStruct((line, 1, tokens), f32),
            jax.ShapeDtypeStruct((line, 1, tokens), f32),
        ],
        in_specs=[vmem, vmem] + [anywhere] * 4,
        out_specs=[vmem] * 4,
        scratch_shapes=[
            pltpu.VMEM((4 * padded, deep), bf16),
            pltpu.VMEM((line * tokens, deep), bf16),
            pltpu.VMEM((2, 4 * padded, tokens), f32),
            pltpu.VMEM((4 * padded, line * tokens), bf16),
            pltpu.VMEM((tokens, deep), f32),
            pltpu.VMEM((line, tokens, deep), bf16),
            pltpu.VMEM((line, half, deep), bf16),
            pltpu.VMEM((line - 1, half, deep), bf16),
            pltpu.VMEM((line, 2, line, 8, tokens), f32),
            pltpu.VMEM((half, deep), bf16),
            dma((4,)),
            dma,
            dma,
            dma,
            dma((2, line)),
            dma((2, line)),
            dma((line,)),
            dma((line,)),
            dma((peers, line)),
            dma((peers, line)),
            dma((line,)),
            dma((line,)),
            dma((line,)),
            dma((line,)),
            dma,
            dma,
        ],
        compiler_params=pltpu.CompilerParams(
            collective_id=collective_id, has_side_effects=True, vmem_limit_bytes=60 * 2**20
        ),
        cost_estimate=pl.CostEstimate(
            flops=24 * line * padded * tokens * deep, bytes_accessed=2**28, transcendentals=0
        ),
    )(final, targets, *heads)


def row_stats(values):
    centred = values - jnp.mean(values, -1, keepdims=True)
    factor = lax.rsqrt(jnp.mean(centred * centred, -1, keepdims=True) + epsilon)
    return centred * factor, factor


def two_heads(block):
    first = lax.broadcasted_iota(jnp.int32, block.shape, 1) < HEAD_DIM
    zero = jnp.zeros_like(block)
    return jnp.concatenate([jnp.where(first, block, zero), jnp.where(first, zero, block)], 0)


def one_block(stacked):
    rows = stacked.shape[0] // 2
    first = lax.broadcasted_iota(jnp.int32, (rows, stacked.shape[1]), 1) < HEAD_DIM
    return jnp.where(first, stacked[:rows], stacked[rows:])


def attention_weights(queries, keys):
    scores = nt(keys, queries) * (1.0 / math.sqrt(HEAD_DIM))
    exped = jnp.exp(scores - jnp.max(scores, 0, keepdims=True))
    return exped * (1.0 / jnp.sum(exped, 0, keepdims=True))


def tile_of(index, size):
    return pl.ds(pl.multiple_of(index * size, size), size)


def forward_kernel(full, seqs, *refs):
    refs = list(refs)

    def take(number):
        return [refs.pop(0) for _ in range(number)]

    start, scale, bias = take(3)
    arrived, gain = take(2) if full else (None, None)
    weights = take(4)
    if full:
        out, final, x, joined, mixed, middle, entry_attn, entry_mlp, slope, hidden = take(10)
    else:
        (out,) = take(1)
        x = start
        joined, mixed, middle, entry_attn = take(4)
        entry_mlp = entry_attn
    w_qkv, w_out, w_up, w_down, total, sems = refs
    width = start.shape[1]
    length = start.shape[0] // seqs
    load_qkv, load_out, load_up, load_down = [
        pltpu.make_async_copy(source.at[0], target, sems.at[n])
        for n, (source, target) in enumerate(zip(weights, (w_qkv, w_out, w_up, w_down)))
    ]
    load_qkv.start()

    for seq in range(seqs):
        rows = pl.ds(seq * length, length)
        if full:
            first = (lax.axis_index("section") == 0).astype(f32)
            x[rows, :] = start[rows, :] * first + arrived[rows, :].astype(f32) * (1.0 - first)
        normed, _ = row_stats(x[rows, :])
        entry_attn[rows, :] = (normed * scale[seq, :, :width]).astype(bf16)

    load_qkv.wait()
    load_out.start()
    load_up.start()
    tile = 512

    @pl.loop(0, 3 * width // tile)
    def _(index):
        cols = tile_of(index, tile)
        joined[:, cols] = nn(entry_attn[...], w_qkv[:, cols]).astype(bf16)

    load_out.wait()
    load_down.start()
    pairs = width // 128

    @pl.loop(0, pairs)
    def _(pair):
        cols = tile_of(pair, 128)
        for seq in range(seqs):
            rows = pl.ds(seq * length, length)
            queries = two_heads(joined[rows, cols])
            keys = joined[rows, tile_of(pair + pairs, 128)]
            values = joined[rows, tile_of(pair + 2 * pairs, 128)]
            probs = attention_weights(queries, keys).astype(bf16)
            mixed[rows, cols] = one_block(tn(probs, values)).astype(bf16)

    @pl.loop(0, width // tile)
    def _(index):
        cols = tile_of(index, tile)
        middle[:, cols] = x[:, cols] + nn(mixed[...], w_out[:, cols])

    for seq in range(seqs):
        rows = pl.ds(seq * length, length)
        normed, _ = row_stats(middle[rows, :])
        entry_mlp[rows, :] = (normed * scale[seq, :, width:]).astype(bf16)

    load_up.wait()
    load_down.wait()
    total[...] = middle[...]

    def gelu_of(up, cols):
        below = 0.5 + 0.5 * lax.erf(up * math.sqrt(0.5))
        value = (up * below).astype(bf16)
        if full:
            density = jnp.exp(-0.5 * up * up) * (1.0 / math.sqrt(2.0 * math.pi))
            slope[:, cols] = (below + up * density).astype(bf16)
            hidden[:, cols] = value
        return value

    @pl.loop(0, w_up.shape[1] // (2 * tile))
    def _(index):
        sides = [tile_of(2 * index + side, tile) for side in range(2)]
        ups = [nn(entry_mlp[...], w_up[:, cols]) + bias[:, cols] for cols in sides]
        both = jnp.concatenate([gelu_of(up, cols) for up, cols in zip(ups, sides)], 1)
        total[...] += nn(both, w_down[tile_of(index, 2 * tile), :])

    for seq in range(seqs):
        rows = pl.ds(seq * length, length)
        value = total[rows, :].astype(bf16)
        out[rows, :] = value
        if full:
            normed, _ = row_stats(value.astype(f32))
            final[rows, :] = (normed * gain[...]).astype(bf16)


def layer_scratch(width, hidden):
    return [
        pltpu.VMEM((width, 3 * width), bf16),
        pltpu.VMEM((width, width), bf16),
        pltpu.VMEM((width, hidden), bf16),
        pltpu.VMEM((hidden, width), bf16),
    ]


def forward_pass(start, scale, weights, arrived=None, gain=None):
    w_qkv, w_out, w_up, b_hidden, w_down = weights
    tokens, width = start.shape
    wide = w_up.shape[-1]
    full = arrived is not None
    vmem = pl.BlockSpec(memory_space=pltpu.VMEM)
    anywhere = pl.BlockSpec(memory_space=pl.ANY)

    def low(columns):
        return (tokens, columns), bf16

    exact = ((tokens, width), f32)
    out_shape = [jax.ShapeDtypeStruct((tokens, width), bf16)]
    scratch = layer_scratch(width, wide)
    scratch += [pltpu.VMEM(*exact), pltpu.SemaphoreType.DMA((4,))]
    operands = [start, scale, b_hidden]
    if full:
        operands += [arrived, gain]
        kept = [low(width), exact, low(3 * width), low(width), exact, low(width), low(width)]
        out_shape += [jax.ShapeDtypeStruct(*item) for item in kept + [low(wide), low(wide)]]
    else:
        inside = [low(3 * width), low(width), exact, low(width)]
        scratch = [pltpu.VMEM(*item) for item in inside] + scratch
    flops = 2 * tokens * (4 * width * width + 2 * width * wide)
    return pl.pallas_call(
        partial(forward_kernel, full, scale.shape[0]),
        out_shape=out_shape,
        in_specs=[vmem] * len(operands) + [anywhere] * 4,
        out_specs=[vmem] * len(out_shape),
        scratch_shapes=scratch,
        compiler_params=pltpu.CompilerParams(vmem_limit_bytes=60 * 2**20),
        cost_estimate=pl.CostEstimate(flops=2 * flops, bytes_accessed=2**25, transcendentals=0),
    )(*operands, w_qkv, w_out, w_up, w_down)


def norm_grads(source, total, grad_middle, scale, grad_cond, half, seq, store):
    width = total.shape[1]
    length = total.shape[0] // scale.shape[0]
    rows = pl.ds(seq * length, length)
    cols = pl.ds(half * width, width)
    normed, factor = row_stats(source[rows, :])
    gradient = total[rows, :]
    if grad_cond is not None:
        grad_cond[seq, :, cols] = jnp.sum(gradient * normed, 0, keepdims=True)
    scaled = gradient * scale[seq, :, cols]
    back = factor * (
        scaled
        - jnp.mean(scaled, -1, keepdims=True)
        - normed * jnp.mean(scaled * normed, -1, keepdims=True)
    )
    store(rows, grad_middle[rows, :] + back)


def attention_grads(joined, grad_mixed, grad_joined, pair, seqs):
    pairs = grad_mixed.shape[1] // 128
    length = grad_mixed.shape[0] // seqs
    shrink = 1.0 / math.sqrt(HEAD_DIM)
    cols = tile_of(pair, 128)
    key_cols = tile_of(pair + pairs, 128)
    value_cols = tile_of(pair + 2 * pairs, 128)
    for seq in range(seqs):
        rows = pl.ds(seq * length, length)
        queries = two_heads(joined[rows, cols])
        keys = joined[rows, key_cols]
        probs = attention_weights(queries, keys)
        grads = two_heads(grad_mixed[rows, cols])
        grad_probs = nt(joined[rows, value_cols], grads)
        inner = jnp.sum(grad_probs * probs, 0, keepdims=True)
        grad_scores = (probs * (grad_probs - inner)).astype(bf16)
        grad_joined[rows, cols] = (one_block(tn(grad_scores, keys)) * shrink).astype(bf16)
        grad_joined[rows, key_cols] = (nn(grad_scores, queries) * shrink).astype(bf16)
        grad_joined[rows, value_cols] = nn(probs.astype(bf16), grads).astype(bf16)


def backward_kernel(begin, seqs, *refs):
    refs = list(refs)

    def take(number):
        return [refs.pop(0) for _ in range(number)]

    if begin:
        incoming, other = take(2)
        far = take(3)
        grad_middle, total, grad_low, grad_up, grad_bias = take(5)
        near = take(3)
    else:
        scale, incoming, other, gain = take(4)
        far = take(8)
        out, grad_top, grad_gain = take(3)
        grad_low, grad_up, grad_attn, grad_joined = take(4)
        near = take(8)
        total, grad_middle, grad_mixed = take(3)
    (sems,) = refs
    if begin:
        slope, w_up, w_down = near
        load_slope = pltpu.make_async_copy(far[0], slope, sems.at[0])
        load_up = pltpu.make_async_copy(far[1].at[0], w_up, sems.at[1])
        load_down = pltpu.make_async_copy(far[2].at[0], w_down, sems.at[2])
    else:
        slope, w_up, w_down, x, middle, joined, w_qkv, w_out = near
        load_slope = pltpu.make_async_copy(far[0], slope, sems.at[0])
        load_up = pltpu.make_async_copy(far[1].at[0], w_up, sems.at[1])
        load_down = pltpu.make_async_copy(far[2].at[0], w_down, sems.at[2])
        load_x = pltpu.make_async_copy(far[3], x, sems.at[3])
        load_middle = pltpu.make_async_copy(far[4], middle, sems.at[4])
        load_joined = pltpu.make_async_copy(far[5], joined, sems.at[5])
        load_qkv = pltpu.make_async_copy(far[6].at[0], w_qkv, sems.at[6])
        load_out = pltpu.make_async_copy(far[7].at[0], w_out, sems.at[7])
    width = incoming.shape[1]
    length = incoming.shape[0] // seqs
    load_down.start()
    load_slope.start()

    for seq in range(seqs):
        rows = pl.ds(seq * length, length)
        if begin:
            first = (lax.axis_index("section") == 0).astype(f32)
            value = incoming[rows, :].astype(f32) * first + other[rows, :] * (1.0 - first)
        else:
            normed, factor = row_stats(other[rows, :].astype(f32))
            gradient = incoming[rows, :].astype(f32)
            part = jnp.sum(gradient * normed, 0, keepdims=True)
            grad_gain[...] = part if seq == 0 else grad_gain[...] + part
            scaled = gradient * gain[...]
            value = factor * (
                scaled
                - jnp.mean(scaled, -1, keepdims=True)
                - normed * jnp.mean(scaled * normed, -1, keepdims=True)
            )
            grad_top[rows, :] = value
        grad_middle[rows, :] = value
        grad_low[rows, :] = value.astype(bf16)

    load_down.wait()
    load_slope.wait()
    load_up.start()
    if not begin:
        load_middle.start()
        load_out.start()
        load_joined.start()
    tile = 1024

    @pl.loop(0, w_up.shape[1] // tile)
    def _(index):
        cols = tile_of(index, tile)
        grad_hidden = nt(grad_low[...], w_down[cols, :])
        value = (grad_hidden * slope[:, cols].astype(f32)).astype(bf16)
        grad_up[:, cols] = value
        if begin:
            grad_bias[:, cols] = jnp.sum(value.astype(f32), 0, keepdims=True)

    load_up.wait()
    if not begin:
        load_middle.wait()
        load_out.wait()
        load_joined.wait()
        load_qkv.start()
        load_x.start()

    @pl.loop(0, width // 256)
    def _(index):
        total[:, tile_of(index, 256)] = nt(grad_up[...], w_up[tile_of(index, 256), :])

    if begin:
        return

    def store_middle(rows, value):
        grad_middle[rows, :] = value
        grad_attn[rows, :] = value.astype(bf16)

    for seq in range(seqs):
        norm_grads(middle, total, grad_middle, scale, None, 1, seq, store_middle)

    @pl.loop(0, width // 512)
    def _(index):
        part = tile_of(index, 512)
        grad_mixed[:, part] = nt(grad_attn[...], w_out[part, :]).astype(bf16)

    @pl.loop(0, width // 128)
    def _(pair):
        attention_grads(joined, grad_mixed, grad_joined, pair, seqs)

    load_qkv.wait()
    load_x.wait()

    @pl.loop(0, width // 256)
    def _(index):
        total[:, tile_of(index, 256)] = nt(grad_joined[...], w_qkv[tile_of(index, 256), :])

    def store_out(rows, value):
        out[rows, :] = value.astype(bf16)

    for seq in range(seqs):
        norm_grads(x, total, grad_middle, scale, None, 0, seq, store_out)


def backward_pass(grad_final, block_out, gain, scale, kept, weights):
    w_qkv, w_out, w_up, _, w_down = weights
    x, joined, _, middle, _, _, slope, _ = kept
    tokens, width = x.shape
    wide = w_up.shape[-1]
    vmem = pl.BlockSpec(memory_space=pltpu.VMEM)
    anywhere = pl.BlockSpec(memory_space=pl.ANY)
    exact = ((tokens, width), f32)
    low = ((tokens, width), bf16)
    lows = [low, ((tokens, wide), bf16), low, ((tokens, 3 * width), bf16)]
    near = [
        ((tokens, wide), bf16),
        ((width, wide), bf16),
        ((wide, width), bf16),
        exact,
        exact,
        ((tokens, 3 * width), bf16),
        ((width, 3 * width), bf16),
        ((width, width), bf16),
    ]
    flops = 4 * tokens * (4 * width * width + 2 * width * wide)
    return pl.pallas_call(
        partial(backward_kernel, False, scale.shape[0]),
        out_shape=[jax.ShapeDtypeStruct(*item) for item in [low, exact, ((1, width), f32)]],
        in_specs=[vmem] * 4 + [anywhere] * 8,
        out_specs=[vmem] * 3,
        scratch_shapes=[pltpu.VMEM(*item) for item in lows + near + [exact, exact, low]]
        + [pltpu.SemaphoreType.DMA((8,))],
        compiler_params=pltpu.CompilerParams(vmem_limit_bytes=60 * 2**20),
        cost_estimate=pl.CostEstimate(flops=flops, bytes_accessed=2**25, transcendentals=0),
    )(scale, grad_final, block_out, gain, slope, w_up, w_down, x, middle, joined, w_qkv, w_out)


def backward_begin(returned, grad_top, seqs, slope, w_up, w_down):
    tokens, width = grad_top.shape
    wide = w_up.shape[-1]
    vmem = pl.BlockSpec(memory_space=pltpu.VMEM)
    anywhere = pl.BlockSpec(memory_space=pl.ANY)
    exact = ((tokens, width), f32)
    results = [exact, exact, ((tokens, width), bf16), ((tokens, wide), bf16), ((1, wide), f32)]
    near = [((tokens, wide), bf16), ((width, wide), bf16), ((wide, width), bf16)]
    return pl.pallas_call(
        partial(backward_kernel, True, seqs),
        out_shape=[jax.ShapeDtypeStruct(*item) for item in results],
        in_specs=[vmem] * 2 + [anywhere] * 3,
        out_specs=[vmem] * 5,
        scratch_shapes=[pltpu.VMEM(*item) for item in near] + [pltpu.SemaphoreType.DMA((3,))],
        compiler_params=pltpu.CompilerParams(vmem_limit_bytes=60 * 2**20),
        cost_estimate=pl.CostEstimate(
            flops=8 * tokens * width * wide, bytes_accessed=2**25, transcendentals=0
        ),
    )(returned, grad_top, slope, w_up, w_down)


def tail_kernel(line, seqs, lag, *refs):
    refs = list(refs)

    def take(number):
        return [refs.pop(0) for _ in range(number)]

    scale, rest, factor_one, factor_two, embedded, noisy, w_in = take(7)
    far = take(9)
    parts = take(2)
    (head_part,) = take(1)
    outs = take(5)
    head_out, smalls, rows_all = take(3)
    near = take(9)
    grad_attn, grad_mixed, grad_joined, grad_first, grad_cond, in_weight = take(6)
    rows_own, small_wide, small_own = take(3)
    own, from_core, slots = take(2), take(5), take(5)
    head_own, head_core, head_section, last_total = take(4)
    far_sem, load_sem, core_send, core_recv, ring_send, ring_recv, credit = take(7)
    keep_sem, packet_send, packet_recv, wide_send, wide_recv, rows_send, rows_recv = take(7)
    head_sem, head_send, head_recv, cross_send, cross_recv = take(5)
    grad_middle, grad_entry, middle, x, joined, mixed, entry_attn, w_out, w_qkv = near
    inside = [w_qkv, w_out, in_weight]
    groups = ((0, 1), (2, 3, 4))
    chips = 2 * line
    width = x.shape[1]
    me_section = lax.axis_index("section")
    me_line = lax.axis_index("line")
    me_pair = lax.axis_index("pair")
    me_core = lax.axis_index("core")
    position = me_line + me_pair * (chips - 1 - 2 * me_line)
    section_peer = {"section": 1 - me_section}
    core_peer = {"core": 1 - me_core}
    ways = (1, -1)
    ring_peers = []
    for way in ways:
        peer_line, peer_pair = ring_place(lax.rem(position + way + chips, chips), line)
        ring_peers.append({"line": peer_line, "pair": peer_pair})
    greet([core_peer, section_peer] + ring_peers)

    shapes = [ref.shape[-2:] for ref in from_core]

    def block_of(turn, step):
        ahead = lax.rem(position - ways[turn] * (1 + step) + 2 * chips, chips)
        return ring_place(ahead, line)

    def columns(index, turn):
        wide = shapes[index][-1] // 2
        return pl.ds(turn * wide, wide)

    def block_rows(index, place, pair, core):
        high = shapes[index][0]
        return pl.ds(pl.multiple_of(((place * 2 + pair) * 2 + core) * high, 16), high)

    def source(index, turn, step, core):
        place, pair = block_of(turn, step)
        cols = columns(index, turn)
        if index < 2:
            return parts[index].at[place, pair, core, :, cols]
        return inside[index - 2].at[block_rows(index, place, pair, core), cols]

    def load(index, turn, step):
        return pltpu.make_async_copy(
            source(index, turn, step, me_core),
            own[index].at[step % 2, :, columns(index, turn)],
            load_sem.at[index, turn, step],
        )

    def core_copy(index, turn, step):
        return remote(
            source(index, turn, step, 1 - me_core),
            from_core[index].at[step % 3, :, columns(index, turn)],
            core_send.at[index, turn, step],
            core_recv.at[index, turn, step],
            core_peer,
        )

    def ring_copy(index, turn, step):
        cols = columns(index, turn)
        passed = from_core[index].at[0, :, cols] if step == 0 else slots[index].at[step - 1, :, cols]
        return remote(
            passed,
            slots[index].at[step, :, cols],
            ring_send.at[index, turn, step],
            ring_recv.at[index, turn, step],
            ring_peers[turn],
        )

    def to_core(group, step):
        if step >= 3:
            pl.semaphore_wait(credit.at[group], 1)
        for index in groups[group]:
            for turn in range(2):
                if index < 2:
                    load(index, turn, step).start()
                core_copy(index, turn, step).start()

    def stop(group, step, between):
        first, last = step == 0, step == chips - 1
        for index in groups[group]:
            rows, wide = shapes[index][0], shapes[index][1] // 2
            tile = min(wide, 512)
            for turn in range(2):
                if index < 2:
                    load(index, turn, step).wait()
                core_copy(index, turn, step).wait_recv()
                if not first:
                    ring_copy(index, turn, step - 1).wait_recv()
                place, pair = block_of(turn, step)

                @pl.loop(0, rows // 16)
                def _(block):
                    row = pl.ds(pl.multiple_of(block * 16, 16), 16)
                    if index >= 2:
                        base = ((place * 2 + pair) * 2 + me_core) * rows + block * 16
                        own_row = pl.ds(pl.multiple_of(base, 16), 16)
                    for col in range(turn * wide, (turn + 1) * wide, tile):
                        cols = pl.ds(col, tile)
                        if index < 2:
                            mine = own[index][step % 2, row, cols]
                        else:
                            mine = inside[index - 2][own_row, cols]
                        total = from_core[index][step % 3, row, cols].astype(f32)
                        total = total + mine.astype(f32)
                        if not first:
                            total = total + slots[index][step - 1, row, cols].astype(f32)
                        if last and index == 4:
                            last_total[row, cols] = total
                        elif last:
                            outs[index][row, cols] = total.astype(bf16)
                        elif first:
                            from_core[index][0, row, cols] = total.astype(bf16)
                        else:
                            slots[index][step - 1, row, cols] = total.astype(bf16)

                if not last:
                    ring_copy(index, turn, step).start()
                between()
        if step == 1:
            for index in groups[group]:
                for turn in range(2):
                    ring_copy(index, turn, 0).wait_send()
        if 1 <= step <= 4:
            amount = 2 if step == 1 else 1
            pl.semaphore_signal(
                credit.at[group], inc=amount, device_id=core_peer, device_id_type=MESH
            )

    hops = (line, line - 1)

    def packet_blocks(place, pair):
        return [smalls.at[place, pair, me_core], rows_all.at[place, pair, me_core]]

    def packet_hops(turn, hop, away):
        place, pair = ring_place(
            lax.rem(position - ways[turn] * (hop + away) + 2 * chips, chips), line
        )
        return [
            remote(
                block,
                block,
                packet_send.at[n, turn, hop],
                packet_recv.at[n, turn, hop],
                ring_peers[turn],
            )
            for n, block in enumerate(packet_blocks(place, pair))
        ]

    def pass_packets(hop):
        for turn in range(2):
            if 0 < hop <= hops[turn]:
                for copy in packet_hops(turn, hop - 1, 1):
                    copy.wait_recv()
            if hop < hops[turn]:
                for copy in packet_hops(turn, hop, 0):
                    copy.start()

    small_slot, rows_slot = packet_blocks(me_line, me_pair)
    keep_small = pltpu.make_async_copy(small_own, small_slot, keep_sem.at[0])
    keep_rows = pltpu.make_async_copy(rows_own, rows_slot, keep_sem.at[1])
    rows_over = remote(rows_own, rows_slot, rows_send, rows_recv, section_peer)
    across = [
        remote(block, block, wide_send.at[n], wide_recv.at[n], core_peer)
        for n, block in enumerate([smalls.at[:, :, me_core], rows_all.at[:, :, me_core]])
    ]

    high = head_part.shape[0] // 4

    def shard(n):
        return head_part.at[pl.ds(n * high, high)]

    head_loads = [
        pltpu.make_async_copy(shard(2 * n), head_own.at[n], head_sem.at[n]) for n in range(2)
    ]
    head_copies = [
        remote(shard(2 * n + 1), head_core.at[n], head_send.at[n], head_recv.at[n], core_peer)
        for n in range(2)
    ]
    head_copies.append(
        remote(head_core.at[1], head_section, head_send.at[2], head_recv.at[2], section_peer)
    )

    def head_over_cores():
        for copy in head_loads:
            copy.wait()
        for copy in head_copies[:2]:
            copy.wait_recv()

        @pl.loop(0, high // 16)
        def _(block):
            rows = pl.ds(pl.multiple_of(block * 16, 16), 16)
            value = head_core[1, rows, :].astype(f32) + head_own[1, rows, :].astype(f32)
            head_core[1, rows, :] = value.astype(bf16)

        head_copies[2].start()

    def head_over_sections():
        head_copies[2].wait_recv()

        @pl.loop(0, high // 16)
        def _(block):
            rows = pl.ds(pl.multiple_of(block * 16, 16), 16)
            value = head_core[0, rows, :].astype(f32) + head_own[0, rows, :].astype(f32)
            value = value + head_section[rows, :].astype(f32)
            head_out[rows, :] = value.astype(bf16)

    far_copies = []
    for n, (where, target) in enumerate(zip(far, near)):
        where = where.at[0] if n >= 7 else where
        far_copies.append(pltpu.make_async_copy(where, target, far_sem.at[n]))

    def waits(*numbers):
        for n in numbers:
            far_copies[n].wait()

    def store_middle(rows, value):
        grad_middle[rows, :] = value
        grad_attn[rows, :] = value.astype(bf16)

    def store_first(rows, value):
        grad_first[rows, :] = value.astype(bf16)

    def second_norm(seq):
        if seq == 0:
            waits(0, 1, 2)
        norm_grads(middle, grad_entry, grad_middle, scale, grad_cond, 1, seq, store_middle)

    def mixed_grads(index):
        if index == 0:
            waits(7)
        part = pl.ds(index * 512, 512)
        grad_mixed[:, part] = nt(grad_attn[...], w_out[part, :]).astype(bf16)

    def heads_grads(pair):
        if pair == 0:
            waits(4)
        attention_grads(joined, grad_mixed, grad_joined, pair, seqs)

    def entry_grads(index):
        if index == 0:
            waits(8)
        part = pl.ds(index * 256, 256)
        grad_entry[:, part] = nt(grad_joined[...], w_qkv[part, :])

    def first_norm(seq):
        if seq == 0:
            waits(3)
        norm_grads(x, grad_entry, grad_middle, scale, grad_cond, 0, seq, store_first)

    def embedding_rows(_):
        grad_noisy = nt(grad_first[...], w_in[...])
        inner = jnp.mean(grad_noisy * embedded[...], -1, keepdims=True)
        value = factor_one[...] * grad_noisy - factor_two[...] * embedded[...] * inner
        rows_own[...] = value.astype(bf16)

        @pl.when(me_section == 0)
        def _():
            keep_rows.start()
            rows_over.start()

    def small_rows(_):
        each = small_wide.shape[1]
        for seq in range(seqs):
            for n in range(2 * width // each):
                row = pl.ds(seq * (2 * width // each) + n, 1)
                small_wide[row, :] = grad_cond[seq, :, pl.ds(n * each, each)]
        small_wide[pl.ds(seqs * 2 * width // each, rest.shape[0]), :] = rest[...]
        small_own[...] = small_wide[...].astype(bf16)
        keep_small.start()

    def input_weight(_):
        in_weight[...] = tn(noisy[...], grad_first[...]).astype(bf16)

    def qkv_weight(index):
        if index == 0:
            waits(6)
        part = pl.ds(index * 256, 256)
        w_qkv[part, :] = tn(entry_attn[:, part], grad_joined[...]).astype(bf16)

    def out_weight(index):
        if index == 0:
            waits(5)
        part = pl.ds(index * 512, 512)
        w_out[part, :] = tn(mixed[:, part], grad_attn[...]).astype(bf16)

    steps = []
    for step, number in (
        (second_norm, seqs),
        (mixed_grads, width // 512),
        (heads_grads, width // 128),
        (entry_grads, width // 256),
        (first_norm, seqs),
        (embedding_rows, 1),
        (small_rows, 1),
        (input_weight, 1),
        (qkv_weight, width // 256),
        (out_weight, width // 512),
    ):
        steps += [partial(step, n) for n in range(number)]
    at_once = -(-len(steps) // (4 * lag))

    def work():
        for _ in range(at_once):
            if steps:
                steps.pop(0)()

    def nothing():
        pass

    to_core(0, 0)
    to_core(0, 1)
    for copy in far_copies:
        copy.start()
    stop(0, 0, work)
    for turn in range(1, chips + lag):
        if turn + 1 < chips:
            to_core(0, turn + 1)
        if turn == 1:
            for copy in head_loads + head_copies[:2]:
                copy.start()
        if turn == lag:
            to_core(1, 0)
        if lag <= turn and turn - lag + 1 < chips:
            to_core(1, turn - lag + 1)
        if turn < chips:
            stop(0, turn, work if turn < lag else nothing)
        if turn >= lag:
            stop(1, turn - lag, nothing)
        hop = turn - lag
        if hop == 0:
            keep_small.wait()

            @pl.when(me_section == 0)
            def _():
                keep_rows.wait()

            @pl.when(me_section == 1)
            def _():
                rows_over.wait_recv()

        if 0 <= hop <= line:
            pass_packets(hop)
        if hop == line:
            for copy in across:
                copy.start()
        if hop == 1:
            head_over_cores()
        if turn == chips + lag - 2:
            head_over_sections()
    each = outs[4].shape[0]
    give = remote(last_total.at[pl.ds(each, each)], outs[4], cross_send, cross_recv, section_peer)

    @pl.when(me_section == 0)
    def _():
        give.start()
        outs[4][...] = last_total[pl.ds(0, each), :]

    for copy in across:
        copy.wait()
    for copy in head_copies:
        copy.wait_send()
    for turn in range(2):
        for hop in range(hops[turn]):
            for copy in packet_hops(turn, hop, 0):
                copy.wait_send()
    for index in range(5):
        for turn in range(2):
            for step in range(chips):
                core_copy(index, turn, step).wait_send()
                if 0 < step < chips - 1:
                    ring_copy(index, turn, step).wait_send()

    @pl.when(me_section == 0)
    def _():
        rows_over.wait_send()
        give.wait_send()

    @pl.when(me_section == 1)
    def _():
        give.wait_recv()


def tail_pass(scale, rest, factors, embedded, noisy, w_in, far, parts, head_part, collective_id):
    grad_middle = far[0]
    tokens, width = grad_middle.shape
    seqs = scale.shape[0]
    line = parts[0].shape[0]
    chips = 2 * line
    count = 4 * line
    emb_width = noisy.shape[1]
    vmem = pl.BlockSpec(memory_space=pltpu.VMEM)
    anywhere = pl.BlockSpec(memory_space=pl.ANY)
    dma = pltpu.SemaphoreType.DMA
    shapes = [part.shape[-2:] for part in parts]
    shapes += [
        (width // count, 3 * width),
        (width // count, width),
        (emb_width // count, width),
    ]
    each = shapes[4][0] // 2
    high = head_part.shape[0] // 4
    small = (seqs * 2 * width // emb_width + rest.shape[0], emb_width)
    exact = ((tokens, width), f32)
    low = ((tokens, width), bf16)
    three = ((tokens, 3 * width), bf16)
    rows = (tokens, emb_width)
    results = [(shape, bf16) for shape in shapes[:4]]
    results += [((each, width), f32), ((high, width), bf16)]
    results += [((line, 2, 2) + small, bf16), ((line, 2, 2) + rows, bf16)]
    room = [exact, exact, exact, exact, three, low, low]
    room += [((width, width), bf16), ((width, 3 * width), bf16)]
    room += [low, low, three, low, ((seqs, 1, 2 * width), f32), ((emb_width, width), bf16)]
    room += [(rows, bf16), (small, f32), (small, bf16)]
    room += [((2,) + shape, bf16) for shape in shapes[:2]]
    room += [((3,) + shape, bf16) for shape in shapes]
    room += [((chips - 1,) + shape, bf16) for shape in shapes]
    room += [((2, high, width), bf16), ((2, high, width), bf16), ((high, width), bf16)]
    room += [(shapes[4], f32)]
    scratch = [pltpu.VMEM(*item) for item in room]
    scratch += [dma((9,)), dma((2, 2, chips)), dma((5, 2, chips)), dma((5, 2, chips))]
    scratch += [dma((5, 2, chips - 1)), dma((5, 2, chips - 1)), pltpu.SemaphoreType.REGULAR((2,))]
    scratch += [dma((2,)), dma((2, 2, line)), dma((2, 2, line)), dma((2,)), dma((2,)), dma, dma]
    scratch += [dma((2,)), dma((3,)), dma((3,)), dma, dma]
    return pl.pallas_call(
        partial(tail_kernel, line, seqs, 3),
        out_shape=[jax.ShapeDtypeStruct(*item) for item in results],
        in_specs=[vmem] * 7 + [anywhere] * 12,
        out_specs=[vmem] * 6 + [anywhere] * 2,
        scratch_shapes=scratch,
        compiler_params=pltpu.CompilerParams(
            collective_id=collective_id, has_side_effects=True, vmem_limit_bytes=62 * 2**20
        ),
        cost_estimate=pl.CostEstimate(flops=0, bytes_accessed=2**29, transcendentals=0),
    )(scale, rest, *factors, embedded, noisy, w_in, *far, *parts, head_part)


def norm_rows(values):
    centred = values - jnp.mean(values, -1, keepdims=True)
    factor = lax.rsqrt(jnp.mean(centred * centred, -1, keepdims=True) + epsilon)
    return (centred * factor, factor)


def norm_back(gradient, normed, factor):
    return factor * (
        gradient
        - jnp.mean(gradient, -1, keepdims=True)
        - normed * jnp.mean(gradient * normed, -1, keepdims=True)
    )


def time_features(noise_level):
    half_width = TFEAT // 2
    rates = jnp.exp(jnp.arange(half_width, dtype=f32) * (math.log(1000.0) / half_width))
    angles = (jnp.log(noise_level) / 4.0)[:, None] * rates[None, :]
    return jnp.concatenate([jnp.cos(angles), jnp.sin(angles)], -1)


def levels_of(bins, table):
    hits = bins[:, None] == jnp.arange(table.shape[0])[None, :]
    return jnp.sum(jnp.where(hits, table[None, :], 0.0), -1)


def over_dp(part):
    part = part.reshape((part.shape[0] // 4, 2, 2) + part.shape[1:])
    part = lax.psum_scatter(part, "core", scatter_dimension=2)
    part = lax.psum_scatter(part, "pair", scatter_dimension=1)
    return lax.psum_scatter(part, "line", scatter_dimension=0)


def by_owner(part):
    line = lax.axis_size("line")
    return part.astype(bf16).reshape((line, 2, 2, part.shape[0] // (line * 4)) + part.shape[1:])


def mm(spec, left, right):
    return jnp.einsum(spec, left, right, preferred_element_type=f32)


def layer_forward(stream, scale_attn, scale_mlp, weights):
    w_qkv, w_out, w_up, b_hidden, w_down = weights
    seq_count, length, model_width = stream.shape
    normed_attn, factor_attn = norm_rows(stream)
    attn_entry = (normed_attn * scale_attn).astype(bf16)
    joined = mm("nsd,de->nse", attn_entry, w_qkv).astype(bf16)
    qkv_parts = joined.reshape(seq_count, length, 3, HEADS, HEAD_DIM)
    query_rows = qkv_parts[:, :, 0]
    key_rows = qkv_parts[:, :, 1]
    value_rows = qkv_parts[:, :, 2]
    scores = mm("nqhe,nkhe->nhqk", query_rows, key_rows) / math.sqrt(HEAD_DIM)
    exp_scores = jnp.exp(scores - jnp.max(scores, -1, keepdims=True))
    attn_probs = exp_scores / jnp.sum(exp_scores, -1, keepdims=True)
    probs_low = attn_probs.astype(bf16)
    attn_mixed = mm("nhqk,nkhe->nqhe", probs_low, value_rows).astype(bf16)
    attn_mixed = attn_mixed.reshape(seq_count, length, model_width)
    middle = stream + mm("nsd,de->nse", attn_mixed, w_out)
    normed_mlp, factor_mlp = norm_rows(middle)
    mlp_entry = (normed_mlp * scale_mlp).astype(bf16)
    up_proj = mm("nsd,df->nsf", mlp_entry, w_up) + b_hidden
    below = 0.5 + 0.5 * lax.erf(up_proj * math.sqrt(0.5))
    hidden = (up_proj * below).astype(bf16)
    density = jnp.exp(-0.5 * up_proj * up_proj) * (1.0 / math.sqrt(2.0 * math.pi))
    slope = (below + up_proj * density).astype(bf16)
    block_out = middle + mm("nsf,fd->nsd", hidden, w_down)
    kept = (
        normed_attn,
        factor_attn,
        attn_entry,
        query_rows,
        key_rows,
        value_rows,
        attn_probs,
        probs_low,
        attn_mixed,
        normed_mlp,
        factor_mlp,
        mlp_entry,
        slope,
        hidden,
    )
    return (block_out, kept)


def layer_backward(grad_out, kept, scale_attn, scale_mlp, weights, whole):
    w_qkv, w_out, w_up, b_hidden, w_down = weights
    (
        normed_attn,
        factor_attn,
        attn_entry,
        query_rows,
        key_rows,
        value_rows,
        attn_probs,
        probs_low,
        attn_mixed,
        normed_mlp,
        factor_mlp,
        mlp_entry,
        slope,
        hidden,
    ) = kept
    seq_count, length, model_width = grad_out.shape
    grads = {}
    grad_branch = grad_out.astype(bf16)
    if whole:
        grads["down"] = by_owner(mm("nsf,nsd->fd", hidden, grad_branch))
    grad_hidden = mm("nsd,fd->nsf", grad_branch, w_down)
    grad_up_proj = (grad_hidden * slope.astype(f32)).astype(bf16)
    if whole:
        grads["bias"] = jnp.sum(grad_up_proj.astype(f32), (0, 1))
        grads["up"] = by_owner(mm("nsd,nsf->df", mlp_entry, grad_up_proj))
    grad_entry = mm("nsf,df->nsd", grad_up_proj, w_up)
    grad_middle = grad_out + norm_back(grad_entry * scale_mlp, normed_mlp, factor_mlp)
    grad_attn = grad_middle.astype(bf16)
    if whole:
        grads["out"] = by_owner(mm("nsd,nse->de", attn_mixed, grad_attn))
    grad_mixed = mm("nse,de->nsd", grad_attn, w_out)
    grad_mixed = grad_mixed.astype(bf16).reshape(seq_count, length, HEADS, HEAD_DIM)
    grad_probs = mm("nqhe,nkhe->nhqk", grad_mixed, value_rows)
    grad_values = mm("nhqk,nqhe->nkhe", probs_low, grad_mixed)
    grad_scores = (
        attn_probs * (grad_probs - jnp.sum(grad_probs * attn_probs, -1, keepdims=True))
    ).astype(bf16)
    grad_query = mm("nhqk,nkhe->nqhe", grad_scores, key_rows) / math.sqrt(HEAD_DIM)
    grad_keys = mm("nhqk,nqhe->nkhe", grad_scores, query_rows) / math.sqrt(HEAD_DIM)
    grad_joined = jnp.stack([grad_query, grad_keys, grad_values], 2).astype(bf16)
    grad_joined = grad_joined.reshape(seq_count, length, 3 * model_width)
    if whole:
        grads["qkv"] = by_owner(mm("nsd,nse->de", attn_entry, grad_joined))
    grad_attn_entry = mm("nse,de->nsd", grad_joined, w_qkv)
    grad_stream = grad_middle + norm_back(grad_attn_entry * scale_attn, normed_attn, factor_attn)
    if whole:
        grads["cond"] = jnp.concatenate(
            [jnp.sum(grad_attn_entry * normed_attn, 1), jnp.sum(grad_entry * normed_mlp, 1)], -1
        )
    return (grad_stream, grads)


def local(
    token_ids,
    target_ids,
    time_bins,
    sigma_table,
    noise,
    embed,
    w_in,
    w_time,
    norm_gain,
    w_qkv,
    w_out,
    w_up,
    b_hidden,
    w_down,
    out_gain,
    head,
):
    section = lax.axis_index("section")
    line_at = lax.axis_index("line")
    pair_at = lax.axis_index("pair")
    core = lax.axis_index("core")
    sections = lax.axis_size("section")
    line = lax.axis_size("line")
    chip = line_at * 2 + pair_at
    chips = line * 2
    cores = 2
    dp_count = chips * cores
    dp_index = chip * cores + core
    is_first = section == 0
    seqs, length = token_ids.shape
    tokens = seqs * length
    half = tokens // sections
    model_width = w_out.shape[-1]
    emb_rows, emb_width = embed.shape
    straight = line <= 4 and half % 16 == 0 and model_width // dp_count % 16 == 0

    own_ids = jnp.concatenate([token_ids.reshape(-1), target_ids.reshape(-1), time_bins])
    if straight:
        padded = jnp.pad(own_ids, (0, -own_ids.shape[0] % 1024)).reshape(-1, 128)
        all_ids = gathered_small(padded, line, 0).reshape(dp_count, -1)[:, : own_ids.shape[0]]
    else:
        all_ids = lax.all_gather(own_ids, DP)
    all_tokens = all_ids[:, :tokens]
    all_targets = all_ids[:, tokens : 2 * tokens]
    all_bins = all_ids[:, 2 * tokens :].reshape(-1)

    own_rows = dp_index * emb_rows + jnp.arange(emb_rows)
    half_tokens = lax.dynamic_slice_in_dim(all_tokens, section * half, half, 1)
    picked = (half_tokens.reshape(-1)[:, None] == own_rows[None, :]).astype(bf16)
    found = jnp.dot(picked, embed, preferred_element_type=f32).astype(bf16)
    if straight:
        found = found.reshape(line, 2, 2, half, emb_width)
        embedded = rows_over_dp(found, 1)
    else:
        embedded = lax.all_gather(over_dp(found.reshape(dp_count, half, emb_width)), "section")
    embedded = embedded.astype(f32).reshape(seqs, length, emb_width)

    head_rows = head.shape[0]
    swapped = [(0, 1), (1, 0)]
    if straight:
        head_own = jnp.pad(head, ((0, -head_rows % 512), (0, 0)))
        head_section = lax.ppermute(head_own, "section", swapped)
    else:
        head_group = lax.all_gather(lax.all_gather(head, "core"), "section")
        head_group = head_group.reshape(-1, model_width)
        vocab_base = (
            (jnp.arange(sections)[:, None] * chips + chip) * cores + jnp.arange(cores)[None, :]
        ) * head_rows
        columns = (vocab_base[:, :, None] + jnp.arange(head_rows)[None, None, :]).reshape(-1)

    noise_level = levels_of(time_bins, sigma_table)
    unit_factor = lax.rsqrt(jnp.mean(embedded * embedded, -1, keepdims=True) + epsilon)
    level_col = noise_level[:, None, None]
    noise_scale = lax.rsqrt(level_col * level_col + 1.0)
    noisy_rows = ((embedded * unit_factor + level_col * noise) * noise_scale).astype(bf16)
    time_feats = time_features(noise_level)
    conditioned = jnp.dot(time_feats, w_time[0].astype(f32), precision=highest) + norm_gain[0]
    scale_attn = conditioned[:, None, :model_width]
    scale_mlp = conditioned[:, None, model_width:]
    scale = conditioned[:, None, :]
    weights = (w_qkv[0], w_out[0], w_up[0], b_hidden[0], w_down[0])
    stacked = (w_qkv, w_out, w_up, b_hidden, w_down)
    if straight:
        noisy_rows, head_own, head_section = lax.optimization_barrier(
            (noisy_rows, head_own, head_section)
        )
        heads = [head_own, lax.ppermute(head_own, "core", swapped)]
        heads += [head_section, lax.ppermute(head_section, "core", swapped)]

    stream0 = mm("nse,ed->nsd", noisy_rows, w_in)
    flat = (tokens, model_width)
    if straight:
        start = stream0.reshape(flat)
        (first_out,) = forward_pass(start, scale, stacked)
        arrived = lax.ppermute(first_out, "section", swapped)
        block_out, final_rows, *kept = forward_pass(
            start, scale, stacked, arrived, out_gain[None, :]
        )
    else:
        first_out = layer_forward(stream0, scale_attn, scale_mlp, weights)[0].astype(bf16)
        arrived = lax.ppermute(first_out, "section", swapped)
        stream = jnp.where(is_first, stream0, arrived.astype(f32))
        block_out, kept = layer_forward(stream, scale_attn, scale_mlp, weights)
        final_normed, final_factor = norm_rows(block_out.astype(bf16).astype(f32))
        final_rows = (final_normed * out_gain).astype(bf16).reshape(flat)

    targets_group = lax.dynamic_slice_in_dim(
        all_targets.reshape(chips, cores, tokens), core, 1, 1
    )[:, 0]
    targets_group = lax.dynamic_slice_in_dim(targets_group, section * half, half, 1)
    if straight:
        grad_final, grad_head, lse, picks = head_pass(
            final_rows, targets_group.reshape(line, 1, tokens), heads, line, head_rows, length, 3
        )
        ce_part = jnp.sum(lse) / chips - jnp.sum(picks)
    else:
        targets_group = targets_group.reshape(-1)
        handed = lax.ppermute(final_rows[:half], "section", [(1, 0), (0, 1)])
        own_final = jnp.where(is_first, handed, final_rows[half:])
        group_final = lax.all_gather(own_final, ("line", "pair"), tiled=True)
        logits = mm("td,vd->tv", group_final, head_group)
        local_top = jnp.max(logits, -1)
        local_total = jnp.sum(jnp.exp(logits - local_top[:, None]), -1)
        mark = columns[None, :] == targets_group[:, None]
        local_pick = jnp.sum(jnp.where(mark, logits, 0.0))
        stats = lax.all_gather(jnp.stack([local_top, local_total]), ("line", "pair"))
        all_top = jnp.max(stats[:, 0], 0)
        all_total = jnp.sum(stats[:, 1] * jnp.exp(stats[:, 0] - all_top), 0)
        log_total = all_top + jnp.log(all_total)
        soft_rows = jnp.exp(logits - log_total[:, None])
        logit_grads = ((soft_rows - jnp.where(mark, 1.0, 0.0)) / length).astype(bf16)
        grad_final = jnp.dot(logit_grads, head_group, preferred_element_type=f32).astype(bf16)
        grad_final = lax.psum_scatter(grad_final, ("line", "pair"), scatter_dimension=0, tiled=True)
        handed = lax.ppermute(grad_final, "section", swapped)
        grad_final = jnp.concatenate([handed, grad_final], 0)
        grad_head = mm("tv,td->vd", logit_grads, group_final).astype(bf16)
        grad_head = grad_head.reshape(sections, cores, head_rows, model_width)
        grad_head = lax.psum_scatter(grad_head, "core", scatter_dimension=1)
        grad_head = lax.psum_scatter(grad_head, "section", scatter_dimension=0).astype(f32)

        ce_part = jnp.sum(log_total) / chips - local_pick
    if straight:
        grad_second, grad_top, out_part = backward_pass(
            grad_final, block_out, out_gain[None, :], scale, kept, stacked
        )
        returned = lax.ppermute(grad_second, "section", swapped)
        out_part = out_part.reshape(-1)
        x, joined, mixed, middle, entry_attn, entry_mlp, slope, hidden = kept
        grad_middle, grad_entry, grad_branch, grad_up, grad_bias = backward_begin(
            returned, grad_top, seqs, slope, w_up, w_down
        )
        parts = [
            by_owner(mm("tf,td->fd", hidden, grad_branch)),
            by_owner(mm("td,tf->df", entry_mlp, grad_up)),
        ]
        grad_bias = grad_bias.reshape(-1)
    else:
        grad_final = grad_final.astype(f32).reshape(stream0.shape)
        out_part = jnp.sum(grad_final * final_normed, (0, 1))
        grad_top = norm_back(grad_final * out_gain, final_normed, final_factor)
        grad_second = layer_backward(grad_top, kept, scale_attn, scale_mlp, weights, False)[0]
        returned = lax.ppermute(grad_second.astype(bf16), "section", swapped)
        grad_cot = jnp.where(is_first, returned.astype(f32), grad_top)
        grad_stream, grads = layer_backward(grad_cot, kept, scale_attn, scale_mlp, weights, True)
        grad_first = grad_stream.astype(bf16)
    out_part = jnp.where(is_first, 0.0, out_part)

    ce_high = ce_part.astype(bf16).astype(f32)
    ce_mid = (ce_part - ce_high).astype(bf16).astype(f32)
    ce_low = ce_part - ce_high - ce_mid
    shared = jnp.concatenate([out_part, jnp.stack([ce_high, ce_mid, ce_low])])
    shared_rows = -(-shared.shape[0] // emb_width)
    shared = jnp.pad(shared, (0, shared_rows * emb_width - shared.shape[0]))
    shared = shared.reshape(-1, emb_width).astype(bf16)
    both = [shared, lax.ppermute(shared, "section", swapped)]

    cubed = unit_factor * unit_factor * unit_factor
    cond_rows = seqs * 2 * model_width // emb_width
    bias_rows = b_hidden.shape[1] // emb_width
    if straight:
        rest = jnp.concatenate([grad_bias.reshape(-1, emb_width)] + both, 0).astype(f32)
        rest = jnp.pad(rest, ((0, -(cond_rows + rest.shape[0]) % 16), (0, 0)))
        factors = [
            (value * noise_scale).reshape(tokens, 1) for value in (unit_factor, cubed)
        ]
        owned = noisy_rows.reshape(tokens, sections, dp_count, -1)
        owned = owned.swapaxes(1, 2).reshape(tokens, emb_width)
        far = [grad_middle, grad_entry, middle, x, joined, mixed, entry_attn, w_out, w_qkv]
        grad_down, grad_up, grad_qkv, grad_wout, grad_w_in, grad_head, smalls, rows_all = tail_pass(
            scale,
            rest,
            factors,
            embedded.reshape(tokens, emb_width),
            owned,
            w_in,
            far,
            parts,
            grad_head,
            2,
        )
        grad_head = grad_head[:head_rows]
        grad_down, grad_up, grad_qkv, grad_wout, grad_head = [
            value.astype(f32) for value in (grad_down, grad_up, grad_qkv, grad_wout, grad_head)
        ]
    else:
        in_part = mm("nse,nsd->ed", noisy_rows, grad_first).astype(bf16)
        in_part = in_part.reshape(sections, dp_count, -1, model_width).swapaxes(0, 1)
        in_sum = over_dp(in_part).astype(f32)
        in_handed = lax.ppermute(in_sum[1], "section", swapped)
        grad_w_in = jnp.where(is_first, in_sum[0], in_handed)
        grad_noisy = mm("nsd,ed->nse", grad_first, w_in)
        grad_unit = grad_noisy * noise_scale
        grad_embedded = unit_factor * grad_unit - cubed * embedded * jnp.mean(
            grad_unit * embedded, -1, keepdims=True
        )
        grad_flat = grad_embedded.reshape(tokens, emb_width).astype(bf16)
        handed = lax.ppermute(grad_flat, "section", swapped)
        rows_all = lax.all_gather(jnp.where(is_first, grad_flat, handed), DP)
        small = [grads["cond"].reshape(-1, emb_width), grads["bias"].reshape(-1, emb_width)]
        smalls = lax.all_gather(
            jnp.concatenate([value.astype(bf16) for value in small] + both, 0), DP
        )
        grad_down, grad_up, grad_qkv, grad_wout = [
            over_dp(part.reshape((dp_count,) + part.shape[3:])).astype(f32)
            for part in (grads["down"], grads["up"], grads["qkv"], grads["out"])
        ]

    grad_all = rows_all.reshape(-1, emb_width)
    out_rows = emb_rows // sections
    target_rows = (section * dp_count + dp_index) * out_rows + jnp.arange(out_rows)
    place = (target_rows[:, None] == all_tokens.reshape(-1)[None, :]).astype(bf16)
    grad_embed = jnp.dot(place, grad_all, preferred_element_type=f32)

    smalls = smalls.reshape(dp_count, -1, emb_width).astype(f32)
    cond_all = smalls[:, :cond_rows].reshape(dp_count * seqs, 2 * model_width)
    bias_all = smalls[:, cond_rows : cond_rows + bias_rows].reshape(dp_count, -1)
    hidden_rows = bias_all.shape[1] // dp_count
    grad_bias = jnp.sum(
        lax.dynamic_slice_in_dim(bias_all, dp_index * hidden_rows, hidden_rows, 1), 0
    )
    norm_cols = 2 * model_width // dp_count
    grad_gain = jnp.sum(lax.dynamic_slice_in_dim(cond_all, dp_index * norm_cols, norm_cols, 1), 0)
    feats_all = time_features(levels_of(all_bins, sigma_table))
    feat_rows = TFEAT // dp_count
    feats_own = lax.dynamic_slice_in_dim(feats_all, dp_index * feat_rows, feat_rows, 1)
    grad_time = jnp.dot(feats_own.T, cond_all, precision=highest)
    shared_first = cond_rows + bias_rows
    both = smalls[:, shared_first : shared_first + 2 * shared_rows]
    both = jnp.sum(both.reshape(dp_count, 2, -1), (0, 1))
    loss = jnp.sum(both[model_width : model_width + 3]) / (tokens * dp_count)
    gain_rows = model_width // dp_count
    grad_out_gain = lax.dynamic_slice_in_dim(both, dp_index * gain_rows, gain_rows)
    return (
        loss,
        grad_embed,
        grad_w_in,
        grad_time[None],
        grad_gain[None],
        grad_qkv[None],
        grad_wout[None],
        grad_up[None],
        grad_bias[None],
        grad_down[None],
        grad_out_gain,
        grad_head,
    )


def solution(mesh):
    sections, dp_count = mesh.shape["section"], mesh.shape["dp"]
    fine = Mesh(mesh.devices.reshape(sections, dp_count // 4, 2, 2), ("section",) + DP)
    everywhere = ("section",) + DP
    in_specs = (
        P(DP, None),
        P(DP, None),
        P(DP),
        P(),
        P(DP, None, None),
        P(DP, None),
        P(),
        P("section", None, None),
        P("section", None),
        P("section", None, None),
        P("section", None, None),
        P("section", None, None),
        P("section", None),
        P("section", None, None),
        P(),
        P(everywhere, None),
    )
    out_specs = (
        P(),
        P(everywhere, None),
        P(everywhere, None),
        P("section", DP, None),
        P("section", DP),
        P("section", DP, None),
        P("section", DP, None),
        P("section", DP, None),
        P("section", DP),
        P("section", DP, None),
        P(DP),
        P(everywhere, None),
    )
    return jax.shard_map(local, mesh=fine, in_specs=in_specs, out_specs=out_specs, check_vma=False)
```

```python
from functools import partial
import math

import jax
import jax.numpy as jnp
from jax import lax
from jax.experimental import pallas as pl
from jax.experimental.pallas import tpu as pltpu
from jax.sharding import Mesh, PartitionSpec as P

HEADS = 16
HEAD_DIM = 64
TFEAT = 256

epsilon = 1e-05
highest = lax.Precision.HIGHEST
f32 = jnp.float32
bf16 = jnp.bfloat16
DP = ("line", "pair", "core")


MESH = pl.DeviceIdType.MESH


def nt(left, right):
    return lax.dot_general(left, right, (((1,), (1,)), ((), ())), preferred_element_type=f32)


def tn(left, right):
    return lax.dot_general(left, right, (((0,), (0,)), ((), ())), preferred_element_type=f32)


def nn(left, right):
    return jnp.dot(left, right, preferred_element_type=f32)


def greet(peers):
    barrier = pltpu.get_barrier_semaphore()
    for peer in peers:
        pl.semaphore_signal(barrier, inc=1, device_id=peer, device_id_type=MESH)
    pl.semaphore_wait(barrier, len(peers))


def remote(source, target, send, recv, peer):
    return pltpu.make_async_remote_copy(
        src_ref=source,
        dst_ref=target,
        send_sem=send,
        recv_sem=recv,
        device_id=peer,
        device_id_type=MESH,
    )


def ring_place(position, line):
    turned = position // line
    return position * (1 - turned) + (2 * line - 1 - position) * turned, turned


def rows_kernel(line, found, out, own, from_core, from_pair, from_line, *sems):
    load_sem, core_send, core_recv, pair_send, pair_recv, line_send, line_recv, swap_send, swap_recv = (
        sems
    )
    me_section = lax.axis_index("section")
    me_line = lax.axis_index("line")
    me_pair = lax.axis_index("pair")
    me_core = lax.axis_index("core")
    section_peer = {"section": 1 - me_section}
    core_peer = {"core": 1 - me_core}
    pair_peer = {"pair": 1 - me_pair}
    line_at = [lax.rem(me_line + step, line) for step in range(1, line)]
    greet([section_peer, core_peer, pair_peer] + [{"line": place} for place in line_at])
    rows, width = out.shape[-2:]
    wide = width // 2
    sides = (1 - me_pair, me_pair)
    loads, core_copies, pair_copies, line_copies = {}, {}, {}, {}
    for turn, side in enumerate(sides):
        for piece in range(2):
            cols = pl.ds(piece * wide, wide)
            loads[piece, turn] = pltpu.make_async_copy(
                found.at[:, side, me_core, :, cols],
                own.at[:, side, :, cols],
                load_sem.at[piece, turn],
            )
            core_copies[piece, turn] = remote(
                found.at[:, side, 1 - me_core, :, cols],
                from_core.at[:, side, :, cols],
                core_send.at[piece, turn],
                core_recv.at[piece, turn],
                core_peer,
            )
            loads[piece, turn].start()
            core_copies[piece, turn].start()

    def tiles(body):
        @pl.loop(0, rows // 16)
        def _(block):
            body(pl.ds(pl.multiple_of(block * 16, 16), 16))

    for piece in range(2):
        cols = pl.ds(piece * wide, wide)
        side = sides[0]
        loads[piece, 0].wait()
        core_copies[piece, 0].wait_recv()

        def add(row):
            for place in range(line):
                total = from_core[place, side, row, cols] + own[place, side, row, cols]
                from_core[place, side, row, cols] = total

        tiles(add)
        pair_copies[piece] = remote(
            from_core.at[:, side, :, cols],
            from_pair.at[:, :, cols],
            pair_send.at[piece],
            pair_recv.at[piece],
            pair_peer,
        )
        pair_copies[piece].start()
    for piece in range(2):
        cols = pl.ds(piece * wide, wide)
        loads[piece, 1].wait()
        core_copies[piece, 1].wait_recv()
        pair_copies[piece].wait_recv()

        def add(row):
            for place in range(line):
                total = from_core[place, me_pair, row, cols] + own[place, me_pair, row, cols]
                from_core[place, me_pair, row, cols] = total + from_pair[place, row, cols]

        tiles(add)
        for n in range(line - 1):
            line_copies[piece, n] = remote(
                from_core.at[line_at[n], me_pair, :, cols],
                from_line.at[n, :, cols],
                line_send.at[piece, n],
                line_recv.at[piece, n],
                {"line": line_at[n]},
            )
            line_copies[piece, n].start()
    for piece in range(2):
        cols = pl.ds(piece * wide, wide)
        for n in range(line - 1):
            line_copies[piece, n].wait_recv()

        def add(row):
            total = from_core[me_line, me_pair, row, cols]
            for n in range(line - 1):
                total = total + from_line[n, row, cols]
            out[me_section, row, cols] = total

        tiles(add)
    swap = remote(out.at[me_section], out.at[me_section], swap_send, swap_recv, section_peer)
    swap.start()
    for copy in list(core_copies.values()) + list(pair_copies.values()) + list(line_copies.values()):
        copy.wait_send()
    swap.wait()


def rows_over_dp(found, collective_id):
    line = found.shape[0]
    shape = found.shape[-2:]
    dma = pltpu.SemaphoreType.DMA
    return pl.pallas_call(
        partial(rows_kernel, line),
        out_shape=jax.ShapeDtypeStruct((2,) + shape, bf16),
        in_specs=[pl.BlockSpec(memory_space=pl.ANY)],
        out_specs=pl.BlockSpec(memory_space=pltpu.VMEM),
        scratch_shapes=[
            pltpu.VMEM((line, 2) + shape, bf16),
            pltpu.VMEM((line, 2) + shape, bf16),
            pltpu.VMEM((line,) + shape, bf16),
            pltpu.VMEM((line - 1,) + shape, bf16),
        ]
        + [dma((2, 2))] * 3
        + [dma((2,))] * 2
        + [dma((2, line - 1))] * 2
        + [dma, dma],
        compiler_params=pltpu.CompilerParams(
            collective_id=collective_id, has_side_effects=True, vmem_limit_bytes=32 * 2**20
        ),
        cost_estimate=pl.CostEstimate(flops=0, bytes_accessed=2**26, transcendentals=0),
    )(found)


def gather_kernel(line, mine, out, send, recv, own_sem):
    me_line = lax.axis_index("line")
    me_pair = lax.axis_index("pair")
    me_core = lax.axis_index("core")
    peers = []
    for step in range(1, line * 4):
        peers.append(
            {
                "line": lax.rem(me_line + step // 4, line),
                "pair": lax.rem(me_pair + step // 2 % 2, 2),
                "core": lax.rem(me_core + step % 2, 2),
            }
        )
    greet(peers)
    place = out.at[me_line, me_pair, me_core]
    keep = pltpu.make_async_copy(mine, place, own_sem)
    keep.start()
    copies = [remote(mine, place, send.at[n], recv.at[n], peer) for n, peer in enumerate(peers)]
    for copy in copies:
        copy.start()
    keep.wait()
    for copy in copies:
        copy.wait()


def gathered_small(block, line, collective_id):
    count = line * 4 - 1
    vmem = pl.BlockSpec(memory_space=pltpu.VMEM)
    return pl.pallas_call(
        partial(gather_kernel, line),
        out_shape=jax.ShapeDtypeStruct((line, 2, 2) + block.shape, block.dtype),
        in_specs=[vmem],
        out_specs=vmem,
        scratch_shapes=[
            pltpu.SemaphoreType.DMA((count,)),
            pltpu.SemaphoreType.DMA((count,)),
            pltpu.SemaphoreType.DMA,
        ],
        compiler_params=pltpu.CompilerParams(collective_id=collective_id, has_side_effects=True),
        cost_estimate=pl.CostEstimate(flops=0, bytes_accessed=2**25, transcendentals=0),
    )(block)


def head_kernel(line, head_rows, length, *refs):
    final, targets, *heads = refs[:6]
    out, grads, lse_out, pick_out = refs[6:10]
    (table, rows_all, logits, probs, acc, parts, from_pair, from_line, stats, done) = refs[10:20]
    (head_sem, own_sem, give_send, give_recv, along_send, along_recv, pair_send, pair_recv) = refs[20:28]
    (stat_send, stat_recv, sum_send, sum_recv, line_send, line_recv, back_send, back_recv) = refs[28:]
    half = final.shape[0] // 2
    width = 2 * half
    padded = heads[0].shape[0]
    me_section = lax.axis_index("section")
    me_line = lax.axis_index("line")
    me_pair = lax.axis_index("pair")
    me_core = lax.axis_index("core")
    section_peer = {"section": 1 - me_section}
    pair_peer = {"pair": 1 - me_pair}
    chip_peers = []
    for step in range(1, 2 * line):
        chip_peers.append(
            {"line": lax.rem(me_line + step // 2, line), "pair": lax.rem(me_pair + step % 2, 2)}
        )
    greet(chip_peers + [section_peer])

    def side(pair):
        return pl.ds(pl.multiple_of(pair * half, 16), half)

    loads = [
        pltpu.make_async_copy(part, table.at[pl.ds(n * padded, padded)], head_sem.at[n])
        for n, part in enumerate(heads)
    ]
    for load in loads:
        load.start()

    quarter = half // 2

    def token_rows(place, pair, chunk):
        first = place * width + pair * half + chunk * quarter
        return pl.ds(pl.multiple_of(first, 16), quarter)

    def group(place):
        return pl.ds(pl.multiple_of(place * width, 128), width)

    def column_block(place, chunk):
        return rows_all.at[token_rows(place, me_pair, chunk)]

    def give(chunk):
        return remote(
            final.at[pl.ds(chunk * quarter, quarter)],
            column_block(me_line, chunk),
            give_send.at[chunk],
            give_recv.at[chunk],
            section_peer,
        )

    def along(step, way, chunk):
        block = column_block(me_line - way * step, chunk)
        turn = (way + 1) // 2
        return remote(
            block,
            block,
            along_send.at[turn, step, chunk],
            along_recv.at[turn, step, chunk],
            {"line": me_line + way},
        )

    def inside(place):
        return (place >= 0) & (place < line)

    def sends_along(step, way):
        return inside(me_line - way * step) & inside(me_line + way)

    def sideways(place, chunk):
        block = column_block(place, chunk)
        return remote(
            block, block, pair_send.at[place, chunk], pair_recv.at[place, chunk], pair_peer
        )

    def arrived_sideways(place, chunk):
        block = rows_all.at[token_rows(place, 1 - me_pair, chunk)]
        return remote(
            block, block, pair_send.at[place, chunk], pair_recv.at[place, chunk], pair_peer
        )

    @pl.when(me_section == 1)
    def _():
        for chunk in range(2):
            give(chunk).start()
        for chunk in range(2):
            keep = pltpu.make_async_copy(
                final.at[pl.ds(half + chunk * quarter, quarter)],
                column_block(me_line, chunk),
                own_sem.at[chunk],
            )
            keep.start()
            keep.wait()

    for chunk in range(2):

        @pl.when(me_section == 0)
        def _():
            give(chunk).wait_recv()

        for way in (1, -1):

            @pl.when(sends_along(0, way))
            def _():
                along(0, way, chunk).start()

        sideways(me_line, chunk).start()

    def pass_on(step):
        for chunk in range(2):
            for way in (1, -1):
                place = me_line - way * step

                @pl.when(inside(place))
                def _():
                    block = column_block(place, chunk)
                    turn = (way + 1) // 2
                    remote(
                        block,
                        block,
                        along_send.at[turn, step - 1, chunk],
                        along_recv.at[turn, step - 1, chunk],
                        {"line": me_line - way},
                    ).wait_recv()

                    @pl.when(inside(me_line + way))
                    def _():
                        along(step, way, chunk).start()

                    sideways(place, chunk).start()

    nearest = []
    for own in range(line):
        near = [own]
        for step in range(1, line):
            near += [place for place in (own - step, own + step) if 0 <= place < line]
        nearest.append(near)

    def by_distance(turn):
        place = 0
        for own in range(line):
            for n in range(line):
                hit = ((me_line == own) & (turn == n)).astype(jnp.int32)
                place = place + hit * nearest[own][n]
        return place

    def vocabulary(tile, rows):
        shard = tile * rows // padded
        first = lax.rem(tile * rows, padded)
        shard_section = lax.rem(me_section + shard // 2, 2)
        shard_core = lax.rem(me_core + lax.rem(shard, 2), 2)
        base = (((shard_section * line + me_line) * 2 + me_pair) * 2 + shard_core) * head_rows
        row = lax.broadcasted_iota(jnp.int32, (rows, 1), 0) + first
        return jnp.where(row < head_rows, row + base, -1)

    tile_rows = 512
    tiles = 4 * padded // tile_rows
    lowest = -1e30

    def score(turn, tops):
        place = by_distance(turn) if turn < line else None
        before = by_distance(turn - 1) if turn > 0 else None
        wanted = None if place is None else targets[place]

        def one(tile, carry):
            rows = pl.ds(pl.multiple_of(tile * tile_rows, tile_rows), tile_rows)
            out = []
            if place is not None:
                top, pick = carry[:2]
                entry = vocabulary(tile, tile_rows)
                part = nt(table[rows, :], rows_all[group(place), :])
                part = jnp.where(entry >= 0, part, lowest)
                logits[turn % 2, rows, :] = part
                out.append(jnp.maximum(top, jnp.max(part, 0, keepdims=True)))
                out.append(
                    pick + jnp.sum(jnp.where(entry == wanted, part, 0.0), 0, keepdims=True)
                )
            if before is not None:
                value = jnp.exp(logits[(turn - 1) % 2, rows, :] - tops)
                probs[rows, group(before)] = value.astype(bf16)
                out.append(carry[-1] + jnp.sum(value, 0, keepdims=True))
            return tuple(out)

        none = jnp.zeros((1, width), f32)
        start = () if place is None else (jnp.full((1, width), lowest, f32), none)
        start += () if before is None else (none,)
        result = lax.fori_loop(0, tiles, one, start)
        if place is not None:
            pick_out[place] = result[1]
        if before is not None:
            own = stats.at[me_line, me_pair, before]
            own[:, 0:width] = tops
            own[:, width : 2 * width] = result[-1]
            for n in range(len(chip_peers)):
                stat_copy(n, before).start()
        return None if place is None else result[0]

    def stat_copy(n, place):
        own = stats.at[me_line, me_pair, place]
        return remote(own, own, stat_send.at[n, place], stat_recv.at[n, place], chip_peers[n])

    def stat_wait(n, place):
        peer = chip_peers[n]
        source_line = lax.rem(2 * me_line + line - peer["line"], line)
        source_pair = peer["pair"]
        block = stats.at[source_line, source_pair, place]
        remote(block, block, stat_send.at[n, place], stat_recv.at[n, place], peer).wait_recv()

    for load in loads:
        load.wait()

    tops = None
    for turn in range(line + 1):
        if turn + 1 < line:
            pass_on(turn + 1)
        if turn < line:
            for chunk in range(2):
                arrived_sideways(by_distance(turn), chunk).wait_recv()
        tops = score(turn, tops)

    def part_rows(pair, chunk):
        return pl.ds(pl.multiple_of(pair * half + chunk * quarter, 16), quarter)

    def sum_copy(turn, chunk):
        place = lax.rem(me_line + turn + 1, line)
        return remote(
            parts.at[place, part_rows(1 - me_pair, chunk)],
            from_pair.at[turn, pl.ds(chunk * quarter, quarter)],
            sum_send.at[turn, chunk],
            sum_recv.at[turn, chunk],
            pair_peer,
        )

    def line_copy(turn, chunk):
        place = lax.rem(me_line + turn + 1, line)
        return remote(
            parts.at[place, part_rows(me_pair, chunk)],
            from_line.at[turn, pl.ds(chunk * quarter, quarter)],
            line_send.at[turn, chunk],
            line_recv.at[turn, chunk],
            {"line": place},
        )

    def finish(turn, chunk):
        place = lax.rem(me_line + turn + 1, line)
        sum_copy(turn, chunk).wait_recv()
        own = parts.at[place, part_rows(me_pair, chunk)]
        other = from_pair.at[turn, pl.ds(chunk * quarter, quarter)]

        @pl.loop(0, quarter // 16)
        def _(block):
            rows = pl.ds(pl.multiple_of(block * 16, 16), 16)
            own[rows, :] = (own[rows, :].astype(f32) + other[rows, :].astype(f32)).astype(bf16)

    @pl.loop(0, line)
    def _(turn):
        place = lax.rem(me_line + turn + 1, line)
        for n in range(len(chip_peers)):
            stat_wait(n, place)
        tops = [stats[a, b, place, :, 0:width] for a in range(line) for b in range(2)]
        totals = [
            stats[a, b, place, :, width : 2 * width] for a in range(line) for b in range(2)
        ]
        top = tops[0]
        for value in tops[1:]:
            top = jnp.maximum(top, value)
        total = jnp.zeros_like(top)
        for peak, part in zip(tops, totals):
            total = total + part * jnp.exp(peak - top)
        lse = top + jnp.log(total)
        lse_out[place] = lse
        factor = jnp.exp(stats[me_line, me_pair, place, :, 0:width] - lse) / length
        wanted = targets[place]

        def scaled(tile):
            rows = pl.ds(tile * padded, padded)
            entry = vocabulary(tile, padded)
            grad = probs[rows, group(place)].astype(f32) * factor
            grad = (grad - jnp.where(entry == wanted, 1.0 / length, 0.0)).astype(bf16)
            probs[rows, group(place)] = grad
            return grad

        grad = scaled(0)
        for tile in range(4):
            product = tn(grad, table[pl.ds(tile * padded, padded), :])
            if tile < 3:
                grad = scaled(tile + 1)
                acc[...] = product if tile == 0 else acc[...] + product
            else:
                parts[place] = (acc[...] + product).astype(bf16)

        for chunk in range(2):
            sum_copy(turn, chunk).start()

        @pl.when(turn > 0)
        def _():
            for chunk in range(2):
                finish(turn - 1, chunk)
                line_copy(turn - 1, chunk).start()

    gh_rows = 256
    gh_tiles = 4 * padded // gh_rows

    def head_grads(first, last):
        @pl.loop(first, last)
        def _(tile):
            rows = pl.ds(pl.multiple_of(tile * gh_rows, gh_rows), gh_rows)
            value = jnp.dot(probs[rows, :], rows_all[...], preferred_element_type=f32)
            grads[rows, :] = value.astype(bf16)

    def back(chunk):
        part = pl.ds(chunk * quarter, quarter)
        return remote(
            done.at[part], out.at[part], back_send.at[chunk], back_recv.at[chunk], section_peer
        )

    head_grads(0, gh_tiles // 2)
    for chunk in range(2):
        finish(line - 1, chunk)
        for turn in range(line - 1):
            line_copy(turn, chunk).wait_recv()
        own = parts.at[me_line, part_rows(me_pair, chunk)]

        @pl.loop(0, quarter // 16)
        def _(block):
            rows = pl.ds(pl.multiple_of(block * 16, 16), 16)
            chunk_rows = pl.ds(pl.multiple_of(chunk * quarter + block * 16, 16), 16)
            value = own[rows, :].astype(f32)
            for turn in range(line - 1):
                value = value + from_line[turn, chunk_rows, :].astype(f32)
            done[chunk_rows, :] = value.astype(bf16)

        @pl.when(me_section == 0)
        def _():
            back(chunk).start()

    @pl.when(me_section == 0)
    def _():
        out[...] = jnp.zeros_like(out)

    @pl.when(me_section == 1)
    def _():
        out[pl.ds(half, half), :] = done[...]

    head_grads(gh_tiles // 2, gh_tiles)
    for chunk in range(2):

        @pl.when(me_section == 0)
        def _():
            back(chunk).wait_send()

        @pl.when(me_section == 1)
        def _():
            back(chunk).wait_recv()
            give(chunk).wait_send()

        for way in (1, -1):
            for step in range(line - 1):

                @pl.when(sends_along(step, way))
                def _():
                    along(step, way, chunk).wait_send()

        for place in range(line):
            sideways(place, chunk).wait_send()
        for turn in range(line):
            sum_copy(turn, chunk).wait_send()
        for turn in range(line - 1):
            line_copy(turn, chunk).wait_send()
    for place in range(line):
        for n in range(len(chip_peers)):
            stat_copy(n, place).wait_send()


def head_pass(final, targets, heads, line, head_rows, length, collective_id):
    tokens, deep = final.shape
    half = tokens // 2
    padded = heads[0].shape[0]
    vmem = pl.BlockSpec(memory_space=pltpu.VMEM)
    anywhere = pl.BlockSpec(memory_space=pl.ANY)
    dma = pltpu.SemaphoreType.DMA
    peers = 2 * line - 1
    return pl.pallas_call(
        partial(head_kernel, line, head_rows, length),
        out_shape=[
            jax.ShapeDtypeStruct((tokens, deep), bf16),
            jax.ShapeDtypeStruct((4 * padded, deep), bf16),
            jax.ShapeDtypeStruct((line, 1, tokens), f32),
            jax.ShapeDtypeStruct((line, 1, tokens), f32),
        ],
        in_specs=[vmem, vmem] + [anywhere] * 4,
        out_specs=[vmem] * 4,
        scratch_shapes=[
            pltpu.VMEM((4 * padded, deep), bf16),
            pltpu.VMEM((line * tokens, deep), bf16),
            pltpu.VMEM((2, 4 * padded, tokens), f32),
            pltpu.VMEM((4 * padded, line * tokens), bf16),
            pltpu.VMEM((tokens, deep), f32),
            pltpu.VMEM((line, tokens, deep), bf16),
            pltpu.VMEM((line, half, deep), bf16),
            pltpu.VMEM((line - 1, half, deep), bf16),
            pltpu.VMEM((line, 2, line, 1, 2 * tokens), f32),
            pltpu.VMEM((half, deep), bf16),
            dma((4,)),
            dma((2,)),
            dma((2,)),
            dma((2,)),
            dma((2, line, 2)),
            dma((2, line, 2)),
            dma((line, 2)),
            dma((line, 2)),
            dma((peers, line)),
            dma((peers, line)),
            dma((line, 2)),
            dma((line, 2)),
            dma((line, 2)),
            dma((line, 2)),
            dma((2,)),
            dma((2,)),
        ],
        compiler_params=pltpu.CompilerParams(
            collective_id=collective_id, has_side_effects=True, vmem_limit_bytes=60 * 2**20
        ),
        cost_estimate=pl.CostEstimate(
            flops=24 * line * padded * tokens * deep, bytes_accessed=2**28, transcendentals=0
        ),
    )(final, targets, *heads)


def row_stats(values):
    centred = values - jnp.mean(values, -1, keepdims=True)
    factor = lax.rsqrt(jnp.mean(centred * centred, -1, keepdims=True) + epsilon)
    return centred * factor, factor


def two_heads(block):
    first = lax.broadcasted_iota(jnp.int32, block.shape, 1) < HEAD_DIM
    zero = jnp.zeros_like(block)
    return jnp.concatenate([jnp.where(first, block, zero), jnp.where(first, zero, block)], 0)


def one_block(stacked):
    rows = stacked.shape[0] // 2
    first = lax.broadcasted_iota(jnp.int32, (rows, stacked.shape[1]), 1) < HEAD_DIM
    return jnp.where(first, stacked[:rows], stacked[rows:])


def attention_weights(queries, keys):
    scores = nt(keys, queries) * (1.0 / math.sqrt(HEAD_DIM))
    exped = jnp.exp(scores - jnp.max(scores, 0, keepdims=True))
    return exped * (1.0 / jnp.sum(exped, 0, keepdims=True))


def tile_of(index, size):
    return pl.ds(pl.multiple_of(index * size, size), size)


def forward_kernel(full, seqs, *refs):
    refs = list(refs)

    def take(number):
        return [refs.pop(0) for _ in range(number)]

    start, scale, bias = take(3)
    arrived, gain = take(2) if full else (None, None)
    weights = take(4)
    if full:
        out, final, x, joined, mixed, middle, entry_attn, entry_mlp, slope, hidden = take(10)
    else:
        (out,) = take(1)
        x = start
        joined, mixed, middle, entry_attn = take(4)
        entry_mlp = entry_attn
    w_qkv, w_out, w_up, w_down, total, sems = refs
    width = start.shape[1]
    length = start.shape[0] // seqs
    load_qkv, load_out, load_up, load_down = [
        pltpu.make_async_copy(source.at[0], target, sems.at[n])
        for n, (source, target) in enumerate(zip(weights, (w_qkv, w_out, w_up, w_down)))
    ]
    load_qkv.start()

    for seq in range(seqs):
        rows = pl.ds(seq * length, length)
        if full:
            first = (lax.axis_index("section") == 0).astype(f32)
            x[rows, :] = start[rows, :] * first + arrived[rows, :].astype(f32) * (1.0 - first)
        normed, _ = row_stats(x[rows, :])
        entry_attn[rows, :] = (normed * scale[seq, :, :width]).astype(bf16)

    load_qkv.wait()
    load_out.start()
    load_up.start()
    tile = 512

    @pl.loop(0, 3 * width // tile)
    def _(index):
        cols = tile_of(index, tile)
        joined[:, cols] = nn(entry_attn[...], w_qkv[:, cols]).astype(bf16)

    load_out.wait()
    load_down.start()
    pairs = width // 128

    @pl.loop(0, pairs)
    def _(pair):
        cols = tile_of(pair, 128)
        for seq in range(seqs):
            rows = pl.ds(seq * length, length)
            queries = two_heads(joined[rows, cols])
            keys = joined[rows, tile_of(pair + pairs, 128)]
            values = joined[rows, tile_of(pair + 2 * pairs, 128)]
            probs = attention_weights(queries, keys).astype(bf16)
            mixed[rows, cols] = one_block(tn(probs, values)).astype(bf16)

    @pl.loop(0, width // tile)
    def _(index):
        cols = tile_of(index, tile)
        middle[:, cols] = x[:, cols] + nn(mixed[...], w_out[:, cols])

    for seq in range(seqs):
        rows = pl.ds(seq * length, length)
        normed, _ = row_stats(middle[rows, :])
        entry_mlp[rows, :] = (normed * scale[seq, :, width:]).astype(bf16)

    load_up.wait()
    load_down.wait()
    total[...] = middle[...]

    def gelu_of(up, cols):
        below = 0.5 + 0.5 * lax.erf(up * math.sqrt(0.5))
        value = (up * below).astype(bf16)
        if full:
            density = jnp.exp(-0.5 * up * up) * (1.0 / math.sqrt(2.0 * math.pi))
            slope[:, cols] = (below + up * density).astype(bf16)
            hidden[:, cols] = value
        return value

    @pl.loop(0, w_up.shape[1] // (2 * tile))
    def _(index):
        sides = [tile_of(2 * index + side, tile) for side in range(2)]
        ups = [nn(entry_mlp[...], w_up[:, cols]) + bias[:, cols] for cols in sides]
        both = jnp.concatenate([gelu_of(up, cols) for up, cols in zip(ups, sides)], 1)
        total[...] += nn(both, w_down[tile_of(index, 2 * tile), :])

    for seq in range(seqs):
        rows = pl.ds(seq * length, length)
        value = total[rows, :].astype(bf16)
        out[rows, :] = value
        if full:
            normed, _ = row_stats(value.astype(f32))
            final[rows, :] = (normed * gain[...]).astype(bf16)


def layer_scratch(width, hidden):
    return [
        pltpu.VMEM((width, 3 * width), bf16),
        pltpu.VMEM((width, width), bf16),
        pltpu.VMEM((width, hidden), bf16),
        pltpu.VMEM((hidden, width), bf16),
    ]


def forward_pass(start, scale, weights, arrived=None, gain=None):
    w_qkv, w_out, w_up, b_hidden, w_down = weights
    tokens, width = start.shape
    wide = w_up.shape[-1]
    full = arrived is not None
    vmem = pl.BlockSpec(memory_space=pltpu.VMEM)
    anywhere = pl.BlockSpec(memory_space=pl.ANY)

    def low(columns):
        return (tokens, columns), bf16

    exact = ((tokens, width), f32)
    out_shape = [jax.ShapeDtypeStruct((tokens, width), bf16)]
    scratch = layer_scratch(width, wide)
    scratch += [pltpu.VMEM(*exact), pltpu.SemaphoreType.DMA((4,))]
    operands = [start, scale, b_hidden]
    if full:
        operands += [arrived, gain]
        kept = [low(width), exact, low(3 * width), low(width), exact, low(width), low(width)]
        out_shape += [jax.ShapeDtypeStruct(*item) for item in kept + [low(wide), low(wide)]]
    else:
        inside = [low(3 * width), low(width), exact, low(width)]
        scratch = [pltpu.VMEM(*item) for item in inside] + scratch
    flops = 2 * tokens * (4 * width * width + 2 * width * wide)
    return pl.pallas_call(
        partial(forward_kernel, full, scale.shape[0]),
        out_shape=out_shape,
        in_specs=[vmem] * len(operands) + [anywhere] * 4,
        out_specs=[vmem] * len(out_shape),
        scratch_shapes=scratch,
        compiler_params=pltpu.CompilerParams(vmem_limit_bytes=60 * 2**20),
        cost_estimate=pl.CostEstimate(flops=2 * flops, bytes_accessed=2**25, transcendentals=0),
    )(*operands, w_qkv, w_out, w_up, w_down)


def norm_grads(source, total, grad_middle, scale, grad_cond, half, seq, store):
    width = total.shape[1]
    length = total.shape[0] // scale.shape[0]
    rows = pl.ds(seq * length, length)
    cols = pl.ds(half * width, width)
    normed, factor = row_stats(source[rows, :])
    gradient = total[rows, :]
    if grad_cond is not None:
        grad_cond[seq, :, cols] = jnp.sum(gradient * normed, 0, keepdims=True)
    scaled = gradient * scale[seq, :, cols]
    back = factor * (
        scaled
        - jnp.mean(scaled, -1, keepdims=True)
        - normed * jnp.mean(scaled * normed, -1, keepdims=True)
    )
    store(rows, grad_middle[rows, :] + back)


def attention_grads(joined, grad_mixed, grad_joined, pair, seqs):
    pairs = grad_mixed.shape[1] // 128
    length = grad_mixed.shape[0] // seqs
    shrink = 1.0 / math.sqrt(HEAD_DIM)
    cols = tile_of(pair, 128)
    key_cols = tile_of(pair + pairs, 128)
    value_cols = tile_of(pair + 2 * pairs, 128)
    for seq in range(seqs):
        rows = pl.ds(seq * length, length)
        queries = two_heads(joined[rows, cols])
        keys = joined[rows, key_cols]
        probs = attention_weights(queries, keys)
        grads = two_heads(grad_mixed[rows, cols])
        grad_probs = nt(joined[rows, value_cols], grads)
        inner = jnp.sum(grad_probs * probs, 0, keepdims=True)
        grad_scores = (probs * (grad_probs - inner)).astype(bf16)
        grad_joined[rows, cols] = (one_block(tn(grad_scores, keys)) * shrink).astype(bf16)
        grad_joined[rows, key_cols] = (nn(grad_scores, queries) * shrink).astype(bf16)
        grad_joined[rows, value_cols] = nn(probs.astype(bf16), grads).astype(bf16)


def backward_kernel(begin, seqs, *refs):
    refs = list(refs)

    def take(number):
        return [refs.pop(0) for _ in range(number)]

    if begin:
        incoming, other, hidden, entry = take(4)
        far = take(3)
        grad_middle, total, grad_bias, down_out, up_out = take(5)
        grad_low, grad_up, entry_turned, down_weight, up_weight, out_sem = take(6)
        near = take(3)
    else:
        scale, incoming, other, gain = take(4)
        far = take(8)
        out, grad_top, grad_gain = take(3)
        grad_low, grad_up, grad_attn, grad_joined = take(4)
        near = take(8)
        total, grad_middle, grad_mixed = take(3)
    (sems,) = refs
    if begin:
        slope, w_up, w_down = near
        load_slope = pltpu.make_async_copy(far[0], slope, sems.at[0])
        load_up = pltpu.make_async_copy(far[1].at[0], w_up, sems.at[1])
        load_down = pltpu.make_async_copy(far[2].at[0], w_down, sems.at[2])
    else:
        slope, w_up, w_down, x, middle, joined, w_qkv, w_out = near
        load_slope = pltpu.make_async_copy(far[0], slope, sems.at[0])
        load_up = pltpu.make_async_copy(far[1].at[0], w_up, sems.at[1])
        load_down = pltpu.make_async_copy(far[2].at[0], w_down, sems.at[2])
        load_x = pltpu.make_async_copy(far[3], x, sems.at[3])
        load_middle = pltpu.make_async_copy(far[4], middle, sems.at[4])
        load_joined = pltpu.make_async_copy(far[5], joined, sems.at[5])
        load_qkv = pltpu.make_async_copy(far[6].at[0], w_qkv, sems.at[6])
        load_out = pltpu.make_async_copy(far[7].at[0], w_out, sems.at[7])
    width = incoming.shape[1]
    length = incoming.shape[0] // seqs
    load_down.start()
    load_slope.start()
    if begin:
        entry_turned[...] = entry[...].T

    for seq in range(seqs):
        rows = pl.ds(seq * length, length)
        if begin:
            first = (lax.axis_index("section") == 0).astype(f32)
            value = incoming[rows, :].astype(f32) * first + other[rows, :] * (1.0 - first)
        else:
            normed, factor = row_stats(other[rows, :].astype(f32))
            gradient = incoming[rows, :].astype(f32)
            part = jnp.sum(gradient * normed, 0, keepdims=True)
            grad_gain[...] = part if seq == 0 else grad_gain[...] + part
            scaled = gradient * gain[...]
            value = factor * (
                scaled
                - jnp.mean(scaled, -1, keepdims=True)
                - normed * jnp.mean(scaled * normed, -1, keepdims=True)
            )
            grad_top[rows, :] = value
        grad_middle[rows, :] = value
        grad_low[rows, :] = value.astype(bf16)

    load_down.wait()
    load_slope.wait()
    load_up.start()
    if not begin:
        load_middle.start()
        load_out.start()
        load_joined.start()
    tile = 1024

    @pl.loop(0, w_up.shape[1] // tile)
    def _(index):
        cols = tile_of(index, tile)
        grad_hidden = nt(grad_low[...], w_down[cols, :])
        value = (grad_hidden * slope[:, cols].astype(f32)).astype(bf16)
        grad_up[:, cols] = value
        if begin:
            grad_bias[:, cols] = jnp.sum(value.astype(f32), 0, keepdims=True)
            down_weight[cols, :] = tn(hidden[:, cols], grad_low[...]).astype(bf16)
            pltpu.make_async_copy(
                down_weight.at[cols], down_out.at[cols], out_sem.at[0, index]
            ).start()
            up_weight[:, cols] = nn(entry_turned[...], value).astype(bf16)

    if begin:
        whole_up = pltpu.make_async_copy(up_weight, up_out, out_sem.at[1, 0])
        whole_up.start()
    load_up.wait()
    if not begin:
        load_middle.wait()
        load_out.wait()
        load_joined.wait()
        load_qkv.start()
        load_x.start()

    @pl.loop(0, width // 256)
    def _(index):
        total[:, tile_of(index, 256)] = nt(grad_up[...], w_up[tile_of(index, 256), :])

    if begin:
        for index in range(w_up.shape[1] // tile):
            cols = pl.ds(index * tile, tile)
            pltpu.make_async_copy(
                down_weight.at[cols], down_out.at[cols], out_sem.at[0, index]
            ).wait()
        whole_up.wait()
        return

    def store_middle(rows, value):
        grad_middle[rows, :] = value
        grad_attn[rows, :] = value.astype(bf16)

    for seq in range(seqs):
        norm_grads(middle, total, grad_middle, scale, None, 1, seq, store_middle)

    @pl.loop(0, width // 512)
    def _(index):
        part = tile_of(index, 512)
        grad_mixed[:, part] = nt(grad_attn[...], w_out[part, :]).astype(bf16)

    @pl.loop(0, width // 128)
    def _(pair):
        attention_grads(joined, grad_mixed, grad_joined, pair, seqs)

    load_qkv.wait()
    load_x.wait()

    @pl.loop(0, width // 256)
    def _(index):
        total[:, tile_of(index, 256)] = nt(grad_joined[...], w_qkv[tile_of(index, 256), :])

    def store_out(rows, value):
        out[rows, :] = value.astype(bf16)

    for seq in range(seqs):
        norm_grads(x, total, grad_middle, scale, None, 0, seq, store_out)


def backward_pass(grad_final, block_out, gain, scale, kept, weights):
    w_qkv, w_out, w_up, _, w_down = weights
    x, joined, _, middle, _, _, slope, _ = kept
    tokens, width = x.shape
    wide = w_up.shape[-1]
    vmem = pl.BlockSpec(memory_space=pltpu.VMEM)
    anywhere = pl.BlockSpec(memory_space=pl.ANY)
    exact = ((tokens, width), f32)
    low = ((tokens, width), bf16)
    lows = [low, ((tokens, wide), bf16), low, ((tokens, 3 * width), bf16)]
    near = [
        ((tokens, wide), bf16),
        ((width, wide), bf16),
        ((wide, width), bf16),
        exact,
        exact,
        ((tokens, 3 * width), bf16),
        ((width, 3 * width), bf16),
        ((width, width), bf16),
    ]
    flops = 4 * tokens * (4 * width * width + 2 * width * wide)
    return pl.pallas_call(
        partial(backward_kernel, False, scale.shape[0]),
        out_shape=[jax.ShapeDtypeStruct(*item) for item in [low, exact, ((1, width), f32)]],
        in_specs=[vmem] * 4 + [anywhere] * 8,
        out_specs=[vmem] * 3,
        scratch_shapes=[pltpu.VMEM(*item) for item in lows + near + [exact, exact, low]]
        + [pltpu.SemaphoreType.DMA((8,))],
        compiler_params=pltpu.CompilerParams(vmem_limit_bytes=60 * 2**20),
        cost_estimate=pl.CostEstimate(flops=flops, bytes_accessed=2**25, transcendentals=0),
    )(scale, grad_final, block_out, gain, slope, w_up, w_down, x, middle, joined, w_qkv, w_out)


def backward_begin(returned, grad_top, seqs, hidden, entry, slope, w_up, w_down):
    tokens, width = grad_top.shape
    wide = w_up.shape[-1]
    vmem = pl.BlockSpec(memory_space=pltpu.VMEM)
    anywhere = pl.BlockSpec(memory_space=pl.ANY)
    exact = ((tokens, width), f32)
    low = ((tokens, width), bf16)
    wide_low = ((tokens, wide), bf16)
    up, down = ((width, wide), bf16), ((wide, width), bf16)
    results = [exact, exact, ((1, wide), f32), down, up]
    inside = [low, wide_low, ((width, tokens), bf16), down, up]
    return pl.pallas_call(
        partial(backward_kernel, True, seqs),
        out_shape=[jax.ShapeDtypeStruct(*item) for item in results],
        in_specs=[vmem] * 4 + [anywhere] * 3,
        out_specs=[vmem] * 3 + [anywhere] * 2,
        scratch_shapes=[pltpu.VMEM(*item) for item in inside]
        + [pltpu.SemaphoreType.DMA((2, wide // 1024))]
        + [pltpu.VMEM(*item) for item in (wide_low, up, down)]
        + [pltpu.SemaphoreType.DMA((3,))],
        compiler_params=pltpu.CompilerParams(vmem_limit_bytes=60 * 2**20),
        cost_estimate=pl.CostEstimate(
            flops=16 * tokens * width * wide, bytes_accessed=2**25, transcendentals=0
        ),
    )(returned, grad_top, hidden, entry, slope, w_up, w_down)


def tail_kernel(line, seqs, lag, *refs):
    refs = list(refs)

    def take(number):
        return [refs.pop(0) for _ in range(number)]

    scale, rest, factor_one, factor_two, embedded, noisy, w_in = take(7)
    far = take(9)
    parts = take(2)
    (head_part,) = take(1)
    outs = take(5)
    head_out, smalls, halves = take(3)
    near = take(9)
    grad_attn, grad_mixed, grad_joined, grad_first, grad_cond, in_weight = take(6)
    rows_own, small_wide, small_own = take(3)
    own, from_core, slots = take(2), take(5), take(5)
    head_own, head_core, head_section, last_total = take(4)
    far_sem, load_sem, core_send, core_recv, ring_send, ring_recv, credit = take(7)
    keep_sem, packet_send, packet_recv, wide_send, wide_recv, rows_send, rows_recv = take(7)
    head_sem, head_send, head_recv, cross_send, cross_recv, swap_send, swap_recv = take(7)
    grad_middle, grad_entry, middle, x, joined, mixed, entry_attn, w_out, w_qkv = near
    inside = [w_qkv, w_out, in_weight]
    groups = ((0, 1), (2, 3, 4))
    chips = 2 * line
    width = x.shape[1]
    me_section = lax.axis_index("section")
    me_line = lax.axis_index("line")
    me_pair = lax.axis_index("pair")
    me_core = lax.axis_index("core")
    position = me_line + me_pair * (chips - 1 - 2 * me_line)
    section_peer = {"section": 1 - me_section}
    core_peer = {"core": 1 - me_core}
    ways = (1, -1)
    ring_peers = []
    for way in ways:
        peer_line, peer_pair = ring_place(lax.rem(position + way + chips, chips), line)
        ring_peers.append({"line": peer_line, "pair": peer_pair})
    greet([core_peer, section_peer] + ring_peers)

    shapes = [ref.shape[-2:] for ref in from_core]

    def block_of(turn, step):
        ahead = lax.rem(position - ways[turn] * (1 + step) + 2 * chips, chips)
        return ring_place(ahead, line)

    def columns(index, turn):
        wide = shapes[index][-1] // 2
        return pl.ds(turn * wide, wide)

    def block_rows(index, place, pair, core):
        high = shapes[index][0]
        return pl.ds(pl.multiple_of(((place * 2 + pair) * 2 + core) * high, 16), high)

    def source(index, turn, step, core):
        place, pair = block_of(turn, step)
        cols = columns(index, turn)
        if index < 2:
            return parts[index].at[place, pair, core, :, cols]
        return inside[index - 2].at[block_rows(index, place, pair, core), cols]

    def load(index, turn, step):
        return pltpu.make_async_copy(
            source(index, turn, step, me_core),
            own[index].at[step % 2, :, columns(index, turn)],
            load_sem.at[index, turn, step],
        )

    def core_copy(index, turn, step):
        return remote(
            source(index, turn, step, 1 - me_core),
            from_core[index].at[step % 3, :, columns(index, turn)],
            core_send.at[index, turn, step],
            core_recv.at[index, turn, step],
            core_peer,
        )

    def ring_copy(index, turn, step):
        cols = columns(index, turn)
        passed = from_core[index].at[0, :, cols] if step == 0 else slots[index].at[step - 1, :, cols]
        return remote(
            passed,
            slots[index].at[step, :, cols],
            ring_send.at[index, turn, step],
            ring_recv.at[index, turn, step],
            ring_peers[turn],
        )

    def to_core(group, step):
        if step >= 3:
            pl.semaphore_wait(credit.at[group], 1)
        for index in groups[group]:
            for turn in range(2):
                if index < 2:
                    load(index, turn, step).start()
                core_copy(index, turn, step).start()

    def stop(group, step, between):
        first, last = step == 0, step == chips - 1
        for index in groups[group]:
            rows, wide = shapes[index][0], shapes[index][1] // 2
            tile = min(wide, 512)
            for turn in range(2):
                if index < 2:
                    load(index, turn, step).wait()
                core_copy(index, turn, step).wait_recv()
                if not first:
                    ring_copy(index, turn, step - 1).wait_recv()
                place, pair = block_of(turn, step)

                @pl.loop(0, rows // 16)
                def _(block):
                    row = pl.ds(pl.multiple_of(block * 16, 16), 16)
                    if index >= 2:
                        base = ((place * 2 + pair) * 2 + me_core) * rows + block * 16
                        own_row = pl.ds(pl.multiple_of(base, 16), 16)
                    for col in range(turn * wide, (turn + 1) * wide, tile):
                        cols = pl.ds(col, tile)
                        if index < 2:
                            mine = own[index][step % 2, row, cols]
                        else:
                            mine = inside[index - 2][own_row, cols]
                        total = from_core[index][step % 3, row, cols].astype(f32)
                        total = total + mine.astype(f32)
                        if not first:
                            total = total + slots[index][step - 1, row, cols].astype(f32)
                        if last and index == 4:
                            last_total[row, cols] = total
                        elif last:
                            outs[index][row, cols] = total.astype(bf16)
                        elif first:
                            from_core[index][0, row, cols] = total.astype(bf16)
                        else:
                            slots[index][step - 1, row, cols] = total.astype(bf16)

                if not last:
                    ring_copy(index, turn, step).start()
                between()
        if step == 1:
            for index in groups[group]:
                for turn in range(2):
                    ring_copy(index, turn, 0).wait_send()
        if 1 <= step <= 4:
            amount = 2 if step == 1 else 1
            pl.semaphore_signal(
                credit.at[group], inc=amount, device_id=core_peer, device_id_type=MESH
            )

    hops = (line, line - 1)

    def packet_blocks(place, pair):
        return [smalls.at[place, pair, me_core], halves.at[me_section, place, pair, me_core]]

    def packet_hops(turn, hop, away):
        place, pair = ring_place(
            lax.rem(position - ways[turn] * (hop + away) + 2 * chips, chips), line
        )
        return [
            remote(
                block,
                block,
                packet_send.at[n, turn, hop],
                packet_recv.at[n, turn, hop],
                ring_peers[turn],
            )
            for n, block in enumerate(packet_blocks(place, pair))
        ]

    def pass_packets(hop):
        for turn in range(2):
            if 0 < hop <= hops[turn]:
                for copy in packet_hops(turn, hop - 1, 1):
                    copy.wait_recv()
            if hop < hops[turn]:
                for copy in packet_hops(turn, hop, 0):
                    copy.start()

    small_slot, rows_slot = packet_blocks(me_line, me_pair)
    keep_small = pltpu.make_async_copy(small_own, small_slot, keep_sem.at[0])
    half = rows_own.shape[0] // 2
    keep_rows = pltpu.make_async_copy(rows_own.at[pl.ds(0, half)], rows_slot, keep_sem.at[1])
    rows_over = remote(
        rows_own.at[pl.ds(half, half)],
        halves.at[1, me_line, me_pair, me_core],
        rows_send,
        rows_recv,
        section_peer,
    )
    across = [
        remote(block, block, wide_send.at[n], wide_recv.at[n], core_peer)
        for n, block in enumerate([smalls.at[:, :, me_core], halves.at[me_section, :, :, me_core]])
    ]
    swap = remote(
        halves.at[me_section], halves.at[me_section], swap_send, swap_recv, section_peer
    )

    def packets_ready():
        keep_small.wait()

        @pl.when(me_section == 0)
        def _():
            keep_rows.wait()

        @pl.when(me_section == 1)
        def _():
            rows_over.wait_recv()

        pass_packets(0)

    def packets_over_cores():
        for copy in across:
            copy.start()

    def packets_over_sections():
        for copy in across:
            copy.wait_recv()
        swap.start()

    gather = [packets_ready] + [partial(pass_packets, hop) for hop in range(1, line + 1)]
    gather += [packets_over_cores, packets_over_sections]
    pauses = [0]

    high = head_part.shape[0] // 4

    def shard(n):
        return head_part.at[pl.ds(n * high, high)]

    head_loads = [
        pltpu.make_async_copy(shard(2 * n), head_own.at[n], head_sem.at[n]) for n in range(2)
    ]
    head_copies = [
        remote(shard(2 * n + 1), head_core.at[n], head_send.at[n], head_recv.at[n], core_peer)
        for n in range(2)
    ]
    head_copies.append(
        remote(head_core.at[1], head_section, head_send.at[2], head_recv.at[2], section_peer)
    )

    def head_over_cores():
        for copy in head_loads:
            copy.wait()
        for copy in head_copies[:2]:
            copy.wait_recv()

        @pl.loop(0, high // 16)
        def _(block):
            rows = pl.ds(pl.multiple_of(block * 16, 16), 16)
            value = head_core[1, rows, :].astype(f32) + head_own[1, rows, :].astype(f32)
            head_core[1, rows, :] = value.astype(bf16)

        head_copies[2].start()

    def head_over_sections():
        head_copies[2].wait_recv()

        @pl.loop(0, high // 16)
        def _(block):
            rows = pl.ds(pl.multiple_of(block * 16, 16), 16)
            value = head_core[0, rows, :].astype(f32) + head_own[0, rows, :].astype(f32)
            value = value + head_section[rows, :].astype(f32)
            head_out[rows, :] = value.astype(bf16)

    far_copies = []
    for n, (where, target) in enumerate(zip(far, near)):
        where = where.at[0] if n >= 7 else where
        far_copies.append(pltpu.make_async_copy(where, target, far_sem.at[n]))

    def waits(*numbers):
        for n in numbers:
            far_copies[n].wait()

    def store_middle(rows, value):
        grad_middle[rows, :] = value
        grad_attn[rows, :] = value.astype(bf16)

    def store_first(rows, value):
        grad_first[rows, :] = value.astype(bf16)

    def second_norm(seq):
        if seq == 0:
            waits(0, 1, 2)
        norm_grads(middle, grad_entry, grad_middle, scale, grad_cond, 1, seq, store_middle)

    def mixed_grads(index):
        if index == 0:
            waits(7)
        part = pl.ds(index * 512, 512)
        grad_mixed[:, part] = nt(grad_attn[...], w_out[part, :]).astype(bf16)

    def heads_grads(pair):
        if pair == 0:
            waits(4)
        attention_grads(joined, grad_mixed, grad_joined, pair, seqs)

    def entry_grads(index):
        if index == 0:
            waits(8)
        part = pl.ds(index * 256, 256)
        grad_entry[:, part] = nt(grad_joined[...], w_qkv[part, :])

    def first_norm(seq):
        if seq == 0:
            waits(3)
        norm_grads(x, grad_entry, grad_middle, scale, grad_cond, 0, seq, store_first)

    def embedding_rows(_):
        grad_noisy = nt(grad_first[...], w_in[...])
        inner = jnp.mean(grad_noisy * embedded[...], -1, keepdims=True)
        value = factor_one[...] * grad_noisy - factor_two[...] * embedded[...] * inner
        rows_own[...] = value.astype(bf16)

        @pl.when(me_section == 0)
        def _():
            keep_rows.start()
            rows_over.start()

    def small_rows(_):
        each = small_wide.shape[1]
        for seq in range(seqs):
            for n in range(2 * width // each):
                row = pl.ds(seq * (2 * width // each) + n, 1)
                small_wide[row, :] = grad_cond[seq, :, pl.ds(n * each, each)]
        small_wide[pl.ds(seqs * 2 * width // each, rest.shape[0]), :] = rest[...]
        small_own[...] = small_wide[...].astype(bf16)
        keep_small.start()

    def input_weight(_):
        in_weight[...] = tn(noisy[...], grad_first[...]).astype(bf16)

    def qkv_weight(index):
        if index == 0:
            waits(6)
        part = pl.ds(index * 256, 256)
        w_qkv[part, :] = tn(entry_attn[:, part], grad_joined[...]).astype(bf16)

    def out_weight(index):
        if index == 0:
            waits(5)
        part = pl.ds(index * 512, 512)
        w_out[part, :] = tn(mixed[:, part], grad_attn[...]).astype(bf16)

    steps = []
    for step, number in (
        (second_norm, seqs),
        (mixed_grads, width // 512),
        (heads_grads, width // 128),
        (entry_grads, width // 256),
        (first_norm, seqs),
        (embedding_rows, 1),
        (small_rows, 1),
        (input_weight, 1),
        (qkv_weight, width // 256),
        (out_weight, width // 512),
    ):
        steps += [partial(step, n) for n in range(number)]
    at_once = -(-len(steps) // (4 * lag))

    def work():
        for _ in range(at_once):
            if steps:
                steps.pop(0)()

    def gathering():
        pauses[0] += 1
        if gather and pauses[0] % 3 == 0:
            gather.pop(0)()

    to_core(0, 0)
    to_core(0, 1)
    for copy in far_copies:
        copy.start()
    stop(0, 0, work)
    for turn in range(1, chips + lag):
        if turn + 1 < chips:
            to_core(0, turn + 1)
        if turn == 1:
            for copy in head_loads + head_copies[:2]:
                copy.start()
        if turn == lag:
            to_core(1, 0)
        if lag <= turn and turn - lag + 1 < chips:
            to_core(1, turn - lag + 1)
        if turn < chips:
            stop(0, turn, work if turn < lag else gathering)
        if turn >= lag:
            stop(1, turn - lag, gathering)
        if turn == lag + 1:
            head_over_cores()
        if turn == chips + lag - 2:
            head_over_sections()
    each = outs[4].shape[0]
    give = remote(last_total.at[pl.ds(each, each)], outs[4], cross_send, cross_recv, section_peer)

    @pl.when(me_section == 0)
    def _():
        give.start()
        outs[4][...] = last_total[pl.ds(0, each), :]

    while gather:
        gather.pop(0)()
    swap.wait()
    for copy in across:
        copy.wait_send()
    for copy in head_copies:
        copy.wait_send()
    for turn in range(2):
        for hop in range(hops[turn]):
            for copy in packet_hops(turn, hop, 0):
                copy.wait_send()
    for index in range(5):
        for turn in range(2):
            for step in range(chips):
                core_copy(index, turn, step).wait_send()
                if 0 < step < chips - 1:
                    ring_copy(index, turn, step).wait_send()

    @pl.when(me_section == 0)
    def _():
        rows_over.wait_send()
        give.wait_send()

    @pl.when(me_section == 1)
    def _():
        give.wait_recv()


def tail_pass(scale, rest, factors, embedded, noisy, w_in, far, parts, head_part, collective_id):
    grad_middle = far[0]
    tokens, width = grad_middle.shape
    seqs = scale.shape[0]
    line = parts[0].shape[0]
    chips = 2 * line
    count = 4 * line
    emb_width = noisy.shape[1]
    vmem = pl.BlockSpec(memory_space=pltpu.VMEM)
    anywhere = pl.BlockSpec(memory_space=pl.ANY)
    dma = pltpu.SemaphoreType.DMA
    shapes = [part.shape[-2:] for part in parts]
    shapes += [
        (width // count, 3 * width),
        (width // count, width),
        (emb_width // count, width),
    ]
    each = shapes[4][0] // 2
    high = head_part.shape[0] // 4
    small = (seqs * 2 * width // emb_width + rest.shape[0], emb_width)
    exact = ((tokens, width), f32)
    low = ((tokens, width), bf16)
    three = ((tokens, 3 * width), bf16)
    rows = (tokens, emb_width)
    results = [(shape, bf16) for shape in shapes[:4]]
    results += [((each, width), f32), ((high, width), bf16)]
    results += [((line, 2, 2) + small, bf16)]
    results += [((2, line, 2, 2, tokens // 2, emb_width), bf16)]
    room = [exact, exact, exact, exact, three, low, low]
    room += [((width, width), bf16), ((width, 3 * width), bf16)]
    room += [low, low, three, low, ((seqs, 1, 2 * width), f32), ((emb_width, width), bf16)]
    room += [(rows, bf16), (small, f32), (small, bf16)]
    room += [((2,) + shape, bf16) for shape in shapes[:2]]
    room += [((3,) + shape, bf16) for shape in shapes]
    room += [((chips - 1,) + shape, bf16) for shape in shapes]
    room += [((2, high, width), bf16), ((2, high, width), bf16), ((high, width), bf16)]
    room += [(shapes[4], f32)]
    scratch = [pltpu.VMEM(*item) for item in room]
    scratch += [dma((9,)), dma((2, 2, chips)), dma((5, 2, chips)), dma((5, 2, chips))]
    scratch += [dma((5, 2, chips - 1)), dma((5, 2, chips - 1)), pltpu.SemaphoreType.REGULAR((2,))]
    scratch += [dma((2,)), dma((2, 2, line)), dma((2, 2, line)), dma((2,)), dma((2,)), dma, dma]
    scratch += [dma((2,)), dma((3,)), dma((3,)), dma, dma, dma, dma]
    return pl.pallas_call(
        partial(tail_kernel, line, seqs, 3),
        out_shape=[jax.ShapeDtypeStruct(*item) for item in results],
        in_specs=[vmem] * 7 + [anywhere] * 12,
        out_specs=[vmem] * 6 + [anywhere] * 2,
        scratch_shapes=scratch,
        compiler_params=pltpu.CompilerParams(
            collective_id=collective_id, has_side_effects=True, vmem_limit_bytes=62 * 2**20
        ),
        cost_estimate=pl.CostEstimate(flops=0, bytes_accessed=2**29, transcendentals=0),
    )(scale, rest, *factors, embedded, noisy, w_in, *far, *parts, head_part)


def finish_kernel(line, head_rows, *refs):
    ids, rows, *lows = refs[:7]
    *exacts, grad_embed, total = refs[7:]
    me_section = lax.axis_index("section")
    me_line = lax.axis_index("line")
    me_pair = lax.axis_index("pair")
    me_core = lax.axis_index("core")
    high = total.shape[0]
    base = (((me_section * line + me_line) * 2 + me_pair) * 2 + me_core) * grad_embed.shape[0]
    tile = 768
    for index in range(rows.shape[0] // tile):
        part = pl.ds(index * tile, tile)
        entry = lax.broadcasted_iota(jnp.int32, (high, tile), 0) + base
        place = jnp.where(entry == ids[:, part], 1.0, 0.0).astype(bf16)
        product = nn(place, rows[part, :])
        total[...] = product if index == 0 else total[...] + product
    grad_embed[...] = total[pl.ds(0, grad_embed.shape[0]), :]
    for low, exact in zip(lows, exacts):
        whole = exact.shape[0] // 16
        left = exact.shape[0] % 16

        @pl.loop(0, whole)
        def _(block):
            part = pl.ds(pl.multiple_of(block * 16, 16), 16)
            exact[part, :] = low[part, :].astype(f32)

        if left:
            value = low[pl.ds(whole * 16, 16), :].astype(f32)
            exact[pl.ds(whole * 16, left), :] = value[:left]


def finish(ids, rows, lows, line, head_rows, out_rows):
    vmem = pl.BlockSpec(memory_space=pltpu.VMEM)
    shapes = [low.shape for low in lows[:-1]] + [(head_rows, lows[-1].shape[1])]
    shapes.append((out_rows, rows.shape[1]))
    return pl.pallas_call(
        partial(finish_kernel, line, head_rows),
        out_shape=[jax.ShapeDtypeStruct(shape, f32) for shape in shapes],
        in_specs=[vmem] * 7,
        out_specs=[vmem] * 6,
        scratch_shapes=[pltpu.VMEM((-(-out_rows // 16) * 16, rows.shape[1]), f32)],
        compiler_params=pltpu.CompilerParams(vmem_limit_bytes=60 * 2**20),
        cost_estimate=pl.CostEstimate(
            flops=2 * out_rows * rows.size, bytes_accessed=2**24, transcendentals=0
        ),
    )(ids, rows, *lows)


def norm_rows(values):
    centred = values - jnp.mean(values, -1, keepdims=True)
    factor = lax.rsqrt(jnp.mean(centred * centred, -1, keepdims=True) + epsilon)
    return (centred * factor, factor)


def norm_back(gradient, normed, factor):
    return factor * (
        gradient
        - jnp.mean(gradient, -1, keepdims=True)
        - normed * jnp.mean(gradient * normed, -1, keepdims=True)
    )


def time_features(noise_level):
    half_width = TFEAT // 2
    rates = jnp.exp(jnp.arange(half_width, dtype=f32) * (math.log(1000.0) / half_width))
    angles = (jnp.log(noise_level) / 4.0)[:, None] * rates[None, :]
    return jnp.concatenate([jnp.cos(angles), jnp.sin(angles)], -1)


def levels_of(bins, table):
    hits = bins[:, None] == jnp.arange(table.shape[0])[None, :]
    return jnp.sum(jnp.where(hits, table[None, :], 0.0), -1)


def over_dp(part):
    part = part.reshape((part.shape[0] // 4, 2, 2) + part.shape[1:])
    part = lax.psum_scatter(part, "core", scatter_dimension=2)
    part = lax.psum_scatter(part, "pair", scatter_dimension=1)
    return lax.psum_scatter(part, "line", scatter_dimension=0)


def by_owner(part):
    line = lax.axis_size("line")
    return part.astype(bf16).reshape((line, 2, 2, part.shape[0] // (line * 4)) + part.shape[1:])


def mm(spec, left, right):
    return jnp.einsum(spec, left, right, preferred_element_type=f32)


def layer_forward(stream, scale_attn, scale_mlp, weights):
    w_qkv, w_out, w_up, b_hidden, w_down = weights
    seq_count, length, model_width = stream.shape
    normed_attn, factor_attn = norm_rows(stream)
    attn_entry = (normed_attn * scale_attn).astype(bf16)
    joined = mm("nsd,de->nse", attn_entry, w_qkv).astype(bf16)
    qkv_parts = joined.reshape(seq_count, length, 3, HEADS, HEAD_DIM)
    query_rows = qkv_parts[:, :, 0]
    key_rows = qkv_parts[:, :, 1]
    value_rows = qkv_parts[:, :, 2]
    scores = mm("nqhe,nkhe->nhqk", query_rows, key_rows) / math.sqrt(HEAD_DIM)
    exp_scores = jnp.exp(scores - jnp.max(scores, -1, keepdims=True))
    attn_probs = exp_scores / jnp.sum(exp_scores, -1, keepdims=True)
    probs_low = attn_probs.astype(bf16)
    attn_mixed = mm("nhqk,nkhe->nqhe", probs_low, value_rows).astype(bf16)
    attn_mixed = attn_mixed.reshape(seq_count, length, model_width)
    middle = stream + mm("nsd,de->nse", attn_mixed, w_out)
    normed_mlp, factor_mlp = norm_rows(middle)
    mlp_entry = (normed_mlp * scale_mlp).astype(bf16)
    up_proj = mm("nsd,df->nsf", mlp_entry, w_up) + b_hidden
    below = 0.5 + 0.5 * lax.erf(up_proj * math.sqrt(0.5))
    hidden = (up_proj * below).astype(bf16)
    density = jnp.exp(-0.5 * up_proj * up_proj) * (1.0 / math.sqrt(2.0 * math.pi))
    slope = (below + up_proj * density).astype(bf16)
    block_out = middle + mm("nsf,fd->nsd", hidden, w_down)
    kept = (
        normed_attn,
        factor_attn,
        attn_entry,
        query_rows,
        key_rows,
        value_rows,
        attn_probs,
        probs_low,
        attn_mixed,
        normed_mlp,
        factor_mlp,
        mlp_entry,
        slope,
        hidden,
    )
    return (block_out, kept)


def layer_backward(grad_out, kept, scale_attn, scale_mlp, weights, whole):
    w_qkv, w_out, w_up, b_hidden, w_down = weights
    (
        normed_attn,
        factor_attn,
        attn_entry,
        query_rows,
        key_rows,
        value_rows,
        attn_probs,
        probs_low,
        attn_mixed,
        normed_mlp,
        factor_mlp,
        mlp_entry,
        slope,
        hidden,
    ) = kept
    seq_count, length, model_width = grad_out.shape
    grads = {}
    grad_branch = grad_out.astype(bf16)
    if whole:
        grads["down"] = by_owner(mm("nsf,nsd->fd", hidden, grad_branch))
    grad_hidden = mm("nsd,fd->nsf", grad_branch, w_down)
    grad_up_proj = (grad_hidden * slope.astype(f32)).astype(bf16)
    if whole:
        grads["bias"] = jnp.sum(grad_up_proj.astype(f32), (0, 1))
        grads["up"] = by_owner(mm("nsd,nsf->df", mlp_entry, grad_up_proj))
    grad_entry = mm("nsf,df->nsd", grad_up_proj, w_up)
    grad_middle = grad_out + norm_back(grad_entry * scale_mlp, normed_mlp, factor_mlp)
    grad_attn = grad_middle.astype(bf16)
    if whole:
        grads["out"] = by_owner(mm("nsd,nse->de", attn_mixed, grad_attn))
    grad_mixed = mm("nse,de->nsd", grad_attn, w_out)
    grad_mixed = grad_mixed.astype(bf16).reshape(seq_count, length, HEADS, HEAD_DIM)
    grad_probs = mm("nqhe,nkhe->nhqk", grad_mixed, value_rows)
    grad_values = mm("nhqk,nqhe->nkhe", probs_low, grad_mixed)
    grad_scores = (
        attn_probs * (grad_probs - jnp.sum(grad_probs * attn_probs, -1, keepdims=True))
    ).astype(bf16)
    grad_query = mm("nhqk,nkhe->nqhe", grad_scores, key_rows) / math.sqrt(HEAD_DIM)
    grad_keys = mm("nhqk,nqhe->nkhe", grad_scores, query_rows) / math.sqrt(HEAD_DIM)
    grad_joined = jnp.stack([grad_query, grad_keys, grad_values], 2).astype(bf16)
    grad_joined = grad_joined.reshape(seq_count, length, 3 * model_width)
    if whole:
        grads["qkv"] = by_owner(mm("nsd,nse->de", attn_entry, grad_joined))
    grad_attn_entry = mm("nse,de->nsd", grad_joined, w_qkv)
    grad_stream = grad_middle + norm_back(grad_attn_entry * scale_attn, normed_attn, factor_attn)
    if whole:
        grads["cond"] = jnp.concatenate(
            [jnp.sum(grad_attn_entry * normed_attn, 1), jnp.sum(grad_entry * normed_mlp, 1)], -1
        )
    return (grad_stream, grads)


def local(
    token_ids,
    target_ids,
    time_bins,
    sigma_table,
    noise,
    embed,
    w_in,
    w_time,
    norm_gain,
    w_qkv,
    w_out,
    w_up,
    b_hidden,
    w_down,
    out_gain,
    head,
):
    section = lax.axis_index("section")
    line_at = lax.axis_index("line")
    pair_at = lax.axis_index("pair")
    core = lax.axis_index("core")
    sections = lax.axis_size("section")
    line = lax.axis_size("line")
    chip = line_at * 2 + pair_at
    chips = line * 2
    cores = 2
    dp_count = chips * cores
    dp_index = chip * cores + core
    is_first = section == 0
    seqs, length = token_ids.shape
    tokens = seqs * length
    half = tokens // sections
    model_width = w_out.shape[-1]
    emb_rows, emb_width = embed.shape
    straight = line <= 4 and half % 16 == 0 and model_width // dp_count % 16 == 0

    own_ids = jnp.concatenate([token_ids.reshape(-1), target_ids.reshape(-1), time_bins])
    if straight:
        padded = jnp.pad(own_ids, (0, -own_ids.shape[0] % 1024)).reshape(-1, 128)
        all_ids = gathered_small(padded, line, 0).reshape(dp_count, -1)[:, : own_ids.shape[0]]
    else:
        all_ids = lax.all_gather(own_ids, DP)
    all_tokens = all_ids[:, :tokens]
    all_targets = all_ids[:, tokens : 2 * tokens]
    all_bins = all_ids[:, 2 * tokens :].reshape(-1)

    own_rows = dp_index * emb_rows + jnp.arange(emb_rows)
    half_tokens = lax.dynamic_slice_in_dim(all_tokens, section * half, half, 1)
    picked = (half_tokens.reshape(-1)[:, None] == own_rows[None, :]).astype(bf16)
    found = jnp.dot(picked, embed, preferred_element_type=f32).astype(bf16)
    if straight:
        found = found.reshape(line, 2, 2, half, emb_width)
        embedded = rows_over_dp(found, 1)
    else:
        embedded = lax.all_gather(over_dp(found.reshape(dp_count, half, emb_width)), "section")
    embedded = embedded.astype(f32).reshape(seqs, length, emb_width)

    head_rows = head.shape[0]
    swapped = [(0, 1), (1, 0)]
    if straight:
        head_own = jnp.pad(head, ((0, -head_rows % 512), (0, 0)))
        head_section = lax.ppermute(head_own, "section", swapped)
    else:
        head_group = lax.all_gather(lax.all_gather(head, "core"), "section")
        head_group = head_group.reshape(-1, model_width)
        vocab_base = (
            (jnp.arange(sections)[:, None] * chips + chip) * cores + jnp.arange(cores)[None, :]
        ) * head_rows
        columns = (vocab_base[:, :, None] + jnp.arange(head_rows)[None, None, :]).reshape(-1)

    noise_level = levels_of(time_bins, sigma_table)
    unit_factor = lax.rsqrt(jnp.mean(embedded * embedded, -1, keepdims=True) + epsilon)
    level_col = noise_level[:, None, None]
    noise_scale = lax.rsqrt(level_col * level_col + 1.0)
    noisy_rows = ((embedded * unit_factor + level_col * noise) * noise_scale).astype(bf16)
    time_feats = time_features(noise_level)
    conditioned = jnp.dot(time_feats, w_time[0].astype(f32), precision=highest) + norm_gain[0]
    scale_attn = conditioned[:, None, :model_width]
    scale_mlp = conditioned[:, None, model_width:]
    scale = conditioned[:, None, :]
    weights = (w_qkv[0], w_out[0], w_up[0], b_hidden[0], w_down[0])
    stacked = (w_qkv, w_out, w_up, b_hidden, w_down)
    if straight:
        noisy_rows, head_own, head_section = lax.optimization_barrier(
            (noisy_rows, head_own, head_section)
        )
        heads = [head_own, lax.ppermute(head_own, "core", swapped)]
        heads += [head_section, lax.ppermute(head_section, "core", swapped)]

    stream0 = mm("nse,ed->nsd", noisy_rows, w_in)
    flat = (tokens, model_width)
    if straight:
        start = stream0.reshape(flat)
        (first_out,) = forward_pass(start, scale, stacked)
        arrived = lax.ppermute(first_out, "section", swapped)
        block_out, final_rows, *kept = forward_pass(
            start, scale, stacked, arrived, out_gain[None, :]
        )
    else:
        first_out = layer_forward(stream0, scale_attn, scale_mlp, weights)[0].astype(bf16)
        arrived = lax.ppermute(first_out, "section", swapped)
        stream = jnp.where(is_first, stream0, arrived.astype(f32))
        block_out, kept = layer_forward(stream, scale_attn, scale_mlp, weights)
        final_normed, final_factor = norm_rows(block_out.astype(bf16).astype(f32))
        final_rows = (final_normed * out_gain).astype(bf16).reshape(flat)

    targets_group = lax.dynamic_slice_in_dim(
        all_targets.reshape(chips, cores, tokens), core, 1, 1
    )[:, 0]
    targets_group = lax.dynamic_slice_in_dim(targets_group, section * half, half, 1)
    if straight:
        grad_final, grad_head, lse, picks = head_pass(
            final_rows, targets_group.reshape(line, 1, tokens), heads, line, head_rows, length, 3
        )
        ce_part = jnp.sum(lse) / chips - jnp.sum(picks)
    else:
        targets_group = targets_group.reshape(-1)
        handed = lax.ppermute(final_rows[:half], "section", [(1, 0), (0, 1)])
        own_final = jnp.where(is_first, handed, final_rows[half:])
        group_final = lax.all_gather(own_final, ("line", "pair"), tiled=True)
        logits = mm("td,vd->tv", group_final, head_group)
        local_top = jnp.max(logits, -1)
        local_total = jnp.sum(jnp.exp(logits - local_top[:, None]), -1)
        mark = columns[None, :] == targets_group[:, None]
        local_pick = jnp.sum(jnp.where(mark, logits, 0.0))
        stats = lax.all_gather(jnp.stack([local_top, local_total]), ("line", "pair"))
        all_top = jnp.max(stats[:, 0], 0)
        all_total = jnp.sum(stats[:, 1] * jnp.exp(stats[:, 0] - all_top), 0)
        log_total = all_top + jnp.log(all_total)
        soft_rows = jnp.exp(logits - log_total[:, None])
        logit_grads = ((soft_rows - jnp.where(mark, 1.0, 0.0)) / length).astype(bf16)
        grad_final = jnp.dot(logit_grads, head_group, preferred_element_type=f32).astype(bf16)
        grad_final = lax.psum_scatter(grad_final, ("line", "pair"), scatter_dimension=0, tiled=True)
        handed = lax.ppermute(grad_final, "section", swapped)
        grad_final = jnp.concatenate([handed, grad_final], 0)
        grad_head = mm("tv,td->vd", logit_grads, group_final).astype(bf16)
        grad_head = grad_head.reshape(sections, cores, head_rows, model_width)
        grad_head = lax.psum_scatter(grad_head, "core", scatter_dimension=1)
        grad_head = lax.psum_scatter(grad_head, "section", scatter_dimension=0).astype(f32)

        ce_part = jnp.sum(log_total) / chips - local_pick
    if straight:
        grad_second, grad_top, out_part = backward_pass(
            grad_final, block_out, out_gain[None, :], scale, kept, stacked
        )
        returned = lax.ppermute(grad_second, "section", swapped)
        out_part = out_part.reshape(-1)
        x, joined, mixed, middle, entry_attn, entry_mlp, slope, hidden = kept
        grad_middle, grad_entry, grad_bias, down_part, up_part = backward_begin(
            returned, grad_top, seqs, hidden, entry_mlp, slope, w_up, w_down
        )
        parts = [by_owner(down_part), by_owner(up_part)]
        grad_bias = grad_bias.reshape(-1)
    else:
        grad_final = grad_final.astype(f32).reshape(stream0.shape)
        out_part = jnp.sum(grad_final * final_normed, (0, 1))
        grad_top = norm_back(grad_final * out_gain, final_normed, final_factor)
        grad_second = layer_backward(grad_top, kept, scale_attn, scale_mlp, weights, False)[0]
        returned = lax.ppermute(grad_second.astype(bf16), "section", swapped)
        grad_cot = jnp.where(is_first, returned.astype(f32), grad_top)
        grad_stream, grads = layer_backward(grad_cot, kept, scale_attn, scale_mlp, weights, True)
        grad_first = grad_stream.astype(bf16)
    out_part = jnp.where(is_first, 0.0, out_part)

    ce_high = ce_part.astype(bf16).astype(f32)
    ce_mid = (ce_part - ce_high).astype(bf16).astype(f32)
    ce_low = ce_part - ce_high - ce_mid
    shared = jnp.concatenate([out_part, jnp.stack([ce_high, ce_mid, ce_low])])
    shared_rows = -(-shared.shape[0] // emb_width)
    shared = jnp.pad(shared, (0, shared_rows * emb_width - shared.shape[0]))
    shared = shared.reshape(-1, emb_width).astype(bf16)
    both = [shared, lax.ppermute(shared, "section", swapped)]

    cubed = unit_factor * unit_factor * unit_factor
    cond_rows = seqs * 2 * model_width // emb_width
    bias_rows = b_hidden.shape[1] // emb_width
    if straight:
        rest = jnp.concatenate([grad_bias.reshape(-1, emb_width)] + both, 0).astype(f32)
        rest = jnp.pad(rest, ((0, -(cond_rows + rest.shape[0]) % 16), (0, 0)))
        factors = [
            (value * noise_scale).reshape(tokens, 1) for value in (unit_factor, cubed)
        ]
        owned = noisy_rows.reshape(tokens, sections, dp_count, -1)
        owned = owned.swapaxes(1, 2).reshape(tokens, emb_width)
        far = [grad_middle, grad_entry, middle, x, joined, mixed, entry_attn, w_out, w_qkv]
        grad_down, grad_up, grad_qkv, grad_wout, grad_w_in, grad_head, smalls, halves = tail_pass(
            scale,
            rest,
            factors,
            embedded.reshape(tokens, emb_width),
            owned,
            w_in,
            far,
            parts,
            grad_head,
            2,
        )
        ids = all_tokens.reshape(dp_count, sections, half).swapaxes(0, 1).reshape(1, -1)
        grad_down, grad_up, grad_qkv, grad_wout, grad_head, grad_embed = finish(
            ids,
            halves.reshape(-1, emb_width),
            [grad_down, grad_up, grad_qkv, grad_wout, grad_head],
            line,
            head_rows,
            emb_rows // sections,
        )
    else:
        in_part = mm("nse,nsd->ed", noisy_rows, grad_first).astype(bf16)
        in_part = in_part.reshape(sections, dp_count, -1, model_width).swapaxes(0, 1)
        in_sum = over_dp(in_part).astype(f32)
        in_handed = lax.ppermute(in_sum[1], "section", swapped)
        grad_w_in = jnp.where(is_first, in_sum[0], in_handed)
        grad_noisy = mm("nsd,ed->nse", grad_first, w_in)
        grad_unit = grad_noisy * noise_scale
        grad_embedded = unit_factor * grad_unit - cubed * embedded * jnp.mean(
            grad_unit * embedded, -1, keepdims=True
        )
        grad_flat = grad_embedded.reshape(tokens, emb_width).astype(bf16)
        handed = lax.ppermute(grad_flat, "section", swapped)
        rows_all = lax.all_gather(jnp.where(is_first, grad_flat, handed), DP)
        small = [grads["cond"].reshape(-1, emb_width), grads["bias"].reshape(-1, emb_width)]
        smalls = lax.all_gather(
            jnp.concatenate([value.astype(bf16) for value in small] + both, 0), DP
        )
        grad_down, grad_up, grad_qkv, grad_wout = [
            over_dp(part.reshape((dp_count,) + part.shape[3:])).astype(f32)
            for part in (grads["down"], grads["up"], grads["qkv"], grads["out"])
        ]
        grad_all = rows_all.reshape(-1, emb_width)
        out_rows = emb_rows // sections
        target_rows = (section * dp_count + dp_index) * out_rows + jnp.arange(out_rows)
        place = (target_rows[:, None] == all_tokens.reshape(-1)[None, :]).astype(bf16)
        grad_embed = jnp.dot(place, grad_all, preferred_element_type=f32)

    smalls = smalls.reshape(dp_count, -1, emb_width).astype(f32)
    cond_all = smalls[:, :cond_rows].reshape(dp_count * seqs, 2 * model_width)
    bias_all = smalls[:, cond_rows : cond_rows + bias_rows].reshape(dp_count, -1)
    hidden_rows = bias_all.shape[1] // dp_count
    grad_bias = jnp.sum(
        lax.dynamic_slice_in_dim(bias_all, dp_index * hidden_rows, hidden_rows, 1), 0
    )
    norm_cols = 2 * model_width // dp_count
    grad_gain = jnp.sum(lax.dynamic_slice_in_dim(cond_all, dp_index * norm_cols, norm_cols, 1), 0)
    feats_all = time_features(levels_of(all_bins, sigma_table))
    feat_rows = TFEAT // dp_count
    feats_own = lax.dynamic_slice_in_dim(feats_all, dp_index * feat_rows, feat_rows, 1)
    grad_time = jnp.dot(feats_own.T, cond_all, precision=highest)
    shared_first = cond_rows + bias_rows
    both = smalls[:, shared_first : shared_first + 2 * shared_rows]
    both = jnp.sum(both.reshape(dp_count, 2, -1), (0, 1))
    loss = jnp.sum(both[model_width : model_width + 3]) / (tokens * dp_count)
    gain_rows = model_width // dp_count
    grad_out_gain = lax.dynamic_slice_in_dim(both, dp_index * gain_rows, gain_rows)
    return (
        loss,
        grad_embed,
        grad_w_in,
        grad_time[None],
        grad_gain[None],
        grad_qkv[None],
        grad_wout[None],
        grad_up[None],
        grad_bias[None],
        grad_down[None],
        grad_out_gain,
        grad_head,
    )


def solution(mesh):
    sections, dp_count = mesh.shape["section"], mesh.shape["dp"]
    fine = Mesh(mesh.devices.reshape(sections, dp_count // 4, 2, 2), ("section",) + DP)
    everywhere = ("section",) + DP
    in_specs = (
        P(DP, None),
        P(DP, None),
        P(DP),
        P(),
        P(DP, None, None),
        P(DP, None),
        P(),
        P("section", None, None),
        P("section", None),
        P("section", None, None),
        P("section", None, None),
        P("section", None, None),
        P("section", None),
        P("section", None, None),
        P(),
        P(everywhere, None),
    )
    out_specs = (
        P(),
        P(everywhere, None),
        P(everywhere, None),
        P("section", DP, None),
        P("section", DP),
        P("section", DP, None),
        P("section", DP, None),
        P("section", DP, None),
        P("section", DP),
        P("section", DP, None),
        P(DP),
        P(everywhere, None),
    )
    return jax.shard_map(local, mesh=fine, in_specs=in_specs, out_specs=out_specs, check_vma=False)
```

```python
from functools import partial
import math

import jax
import jax.numpy as jnp
from jax import lax
from jax.experimental import pallas as pl
from jax.experimental.pallas import tpu as pltpu
from jax.sharding import Mesh, PartitionSpec as P

HEADS = 16
HEAD_DIM = 64
TFEAT = 256

epsilon = 1e-05
highest = lax.Precision.HIGHEST
f32 = jnp.float32
bf16 = jnp.bfloat16
DP = ("line", "pair", "core")


MESH = pl.DeviceIdType.MESH


def nt(left, right):
    return lax.dot_general(left, right, (((1,), (1,)), ((), ())), preferred_element_type=f32)


def tn(left, right):
    return lax.dot_general(left, right, (((0,), (0,)), ((), ())), preferred_element_type=f32)


def nn(left, right):
    return jnp.dot(left, right, preferred_element_type=f32)


def greet(peers):
    barrier = pltpu.get_barrier_semaphore()
    for peer in peers:
        pl.semaphore_signal(barrier, inc=1, device_id=peer, device_id_type=MESH)
    pl.semaphore_wait(barrier, len(peers))


def remote(source, target, send, recv, peer):
    return pltpu.make_async_remote_copy(
        src_ref=source,
        dst_ref=target,
        send_sem=send,
        recv_sem=recv,
        device_id=peer,
        device_id_type=MESH,
    )


def ring_place(position, line):
    turned = position // line
    return position * (1 - turned) + (2 * line - 1 - position) * turned, turned


def start_kernel(line, ids, embed, all_ids, out, table, found, own, from_core, from_pair, from_line, *sems):
    ids_send, ids_recv, own_sem, core_send, core_recv, pair_send, pair_recv = sems[:7]
    line_send, line_recv, swap_send, swap_recv = sems[7:]
    me_section = lax.axis_index("section")
    me_line = lax.axis_index("line")
    me_pair = lax.axis_index("pair")
    me_core = lax.axis_index("core")
    section_peer = {"section": 1 - me_section}
    core_peer = {"core": 1 - me_core}
    pair_peer = {"pair": 1 - me_pair}
    peers = []
    for step in range(1, line * 4):
        peers.append(
            {
                "line": lax.rem(me_line + step // 4, line),
                "pair": lax.rem(me_pair + step // 2 % 2, 2),
                "core": lax.rem(me_core + step % 2, 2),
            }
        )
    greet(peers + [section_peer])
    place = all_ids.at[me_line, me_pair, me_core]
    copies = [remote(ids, place, ids_send.at[n], ids_recv.at[n], peer) for n, peer in enumerate(peers)]
    for copy in copies:
        copy.start()
    keep = pltpu.make_async_copy(ids, place, own_sem)
    keep.start()
    rows = embed.shape[0]
    high = table.shape[1]
    half = out.shape[-1]
    padded = jnp.concatenate(
        [embed[...].astype(f32), jnp.zeros((high - rows, embed.shape[1]), f32)], 0
    )
    table[...] = padded.T.astype(bf16)
    keep.wait()
    for copy in copies:
        copy.wait_recv()
    base = ((me_line * 2 + me_pair) * 2 + me_core) * rows

    def pick(spot, pair, core):
        wanted = all_ids[spot, pair, core, pl.ds(me_section, 1), :][:, :half]
        entry = lax.broadcasted_iota(jnp.int32, (high, half), 0)
        entry = jnp.where(entry < rows, entry + base, -1)
        hot = jnp.where(entry == wanted, 1.0, 0.0).astype(bf16)
        return nn(table[...], hot).astype(bf16)

    def core_copy(spot, pair, turn):
        return remote(
            found.at[turn, spot],
            from_core.at[turn, spot],
            core_send.at[turn, spot],
            core_recv.at[turn, spot],
            core_peer,
        )

    def pair_copy(spot):
        return remote(
            from_core.at[0, spot], from_pair.at[spot], pair_send.at[spot], pair_recv.at[spot], pair_peer
        )

    def line_copy(step):
        spot = lax.rem(me_line + step, line)
        return remote(
            from_core.at[1, spot],
            from_line.at[step - 1],
            line_send.at[step - 1],
            line_recv.at[step - 1],
            {"line": spot},
        )

    order = [lax.rem(me_line + step, line) for step in list(range(1, line)) + [0]]
    for turn, pair in enumerate((1 - me_pair, me_pair)):

        @pl.loop(0, line)
        def _(step):
            spot = lax.rem(me_line + 1 + step, line)
            found[turn, spot] = pick(spot, pair, 1 - me_core)
            core_copy(spot, pair, turn).start()
            own[turn, spot] = pick(spot, pair, me_core)

        if turn == 0:
            for spot in order:
                core_copy(spot, pair, 0).wait_recv()
                from_core[0, spot] = from_core[0, spot] + own[0, spot]
                pair_copy(spot).start()
    for step in list(range(1, line)) + [0]:
        spot = lax.rem(me_line + step, line)
        core_copy(spot, me_pair, 1).wait_recv()
        pair_copy(spot).wait_recv()
        from_core[1, spot] = from_core[1, spot] + own[1, spot] + from_pair[spot]
        if step:
            line_copy(step).start()
    total = from_core[1, me_line]
    for step in range(1, line):
        line_copy(step).wait_recv()
        total = total + from_line[step - 1]
    out[me_section] = total
    swap = remote(out.at[me_section], out.at[me_section], swap_send, swap_recv, section_peer)
    swap.start()
    for copy in copies:
        copy.wait_send()
    for spot in range(line):
        for turn in range(2):
            core_copy(spot, me_pair, turn).wait_send()
        pair_copy(spot).wait_send()
    for step in range(1, line):
        line_copy(step).wait_send()
    swap.wait()


def start_pass(ids, embed, half, line, collective_id):
    rows, width = embed.shape
    high = -(-rows // 256) * 256
    vmem = pl.BlockSpec(memory_space=pltpu.VMEM)
    dma = pltpu.SemaphoreType.DMA
    block = (width, half)
    return pl.pallas_call(
        partial(start_kernel, line),
        out_shape=[
            jax.ShapeDtypeStruct((line, 2, 2) + ids.shape, ids.dtype),
            jax.ShapeDtypeStruct((2,) + block, bf16),
        ],
        in_specs=[vmem, vmem],
        out_specs=[vmem, vmem],
        scratch_shapes=[
            pltpu.VMEM((width, high), bf16),
            pltpu.VMEM((2, line) + block, bf16),
            pltpu.VMEM((2, line) + block, bf16),
            pltpu.VMEM((2, line) + block, bf16),
            pltpu.VMEM((line,) + block, bf16),
            pltpu.VMEM((line - 1,) + block, bf16),
            dma((line * 4 - 1,)),
            dma((line * 4 - 1,)),
            dma,
            dma((2, line)),
            dma((2, line)),
            dma((line,)),
            dma((line,)),
            dma((line - 1,)),
            dma((line - 1,)),
            dma,
            dma,
        ],
        compiler_params=pltpu.CompilerParams(
            collective_id=collective_id, has_side_effects=True, vmem_limit_bytes=40 * 2**20
        ),
        cost_estimate=pl.CostEstimate(flops=0, bytes_accessed=2**27, transcendentals=0),
    )(ids, embed)


def head_kernel(line, head_rows, length, *refs):
    final, targets, *heads = refs[:6]
    out, grads, lse_out, pick_out = refs[6:10]
    (table, rows_all, logits, probs, acc, parts, from_pair, from_line, stats, done) = refs[10:20]
    (head_sem, own_sem, give_send, give_recv, along_send, along_recv, pair_send, pair_recv) = refs[20:28]
    (stat_send, stat_recv, sum_send, sum_recv, line_send, line_recv, back_send, back_recv) = refs[28:]
    half = final.shape[0] // 2
    width = 2 * half
    padded = heads[0].shape[0]
    me_section = lax.axis_index("section")
    me_line = lax.axis_index("line")
    me_pair = lax.axis_index("pair")
    me_core = lax.axis_index("core")
    section_peer = {"section": 1 - me_section}
    pair_peer = {"pair": 1 - me_pair}
    chip_peers = []
    for step in range(1, 2 * line):
        chip_peers.append(
            {"line": lax.rem(me_line + step // 2, line), "pair": lax.rem(me_pair + step % 2, 2)}
        )
    greet(chip_peers + [section_peer])

    def side(pair):
        return pl.ds(pl.multiple_of(pair * half, 16), half)

    loads = [
        pltpu.make_async_copy(part, table.at[pl.ds(n * padded, padded)], head_sem.at[n])
        for n, part in enumerate(heads)
    ]
    for load in loads:
        load.start()

    quarter = half // 2

    def token_rows(place, pair, chunk):
        first = place * width + pair * half + chunk * quarter
        return pl.ds(pl.multiple_of(first, 16), quarter)

    def group(place):
        return pl.ds(pl.multiple_of(place * width, 128), width)

    def column_block(place, chunk):
        return rows_all.at[token_rows(place, me_pair, chunk)]

    def give(chunk):
        return remote(
            final.at[pl.ds(chunk * quarter, quarter)],
            column_block(me_line, chunk),
            give_send.at[chunk],
            give_recv.at[chunk],
            section_peer,
        )

    def along(step, way, chunk):
        block = column_block(me_line - way * step, chunk)
        turn = (way + 1) // 2
        return remote(
            block,
            block,
            along_send.at[turn, step, chunk],
            along_recv.at[turn, step, chunk],
            {"line": me_line + way},
        )

    def inside(place):
        return (place >= 0) & (place < line)

    def sends_along(step, way):
        return inside(me_line - way * step) & inside(me_line + way)

    def sideways(place, chunk):
        block = column_block(place, chunk)
        return remote(
            block, block, pair_send.at[place, chunk], pair_recv.at[place, chunk], pair_peer
        )

    def arrived_sideways(place, chunk):
        block = rows_all.at[token_rows(place, 1 - me_pair, chunk)]
        return remote(
            block, block, pair_send.at[place, chunk], pair_recv.at[place, chunk], pair_peer
        )

    @pl.when(me_section == 1)
    def _():
        for chunk in range(2):
            give(chunk).start()
        for chunk in range(2):
            keep = pltpu.make_async_copy(
                final.at[pl.ds(half + chunk * quarter, quarter)],
                column_block(me_line, chunk),
                own_sem.at[chunk],
            )
            keep.start()
            keep.wait()

    for chunk in range(2):

        @pl.when(me_section == 0)
        def _():
            give(chunk).wait_recv()

        for way in (1, -1):

            @pl.when(sends_along(0, way))
            def _():
                along(0, way, chunk).start()

        sideways(me_line, chunk).start()

    def pass_on(step):
        for chunk in range(2):
            for way in (1, -1):
                place = me_line - way * step

                @pl.when(inside(place))
                def _():
                    block = column_block(place, chunk)
                    turn = (way + 1) // 2
                    remote(
                        block,
                        block,
                        along_send.at[turn, step - 1, chunk],
                        along_recv.at[turn, step - 1, chunk],
                        {"line": me_line - way},
                    ).wait_recv()

                    @pl.when(inside(me_line + way))
                    def _():
                        along(step, way, chunk).start()

                    sideways(place, chunk).start()

    nearest = []
    for own in range(line):
        near = [own]
        for step in range(1, line):
            near += [place for place in (own - step, own + step) if 0 <= place < line]
        nearest.append(near)

    def by_distance(turn):
        place = 0
        for own in range(line):
            for n in range(line):
                hit = ((me_line == own) & (turn == n)).astype(jnp.int32)
                place = place + hit * nearest[own][n]
        return place

    def vocabulary(tile, rows):
        shard = tile * rows // padded
        first = lax.rem(tile * rows, padded)
        shard_section = lax.rem(me_section + shard // 2, 2)
        shard_core = lax.rem(me_core + lax.rem(shard, 2), 2)
        base = (((shard_section * line + me_line) * 2 + me_pair) * 2 + shard_core) * head_rows
        row = lax.broadcasted_iota(jnp.int32, (rows, 1), 0) + first
        return jnp.where(row < head_rows, row + base, -1)

    tile_rows = 512
    tiles = 4 * padded // tile_rows
    lowest = -1e30

    def score(turn, tops):
        place = by_distance(turn) if turn < line else None
        before = by_distance(turn - 1) if turn > 0 else None
        wanted = None if place is None else targets[place]

        def one(tile, carry):
            rows = pl.ds(pl.multiple_of(tile * tile_rows, tile_rows), tile_rows)
            out = []
            if place is not None:
                top, pick = carry[:2]
                entry = vocabulary(tile, tile_rows)
                part = nt(table[rows, :], rows_all[group(place), :])
                part = jnp.where(entry >= 0, part, lowest)
                logits[turn % 2, rows, :] = part
                out.append(jnp.maximum(top, jnp.max(part, 0, keepdims=True)))
                out.append(
                    pick + jnp.sum(jnp.where(entry == wanted, part, 0.0), 0, keepdims=True)
                )
            if before is not None:
                value = jnp.exp(logits[(turn - 1) % 2, rows, :] - tops)
                probs[rows, group(before)] = value.astype(bf16)
                out.append(carry[-1] + jnp.sum(value, 0, keepdims=True))
            return tuple(out)

        none = jnp.zeros((1, width), f32)
        start = () if place is None else (jnp.full((1, width), lowest, f32), none)
        start += () if before is None else (none,)
        result = lax.fori_loop(0, tiles, one, start)
        if place is not None:
            pick_out[place] = result[1]
        if before is not None:
            own = stats.at[me_line, me_pair, before]
            own[:, 0:width] = tops
            own[:, width : 2 * width] = result[-1]
            for n in range(len(chip_peers)):
                stat_copy(n, before).start()
        return None if place is None else result[0]

    def stat_copy(n, place):
        own = stats.at[me_line, me_pair, place]
        return remote(own, own, stat_send.at[n, place], stat_recv.at[n, place], chip_peers[n])

    def stat_wait(n, place):
        peer = chip_peers[n]
        source_line = lax.rem(2 * me_line + line - peer["line"], line)
        source_pair = peer["pair"]
        block = stats.at[source_line, source_pair, place]
        remote(block, block, stat_send.at[n, place], stat_recv.at[n, place], peer).wait_recv()

    for load in loads:
        load.wait()

    tops = None
    for turn in range(line + 1):
        if turn + 1 < line:
            pass_on(turn + 1)
        if turn < line:
            for chunk in range(2):
                arrived_sideways(by_distance(turn), chunk).wait_recv()
        tops = score(turn, tops)

    def part_rows(pair, chunk):
        return pl.ds(pl.multiple_of(pair * half + chunk * quarter, 16), quarter)

    def sum_copy(turn, chunk):
        place = lax.rem(me_line + turn + 1, line)
        return remote(
            parts.at[place, part_rows(1 - me_pair, chunk)],
            from_pair.at[turn, pl.ds(chunk * quarter, quarter)],
            sum_send.at[turn, chunk],
            sum_recv.at[turn, chunk],
            pair_peer,
        )

    def line_copy(turn, chunk):
        place = lax.rem(me_line + turn + 1, line)
        return remote(
            parts.at[place, part_rows(me_pair, chunk)],
            from_line.at[turn, pl.ds(chunk * quarter, quarter)],
            line_send.at[turn, chunk],
            line_recv.at[turn, chunk],
            {"line": place},
        )

    def finish(turn, chunk):
        place = lax.rem(me_line + turn + 1, line)
        sum_copy(turn, chunk).wait_recv()
        own = parts.at[place, part_rows(me_pair, chunk)]
        other = from_pair.at[turn, pl.ds(chunk * quarter, quarter)]

        @pl.loop(0, quarter // 16)
        def _(block):
            rows = pl.ds(pl.multiple_of(block * 16, 16), 16)
            own[rows, :] = (own[rows, :].astype(f32) + other[rows, :].astype(f32)).astype(bf16)

    @pl.loop(0, line)
    def _(turn):
        place = lax.rem(me_line + turn + 1, line)
        for n in range(len(chip_peers)):
            stat_wait(n, place)
        tops = [stats[a, b, place, :, 0:width] for a in range(line) for b in range(2)]
        totals = [
            stats[a, b, place, :, width : 2 * width] for a in range(line) for b in range(2)
        ]
        top = tops[0]
        for value in tops[1:]:
            top = jnp.maximum(top, value)
        total = jnp.zeros_like(top)
        for peak, part in zip(tops, totals):
            total = total + part * jnp.exp(peak - top)
        lse = top + jnp.log(total)
        lse_out[place] = lse
        factor = jnp.exp(stats[me_line, me_pair, place, :, 0:width] - lse) / length
        wanted = targets[place]

        def scaled(tile):
            rows = pl.ds(tile * padded, padded)
            entry = vocabulary(tile, padded)
            grad = probs[rows, group(place)].astype(f32) * factor
            grad = (grad - jnp.where(entry == wanted, 1.0 / length, 0.0)).astype(bf16)
            probs[rows, group(place)] = grad
            return grad

        grad = scaled(0)
        for tile in range(4):
            product = tn(grad, table[pl.ds(tile * padded, padded), :])
            if tile < 3:
                grad = scaled(tile + 1)
                acc[...] = product if tile == 0 else acc[...] + product
            else:
                parts[place] = (acc[...] + product).astype(bf16)

        for chunk in range(2):
            sum_copy(turn, chunk).start()

        @pl.when(turn > 0)
        def _():
            for chunk in range(2):
                finish(turn - 1, chunk)
                line_copy(turn - 1, chunk).start()

    gh_rows = 256
    gh_tiles = 4 * padded // gh_rows

    def head_grads(first, last):
        @pl.loop(first, last)
        def _(tile):
            rows = pl.ds(pl.multiple_of(tile * gh_rows, gh_rows), gh_rows)
            value = jnp.dot(probs[rows, :], rows_all[...], preferred_element_type=f32)
            grads[rows, :] = value.astype(bf16)

    def back(chunk):
        part = pl.ds(chunk * quarter, quarter)
        return remote(
            done.at[part], out.at[part], back_send.at[chunk], back_recv.at[chunk], section_peer
        )

    head_grads(0, gh_tiles // 2)
    for chunk in range(2):
        finish(line - 1, chunk)
        for turn in range(line - 1):
            line_copy(turn, chunk).wait_recv()
        own = parts.at[me_line, part_rows(me_pair, chunk)]

        @pl.loop(0, quarter // 16)
        def _(block):
            rows = pl.ds(pl.multiple_of(block * 16, 16), 16)
            chunk_rows = pl.ds(pl.multiple_of(chunk * quarter + block * 16, 16), 16)
            value = own[rows, :].astype(f32)
            for turn in range(line - 1):
                value = value + from_line[turn, chunk_rows, :].astype(f32)
            done[chunk_rows, :] = value.astype(bf16)

        @pl.when(me_section == 0)
        def _():
            back(chunk).start()

    @pl.when(me_section == 0)
    def _():
        out[...] = jnp.zeros_like(out)

    @pl.when(me_section == 1)
    def _():
        out[pl.ds(half, half), :] = done[...]

    head_grads(gh_tiles // 2, gh_tiles)
    for chunk in range(2):

        @pl.when(me_section == 0)
        def _():
            back(chunk).wait_send()

        @pl.when(me_section == 1)
        def _():
            back(chunk).wait_recv()
            give(chunk).wait_send()

        for way in (1, -1):
            for step in range(line - 1):

                @pl.when(sends_along(step, way))
                def _():
                    along(step, way, chunk).wait_send()

        for place in range(line):
            sideways(place, chunk).wait_send()
        for turn in range(line):
            sum_copy(turn, chunk).wait_send()
        for turn in range(line - 1):
            line_copy(turn, chunk).wait_send()
    for place in range(line):
        for n in range(len(chip_peers)):
            stat_copy(n, place).wait_send()


def head_pass(final, targets, heads, line, head_rows, length, collective_id):
    tokens, deep = final.shape
    half = tokens // 2
    padded = heads[0].shape[0]
    vmem = pl.BlockSpec(memory_space=pltpu.VMEM)
    anywhere = pl.BlockSpec(memory_space=pl.ANY)
    dma = pltpu.SemaphoreType.DMA
    peers = 2 * line - 1
    return pl.pallas_call(
        partial(head_kernel, line, head_rows, length),
        out_shape=[
            jax.ShapeDtypeStruct((tokens, deep), bf16),
            jax.ShapeDtypeStruct((4 * padded, deep), bf16),
            jax.ShapeDtypeStruct((line, 1, tokens), f32),
            jax.ShapeDtypeStruct((line, 1, tokens), f32),
        ],
        in_specs=[vmem, vmem] + [anywhere] * 4,
        out_specs=[vmem] * 4,
        scratch_shapes=[
            pltpu.VMEM((4 * padded, deep), bf16),
            pltpu.VMEM((line * tokens, deep), bf16),
            pltpu.VMEM((2, 4 * padded, tokens), f32),
            pltpu.VMEM((4 * padded, line * tokens), bf16),
            pltpu.VMEM((tokens, deep), f32),
            pltpu.VMEM((line, tokens, deep), bf16),
            pltpu.VMEM((line, half, deep), bf16),
            pltpu.VMEM((line - 1, half, deep), bf16),
            pltpu.VMEM((line, 2, line, 1, 2 * tokens), f32),
            pltpu.VMEM((half, deep), bf16),
            dma((4,)),
            dma((2,)),
            dma((2,)),
            dma((2,)),
            dma((2, line, 2)),
            dma((2, line, 2)),
            dma((line, 2)),
            dma((line, 2)),
            dma((peers, line)),
            dma((peers, line)),
            dma((line, 2)),
            dma((line, 2)),
            dma((line, 2)),
            dma((line, 2)),
            dma((2,)),
            dma((2,)),
        ],
        compiler_params=pltpu.CompilerParams(
            collective_id=collective_id, has_side_effects=True, vmem_limit_bytes=60 * 2**20
        ),
        cost_estimate=pl.CostEstimate(
            flops=24 * line * padded * tokens * deep, bytes_accessed=2**28, transcendentals=0
        ),
    )(final, targets, *heads)


def row_stats(values):
    centred = values - jnp.mean(values, -1, keepdims=True)
    factor = lax.rsqrt(jnp.mean(centred * centred, -1, keepdims=True) + epsilon)
    return centred * factor, factor


def two_heads(block):
    first = lax.broadcasted_iota(jnp.int32, block.shape, 1) < HEAD_DIM
    zero = jnp.zeros_like(block)
    return jnp.concatenate([jnp.where(first, block, zero), jnp.where(first, zero, block)], 0)


def one_block(stacked):
    rows = stacked.shape[0] // 2
    first = lax.broadcasted_iota(jnp.int32, (rows, stacked.shape[1]), 1) < HEAD_DIM
    return jnp.where(first, stacked[:rows], stacked[rows:])


def attention_weights(queries, keys):
    scores = nt(keys, queries) * (1.0 / math.sqrt(HEAD_DIM))
    exped = jnp.exp(scores - jnp.max(scores, 0, keepdims=True))
    return exped * (1.0 / jnp.sum(exped, 0, keepdims=True))


def tile_of(index, size):
    return pl.ds(pl.multiple_of(index * size, size), size)


def forward_kernel(full, seqs, *refs):
    refs = list(refs)

    def take(number):
        return [refs.pop(0) for _ in range(number)]

    start, scale, bias = take(3)
    arrived, gain = take(2) if full else (None, None)
    weights = take(4)
    if full:
        out, final, x, joined, mixed, middle, entry_attn, entry_mlp, slope, hidden = take(10)
    else:
        (out,) = take(1)
        x = start
        joined, mixed, middle, entry_attn = take(4)
        entry_mlp = entry_attn
    w_qkv, w_out, w_up, w_down, total, sems = refs
    width = start.shape[1]
    length = start.shape[0] // seqs
    load_qkv, load_out, load_up, load_down = [
        pltpu.make_async_copy(source.at[0], target, sems.at[n])
        for n, (source, target) in enumerate(zip(weights, (w_qkv, w_out, w_up, w_down)))
    ]
    load_qkv.start()

    for seq in range(seqs):
        rows = pl.ds(seq * length, length)
        if full:
            first = (lax.axis_index("section") == 0).astype(f32)
            x[rows, :] = start[rows, :] * first + arrived[rows, :].astype(f32) * (1.0 - first)
        normed, _ = row_stats(x[rows, :])
        entry_attn[rows, :] = (normed * scale[seq, :, :width]).astype(bf16)

    load_qkv.wait()
    load_out.start()
    load_up.start()
    tile = 512

    @pl.loop(0, 3 * width // tile)
    def _(index):
        cols = tile_of(index, tile)
        joined[:, cols] = nn(entry_attn[...], w_qkv[:, cols]).astype(bf16)

    load_out.wait()
    load_down.start()
    pairs = width // 128

    @pl.loop(0, pairs)
    def _(pair):
        cols = tile_of(pair, 128)
        for seq in range(seqs):
            rows = pl.ds(seq * length, length)
            queries = two_heads(joined[rows, cols])
            keys = joined[rows, tile_of(pair + pairs, 128)]
            values = joined[rows, tile_of(pair + 2 * pairs, 128)]
            probs = attention_weights(queries, keys).astype(bf16)
            mixed[rows, cols] = one_block(tn(probs, values)).astype(bf16)

    @pl.loop(0, width // tile)
    def _(index):
        cols = tile_of(index, tile)
        middle[:, cols] = x[:, cols] + nn(mixed[...], w_out[:, cols])

    for seq in range(seqs):
        rows = pl.ds(seq * length, length)
        normed, _ = row_stats(middle[rows, :])
        entry_mlp[rows, :] = (normed * scale[seq, :, width:]).astype(bf16)

    load_up.wait()
    load_down.wait()
    total[...] = middle[...]

    def gelu_of(up, cols):
        below = 0.5 + 0.5 * lax.erf(up * math.sqrt(0.5))
        value = (up * below).astype(bf16)
        if full:
            density = jnp.exp(-0.5 * up * up) * (1.0 / math.sqrt(2.0 * math.pi))
            slope[:, cols] = (below + up * density).astype(bf16)
            hidden[:, cols] = value
        return value

    @pl.loop(0, w_up.shape[1] // (2 * tile))
    def _(index):
        sides = [tile_of(2 * index + side, tile) for side in range(2)]
        ups = [nn(entry_mlp[...], w_up[:, cols]) + bias[:, cols] for cols in sides]
        both = jnp.concatenate([gelu_of(up, cols) for up, cols in zip(ups, sides)], 1)
        total[...] += nn(both, w_down[tile_of(index, 2 * tile), :])

    for seq in range(seqs):
        rows = pl.ds(seq * length, length)
        value = total[rows, :].astype(bf16)
        out[rows, :] = value
        if full:
            normed, _ = row_stats(value.astype(f32))
            final[rows, :] = (normed * gain[...]).astype(bf16)


def layer_scratch(width, hidden):
    return [
        pltpu.VMEM((width, 3 * width), bf16),
        pltpu.VMEM((width, width), bf16),
        pltpu.VMEM((width, hidden), bf16),
        pltpu.VMEM((hidden, width), bf16),
    ]


def forward_pass(start, scale, weights, arrived=None, gain=None):
    w_qkv, w_out, w_up, b_hidden, w_down = weights
    tokens, width = start.shape
    wide = w_up.shape[-1]
    full = arrived is not None
    vmem = pl.BlockSpec(memory_space=pltpu.VMEM)
    anywhere = pl.BlockSpec(memory_space=pl.ANY)

    def low(columns):
        return (tokens, columns), bf16

    exact = ((tokens, width), f32)
    out_shape = [jax.ShapeDtypeStruct((tokens, width), bf16)]
    scratch = layer_scratch(width, wide)
    scratch += [pltpu.VMEM(*exact), pltpu.SemaphoreType.DMA((4,))]
    operands = [start, scale, b_hidden]
    if full:
        operands += [arrived, gain]
        kept = [low(width), exact, low(3 * width), low(width), exact, low(width), low(width)]
        out_shape += [jax.ShapeDtypeStruct(*item) for item in kept + [low(wide), low(wide)]]
    else:
        inside = [low(3 * width), low(width), exact, low(width)]
        scratch = [pltpu.VMEM(*item) for item in inside] + scratch
    flops = 2 * tokens * (4 * width * width + 2 * width * wide)
    return pl.pallas_call(
        partial(forward_kernel, full, scale.shape[0]),
        out_shape=out_shape,
        in_specs=[vmem] * len(operands) + [anywhere] * 4,
        out_specs=[vmem] * len(out_shape),
        scratch_shapes=scratch,
        compiler_params=pltpu.CompilerParams(vmem_limit_bytes=60 * 2**20),
        cost_estimate=pl.CostEstimate(flops=2 * flops, bytes_accessed=2**25, transcendentals=0),
    )(*operands, w_qkv, w_out, w_up, w_down)


def norm_grads(source, total, grad_middle, scale, grad_cond, half, seq, store):
    width = total.shape[1]
    length = total.shape[0] // scale.shape[0]
    rows = pl.ds(seq * length, length)
    cols = pl.ds(half * width, width)
    normed, factor = row_stats(source[rows, :])
    gradient = total[rows, :]
    if grad_cond is not None:
        grad_cond[seq, :, cols] = jnp.sum(gradient * normed, 0, keepdims=True)
    scaled = gradient * scale[seq, :, cols]
    back = factor * (
        scaled
        - jnp.mean(scaled, -1, keepdims=True)
        - normed * jnp.mean(scaled * normed, -1, keepdims=True)
    )
    store(rows, grad_middle[rows, :] + back)


def attention_grads(joined, grad_mixed, grad_joined, pair, seqs):
    pairs = grad_mixed.shape[1] // 128
    length = grad_mixed.shape[0] // seqs
    shrink = 1.0 / math.sqrt(HEAD_DIM)
    cols = tile_of(pair, 128)
    key_cols = tile_of(pair + pairs, 128)
    value_cols = tile_of(pair + 2 * pairs, 128)
    for seq in range(seqs):
        rows = pl.ds(seq * length, length)
        queries = two_heads(joined[rows, cols])
        keys = joined[rows, key_cols]
        probs = attention_weights(queries, keys)
        grads = two_heads(grad_mixed[rows, cols])
        grad_probs = nt(joined[rows, value_cols], grads)
        inner = jnp.sum(grad_probs * probs, 0, keepdims=True)
        grad_scores = (probs * (grad_probs - inner)).astype(bf16)
        grad_joined[rows, cols] = (one_block(tn(grad_scores, keys)) * shrink).astype(bf16)
        grad_joined[rows, key_cols] = (nn(grad_scores, queries) * shrink).astype(bf16)
        grad_joined[rows, value_cols] = nn(probs.astype(bf16), grads).astype(bf16)


def backward_kernel(begin, seqs, *refs):
    refs = list(refs)

    def take(number):
        return [refs.pop(0) for _ in range(number)]

    if begin:
        incoming, other, hidden, entry = take(4)
        far = take(3)
        grad_middle, total, grad_bias, down_out, up_out = take(5)
        grad_low, grad_up, entry_turned, down_weight, up_weight, out_sem = take(6)
        near = take(3)
    else:
        scale, incoming, other, gain = take(4)
        far = take(8)
        out, grad_top, grad_gain = take(3)
        grad_low, grad_up, grad_attn, grad_joined = take(4)
        near = take(8)
        total, grad_middle, grad_mixed = take(3)
    (sems,) = refs
    if begin:
        slope, w_up, w_down = near
        load_slope = pltpu.make_async_copy(far[0], slope, sems.at[0])
        load_up = pltpu.make_async_copy(far[1].at[0], w_up, sems.at[1])
        load_down = pltpu.make_async_copy(far[2].at[0], w_down, sems.at[2])
    else:
        slope, w_up, w_down, x, middle, joined, w_qkv, w_out = near
        load_slope = pltpu.make_async_copy(far[0], slope, sems.at[0])
        load_up = pltpu.make_async_copy(far[1].at[0], w_up, sems.at[1])
        load_down = pltpu.make_async_copy(far[2].at[0], w_down, sems.at[2])
        load_x = pltpu.make_async_copy(far[3], x, sems.at[3])
        load_middle = pltpu.make_async_copy(far[4], middle, sems.at[4])
        load_joined = pltpu.make_async_copy(far[5], joined, sems.at[5])
        load_qkv = pltpu.make_async_copy(far[6].at[0], w_qkv, sems.at[6])
        load_out = pltpu.make_async_copy(far[7].at[0], w_out, sems.at[7])
    width = incoming.shape[1]
    length = incoming.shape[0] // seqs
    load_down.start()
    load_slope.start()
    if begin:
        entry_turned[...] = entry[...].T

    for seq in range(seqs):
        rows = pl.ds(seq * length, length)
        if begin:
            first = (lax.axis_index("section") == 0).astype(f32)
            value = incoming[rows, :].astype(f32) * first + other[rows, :] * (1.0 - first)
        else:
            normed, factor = row_stats(other[rows, :].astype(f32))
            gradient = incoming[rows, :].astype(f32)
            part = jnp.sum(gradient * normed, 0, keepdims=True)
            grad_gain[...] = part if seq == 0 else grad_gain[...] + part
            scaled = gradient * gain[...]
            value = factor * (
                scaled
                - jnp.mean(scaled, -1, keepdims=True)
                - normed * jnp.mean(scaled * normed, -1, keepdims=True)
            )
            grad_top[rows, :] = value
        grad_middle[rows, :] = value
        grad_low[rows, :] = value.astype(bf16)

    load_down.wait()
    load_slope.wait()
    load_up.start()
    if not begin:
        load_middle.start()
        load_out.start()
        load_joined.start()
    tile = 1024

    @pl.loop(0, w_up.shape[1] // tile)
    def _(index):
        cols = tile_of(index, tile)
        grad_hidden = nt(grad_low[...], w_down[cols, :])
        value = (grad_hidden * slope[:, cols].astype(f32)).astype(bf16)
        grad_up[:, cols] = value
        if begin:
            grad_bias[:, cols] = jnp.sum(value.astype(f32), 0, keepdims=True)
            down_weight[cols, :] = tn(hidden[:, cols], grad_low[...]).astype(bf16)
            pltpu.make_async_copy(
                down_weight.at[cols], down_out.at[cols], out_sem.at[0, index]
            ).start()
            up_weight[:, cols] = nn(entry_turned[...], value).astype(bf16)

    if begin:
        whole_up = pltpu.make_async_copy(up_weight, up_out, out_sem.at[1, 0])
        whole_up.start()
    load_up.wait()
    if not begin:
        load_middle.wait()
        load_out.wait()
        load_joined.wait()
        load_qkv.start()
        load_x.start()

    @pl.loop(0, width // 256)
    def _(index):
        total[:, tile_of(index, 256)] = nt(grad_up[...], w_up[tile_of(index, 256), :])

    if begin:
        for index in range(w_up.shape[1] // tile):
            cols = pl.ds(index * tile, tile)
            pltpu.make_async_copy(
                down_weight.at[cols], down_out.at[cols], out_sem.at[0, index]
            ).wait()
        whole_up.wait()
        return

    def store_middle(rows, value):
        grad_middle[rows, :] = value
        grad_attn[rows, :] = value.astype(bf16)

    for seq in range(seqs):
        norm_grads(middle, total, grad_middle, scale, None, 1, seq, store_middle)

    @pl.loop(0, width // 512)
    def _(index):
        part = tile_of(index, 512)
        grad_mixed[:, part] = nt(grad_attn[...], w_out[part, :]).astype(bf16)

    @pl.loop(0, width // 128)
    def _(pair):
        attention_grads(joined, grad_mixed, grad_joined, pair, seqs)

    load_qkv.wait()
    load_x.wait()

    @pl.loop(0, width // 256)
    def _(index):
        total[:, tile_of(index, 256)] = nt(grad_joined[...], w_qkv[tile_of(index, 256), :])

    def store_out(rows, value):
        out[rows, :] = value.astype(bf16)

    for seq in range(seqs):
        norm_grads(x, total, grad_middle, scale, None, 0, seq, store_out)


def backward_pass(grad_final, block_out, gain, scale, kept, weights):
    w_qkv, w_out, w_up, _, w_down = weights
    x, joined, _, middle, _, _, slope, _ = kept
    tokens, width = x.shape
    wide = w_up.shape[-1]
    vmem = pl.BlockSpec(memory_space=pltpu.VMEM)
    anywhere = pl.BlockSpec(memory_space=pl.ANY)
    exact = ((tokens, width), f32)
    low = ((tokens, width), bf16)
    lows = [low, ((tokens, wide), bf16), low, ((tokens, 3 * width), bf16)]
    near = [
        ((tokens, wide), bf16),
        ((width, wide), bf16),
        ((wide, width), bf16),
        exact,
        exact,
        ((tokens, 3 * width), bf16),
        ((width, 3 * width), bf16),
        ((width, width), bf16),
    ]
    flops = 4 * tokens * (4 * width * width + 2 * width * wide)
    return pl.pallas_call(
        partial(backward_kernel, False, scale.shape[0]),
        out_shape=[jax.ShapeDtypeStruct(*item) for item in [low, exact, ((1, width), f32)]],
        in_specs=[vmem] * 4 + [anywhere] * 8,
        out_specs=[vmem] * 3,
        scratch_shapes=[pltpu.VMEM(*item) for item in lows + near + [exact, exact, low]]
        + [pltpu.SemaphoreType.DMA((8,))],
        compiler_params=pltpu.CompilerParams(vmem_limit_bytes=60 * 2**20),
        cost_estimate=pl.CostEstimate(flops=flops, bytes_accessed=2**25, transcendentals=0),
    )(scale, grad_final, block_out, gain, slope, w_up, w_down, x, middle, joined, w_qkv, w_out)


def backward_begin(returned, grad_top, seqs, hidden, entry, slope, w_up, w_down):
    tokens, width = grad_top.shape
    wide = w_up.shape[-1]
    vmem = pl.BlockSpec(memory_space=pltpu.VMEM)
    anywhere = pl.BlockSpec(memory_space=pl.ANY)
    exact = ((tokens, width), f32)
    low = ((tokens, width), bf16)
    wide_low = ((tokens, wide), bf16)
    up, down = ((width, wide), bf16), ((wide, width), bf16)
    results = [exact, exact, ((1, wide), f32), down, up]
    inside = [low, wide_low, ((width, tokens), bf16), down, up]
    return pl.pallas_call(
        partial(backward_kernel, True, seqs),
        out_shape=[jax.ShapeDtypeStruct(*item) for item in results],
        in_specs=[vmem] * 4 + [anywhere] * 3,
        out_specs=[vmem] * 3 + [anywhere] * 2,
        scratch_shapes=[pltpu.VMEM(*item) for item in inside]
        + [pltpu.SemaphoreType.DMA((2, wide // 1024))]
        + [pltpu.VMEM(*item) for item in (wide_low, up, down)]
        + [pltpu.SemaphoreType.DMA((3,))],
        compiler_params=pltpu.CompilerParams(vmem_limit_bytes=60 * 2**20),
        cost_estimate=pl.CostEstimate(
            flops=16 * tokens * width * wide, bytes_accessed=2**25, transcendentals=0
        ),
    )(returned, grad_top, hidden, entry, slope, w_up, w_down)


def tail_kernel(line, seqs, lag, *refs):
    refs = list(refs)

    def take(number):
        return [refs.pop(0) for _ in range(number)]

    scale, rest, factor_one, factor_two, embedded, noisy, w_in = take(7)
    far = take(9)
    parts = take(2)
    (head_part,) = take(1)
    outs = take(5)
    head_out, smalls, rows_all = take(3)
    near = take(9)
    grad_attn, grad_mixed, grad_joined, grad_first, grad_cond, in_weight = take(6)
    rows_own, small_wide, small_own = take(3)
    own, from_core, slots = take(2), take(5), take(5)
    head_own, head_core, head_section, last_total = take(4)
    far_sem, load_sem, core_send, core_recv, ring_send, ring_recv, credit = take(7)
    keep_sem, packet_send, packet_recv, wide_send, wide_recv, rows_send, rows_recv = take(7)
    head_sem, head_send, head_recv, cross_send, cross_recv = take(5)
    grad_middle, grad_entry, middle, x, joined, mixed, entry_attn, w_out, w_qkv = near
    inside = [w_qkv, w_out, in_weight]
    groups = ((0, 1), (2, 3, 4))
    chips = 2 * line
    width = x.shape[1]
    me_section = lax.axis_index("section")
    me_line = lax.axis_index("line")
    me_pair = lax.axis_index("pair")
    me_core = lax.axis_index("core")
    position = me_line + me_pair * (chips - 1 - 2 * me_line)
    section_peer = {"section": 1 - me_section}
    core_peer = {"core": 1 - me_core}
    ways = (1, -1)
    ring_peers = []
    for way in ways:
        peer_line, peer_pair = ring_place(lax.rem(position + way + chips, chips), line)
        ring_peers.append({"line": peer_line, "pair": peer_pair})
    greet([core_peer, section_peer] + ring_peers)

    shapes = [ref.shape[-2:] for ref in from_core]

    def block_of(turn, step):
        ahead = lax.rem(position - ways[turn] * (1 + step) + 2 * chips, chips)
        return ring_place(ahead, line)

    def columns(index, turn):
        wide = shapes[index][-1] // 2
        return pl.ds(turn * wide, wide)

    def block_rows(index, place, pair, core):
        high = shapes[index][0]
        return pl.ds(pl.multiple_of(((place * 2 + pair) * 2 + core) * high, 16), high)

    def source(index, turn, step, core):
        place, pair = block_of(turn, step)
        cols = columns(index, turn)
        if index < 2:
            return parts[index].at[place, pair, core, :, cols]
        return inside[index - 2].at[block_rows(index, place, pair, core), cols]

    def load(index, turn, step):
        return pltpu.make_async_copy(
            source(index, turn, step, me_core),
            own[index].at[step % 2, :, columns(index, turn)],
            load_sem.at[index, turn, step],
        )

    def core_copy(index, turn, step):
        return remote(
            source(index, turn, step, 1 - me_core),
            from_core[index].at[step % 3, :, columns(index, turn)],
            core_send.at[index, turn, step],
            core_recv.at[index, turn, step],
            core_peer,
        )

    def ring_copy(index, turn, step):
        cols = columns(index, turn)
        passed = from_core[index].at[0, :, cols] if step == 0 else slots[index].at[step - 1, :, cols]
        return remote(
            passed,
            slots[index].at[step, :, cols],
            ring_send.at[index, turn, step],
            ring_recv.at[index, turn, step],
            ring_peers[turn],
        )

    def to_core(group, step):
        if step >= 3:
            pl.semaphore_wait(credit.at[group], 1)
        for index in groups[group]:
            for turn in range(2):
                if index < 2:
                    load(index, turn, step).start()
                core_copy(index, turn, step).start()

    def stop(group, step, between):
        first, last = step == 0, step == chips - 1
        for index in groups[group]:
            rows, wide = shapes[index][0], shapes[index][1] // 2
            tile = min(wide, 512)
            for turn in range(2):
                if index < 2:
                    load(index, turn, step).wait()
                core_copy(index, turn, step).wait_recv()
                if not first:
                    ring_copy(index, turn, step - 1).wait_recv()
                place, pair = block_of(turn, step)

                @pl.loop(0, rows // 16)
                def _(block):
                    row = pl.ds(pl.multiple_of(block * 16, 16), 16)
                    if index >= 2:
                        base = ((place * 2 + pair) * 2 + me_core) * rows + block * 16
                        own_row = pl.ds(pl.multiple_of(base, 16), 16)
                    for col in range(turn * wide, (turn + 1) * wide, tile):
                        cols = pl.ds(col, tile)
                        if index < 2:
                            mine = own[index][step % 2, row, cols]
                        else:
                            mine = inside[index - 2][own_row, cols]
                        total = from_core[index][step % 3, row, cols].astype(f32)
                        total = total + mine.astype(f32)
                        if not first:
                            total = total + slots[index][step - 1, row, cols].astype(f32)
                        if last and index == 4:
                            last_total[row, cols] = total
                        elif last:
                            outs[index][row, cols] = total.astype(bf16)
                        elif first:
                            from_core[index][0, row, cols] = total.astype(bf16)
                        else:
                            slots[index][step - 1, row, cols] = total.astype(bf16)

                if not last:
                    ring_copy(index, turn, step).start()
                between()
        if step == 1:
            for index in groups[group]:
                for turn in range(2):
                    ring_copy(index, turn, 0).wait_send()
        if 1 <= step <= 4:
            amount = 2 if step == 1 else 1
            pl.semaphore_signal(
                credit.at[group], inc=amount, device_id=core_peer, device_id_type=MESH
            )

    hops = (line, line - 1)

    def packet_blocks(place, pair):
        return [smalls.at[place, pair, me_core], rows_all.at[place, pair, me_core]]

    def packet_hops(turn, hop, away):
        place, pair = ring_place(
            lax.rem(position - ways[turn] * (hop + away) + 2 * chips, chips), line
        )
        return [
            remote(
                block,
                block,
                packet_send.at[n, turn, hop],
                packet_recv.at[n, turn, hop],
                ring_peers[turn],
            )
            for n, block in enumerate(packet_blocks(place, pair))
        ]

    def pass_packets(hop):
        for turn in range(2):
            if 0 < hop <= hops[turn]:
                for copy in packet_hops(turn, hop - 1, 1):
                    copy.wait_recv()
            if hop < hops[turn]:
                for copy in packet_hops(turn, hop, 0):
                    copy.start()

    small_slot, rows_slot = packet_blocks(me_line, me_pair)
    keep_small = pltpu.make_async_copy(small_own, small_slot, keep_sem.at[0])
    keep_rows = pltpu.make_async_copy(rows_own, rows_slot, keep_sem.at[1])
    rows_over = remote(rows_own, rows_slot, rows_send, rows_recv, section_peer)
    across = [
        remote(block, block, wide_send.at[n], wide_recv.at[n], core_peer)
        for n, block in enumerate([smalls.at[:, :, me_core], rows_all.at[:, :, me_core]])
    ]
    def packets_ready():
        keep_small.wait()

        @pl.when(me_section == 0)
        def _():
            keep_rows.wait()

        @pl.when(me_section == 1)
        def _():
            rows_over.wait_recv()

    high = head_part.shape[0] // 4

    def shard(n):
        return head_part.at[pl.ds(n * high, high)]

    head_loads = [
        pltpu.make_async_copy(shard(2 * n), head_own.at[n], head_sem.at[n]) for n in range(2)
    ]
    head_copies = [
        remote(shard(2 * n + 1), head_core.at[n], head_send.at[n], head_recv.at[n], core_peer)
        for n in range(2)
    ]
    head_copies.append(
        remote(head_core.at[1], head_section, head_send.at[2], head_recv.at[2], section_peer)
    )

    def head_over_cores():
        for copy in head_loads:
            copy.wait()
        for copy in head_copies[:2]:
            copy.wait_recv()

        @pl.loop(0, high // 16)
        def _(block):
            rows = pl.ds(pl.multiple_of(block * 16, 16), 16)
            value = head_core[1, rows, :].astype(f32) + head_own[1, rows, :].astype(f32)
            head_core[1, rows, :] = value.astype(bf16)

        head_copies[2].start()

    def head_over_sections():
        head_copies[2].wait_recv()

        @pl.loop(0, high // 16)
        def _(block):
            rows = pl.ds(pl.multiple_of(block * 16, 16), 16)
            value = head_core[0, rows, :].astype(f32) + head_own[0, rows, :].astype(f32)
            value = value + head_section[rows, :].astype(f32)
            head_out[rows, :] = value.astype(bf16)

    far_copies = []
    for n, (where, target) in enumerate(zip(far, near)):
        where = where.at[0] if n >= 7 else where
        far_copies.append(pltpu.make_async_copy(where, target, far_sem.at[n]))

    def waits(*numbers):
        for n in numbers:
            far_copies[n].wait()

    def store_middle(rows, value):
        grad_middle[rows, :] = value
        grad_attn[rows, :] = value.astype(bf16)

    def store_first(rows, value):
        grad_first[rows, :] = value.astype(bf16)

    def second_norm(seq):
        if seq == 0:
            waits(0, 1, 2)
        norm_grads(middle, grad_entry, grad_middle, scale, grad_cond, 1, seq, store_middle)

    def mixed_grads(index):
        if index == 0:
            waits(7)
        part = pl.ds(index * 512, 512)
        grad_mixed[:, part] = nt(grad_attn[...], w_out[part, :]).astype(bf16)

    def heads_grads(pair):
        if pair == 0:
            waits(4)
        attention_grads(joined, grad_mixed, grad_joined, pair, seqs)

    def entry_grads(index):
        if index == 0:
            waits(8)
        part = pl.ds(index * 256, 256)
        grad_entry[:, part] = nt(grad_joined[...], w_qkv[part, :])

    def first_norm(seq):
        if seq == 0:
            waits(3)
        norm_grads(x, grad_entry, grad_middle, scale, grad_cond, 0, seq, store_first)

    def embedding_rows(_):
        grad_noisy = nt(grad_first[...], w_in[...])
        inner = jnp.mean(grad_noisy * embedded[...], -1, keepdims=True)
        value = factor_one[...] * grad_noisy - factor_two[...] * embedded[...] * inner
        rows_own[...] = value.astype(bf16)

        @pl.when(me_section == 0)
        def _():
            keep_rows.start()
            rows_over.start()

    def small_rows(_):
        each = small_wide.shape[1]
        for seq in range(seqs):
            for n in range(2 * width // each):
                row = pl.ds(seq * (2 * width // each) + n, 1)
                small_wide[row, :] = grad_cond[seq, :, pl.ds(n * each, each)]
        small_wide[pl.ds(seqs * 2 * width // each, rest.shape[0]), :] = rest[...]
        small_own[...] = small_wide[...].astype(bf16)
        keep_small.start()

    def input_weight(_):
        in_weight[...] = tn(noisy[...], grad_first[...]).astype(bf16)

    def qkv_weight(index):
        if index == 0:
            waits(6)
        part = pl.ds(index * 256, 256)
        w_qkv[part, :] = tn(entry_attn[:, part], grad_joined[...]).astype(bf16)

    def out_weight(index):
        if index == 0:
            waits(5)
        part = pl.ds(index * 512, 512)
        w_out[part, :] = tn(mixed[:, part], grad_attn[...]).astype(bf16)

    steps = []
    for step, number in (
        (second_norm, seqs),
        (mixed_grads, width // 512),
        (heads_grads, width // 128),
        (entry_grads, width // 256),
        (first_norm, seqs),
        (embedding_rows, 1),
        (small_rows, 1),
        (input_weight, 1),
        (qkv_weight, width // 256),
        (out_weight, width // 512),
    ):
        steps += [partial(step, n) for n in range(number)]
    at_once = -(-len(steps) // (4 * lag))

    def work():
        for _ in range(at_once):
            if steps:
                steps.pop(0)()

    def nothing():
        pass

    to_core(0, 0)
    to_core(0, 1)
    for copy in far_copies:
        copy.start()
    stop(0, 0, work)
    for turn in range(1, chips + lag):
        if turn + 1 < chips:
            to_core(0, turn + 1)
        if turn == 1:
            for copy in head_loads + head_copies[:2]:
                copy.start()
        if turn == lag:
            to_core(1, 0)
        if lag <= turn and turn - lag + 1 < chips:
            to_core(1, turn - lag + 1)
        if turn < chips:
            stop(0, turn, work if turn < lag else nothing)
        if turn >= lag:
            stop(1, turn - lag, nothing)
        hop = turn - lag - 2
        if hop == 0:
            packets_ready()
        if 0 <= hop <= line:
            pass_packets(hop)
        if hop == line:
            for copy in across:
                copy.start()
        if turn == 3:
            head_over_cores()
        if turn == chips + lag - 2:
            head_over_sections()
    each = outs[4].shape[0]
    give = remote(last_total.at[pl.ds(each, each)], outs[4], cross_send, cross_recv, section_peer)

    @pl.when(me_section == 0)
    def _():
        give.start()
        outs[4][...] = last_total[pl.ds(0, each), :]

    for copy in across:
        copy.wait()
    for copy in head_copies:
        copy.wait_send()
    for turn in range(2):
        for hop in range(hops[turn]):
            for copy in packet_hops(turn, hop, 0):
                copy.wait_send()
    for index in range(5):
        for turn in range(2):
            for step in range(chips):
                core_copy(index, turn, step).wait_send()
                if 0 < step < chips - 1:
                    ring_copy(index, turn, step).wait_send()

    @pl.when(me_section == 0)
    def _():
        rows_over.wait_send()
        give.wait_send()

    @pl.when(me_section == 1)
    def _():
        give.wait_recv()


def tail_pass(scale, rest, factors, embedded, noisy, w_in, far, parts, head_part, collective_id):
    grad_middle = far[0]
    tokens, width = grad_middle.shape
    seqs = scale.shape[0]
    line = parts[0].shape[0]
    chips = 2 * line
    count = 4 * line
    emb_width = noisy.shape[1]
    vmem = pl.BlockSpec(memory_space=pltpu.VMEM)
    anywhere = pl.BlockSpec(memory_space=pl.ANY)
    dma = pltpu.SemaphoreType.DMA
    shapes = [part.shape[-2:] for part in parts]
    shapes += [
        (width // count, 3 * width),
        (width // count, width),
        (emb_width // count, width),
    ]
    each = shapes[4][0] // 2
    high = head_part.shape[0] // 4
    small = (seqs * 2 * width // emb_width + rest.shape[0], emb_width)
    exact = ((tokens, width), f32)
    low = ((tokens, width), bf16)
    three = ((tokens, 3 * width), bf16)
    rows = (tokens, emb_width)
    results = [(shape, bf16) for shape in shapes[:4]]
    results += [((each, width), f32), ((high, width), bf16)]
    results += [((line, 2, 2) + small, bf16), ((line, 2, 2) + rows, bf16)]
    room = [exact, exact, exact, exact, three, low, low]
    room += [((width, width), bf16), ((width, 3 * width), bf16)]
    room += [low, low, three, low, ((seqs, 1, 2 * width), f32), ((emb_width, width), bf16)]
    room += [(rows, bf16), (small, f32), (small, bf16)]
    room += [((2,) + shape, bf16) for shape in shapes[:2]]
    room += [((3,) + shape, bf16) for shape in shapes]
    room += [((chips - 1,) + shape, bf16) for shape in shapes]
    room += [((2, high, width), bf16), ((2, high, width), bf16), ((high, width), bf16)]
    room += [(shapes[4], f32)]
    scratch = [pltpu.VMEM(*item) for item in room]
    scratch += [dma((9,)), dma((2, 2, chips)), dma((5, 2, chips)), dma((5, 2, chips))]
    scratch += [dma((5, 2, chips - 1)), dma((5, 2, chips - 1)), pltpu.SemaphoreType.REGULAR((2,))]
    scratch += [dma((2,)), dma((2, 2, line)), dma((2, 2, line)), dma((2,)), dma((2,)), dma, dma]
    scratch += [dma((2,)), dma((3,)), dma((3,)), dma, dma]
    return pl.pallas_call(
        partial(tail_kernel, line, seqs, line),
        out_shape=[jax.ShapeDtypeStruct(*item) for item in results],
        in_specs=[vmem] * 7 + [anywhere] * 12,
        out_specs=[vmem] * 6 + [anywhere] * 2,
        scratch_shapes=scratch,
        compiler_params=pltpu.CompilerParams(
            collective_id=collective_id, has_side_effects=True, vmem_limit_bytes=62 * 2**20
        ),
        cost_estimate=pl.CostEstimate(flops=0, bytes_accessed=2**29, transcendentals=0),
    )(scale, rest, *factors, embedded, noisy, w_in, *far, *parts, head_part)


def finish_kernel(line, head_rows, *refs):
    ids, rows, *lows = refs[:7]
    *exacts, grad_embed, total = refs[7:]
    me_section = lax.axis_index("section")
    me_line = lax.axis_index("line")
    me_pair = lax.axis_index("pair")
    me_core = lax.axis_index("core")
    high = total.shape[0]
    base = (((me_section * line + me_line) * 2 + me_pair) * 2 + me_core) * grad_embed.shape[0]
    tile = 768
    for index in range(rows.shape[0] // tile):
        part = pl.ds(index * tile, tile)
        entry = lax.broadcasted_iota(jnp.int32, (high, tile), 0) + base
        place = jnp.where(entry == ids[:, part], 1.0, 0.0).astype(bf16)
        product = nn(place, rows[part, :])
        total[...] = product if index == 0 else total[...] + product
    grad_embed[...] = total[pl.ds(0, grad_embed.shape[0]), :]
    for low, exact in zip(lows, exacts):
        whole = exact.shape[0] // 16
        left = exact.shape[0] % 16

        @pl.loop(0, whole)
        def _(block):
            part = pl.ds(pl.multiple_of(block * 16, 16), 16)
            exact[part, :] = low[part, :].astype(f32)

        if left:
            value = low[pl.ds(whole * 16, 16), :].astype(f32)
            exact[pl.ds(whole * 16, left), :] = value[:left]


def finish(ids, rows, lows, line, head_rows, out_rows):
    vmem = pl.BlockSpec(memory_space=pltpu.VMEM)
    shapes = [low.shape for low in lows[:-1]] + [(head_rows, lows[-1].shape[1])]
    shapes.append((out_rows, rows.shape[1]))
    return pl.pallas_call(
        partial(finish_kernel, line, head_rows),
        out_shape=[jax.ShapeDtypeStruct(shape, f32) for shape in shapes],
        in_specs=[vmem] * 7,
        out_specs=[vmem] * 6,
        scratch_shapes=[pltpu.VMEM((-(-out_rows // 16) * 16, rows.shape[1]), f32)],
        compiler_params=pltpu.CompilerParams(vmem_limit_bytes=60 * 2**20),
        cost_estimate=pl.CostEstimate(
            flops=2 * out_rows * rows.size, bytes_accessed=2**24, transcendentals=0
        ),
    )(ids, rows, *lows)


def norm_rows(values):
    centred = values - jnp.mean(values, -1, keepdims=True)
    factor = lax.rsqrt(jnp.mean(centred * centred, -1, keepdims=True) + epsilon)
    return (centred * factor, factor)


def norm_back(gradient, normed, factor):
    return factor * (
        gradient
        - jnp.mean(gradient, -1, keepdims=True)
        - normed * jnp.mean(gradient * normed, -1, keepdims=True)
    )


def time_features(noise_level):
    half_width = TFEAT // 2
    rates = jnp.exp(jnp.arange(half_width, dtype=f32) * (math.log(1000.0) / half_width))
    angles = (jnp.log(noise_level) / 4.0)[:, None] * rates[None, :]
    return jnp.concatenate([jnp.cos(angles), jnp.sin(angles)], -1)


def levels_of(bins, table):
    hits = bins[:, None] == jnp.arange(table.shape[0])[None, :]
    return jnp.sum(jnp.where(hits, table[None, :], 0.0), -1)


def over_dp(part):
    part = part.reshape((part.shape[0] // 4, 2, 2) + part.shape[1:])
    part = lax.psum_scatter(part, "core", scatter_dimension=2)
    part = lax.psum_scatter(part, "pair", scatter_dimension=1)
    return lax.psum_scatter(part, "line", scatter_dimension=0)


def by_owner(part):
    line = lax.axis_size("line")
    return part.astype(bf16).reshape((line, 2, 2, part.shape[0] // (line * 4)) + part.shape[1:])


def mm(spec, left, right):
    return jnp.einsum(spec, left, right, preferred_element_type=f32)


def layer_forward(stream, scale_attn, scale_mlp, weights):
    w_qkv, w_out, w_up, b_hidden, w_down = weights
    seq_count, length, model_width = stream.shape
    normed_attn, factor_attn = norm_rows(stream)
    attn_entry = (normed_attn * scale_attn).astype(bf16)
    joined = mm("nsd,de->nse", attn_entry, w_qkv).astype(bf16)
    qkv_parts = joined.reshape(seq_count, length, 3, HEADS, HEAD_DIM)
    query_rows = qkv_parts[:, :, 0]
    key_rows = qkv_parts[:, :, 1]
    value_rows = qkv_parts[:, :, 2]
    scores = mm("nqhe,nkhe->nhqk", query_rows, key_rows) / math.sqrt(HEAD_DIM)
    exp_scores = jnp.exp(scores - jnp.max(scores, -1, keepdims=True))
    attn_probs = exp_scores / jnp.sum(exp_scores, -1, keepdims=True)
    probs_low = attn_probs.astype(bf16)
    attn_mixed = mm("nhqk,nkhe->nqhe", probs_low, value_rows).astype(bf16)
    attn_mixed = attn_mixed.reshape(seq_count, length, model_width)
    middle = stream + mm("nsd,de->nse", attn_mixed, w_out)
    normed_mlp, factor_mlp = norm_rows(middle)
    mlp_entry = (normed_mlp * scale_mlp).astype(bf16)
    up_proj = mm("nsd,df->nsf", mlp_entry, w_up) + b_hidden
    below = 0.5 + 0.5 * lax.erf(up_proj * math.sqrt(0.5))
    hidden = (up_proj * below).astype(bf16)
    density = jnp.exp(-0.5 * up_proj * up_proj) * (1.0 / math.sqrt(2.0 * math.pi))
    slope = (below + up_proj * density).astype(bf16)
    block_out = middle + mm("nsf,fd->nsd", hidden, w_down)
    kept = (
        normed_attn,
        factor_attn,
        attn_entry,
        query_rows,
        key_rows,
        value_rows,
        attn_probs,
        probs_low,
        attn_mixed,
        normed_mlp,
        factor_mlp,
        mlp_entry,
        slope,
        hidden,
    )
    return (block_out, kept)


def layer_backward(grad_out, kept, scale_attn, scale_mlp, weights, whole):
    w_qkv, w_out, w_up, b_hidden, w_down = weights
    (
        normed_attn,
        factor_attn,
        attn_entry,
        query_rows,
        key_rows,
        value_rows,
        attn_probs,
        probs_low,
        attn_mixed,
        normed_mlp,
        factor_mlp,
        mlp_entry,
        slope,
        hidden,
    ) = kept
    seq_count, length, model_width = grad_out.shape
    grads = {}
    grad_branch = grad_out.astype(bf16)
    if whole:
        grads["down"] = by_owner(mm("nsf,nsd->fd", hidden, grad_branch))
    grad_hidden = mm("nsd,fd->nsf", grad_branch, w_down)
    grad_up_proj = (grad_hidden * slope.astype(f32)).astype(bf16)
    if whole:
        grads["bias"] = jnp.sum(grad_up_proj.astype(f32), (0, 1))
        grads["up"] = by_owner(mm("nsd,nsf->df", mlp_entry, grad_up_proj))
    grad_entry = mm("nsf,df->nsd", grad_up_proj, w_up)
    grad_middle = grad_out + norm_back(grad_entry * scale_mlp, normed_mlp, factor_mlp)
    grad_attn = grad_middle.astype(bf16)
    if whole:
        grads["out"] = by_owner(mm("nsd,nse->de", attn_mixed, grad_attn))
    grad_mixed = mm("nse,de->nsd", grad_attn, w_out)
    grad_mixed = grad_mixed.astype(bf16).reshape(seq_count, length, HEADS, HEAD_DIM)
    grad_probs = mm("nqhe,nkhe->nhqk", grad_mixed, value_rows)
    grad_values = mm("nhqk,nqhe->nkhe", probs_low, grad_mixed)
    grad_scores = (
        attn_probs * (grad_probs - jnp.sum(grad_probs * attn_probs, -1, keepdims=True))
    ).astype(bf16)
    grad_query = mm("nhqk,nkhe->nqhe", grad_scores, key_rows) / math.sqrt(HEAD_DIM)
    grad_keys = mm("nhqk,nqhe->nkhe", grad_scores, query_rows) / math.sqrt(HEAD_DIM)
    grad_joined = jnp.stack([grad_query, grad_keys, grad_values], 2).astype(bf16)
    grad_joined = grad_joined.reshape(seq_count, length, 3 * model_width)
    if whole:
        grads["qkv"] = by_owner(mm("nsd,nse->de", attn_entry, grad_joined))
    grad_attn_entry = mm("nse,de->nsd", grad_joined, w_qkv)
    grad_stream = grad_middle + norm_back(grad_attn_entry * scale_attn, normed_attn, factor_attn)
    if whole:
        grads["cond"] = jnp.concatenate(
            [jnp.sum(grad_attn_entry * normed_attn, 1), jnp.sum(grad_entry * normed_mlp, 1)], -1
        )
    return (grad_stream, grads)


def local(
    token_ids,
    target_ids,
    time_bins,
    sigma_table,
    noise,
    embed,
    w_in,
    w_time,
    norm_gain,
    w_qkv,
    w_out,
    w_up,
    b_hidden,
    w_down,
    out_gain,
    head,
):
    section = lax.axis_index("section")
    line_at = lax.axis_index("line")
    pair_at = lax.axis_index("pair")
    core = lax.axis_index("core")
    sections = lax.axis_size("section")
    line = lax.axis_size("line")
    chip = line_at * 2 + pair_at
    chips = line * 2
    cores = 2
    dp_count = chips * cores
    dp_index = chip * cores + core
    is_first = section == 0
    seqs, length = token_ids.shape
    tokens = seqs * length
    half = tokens // sections
    model_width = w_out.shape[-1]
    emb_rows, emb_width = embed.shape
    straight = line <= 4 and half % 16 == 0 and model_width // dp_count % 16 == 0

    if straight:
        lanes = -(-half // 128) * 128
        blocks = [part.reshape(2, half) for part in (token_ids, target_ids)]
        blocks.append(jnp.pad(time_bins[None, :], ((0, 0), (0, half - seqs))))
        own_ids = jnp.pad(jnp.concatenate(blocks, 0), ((0, 3), (0, lanes - half)))
        all_ids, embedded = start_pass(own_ids, embed, half, line, 0)
        all_ids = all_ids.reshape(dp_count, 8, lanes)
        all_tokens = all_ids[:, 0:2, :half].reshape(dp_count, tokens)
        all_targets = all_ids[:, 2:4, :half].reshape(dp_count, tokens)
        all_bins = all_ids[:, 4, :seqs].reshape(-1)
        embedded = embedded.swapaxes(1, 2)
    else:
        own_ids = jnp.concatenate([token_ids.reshape(-1), target_ids.reshape(-1), time_bins])
        all_ids = lax.all_gather(own_ids, DP)
        all_tokens = all_ids[:, :tokens]
        all_targets = all_ids[:, tokens : 2 * tokens]
        all_bins = all_ids[:, 2 * tokens :].reshape(-1)
        own_rows = dp_index * emb_rows + jnp.arange(emb_rows)
        half_tokens = lax.dynamic_slice_in_dim(all_tokens, section * half, half, 1)
        picked = (half_tokens.reshape(-1)[:, None] == own_rows[None, :]).astype(bf16)
        found = jnp.dot(picked, embed, preferred_element_type=f32).astype(bf16)
        embedded = lax.all_gather(over_dp(found.reshape(dp_count, half, emb_width)), "section")
    embedded = embedded.astype(f32).reshape(seqs, length, emb_width)

    head_rows = head.shape[0]
    swapped = [(0, 1), (1, 0)]
    if straight:
        head_own = jnp.pad(head, ((0, -head_rows % 512), (0, 0)))
        head_section = lax.ppermute(head_own, "section", swapped)
    else:
        head_group = lax.all_gather(lax.all_gather(head, "core"), "section")
        head_group = head_group.reshape(-1, model_width)
        vocab_base = (
            (jnp.arange(sections)[:, None] * chips + chip) * cores + jnp.arange(cores)[None, :]
        ) * head_rows
        columns = (vocab_base[:, :, None] + jnp.arange(head_rows)[None, None, :]).reshape(-1)

    noise_level = levels_of(time_bins, sigma_table)
    unit_factor = lax.rsqrt(jnp.mean(embedded * embedded, -1, keepdims=True) + epsilon)
    level_col = noise_level[:, None, None]
    noise_scale = lax.rsqrt(level_col * level_col + 1.0)
    noisy_rows = ((embedded * unit_factor + level_col * noise) * noise_scale).astype(bf16)
    time_feats = time_features(noise_level)
    conditioned = jnp.dot(time_feats, w_time[0].astype(f32), precision=highest) + norm_gain[0]
    scale_attn = conditioned[:, None, :model_width]
    scale_mlp = conditioned[:, None, model_width:]
    scale = conditioned[:, None, :]
    weights = (w_qkv[0], w_out[0], w_up[0], b_hidden[0], w_down[0])
    stacked = (w_qkv, w_out, w_up, b_hidden, w_down)
    if straight:
        noisy_rows, head_own, head_section = lax.optimization_barrier(
            (noisy_rows, head_own, head_section)
        )
        heads = [head_own, lax.ppermute(head_own, "core", swapped)]
        heads += [head_section, lax.ppermute(head_section, "core", swapped)]

    stream0 = mm("nse,ed->nsd", noisy_rows, w_in)
    flat = (tokens, model_width)
    if straight:
        start = stream0.reshape(flat)
        (first_out,) = forward_pass(start, scale, stacked)
        arrived = lax.ppermute(first_out, "section", swapped)
        block_out, final_rows, *kept = forward_pass(
            start, scale, stacked, arrived, out_gain[None, :]
        )
    else:
        first_out = layer_forward(stream0, scale_attn, scale_mlp, weights)[0].astype(bf16)
        arrived = lax.ppermute(first_out, "section", swapped)
        stream = jnp.where(is_first, stream0, arrived.astype(f32))
        block_out, kept = layer_forward(stream, scale_attn, scale_mlp, weights)
        final_normed, final_factor = norm_rows(block_out.astype(bf16).astype(f32))
        final_rows = (final_normed * out_gain).astype(bf16).reshape(flat)

    targets_group = lax.dynamic_slice_in_dim(
        all_targets.reshape(chips, cores, tokens), core, 1, 1
    )[:, 0]
    targets_group = lax.dynamic_slice_in_dim(targets_group, section * half, half, 1)
    if straight:
        grad_final, grad_head, lse, picks = head_pass(
            final_rows, targets_group.reshape(line, 1, tokens), heads, line, head_rows, length, 3
        )
        ce_part = jnp.sum(lse) / chips - jnp.sum(picks)
    else:
        targets_group = targets_group.reshape(-1)
        handed = lax.ppermute(final_rows[:half], "section", [(1, 0), (0, 1)])
        own_final = jnp.where(is_first, handed, final_rows[half:])
        group_final = lax.all_gather(own_final, ("line", "pair"), tiled=True)
        logits = mm("td,vd->tv", group_final, head_group)
        local_top = jnp.max(logits, -1)
        local_total = jnp.sum(jnp.exp(logits - local_top[:, None]), -1)
        mark = columns[None, :] == targets_group[:, None]
        local_pick = jnp.sum(jnp.where(mark, logits, 0.0))
        stats = lax.all_gather(jnp.stack([local_top, local_total]), ("line", "pair"))
        all_top = jnp.max(stats[:, 0], 0)
        all_total = jnp.sum(stats[:, 1] * jnp.exp(stats[:, 0] - all_top), 0)
        log_total = all_top + jnp.log(all_total)
        soft_rows = jnp.exp(logits - log_total[:, None])
        logit_grads = ((soft_rows - jnp.where(mark, 1.0, 0.0)) / length).astype(bf16)
        grad_final = jnp.dot(logit_grads, head_group, preferred_element_type=f32).astype(bf16)
        grad_final = lax.psum_scatter(grad_final, ("line", "pair"), scatter_dimension=0, tiled=True)
        handed = lax.ppermute(grad_final, "section", swapped)
        grad_final = jnp.concatenate([handed, grad_final], 0)
        grad_head = mm("tv,td->vd", logit_grads, group_final).astype(bf16)
        grad_head = grad_head.reshape(sections, cores, head_rows, model_width)
        grad_head = lax.psum_scatter(grad_head, "core", scatter_dimension=1)
        grad_head = lax.psum_scatter(grad_head, "section", scatter_dimension=0).astype(f32)

        ce_part = jnp.sum(log_total) / chips - local_pick
    if straight:
        grad_second, grad_top, out_part = backward_pass(
            grad_final, block_out, out_gain[None, :], scale, kept, stacked
        )
        returned = lax.ppermute(grad_second, "section", swapped)
        out_part = out_part.reshape(-1)
        x, joined, mixed, middle, entry_attn, entry_mlp, slope, hidden = kept
        grad_middle, grad_entry, grad_bias, down_part, up_part = backward_begin(
            returned, grad_top, seqs, hidden, entry_mlp, slope, w_up, w_down
        )
        parts = [by_owner(down_part), by_owner(up_part)]
        grad_bias = grad_bias.reshape(-1)
    else:
        grad_final = grad_final.astype(f32).reshape(stream0.shape)
        out_part = jnp.sum(grad_final * final_normed, (0, 1))
        grad_top = norm_back(grad_final * out_gain, final_normed, final_factor)
        grad_second = layer_backward(grad_top, kept, scale_attn, scale_mlp, weights, False)[0]
        returned = lax.ppermute(grad_second.astype(bf16), "section", swapped)
        grad_cot = jnp.where(is_first, returned.astype(f32), grad_top)
        grad_stream, grads = layer_backward(grad_cot, kept, scale_attn, scale_mlp, weights, True)
        grad_first = grad_stream.astype(bf16)
    out_part = jnp.where(is_first, 0.0, out_part)

    ce_high = ce_part.astype(bf16).astype(f32)
    ce_mid = (ce_part - ce_high).astype(bf16).astype(f32)
    ce_low = ce_part - ce_high - ce_mid
    shared = jnp.concatenate([out_part, jnp.stack([ce_high, ce_mid, ce_low])])
    shared_rows = -(-shared.shape[0] // emb_width)
    shared = jnp.pad(shared, (0, shared_rows * emb_width - shared.shape[0]))
    shared = shared.reshape(-1, emb_width).astype(bf16)
    both = [shared, lax.ppermute(shared, "section", swapped)]

    cubed = unit_factor * unit_factor * unit_factor
    cond_rows = seqs * 2 * model_width // emb_width
    bias_rows = b_hidden.shape[1] // emb_width
    if straight:
        rest = jnp.concatenate([grad_bias.reshape(-1, emb_width)] + both, 0).astype(f32)
        rest = jnp.pad(rest, ((0, -(cond_rows + rest.shape[0]) % 16), (0, 0)))
        factors = [
            (value * noise_scale).reshape(tokens, 1) for value in (unit_factor, cubed)
        ]
        owned = noisy_rows.reshape(tokens, sections, dp_count, -1)
        owned = owned.swapaxes(1, 2).reshape(tokens, emb_width)
        far = [grad_middle, grad_entry, middle, x, joined, mixed, entry_attn, w_out, w_qkv]
        grad_down, grad_up, grad_qkv, grad_wout, grad_w_in, grad_head, smalls, rows_all = tail_pass(
            scale,
            rest,
            factors,
            embedded.reshape(tokens, emb_width),
            owned,
            w_in,
            far,
            parts,
            grad_head,
            2,
        )
        ids = all_tokens.reshape(1, -1)
        grad_down, grad_up, grad_qkv, grad_wout, grad_head, grad_embed = finish(
            ids,
            rows_all.reshape(-1, emb_width),
            [grad_down, grad_up, grad_qkv, grad_wout, grad_head],
            line,
            head_rows,
            emb_rows // sections,
        )
    else:
        in_part = mm("nse,nsd->ed", noisy_rows, grad_first).astype(bf16)
        in_part = in_part.reshape(sections, dp_count, -1, model_width).swapaxes(0, 1)
        in_sum = over_dp(in_part).astype(f32)
        in_handed = lax.ppermute(in_sum[1], "section", swapped)
        grad_w_in = jnp.where(is_first, in_sum[0], in_handed)
        grad_noisy = mm("nsd,ed->nse", grad_first, w_in)
        grad_unit = grad_noisy * noise_scale
        grad_embedded = unit_factor * grad_unit - cubed * embedded * jnp.mean(
            grad_unit * embedded, -1, keepdims=True
        )
        grad_flat = grad_embedded.reshape(tokens, emb_width).astype(bf16)
        handed = lax.ppermute(grad_flat, "section", swapped)
        rows_all = lax.all_gather(jnp.where(is_first, grad_flat, handed), DP)
        small = [grads["cond"].reshape(-1, emb_width), grads["bias"].reshape(-1, emb_width)]
        smalls = lax.all_gather(
            jnp.concatenate([value.astype(bf16) for value in small] + both, 0), DP
        )
        grad_down, grad_up, grad_qkv, grad_wout = [
            over_dp(part.reshape((dp_count,) + part.shape[3:])).astype(f32)
            for part in (grads["down"], grads["up"], grads["qkv"], grads["out"])
        ]
        grad_all = rows_all.reshape(-1, emb_width)
        out_rows = emb_rows // sections
        target_rows = (section * dp_count + dp_index) * out_rows + jnp.arange(out_rows)
        place = (target_rows[:, None] == all_tokens.reshape(-1)[None, :]).astype(bf16)
        grad_embed = jnp.dot(place, grad_all, preferred_element_type=f32)

    smalls = smalls.reshape(dp_count, -1, emb_width).astype(f32)
    cond_all = smalls[:, :cond_rows].reshape(dp_count * seqs, 2 * model_width)
    bias_all = smalls[:, cond_rows : cond_rows + bias_rows].reshape(dp_count, -1)
    hidden_rows = bias_all.shape[1] // dp_count
    grad_bias = jnp.sum(
        lax.dynamic_slice_in_dim(bias_all, dp_index * hidden_rows, hidden_rows, 1), 0
    )
    norm_cols = 2 * model_width // dp_count
    grad_gain = jnp.sum(lax.dynamic_slice_in_dim(cond_all, dp_index * norm_cols, norm_cols, 1), 0)
    feats_all = time_features(levels_of(all_bins, sigma_table))
    feat_rows = TFEAT // dp_count
    feats_own = lax.dynamic_slice_in_dim(feats_all, dp_index * feat_rows, feat_rows, 1)
    grad_time = jnp.dot(feats_own.T, cond_all, precision=highest)
    shared_first = cond_rows + bias_rows
    both = smalls[:, shared_first : shared_first + 2 * shared_rows]
    both = jnp.sum(both.reshape(dp_count, 2, -1), (0, 1))
    loss = jnp.sum(both[model_width : model_width + 3]) / (tokens * dp_count)
    gain_rows = model_width // dp_count
    grad_out_gain = lax.dynamic_slice_in_dim(both, dp_index * gain_rows, gain_rows)
    return (
        loss,
        grad_embed,
        grad_w_in,
        grad_time[None],
        grad_gain[None],
        grad_qkv[None],
        grad_wout[None],
        grad_up[None],
        grad_bias[None],
        grad_down[None],
        grad_out_gain,
        grad_head,
    )


def solution(mesh):
    sections, dp_count = mesh.shape["section"], mesh.shape["dp"]
    fine = Mesh(mesh.devices.reshape(sections, dp_count // 4, 2, 2), ("section",) + DP)
    everywhere = ("section",) + DP
    in_specs = (
        P(DP, None),
        P(DP, None),
        P(DP),
        P(),
        P(DP, None, None),
        P(DP, None),
        P(),
        P("section", None, None),
        P("section", None),
        P("section", None, None),
        P("section", None, None),
        P("section", None, None),
        P("section", None),
        P("section", None, None),
        P(),
        P(everywhere, None),
    )
    out_specs = (
        P(),
        P(everywhere, None),
        P(everywhere, None),
        P("section", DP, None),
        P("section", DP),
        P("section", DP, None),
        P("section", DP, None),
        P("section", DP, None),
        P("section", DP),
        P("section", DP, None),
        P(DP),
        P(everywhere, None),
    )
    return jax.shard_map(local, mesh=fine, in_specs=in_specs, out_specs=out_specs, check_vma=False)
```

```python
from functools import partial
import math

import jax
import jax.numpy as jnp
from jax import lax
from jax.experimental import pallas as pl
from jax.experimental.pallas import tpu as pltpu
from jax.sharding import Mesh, PartitionSpec as P

HEADS = 16
HEAD_DIM = 64
TFEAT = 256

epsilon = 1e-05
highest = lax.Precision.HIGHEST
f32 = jnp.float32
bf16 = jnp.bfloat16
DP = ("line", "pair", "core")


MESH = pl.DeviceIdType.MESH


def nt(left, right):
    return lax.dot_general(left, right, (((1,), (1,)), ((), ())), preferred_element_type=f32)


def tn(left, right):
    return lax.dot_general(left, right, (((0,), (0,)), ((), ())), preferred_element_type=f32)


def nn(left, right):
    return jnp.dot(left, right, preferred_element_type=f32)


def greet(peers):
    barrier = pltpu.get_barrier_semaphore()
    for peer in peers:
        pl.semaphore_signal(barrier, inc=1, device_id=peer, device_id_type=MESH)
    pl.semaphore_wait(barrier, len(peers))


def remote(source, target, send, recv, peer):
    return pltpu.make_async_remote_copy(
        src_ref=source,
        dst_ref=target,
        send_sem=send,
        recv_sem=recv,
        device_id=peer,
        device_id_type=MESH,
    )


def ring_place(position, line):
    turned = position // line
    return position * (1 - turned) + (2 * line - 1 - position) * turned, turned


def start_kernel(line, ids, embed, all_ids, out, table, found, own, from_core, from_pair, from_line, *sems):
    ids_send, ids_recv, own_sem, core_send, core_recv, pair_send, pair_recv = sems[:7]
    line_send, line_recv, swap_send, swap_recv = sems[7:]
    me_section = lax.axis_index("section")
    me_line = lax.axis_index("line")
    me_pair = lax.axis_index("pair")
    me_core = lax.axis_index("core")
    section_peer = {"section": 1 - me_section}
    core_peer = {"core": 1 - me_core}
    pair_peer = {"pair": 1 - me_pair}
    peers = []
    for step in range(1, line * 4):
        peers.append(
            {
                "line": lax.rem(me_line + step // 4, line),
                "pair": lax.rem(me_pair + step // 2 % 2, 2),
                "core": lax.rem(me_core + step % 2, 2),
            }
        )
    greet(peers + [section_peer])
    place = all_ids.at[me_line, me_pair, me_core]
    copies = [remote(ids, place, ids_send.at[n], ids_recv.at[n], peer) for n, peer in enumerate(peers)]
    for copy in copies:
        copy.start()
    keep = pltpu.make_async_copy(ids, place, own_sem)
    keep.start()
    rows = embed.shape[0]
    high = table.shape[1]
    half = out.shape[-1]
    padded = jnp.concatenate(
        [embed[...].astype(f32), jnp.zeros((high - rows, embed.shape[1]), f32)], 0
    )
    table[...] = padded.T.astype(bf16)
    keep.wait()
    for copy in copies:
        copy.wait_recv()
    base = ((me_line * 2 + me_pair) * 2 + me_core) * rows

    def pick(spot, pair, core):
        wanted = all_ids[spot, pair, core, pl.ds(me_section, 1), :][:, :half]
        entry = lax.broadcasted_iota(jnp.int32, (high, half), 0)
        entry = jnp.where(entry < rows, entry + base, -1)
        hot = jnp.where(entry == wanted, 1.0, 0.0).astype(bf16)
        return nn(table[...], hot).astype(bf16)

    def core_copy(spot, pair, turn):
        return remote(
            found.at[turn, spot],
            from_core.at[turn, spot],
            core_send.at[turn, spot],
            core_recv.at[turn, spot],
            core_peer,
        )

    def pair_copy(spot):
        return remote(
            from_core.at[0, spot], from_pair.at[spot], pair_send.at[spot], pair_recv.at[spot], pair_peer
        )

    def line_copy(step):
        spot = lax.rem(me_line + step, line)
        return remote(
            from_core.at[1, spot],
            from_line.at[step - 1],
            line_send.at[step - 1],
            line_recv.at[step - 1],
            {"line": spot},
        )

    order = [lax.rem(me_line + step, line) for step in list(range(1, line)) + [0]]
    for turn, pair in enumerate((1 - me_pair, me_pair)):

        @pl.loop(0, line)
        def _(step):
            spot = lax.rem(me_line + 1 + step, line)
            found[turn, spot] = pick(spot, pair, 1 - me_core)
            core_copy(spot, pair, turn).start()
            own[turn, spot] = pick(spot, pair, me_core)

        if turn == 0:
            for spot in order:
                core_copy(spot, pair, 0).wait_recv()
                from_core[0, spot] = from_core[0, spot] + own[0, spot]
                pair_copy(spot).start()
    for step in list(range(1, line)) + [0]:
        spot = lax.rem(me_line + step, line)
        core_copy(spot, me_pair, 1).wait_recv()
        pair_copy(spot).wait_recv()
        from_core[1, spot] = from_core[1, spot] + own[1, spot] + from_pair[spot]
        if step:
            line_copy(step).start()
    total = from_core[1, me_line]
    for step in range(1, line):
        line_copy(step).wait_recv()
        total = total + from_line[step - 1]
    out[me_section] = total
    swap = remote(out.at[me_section], out.at[me_section], swap_send, swap_recv, section_peer)
    swap.start()
    for copy in copies:
        copy.wait_send()
    for spot in range(line):
        for turn in range(2):
            core_copy(spot, me_pair, turn).wait_send()
        pair_copy(spot).wait_send()
    for step in range(1, line):
        line_copy(step).wait_send()
    swap.wait()


def start_pass(ids, embed, half, line, collective_id):
    rows, width = embed.shape
    high = -(-rows // 256) * 256
    vmem = pl.BlockSpec(memory_space=pltpu.VMEM)
    dma = pltpu.SemaphoreType.DMA
    block = (width, half)
    return pl.pallas_call(
        partial(start_kernel, line),
        out_shape=[
            jax.ShapeDtypeStruct((line, 2, 2) + ids.shape, ids.dtype),
            jax.ShapeDtypeStruct((2,) + block, bf16),
        ],
        in_specs=[vmem, vmem],
        out_specs=[vmem, vmem],
        scratch_shapes=[
            pltpu.VMEM((width, high), bf16),
            pltpu.VMEM((2, line) + block, bf16),
            pltpu.VMEM((2, line) + block, bf16),
            pltpu.VMEM((2, line) + block, bf16),
            pltpu.VMEM((line,) + block, bf16),
            pltpu.VMEM((line - 1,) + block, bf16),
            dma((line * 4 - 1,)),
            dma((line * 4 - 1,)),
            dma,
            dma((2, line)),
            dma((2, line)),
            dma((line,)),
            dma((line,)),
            dma((line - 1,)),
            dma((line - 1,)),
            dma,
            dma,
        ],
        compiler_params=pltpu.CompilerParams(
            collective_id=collective_id, has_side_effects=True, vmem_limit_bytes=40 * 2**20
        ),
        cost_estimate=pl.CostEstimate(flops=0, bytes_accessed=2**27, transcendentals=0),
    )(ids, embed)


def head_kernel(line, head_rows, length, *refs):
    final, targets, *heads = refs[:7]
    out, grads, lse_out, pick_out = refs[7:11]
    (table, rows_all, logits, probs, acc, parts, from_pair, from_line, stats, done) = refs[11:21]
    (head_sem, own_sem, give_send, give_recv, along_send, along_recv, pair_send, pair_recv) = refs[21:29]
    (stat_send, stat_recv, sum_send, sum_recv, line_send, line_recv, back_send, back_recv) = refs[29:37]
    last_send, last_recv = refs[37:]
    half = final.shape[0] // 2
    width = 2 * half
    padded = heads[0].shape[0]
    me_section = lax.axis_index("section")
    me_line = lax.axis_index("line")
    me_pair = lax.axis_index("pair")
    me_core = lax.axis_index("core")
    section_peer = {"section": 1 - me_section}
    pair_peer = {"pair": 1 - me_pair}
    chip_peers = []
    for step in range(1, 2 * line):
        chip_peers.append(
            {"line": lax.rem(me_line + step // 2, line), "pair": lax.rem(me_pair + step % 2, 2)}
        )
    greet(chip_peers + [section_peer, {"core": 1 - me_core}])

    def side(pair):
        return pl.ds(pl.multiple_of(pair * half, 16), half)

    loads = []
    for n, part in enumerate(heads):
        first = sum(other.shape[0] for other in heads[:n])
        target = table.at[pl.ds(first, part.shape[0])]
        loads.append(pltpu.make_async_copy(part, target, head_sem.at[n]))
    late = heads[3]
    last = remote(
        late,
        table.at[pl.ds(4 * padded - late.shape[0], late.shape[0])],
        last_send,
        last_recv,
        {"core": 1 - me_core},
    )
    last.start()
    for load in loads:
        load.start()

    quarter = half // 2

    def token_rows(place, pair, chunk):
        first = place * width + pair * half + chunk * quarter
        return pl.ds(pl.multiple_of(first, 16), quarter)

    def group(place):
        return pl.ds(pl.multiple_of(place * width, 128), width)

    def column_block(place, chunk):
        return rows_all.at[token_rows(place, me_pair, chunk)]

    def give(chunk):
        return remote(
            final.at[pl.ds(chunk * quarter, quarter)],
            column_block(me_line, chunk),
            give_send.at[chunk],
            give_recv.at[chunk],
            section_peer,
        )

    def along(step, way, chunk):
        block = column_block(me_line - way * step, chunk)
        turn = (way + 1) // 2
        return remote(
            block,
            block,
            along_send.at[turn, step, chunk],
            along_recv.at[turn, step, chunk],
            {"line": me_line + way},
        )

    def inside(place):
        return (place >= 0) & (place < line)

    def sends_along(step, way):
        return inside(me_line - way * step) & inside(me_line + way)

    def sideways(place, chunk):
        block = column_block(place, chunk)
        return remote(
            block, block, pair_send.at[place, chunk], pair_recv.at[place, chunk], pair_peer
        )

    def arrived_sideways(place, chunk):
        block = rows_all.at[token_rows(place, 1 - me_pair, chunk)]
        return remote(
            block, block, pair_send.at[place, chunk], pair_recv.at[place, chunk], pair_peer
        )

    @pl.when(me_section == 1)
    def _():
        for chunk in range(2):
            give(chunk).start()
        for chunk in range(2):
            keep = pltpu.make_async_copy(
                final.at[pl.ds(half + chunk * quarter, quarter)],
                column_block(me_line, chunk),
                own_sem.at[chunk],
            )
            keep.start()
            keep.wait()

    for chunk in range(2):

        @pl.when(me_section == 0)
        def _():
            give(chunk).wait_recv()

        for way in (1, -1):

            @pl.when(sends_along(0, way))
            def _():
                along(0, way, chunk).start()

        sideways(me_line, chunk).start()

    def pass_on(step):
        for chunk in range(2):
            for way in (1, -1):
                place = me_line - way * step

                @pl.when(inside(place))
                def _():
                    block = column_block(place, chunk)
                    turn = (way + 1) // 2
                    remote(
                        block,
                        block,
                        along_send.at[turn, step - 1, chunk],
                        along_recv.at[turn, step - 1, chunk],
                        {"line": me_line - way},
                    ).wait_recv()

                    @pl.when(inside(me_line + way))
                    def _():
                        along(step, way, chunk).start()

                    sideways(place, chunk).start()

    nearest = []
    for own in range(line):
        near = [own]
        for step in range(1, line):
            near += [place for place in (own - step, own + step) if 0 <= place < line]
        nearest.append(near)

    def by_distance(turn):
        place = 0
        for own in range(line):
            for n in range(line):
                hit = ((me_line == own) & (turn == n)).astype(jnp.int32)
                place = place + hit * nearest[own][n]
        return place

    def vocabulary(tile, rows):
        shard = tile * rows // padded
        first = lax.rem(tile * rows, padded)
        shard_section = lax.rem(me_section + shard // 2, 2)
        shard_core = lax.rem(me_core + lax.rem(shard, 2), 2)
        base = (((shard_section * line + me_line) * 2 + me_pair) * 2 + shard_core) * head_rows
        row = lax.broadcasted_iota(jnp.int32, (rows, 1), 0) + first
        return jnp.where(row < head_rows, row + base, -1)

    tile_rows = 512
    tiles = 4 * padded // tile_rows
    lowest = -1e30

    def score(turn, tops):
        place = by_distance(turn) if turn < line else None
        before = by_distance(turn - 1) if turn > 0 else None
        wanted = None if place is None else targets[place]

        def one(tile, carry):
            rows = pl.ds(pl.multiple_of(tile * tile_rows, tile_rows), tile_rows)
            out = []
            if place is not None:
                top, pick = carry[:2]
                entry = vocabulary(tile, tile_rows)
                part = nt(table[rows, :], rows_all[group(place), :])
                part = jnp.where(entry >= 0, part, lowest)
                logits[turn % 2, rows, :] = part
                out.append(jnp.maximum(top, jnp.max(part, 0, keepdims=True)))
                out.append(
                    pick + jnp.sum(jnp.where(entry == wanted, part, 0.0), 0, keepdims=True)
                )
            if before is not None:
                value = jnp.exp(logits[(turn - 1) % 2, rows, :] - tops)
                probs[rows, group(before)] = value.astype(bf16)
                out.append(carry[-1] + jnp.sum(value, 0, keepdims=True))
            return tuple(out)

        none = jnp.zeros((1, width), f32)
        start = () if place is None else (jnp.full((1, width), lowest, f32), none)
        start += () if before is None else (none,)
        result = lax.fori_loop(0, tiles, one, start)
        if place is not None:
            pick_out[place] = result[1]
        if before is not None:
            own = stats.at[me_line, me_pair, before]
            own[:, 0:width] = tops
            own[:, width : 2 * width] = result[-1]
            for n in range(len(chip_peers)):
                stat_copy(n, before).start()
        return None if place is None else result[0]

    def stat_copy(n, place):
        own = stats.at[me_line, me_pair, place]
        return remote(own, own, stat_send.at[n, place], stat_recv.at[n, place], chip_peers[n])

    def stat_wait(n, place):
        peer = chip_peers[n]
        source_line = lax.rem(2 * me_line + line - peer["line"], line)
        source_pair = peer["pair"]
        block = stats.at[source_line, source_pair, place]
        remote(block, block, stat_send.at[n, place], stat_recv.at[n, place], peer).wait_recv()

    for load in loads:
        load.wait()
    last.wait()

    tops = None
    for turn in range(line + 1):
        if turn + 1 < line:
            pass_on(turn + 1)
        if turn < line:
            for chunk in range(2):
                arrived_sideways(by_distance(turn), chunk).wait_recv()
        tops = score(turn, tops)

    def part_rows(pair, chunk):
        return pl.ds(pl.multiple_of(pair * half + chunk * quarter, 16), quarter)

    def sum_copy(turn, chunk):
        place = lax.rem(me_line + turn + 1, line)
        return remote(
            parts.at[place, part_rows(1 - me_pair, chunk)],
            from_pair.at[turn, pl.ds(chunk * quarter, quarter)],
            sum_send.at[turn, chunk],
            sum_recv.at[turn, chunk],
            pair_peer,
        )

    def line_copy(turn, chunk):
        place = lax.rem(me_line + turn + 1, line)
        return remote(
            parts.at[place, part_rows(me_pair, chunk)],
            from_line.at[turn, pl.ds(chunk * quarter, quarter)],
            line_send.at[turn, chunk],
            line_recv.at[turn, chunk],
            {"line": place},
        )

    def finish(turn, chunk):
        place = lax.rem(me_line + turn + 1, line)
        sum_copy(turn, chunk).wait_recv()
        own = parts.at[place, part_rows(me_pair, chunk)]
        other = from_pair.at[turn, pl.ds(chunk * quarter, quarter)]

        @pl.loop(0, quarter // 16)
        def _(block):
            rows = pl.ds(pl.multiple_of(block * 16, 16), 16)
            own[rows, :] = (own[rows, :].astype(f32) + other[rows, :].astype(f32)).astype(bf16)

    @pl.loop(0, line)
    def _(turn):
        place = lax.rem(me_line + turn + 1, line)
        for n in range(len(chip_peers)):
            stat_wait(n, place)
        tops = [stats[a, b, place, :, 0:width] for a in range(line) for b in range(2)]
        totals = [
            stats[a, b, place, :, width : 2 * width] for a in range(line) for b in range(2)
        ]
        top = tops[0]
        for value in tops[1:]:
            top = jnp.maximum(top, value)
        total = jnp.zeros_like(top)
        for peak, part in zip(tops, totals):
            total = total + part * jnp.exp(peak - top)
        lse = top + jnp.log(total)
        lse_out[place] = lse
        factor = jnp.exp(stats[me_line, me_pair, place, :, 0:width] - lse) / length
        wanted = targets[place]

        def scaled(tile):
            rows = pl.ds(tile * padded, padded)
            entry = vocabulary(tile, padded)
            grad = probs[rows, group(place)].astype(f32) * factor
            grad = (grad - jnp.where(entry == wanted, 1.0 / length, 0.0)).astype(bf16)
            probs[rows, group(place)] = grad
            return grad

        grad = scaled(0)
        for tile in range(4):
            product = tn(grad, table[pl.ds(tile * padded, padded), :])
            if tile < 3:
                grad = scaled(tile + 1)
                acc[...] = product if tile == 0 else acc[...] + product
            else:
                parts[place] = (acc[...] + product).astype(bf16)

        for chunk in range(2):
            sum_copy(turn, chunk).start()

        @pl.when(turn > 0)
        def _():
            for chunk in range(2):
                finish(turn - 1, chunk)
                line_copy(turn - 1, chunk).start()

    gh_rows = 256
    gh_tiles = 4 * padded // gh_rows

    def head_grads(first, last):
        @pl.loop(first, last)
        def _(tile):
            rows = pl.ds(pl.multiple_of(tile * gh_rows, gh_rows), gh_rows)
            value = jnp.dot(probs[rows, :], rows_all[...], preferred_element_type=f32)
            grads[rows, :] = value.astype(bf16)

    def back(chunk):
        part = pl.ds(chunk * quarter, quarter)
        return remote(
            done.at[part], out.at[part], back_send.at[chunk], back_recv.at[chunk], section_peer
        )

    head_grads(0, gh_tiles // 2)
    for chunk in range(2):
        finish(line - 1, chunk)
        for turn in range(line - 1):
            line_copy(turn, chunk).wait_recv()
        own = parts.at[me_line, part_rows(me_pair, chunk)]

        @pl.loop(0, quarter // 16)
        def _(block):
            rows = pl.ds(pl.multiple_of(block * 16, 16), 16)
            chunk_rows = pl.ds(pl.multiple_of(chunk * quarter + block * 16, 16), 16)
            value = own[rows, :].astype(f32)
            for turn in range(line - 1):
                value = value + from_line[turn, chunk_rows, :].astype(f32)
            done[chunk_rows, :] = value.astype(bf16)

        @pl.when(me_section == 0)
        def _():
            back(chunk).start()

    @pl.when(me_section == 0)
    def _():
        out[...] = jnp.zeros_like(out)

    @pl.when(me_section == 1)
    def _():
        out[pl.ds(half, half), :] = done[...]

    head_grads(gh_tiles // 2, gh_tiles)
    for chunk in range(2):

        @pl.when(me_section == 0)
        def _():
            back(chunk).wait_send()

        @pl.when(me_section == 1)
        def _():
            back(chunk).wait_recv()
            give(chunk).wait_send()

        for way in (1, -1):
            for step in range(line - 1):

                @pl.when(sends_along(step, way))
                def _():
                    along(step, way, chunk).wait_send()

        for place in range(line):
            sideways(place, chunk).wait_send()
        for turn in range(line):
            sum_copy(turn, chunk).wait_send()
        for turn in range(line - 1):
            line_copy(turn, chunk).wait_send()
    for place in range(line):
        for n in range(len(chip_peers)):
            stat_copy(n, place).wait_send()


def head_pass(final, targets, heads, line, head_rows, length, collective_id):
    tokens, deep = final.shape
    half = tokens // 2
    padded = heads[0].shape[0]
    vmem = pl.BlockSpec(memory_space=pltpu.VMEM)
    anywhere = pl.BlockSpec(memory_space=pl.ANY)
    dma = pltpu.SemaphoreType.DMA
    peers = 2 * line - 1
    return pl.pallas_call(
        partial(head_kernel, line, head_rows, length),
        out_shape=[
            jax.ShapeDtypeStruct((tokens, deep), bf16),
            jax.ShapeDtypeStruct((4 * padded, deep), bf16),
            jax.ShapeDtypeStruct((line, 1, tokens), f32),
            jax.ShapeDtypeStruct((line, 1, tokens), f32),
        ],
        in_specs=[vmem, vmem] + [anywhere] * len(heads),
        out_specs=[vmem] * 4,
        scratch_shapes=[
            pltpu.VMEM((4 * padded, deep), bf16),
            pltpu.VMEM((line * tokens, deep), bf16),
            pltpu.VMEM((2, 4 * padded, tokens), f32),
            pltpu.VMEM((4 * padded, line * tokens), bf16),
            pltpu.VMEM((tokens, deep), f32),
            pltpu.VMEM((line, tokens, deep), bf16),
            pltpu.VMEM((line, half, deep), bf16),
            pltpu.VMEM((line - 1, half, deep), bf16),
            pltpu.VMEM((line, 2, line, 1, 2 * tokens), f32),
            pltpu.VMEM((half, deep), bf16),
            dma((len(heads),)),
            dma((2,)),
            dma((2,)),
            dma((2,)),
            dma((2, line, 2)),
            dma((2, line, 2)),
            dma((line, 2)),
            dma((line, 2)),
            dma((peers, line)),
            dma((peers, line)),
            dma((line, 2)),
            dma((line, 2)),
            dma((line, 2)),
            dma((line, 2)),
            dma((2,)),
            dma((2,)),
            dma,
            dma,
        ],
        compiler_params=pltpu.CompilerParams(
            collective_id=collective_id, has_side_effects=True, vmem_limit_bytes=60 * 2**20
        ),
        cost_estimate=pl.CostEstimate(
            flops=24 * line * padded * tokens * deep, bytes_accessed=2**28, transcendentals=0
        ),
    )(final, targets, *heads)


def row_stats(values):
    centred = values - jnp.mean(values, -1, keepdims=True)
    factor = lax.rsqrt(jnp.mean(centred * centred, -1, keepdims=True) + epsilon)
    return centred * factor, factor


def two_heads(block):
    first = lax.broadcasted_iota(jnp.int32, block.shape, 1) < HEAD_DIM
    zero = jnp.zeros_like(block)
    return jnp.concatenate([jnp.where(first, block, zero), jnp.where(first, zero, block)], 0)


def one_block(stacked):
    rows = stacked.shape[0] // 2
    first = lax.broadcasted_iota(jnp.int32, (rows, stacked.shape[1]), 1) < HEAD_DIM
    return jnp.where(first, stacked[:rows], stacked[rows:])


def attention_weights(queries, keys):
    scores = nt(keys, queries) * (1.0 / math.sqrt(HEAD_DIM))
    exped = jnp.exp(scores - jnp.max(scores, 0, keepdims=True))
    return exped * (1.0 / jnp.sum(exped, 0, keepdims=True))


def tile_of(index, size):
    return pl.ds(pl.multiple_of(index * size, size), size)


def forward_kernel(seqs, *refs):
    refs = list(refs)

    def take(number):
        return [refs.pop(0) for _ in range(number)]

    start, scale, bias, gain = take(4)
    weights = take(4)
    out, final, x, joined, mixed, middle, entry_attn, entry_mlp, slope, hidden = take(10)
    w_qkv, w_out, w_up, w_down, x_total, arrived, sems, relay_send, relay_recv = refs
    width = start.shape[1]
    length = start.shape[0] // seqs
    me_section = lax.axis_index("section")
    section_peer = {"section": 1 - me_section}
    load_qkv, load_out, load_up, load_down = [
        pltpu.make_async_copy(source.at[0], target, sems.at[n])
        for n, (source, target) in enumerate(zip(weights, (w_qkv, w_out, w_up, w_down)))
    ]
    load_qkv.start()
    greet([section_peer])

    def relay(seq):
        rows = pl.ds(seq * length, length)
        return remote(
            out.at[rows], arrived.at[rows], relay_send.at[seq], relay_recv.at[seq], section_peer
        )

    tile = 512

    def enter(seq):
        rows = pl.ds(seq * length, length)

        @pl.when(me_section == 0)
        def _():
            x[rows, :] = start[rows, :]

        @pl.when(me_section == 1)
        def _():
            relay(seq).wait_recv()
            x[rows, :] = arrived[rows, :].astype(f32)

        normed, _ = row_stats(x[rows, :])
        entry_attn[rows, :] = (normed * scale[seq, :, :width]).astype(bf16)

    def join(first, count):
        rows = pl.ds(first * length, count * length)

        @pl.loop(0, 3 * width // tile)
        def _(index):
            cols = tile_of(index, tile)
            joined[rows, cols] = nn(entry_attn[rows, :], w_qkv[:, cols]).astype(bf16)

    for seq in range(seqs - 1):
        enter(seq)
    load_qkv.wait()
    load_out.start()
    load_up.start()
    join(0, seqs - 1)
    enter(seqs - 1)
    join(seqs - 1, 1)
    load_out.wait()
    load_down.start()
    pairs = width // 128

    @pl.loop(0, pairs)
    def _(pair):
        cols = tile_of(pair, 128)
        for seq in range(seqs):
            rows = pl.ds(seq * length, length)
            queries = two_heads(joined[rows, cols])
            keys = joined[rows, tile_of(pair + pairs, 128)]
            values = joined[rows, tile_of(pair + 2 * pairs, 128)]
            probs = attention_weights(queries, keys).astype(bf16)
            mixed[rows, cols] = one_block(tn(probs, values)).astype(bf16)

    @pl.loop(0, width // tile)
    def _(index):
        cols = tile_of(index, tile)
        middle[:, cols] = x[:, cols] + nn(mixed[...], w_out[:, cols])

    for seq in range(seqs):
        rows = pl.ds(seq * length, length)
        normed, _ = row_stats(middle[rows, :])
        entry_mlp[rows, :] = (normed * scale[seq, :, width:]).astype(bf16)

    load_up.wait()
    load_down.wait()

    def gelu_of(up, rows, cols):
        below = 0.5 + 0.5 * lax.erf(up * math.sqrt(0.5))
        value = (up * below).astype(bf16)
        density = jnp.exp(-0.5 * up * up) * (1.0 / math.sqrt(2.0 * math.pi))
        slope[rows, cols] = (below + up * density).astype(bf16)
        hidden[rows, cols] = value
        return value

    def feed_forward(first, count):
        rows = pl.ds(first * length, count * length)

        def one(index, total):
            sides = [tile_of(2 * index + side, tile) for side in range(2)]
            ups = [nn(entry_mlp[rows, :], w_up[:, cols]) + bias[:, cols] for cols in sides]
            both = jnp.concatenate([gelu_of(up, rows, cols) for up, cols in zip(ups, sides)], 1)
            x_total[rows, :] += nn(both, w_down[tile_of(index, 2 * tile), :])
            return total

        x_total[rows, :] = middle[rows, :]
        lax.fori_loop(0, w_up.shape[1] // (2 * tile), one, 0)
        for seq in range(first, first + count):
            rows = pl.ds(seq * length, length)
            value = x_total[rows, :].astype(bf16)
            out[rows, :] = value

            @pl.when(me_section == 0)
            def _():
                relay(seq).start()

            normed, _ = row_stats(value.astype(f32))
            final[rows, :] = (normed * gain[...]).astype(bf16)

    feed_forward(0, 1)
    feed_forward(1, seqs - 1)

    @pl.when(me_section == 0)
    def _():
        for seq in range(seqs):
            relay(seq).wait_send()


def layer_scratch(width, hidden):
    return [
        pltpu.VMEM((width, 3 * width), bf16),
        pltpu.VMEM((width, width), bf16),
        pltpu.VMEM((width, hidden), bf16),
        pltpu.VMEM((hidden, width), bf16),
    ]


def forward_pass(start, scale, weights, gain, collective_id):
    w_qkv, w_out, w_up, b_hidden, w_down = weights
    tokens, width = start.shape
    wide = w_up.shape[-1]
    seqs = scale.shape[0]
    vmem = pl.BlockSpec(memory_space=pltpu.VMEM)
    anywhere = pl.BlockSpec(memory_space=pl.ANY)

    def low(columns):
        return (tokens, columns), bf16

    exact = ((tokens, width), f32)
    results = [low(width), low(width), exact, low(3 * width), low(width), exact, low(width)]
    results += [low(width), low(wide), low(wide)]
    scratch = layer_scratch(width, wide) + [pltpu.VMEM(*exact), pltpu.VMEM(*low(width))]
    dma = pltpu.SemaphoreType.DMA
    flops = 4 * tokens * (4 * width * width + 2 * width * wide)
    return pl.pallas_call(
        partial(forward_kernel, seqs),
        out_shape=[jax.ShapeDtypeStruct(*item) for item in results],
        in_specs=[vmem] * 4 + [anywhere] * 4,
        out_specs=[vmem] * len(results),
        scratch_shapes=scratch + [dma((4,)), dma((seqs,)), dma((seqs,))],
        compiler_params=pltpu.CompilerParams(
            collective_id=collective_id, has_side_effects=True, vmem_limit_bytes=60 * 2**20
        ),
        cost_estimate=pl.CostEstimate(flops=2 * flops, bytes_accessed=2**25, transcendentals=0),
    )(start, scale, b_hidden, gain, w_qkv, w_out, w_up, w_down)


def norm_grads(source, total, grad_middle, scale, grad_cond, half, seq, store):
    width = total.shape[1]
    length = total.shape[0] // scale.shape[0]
    rows = pl.ds(seq * length, length)
    cols = pl.ds(half * width, width)
    normed, factor = row_stats(source[rows, :])
    gradient = total[rows, :]
    if grad_cond is not None:
        grad_cond[seq, :, cols] = jnp.sum(gradient * normed, 0, keepdims=True)
    scaled = gradient * scale[seq, :, cols]
    back = factor * (
        scaled
        - jnp.mean(scaled, -1, keepdims=True)
        - normed * jnp.mean(scaled * normed, -1, keepdims=True)
    )
    store(rows, grad_middle[rows, :] + back)


def attention_grads(joined, grad_mixed, grad_joined, pair, seqs):
    pairs = grad_mixed.shape[1] // 128
    length = grad_mixed.shape[0] // seqs
    shrink = 1.0 / math.sqrt(HEAD_DIM)
    cols = tile_of(pair, 128)
    key_cols = tile_of(pair + pairs, 128)
    value_cols = tile_of(pair + 2 * pairs, 128)
    for seq in range(seqs):
        rows = pl.ds(seq * length, length)
        queries = two_heads(joined[rows, cols])
        keys = joined[rows, key_cols]
        probs = attention_weights(queries, keys)
        grads = two_heads(grad_mixed[rows, cols])
        grad_probs = nt(joined[rows, value_cols], grads)
        inner = jnp.sum(grad_probs * probs, 0, keepdims=True)
        grad_scores = (probs * (grad_probs - inner)).astype(bf16)
        grad_joined[rows, cols] = (one_block(tn(grad_scores, keys)) * shrink).astype(bf16)
        grad_joined[rows, key_cols] = (nn(grad_scores, queries) * shrink).astype(bf16)
        grad_joined[rows, value_cols] = nn(probs.astype(bf16), grads).astype(bf16)


def backward_kernel(begin, seqs, *refs):
    refs = list(refs)

    def take(number):
        return [refs.pop(0) for _ in range(number)]

    if begin:
        incoming, other, hidden, entry = take(4)
        far = take(3)
        grad_middle, total, grad_bias, down_out, up_out = take(5)
        grad_low, grad_up, entry_turned, down_weight, up_weight, out_sem = take(6)
        near = take(3)
    else:
        scale, incoming, other, gain = take(4)
        far = take(8)
        out, grad_top, grad_gain = take(3)
        grad_low, grad_up, grad_attn, grad_joined = take(4)
        near = take(8)
        total, grad_middle, grad_mixed = take(3)
    (sems,) = refs
    if begin:
        slope, w_up, w_down = near
        load_slope = pltpu.make_async_copy(far[0], slope, sems.at[0])
        load_up = pltpu.make_async_copy(far[1].at[0], w_up, sems.at[1])
        load_down = pltpu.make_async_copy(far[2].at[0], w_down, sems.at[2])
    else:
        slope, w_up, w_down, x, middle, joined, w_qkv, w_out = near
        load_slope = pltpu.make_async_copy(far[0], slope, sems.at[0])
        load_up = pltpu.make_async_copy(far[1].at[0], w_up, sems.at[1])
        load_down = pltpu.make_async_copy(far[2].at[0], w_down, sems.at[2])
        load_x = pltpu.make_async_copy(far[3], x, sems.at[3])
        load_middle = pltpu.make_async_copy(far[4], middle, sems.at[4])
        load_joined = pltpu.make_async_copy(far[5], joined, sems.at[5])
        load_qkv = pltpu.make_async_copy(far[6].at[0], w_qkv, sems.at[6])
        load_out = pltpu.make_async_copy(far[7].at[0], w_out, sems.at[7])
    width = incoming.shape[1]
    length = incoming.shape[0] // seqs
    load_down.start()
    load_slope.start()
    if begin:
        entry_turned[...] = entry[...].T

    for seq in range(seqs):
        rows = pl.ds(seq * length, length)
        if begin:
            first = (lax.axis_index("section") == 0).astype(f32)
            value = incoming[rows, :].astype(f32) * first + other[rows, :] * (1.0 - first)
        else:
            normed, factor = row_stats(other[rows, :].astype(f32))
            gradient = incoming[rows, :].astype(f32)
            part = jnp.sum(gradient * normed, 0, keepdims=True)
            grad_gain[...] = part if seq == 0 else grad_gain[...] + part
            scaled = gradient * gain[...]
            value = factor * (
                scaled
                - jnp.mean(scaled, -1, keepdims=True)
                - normed * jnp.mean(scaled * normed, -1, keepdims=True)
            )
            grad_top[rows, :] = value
        grad_middle[rows, :] = value
        grad_low[rows, :] = value.astype(bf16)

    load_down.wait()
    load_slope.wait()
    load_up.start()
    if not begin:
        load_middle.start()
        load_out.start()
        load_joined.start()
    tile = 1024

    @pl.loop(0, w_up.shape[1] // tile)
    def _(index):
        cols = tile_of(index, tile)
        grad_hidden = nt(grad_low[...], w_down[cols, :])
        value = (grad_hidden * slope[:, cols].astype(f32)).astype(bf16)
        grad_up[:, cols] = value
        if begin:
            grad_bias[:, cols] = jnp.sum(value.astype(f32), 0, keepdims=True)
            down_weight[cols, :] = tn(hidden[:, cols], grad_low[...]).astype(bf16)
            pltpu.make_async_copy(
                down_weight.at[cols], down_out.at[cols], out_sem.at[0, index]
            ).start()
            up_weight[:, cols] = nn(entry_turned[...], value).astype(bf16)

    if begin:
        whole_up = pltpu.make_async_copy(up_weight, up_out, out_sem.at[1, 0])
        whole_up.start()
    load_up.wait()
    if not begin:
        load_middle.wait()
        load_out.wait()
        load_joined.wait()
        load_qkv.start()
        load_x.start()

    @pl.loop(0, width // 256)
    def _(index):
        total[:, tile_of(index, 256)] = nt(grad_up[...], w_up[tile_of(index, 256), :])

    if begin:
        for index in range(w_up.shape[1] // tile):
            cols = pl.ds(index * tile, tile)
            pltpu.make_async_copy(
                down_weight.at[cols], down_out.at[cols], out_sem.at[0, index]
            ).wait()
        whole_up.wait()
        return

    def store_middle(rows, value):
        grad_middle[rows, :] = value
        grad_attn[rows, :] = value.astype(bf16)

    for seq in range(seqs):
        norm_grads(middle, total, grad_middle, scale, None, 1, seq, store_middle)

    @pl.loop(0, width // 512)
    def _(index):
        part = tile_of(index, 512)
        grad_mixed[:, part] = nt(grad_attn[...], w_out[part, :]).astype(bf16)

    @pl.loop(0, width // 128)
    def _(pair):
        attention_grads(joined, grad_mixed, grad_joined, pair, seqs)

    load_qkv.wait()
    load_x.wait()

    @pl.loop(0, width // 256)
    def _(index):
        total[:, tile_of(index, 256)] = nt(grad_joined[...], w_qkv[tile_of(index, 256), :])

    def store_out(rows, value):
        out[rows, :] = value.astype(bf16)

    for seq in range(seqs):
        norm_grads(x, total, grad_middle, scale, None, 0, seq, store_out)


def backward_pass(grad_final, block_out, gain, scale, kept, weights):
    w_qkv, w_out, w_up, _, w_down = weights
    x, joined, _, middle, _, _, slope, _ = kept
    tokens, width = x.shape
    wide = w_up.shape[-1]
    vmem = pl.BlockSpec(memory_space=pltpu.VMEM)
    anywhere = pl.BlockSpec(memory_space=pl.ANY)
    exact = ((tokens, width), f32)
    low = ((tokens, width), bf16)
    lows = [low, ((tokens, wide), bf16), low, ((tokens, 3 * width), bf16)]
    near = [
        ((tokens, wide), bf16),
        ((width, wide), bf16),
        ((wide, width), bf16),
        exact,
        exact,
        ((tokens, 3 * width), bf16),
        ((width, 3 * width), bf16),
        ((width, width), bf16),
    ]
    flops = 4 * tokens * (4 * width * width + 2 * width * wide)
    return pl.pallas_call(
        partial(backward_kernel, False, scale.shape[0]),
        out_shape=[jax.ShapeDtypeStruct(*item) for item in [low, exact, ((1, width), f32)]],
        in_specs=[vmem] * 4 + [anywhere] * 8,
        out_specs=[vmem] * 3,
        scratch_shapes=[pltpu.VMEM(*item) for item in lows + near + [exact, exact, low]]
        + [pltpu.SemaphoreType.DMA((8,))],
        compiler_params=pltpu.CompilerParams(vmem_limit_bytes=60 * 2**20),
        cost_estimate=pl.CostEstimate(flops=flops, bytes_accessed=2**25, transcendentals=0),
    )(scale, grad_final, block_out, gain, slope, w_up, w_down, x, middle, joined, w_qkv, w_out)


def backward_begin(returned, grad_top, seqs, hidden, entry, slope, w_up, w_down):
    tokens, width = grad_top.shape
    wide = w_up.shape[-1]
    vmem = pl.BlockSpec(memory_space=pltpu.VMEM)
    anywhere = pl.BlockSpec(memory_space=pl.ANY)
    exact = ((tokens, width), f32)
    low = ((tokens, width), bf16)
    wide_low = ((tokens, wide), bf16)
    up, down = ((width, wide), bf16), ((wide, width), bf16)
    results = [exact, exact, ((1, wide), f32), down, up]
    inside = [low, wide_low, ((width, tokens), bf16), down, up]
    return pl.pallas_call(
        partial(backward_kernel, True, seqs),
        out_shape=[jax.ShapeDtypeStruct(*item) for item in results],
        in_specs=[vmem] * 4 + [anywhere] * 3,
        out_specs=[vmem] * 3 + [anywhere] * 2,
        scratch_shapes=[pltpu.VMEM(*item) for item in inside]
        + [pltpu.SemaphoreType.DMA((2, wide // 1024))]
        + [pltpu.VMEM(*item) for item in (wide_low, up, down)]
        + [pltpu.SemaphoreType.DMA((3,))],
        compiler_params=pltpu.CompilerParams(vmem_limit_bytes=60 * 2**20),
        cost_estimate=pl.CostEstimate(
            flops=16 * tokens * width * wide, bytes_accessed=2**25, transcendentals=0
        ),
    )(returned, grad_top, hidden, entry, slope, w_up, w_down)


def tail_kernel(line, seqs, lag, *refs):
    refs = list(refs)

    def take(number):
        return [refs.pop(0) for _ in range(number)]

    scale, rest, factor_one, factor_two, embedded, noisy, w_in = take(7)
    far = take(9)
    parts = take(2)
    (head_part,) = take(1)
    outs = take(5)
    head_out, smalls, rows_all = take(3)
    near = take(9)
    grad_attn, grad_mixed, grad_joined, grad_first, grad_cond, in_weight = take(6)
    rows_own, small_wide, small_own = take(3)
    own, from_core, slots = take(2), take(5), take(5)
    head_own, head_core, head_section, last_total = take(4)
    far_sem, load_sem, core_send, core_recv, ring_send, ring_recv, credit = take(7)
    keep_sem, packet_send, packet_recv, wide_send, wide_recv, rows_send, rows_recv = take(7)
    head_sem, head_send, head_recv, cross_send, cross_recv = take(5)
    grad_middle, grad_entry, middle, x, joined, mixed, entry_attn, w_out, w_qkv = near
    inside = [w_qkv, w_out, in_weight]
    groups = ((0, 1), (2, 3, 4))
    chips = 2 * line
    width = x.shape[1]
    me_section = lax.axis_index("section")
    me_line = lax.axis_index("line")
    me_pair = lax.axis_index("pair")
    me_core = lax.axis_index("core")
    position = me_line + me_pair * (chips - 1 - 2 * me_line)
    section_peer = {"section": 1 - me_section}
    core_peer = {"core": 1 - me_core}
    ways = (1, -1)
    ring_peers = []
    for way in ways:
        peer_line, peer_pair = ring_place(lax.rem(position + way + chips, chips), line)
        ring_peers.append({"line": peer_line, "pair": peer_pair})
    greet([core_peer, section_peer] + ring_peers)

    shapes = [ref.shape[-2:] for ref in from_core]

    def block_of(turn, step):
        ahead = lax.rem(position - ways[turn] * (1 + step) + 2 * chips, chips)
        return ring_place(ahead, line)

    def columns(index, turn):
        wide = shapes[index][-1] // 2
        return pl.ds(turn * wide, wide)

    def block_rows(index, place, pair, core):
        high = shapes[index][0]
        return pl.ds(pl.multiple_of(((place * 2 + pair) * 2 + core) * high, 16), high)

    def source(index, turn, step, core):
        place, pair = block_of(turn, step)
        cols = columns(index, turn)
        if index < 2:
            return parts[index].at[place, pair, core, :, cols]
        return inside[index - 2].at[block_rows(index, place, pair, core), cols]

    def load(index, turn, step):
        return pltpu.make_async_copy(
            source(index, turn, step, me_core),
            own[index].at[step % 2, :, columns(index, turn)],
            load_sem.at[index, turn, step],
        )

    def core_copy(index, turn, step):
        return remote(
            source(index, turn, step, 1 - me_core),
            from_core[index].at[step % 3, :, columns(index, turn)],
            core_send.at[index, turn, step],
            core_recv.at[index, turn, step],
            core_peer,
        )

    def ring_copy(index, turn, step):
        cols = columns(index, turn)
        passed = from_core[index].at[0, :, cols] if step == 0 else slots[index].at[step - 1, :, cols]
        return remote(
            passed,
            slots[index].at[step, :, cols],
            ring_send.at[index, turn, step],
            ring_recv.at[index, turn, step],
            ring_peers[turn],
        )

    def to_core(group, step):
        if step >= 3:
            pl.semaphore_wait(credit.at[group], 1)
        for index in groups[group]:
            for turn in range(2):
                if index < 2:
                    load(index, turn, step).start()
                core_copy(index, turn, step).start()

    def stop(group, step, between):
        first, last = step == 0, step == chips - 1
        for index in groups[group]:
            rows, wide = shapes[index][0], shapes[index][1] // 2
            tile = min(wide, 512)
            for turn in range(2):
                if index < 2:
                    load(index, turn, step).wait()
                core_copy(index, turn, step).wait_recv()
                if not first:
                    ring_copy(index, turn, step - 1).wait_recv()
                place, pair = block_of(turn, step)

                @pl.loop(0, rows // 16)
                def _(block):
                    row = pl.ds(pl.multiple_of(block * 16, 16), 16)
                    if index >= 2:
                        base = ((place * 2 + pair) * 2 + me_core) * rows + block * 16
                        own_row = pl.ds(pl.multiple_of(base, 16), 16)
                    for col in range(turn * wide, (turn + 1) * wide, tile):
                        cols = pl.ds(col, tile)
                        if index < 2:
                            mine = own[index][step % 2, row, cols]
                        else:
                            mine = inside[index - 2][own_row, cols]
                        total = from_core[index][step % 3, row, cols].astype(f32)
                        total = total + mine.astype(f32)
                        if not first:
                            total = total + slots[index][step - 1, row, cols].astype(f32)
                        if last and index == 4:
                            last_total[row, cols] = total
                        elif last:
                            outs[index][row, cols] = total.astype(bf16)
                        elif first:
                            from_core[index][0, row, cols] = total.astype(bf16)
                        else:
                            slots[index][step - 1, row, cols] = total.astype(bf16)

                if not last:
                    ring_copy(index, turn, step).start()
                between()
        if step == 1:
            for index in groups[group]:
                for turn in range(2):
                    ring_copy(index, turn, 0).wait_send()
        if 1 <= step <= 4:
            amount = 2 if step == 1 else 1
            pl.semaphore_signal(
                credit.at[group], inc=amount, device_id=core_peer, device_id_type=MESH
            )

    hops = (line, line - 1)

    def packet_blocks(place, pair):
        return [smalls.at[place, pair, me_core], rows_all.at[place, pair, me_core]]

    def packet_hops(turn, hop, away):
        place, pair = ring_place(
            lax.rem(position - ways[turn] * (hop + away) + 2 * chips, chips), line
        )
        return [
            remote(
                block,
                block,
                packet_send.at[n, turn, hop],
                packet_recv.at[n, turn, hop],
                ring_peers[turn],
            )
            for n, block in enumerate(packet_blocks(place, pair))
        ]

    def pass_packets(hop):
        for turn in range(2):
            if 0 < hop <= hops[turn]:
                for copy in packet_hops(turn, hop - 1, 1):
                    copy.wait_recv()
            if hop < hops[turn]:
                for copy in packet_hops(turn, hop, 0):
                    copy.start()

    small_slot, rows_slot = packet_blocks(me_line, me_pair)
    keep_small = pltpu.make_async_copy(small_own, small_slot, keep_sem.at[0])
    keep_rows = pltpu.make_async_copy(rows_own, rows_slot, keep_sem.at[1])
    rows_over = remote(rows_own, rows_slot, rows_send, rows_recv, section_peer)
    across = [
        remote(block, block, wide_send.at[n], wide_recv.at[n], core_peer)
        for n, block in enumerate([smalls.at[:, :, me_core], rows_all.at[:, :, me_core]])
    ]
    def packets_ready():
        keep_small.wait()

        @pl.when(me_section == 0)
        def _():
            keep_rows.wait()

        @pl.when(me_section == 1)
        def _():
            rows_over.wait_recv()

    high = head_part.shape[0] // 4

    def shard(n):
        return head_part.at[pl.ds(n * high, high)]

    head_loads = [
        pltpu.make_async_copy(shard(2 * n), head_own.at[n], head_sem.at[n]) for n in range(2)
    ]
    head_copies = [
        remote(shard(2 * n + 1), head_core.at[n], head_send.at[n], head_recv.at[n], core_peer)
        for n in range(2)
    ]
    head_copies.append(
        remote(head_core.at[1], head_section, head_send.at[2], head_recv.at[2], section_peer)
    )

    def head_over_cores():
        for copy in head_loads:
            copy.wait()
        for copy in head_copies[:2]:
            copy.wait_recv()

        @pl.loop(0, high // 16)
        def _(block):
            rows = pl.ds(pl.multiple_of(block * 16, 16), 16)
            value = head_core[1, rows, :].astype(f32) + head_own[1, rows, :].astype(f32)
            head_core[1, rows, :] = value.astype(bf16)

        head_copies[2].start()

    def head_over_sections():
        head_copies[2].wait_recv()

        @pl.loop(0, high // 16)
        def _(block):
            rows = pl.ds(pl.multiple_of(block * 16, 16), 16)
            value = head_core[0, rows, :].astype(f32) + head_own[0, rows, :].astype(f32)
            value = value + head_section[rows, :].astype(f32)
            head_out[rows, :] = value.astype(bf16)

    far_copies = []
    for n, (where, target) in enumerate(zip(far, near)):
        where = where.at[0] if n >= 7 else where
        far_copies.append(pltpu.make_async_copy(where, target, far_sem.at[n]))

    def waits(*numbers):
        for n in numbers:
            far_copies[n].wait()

    def store_middle(rows, value):
        grad_middle[rows, :] = value
        grad_attn[rows, :] = value.astype(bf16)

    def store_first(rows, value):
        grad_first[rows, :] = value.astype(bf16)

    def second_norm(seq):
        if seq == 0:
            waits(0, 1, 2)
        norm_grads(middle, grad_entry, grad_middle, scale, grad_cond, 1, seq, store_middle)

    def mixed_grads(index):
        if index == 0:
            waits(7)
        part = pl.ds(index * 512, 512)
        grad_mixed[:, part] = nt(grad_attn[...], w_out[part, :]).astype(bf16)

    def heads_grads(pair):
        if pair == 0:
            waits(4)
        attention_grads(joined, grad_mixed, grad_joined, pair, seqs)

    def entry_grads(index):
        if index == 0:
            waits(8)
        part = pl.ds(index * 256, 256)
        grad_entry[:, part] = nt(grad_joined[...], w_qkv[part, :])

    def first_norm(seq):
        if seq == 0:
            waits(3)
        norm_grads(x, grad_entry, grad_middle, scale, grad_cond, 0, seq, store_first)

    def embedding_rows(_):
        grad_noisy = nt(grad_first[...], w_in[...])
        inner = jnp.mean(grad_noisy * embedded[...], -1, keepdims=True)
        value = factor_one[...] * grad_noisy - factor_two[...] * embedded[...] * inner
        rows_own[...] = value.astype(bf16)

        @pl.when(me_section == 0)
        def _():
            keep_rows.start()
            rows_over.start()

    def small_rows(_):
        each = small_wide.shape[1]
        for seq in range(seqs):
            for n in range(2 * width // each):
                row = pl.ds(seq * (2 * width // each) + n, 1)
                small_wide[row, :] = grad_cond[seq, :, pl.ds(n * each, each)]
        small_wide[pl.ds(seqs * 2 * width // each, rest.shape[0]), :] = rest[...]
        small_own[...] = small_wide[...].astype(bf16)
        keep_small.start()

    def input_weight(_):
        in_weight[...] = tn(noisy[...], grad_first[...]).astype(bf16)

    def qkv_weight(index):
        if index == 0:
            waits(6)
        part = pl.ds(index * 256, 256)
        w_qkv[part, :] = tn(entry_attn[:, part], grad_joined[...]).astype(bf16)

    def out_weight(index):
        if index == 0:
            waits(5)
        part = pl.ds(index * 512, 512)
        w_out[part, :] = tn(mixed[:, part], grad_attn[...]).astype(bf16)

    steps = []
    for step, number in (
        (second_norm, seqs),
        (mixed_grads, width // 512),
        (heads_grads, width // 128),
        (entry_grads, width // 256),
        (first_norm, seqs),
        (embedding_rows, 1),
        (small_rows, 1),
        (input_weight, 1),
        (qkv_weight, width // 256),
        (out_weight, width // 512),
    ):
        steps += [partial(step, n) for n in range(number)]
    at_once = -(-len(steps) // (4 * lag))

    def work():
        for _ in range(at_once):
            if steps:
                steps.pop(0)()

    def nothing():
        pass

    to_core(0, 0)
    to_core(0, 1)
    for copy in far_copies:
        copy.start()
    stop(0, 0, work)
    for turn in range(1, chips + lag):
        if turn + 1 < chips:
            to_core(0, turn + 1)
        if turn == 1:
            for copy in head_loads + head_copies[:2]:
                copy.start()
        if turn == lag:
            to_core(1, 0)
        if lag <= turn and turn - lag + 1 < chips:
            to_core(1, turn - lag + 1)
        if turn < chips:
            stop(0, turn, work if turn < lag else nothing)
        if turn >= lag:
            stop(1, turn - lag, nothing)
        hop = turn - lag - 2
        if hop == 0:
            packets_ready()
        if 0 <= hop <= line:
            pass_packets(hop)
        if hop == line:
            for copy in across:
                copy.start()
        if turn == 3:
            head_over_cores()
        if turn == chips + lag - 2:
            head_over_sections()
    each = outs[4].shape[0]
    give = remote(last_total.at[pl.ds(each, each)], outs[4], cross_send, cross_recv, section_peer)

    @pl.when(me_section == 0)
    def _():
        give.start()
        outs[4][...] = last_total[pl.ds(0, each), :]

    for copy in across:
        copy.wait()
    for copy in head_copies:
        copy.wait_send()
    for turn in range(2):
        for hop in range(hops[turn]):
            for copy in packet_hops(turn, hop, 0):
                copy.wait_send()
    for index in range(5):
        for turn in range(2):
            for step in range(chips):
                core_copy(index, turn, step).wait_send()
                if 0 < step < chips - 1:
                    ring_copy(index, turn, step).wait_send()

    @pl.when(me_section == 0)
    def _():
        rows_over.wait_send()
        give.wait_send()

    @pl.when(me_section == 1)
    def _():
        give.wait_recv()


def tail_pass(scale, rest, factors, embedded, noisy, w_in, far, parts, head_part, collective_id):
    grad_middle = far[0]
    tokens, width = grad_middle.shape
    seqs = scale.shape[0]
    line = parts[0].shape[0]
    chips = 2 * line
    count = 4 * line
    emb_width = noisy.shape[1]
    vmem = pl.BlockSpec(memory_space=pltpu.VMEM)
    anywhere = pl.BlockSpec(memory_space=pl.ANY)
    dma = pltpu.SemaphoreType.DMA
    shapes = [part.shape[-2:] for part in parts]
    shapes += [
        (width // count, 3 * width),
        (width // count, width),
        (emb_width // count, width),
    ]
    each = shapes[4][0] // 2
    high = head_part.shape[0] // 4
    small = (seqs * 2 * width // emb_width + rest.shape[0], emb_width)
    exact = ((tokens, width), f32)
    low = ((tokens, width), bf16)
    three = ((tokens, 3 * width), bf16)
    rows = (tokens, emb_width)
    results = [(shape, bf16) for shape in shapes[:4]]
    results += [((each, width), f32), ((high, width), bf16)]
    results += [((line, 2, 2) + small, bf16), ((line, 2, 2) + rows, bf16)]
    room = [exact, exact, exact, exact, three, low, low]
    room += [((width, width), bf16), ((width, 3 * width), bf16)]
    room += [low, low, three, low, ((seqs, 1, 2 * width), f32), ((emb_width, width), bf16)]
    room += [(rows, bf16), (small, f32), (small, bf16)]
    room += [((2,) + shape, bf16) for shape in shapes[:2]]
    room += [((3,) + shape, bf16) for shape in shapes]
    room += [((chips - 1,) + shape, bf16) for shape in shapes]
    room += [((2, high, width), bf16), ((2, high, width), bf16), ((high, width), bf16)]
    room += [(shapes[4], f32)]
    scratch = [pltpu.VMEM(*item) for item in room]
    scratch += [dma((9,)), dma((2, 2, chips)), dma((5, 2, chips)), dma((5, 2, chips))]
    scratch += [dma((5, 2, chips - 1)), dma((5, 2, chips - 1)), pltpu.SemaphoreType.REGULAR((2,))]
    scratch += [dma((2,)), dma((2, 2, line)), dma((2, 2, line)), dma((2,)), dma((2,)), dma, dma]
    scratch += [dma((2,)), dma((3,)), dma((3,)), dma, dma]
    return pl.pallas_call(
        partial(tail_kernel, line, seqs, line),
        out_shape=[jax.ShapeDtypeStruct(*item) for item in results],
        in_specs=[vmem] * 7 + [anywhere] * 12,
        out_specs=[vmem] * 6 + [anywhere] * 2,
        scratch_shapes=scratch,
        compiler_params=pltpu.CompilerParams(
            collective_id=collective_id, has_side_effects=True, vmem_limit_bytes=62 * 2**20
        ),
        cost_estimate=pl.CostEstimate(flops=0, bytes_accessed=2**29, transcendentals=0),
    )(scale, rest, *factors, embedded, noisy, w_in, *far, *parts, head_part)


def finish_kernel(line, head_rows, *refs):
    ids, rows, *lows = refs[:7]
    *exacts, grad_embed, total = refs[7:]
    me_section = lax.axis_index("section")
    me_line = lax.axis_index("line")
    me_pair = lax.axis_index("pair")
    me_core = lax.axis_index("core")
    high = total.shape[0]
    base = (((me_section * line + me_line) * 2 + me_pair) * 2 + me_core) * grad_embed.shape[0]
    tile = 768
    for index in range(rows.shape[0] // tile):
        part = pl.ds(index * tile, tile)
        entry = lax.broadcasted_iota(jnp.int32, (high, tile), 0) + base
        place = jnp.where(entry == ids[:, part], 1.0, 0.0).astype(bf16)
        product = nn(place, rows[part, :])
        total[...] = product if index == 0 else total[...] + product
    grad_embed[...] = total[pl.ds(0, grad_embed.shape[0]), :]
    for low, exact in zip(lows, exacts):
        whole = exact.shape[0] // 16
        left = exact.shape[0] % 16

        @pl.loop(0, whole)
        def _(block):
            part = pl.ds(pl.multiple_of(block * 16, 16), 16)
            exact[part, :] = low[part, :].astype(f32)

        if left:
            value = low[pl.ds(whole * 16, 16), :].astype(f32)
            exact[pl.ds(whole * 16, left), :] = value[:left]


def finish(ids, rows, lows, line, head_rows, out_rows):
    vmem = pl.BlockSpec(memory_space=pltpu.VMEM)
    shapes = [low.shape for low in lows[:-1]] + [(head_rows, lows[-1].shape[1])]
    shapes.append((out_rows, rows.shape[1]))
    return pl.pallas_call(
        partial(finish_kernel, line, head_rows),
        out_shape=[jax.ShapeDtypeStruct(shape, f32) for shape in shapes],
        in_specs=[vmem] * 7,
        out_specs=[vmem] * 6,
        scratch_shapes=[pltpu.VMEM((-(-out_rows // 16) * 16, rows.shape[1]), f32)],
        compiler_params=pltpu.CompilerParams(vmem_limit_bytes=60 * 2**20),
        cost_estimate=pl.CostEstimate(
            flops=2 * out_rows * rows.size, bytes_accessed=2**24, transcendentals=0
        ),
    )(ids, rows, *lows)


def norm_rows(values):
    centred = values - jnp.mean(values, -1, keepdims=True)
    factor = lax.rsqrt(jnp.mean(centred * centred, -1, keepdims=True) + epsilon)
    return (centred * factor, factor)


def norm_back(gradient, normed, factor):
    return factor * (
        gradient
        - jnp.mean(gradient, -1, keepdims=True)
        - normed * jnp.mean(gradient * normed, -1, keepdims=True)
    )


def time_features(noise_level):
    half_width = TFEAT // 2
    rates = jnp.exp(jnp.arange(half_width, dtype=f32) * (math.log(1000.0) / half_width))
    angles = (jnp.log(noise_level) / 4.0)[:, None] * rates[None, :]
    return jnp.concatenate([jnp.cos(angles), jnp.sin(angles)], -1)


def levels_of(bins, table):
    hits = bins[:, None] == jnp.arange(table.shape[0])[None, :]
    return jnp.sum(jnp.where(hits, table[None, :], 0.0), -1)


def over_dp(part):
    part = part.reshape((part.shape[0] // 4, 2, 2) + part.shape[1:])
    part = lax.psum_scatter(part, "core", scatter_dimension=2)
    part = lax.psum_scatter(part, "pair", scatter_dimension=1)
    return lax.psum_scatter(part, "line", scatter_dimension=0)


def by_owner(part):
    line = lax.axis_size("line")
    return part.astype(bf16).reshape((line, 2, 2, part.shape[0] // (line * 4)) + part.shape[1:])


def mm(spec, left, right):
    return jnp.einsum(spec, left, right, preferred_element_type=f32)


def layer_forward(stream, scale_attn, scale_mlp, weights):
    w_qkv, w_out, w_up, b_hidden, w_down = weights
    seq_count, length, model_width = stream.shape
    normed_attn, factor_attn = norm_rows(stream)
    attn_entry = (normed_attn * scale_attn).astype(bf16)
    joined = mm("nsd,de->nse", attn_entry, w_qkv).astype(bf16)
    qkv_parts = joined.reshape(seq_count, length, 3, HEADS, HEAD_DIM)
    query_rows = qkv_parts[:, :, 0]
    key_rows = qkv_parts[:, :, 1]
    value_rows = qkv_parts[:, :, 2]
    scores = mm("nqhe,nkhe->nhqk", query_rows, key_rows) / math.sqrt(HEAD_DIM)
    exp_scores = jnp.exp(scores - jnp.max(scores, -1, keepdims=True))
    attn_probs = exp_scores / jnp.sum(exp_scores, -1, keepdims=True)
    probs_low = attn_probs.astype(bf16)
    attn_mixed = mm("nhqk,nkhe->nqhe", probs_low, value_rows).astype(bf16)
    attn_mixed = attn_mixed.reshape(seq_count, length, model_width)
    middle = stream + mm("nsd,de->nse", attn_mixed, w_out)
    normed_mlp, factor_mlp = norm_rows(middle)
    mlp_entry = (normed_mlp * scale_mlp).astype(bf16)
    up_proj = mm("nsd,df->nsf", mlp_entry, w_up) + b_hidden
    below = 0.5 + 0.5 * lax.erf(up_proj * math.sqrt(0.5))
    hidden = (up_proj * below).astype(bf16)
    density = jnp.exp(-0.5 * up_proj * up_proj) * (1.0 / math.sqrt(2.0 * math.pi))
    slope = (below + up_proj * density).astype(bf16)
    block_out = middle + mm("nsf,fd->nsd", hidden, w_down)
    kept = (
        normed_attn,
        factor_attn,
        attn_entry,
        query_rows,
        key_rows,
        value_rows,
        attn_probs,
        probs_low,
        attn_mixed,
        normed_mlp,
        factor_mlp,
        mlp_entry,
        slope,
        hidden,
    )
    return (block_out, kept)


def layer_backward(grad_out, kept, scale_attn, scale_mlp, weights, whole):
    w_qkv, w_out, w_up, b_hidden, w_down = weights
    (
        normed_attn,
        factor_attn,
        attn_entry,
        query_rows,
        key_rows,
        value_rows,
        attn_probs,
        probs_low,
        attn_mixed,
        normed_mlp,
        factor_mlp,
        mlp_entry,
        slope,
        hidden,
    ) = kept
    seq_count, length, model_width = grad_out.shape
    grads = {}
    grad_branch = grad_out.astype(bf16)
    if whole:
        grads["down"] = by_owner(mm("nsf,nsd->fd", hidden, grad_branch))
    grad_hidden = mm("nsd,fd->nsf", grad_branch, w_down)
    grad_up_proj = (grad_hidden * slope.astype(f32)).astype(bf16)
    if whole:
        grads["bias"] = jnp.sum(grad_up_proj.astype(f32), (0, 1))
        grads["up"] = by_owner(mm("nsd,nsf->df", mlp_entry, grad_up_proj))
    grad_entry = mm("nsf,df->nsd", grad_up_proj, w_up)
    grad_middle = grad_out + norm_back(grad_entry * scale_mlp, normed_mlp, factor_mlp)
    grad_attn = grad_middle.astype(bf16)
    if whole:
        grads["out"] = by_owner(mm("nsd,nse->de", attn_mixed, grad_attn))
    grad_mixed = mm("nse,de->nsd", grad_attn, w_out)
    grad_mixed = grad_mixed.astype(bf16).reshape(seq_count, length, HEADS, HEAD_DIM)
    grad_probs = mm("nqhe,nkhe->nhqk", grad_mixed, value_rows)
    grad_values = mm("nhqk,nqhe->nkhe", probs_low, grad_mixed)
    grad_scores = (
        attn_probs * (grad_probs - jnp.sum(grad_probs * attn_probs, -1, keepdims=True))
    ).astype(bf16)
    grad_query = mm("nhqk,nkhe->nqhe", grad_scores, key_rows) / math.sqrt(HEAD_DIM)
    grad_keys = mm("nhqk,nqhe->nkhe", grad_scores, query_rows) / math.sqrt(HEAD_DIM)
    grad_joined = jnp.stack([grad_query, grad_keys, grad_values], 2).astype(bf16)
    grad_joined = grad_joined.reshape(seq_count, length, 3 * model_width)
    if whole:
        grads["qkv"] = by_owner(mm("nsd,nse->de", attn_entry, grad_joined))
    grad_attn_entry = mm("nse,de->nsd", grad_joined, w_qkv)
    grad_stream = grad_middle + norm_back(grad_attn_entry * scale_attn, normed_attn, factor_attn)
    if whole:
        grads["cond"] = jnp.concatenate(
            [jnp.sum(grad_attn_entry * normed_attn, 1), jnp.sum(grad_entry * normed_mlp, 1)], -1
        )
    return (grad_stream, grads)


def local(
    token_ids,
    target_ids,
    time_bins,
    sigma_table,
    noise,
    embed,
    w_in,
    w_time,
    norm_gain,
    w_qkv,
    w_out,
    w_up,
    b_hidden,
    w_down,
    out_gain,
    head,
):
    section = lax.axis_index("section")
    line_at = lax.axis_index("line")
    pair_at = lax.axis_index("pair")
    core = lax.axis_index("core")
    sections = lax.axis_size("section")
    line = lax.axis_size("line")
    chip = line_at * 2 + pair_at
    chips = line * 2
    cores = 2
    dp_count = chips * cores
    dp_index = chip * cores + core
    is_first = section == 0
    seqs, length = token_ids.shape
    tokens = seqs * length
    half = tokens // sections
    model_width = w_out.shape[-1]
    emb_rows, emb_width = embed.shape
    straight = line <= 4 and half % 16 == 0 and model_width // dp_count % 16 == 0

    if straight:
        lanes = -(-half // 128) * 128
        blocks = [part.reshape(2, half) for part in (token_ids, target_ids)]
        blocks.append(jnp.pad(time_bins[None, :], ((0, 0), (0, half - seqs))))
        own_ids = jnp.pad(jnp.concatenate(blocks, 0), ((0, 3), (0, lanes - half)))
        all_ids, embedded = start_pass(own_ids, embed, half, line, 0)
        all_ids = all_ids.reshape(dp_count, 8, lanes)
        all_tokens = all_ids[:, 0:2, :half].reshape(dp_count, tokens)
        all_targets = all_ids[:, 2:4, :half].reshape(dp_count, tokens)
        all_bins = all_ids[:, 4, :seqs].reshape(-1)
        embedded = embedded.swapaxes(1, 2)
    else:
        own_ids = jnp.concatenate([token_ids.reshape(-1), target_ids.reshape(-1), time_bins])
        all_ids = lax.all_gather(own_ids, DP)
        all_tokens = all_ids[:, :tokens]
        all_targets = all_ids[:, tokens : 2 * tokens]
        all_bins = all_ids[:, 2 * tokens :].reshape(-1)
        own_rows = dp_index * emb_rows + jnp.arange(emb_rows)
        half_tokens = lax.dynamic_slice_in_dim(all_tokens, section * half, half, 1)
        picked = (half_tokens.reshape(-1)[:, None] == own_rows[None, :]).astype(bf16)
        found = jnp.dot(picked, embed, preferred_element_type=f32).astype(bf16)
        embedded = lax.all_gather(over_dp(found.reshape(dp_count, half, emb_width)), "section")
    embedded = embedded.astype(f32).reshape(seqs, length, emb_width)

    head_rows = head.shape[0]
    swapped = [(0, 1), (1, 0)]
    if straight:
        head_own = jnp.pad(head, ((0, -head_rows % 512), (0, 0)))
        each = head_own.shape[0] // 2
        early = lax.ppermute(head_own[:each], "section", swapped)
        early, late, embedded = lax.optimization_barrier((early, head_own[each:], embedded))
        late = lax.ppermute(late, "section", swapped)
    else:
        head_group = lax.all_gather(lax.all_gather(head, "core"), "section")
        head_group = head_group.reshape(-1, model_width)
        vocab_base = (
            (jnp.arange(sections)[:, None] * chips + chip) * cores + jnp.arange(cores)[None, :]
        ) * head_rows
        columns = (vocab_base[:, :, None] + jnp.arange(head_rows)[None, None, :]).reshape(-1)

    noise_level = levels_of(time_bins, sigma_table)
    unit_factor = lax.rsqrt(jnp.mean(embedded * embedded, -1, keepdims=True) + epsilon)
    level_col = noise_level[:, None, None]
    noise_scale = lax.rsqrt(level_col * level_col + 1.0)
    noisy_rows = ((embedded * unit_factor + level_col * noise) * noise_scale).astype(bf16)
    time_feats = time_features(noise_level)
    conditioned = jnp.dot(time_feats, w_time[0].astype(f32), precision=highest) + norm_gain[0]
    scale_attn = conditioned[:, None, :model_width]
    scale_mlp = conditioned[:, None, model_width:]
    scale = conditioned[:, None, :]
    weights = (w_qkv[0], w_out[0], w_up[0], b_hidden[0], w_down[0])
    stacked = (w_qkv, w_out, w_up, b_hidden, w_down)
    stream0 = mm("nse,ed->nsd", noisy_rows, w_in)
    flat = (tokens, model_width)
    if straight:
        block_out, final_rows, *kept = forward_pass(
            stream0.reshape(flat), scale, stacked, out_gain[None, :], 1
        )
        late, final_rows = lax.optimization_barrier((late, final_rows))
        heads = [head_own, lax.ppermute(head_own, "core", swapped), early, late]
        heads.append(lax.ppermute(early, "core", swapped))
    else:
        first_out = layer_forward(stream0, scale_attn, scale_mlp, weights)[0].astype(bf16)
        arrived = lax.ppermute(first_out, "section", swapped)
        stream = jnp.where(is_first, stream0, arrived.astype(f32))
        block_out, kept = layer_forward(stream, scale_attn, scale_mlp, weights)
        final_normed, final_factor = norm_rows(block_out.astype(bf16).astype(f32))
        final_rows = (final_normed * out_gain).astype(bf16).reshape(flat)

    targets_group = lax.dynamic_slice_in_dim(
        all_targets.reshape(chips, cores, tokens), core, 1, 1
    )[:, 0]
    targets_group = lax.dynamic_slice_in_dim(targets_group, section * half, half, 1)
    if straight:
        grad_final, grad_head, lse, picks = head_pass(
            final_rows, targets_group.reshape(line, 1, tokens), heads, line, head_rows, length, 3
        )
        ce_part = jnp.sum(lse) / chips - jnp.sum(picks)
    else:
        targets_group = targets_group.reshape(-1)
        handed = lax.ppermute(final_rows[:half], "section", [(1, 0), (0, 1)])
        own_final = jnp.where(is_first, handed, final_rows[half:])
        group_final = lax.all_gather(own_final, ("line", "pair"), tiled=True)
        logits = mm("td,vd->tv", group_final, head_group)
        local_top = jnp.max(logits, -1)
        local_total = jnp.sum(jnp.exp(logits - local_top[:, None]), -1)
        mark = columns[None, :] == targets_group[:, None]
        local_pick = jnp.sum(jnp.where(mark, logits, 0.0))
        stats = lax.all_gather(jnp.stack([local_top, local_total]), ("line", "pair"))
        all_top = jnp.max(stats[:, 0], 0)
        all_total = jnp.sum(stats[:, 1] * jnp.exp(stats[:, 0] - all_top), 0)
        log_total = all_top + jnp.log(all_total)
        soft_rows = jnp.exp(logits - log_total[:, None])
        logit_grads = ((soft_rows - jnp.where(mark, 1.0, 0.0)) / length).astype(bf16)
        grad_final = jnp.dot(logit_grads, head_group, preferred_element_type=f32).astype(bf16)
        grad_final = lax.psum_scatter(grad_final, ("line", "pair"), scatter_dimension=0, tiled=True)
        handed = lax.ppermute(grad_final, "section", swapped)
        grad_final = jnp.concatenate([handed, grad_final], 0)
        grad_head = mm("tv,td->vd", logit_grads, group_final).astype(bf16)
        grad_head = grad_head.reshape(sections, cores, head_rows, model_width)
        grad_head = lax.psum_scatter(grad_head, "core", scatter_dimension=1)
        grad_head = lax.psum_scatter(grad_head, "section", scatter_dimension=0).astype(f32)

        ce_part = jnp.sum(log_total) / chips - local_pick
    if straight:
        grad_second, grad_top, out_part = backward_pass(
            grad_final, block_out, out_gain[None, :], scale, kept, stacked
        )
        returned = lax.ppermute(grad_second, "section", swapped)
        out_part = out_part.reshape(-1)
        x, joined, mixed, middle, entry_attn, entry_mlp, slope, hidden = kept
        grad_middle, grad_entry, grad_bias, down_part, up_part = backward_begin(
            returned, grad_top, seqs, hidden, entry_mlp, slope, w_up, w_down
        )
        parts = [by_owner(down_part), by_owner(up_part)]
        grad_bias = grad_bias.reshape(-1)
    else:
        grad_final = grad_final.astype(f32).reshape(stream0.shape)
        out_part = jnp.sum(grad_final * final_normed, (0, 1))
        grad_top = norm_back(grad_final * out_gain, final_normed, final_factor)
        grad_second = layer_backward(grad_top, kept, scale_attn, scale_mlp, weights, False)[0]
        returned = lax.ppermute(grad_second.astype(bf16), "section", swapped)
        grad_cot = jnp.where(is_first, returned.astype(f32), grad_top)
        grad_stream, grads = layer_backward(grad_cot, kept, scale_attn, scale_mlp, weights, True)
        grad_first = grad_stream.astype(bf16)
    out_part = jnp.where(is_first, 0.0, out_part)

    ce_high = ce_part.astype(bf16).astype(f32)
    ce_mid = (ce_part - ce_high).astype(bf16).astype(f32)
    ce_low = ce_part - ce_high - ce_mid
    shared = jnp.concatenate([out_part, jnp.stack([ce_high, ce_mid, ce_low])])
    shared_rows = -(-shared.shape[0] // emb_width)
    shared = jnp.pad(shared, (0, shared_rows * emb_width - shared.shape[0]))
    shared = shared.reshape(-1, emb_width).astype(bf16)
    both = [shared, lax.ppermute(shared, "section", swapped)]

    cubed = unit_factor * unit_factor * unit_factor
    cond_rows = seqs * 2 * model_width // emb_width
    bias_rows = b_hidden.shape[1] // emb_width
    if straight:
        rest = jnp.concatenate([grad_bias.reshape(-1, emb_width)] + both, 0).astype(f32)
        rest = jnp.pad(rest, ((0, -(cond_rows + rest.shape[0]) % 16), (0, 0)))
        factors = [
            (value * noise_scale).reshape(tokens, 1) for value in (unit_factor, cubed)
        ]
        owned = noisy_rows.reshape(tokens, sections, dp_count, -1)
        owned = owned.swapaxes(1, 2).reshape(tokens, emb_width)
        far = [grad_middle, grad_entry, middle, x, joined, mixed, entry_attn, w_out, w_qkv]
        grad_down, grad_up, grad_qkv, grad_wout, grad_w_in, grad_head, smalls, rows_all = tail_pass(
            scale,
            rest,
            factors,
            embedded.reshape(tokens, emb_width),
            owned,
            w_in,
            far,
            parts,
            grad_head,
            2,
        )
        ids = all_tokens.reshape(1, -1)
        grad_down, grad_up, grad_qkv, grad_wout, grad_head, grad_embed = finish(
            ids,
            rows_all.reshape(-1, emb_width),
            [grad_down, grad_up, grad_qkv, grad_wout, grad_head],
            line,
            head_rows,
            emb_rows // sections,
        )
    else:
        in_part = mm("nse,nsd->ed", noisy_rows, grad_first).astype(bf16)
        in_part = in_part.reshape(sections, dp_count, -1, model_width).swapaxes(0, 1)
        in_sum = over_dp(in_part).astype(f32)
        in_handed = lax.ppermute(in_sum[1], "section", swapped)
        grad_w_in = jnp.where(is_first, in_sum[0], in_handed)
        grad_noisy = mm("nsd,ed->nse", grad_first, w_in)
        grad_unit = grad_noisy * noise_scale
        grad_embedded = unit_factor * grad_unit - cubed * embedded * jnp.mean(
            grad_unit * embedded, -1, keepdims=True
        )
        grad_flat = grad_embedded.reshape(tokens, emb_width).astype(bf16)
        handed = lax.ppermute(grad_flat, "section", swapped)
        rows_all = lax.all_gather(jnp.where(is_first, grad_flat, handed), DP)
        small = [grads["cond"].reshape(-1, emb_width), grads["bias"].reshape(-1, emb_width)]
        smalls = lax.all_gather(
            jnp.concatenate([value.astype(bf16) for value in small] + both, 0), DP
        )
        grad_down, grad_up, grad_qkv, grad_wout = [
            over_dp(part.reshape((dp_count,) + part.shape[3:])).astype(f32)
            for part in (grads["down"], grads["up"], grads["qkv"], grads["out"])
        ]
        grad_all = rows_all.reshape(-1, emb_width)
        out_rows = emb_rows // sections
        target_rows = (section * dp_count + dp_index) * out_rows + jnp.arange(out_rows)
        place = (target_rows[:, None] == all_tokens.reshape(-1)[None, :]).astype(bf16)
        grad_embed = jnp.dot(place, grad_all, preferred_element_type=f32)

    smalls = smalls.reshape(dp_count, -1, emb_width).astype(f32)
    cond_all = smalls[:, :cond_rows].reshape(dp_count * seqs, 2 * model_width)
    bias_all = smalls[:, cond_rows : cond_rows + bias_rows].reshape(dp_count, -1)
    hidden_rows = bias_all.shape[1] // dp_count
    grad_bias = jnp.sum(
        lax.dynamic_slice_in_dim(bias_all, dp_index * hidden_rows, hidden_rows, 1), 0
    )
    norm_cols = 2 * model_width // dp_count
    grad_gain = jnp.sum(lax.dynamic_slice_in_dim(cond_all, dp_index * norm_cols, norm_cols, 1), 0)
    feats_all = time_features(levels_of(all_bins, sigma_table))
    feat_rows = TFEAT // dp_count
    feats_own = lax.dynamic_slice_in_dim(feats_all, dp_index * feat_rows, feat_rows, 1)
    grad_time = jnp.dot(feats_own.T, cond_all, precision=highest)
    shared_first = cond_rows + bias_rows
    both = smalls[:, shared_first : shared_first + 2 * shared_rows]
    both = jnp.sum(both.reshape(dp_count, 2, -1), (0, 1))
    loss = jnp.sum(both[model_width : model_width + 3]) / (tokens * dp_count)
    gain_rows = model_width // dp_count
    grad_out_gain = lax.dynamic_slice_in_dim(both, dp_index * gain_rows, gain_rows)
    return (
        loss,
        grad_embed,
        grad_w_in,
        grad_time[None],
        grad_gain[None],
        grad_qkv[None],
        grad_wout[None],
        grad_up[None],
        grad_bias[None],
        grad_down[None],
        grad_out_gain,
        grad_head,
    )


def solution(mesh):
    sections, dp_count = mesh.shape["section"], mesh.shape["dp"]
    fine = Mesh(mesh.devices.reshape(sections, dp_count // 4, 2, 2), ("section",) + DP)
    everywhere = ("section",) + DP
    in_specs = (
        P(DP, None),
        P(DP, None),
        P(DP),
        P(),
        P(DP, None, None),
        P(DP, None),
        P(),
        P("section", None, None),
        P("section", None),
        P("section", None, None),
        P("section", None, None),
        P("section", None, None),
        P("section", None),
        P("section", None, None),
        P(),
        P(everywhere, None),
    )
    out_specs = (
        P(),
        P(everywhere, None),
        P(everywhere, None),
        P("section", DP, None),
        P("section", DP),
        P("section", DP, None),
        P("section", DP, None),
        P("section", DP, None),
        P("section", DP),
        P("section", DP, None),
        P(DP),
        P(everywhere, None),
    )
    return jax.shard_map(local, mesh=fine, in_specs=in_specs, out_specs=out_specs, check_vma=False)
```

```python
from functools import partial
import math

import jax
import jax.numpy as jnp
from jax import lax
from jax.experimental import pallas as pl
from jax.experimental.pallas import tpu as pltpu
from jax.sharding import Mesh, PartitionSpec as P

HEADS = 16
HEAD_DIM = 64
TFEAT = 256

epsilon = 1e-05
highest = lax.Precision.HIGHEST
f32 = jnp.float32
bf16 = jnp.bfloat16
DP = ("line", "pair", "core")


MESH = pl.DeviceIdType.MESH


def nt(left, right):
    return lax.dot_general(left, right, (((1,), (1,)), ((), ())), preferred_element_type=f32)


def tn(left, right):
    return lax.dot_general(left, right, (((0,), (0,)), ((), ())), preferred_element_type=f32)


def nn(left, right):
    return jnp.dot(left, right, preferred_element_type=f32)


def greet(peers):
    barrier = pltpu.get_barrier_semaphore()
    for peer in peers:
        pl.semaphore_signal(barrier, inc=1, device_id=peer, device_id_type=MESH)
    pl.semaphore_wait(barrier, len(peers))


def remote(source, target, send, recv, peer):
    return pltpu.make_async_remote_copy(
        src_ref=source,
        dst_ref=target,
        send_sem=send,
        recv_sem=recv,
        device_id=peer,
        device_id_type=MESH,
    )


def ring_place(position, line):
    turned = position // line
    return position * (1 - turned) + (2 * line - 1 - position) * turned, turned


def start_kernel(line, *refs):
    ids, embed, head, all_ids, out, head_early, head_core = refs[:7]
    table, found, own, from_core, from_pair, from_line = refs[7:13]
    ids_send, ids_recv, own_sem, core_send, core_recv, pair_send, pair_recv = refs[13:20]
    line_send, line_recv, swap_send, swap_recv, head_send, head_recv = refs[20:]
    me_section = lax.axis_index("section")
    me_line = lax.axis_index("line")
    me_pair = lax.axis_index("pair")
    me_core = lax.axis_index("core")
    section_peer = {"section": 1 - me_section}
    core_peer = {"core": 1 - me_core}
    pair_peer = {"pair": 1 - me_pair}
    peers = []
    for step in range(1, line * 4):
        peers.append(
            {
                "line": lax.rem(me_line + step // 4, line),
                "pair": lax.rem(me_pair + step // 2 % 2, 2),
                "core": lax.rem(me_core + step % 2, 2),
            }
        )
    greet(peers + [section_peer])
    each = head_early.shape[0]
    to_section = remote(
        head.at[pl.ds(0, each)], head_early, head_send.at[0], head_recv.at[0], section_peer
    )
    to_section.start()
    to_other_core = remote(head, head_core, head_send.at[1], head_recv.at[1], core_peer)
    place = all_ids.at[me_line, me_pair, me_core]
    copies = [remote(ids, place, ids_send.at[n], ids_recv.at[n], peer) for n, peer in enumerate(peers)]
    for copy in copies:
        copy.start()
    keep = pltpu.make_async_copy(ids, place, own_sem)
    keep.start()
    rows = embed.shape[0]
    high = table.shape[1]
    half = out.shape[-1]
    padded = jnp.concatenate(
        [embed[...].astype(f32), jnp.zeros((high - rows, embed.shape[1]), f32)], 0
    )
    table[...] = padded.T.astype(bf16)
    keep.wait()
    for copy in copies:
        copy.wait_recv()
    base = ((me_line * 2 + me_pair) * 2 + me_core) * rows

    def pick(spot, pair, core):
        wanted = all_ids[spot, pair, core, pl.ds(me_section, 1), :][:, :half]
        entry = lax.broadcasted_iota(jnp.int32, (high, half), 0)
        entry = jnp.where(entry < rows, entry + base, -1)
        hot = jnp.where(entry == wanted, 1.0, 0.0).astype(bf16)
        return nn(table[...], hot).astype(bf16)

    def core_copy(spot, pair, turn):
        return remote(
            found.at[turn, spot],
            from_core.at[turn, spot],
            core_send.at[turn, spot],
            core_recv.at[turn, spot],
            core_peer,
        )

    def pair_copy(spot):
        return remote(
            from_core.at[0, spot], from_pair.at[spot], pair_send.at[spot], pair_recv.at[spot], pair_peer
        )

    def line_copy(step):
        spot = lax.rem(me_line + step, line)
        return remote(
            from_core.at[1, spot],
            from_line.at[step - 1],
            line_send.at[step - 1],
            line_recv.at[step - 1],
            {"line": spot},
        )

    order = [lax.rem(me_line + step, line) for step in list(range(1, line)) + [0]]
    for turn, pair in enumerate((1 - me_pair, me_pair)):

        @pl.loop(0, line)
        def _(step):
            spot = lax.rem(me_line + 1 + step, line)
            found[turn, spot] = pick(spot, pair, 1 - me_core)
            core_copy(spot, pair, turn).start()
            own[turn, spot] = pick(spot, pair, me_core)

        if turn == 0:
            for spot in order:
                core_copy(spot, pair, 0).wait_recv()
                from_core[0, spot] = from_core[0, spot] + own[0, spot]
                pair_copy(spot).start()
    for step in list(range(1, line)) + [0]:
        spot = lax.rem(me_line + step, line)
        core_copy(spot, me_pair, 1).wait_recv()
        pair_copy(spot).wait_recv()
        from_core[1, spot] = from_core[1, spot] + own[1, spot] + from_pair[spot]
        if step:
            line_copy(step).start()
    to_other_core.start()
    total = from_core[1, me_line]
    for step in range(1, line):
        line_copy(step).wait_recv()
        total = total + from_line[step - 1]
    out[me_section] = total
    swap = remote(out.at[me_section], out.at[me_section], swap_send, swap_recv, section_peer)
    swap.start()
    for copy in copies:
        copy.wait_send()
    for spot in range(line):
        for turn in range(2):
            core_copy(spot, me_pair, turn).wait_send()
        pair_copy(spot).wait_send()
    for step in range(1, line):
        line_copy(step).wait_send()
    swap.wait()
    to_section.wait()
    to_other_core.wait()


def start_pass(ids, embed, head, half, line, collective_id):
    rows, width = embed.shape
    high = -(-rows // 256) * 256
    vmem = pl.BlockSpec(memory_space=pltpu.VMEM)
    anywhere = pl.BlockSpec(memory_space=pl.ANY)
    dma = pltpu.SemaphoreType.DMA
    block = (width, half)
    return pl.pallas_call(
        partial(start_kernel, line),
        out_shape=[
            jax.ShapeDtypeStruct((line, 2, 2) + ids.shape, ids.dtype),
            jax.ShapeDtypeStruct((2,) + block, bf16),
            jax.ShapeDtypeStruct((head.shape[0] // 2, head.shape[1]), bf16),
            jax.ShapeDtypeStruct(head.shape, bf16),
        ],
        in_specs=[vmem, vmem, anywhere],
        out_specs=[vmem, vmem, anywhere, anywhere],
        scratch_shapes=[
            pltpu.VMEM((width, high), bf16),
            pltpu.VMEM((2, line) + block, bf16),
            pltpu.VMEM((2, line) + block, bf16),
            pltpu.VMEM((2, line) + block, bf16),
            pltpu.VMEM((line,) + block, bf16),
            pltpu.VMEM((line - 1,) + block, bf16),
            dma((line * 4 - 1,)),
            dma((line * 4 - 1,)),
            dma,
            dma((2, line)),
            dma((2, line)),
            dma((line,)),
            dma((line,)),
            dma((line - 1,)),
            dma((line - 1,)),
            dma,
            dma,
            dma((2,)),
            dma((2,)),
        ],
        compiler_params=pltpu.CompilerParams(
            collective_id=collective_id, has_side_effects=True, vmem_limit_bytes=40 * 2**20
        ),
        cost_estimate=pl.CostEstimate(flops=0, bytes_accessed=2**27, transcendentals=0),
    )(ids, embed, head)


def head_kernel(line, head_rows, length, *refs):
    final, targets, *heads = refs[:7]
    out, grads, lse_out, pick_out = refs[7:11]
    (table, rows_all, logits, probs, acc, parts, from_pair, from_line, stats, done) = refs[11:21]
    (head_sem, own_sem, give_send, give_recv, along_send, along_recv, pair_send, pair_recv) = refs[21:29]
    (stat_send, stat_recv, sum_send, sum_recv, line_send, line_recv, back_send, back_recv) = refs[29:37]
    last_send, last_recv = refs[37:]
    half = final.shape[0] // 2
    width = 2 * half
    padded = heads[0].shape[0]
    me_section = lax.axis_index("section")
    me_line = lax.axis_index("line")
    me_pair = lax.axis_index("pair")
    me_core = lax.axis_index("core")
    section_peer = {"section": 1 - me_section}
    pair_peer = {"pair": 1 - me_pair}
    chip_peers = []
    for step in range(1, 2 * line):
        chip_peers.append(
            {"line": lax.rem(me_line + step // 2, line), "pair": lax.rem(me_pair + step % 2, 2)}
        )
    greet(chip_peers + [section_peer, {"core": 1 - me_core}])

    def side(pair):
        return pl.ds(pl.multiple_of(pair * half, 16), half)

    loads = []
    for n, part in enumerate(heads):
        first = sum(other.shape[0] for other in heads[:n])
        target = table.at[pl.ds(first, part.shape[0])]
        loads.append(pltpu.make_async_copy(part, target, head_sem.at[n]))
    late = heads[3]
    last = remote(
        late,
        table.at[pl.ds(4 * padded - late.shape[0], late.shape[0])],
        last_send,
        last_recv,
        {"core": 1 - me_core},
    )
    last.start()
    for load in loads:
        load.start()

    quarter = half // 2

    def token_rows(place, pair, chunk):
        first = place * width + pair * half + chunk * quarter
        return pl.ds(pl.multiple_of(first, 16), quarter)

    def group(place):
        return pl.ds(pl.multiple_of(place * width, 128), width)

    def column_block(place, chunk):
        return rows_all.at[token_rows(place, me_pair, chunk)]

    def give(chunk):
        return remote(
            final.at[pl.ds(chunk * quarter, quarter)],
            column_block(me_line, chunk),
            give_send.at[chunk],
            give_recv.at[chunk],
            section_peer,
        )

    def along(step, way, chunk):
        block = column_block(me_line - way * step, chunk)
        turn = (way + 1) // 2
        return remote(
            block,
            block,
            along_send.at[turn, step, chunk],
            along_recv.at[turn, step, chunk],
            {"line": me_line + way},
        )

    def inside(place):
        return (place >= 0) & (place < line)

    def sends_along(step, way):
        return inside(me_line - way * step) & inside(me_line + way)

    def sideways(place, chunk):
        block = column_block(place, chunk)
        return remote(
            block, block, pair_send.at[place, chunk], pair_recv.at[place, chunk], pair_peer
        )

    def arrived_sideways(place, chunk):
        block = rows_all.at[token_rows(place, 1 - me_pair, chunk)]
        return remote(
            block, block, pair_send.at[place, chunk], pair_recv.at[place, chunk], pair_peer
        )

    @pl.when(me_section == 1)
    def _():
        for chunk in range(2):
            give(chunk).start()
        for chunk in range(2):
            keep = pltpu.make_async_copy(
                final.at[pl.ds(half + chunk * quarter, quarter)],
                column_block(me_line, chunk),
                own_sem.at[chunk],
            )
            keep.start()
            keep.wait()

    for chunk in range(2):

        @pl.when(me_section == 0)
        def _():
            give(chunk).wait_recv()

        for way in (1, -1):

            @pl.when(sends_along(0, way))
            def _():
                along(0, way, chunk).start()

        sideways(me_line, chunk).start()

    def pass_on(step):
        for chunk in range(2):
            for way in (1, -1):
                place = me_line - way * step

                @pl.when(inside(place))
                def _():
                    block = column_block(place, chunk)
                    turn = (way + 1) // 2
                    remote(
                        block,
                        block,
                        along_send.at[turn, step - 1, chunk],
                        along_recv.at[turn, step - 1, chunk],
                        {"line": me_line - way},
                    ).wait_recv()

                    @pl.when(inside(me_line + way))
                    def _():
                        along(step, way, chunk).start()

                    sideways(place, chunk).start()

    nearest = []
    for own in range(line):
        near = [own]
        for step in range(1, line):
            near += [place for place in (own - step, own + step) if 0 <= place < line]
        nearest.append(near)

    def by_distance(turn):
        place = 0
        for own in range(line):
            for n in range(line):
                hit = ((me_line == own) & (turn == n)).astype(jnp.int32)
                place = place + hit * nearest[own][n]
        return place

    def vocabulary(tile, rows):
        shard = tile * rows // padded
        first = lax.rem(tile * rows, padded)
        shard_section = lax.rem(me_section + shard // 2, 2)
        shard_core = lax.rem(me_core + lax.rem(shard, 2), 2)
        base = (((shard_section * line + me_line) * 2 + me_pair) * 2 + shard_core) * head_rows
        row = lax.broadcasted_iota(jnp.int32, (rows, 1), 0) + first
        return jnp.where(row < head_rows, row + base, -1)

    tile_rows = 512
    tiles = 4 * padded // tile_rows
    lowest = -1e30

    def score(turn, tops):
        place = by_distance(turn) if turn < line else None
        before = by_distance(turn - 1) if turn > 0 else None
        wanted = None if place is None else targets[place]

        def one(tile, carry):
            rows = pl.ds(pl.multiple_of(tile * tile_rows, tile_rows), tile_rows)
            out = []
            if place is not None:
                top, pick = carry[:2]
                entry = vocabulary(tile, tile_rows)
                part = nt(table[rows, :], rows_all[group(place), :])
                part = jnp.where(entry >= 0, part, lowest)
                logits[turn % 2, rows, :] = part
                out.append(jnp.maximum(top, jnp.max(part, 0, keepdims=True)))
                out.append(
                    pick + jnp.sum(jnp.where(entry == wanted, part, 0.0), 0, keepdims=True)
                )
            if before is not None:
                value = jnp.exp(logits[(turn - 1) % 2, rows, :] - tops)
                probs[rows, group(before)] = value.astype(bf16)
                out.append(carry[-1] + jnp.sum(value, 0, keepdims=True))
            return tuple(out)

        none = jnp.zeros((1, width), f32)
        start = () if place is None else (jnp.full((1, width), lowest, f32), none)
        start += () if before is None else (none,)
        result = lax.fori_loop(0, tiles, one, start)
        if place is not None:
            pick_out[place] = result[1]
        if before is not None:
            own = stats.at[me_line, me_pair, before]
            own[:, 0:width] = tops
            own[:, width : 2 * width] = result[-1]
            for n in range(len(chip_peers)):
                stat_copy(n, before).start()
        return None if place is None else result[0]

    def stat_copy(n, place):
        own = stats.at[me_line, me_pair, place]
        return remote(own, own, stat_send.at[n, place], stat_recv.at[n, place], chip_peers[n])

    def stat_wait(n, place):
        peer = chip_peers[n]
        source_line = lax.rem(2 * me_line + line - peer["line"], line)
        source_pair = peer["pair"]
        block = stats.at[source_line, source_pair, place]
        remote(block, block, stat_send.at[n, place], stat_recv.at[n, place], peer).wait_recv()

    for load in loads:
        load.wait()
    last.wait()

    tops = None
    for turn in range(line + 1):
        if turn + 1 < line:
            pass_on(turn + 1)
        if turn < line:
            for chunk in range(2):
                arrived_sideways(by_distance(turn), chunk).wait_recv()
        tops = score(turn, tops)

    def part_rows(pair, chunk):
        return pl.ds(pl.multiple_of(pair * half + chunk * quarter, 16), quarter)

    def sum_copy(turn, chunk):
        place = lax.rem(me_line + turn + 1, line)
        return remote(
            parts.at[place, part_rows(1 - me_pair, chunk)],
            from_pair.at[turn, pl.ds(chunk * quarter, quarter)],
            sum_send.at[turn, chunk],
            sum_recv.at[turn, chunk],
            pair_peer,
        )

    def line_copy(turn, chunk):
        place = lax.rem(me_line + turn + 1, line)
        return remote(
            parts.at[place, part_rows(me_pair, chunk)],
            from_line.at[turn, pl.ds(chunk * quarter, quarter)],
            line_send.at[turn, chunk],
            line_recv.at[turn, chunk],
            {"line": place},
        )

    def finish(turn, chunk):
        place = lax.rem(me_line + turn + 1, line)
        sum_copy(turn, chunk).wait_recv()
        own = parts.at[place, part_rows(me_pair, chunk)]
        other = from_pair.at[turn, pl.ds(chunk * quarter, quarter)]

        @pl.loop(0, quarter // 16)
        def _(block):
            rows = pl.ds(pl.multiple_of(block * 16, 16), 16)
            own[rows, :] = (own[rows, :].astype(f32) + other[rows, :].astype(f32)).astype(bf16)

    @pl.loop(0, line)
    def _(turn):
        place = lax.rem(me_line + turn + 1, line)
        for n in range(len(chip_peers)):
            stat_wait(n, place)
        tops = [stats[a, b, place, :, 0:width] for a in range(line) for b in range(2)]
        totals = [
            stats[a, b, place, :, width : 2 * width] for a in range(line) for b in range(2)
        ]
        top = tops[0]
        for value in tops[1:]:
            top = jnp.maximum(top, value)
        total = jnp.zeros_like(top)
        for peak, part in zip(tops, totals):
            total = total + part * jnp.exp(peak - top)
        lse = top + jnp.log(total)
        lse_out[place] = lse
        factor = jnp.exp(stats[me_line, me_pair, place, :, 0:width] - lse) / length
        wanted = targets[place]

        def scaled(tile):
            rows = pl.ds(tile * padded, padded)
            entry = vocabulary(tile, padded)
            grad = probs[rows, group(place)].astype(f32) * factor
            grad = (grad - jnp.where(entry == wanted, 1.0 / length, 0.0)).astype(bf16)
            probs[rows, group(place)] = grad
            return grad

        grad = scaled(0)
        for tile in range(4):
            product = tn(grad, table[pl.ds(tile * padded, padded), :])
            if tile < 3:
                grad = scaled(tile + 1)
                acc[...] = product if tile == 0 else acc[...] + product
            else:
                parts[place] = (acc[...] + product).astype(bf16)

        for chunk in range(2):
            sum_copy(turn, chunk).start()

        @pl.when(turn > 0)
        def _():
            for chunk in range(2):
                finish(turn - 1, chunk)
                line_copy(turn - 1, chunk).start()

    gh_rows = 256
    gh_tiles = 4 * padded // gh_rows

    def head_grads(first, last):
        @pl.loop(first, last)
        def _(tile):
            rows = pl.ds(pl.multiple_of(tile * gh_rows, gh_rows), gh_rows)
            value = jnp.dot(probs[rows, :], rows_all[...], preferred_element_type=f32)
            grads[rows, :] = value.astype(bf16)

    def back(chunk):
        part = pl.ds(chunk * quarter, quarter)
        return remote(
            done.at[part], out.at[part], back_send.at[chunk], back_recv.at[chunk], section_peer
        )

    head_grads(0, gh_tiles // 2)
    for chunk in range(2):
        finish(line - 1, chunk)
        for turn in range(line - 1):
            line_copy(turn, chunk).wait_recv()
        own = parts.at[me_line, part_rows(me_pair, chunk)]

        @pl.loop(0, quarter // 16)
        def _(block):
            rows = pl.ds(pl.multiple_of(block * 16, 16), 16)
            chunk_rows = pl.ds(pl.multiple_of(chunk * quarter + block * 16, 16), 16)
            value = own[rows, :].astype(f32)
            for turn in range(line - 1):
                value = value + from_line[turn, chunk_rows, :].astype(f32)
            done[chunk_rows, :] = value.astype(bf16)

        @pl.when(me_section == 0)
        def _():
            back(chunk).start()

    @pl.when(me_section == 0)
    def _():
        out[...] = jnp.zeros_like(out)

    @pl.when(me_section == 1)
    def _():
        out[pl.ds(half, half), :] = done[...]

    head_grads(gh_tiles // 2, gh_tiles)
    for chunk in range(2):

        @pl.when(me_section == 0)
        def _():
            back(chunk).wait_send()

        @pl.when(me_section == 1)
        def _():
            back(chunk).wait_recv()
            give(chunk).wait_send()

        for way in (1, -1):
            for step in range(line - 1):

                @pl.when(sends_along(step, way))
                def _():
                    along(step, way, chunk).wait_send()

        for place in range(line):
            sideways(place, chunk).wait_send()
        for turn in range(line):
            sum_copy(turn, chunk).wait_send()
        for turn in range(line - 1):
            line_copy(turn, chunk).wait_send()
    for place in range(line):
        for n in range(len(chip_peers)):
            stat_copy(n, place).wait_send()


def head_pass(final, targets, heads, line, head_rows, length, collective_id):
    tokens, deep = final.shape
    half = tokens // 2
    padded = heads[0].shape[0]
    vmem = pl.BlockSpec(memory_space=pltpu.VMEM)
    anywhere = pl.BlockSpec(memory_space=pl.ANY)
    dma = pltpu.SemaphoreType.DMA
    peers = 2 * line - 1
    return pl.pallas_call(
        partial(head_kernel, line, head_rows, length),
        out_shape=[
            jax.ShapeDtypeStruct((tokens, deep), bf16),
            jax.ShapeDtypeStruct((4 * padded, deep), bf16),
            jax.ShapeDtypeStruct((line, 1, tokens), f32),
            jax.ShapeDtypeStruct((line, 1, tokens), f32),
        ],
        in_specs=[vmem, vmem] + [anywhere] * len(heads),
        out_specs=[vmem] * 4,
        scratch_shapes=[
            pltpu.VMEM((4 * padded, deep), bf16),
            pltpu.VMEM((line * tokens, deep), bf16),
            pltpu.VMEM((2, 4 * padded, tokens), f32),
            pltpu.VMEM((4 * padded, line * tokens), bf16),
            pltpu.VMEM((tokens, deep), f32),
            pltpu.VMEM((line, tokens, deep), bf16),
            pltpu.VMEM((line, half, deep), bf16),
            pltpu.VMEM((line - 1, half, deep), bf16),
            pltpu.VMEM((line, 2, line, 1, 2 * tokens), f32),
            pltpu.VMEM((half, deep), bf16),
            dma((len(heads),)),
            dma((2,)),
            dma((2,)),
            dma((2,)),
            dma((2, line, 2)),
            dma((2, line, 2)),
            dma((line, 2)),
            dma((line, 2)),
            dma((peers, line)),
            dma((peers, line)),
            dma((line, 2)),
            dma((line, 2)),
            dma((line, 2)),
            dma((line, 2)),
            dma((2,)),
            dma((2,)),
            dma,
            dma,
        ],
        compiler_params=pltpu.CompilerParams(
            collective_id=collective_id, has_side_effects=True, vmem_limit_bytes=60 * 2**20
        ),
        cost_estimate=pl.CostEstimate(
            flops=24 * line * padded * tokens * deep, bytes_accessed=2**28, transcendentals=0
        ),
    )(final, targets, *heads)


def row_stats(values):
    centred = values - jnp.mean(values, -1, keepdims=True)
    factor = lax.rsqrt(jnp.mean(centred * centred, -1, keepdims=True) + epsilon)
    return centred * factor, factor


def two_heads(block):
    first = lax.broadcasted_iota(jnp.int32, block.shape, 1) < HEAD_DIM
    zero = jnp.zeros_like(block)
    return jnp.concatenate([jnp.where(first, block, zero), jnp.where(first, zero, block)], 0)


def one_block(stacked):
    rows = stacked.shape[0] // 2
    first = lax.broadcasted_iota(jnp.int32, (rows, stacked.shape[1]), 1) < HEAD_DIM
    return jnp.where(first, stacked[:rows], stacked[rows:])


def attention_weights(queries, keys):
    scores = nt(keys, queries) * (1.0 / math.sqrt(HEAD_DIM))
    exped = jnp.exp(scores - jnp.max(scores, 0, keepdims=True))
    return exped * (1.0 / jnp.sum(exped, 0, keepdims=True))


def tile_of(index, size):
    return pl.ds(pl.multiple_of(index * size, size), size)


def forward_kernel(seqs, *refs):
    refs = list(refs)

    def take(number):
        return [refs.pop(0) for _ in range(number)]

    start, scale, bias, gain = take(4)
    weights = take(4)
    head, head_early = take(2)
    out, final, x, joined, mixed, middle, entry_attn, entry_mlp, slope, hidden = take(10)
    head_late, head_fourth = take(2)
    w_qkv, w_out, w_up, w_down, x_total, arrived, sems, relay_send, relay_recv = take(9)
    head_send, head_recv = refs
    width = start.shape[1]
    length = start.shape[0] // seqs
    me_section = lax.axis_index("section")
    section_peer = {"section": 1 - me_section}
    load_qkv, load_out, load_up, load_down = [
        pltpu.make_async_copy(source.at[0], target, sems.at[n])
        for n, (source, target) in enumerate(zip(weights, (w_qkv, w_out, w_up, w_down)))
    ]
    load_qkv.start()
    core_peer = {"core": 1 - lax.axis_index("core")}
    greet([section_peer, core_peer])
    each = head_early.shape[0]
    to_section = remote(
        head.at[pl.ds(each, each)], head_late, head_send.at[0], head_recv.at[0], section_peer
    )
    to_section.start()
    to_core = remote(head_early, head_fourth, head_send.at[1], head_recv.at[1], core_peer)
    to_core.start()

    def relay(seq):
        rows = pl.ds(seq * length, length)
        return remote(
            out.at[rows], arrived.at[rows], relay_send.at[seq], relay_recv.at[seq], section_peer
        )

    tile = 512

    def enter(seq):
        rows = pl.ds(seq * length, length)

        @pl.when(me_section == 0)
        def _():
            x[rows, :] = start[rows, :]

        @pl.when(me_section == 1)
        def _():
            relay(seq).wait_recv()
            x[rows, :] = arrived[rows, :].astype(f32)

        normed, _ = row_stats(x[rows, :])
        entry_attn[rows, :] = (normed * scale[seq, :, :width]).astype(bf16)

    def join(first, count):
        rows = pl.ds(first * length, count * length)

        @pl.loop(0, 3 * width // tile)
        def _(index):
            cols = tile_of(index, tile)
            joined[rows, cols] = nn(entry_attn[rows, :], w_qkv[:, cols]).astype(bf16)

    for seq in range(seqs - 1):
        enter(seq)
    load_qkv.wait()
    load_out.start()
    load_up.start()
    join(0, seqs - 1)
    enter(seqs - 1)
    join(seqs - 1, 1)
    load_out.wait()
    load_down.start()
    pairs = width // 128

    @pl.loop(0, pairs)
    def _(pair):
        cols = tile_of(pair, 128)
        for seq in range(seqs):
            rows = pl.ds(seq * length, length)
            queries = two_heads(joined[rows, cols])
            keys = joined[rows, tile_of(pair + pairs, 128)]
            values = joined[rows, tile_of(pair + 2 * pairs, 128)]
            probs = attention_weights(queries, keys).astype(bf16)
            mixed[rows, cols] = one_block(tn(probs, values)).astype(bf16)

    @pl.loop(0, width // tile)
    def _(index):
        cols = tile_of(index, tile)
        middle[:, cols] = x[:, cols] + nn(mixed[...], w_out[:, cols])

    for seq in range(seqs):
        rows = pl.ds(seq * length, length)
        normed, _ = row_stats(middle[rows, :])
        entry_mlp[rows, :] = (normed * scale[seq, :, width:]).astype(bf16)

    load_up.wait()
    load_down.wait()

    def gelu_of(up, rows, cols):
        bell = jnp.exp(-0.5 * up * up)
        near = 1.0 / (1.0 + (0.3275911 * math.sqrt(0.5)) * jnp.abs(up))
        tail = 0.5 * 1.061405429 * near - 0.5 * 1.453152027
        for term in (1.421413741, -0.284496736, 0.254829592):
            tail = tail * near + 0.5 * term
        tail = tail * near * bell
        below = jnp.where(up < 0.0, tail, 1.0 - tail)
        value = (up * below).astype(bf16)
        slope[rows, cols] = (below + up * bell * (1.0 / math.sqrt(2.0 * math.pi))).astype(bf16)
        hidden[rows, cols] = value
        return value

    def feed_forward(first, count):
        rows = pl.ds(first * length, count * length)

        def one(index, total):
            sides = [tile_of(2 * index + side, tile) for side in range(2)]
            ups = [nn(entry_mlp[rows, :], w_up[:, cols]) + bias[:, cols] for cols in sides]
            both = jnp.concatenate([gelu_of(up, rows, cols) for up, cols in zip(ups, sides)], 1)
            x_total[rows, :] += nn(both, w_down[tile_of(index, 2 * tile), :])
            return total

        x_total[rows, :] = middle[rows, :]
        lax.fori_loop(0, w_up.shape[1] // (2 * tile), one, 0)
        for seq in range(first, first + count):
            rows = pl.ds(seq * length, length)
            value = x_total[rows, :].astype(bf16)
            out[rows, :] = value

            @pl.when(me_section == 0)
            def _():
                relay(seq).start()

            normed, _ = row_stats(value.astype(f32))
            final[rows, :] = (normed * gain[...]).astype(bf16)

    feed_forward(0, seqs)

    to_section.wait()
    to_core.wait()

    @pl.when(me_section == 0)
    def _():
        for seq in range(seqs):
            relay(seq).wait_send()


def layer_scratch(width, hidden):
    return [
        pltpu.VMEM((width, 3 * width), bf16),
        pltpu.VMEM((width, width), bf16),
        pltpu.VMEM((width, hidden), bf16),
        pltpu.VMEM((hidden, width), bf16),
    ]


def forward_pass(start, scale, weights, gain, head, head_early, collective_id):
    w_qkv, w_out, w_up, b_hidden, w_down = weights
    tokens, width = start.shape
    wide = w_up.shape[-1]
    seqs = scale.shape[0]
    vmem = pl.BlockSpec(memory_space=pltpu.VMEM)
    anywhere = pl.BlockSpec(memory_space=pl.ANY)

    def low(columns):
        return (tokens, columns), bf16

    exact = ((tokens, width), f32)
    results = [low(width), low(width), exact, low(3 * width), low(width), exact, low(width)]
    results += [low(width), low(wide), low(wide)]
    results += [(head_early.shape, bf16)] * 2
    scratch = layer_scratch(width, wide) + [pltpu.VMEM(*exact), pltpu.VMEM(*low(width))]
    dma = pltpu.SemaphoreType.DMA
    flops = 4 * tokens * (4 * width * width + 2 * width * wide)
    return pl.pallas_call(
        partial(forward_kernel, seqs),
        out_shape=[jax.ShapeDtypeStruct(*item) for item in results],
        in_specs=[vmem] * 4 + [anywhere] * 6,
        out_specs=[vmem] * (len(results) - 2) + [anywhere] * 2,
        scratch_shapes=scratch + [dma((4,)), dma((seqs,)), dma((seqs,)), dma((2,)), dma((2,))],
        compiler_params=pltpu.CompilerParams(
            collective_id=collective_id, has_side_effects=True, vmem_limit_bytes=60 * 2**20
        ),
        cost_estimate=pl.CostEstimate(flops=2 * flops, bytes_accessed=2**25, transcendentals=0),
    )(start, scale, b_hidden, gain, w_qkv, w_out, w_up, w_down, head, head_early)


def norm_grads(source, total, grad_middle, scale, grad_cond, half, seq, store):
    width = total.shape[1]
    length = total.shape[0] // scale.shape[0]
    rows = pl.ds(seq * length, length)
    cols = pl.ds(half * width, width)
    normed, factor = row_stats(source[rows, :])
    gradient = total[rows, :]
    if grad_cond is not None:
        grad_cond[seq, :, cols] = jnp.sum(gradient * normed, 0, keepdims=True)
    scaled = gradient * scale[seq, :, cols]
    back = factor * (
        scaled
        - jnp.mean(scaled, -1, keepdims=True)
        - normed * jnp.mean(scaled * normed, -1, keepdims=True)
    )
    store(rows, grad_middle[rows, :] + back)


def attention_grads(joined, grad_mixed, grad_joined, pair, seqs):
    pairs = grad_mixed.shape[1] // 128
    length = grad_mixed.shape[0] // seqs
    shrink = 1.0 / math.sqrt(HEAD_DIM)
    cols = tile_of(pair, 128)
    key_cols = tile_of(pair + pairs, 128)
    value_cols = tile_of(pair + 2 * pairs, 128)
    for seq in range(seqs):
        rows = pl.ds(seq * length, length)
        queries = two_heads(joined[rows, cols])
        keys = joined[rows, key_cols]
        probs = attention_weights(queries, keys)
        grads = two_heads(grad_mixed[rows, cols])
        grad_probs = nt(joined[rows, value_cols], grads)
        inner = jnp.sum(grad_probs * probs, 0, keepdims=True)
        grad_scores = (probs * (grad_probs - inner)).astype(bf16)
        grad_joined[rows, cols] = (one_block(tn(grad_scores, keys)) * shrink).astype(bf16)
        grad_joined[rows, key_cols] = (nn(grad_scores, queries) * shrink).astype(bf16)
        grad_joined[rows, value_cols] = nn(probs.astype(bf16), grads).astype(bf16)


def backward_kernel(begin, seqs, *refs):
    refs = list(refs)

    def take(number):
        return [refs.pop(0) for _ in range(number)]

    if begin:
        incoming, other, hidden, entry = take(4)
        far = take(3)
        grad_middle, total, grad_bias, down_out, up_out = take(5)
        grad_low, grad_up, entry_turned, down_weight, up_weight, out_sem = take(6)
        near = take(3)
    else:
        scale, incoming, other, gain = take(4)
        far = take(8)
        out, grad_top, grad_gain = take(3)
        grad_low, grad_up, grad_attn, grad_joined = take(4)
        near = take(8)
        total, grad_middle, grad_mixed = take(3)
    (sems,) = refs
    if begin:
        slope, w_up, w_down = near
        load_slope = pltpu.make_async_copy(far[0], slope, sems.at[0])
        load_up = pltpu.make_async_copy(far[1].at[0], w_up, sems.at[1])
        load_down = pltpu.make_async_copy(far[2].at[0], w_down, sems.at[2])
    else:
        slope, w_up, w_down, x, middle, joined, w_qkv, w_out = near
        load_slope = pltpu.make_async_copy(far[0], slope, sems.at[0])
        load_up = pltpu.make_async_copy(far[1].at[0], w_up, sems.at[1])
        load_down = pltpu.make_async_copy(far[2].at[0], w_down, sems.at[2])
        load_x = pltpu.make_async_copy(far[3], x, sems.at[3])
        load_middle = pltpu.make_async_copy(far[4], middle, sems.at[4])
        load_joined = pltpu.make_async_copy(far[5], joined, sems.at[5])
        load_qkv = pltpu.make_async_copy(far[6].at[0], w_qkv, sems.at[6])
        load_out = pltpu.make_async_copy(far[7].at[0], w_out, sems.at[7])
    width = incoming.shape[1]
    length = incoming.shape[0] // seqs
    load_down.start()
    load_slope.start()
    if begin:
        entry_turned[...] = entry[...].T

    for seq in range(seqs):
        rows = pl.ds(seq * length, length)
        if begin:
            first = (lax.axis_index("section") == 0).astype(f32)
            value = incoming[rows, :].astype(f32) * first + other[rows, :] * (1.0 - first)
        else:
            normed, factor = row_stats(other[rows, :].astype(f32))
            gradient = incoming[rows, :].astype(f32)
            part = jnp.sum(gradient * normed, 0, keepdims=True)
            grad_gain[...] = part if seq == 0 else grad_gain[...] + part
            scaled = gradient * gain[...]
            value = factor * (
                scaled
                - jnp.mean(scaled, -1, keepdims=True)
                - normed * jnp.mean(scaled * normed, -1, keepdims=True)
            )
            grad_top[rows, :] = value
        grad_middle[rows, :] = value
        grad_low[rows, :] = value.astype(bf16)

    load_down.wait()
    load_slope.wait()
    load_up.start()
    if not begin:
        load_middle.start()
        load_out.start()
        load_joined.start()
    tile = 1024

    @pl.loop(0, w_up.shape[1] // tile)
    def _(index):
        cols = tile_of(index, tile)
        grad_hidden = nt(grad_low[...], w_down[cols, :])
        value = (grad_hidden * slope[:, cols].astype(f32)).astype(bf16)
        grad_up[:, cols] = value
        if begin:
            grad_bias[:, cols] = jnp.sum(value.astype(f32), 0, keepdims=True)
            down_weight[cols, :] = tn(hidden[:, cols], grad_low[...]).astype(bf16)
            pltpu.make_async_copy(
                down_weight.at[cols], down_out.at[cols], out_sem.at[0, index]
            ).start()
            up_weight[:, cols] = nn(entry_turned[...], value).astype(bf16)

    if begin:
        whole_up = pltpu.make_async_copy(up_weight, up_out, out_sem.at[1, 0])
        whole_up.start()
    load_up.wait()
    if not begin:
        load_middle.wait()
        load_out.wait()
        load_joined.wait()
        load_qkv.start()
        load_x.start()

    @pl.loop(0, width // 256)
    def _(index):
        total[:, tile_of(index, 256)] = nt(grad_up[...], w_up[tile_of(index, 256), :])

    if begin:
        for index in range(w_up.shape[1] // tile):
            cols = pl.ds(index * tile, tile)
            pltpu.make_async_copy(
                down_weight.at[cols], down_out.at[cols], out_sem.at[0, index]
            ).wait()
        whole_up.wait()
        return

    def store_middle(rows, value):
        grad_middle[rows, :] = value
        grad_attn[rows, :] = value.astype(bf16)

    for seq in range(seqs):
        norm_grads(middle, total, grad_middle, scale, None, 1, seq, store_middle)

    @pl.loop(0, width // 512)
    def _(index):
        part = tile_of(index, 512)
        grad_mixed[:, part] = nt(grad_attn[...], w_out[part, :]).astype(bf16)

    @pl.loop(0, width // 128)
    def _(pair):
        attention_grads(joined, grad_mixed, grad_joined, pair, seqs)

    load_qkv.wait()
    load_x.wait()

    @pl.loop(0, width // 256)
    def _(index):
        total[:, tile_of(index, 256)] = nt(grad_joined[...], w_qkv[tile_of(index, 256), :])

    def store_out(rows, value):
        out[rows, :] = value.astype(bf16)

    for seq in range(seqs):
        norm_grads(x, total, grad_middle, scale, None, 0, seq, store_out)


def backward_pass(grad_final, block_out, gain, scale, kept, weights):
    w_qkv, w_out, w_up, _, w_down = weights
    x, joined, _, middle, _, _, slope, _ = kept
    tokens, width = x.shape
    wide = w_up.shape[-1]
    vmem = pl.BlockSpec(memory_space=pltpu.VMEM)
    anywhere = pl.BlockSpec(memory_space=pl.ANY)
    exact = ((tokens, width), f32)
    low = ((tokens, width), bf16)
    lows = [low, ((tokens, wide), bf16), low, ((tokens, 3 * width), bf16)]
    near = [
        ((tokens, wide), bf16),
        ((width, wide), bf16),
        ((wide, width), bf16),
        exact,
        exact,
        ((tokens, 3 * width), bf16),
        ((width, 3 * width), bf16),
        ((width, width), bf16),
    ]
    flops = 4 * tokens * (4 * width * width + 2 * width * wide)
    return pl.pallas_call(
        partial(backward_kernel, False, scale.shape[0]),
        out_shape=[jax.ShapeDtypeStruct(*item) for item in [low, exact, ((1, width), f32)]],
        in_specs=[vmem] * 4 + [anywhere] * 8,
        out_specs=[vmem] * 3,
        scratch_shapes=[pltpu.VMEM(*item) for item in lows + near + [exact, exact, low]]
        + [pltpu.SemaphoreType.DMA((8,))],
        compiler_params=pltpu.CompilerParams(vmem_limit_bytes=60 * 2**20),
        cost_estimate=pl.CostEstimate(flops=flops, bytes_accessed=2**25, transcendentals=0),
    )(scale, grad_final, block_out, gain, slope, w_up, w_down, x, middle, joined, w_qkv, w_out)


def backward_begin(returned, grad_top, seqs, hidden, entry, slope, w_up, w_down):
    tokens, width = grad_top.shape
    wide = w_up.shape[-1]
    vmem = pl.BlockSpec(memory_space=pltpu.VMEM)
    anywhere = pl.BlockSpec(memory_space=pl.ANY)
    exact = ((tokens, width), f32)
    low = ((tokens, width), bf16)
    wide_low = ((tokens, wide), bf16)
    up, down = ((width, wide), bf16), ((wide, width), bf16)
    results = [exact, exact, ((1, wide), f32), down, up]
    inside = [low, wide_low, ((width, tokens), bf16), down, up]
    return pl.pallas_call(
        partial(backward_kernel, True, seqs),
        out_shape=[jax.ShapeDtypeStruct(*item) for item in results],
        in_specs=[vmem] * 4 + [anywhere] * 3,
        out_specs=[vmem] * 3 + [anywhere] * 2,
        scratch_shapes=[pltpu.VMEM(*item) for item in inside]
        + [pltpu.SemaphoreType.DMA((2, wide // 1024))]
        + [pltpu.VMEM(*item) for item in (wide_low, up, down)]
        + [pltpu.SemaphoreType.DMA((3,))],
        compiler_params=pltpu.CompilerParams(vmem_limit_bytes=60 * 2**20),
        cost_estimate=pl.CostEstimate(
            flops=16 * tokens * width * wide, bytes_accessed=2**25, transcendentals=0
        ),
    )(returned, grad_top, hidden, entry, slope, w_up, w_down)


def tail_kernel(line, seqs, lag, *refs):
    refs = list(refs)

    def take(number):
        return [refs.pop(0) for _ in range(number)]

    scale, rest, factor_one, factor_two, embedded, noisy, w_in = take(7)
    far = take(9)
    parts = take(2)
    (head_part,) = take(1)
    outs = take(5)
    head_out, smalls, rows_all = take(3)
    near = take(9)
    grad_attn, grad_mixed, grad_joined, grad_first, grad_cond, in_weight = take(6)
    rows_own, small_wide, small_own = take(3)
    own, from_core, slots = take(2), take(5), take(5)
    head_own, head_core, head_section, last_total = take(4)
    far_sem, load_sem, core_send, core_recv, ring_send, ring_recv, credit = take(7)
    keep_sem, packet_send, packet_recv, wide_send, wide_recv, rows_send, rows_recv = take(7)
    head_sem, head_send, head_recv, cross_send, cross_recv = take(5)
    grad_middle, grad_entry, middle, x, joined, mixed, entry_attn, w_out, w_qkv = near
    inside = [w_qkv, w_out, in_weight]
    groups = ((0, 1), (2, 3, 4))
    chips = 2 * line
    width = x.shape[1]
    me_section = lax.axis_index("section")
    me_line = lax.axis_index("line")
    me_pair = lax.axis_index("pair")
    me_core = lax.axis_index("core")
    position = me_line + me_pair * (chips - 1 - 2 * me_line)
    section_peer = {"section": 1 - me_section}
    core_peer = {"core": 1 - me_core}
    ways = (1, -1)
    ring_peers = []
    for way in ways:
        peer_line, peer_pair = ring_place(lax.rem(position + way + chips, chips), line)
        ring_peers.append({"line": peer_line, "pair": peer_pair})
    greet([core_peer, section_peer] + ring_peers)

    shapes = [ref.shape[-2:] for ref in from_core]

    def block_of(turn, step):
        ahead = lax.rem(position - ways[turn] * (1 + step) + 2 * chips, chips)
        return ring_place(ahead, line)

    def columns(index, turn):
        wide = shapes[index][-1] // 2
        return pl.ds(turn * wide, wide)

    def block_rows(index, place, pair, core):
        high = shapes[index][0]
        return pl.ds(pl.multiple_of(((place * 2 + pair) * 2 + core) * high, 16), high)

    def source(index, turn, step, core):
        place, pair = block_of(turn, step)
        cols = columns(index, turn)
        if index < 2:
            return parts[index].at[place, pair, core, :, cols]
        return inside[index - 2].at[block_rows(index, place, pair, core), cols]

    def load(index, turn, step):
        return pltpu.make_async_copy(
            source(index, turn, step, me_core),
            own[index].at[step % 2, :, columns(index, turn)],
            load_sem.at[index, turn, step],
        )

    def core_copy(index, turn, step):
        return remote(
            source(index, turn, step, 1 - me_core),
            from_core[index].at[step % 3, :, columns(index, turn)],
            core_send.at[index, turn, step],
            core_recv.at[index, turn, step],
            core_peer,
        )

    def ring_copy(index, turn, step):
        cols = columns(index, turn)
        passed = from_core[index].at[0, :, cols] if step == 0 else slots[index].at[step - 1, :, cols]
        return remote(
            passed,
            slots[index].at[step, :, cols],
            ring_send.at[index, turn, step],
            ring_recv.at[index, turn, step],
            ring_peers[turn],
        )

    def to_core(group, step):
        if step >= 3:
            pl.semaphore_wait(credit.at[group], 1)
        for index in groups[group]:
            for turn in range(2):
                if index < 2:
                    load(index, turn, step).start()
                core_copy(index, turn, step).start()

    def stop(group, step, between):
        first, last = step == 0, step == chips - 1
        for index in groups[group]:
            rows, wide = shapes[index][0], shapes[index][1] // 2
            tile = min(wide, 512)
            for turn in range(2):
                if index < 2:
                    load(index, turn, step).wait()
                core_copy(index, turn, step).wait_recv()
                if not first:
                    ring_copy(index, turn, step - 1).wait_recv()
                place, pair = block_of(turn, step)

                @pl.loop(0, rows // 16)
                def _(block):
                    row = pl.ds(pl.multiple_of(block * 16, 16), 16)
                    if index >= 2:
                        base = ((place * 2 + pair) * 2 + me_core) * rows + block * 16
                        own_row = pl.ds(pl.multiple_of(base, 16), 16)
                    for col in range(turn * wide, (turn + 1) * wide, tile):
                        cols = pl.ds(col, tile)
                        if index < 2:
                            mine = own[index][step % 2, row, cols]
                        else:
                            mine = inside[index - 2][own_row, cols]
                        total = from_core[index][step % 3, row, cols].astype(f32)
                        total = total + mine.astype(f32)
                        if not first:
                            total = total + slots[index][step - 1, row, cols].astype(f32)
                        if last and index == 4:
                            last_total[row, cols] = total
                        elif last:
                            outs[index][row, cols] = total.astype(bf16)
                        elif first:
                            from_core[index][0, row, cols] = total.astype(bf16)
                        else:
                            slots[index][step - 1, row, cols] = total.astype(bf16)

                if not last:
                    ring_copy(index, turn, step).start()
                between()
        if step == 1:
            for index in groups[group]:
                for turn in range(2):
                    ring_copy(index, turn, 0).wait_send()
        if 1 <= step <= 4:
            amount = 2 if step == 1 else 1
            pl.semaphore_signal(
                credit.at[group], inc=amount, device_id=core_peer, device_id_type=MESH
            )

    hops = (line, line - 1)

    def packet_blocks(place, pair):
        return [smalls.at[place, pair, me_core], rows_all.at[place, pair, me_core]]

    def packet_hops(turn, hop, away):
        place, pair = ring_place(
            lax.rem(position - ways[turn] * (hop + away) + 2 * chips, chips), line
        )
        return [
            remote(
                block,
                block,
                packet_send.at[n, turn, hop],
                packet_recv.at[n, turn, hop],
                ring_peers[turn],
            )
            for n, block in enumerate(packet_blocks(place, pair))
        ]

    def pass_packets(hop):
        for turn in range(2):
            if 0 < hop <= hops[turn]:
                for copy in packet_hops(turn, hop - 1, 1):
                    copy.wait_recv()
            if hop < hops[turn]:
                for copy in packet_hops(turn, hop, 0):
                    copy.start()

    small_slot, rows_slot = packet_blocks(me_line, me_pair)
    keep_small = pltpu.make_async_copy(small_own, small_slot, keep_sem.at[0])
    keep_rows = pltpu.make_async_copy(rows_own, rows_slot, keep_sem.at[1])
    rows_over = remote(rows_own, rows_slot, rows_send, rows_recv, section_peer)
    across = [
        remote(block, block, wide_send.at[n], wide_recv.at[n], core_peer)
        for n, block in enumerate([smalls.at[:, :, me_core], rows_all.at[:, :, me_core]])
    ]
    def packets_ready():
        keep_small.wait()

        @pl.when(me_section == 0)
        def _():
            keep_rows.wait()

        @pl.when(me_section == 1)
        def _():
            rows_over.wait_recv()

    high = head_part.shape[0] // 4

    def shard(n):
        return head_part.at[pl.ds(n * high, high)]

    head_loads = [
        pltpu.make_async_copy(shard(2 * n), head_own.at[n], head_sem.at[n]) for n in range(2)
    ]
    head_copies = [
        remote(shard(2 * n + 1), head_core.at[n], head_send.at[n], head_recv.at[n], core_peer)
        for n in range(2)
    ]
    head_copies.append(
        remote(head_core.at[1], head_section, head_send.at[2], head_recv.at[2], section_peer)
    )

    def head_over_cores():
        for copy in head_loads:
            copy.wait()
        for copy in head_copies[:2]:
            copy.wait_recv()

        @pl.loop(0, high // 16)
        def _(block):
            rows = pl.ds(pl.multiple_of(block * 16, 16), 16)
            value = head_core[1, rows, :].astype(f32) + head_own[1, rows, :].astype(f32)
            head_core[1, rows, :] = value.astype(bf16)

        head_copies[2].start()

    def head_over_sections():
        head_copies[2].wait_recv()

        @pl.loop(0, high // 16)
        def _(block):
            rows = pl.ds(pl.multiple_of(block * 16, 16), 16)
            value = head_core[0, rows, :].astype(f32) + head_own[0, rows, :].astype(f32)
            value = value + head_section[rows, :].astype(f32)
            head_out[rows, :] = value.astype(bf16)

    far_copies = []
    for n, (where, target) in enumerate(zip(far, near)):
        where = where.at[0] if n >= 7 else where
        far_copies.append(pltpu.make_async_copy(where, target, far_sem.at[n]))

    def waits(*numbers):
        for n in numbers:
            far_copies[n].wait()

    def store_middle(rows, value):
        grad_middle[rows, :] = value
        grad_attn[rows, :] = value.astype(bf16)

    def store_first(rows, value):
        grad_first[rows, :] = value.astype(bf16)

    def second_norm(seq):
        if seq == 0:
            waits(0, 1, 2)
        norm_grads(middle, grad_entry, grad_middle, scale, grad_cond, 1, seq, store_middle)

    def mixed_grads(index):
        if index == 0:
            waits(7)
        part = pl.ds(index * 512, 512)
        grad_mixed[:, part] = nt(grad_attn[...], w_out[part, :]).astype(bf16)

    def heads_grads(pair):
        if pair == 0:
            waits(4)
        attention_grads(joined, grad_mixed, grad_joined, pair, seqs)

    def entry_grads(index):
        if index == 0:
            waits(8)
        part = pl.ds(index * 256, 256)
        grad_entry[:, part] = nt(grad_joined[...], w_qkv[part, :])

    def first_norm(seq):
        if seq == 0:
            waits(3)
        norm_grads(x, grad_entry, grad_middle, scale, grad_cond, 0, seq, store_first)

    def embedding_rows(_):
        grad_noisy = nt(grad_first[...], w_in[...])
        inner = jnp.mean(grad_noisy * embedded[...], -1, keepdims=True)
        value = factor_one[...] * grad_noisy - factor_two[...] * embedded[...] * inner
        rows_own[...] = value.astype(bf16)

        @pl.when(me_section == 0)
        def _():
            keep_rows.start()
            rows_over.start()

    def small_rows(_):
        each = small_wide.shape[1]
        for seq in range(seqs):
            for n in range(2 * width // each):
                row = pl.ds(seq * (2 * width // each) + n, 1)
                small_wide[row, :] = grad_cond[seq, :, pl.ds(n * each, each)]
        small_wide[pl.ds(seqs * 2 * width // each, rest.shape[0]), :] = rest[...]
        small_own[...] = small_wide[...].astype(bf16)
        keep_small.start()

    def input_weight(_):
        in_weight[...] = tn(noisy[...], grad_first[...]).astype(bf16)

    def qkv_weight(index):
        if index == 0:
            waits(6)
        part = pl.ds(index * 256, 256)
        w_qkv[part, :] = tn(entry_attn[:, part], grad_joined[...]).astype(bf16)

    def out_weight(index):
        if index == 0:
            waits(5)
        part = pl.ds(index * 512, 512)
        w_out[part, :] = tn(mixed[:, part], grad_attn[...]).astype(bf16)

    steps = []
    for step, number in (
        (second_norm, seqs),
        (mixed_grads, width // 512),
        (heads_grads, width // 128),
        (entry_grads, width // 256),
        (first_norm, seqs),
        (embedding_rows, 1),
        (small_rows, 1),
        (input_weight, 1),
        (qkv_weight, width // 256),
        (out_weight, width // 512),
    ):
        steps += [partial(step, n) for n in range(number)]
    at_once = -(-len(steps) // (4 * lag))

    def work():
        for _ in range(at_once):
            if steps:
                steps.pop(0)()

    def nothing():
        pass

    to_core(0, 0)
    to_core(0, 1)
    for copy in far_copies:
        copy.start()
    stop(0, 0, work)
    for turn in range(1, chips + lag):
        if turn + 1 < chips:
            to_core(0, turn + 1)
        if turn == 1:
            for copy in head_loads + head_copies[:2]:
                copy.start()
        if turn == lag:
            to_core(1, 0)
        if lag <= turn and turn - lag + 1 < chips:
            to_core(1, turn - lag + 1)
        if turn < chips:
            stop(0, turn, work if turn < lag else nothing)
        if turn >= lag:
            stop(1, turn - lag, nothing)
        hop = turn - lag - 2
        if hop == 0:
            packets_ready()
        if 0 <= hop <= line:
            pass_packets(hop)
        if hop == line:
            for copy in across:
                copy.start()
        if turn == 3:
            head_over_cores()
        if turn == chips + lag - 2:
            head_over_sections()
    each = outs[4].shape[0]
    give = remote(last_total.at[pl.ds(each, each)], outs[4], cross_send, cross_recv, section_peer)

    @pl.when(me_section == 0)
    def _():
        give.start()
        outs[4][...] = last_total[pl.ds(0, each), :]

    for copy in across:
        copy.wait()
    for copy in head_copies:
        copy.wait_send()
    for turn in range(2):
        for hop in range(hops[turn]):
            for copy in packet_hops(turn, hop, 0):
                copy.wait_send()
    for index in range(5):
        for turn in range(2):
            for step in range(chips):
                core_copy(index, turn, step).wait_send()
                if 0 < step < chips - 1:
                    ring_copy(index, turn, step).wait_send()

    @pl.when(me_section == 0)
    def _():
        rows_over.wait_send()
        give.wait_send()

    @pl.when(me_section == 1)
    def _():
        give.wait_recv()


def tail_pass(scale, rest, factors, embedded, noisy, w_in, far, parts, head_part, collective_id):
    grad_middle = far[0]
    tokens, width = grad_middle.shape
    seqs = scale.shape[0]
    line = parts[0].shape[0]
    chips = 2 * line
    count = 4 * line
    emb_width = noisy.shape[1]
    vmem = pl.BlockSpec(memory_space=pltpu.VMEM)
    anywhere = pl.BlockSpec(memory_space=pl.ANY)
    dma = pltpu.SemaphoreType.DMA
    shapes = [part.shape[-2:] for part in parts]
    shapes += [
        (width // count, 3 * width),
        (width // count, width),
        (emb_width // count, width),
    ]
    each = shapes[4][0] // 2
    high = head_part.shape[0] // 4
    small = (seqs * 2 * width // emb_width + rest.shape[0], emb_width)
    exact = ((tokens, width), f32)
    low = ((tokens, width), bf16)
    three = ((tokens, 3 * width), bf16)
    rows = (tokens, emb_width)
    results = [(shape, bf16) for shape in shapes[:4]]
    results += [((each, width), f32), ((high, width), bf16)]
    results += [((line, 2, 2) + small, bf16), ((line, 2, 2) + rows, bf16)]
    room = [exact, exact, exact, exact, three, low, low]
    room += [((width, width), bf16), ((width, 3 * width), bf16)]
    room += [low, low, three, low, ((seqs, 1, 2 * width), f32), ((emb_width, width), bf16)]
    room += [(rows, bf16), (small, f32), (small, bf16)]
    room += [((2,) + shape, bf16) for shape in shapes[:2]]
    room += [((3,) + shape, bf16) for shape in shapes]
    room += [((chips - 1,) + shape, bf16) for shape in shapes]
    room += [((2, high, width), bf16), ((2, high, width), bf16), ((high, width), bf16)]
    room += [(shapes[4], f32)]
    scratch = [pltpu.VMEM(*item) for item in room]
    scratch += [dma((9,)), dma((2, 2, chips)), dma((5, 2, chips)), dma((5, 2, chips))]
    scratch += [dma((5, 2, chips - 1)), dma((5, 2, chips - 1)), pltpu.SemaphoreType.REGULAR((2,))]
    scratch += [dma((2,)), dma((2, 2, line)), dma((2, 2, line)), dma((2,)), dma((2,)), dma, dma]
    scratch += [dma((2,)), dma((3,)), dma((3,)), dma, dma]
    return pl.pallas_call(
        partial(tail_kernel, line, seqs, line),
        out_shape=[jax.ShapeDtypeStruct(*item) for item in results],
        in_specs=[vmem] * 7 + [anywhere] * 12,
        out_specs=[vmem] * 6 + [anywhere] * 2,
        scratch_shapes=scratch,
        compiler_params=pltpu.CompilerParams(
            collective_id=collective_id, has_side_effects=True, vmem_limit_bytes=62 * 2**20
        ),
        cost_estimate=pl.CostEstimate(flops=0, bytes_accessed=2**29, transcendentals=0),
    )(scale, rest, *factors, embedded, noisy, w_in, *far, *parts, head_part)


def finish_kernel(line, head_rows, *refs):
    ids, rows, *lows = refs[:7]
    *exacts, grad_embed, total = refs[7:]
    me_section = lax.axis_index("section")
    me_line = lax.axis_index("line")
    me_pair = lax.axis_index("pair")
    me_core = lax.axis_index("core")
    high = total.shape[0]
    base = (((me_section * line + me_line) * 2 + me_pair) * 2 + me_core) * grad_embed.shape[0]
    tile = 768
    for index in range(rows.shape[0] // tile):
        part = pl.ds(index * tile, tile)
        entry = lax.broadcasted_iota(jnp.int32, (high, tile), 0) + base
        place = jnp.where(entry == ids[:, part], 1.0, 0.0).astype(bf16)
        product = nn(place, rows[part, :])
        total[...] = product if index == 0 else total[...] + product
    grad_embed[...] = total[pl.ds(0, grad_embed.shape[0]), :]
    for low, exact in zip(lows, exacts):
        whole = exact.shape[0] // 16
        left = exact.shape[0] % 16

        @pl.loop(0, whole)
        def _(block):
            part = pl.ds(pl.multiple_of(block * 16, 16), 16)
            exact[part, :] = low[part, :].astype(f32)

        if left:
            value = low[pl.ds(whole * 16, 16), :].astype(f32)
            exact[pl.ds(whole * 16, left), :] = value[:left]


def finish(ids, rows, lows, line, head_rows, out_rows):
    vmem = pl.BlockSpec(memory_space=pltpu.VMEM)
    shapes = [low.shape for low in lows[:-1]] + [(head_rows, lows[-1].shape[1])]
    shapes.append((out_rows, rows.shape[1]))
    return pl.pallas_call(
        partial(finish_kernel, line, head_rows),
        out_shape=[jax.ShapeDtypeStruct(shape, f32) for shape in shapes],
        in_specs=[vmem] * 7,
        out_specs=[vmem] * 6,
        scratch_shapes=[pltpu.VMEM((-(-out_rows // 16) * 16, rows.shape[1]), f32)],
        compiler_params=pltpu.CompilerParams(vmem_limit_bytes=60 * 2**20),
        cost_estimate=pl.CostEstimate(
            flops=2 * out_rows * rows.size, bytes_accessed=2**24, transcendentals=0
        ),
    )(ids, rows, *lows)


def norm_rows(values):
    centred = values - jnp.mean(values, -1, keepdims=True)
    factor = lax.rsqrt(jnp.mean(centred * centred, -1, keepdims=True) + epsilon)
    return (centred * factor, factor)


def norm_back(gradient, normed, factor):
    return factor * (
        gradient
        - jnp.mean(gradient, -1, keepdims=True)
        - normed * jnp.mean(gradient * normed, -1, keepdims=True)
    )


def time_features(noise_level):
    half_width = TFEAT // 2
    rates = jnp.exp(jnp.arange(half_width, dtype=f32) * (math.log(1000.0) / half_width))
    angles = (jnp.log(noise_level) / 4.0)[:, None] * rates[None, :]
    return jnp.concatenate([jnp.cos(angles), jnp.sin(angles)], -1)


def levels_of(bins, table):
    hits = bins[:, None] == jnp.arange(table.shape[0])[None, :]
    return jnp.sum(jnp.where(hits, table[None, :], 0.0), -1)


def over_dp(part):
    part = part.reshape((part.shape[0] // 4, 2, 2) + part.shape[1:])
    part = lax.psum_scatter(part, "core", scatter_dimension=2)
    part = lax.psum_scatter(part, "pair", scatter_dimension=1)
    return lax.psum_scatter(part, "line", scatter_dimension=0)


def by_owner(part):
    line = lax.axis_size("line")
    return part.astype(bf16).reshape((line, 2, 2, part.shape[0] // (line * 4)) + part.shape[1:])


def mm(spec, left, right):
    return jnp.einsum(spec, left, right, preferred_element_type=f32)


def layer_forward(stream, scale_attn, scale_mlp, weights):
    w_qkv, w_out, w_up, b_hidden, w_down = weights
    seq_count, length, model_width = stream.shape
    normed_attn, factor_attn = norm_rows(stream)
    attn_entry = (normed_attn * scale_attn).astype(bf16)
    joined = mm("nsd,de->nse", attn_entry, w_qkv).astype(bf16)
    qkv_parts = joined.reshape(seq_count, length, 3, HEADS, HEAD_DIM)
    query_rows = qkv_parts[:, :, 0]
    key_rows = qkv_parts[:, :, 1]
    value_rows = qkv_parts[:, :, 2]
    scores = mm("nqhe,nkhe->nhqk", query_rows, key_rows) / math.sqrt(HEAD_DIM)
    exp_scores = jnp.exp(scores - jnp.max(scores, -1, keepdims=True))
    attn_probs = exp_scores / jnp.sum(exp_scores, -1, keepdims=True)
    probs_low = attn_probs.astype(bf16)
    attn_mixed = mm("nhqk,nkhe->nqhe", probs_low, value_rows).astype(bf16)
    attn_mixed = attn_mixed.reshape(seq_count, length, model_width)
    middle = stream + mm("nsd,de->nse", attn_mixed, w_out)
    normed_mlp, factor_mlp = norm_rows(middle)
    mlp_entry = (normed_mlp * scale_mlp).astype(bf16)
    up_proj = mm("nsd,df->nsf", mlp_entry, w_up) + b_hidden
    below = 0.5 + 0.5 * lax.erf(up_proj * math.sqrt(0.5))
    hidden = (up_proj * below).astype(bf16)
    density = jnp.exp(-0.5 * up_proj * up_proj) * (1.0 / math.sqrt(2.0 * math.pi))
    slope = (below + up_proj * density).astype(bf16)
    block_out = middle + mm("nsf,fd->nsd", hidden, w_down)
    kept = (
        normed_attn,
        factor_attn,
        attn_entry,
        query_rows,
        key_rows,
        value_rows,
        attn_probs,
        probs_low,
        attn_mixed,
        normed_mlp,
        factor_mlp,
        mlp_entry,
        slope,
        hidden,
    )
    return (block_out, kept)


def layer_backward(grad_out, kept, scale_attn, scale_mlp, weights, whole):
    w_qkv, w_out, w_up, b_hidden, w_down = weights
    (
        normed_attn,
        factor_attn,
        attn_entry,
        query_rows,
        key_rows,
        value_rows,
        attn_probs,
        probs_low,
        attn_mixed,
        normed_mlp,
        factor_mlp,
        mlp_entry,
        slope,
        hidden,
    ) = kept
    seq_count, length, model_width = grad_out.shape
    grads = {}
    grad_branch = grad_out.astype(bf16)
    if whole:
        grads["down"] = by_owner(mm("nsf,nsd->fd", hidden, grad_branch))
    grad_hidden = mm("nsd,fd->nsf", grad_branch, w_down)
    grad_up_proj = (grad_hidden * slope.astype(f32)).astype(bf16)
    if whole:
        grads["bias"] = jnp.sum(grad_up_proj.astype(f32), (0, 1))
        grads["up"] = by_owner(mm("nsd,nsf->df", mlp_entry, grad_up_proj))
    grad_entry = mm("nsf,df->nsd", grad_up_proj, w_up)
    grad_middle = grad_out + norm_back(grad_entry * scale_mlp, normed_mlp, factor_mlp)
    grad_attn = grad_middle.astype(bf16)
    if whole:
        grads["out"] = by_owner(mm("nsd,nse->de", attn_mixed, grad_attn))
    grad_mixed = mm("nse,de->nsd", grad_attn, w_out)
    grad_mixed = grad_mixed.astype(bf16).reshape(seq_count, length, HEADS, HEAD_DIM)
    grad_probs = mm("nqhe,nkhe->nhqk", grad_mixed, value_rows)
    grad_values = mm("nhqk,nqhe->nkhe", probs_low, grad_mixed)
    grad_scores = (
        attn_probs * (grad_probs - jnp.sum(grad_probs * attn_probs, -1, keepdims=True))
    ).astype(bf16)
    grad_query = mm("nhqk,nkhe->nqhe", grad_scores, key_rows) / math.sqrt(HEAD_DIM)
    grad_keys = mm("nhqk,nqhe->nkhe", grad_scores, query_rows) / math.sqrt(HEAD_DIM)
    grad_joined = jnp.stack([grad_query, grad_keys, grad_values], 2).astype(bf16)
    grad_joined = grad_joined.reshape(seq_count, length, 3 * model_width)
    if whole:
        grads["qkv"] = by_owner(mm("nsd,nse->de", attn_entry, grad_joined))
    grad_attn_entry = mm("nse,de->nsd", grad_joined, w_qkv)
    grad_stream = grad_middle + norm_back(grad_attn_entry * scale_attn, normed_attn, factor_attn)
    if whole:
        grads["cond"] = jnp.concatenate(
            [jnp.sum(grad_attn_entry * normed_attn, 1), jnp.sum(grad_entry * normed_mlp, 1)], -1
        )
    return (grad_stream, grads)


def local(
    token_ids,
    target_ids,
    time_bins,
    sigma_table,
    noise,
    embed,
    w_in,
    w_time,
    norm_gain,
    w_qkv,
    w_out,
    w_up,
    b_hidden,
    w_down,
    out_gain,
    head,
):
    section = lax.axis_index("section")
    line_at = lax.axis_index("line")
    pair_at = lax.axis_index("pair")
    core = lax.axis_index("core")
    sections = lax.axis_size("section")
    line = lax.axis_size("line")
    chip = line_at * 2 + pair_at
    chips = line * 2
    cores = 2
    dp_count = chips * cores
    dp_index = chip * cores + core
    is_first = section == 0
    seqs, length = token_ids.shape
    tokens = seqs * length
    half = tokens // sections
    model_width = w_out.shape[-1]
    emb_rows, emb_width = embed.shape
    head_rows = head.shape[0]
    straight = line <= 4 and half % 16 == 0 and model_width // dp_count % 16 == 0

    if straight:
        lanes = -(-half // 128) * 128
        blocks = [part.reshape(2, half) for part in (token_ids, target_ids)]
        blocks.append(jnp.pad(time_bins[None, :], ((0, 0), (0, half - seqs))))
        own_ids = jnp.pad(jnp.concatenate(blocks, 0), ((0, 3), (0, lanes - half)))
        head_own = jnp.pad(head, ((0, -head_rows % 512), (0, 0)))
        all_ids, embedded, head_early, head_core = start_pass(
            own_ids, embed, head_own, half, line, 0
        )
        all_ids = all_ids.reshape(dp_count, 8, lanes)
        all_tokens = all_ids[:, 0:2, :half].reshape(dp_count, tokens)
        all_targets = all_ids[:, 2:4, :half].reshape(dp_count, tokens)
        all_bins = all_ids[:, 4, :seqs].reshape(-1)
        embedded = embedded.swapaxes(1, 2)
    else:
        own_ids = jnp.concatenate([token_ids.reshape(-1), target_ids.reshape(-1), time_bins])
        all_ids = lax.all_gather(own_ids, DP)
        all_tokens = all_ids[:, :tokens]
        all_targets = all_ids[:, tokens : 2 * tokens]
        all_bins = all_ids[:, 2 * tokens :].reshape(-1)
        own_rows = dp_index * emb_rows + jnp.arange(emb_rows)
        half_tokens = lax.dynamic_slice_in_dim(all_tokens, section * half, half, 1)
        picked = (half_tokens.reshape(-1)[:, None] == own_rows[None, :]).astype(bf16)
        found = jnp.dot(picked, embed, preferred_element_type=f32).astype(bf16)
        embedded = lax.all_gather(over_dp(found.reshape(dp_count, half, emb_width)), "section")
    embedded = embedded.astype(f32).reshape(seqs, length, emb_width)

    swapped = [(0, 1), (1, 0)]
    if not straight:
        head_group = lax.all_gather(lax.all_gather(head, "core"), "section")
        head_group = head_group.reshape(-1, model_width)
        vocab_base = (
            (jnp.arange(sections)[:, None] * chips + chip) * cores + jnp.arange(cores)[None, :]
        ) * head_rows
        columns = (vocab_base[:, :, None] + jnp.arange(head_rows)[None, None, :]).reshape(-1)

    noise_level = levels_of(time_bins, sigma_table)
    unit_factor = lax.rsqrt(jnp.mean(embedded * embedded, -1, keepdims=True) + epsilon)
    level_col = noise_level[:, None, None]
    noise_scale = lax.rsqrt(level_col * level_col + 1.0)
    noisy_rows = ((embedded * unit_factor + level_col * noise) * noise_scale).astype(bf16)
    time_feats = time_features(noise_level)
    conditioned = jnp.dot(time_feats, w_time[0].astype(f32), precision=highest) + norm_gain[0]
    scale_attn = conditioned[:, None, :model_width]
    scale_mlp = conditioned[:, None, model_width:]
    scale = conditioned[:, None, :]
    weights = (w_qkv[0], w_out[0], w_up[0], b_hidden[0], w_down[0])
    stacked = (w_qkv, w_out, w_up, b_hidden, w_down)
    stream0 = mm("nse,ed->nsd", noisy_rows, w_in)
    flat = (tokens, model_width)
    if straight:
        block_out, final_rows, *kept, head_late, head_fourth = forward_pass(
            stream0.reshape(flat), scale, stacked, out_gain[None, :], head_own, head_early, 1
        )
        heads = [head_own, head_core, head_early, head_late, head_fourth]
    else:
        first_out = layer_forward(stream0, scale_attn, scale_mlp, weights)[0].astype(bf16)
        arrived = lax.ppermute(first_out, "section", swapped)
        stream = jnp.where(is_first, stream0, arrived.astype(f32))
        block_out, kept = layer_forward(stream, scale_attn, scale_mlp, weights)
        final_normed, final_factor = norm_rows(block_out.astype(bf16).astype(f32))
        final_rows = (final_normed * out_gain).astype(bf16).reshape(flat)

    targets_group = lax.dynamic_slice_in_dim(
        all_targets.reshape(chips, cores, tokens), core, 1, 1
    )[:, 0]
    targets_group = lax.dynamic_slice_in_dim(targets_group, section * half, half, 1)
    if straight:
        grad_final, grad_head, lse, picks = head_pass(
            final_rows, targets_group.reshape(line, 1, tokens), heads, line, head_rows, length, 3
        )
        ce_part = jnp.sum(lse) / chips - jnp.sum(picks)
    else:
        targets_group = targets_group.reshape(-1)
        handed = lax.ppermute(final_rows[:half], "section", [(1, 0), (0, 1)])
        own_final = jnp.where(is_first, handed, final_rows[half:])
        group_final = lax.all_gather(own_final, ("line", "pair"), tiled=True)
        logits = mm("td,vd->tv", group_final, head_group)
        local_top = jnp.max(logits, -1)
        local_total = jnp.sum(jnp.exp(logits - local_top[:, None]), -1)
        mark = columns[None, :] == targets_group[:, None]
        local_pick = jnp.sum(jnp.where(mark, logits, 0.0))
        stats = lax.all_gather(jnp.stack([local_top, local_total]), ("line", "pair"))
        all_top = jnp.max(stats[:, 0], 0)
        all_total = jnp.sum(stats[:, 1] * jnp.exp(stats[:, 0] - all_top), 0)
        log_total = all_top + jnp.log(all_total)
        soft_rows = jnp.exp(logits - log_total[:, None])
        logit_grads = ((soft_rows - jnp.where(mark, 1.0, 0.0)) / length).astype(bf16)
        grad_final = jnp.dot(logit_grads, head_group, preferred_element_type=f32).astype(bf16)
        grad_final = lax.psum_scatter(grad_final, ("line", "pair"), scatter_dimension=0, tiled=True)
        handed = lax.ppermute(grad_final, "section", swapped)
        grad_final = jnp.concatenate([handed, grad_final], 0)
        grad_head = mm("tv,td->vd", logit_grads, group_final).astype(bf16)
        grad_head = grad_head.reshape(sections, cores, head_rows, model_width)
        grad_head = lax.psum_scatter(grad_head, "core", scatter_dimension=1)
        grad_head = lax.psum_scatter(grad_head, "section", scatter_dimension=0).astype(f32)

        ce_part = jnp.sum(log_total) / chips - local_pick
    if straight:
        grad_second, grad_top, out_part = backward_pass(
            grad_final, block_out, out_gain[None, :], scale, kept, stacked
        )
        returned = lax.ppermute(grad_second, "section", swapped)
        out_part = out_part.reshape(-1)
        x, joined, mixed, middle, entry_attn, entry_mlp, slope, hidden = kept
        grad_middle, grad_entry, grad_bias, down_part, up_part = backward_begin(
            returned, grad_top, seqs, hidden, entry_mlp, slope, w_up, w_down
        )
        parts = [by_owner(down_part), by_owner(up_part)]
        grad_bias = grad_bias.reshape(-1)
    else:
        grad_final = grad_final.astype(f32).reshape(stream0.shape)
        out_part = jnp.sum(grad_final * final_normed, (0, 1))
        grad_top = norm_back(grad_final * out_gain, final_normed, final_factor)
        grad_second = layer_backward(grad_top, kept, scale_attn, scale_mlp, weights, False)[0]
        returned = lax.ppermute(grad_second.astype(bf16), "section", swapped)
        grad_cot = jnp.where(is_first, returned.astype(f32), grad_top)
        grad_stream, grads = layer_backward(grad_cot, kept, scale_attn, scale_mlp, weights, True)
        grad_first = grad_stream.astype(bf16)
    out_part = jnp.where(is_first, 0.0, out_part)

    ce_high = ce_part.astype(bf16).astype(f32)
    ce_mid = (ce_part - ce_high).astype(bf16).astype(f32)
    ce_low = ce_part - ce_high - ce_mid
    shared = jnp.concatenate([out_part, jnp.stack([ce_high, ce_mid, ce_low])])
    shared_rows = -(-shared.shape[0] // emb_width)
    shared = jnp.pad(shared, (0, shared_rows * emb_width - shared.shape[0]))
    shared = shared.reshape(-1, emb_width).astype(bf16)
    both = [shared, lax.ppermute(shared, "section", swapped)]

    cubed = unit_factor * unit_factor * unit_factor
    cond_rows = seqs * 2 * model_width // emb_width
    bias_rows = b_hidden.shape[1] // emb_width
    if straight:
        rest = jnp.concatenate([grad_bias.reshape(-1, emb_width)] + both, 0).astype(f32)
        rest = jnp.pad(rest, ((0, -(cond_rows + rest.shape[0]) % 16), (0, 0)))
        factors = [
            (value * noise_scale).reshape(tokens, 1) for value in (unit_factor, cubed)
        ]
        owned = noisy_rows.reshape(tokens, sections, dp_count, -1)
        owned = owned.swapaxes(1, 2).reshape(tokens, emb_width)
        far = [grad_middle, grad_entry, middle, x, joined, mixed, entry_attn, w_out, w_qkv]
        grad_down, grad_up, grad_qkv, grad_wout, grad_w_in, grad_head, smalls, rows_all = tail_pass(
            scale,
            rest,
            factors,
            embedded.reshape(tokens, emb_width),
            owned,
            w_in,
            far,
            parts,
            grad_head,
            2,
        )
        ids = all_tokens.reshape(1, -1)
        grad_down, grad_up, grad_qkv, grad_wout, grad_head, grad_embed = finish(
            ids,
            rows_all.reshape(-1, emb_width),
            [grad_down, grad_up, grad_qkv, grad_wout, grad_head],
            line,
            head_rows,
            emb_rows // sections,
        )
    else:
        in_part = mm("nse,nsd->ed", noisy_rows, grad_first).astype(bf16)
        in_part = in_part.reshape(sections, dp_count, -1, model_width).swapaxes(0, 1)
        in_sum = over_dp(in_part).astype(f32)
        in_handed = lax.ppermute(in_sum[1], "section", swapped)
        grad_w_in = jnp.where(is_first, in_sum[0], in_handed)
        grad_noisy = mm("nsd,ed->nse", grad_first, w_in)
        grad_unit = grad_noisy * noise_scale
        grad_embedded = unit_factor * grad_unit - cubed * embedded * jnp.mean(
            grad_unit * embedded, -1, keepdims=True
        )
        grad_flat = grad_embedded.reshape(tokens, emb_width).astype(bf16)
        handed = lax.ppermute(grad_flat, "section", swapped)
        rows_all = lax.all_gather(jnp.where(is_first, grad_flat, handed), DP)
        small = [grads["cond"].reshape(-1, emb_width), grads["bias"].reshape(-1, emb_width)]
        smalls = lax.all_gather(
            jnp.concatenate([value.astype(bf16) for value in small] + both, 0), DP
        )
        grad_down, grad_up, grad_qkv, grad_wout = [
            over_dp(part.reshape((dp_count,) + part.shape[3:])).astype(f32)
            for part in (grads["down"], grads["up"], grads["qkv"], grads["out"])
        ]
        grad_all = rows_all.reshape(-1, emb_width)
        out_rows = emb_rows // sections
        target_rows = (section * dp_count + dp_index) * out_rows + jnp.arange(out_rows)
        place = (target_rows[:, None] == all_tokens.reshape(-1)[None, :]).astype(bf16)
        grad_embed = jnp.dot(place, grad_all, preferred_element_type=f32)

    smalls = smalls.reshape(dp_count, -1, emb_width).astype(f32)
    cond_all = smalls[:, :cond_rows].reshape(dp_count * seqs, 2 * model_width)
    bias_all = smalls[:, cond_rows : cond_rows + bias_rows].reshape(dp_count, -1)
    hidden_rows = bias_all.shape[1] // dp_count
    grad_bias = jnp.sum(
        lax.dynamic_slice_in_dim(bias_all, dp_index * hidden_rows, hidden_rows, 1), 0
    )
    norm_cols = 2 * model_width // dp_count
    grad_gain = jnp.sum(lax.dynamic_slice_in_dim(cond_all, dp_index * norm_cols, norm_cols, 1), 0)
    feats_all = time_features(levels_of(all_bins, sigma_table))
    feat_rows = TFEAT // dp_count
    feats_own = lax.dynamic_slice_in_dim(feats_all, dp_index * feat_rows, feat_rows, 1)
    grad_time = jnp.dot(feats_own.T, cond_all, precision=highest)
    shared_first = cond_rows + bias_rows
    both = smalls[:, shared_first : shared_first + 2 * shared_rows]
    both = jnp.sum(both.reshape(dp_count, 2, -1), (0, 1))
    loss = jnp.sum(both[model_width : model_width + 3]) / (tokens * dp_count)
    gain_rows = model_width // dp_count
    grad_out_gain = lax.dynamic_slice_in_dim(both, dp_index * gain_rows, gain_rows)
    return (
        loss,
        grad_embed,
        grad_w_in,
        grad_time[None],
        grad_gain[None],
        grad_qkv[None],
        grad_wout[None],
        grad_up[None],
        grad_bias[None],
        grad_down[None],
        grad_out_gain,
        grad_head,
    )


def solution(mesh):
    sections, dp_count = mesh.shape["section"], mesh.shape["dp"]
    fine = Mesh(mesh.devices.reshape(sections, dp_count // 4, 2, 2), ("section",) + DP)
    everywhere = ("section",) + DP
    in_specs = (
        P(DP, None),
        P(DP, None),
        P(DP),
        P(),
        P(DP, None, None),
        P(DP, None),
        P(),
        P("section", None, None),
        P("section", None),
        P("section", None, None),
        P("section", None, None),
        P("section", None, None),
        P("section", None),
        P("section", None, None),
        P(),
        P(everywhere, None),
    )
    out_specs = (
        P(),
        P(everywhere, None),
        P(everywhere, None),
        P("section", DP, None),
        P("section", DP),
        P("section", DP, None),
        P("section", DP, None),
        P("section", DP, None),
        P("section", DP),
        P("section", DP, None),
        P(DP),
        P(everywhere, None),
    )
    return jax.shard_map(local, mesh=fine, in_specs=in_specs, out_specs=out_specs, check_vma=False)
```

```python
from functools import partial
import math

import jax
import jax.numpy as jnp
from jax import lax
from jax.experimental import pallas as pl
from jax.experimental.pallas import tpu as pltpu
from jax.sharding import Mesh, PartitionSpec as P

HEADS = 16
HEAD_DIM = 64
TFEAT = 256

epsilon = 1e-05
highest = lax.Precision.HIGHEST
f32 = jnp.float32
bf16 = jnp.bfloat16
DP = ("line", "pair", "core")


MESH = pl.DeviceIdType.MESH


def nt(left, right):
    return lax.dot_general(left, right, (((1,), (1,)), ((), ())), preferred_element_type=f32)


def tn(left, right):
    return lax.dot_general(left, right, (((0,), (0,)), ((), ())), preferred_element_type=f32)


def nn(left, right):
    return jnp.dot(left, right, preferred_element_type=f32)


def greet(peers):
    barrier = pltpu.get_barrier_semaphore()
    for peer in peers:
        pl.semaphore_signal(barrier, inc=1, device_id=peer, device_id_type=MESH)
    pl.semaphore_wait(barrier, len(peers))


def remote(source, target, send, recv, peer):
    return pltpu.make_async_remote_copy(
        src_ref=source,
        dst_ref=target,
        send_sem=send,
        recv_sem=recv,
        device_id=peer,
        device_id_type=MESH,
    )


def ring_place(position, line):
    turned = position // line
    return position * (1 - turned) + (2 * line - 1 - position) * turned, turned


def start_kernel(line, *refs):
    ids, embed, head, all_ids, out, head_early, head_core = refs[:7]
    table, found, own, from_core, from_pair, from_line = refs[7:13]
    ids_send, ids_recv, own_sem, core_send, core_recv, pair_send, pair_recv = refs[13:20]
    line_send, line_recv, swap_send, swap_recv, head_send, head_recv = refs[20:]
    me_section = lax.axis_index("section")
    me_line = lax.axis_index("line")
    me_pair = lax.axis_index("pair")
    me_core = lax.axis_index("core")
    section_peer = {"section": 1 - me_section}
    core_peer = {"core": 1 - me_core}
    pair_peer = {"pair": 1 - me_pair}
    peers = []
    for step in range(1, line * 4):
        peers.append(
            {
                "line": lax.rem(me_line + step // 4, line),
                "pair": lax.rem(me_pair + step // 2 % 2, 2),
                "core": lax.rem(me_core + step % 2, 2),
            }
        )
    greet(peers + [section_peer])
    each = head_early.shape[0]
    to_section = remote(
        head.at[pl.ds(0, each)], head_early, head_send.at[0], head_recv.at[0], section_peer
    )
    to_section.start()
    to_other_core = remote(head, head_core, head_send.at[1], head_recv.at[1], core_peer)
    place = all_ids.at[me_line, me_pair, me_core]
    copies = [remote(ids, place, ids_send.at[n], ids_recv.at[n], peer) for n, peer in enumerate(peers)]
    for copy in copies:
        copy.start()
    keep = pltpu.make_async_copy(ids, place, own_sem)
    keep.start()
    rows = embed.shape[0]
    high = table.shape[1]
    half = out.shape[-1]
    padded = jnp.concatenate(
        [embed[...].astype(f32), jnp.zeros((high - rows, embed.shape[1]), f32)], 0
    )
    table[...] = padded.T.astype(bf16)
    keep.wait()
    for copy in copies:
        copy.wait_recv()
    base = ((me_line * 2 + me_pair) * 2 + me_core) * rows

    def pick(spot, pair, core):
        wanted = all_ids[spot, pair, core, pl.ds(me_section, 1), :][:, :half]
        entry = lax.broadcasted_iota(jnp.int32, (high, half), 0)
        entry = jnp.where(entry < rows, entry + base, -1)
        hot = jnp.where(entry == wanted, 1.0, 0.0).astype(bf16)
        return nn(table[...], hot).astype(bf16)

    def core_copy(spot, pair, turn):
        return remote(
            found.at[turn, spot],
            from_core.at[turn, spot],
            core_send.at[turn, spot],
            core_recv.at[turn, spot],
            core_peer,
        )

    def pair_copy(spot):
        return remote(
            from_core.at[0, spot], from_pair.at[spot], pair_send.at[spot], pair_recv.at[spot], pair_peer
        )

    def line_copy(step):
        spot = lax.rem(me_line + step, line)
        return remote(
            from_core.at[1, spot],
            from_line.at[step - 1],
            line_send.at[step - 1],
            line_recv.at[step - 1],
            {"line": spot},
        )

    order = [lax.rem(me_line + step, line) for step in list(range(1, line)) + [0]]
    for turn, pair in enumerate((1 - me_pair, me_pair)):

        @pl.loop(0, line)
        def _(step):
            spot = lax.rem(me_line + 1 + step, line)
            found[turn, spot] = pick(spot, pair, 1 - me_core)
            core_copy(spot, pair, turn).start()
            own[turn, spot] = pick(spot, pair, me_core)

        if turn == 0:
            for spot in order:
                core_copy(spot, pair, 0).wait_recv()
                from_core[0, spot] = from_core[0, spot] + own[0, spot]
                pair_copy(spot).start()
    for step in list(range(1, line)) + [0]:
        spot = lax.rem(me_line + step, line)
        core_copy(spot, me_pair, 1).wait_recv()
        pair_copy(spot).wait_recv()
        from_core[1, spot] = from_core[1, spot] + own[1, spot] + from_pair[spot]
        if step:
            line_copy(step).start()
    to_other_core.start()
    total = from_core[1, me_line]
    for step in range(1, line):
        line_copy(step).wait_recv()
        total = total + from_line[step - 1]
    out[me_section] = total
    swap = remote(out.at[me_section], out.at[me_section], swap_send, swap_recv, section_peer)
    swap.start()
    for copy in copies:
        copy.wait_send()
    for spot in range(line):
        for turn in range(2):
            core_copy(spot, me_pair, turn).wait_send()
        pair_copy(spot).wait_send()
    for step in range(1, line):
        line_copy(step).wait_send()
    swap.wait()
    to_section.wait()
    to_other_core.wait()


def start_pass(ids, embed, head, half, line, collective_id):
    rows, width = embed.shape
    high = -(-rows // 256) * 256
    vmem = pl.BlockSpec(memory_space=pltpu.VMEM)
    anywhere = pl.BlockSpec(memory_space=pl.ANY)
    dma = pltpu.SemaphoreType.DMA
    block = (width, half)
    return pl.pallas_call(
        partial(start_kernel, line),
        out_shape=[
            jax.ShapeDtypeStruct((line, 2, 2) + ids.shape, ids.dtype),
            jax.ShapeDtypeStruct((2,) + block, bf16),
            jax.ShapeDtypeStruct((head.shape[0] // 8 * 5, head.shape[1]), bf16),
            jax.ShapeDtypeStruct(head.shape, bf16),
        ],
        in_specs=[vmem, vmem, anywhere],
        out_specs=[vmem, vmem, anywhere, anywhere],
        scratch_shapes=[
            pltpu.VMEM((width, high), bf16),
            pltpu.VMEM((2, line) + block, bf16),
            pltpu.VMEM((2, line) + block, bf16),
            pltpu.VMEM((2, line) + block, bf16),
            pltpu.VMEM((line,) + block, bf16),
            pltpu.VMEM((line - 1,) + block, bf16),
            dma((line * 4 - 1,)),
            dma((line * 4 - 1,)),
            dma,
            dma((2, line)),
            dma((2, line)),
            dma((line,)),
            dma((line,)),
            dma((line - 1,)),
            dma((line - 1,)),
            dma,
            dma,
            dma((2,)),
            dma((2,)),
        ],
        compiler_params=pltpu.CompilerParams(
            collective_id=collective_id, has_side_effects=True, vmem_limit_bytes=40 * 2**20
        ),
        cost_estimate=pl.CostEstimate(flops=0, bytes_accessed=2**27, transcendentals=0),
    )(ids, embed, head)


def head_kernel(line, head_rows, length, *refs):
    final, targets, *heads = refs[:7]
    out, grads, lse_out, pick_out = refs[7:11]
    (table, rows_all, logits, probs, acc, parts, from_pair, from_line, stats, done) = refs[11:21]
    (head_sem, own_sem, give_send, give_recv, along_send, along_recv, pair_send, pair_recv) = refs[21:29]
    (stat_send, stat_recv, sum_send, sum_recv, line_send, line_recv, back_send, back_recv) = refs[29:37]
    last_send, last_recv = refs[37:]
    half = final.shape[0] // 2
    width = 2 * half
    padded = heads[0].shape[0]
    me_section = lax.axis_index("section")
    me_line = lax.axis_index("line")
    me_pair = lax.axis_index("pair")
    me_core = lax.axis_index("core")
    section_peer = {"section": 1 - me_section}
    pair_peer = {"pair": 1 - me_pair}
    chip_peers = []
    for step in range(1, 2 * line):
        chip_peers.append(
            {"line": lax.rem(me_line + step // 2, line), "pair": lax.rem(me_pair + step % 2, 2)}
        )
    greet(chip_peers + [section_peer, {"core": 1 - me_core}])

    def side(pair):
        return pl.ds(pl.multiple_of(pair * half, 16), half)

    loads = []
    for n, part in enumerate(heads):
        first = sum(other.shape[0] for other in heads[:n])
        target = table.at[pl.ds(first, part.shape[0])]
        loads.append(pltpu.make_async_copy(part, target, head_sem.at[n]))
    late = heads[3]
    last = remote(
        late,
        table.at[pl.ds(4 * padded - late.shape[0], late.shape[0])],
        last_send,
        last_recv,
        {"core": 1 - me_core},
    )
    last.start()
    for load in loads:
        load.start()

    quarter = half // 2

    def token_rows(place, pair, chunk):
        first = place * width + pair * half + chunk * quarter
        return pl.ds(pl.multiple_of(first, 16), quarter)

    def group(place):
        return pl.ds(pl.multiple_of(place * width, 128), width)

    def column_block(place, chunk):
        return rows_all.at[token_rows(place, me_pair, chunk)]

    def give(chunk):
        return remote(
            final.at[pl.ds(chunk * quarter, quarter)],
            column_block(me_line, chunk),
            give_send.at[chunk],
            give_recv.at[chunk],
            section_peer,
        )

    def along(step, way, chunk):
        block = column_block(me_line - way * step, chunk)
        turn = (way + 1) // 2
        return remote(
            block,
            block,
            along_send.at[turn, step, chunk],
            along_recv.at[turn, step, chunk],
            {"line": me_line + way},
        )

    def inside(place):
        return (place >= 0) & (place < line)

    def sends_along(step, way):
        return inside(me_line - way * step) & inside(me_line + way)

    def sideways(place, chunk):
        block = column_block(place, chunk)
        return remote(
            block, block, pair_send.at[place, chunk], pair_recv.at[place, chunk], pair_peer
        )

    def arrived_sideways(place, chunk):
        block = rows_all.at[token_rows(place, 1 - me_pair, chunk)]
        return remote(
            block, block, pair_send.at[place, chunk], pair_recv.at[place, chunk], pair_peer
        )

    @pl.when(me_section == 1)
    def _():
        for chunk in range(2):
            give(chunk).start()
        for chunk in range(2):
            keep = pltpu.make_async_copy(
                final.at[pl.ds(half + chunk * quarter, quarter)],
                column_block(me_line, chunk),
                own_sem.at[chunk],
            )
            keep.start()
            keep.wait()

    for chunk in range(2):

        @pl.when(me_section == 0)
        def _():
            give(chunk).wait_recv()

        for way in (1, -1):

            @pl.when(sends_along(0, way))
            def _():
                along(0, way, chunk).start()

        sideways(me_line, chunk).start()

    def pass_on(step):
        for chunk in range(2):
            for way in (1, -1):
                place = me_line - way * step

                @pl.when(inside(place))
                def _():
                    block = column_block(place, chunk)
                    turn = (way + 1) // 2
                    remote(
                        block,
                        block,
                        along_send.at[turn, step - 1, chunk],
                        along_recv.at[turn, step - 1, chunk],
                        {"line": me_line - way},
                    ).wait_recv()

                    @pl.when(inside(me_line + way))
                    def _():
                        along(step, way, chunk).start()

                    sideways(place, chunk).start()

    nearest = []
    for own in range(line):
        near = [own]
        for step in range(1, line):
            near += [place for place in (own - step, own + step) if 0 <= place < line]
        nearest.append(near)

    def by_distance(turn):
        place = 0
        for own in range(line):
            for n in range(line):
                hit = ((me_line == own) & (turn == n)).astype(jnp.int32)
                place = place + hit * nearest[own][n]
        return place

    def vocabulary(tile, rows):
        shard = tile * rows // padded
        first = lax.rem(tile * rows, padded)
        shard_section = lax.rem(me_section + shard // 2, 2)
        shard_core = lax.rem(me_core + lax.rem(shard, 2), 2)
        base = (((shard_section * line + me_line) * 2 + me_pair) * 2 + shard_core) * head_rows
        row = lax.broadcasted_iota(jnp.int32, (rows, 1), 0) + first
        return jnp.where(row < head_rows, row + base, -1)

    tile_rows = 512
    tiles = 4 * padded // tile_rows
    lowest = -1e30

    def score(turn, tops):
        place = by_distance(turn) if turn < line else None
        before = by_distance(turn - 1) if turn > 0 else None
        wanted = None if place is None else targets[place]

        def one(tile, carry):
            rows = pl.ds(pl.multiple_of(tile * tile_rows, tile_rows), tile_rows)
            out = []
            if place is not None:
                top, pick = carry[:2]
                entry = vocabulary(tile, tile_rows)
                part = nt(table[rows, :], rows_all[group(place), :])
                part = jnp.where(entry >= 0, part, lowest)
                logits[turn % 2, rows, :] = part
                out.append(jnp.maximum(top, jnp.max(part, 0, keepdims=True)))
                out.append(
                    pick + jnp.sum(jnp.where(entry == wanted, part, 0.0), 0, keepdims=True)
                )
            if before is not None:
                value = jnp.exp(logits[(turn - 1) % 2, rows, :] - tops)
                probs[rows, group(before)] = value.astype(bf16)
                out.append(carry[-1] + jnp.sum(value, 0, keepdims=True))
            return tuple(out)

        none = jnp.zeros((1, width), f32)
        start = () if place is None else (jnp.full((1, width), lowest, f32), none)
        start += () if before is None else (none,)
        result = lax.fori_loop(0, tiles, one, start)
        if place is not None:
            pick_out[place] = result[1]
        if before is not None:
            own = stats.at[me_line, me_pair, before]
            own[:, 0:width] = tops
            own[:, width : 2 * width] = result[-1]
            for n in range(len(chip_peers)):
                stat_copy(n, before).start()
        return None if place is None else result[0]

    def stat_copy(n, place):
        own = stats.at[me_line, me_pair, place]
        return remote(own, own, stat_send.at[n, place], stat_recv.at[n, place], chip_peers[n])

    def stat_wait(n, place):
        peer = chip_peers[n]
        source_line = lax.rem(2 * me_line + line - peer["line"], line)
        source_pair = peer["pair"]
        block = stats.at[source_line, source_pair, place]
        remote(block, block, stat_send.at[n, place], stat_recv.at[n, place], peer).wait_recv()

    for load in loads:
        load.wait()
    last.wait()

    tops = None
    for turn in range(line + 1):
        if turn + 1 < line:
            pass_on(turn + 1)
        if turn < line:
            for chunk in range(2):
                arrived_sideways(by_distance(turn), chunk).wait_recv()
        tops = score(turn, tops)

    def part_rows(pair, chunk):
        return pl.ds(pl.multiple_of(pair * half + chunk * quarter, 16), quarter)

    def sum_copy(turn, chunk):
        place = lax.rem(me_line + turn + 1, line)
        return remote(
            parts.at[place, part_rows(1 - me_pair, chunk)],
            from_pair.at[turn, pl.ds(chunk * quarter, quarter)],
            sum_send.at[turn, chunk],
            sum_recv.at[turn, chunk],
            pair_peer,
        )

    def line_copy(turn, chunk):
        place = lax.rem(me_line + turn + 1, line)
        return remote(
            parts.at[place, part_rows(me_pair, chunk)],
            from_line.at[turn, pl.ds(chunk * quarter, quarter)],
            line_send.at[turn, chunk],
            line_recv.at[turn, chunk],
            {"line": place},
        )

    def finish(turn, chunk):
        place = lax.rem(me_line + turn + 1, line)
        sum_copy(turn, chunk).wait_recv()
        own = parts.at[place, part_rows(me_pair, chunk)]
        other = from_pair.at[turn, pl.ds(chunk * quarter, quarter)]

        @pl.loop(0, quarter // 16)
        def _(block):
            rows = pl.ds(pl.multiple_of(block * 16, 16), 16)
            own[rows, :] = (own[rows, :].astype(f32) + other[rows, :].astype(f32)).astype(bf16)

    @pl.loop(0, line)
    def _(turn):
        place = lax.rem(me_line + turn + 1, line)
        for n in range(len(chip_peers)):
            stat_wait(n, place)
        tops = [stats[a, b, place, :, 0:width] for a in range(line) for b in range(2)]
        totals = [
            stats[a, b, place, :, width : 2 * width] for a in range(line) for b in range(2)
        ]
        top = tops[0]
        for value in tops[1:]:
            top = jnp.maximum(top, value)
        total = jnp.zeros_like(top)
        for peak, part in zip(tops, totals):
            total = total + part * jnp.exp(peak - top)
        lse = top + jnp.log(total)
        lse_out[place] = lse
        factor = jnp.exp(stats[me_line, me_pair, place, :, 0:width] - lse) / length
        wanted = targets[place]

        def scaled(tile):
            rows = pl.ds(tile * padded, padded)
            entry = vocabulary(tile, padded)
            grad = probs[rows, group(place)].astype(f32) * factor
            grad = (grad - jnp.where(entry == wanted, 1.0 / length, 0.0)).astype(bf16)
            probs[rows, group(place)] = grad
            return grad

        grad = scaled(0)
        for tile in range(4):
            product = tn(grad, table[pl.ds(tile * padded, padded), :])
            if tile < 3:
                grad = scaled(tile + 1)
                acc[...] = product if tile == 0 else acc[...] + product
            else:
                parts[place] = (acc[...] + product).astype(bf16)

        for chunk in range(2):
            sum_copy(turn, chunk).start()

        @pl.when(turn > 0)
        def _():
            for chunk in range(2):
                finish(turn - 1, chunk)
                line_copy(turn - 1, chunk).start()

    gh_rows = 256
    gh_tiles = 4 * padded // gh_rows

    def head_grads(first, last):
        @pl.loop(first, last)
        def _(tile):
            rows = pl.ds(pl.multiple_of(tile * gh_rows, gh_rows), gh_rows)
            value = jnp.dot(probs[rows, :], rows_all[...], preferred_element_type=f32)
            grads[rows, :] = value.astype(bf16)

    def back(chunk):
        part = pl.ds(chunk * quarter, quarter)
        return remote(
            done.at[part], out.at[part], back_send.at[chunk], back_recv.at[chunk], section_peer
        )

    head_grads(0, gh_tiles // 2)
    for chunk in range(2):
        finish(line - 1, chunk)
        for turn in range(line - 1):
            line_copy(turn, chunk).wait_recv()
        own = parts.at[me_line, part_rows(me_pair, chunk)]

        @pl.loop(0, quarter // 16)
        def _(block):
            rows = pl.ds(pl.multiple_of(block * 16, 16), 16)
            chunk_rows = pl.ds(pl.multiple_of(chunk * quarter + block * 16, 16), 16)
            value = own[rows, :].astype(f32)
            for turn in range(line - 1):
                value = value + from_line[turn, chunk_rows, :].astype(f32)
            done[chunk_rows, :] = value.astype(bf16)

        @pl.when(me_section == 0)
        def _():
            back(chunk).start()

    @pl.when(me_section == 0)
    def _():
        out[...] = jnp.zeros_like(out)

    @pl.when(me_section == 1)
    def _():
        out[pl.ds(half, half), :] = done[...]

    head_grads(gh_tiles // 2, gh_tiles)
    for chunk in range(2):

        @pl.when(me_section == 0)
        def _():
            back(chunk).wait_send()

        @pl.when(me_section == 1)
        def _():
            back(chunk).wait_recv()
            give(chunk).wait_send()

        for way in (1, -1):
            for step in range(line - 1):

                @pl.when(sends_along(step, way))
                def _():
                    along(step, way, chunk).wait_send()

        for place in range(line):
            sideways(place, chunk).wait_send()
        for turn in range(line):
            sum_copy(turn, chunk).wait_send()
        for turn in range(line - 1):
            line_copy(turn, chunk).wait_send()
    for place in range(line):
        for n in range(len(chip_peers)):
            stat_copy(n, place).wait_send()


def head_pass(final, targets, heads, line, head_rows, length, collective_id):
    tokens, deep = final.shape
    half = tokens // 2
    padded = heads[0].shape[0]
    vmem = pl.BlockSpec(memory_space=pltpu.VMEM)
    anywhere = pl.BlockSpec(memory_space=pl.ANY)
    dma = pltpu.SemaphoreType.DMA
    peers = 2 * line - 1
    return pl.pallas_call(
        partial(head_kernel, line, head_rows, length),
        out_shape=[
            jax.ShapeDtypeStruct((tokens, deep), bf16),
            jax.ShapeDtypeStruct((4 * padded, deep), bf16),
            jax.ShapeDtypeStruct((line, 1, tokens), f32),
            jax.ShapeDtypeStruct((line, 1, tokens), f32),
        ],
        in_specs=[vmem, vmem] + [anywhere] * len(heads),
        out_specs=[vmem] * 4,
        scratch_shapes=[
            pltpu.VMEM((4 * padded, deep), bf16),
            pltpu.VMEM((line * tokens, deep), bf16),
            pltpu.VMEM((2, 4 * padded, tokens), f32),
            pltpu.VMEM((4 * padded, line * tokens), bf16),
            pltpu.VMEM((tokens, deep), f32),
            pltpu.VMEM((line, tokens, deep), bf16),
            pltpu.VMEM((line, half, deep), bf16),
            pltpu.VMEM((line - 1, half, deep), bf16),
            pltpu.VMEM((line, 2, line, 1, 2 * tokens), f32),
            pltpu.VMEM((half, deep), bf16),
            dma((len(heads),)),
            dma((2,)),
            dma((2,)),
            dma((2,)),
            dma((2, line, 2)),
            dma((2, line, 2)),
            dma((line, 2)),
            dma((line, 2)),
            dma((peers, line)),
            dma((peers, line)),
            dma((line, 2)),
            dma((line, 2)),
            dma((line, 2)),
            dma((line, 2)),
            dma((2,)),
            dma((2,)),
            dma,
            dma,
        ],
        compiler_params=pltpu.CompilerParams(
            collective_id=collective_id, has_side_effects=True, vmem_limit_bytes=60 * 2**20
        ),
        cost_estimate=pl.CostEstimate(
            flops=24 * line * padded * tokens * deep, bytes_accessed=2**28, transcendentals=0
        ),
    )(final, targets, *heads)


def row_stats(values):
    centred = values - jnp.mean(values, -1, keepdims=True)
    factor = lax.rsqrt(jnp.mean(centred * centred, -1, keepdims=True) + epsilon)
    return centred * factor, factor


def two_heads(block):
    first = lax.broadcasted_iota(jnp.int32, block.shape, 1) < HEAD_DIM
    zero = jnp.zeros_like(block)
    return jnp.concatenate([jnp.where(first, block, zero), jnp.where(first, zero, block)], 0)


def one_block(stacked):
    rows = stacked.shape[0] // 2
    first = lax.broadcasted_iota(jnp.int32, (rows, stacked.shape[1]), 1) < HEAD_DIM
    return jnp.where(first, stacked[:rows], stacked[rows:])


def attention_weights(queries, keys):
    scores = nt(keys, queries) * (1.0 / math.sqrt(HEAD_DIM))
    exped = jnp.exp(scores - jnp.max(scores, 0, keepdims=True))
    return exped * (1.0 / jnp.sum(exped, 0, keepdims=True))


def tile_of(index, size):
    return pl.ds(pl.multiple_of(index * size, size), size)


def forward_kernel(seqs, *refs):
    refs = list(refs)

    def take(number):
        return [refs.pop(0) for _ in range(number)]

    start, scale, bias, gain = take(4)
    weights = take(4)
    head, head_early = take(2)
    out, final, x, joined, mixed, middle, entry_attn, entry_mlp, slope, hidden = take(10)
    head_late, head_fourth = take(2)
    w_qkv, w_out, w_up, w_down, x_total, arrived, sems, relay_send, relay_recv = take(9)
    head_send, head_recv = refs
    width = start.shape[1]
    length = start.shape[0] // seqs
    me_section = lax.axis_index("section")
    section_peer = {"section": 1 - me_section}
    load_qkv, load_out, load_up, load_down = [
        pltpu.make_async_copy(source.at[0], target, sems.at[n])
        for n, (source, target) in enumerate(zip(weights, (w_qkv, w_out, w_up, w_down)))
    ]
    load_qkv.start()
    core_peer = {"core": 1 - lax.axis_index("core")}
    greet([section_peer, core_peer])
    each = head_early.shape[0]
    to_section = remote(
        head.at[pl.ds(each, head_late.shape[0])],
        head_late,
        head_send.at[0],
        head_recv.at[0],
        section_peer,
    )
    to_section.start()
    to_core = remote(head_early, head_fourth, head_send.at[1], head_recv.at[1], core_peer)
    to_core.start()

    def relay(seq):
        rows = pl.ds(seq * length, length)
        return remote(
            out.at[rows], arrived.at[rows], relay_send.at[seq], relay_recv.at[seq], section_peer
        )

    tile = 512

    def enter(seq):
        rows = pl.ds(seq * length, length)

        @pl.when(me_section == 0)
        def _():
            x[rows, :] = start[rows, :]

        @pl.when(me_section == 1)
        def _():
            relay(seq).wait_recv()
            x[rows, :] = arrived[rows, :].astype(f32)

        normed, _ = row_stats(x[rows, :])
        entry_attn[rows, :] = (normed * scale[seq, :, :width]).astype(bf16)

    def join(first, count):
        rows = pl.ds(first * length, count * length)

        @pl.loop(0, 3 * width // tile)
        def _(index):
            cols = tile_of(index, tile)
            joined[rows, cols] = nn(entry_attn[rows, :], w_qkv[:, cols]).astype(bf16)

    for seq in range(seqs - 1):
        enter(seq)
    load_qkv.wait()
    load_out.start()
    load_up.start()
    join(0, seqs - 1)
    enter(seqs - 1)
    join(seqs - 1, 1)
    load_out.wait()
    load_down.start()
    pairs = width // 128

    @pl.loop(0, pairs)
    def _(pair):
        cols = tile_of(pair, 128)
        for seq in range(seqs):
            rows = pl.ds(seq * length, length)
            queries = two_heads(joined[rows, cols])
            keys = joined[rows, tile_of(pair + pairs, 128)]
            values = joined[rows, tile_of(pair + 2 * pairs, 128)]
            probs = attention_weights(queries, keys).astype(bf16)
            mixed[rows, cols] = one_block(tn(probs, values)).astype(bf16)

    @pl.loop(0, width // tile)
    def _(index):
        cols = tile_of(index, tile)
        middle[:, cols] = x[:, cols] + nn(mixed[...], w_out[:, cols])

    for seq in range(seqs):
        rows = pl.ds(seq * length, length)
        normed, _ = row_stats(middle[rows, :])
        entry_mlp[rows, :] = (normed * scale[seq, :, width:]).astype(bf16)

    load_up.wait()
    load_down.wait()

    def gelu_of(up, rows, cols):
        below = 0.5 + 0.5 * lax.erf(up * math.sqrt(0.5))
        value = (up * below).astype(bf16)
        density = jnp.exp(-0.5 * up * up) * (1.0 / math.sqrt(2.0 * math.pi))
        slope[rows, cols] = (below + up * density).astype(bf16)
        hidden[rows, cols] = value
        return value

    def feed_forward(first, count):
        rows = pl.ds(first * length, count * length)

        def one(index, total):
            sides = [tile_of(2 * index + side, tile) for side in range(2)]
            ups = [nn(entry_mlp[rows, :], w_up[:, cols]) + bias[:, cols] for cols in sides]
            both = jnp.concatenate([gelu_of(up, rows, cols) for up, cols in zip(ups, sides)], 1)
            x_total[rows, :] += nn(both, w_down[tile_of(index, 2 * tile), :])
            return total

        x_total[rows, :] = middle[rows, :]
        lax.fori_loop(0, w_up.shape[1] // (2 * tile), one, 0)
        for seq in range(first, first + count):
            rows = pl.ds(seq * length, length)
            value = x_total[rows, :].astype(bf16)
            out[rows, :] = value

            @pl.when(me_section == 0)
            def _():
                relay(seq).start()

            normed, _ = row_stats(value.astype(f32))
            final[rows, :] = (normed * gain[...]).astype(bf16)

    feed_forward(0, seqs)

    to_section.wait()
    to_core.wait()

    @pl.when(me_section == 0)
    def _():
        for seq in range(seqs):
            relay(seq).wait_send()


def layer_scratch(width, hidden):
    return [
        pltpu.VMEM((width, 3 * width), bf16),
        pltpu.VMEM((width, width), bf16),
        pltpu.VMEM((width, hidden), bf16),
        pltpu.VMEM((hidden, width), bf16),
    ]


def forward_pass(start, scale, weights, gain, head, head_early, collective_id):
    w_qkv, w_out, w_up, b_hidden, w_down = weights
    tokens, width = start.shape
    wide = w_up.shape[-1]
    seqs = scale.shape[0]
    vmem = pl.BlockSpec(memory_space=pltpu.VMEM)
    anywhere = pl.BlockSpec(memory_space=pl.ANY)

    def low(columns):
        return (tokens, columns), bf16

    exact = ((tokens, width), f32)
    results = [low(width), low(width), exact, low(3 * width), low(width), exact, low(width)]
    results += [low(width), low(wide), low(wide)]
    results += [((head.shape[0] - head_early.shape[0], width), bf16), (head_early.shape, bf16)]
    scratch = layer_scratch(width, wide) + [pltpu.VMEM(*exact), pltpu.VMEM(*low(width))]
    dma = pltpu.SemaphoreType.DMA
    flops = 4 * tokens * (4 * width * width + 2 * width * wide)
    return pl.pallas_call(
        partial(forward_kernel, seqs),
        out_shape=[jax.ShapeDtypeStruct(*item) for item in results],
        in_specs=[vmem] * 4 + [anywhere] * 6,
        out_specs=[vmem] * (len(results) - 2) + [anywhere] * 2,
        scratch_shapes=scratch + [dma((4,)), dma((seqs,)), dma((seqs,)), dma((2,)), dma((2,))],
        compiler_params=pltpu.CompilerParams(
            collective_id=collective_id, has_side_effects=True, vmem_limit_bytes=60 * 2**20
        ),
        cost_estimate=pl.CostEstimate(flops=2 * flops, bytes_accessed=2**25, transcendentals=0),
    )(start, scale, b_hidden, gain, w_qkv, w_out, w_up, w_down, head, head_early)


def norm_grads(source, total, grad_middle, scale, grad_cond, half, seq, store):
    width = total.shape[1]
    length = total.shape[0] // scale.shape[0]
    rows = pl.ds(seq * length, length)
    cols = pl.ds(half * width, width)
    normed, factor = row_stats(source[rows, :])
    gradient = total[rows, :]
    if grad_cond is not None:
        grad_cond[seq, :, cols] = jnp.sum(gradient * normed, 0, keepdims=True)
    scaled = gradient * scale[seq, :, cols]
    back = factor * (
        scaled
        - jnp.mean(scaled, -1, keepdims=True)
        - normed * jnp.mean(scaled * normed, -1, keepdims=True)
    )
    store(rows, grad_middle[rows, :] + back)


def attention_grads(joined, grad_mixed, grad_joined, pair, seqs):
    pairs = grad_mixed.shape[1] // 128
    length = grad_mixed.shape[0] // seqs
    shrink = 1.0 / math.sqrt(HEAD_DIM)
    cols = tile_of(pair, 128)
    key_cols = tile_of(pair + pairs, 128)
    value_cols = tile_of(pair + 2 * pairs, 128)
    for seq in range(seqs):
        rows = pl.ds(seq * length, length)
        queries = two_heads(joined[rows, cols])
        keys = joined[rows, key_cols]
        probs = attention_weights(queries, keys)
        grads = two_heads(grad_mixed[rows, cols])
        grad_probs = nt(joined[rows, value_cols], grads)
        inner = jnp.sum(grad_probs * probs, 0, keepdims=True)
        grad_scores = (probs * (grad_probs - inner)).astype(bf16)
        grad_joined[rows, cols] = (one_block(tn(grad_scores, keys)) * shrink).astype(bf16)
        grad_joined[rows, key_cols] = (nn(grad_scores, queries) * shrink).astype(bf16)
        grad_joined[rows, value_cols] = nn(probs.astype(bf16), grads).astype(bf16)


def backward_kernel(begin, seqs, *refs):
    refs = list(refs)

    def take(number):
        return [refs.pop(0) for _ in range(number)]

    if begin:
        incoming, other, hidden, entry = take(4)
        far = take(3)
        grad_middle, total, grad_bias, down_out, up_out = take(5)
        grad_low, grad_up, entry_turned, down_weight, up_weight, out_sem = take(6)
        near = take(3)
    else:
        scale, incoming, other, gain = take(4)
        far = take(8)
        out, grad_top, grad_gain = take(3)
        grad_low, grad_up, grad_attn, grad_joined = take(4)
        near = take(8)
        total, grad_middle, grad_mixed = take(3)
    (sems,) = refs
    if begin:
        slope, w_up, w_down = near
        load_slope = pltpu.make_async_copy(far[0], slope, sems.at[0])
        load_up = pltpu.make_async_copy(far[1].at[0], w_up, sems.at[1])
        load_down = pltpu.make_async_copy(far[2].at[0], w_down, sems.at[2])
    else:
        slope, w_up, w_down, x, middle, joined, w_qkv, w_out = near
        load_slope = pltpu.make_async_copy(far[0], slope, sems.at[0])
        load_up = pltpu.make_async_copy(far[1].at[0], w_up, sems.at[1])
        load_down = pltpu.make_async_copy(far[2].at[0], w_down, sems.at[2])
        load_x = pltpu.make_async_copy(far[3], x, sems.at[3])
        load_middle = pltpu.make_async_copy(far[4], middle, sems.at[4])
        load_joined = pltpu.make_async_copy(far[5], joined, sems.at[5])
        load_qkv = pltpu.make_async_copy(far[6].at[0], w_qkv, sems.at[6])
        load_out = pltpu.make_async_copy(far[7].at[0], w_out, sems.at[7])
    width = incoming.shape[1]
    length = incoming.shape[0] // seqs
    load_down.start()
    load_slope.start()
    if begin:
        entry_turned[...] = entry[...].T

    for seq in range(seqs):
        rows = pl.ds(seq * length, length)
        if begin:
            first = (lax.axis_index("section") == 0).astype(f32)
            value = incoming[rows, :].astype(f32) * first + other[rows, :] * (1.0 - first)
        else:
            normed, factor = row_stats(other[rows, :].astype(f32))
            gradient = incoming[rows, :].astype(f32)
            part = jnp.sum(gradient * normed, 0, keepdims=True)
            grad_gain[...] = part if seq == 0 else grad_gain[...] + part
            scaled = gradient * gain[...]
            value = factor * (
                scaled
                - jnp.mean(scaled, -1, keepdims=True)
                - normed * jnp.mean(scaled * normed, -1, keepdims=True)
            )
            grad_top[rows, :] = value
        grad_middle[rows, :] = value
        grad_low[rows, :] = value.astype(bf16)

    load_down.wait()
    load_slope.wait()
    load_up.start()
    if not begin:
        load_middle.start()
        load_out.start()
        load_joined.start()
    tile = 1024

    @pl.loop(0, w_up.shape[1] // tile)
    def _(index):
        cols = tile_of(index, tile)
        grad_hidden = nt(grad_low[...], w_down[cols, :])
        value = (grad_hidden * slope[:, cols].astype(f32)).astype(bf16)
        grad_up[:, cols] = value
        if begin:
            grad_bias[:, cols] = jnp.sum(value.astype(f32), 0, keepdims=True)
            down_weight[cols, :] = tn(hidden[:, cols], grad_low[...]).astype(bf16)
            pltpu.make_async_copy(
                down_weight.at[cols], down_out.at[cols], out_sem.at[0, index]
            ).start()
            up_weight[:, cols] = nn(entry_turned[...], value).astype(bf16)

    if begin:
        whole_up = pltpu.make_async_copy(up_weight, up_out, out_sem.at[1, 0])
        whole_up.start()
    load_up.wait()
    if not begin:
        load_middle.wait()
        load_out.wait()
        load_joined.wait()
        load_qkv.start()
        load_x.start()

    @pl.loop(0, width // 256)
    def _(index):
        total[:, tile_of(index, 256)] = nt(grad_up[...], w_up[tile_of(index, 256), :])

    if begin:
        for index in range(w_up.shape[1] // tile):
            cols = pl.ds(index * tile, tile)
            pltpu.make_async_copy(
                down_weight.at[cols], down_out.at[cols], out_sem.at[0, index]
            ).wait()
        whole_up.wait()
        return

    def store_middle(rows, value):
        grad_middle[rows, :] = value
        grad_attn[rows, :] = value.astype(bf16)

    for seq in range(seqs):
        norm_grads(middle, total, grad_middle, scale, None, 1, seq, store_middle)

    @pl.loop(0, width // 512)
    def _(index):
        part = tile_of(index, 512)
        grad_mixed[:, part] = nt(grad_attn[...], w_out[part, :]).astype(bf16)

    @pl.loop(0, width // 128)
    def _(pair):
        attention_grads(joined, grad_mixed, grad_joined, pair, seqs)

    load_qkv.wait()
    load_x.wait()

    @pl.loop(0, width // 256)
    def _(index):
        total[:, tile_of(index, 256)] = nt(grad_joined[...], w_qkv[tile_of(index, 256), :])

    def store_out(rows, value):
        out[rows, :] = value.astype(bf16)

    for seq in range(seqs):
        norm_grads(x, total, grad_middle, scale, None, 0, seq, store_out)


def backward_pass(grad_final, block_out, gain, scale, kept, weights):
    w_qkv, w_out, w_up, _, w_down = weights
    x, joined, _, middle, _, _, slope, _ = kept
    tokens, width = x.shape
    wide = w_up.shape[-1]
    vmem = pl.BlockSpec(memory_space=pltpu.VMEM)
    anywhere = pl.BlockSpec(memory_space=pl.ANY)
    exact = ((tokens, width), f32)
    low = ((tokens, width), bf16)
    lows = [low, ((tokens, wide), bf16), low, ((tokens, 3 * width), bf16)]
    near = [
        ((tokens, wide), bf16),
        ((width, wide), bf16),
        ((wide, width), bf16),
        exact,
        exact,
        ((tokens, 3 * width), bf16),
        ((width, 3 * width), bf16),
        ((width, width), bf16),
    ]
    flops = 4 * tokens * (4 * width * width + 2 * width * wide)
    return pl.pallas_call(
        partial(backward_kernel, False, scale.shape[0]),
        out_shape=[jax.ShapeDtypeStruct(*item) for item in [low, exact, ((1, width), f32)]],
        in_specs=[vmem] * 4 + [anywhere] * 8,
        out_specs=[vmem] * 3,
        scratch_shapes=[pltpu.VMEM(*item) for item in lows + near + [exact, exact, low]]
        + [pltpu.SemaphoreType.DMA((8,))],
        compiler_params=pltpu.CompilerParams(vmem_limit_bytes=60 * 2**20),
        cost_estimate=pl.CostEstimate(flops=flops, bytes_accessed=2**25, transcendentals=0),
    )(scale, grad_final, block_out, gain, slope, w_up, w_down, x, middle, joined, w_qkv, w_out)


def backward_begin(returned, grad_top, seqs, hidden, entry, slope, w_up, w_down):
    tokens, width = grad_top.shape
    wide = w_up.shape[-1]
    vmem = pl.BlockSpec(memory_space=pltpu.VMEM)
    anywhere = pl.BlockSpec(memory_space=pl.ANY)
    exact = ((tokens, width), f32)
    low = ((tokens, width), bf16)
    wide_low = ((tokens, wide), bf16)
    up, down = ((width, wide), bf16), ((wide, width), bf16)
    results = [exact, exact, ((1, wide), f32), down, up]
    inside = [low, wide_low, ((width, tokens), bf16), down, up]
    return pl.pallas_call(
        partial(backward_kernel, True, seqs),
        out_shape=[jax.ShapeDtypeStruct(*item) for item in results],
        in_specs=[vmem] * 4 + [anywhere] * 3,
        out_specs=[vmem] * 3 + [anywhere] * 2,
        scratch_shapes=[pltpu.VMEM(*item) for item in inside]
        + [pltpu.SemaphoreType.DMA((2, wide // 1024))]
        + [pltpu.VMEM(*item) for item in (wide_low, up, down)]
        + [pltpu.SemaphoreType.DMA((3,))],
        compiler_params=pltpu.CompilerParams(vmem_limit_bytes=60 * 2**20),
        cost_estimate=pl.CostEstimate(
            flops=16 * tokens * width * wide, bytes_accessed=2**25, transcendentals=0
        ),
    )(returned, grad_top, hidden, entry, slope, w_up, w_down)


def tail_kernel(line, seqs, lag, *refs):
    refs = list(refs)

    def take(number):
        return [refs.pop(0) for _ in range(number)]

    scale, rest, factor_one, factor_two, embedded, noisy, w_in = take(7)
    far = take(9)
    parts = take(2)
    (head_part,) = take(1)
    outs = take(5)
    head_out, smalls, rows_all = take(3)
    near = take(9)
    grad_attn, grad_mixed, grad_joined, grad_first, grad_cond, in_weight = take(6)
    rows_own, small_wide, small_own = take(3)
    own, from_core, slots = take(2), take(5), take(5)
    head_own, head_core, head_section, last_total = take(4)
    far_sem, load_sem, core_send, core_recv, ring_send, ring_recv, credit = take(7)
    keep_sem, packet_send, packet_recv, wide_send, wide_recv, rows_send, rows_recv = take(7)
    head_sem, head_send, head_recv, cross_send, cross_recv = take(5)
    grad_middle, grad_entry, middle, x, joined, mixed, entry_attn, w_out, w_qkv = near
    inside = [w_qkv, w_out, in_weight]
    groups = ((0, 1), (2, 3, 4))
    chips = 2 * line
    width = x.shape[1]
    me_section = lax.axis_index("section")
    me_line = lax.axis_index("line")
    me_pair = lax.axis_index("pair")
    me_core = lax.axis_index("core")
    position = me_line + me_pair * (chips - 1 - 2 * me_line)
    section_peer = {"section": 1 - me_section}
    core_peer = {"core": 1 - me_core}
    ways = (1, -1)
    ring_peers = []
    for way in ways:
        peer_line, peer_pair = ring_place(lax.rem(position + way + chips, chips), line)
        ring_peers.append({"line": peer_line, "pair": peer_pair})
    greet([core_peer, section_peer] + ring_peers)

    shapes = [ref.shape[-2:] for ref in from_core]

    def block_of(turn, step):
        ahead = lax.rem(position - ways[turn] * (1 + step) + 2 * chips, chips)
        return ring_place(ahead, line)

    def portion(index, turn):
        high, wide = shapes[index]
        if high % 32 == 0:
            return turn * (high // 2), high // 2, 0, wide
        return 0, high, turn * (wide // 2), wide // 2

    def half_of(index, turn):
        first, rows, col, cols = portion(index, turn)
        return pl.ds(first, rows), pl.ds(col, cols)

    def inside_rows(index, place, pair, core, first, rows):
        base = ((place * 2 + pair) * 2 + core) * shapes[index][0] + first
        return pl.ds(pl.multiple_of(base, 16), rows)

    def source(index, turn, step, core):
        place, pair = block_of(turn, step)
        rows, cols = half_of(index, turn)
        if index < 2:
            return parts[index].at[place, pair, core, rows, cols]
        first, high = portion(index, turn)[:2]
        return inside[index - 2].at[inside_rows(index, place, pair, core, first, high), cols]

    def load(index, turn, step):
        return pltpu.make_async_copy(
            source(index, turn, step, me_core),
            own[index].at[(step % 2, *half_of(index, turn))],
            load_sem.at[index, turn, step],
        )

    def core_copy(index, turn, step):
        return remote(
            source(index, turn, step, 1 - me_core),
            from_core[index].at[(step % 3, *half_of(index, turn))],
            core_send.at[index, turn, step],
            core_recv.at[index, turn, step],
            core_peer,
        )

    def ring_copy(index, turn, step):
        half = half_of(index, turn)
        passed = from_core[index].at[(0, *half)] if step == 0 else slots[index].at[(step - 1, *half)]
        return remote(
            passed,
            slots[index].at[(step, *half)],
            ring_send.at[index, turn, step],
            ring_recv.at[index, turn, step],
            ring_peers[turn],
        )

    def to_core(group, step):
        if step >= 3:
            pl.semaphore_wait(credit.at[group], 1)
        for index in groups[group]:
            for turn in range(2):
                if index < 2:
                    load(index, turn, step).start()
                core_copy(index, turn, step).start()

    def stop(group, step, between):
        first, last = step == 0, step == chips - 1
        for index in groups[group]:
            for turn in range(2):
                start, rows, left, wide = portion(index, turn)
                tile = min(wide, 512)
                if index < 2:
                    load(index, turn, step).wait()
                core_copy(index, turn, step).wait_recv()
                if not first:
                    ring_copy(index, turn, step - 1).wait_recv()
                place, pair = block_of(turn, step)

                @pl.loop(0, rows // 16)
                def _(block):
                    row = pl.ds(pl.multiple_of(start + block * 16, 16), 16)
                    if index >= 2:
                        own_row = inside_rows(index, place, pair, me_core, start + block * 16, 16)
                    for col in range(left, left + wide, tile):
                        cols = pl.ds(col, tile)
                        if index < 2:
                            mine = own[index][step % 2, row, cols]
                        else:
                            mine = inside[index - 2][own_row, cols]
                        total = from_core[index][step % 3, row, cols].astype(f32)
                        total = total + mine.astype(f32)
                        if not first:
                            total = total + slots[index][step - 1, row, cols].astype(f32)
                        if last and index == 4:
                            last_total[row, cols] = total
                        elif last:
                            outs[index][row, cols] = total.astype(bf16)
                        elif first:
                            from_core[index][0, row, cols] = total.astype(bf16)
                        else:
                            slots[index][step - 1, row, cols] = total.astype(bf16)

                if not last:
                    ring_copy(index, turn, step).start()
                between()
        if step == 1:
            for index in groups[group]:
                for turn in range(2):
                    ring_copy(index, turn, 0).wait_send()
        if 1 <= step <= 4:
            amount = 2 if step == 1 else 1
            pl.semaphore_signal(
                credit.at[group], inc=amount, device_id=core_peer, device_id_type=MESH
            )

    hops = (line, line - 1)

    def packet_blocks(place, pair):
        return [smalls.at[place, pair, me_core], rows_all.at[place, pair, me_core]]

    def packet_hops(turn, hop, away):
        place, pair = ring_place(
            lax.rem(position - ways[turn] * (hop + away) + 2 * chips, chips), line
        )
        return [
            remote(
                block,
                block,
                packet_send.at[n, turn, hop],
                packet_recv.at[n, turn, hop],
                ring_peers[turn],
            )
            for n, block in enumerate(packet_blocks(place, pair))
        ]

    def pass_packets(hop):
        for turn in range(2):
            if 0 < hop <= hops[turn]:
                for copy in packet_hops(turn, hop - 1, 1):
                    copy.wait_recv()
            if hop < hops[turn]:
                for copy in packet_hops(turn, hop, 0):
                    copy.start()

    small_slot, rows_slot = packet_blocks(me_line, me_pair)
    keep_small = pltpu.make_async_copy(small_own, small_slot, keep_sem.at[0])
    keep_rows = pltpu.make_async_copy(rows_own, rows_slot, keep_sem.at[1])
    rows_over = remote(rows_own, rows_slot, rows_send, rows_recv, section_peer)
    across = [
        remote(block, block, wide_send.at[n], wide_recv.at[n], core_peer)
        for n, block in enumerate([smalls.at[:, :, me_core], rows_all.at[:, :, me_core]])
    ]
    def packets_ready():
        keep_small.wait()

        @pl.when(me_section == 0)
        def _():
            keep_rows.wait()

        @pl.when(me_section == 1)
        def _():
            rows_over.wait_recv()

    high = head_part.shape[0] // 4

    def shard(n):
        return head_part.at[pl.ds(n * high, high)]

    head_loads = [
        pltpu.make_async_copy(shard(2 * n), head_own.at[n], head_sem.at[n]) for n in range(2)
    ]
    head_copies = [
        remote(shard(2 * n + 1), head_core.at[n], head_send.at[n], head_recv.at[n], core_peer)
        for n in range(2)
    ]
    head_copies.append(
        remote(head_core.at[1], head_section, head_send.at[2], head_recv.at[2], section_peer)
    )

    def head_over_cores():
        for copy in head_loads:
            copy.wait()
        for copy in head_copies[:2]:
            copy.wait_recv()

        @pl.loop(0, high // 16)
        def _(block):
            rows = pl.ds(pl.multiple_of(block * 16, 16), 16)
            value = head_core[1, rows, :].astype(f32) + head_own[1, rows, :].astype(f32)
            head_core[1, rows, :] = value.astype(bf16)

        head_copies[2].start()

    def head_over_sections():
        head_copies[2].wait_recv()

        @pl.loop(0, high // 16)
        def _(block):
            rows = pl.ds(pl.multiple_of(block * 16, 16), 16)
            value = head_core[0, rows, :].astype(f32) + head_own[0, rows, :].astype(f32)
            value = value + head_section[rows, :].astype(f32)
            head_out[rows, :] = value.astype(bf16)

    far_copies = []
    for n, (where, target) in enumerate(zip(far, near)):
        where = where.at[0] if n >= 7 else where
        far_copies.append(pltpu.make_async_copy(where, target, far_sem.at[n]))

    def waits(*numbers):
        for n in numbers:
            far_copies[n].wait()

    def store_middle(rows, value):
        grad_middle[rows, :] = value
        grad_attn[rows, :] = value.astype(bf16)

    def store_first(rows, value):
        grad_first[rows, :] = value.astype(bf16)

    def second_norm(seq):
        if seq == 0:
            waits(0, 1, 2)
        norm_grads(middle, grad_entry, grad_middle, scale, grad_cond, 1, seq, store_middle)

    def mixed_grads(index):
        if index == 0:
            waits(7)
        part = pl.ds(index * 512, 512)
        grad_mixed[:, part] = nt(grad_attn[...], w_out[part, :]).astype(bf16)

    def heads_grads(pair):
        if pair == 0:
            waits(4)
        attention_grads(joined, grad_mixed, grad_joined, pair, seqs)

    def entry_grads(index):
        if index == 0:
            waits(8)
        part = pl.ds(index * 256, 256)
        grad_entry[:, part] = nt(grad_joined[...], w_qkv[part, :])

    def first_norm(seq):
        if seq == 0:
            waits(3)
        norm_grads(x, grad_entry, grad_middle, scale, grad_cond, 0, seq, store_first)

    def embedding_rows(_):
        grad_noisy = nt(grad_first[...], w_in[...])
        inner = jnp.mean(grad_noisy * embedded[...], -1, keepdims=True)
        value = factor_one[...] * grad_noisy - factor_two[...] * embedded[...] * inner
        rows_own[...] = value.astype(bf16)

        @pl.when(me_section == 0)
        def _():
            keep_rows.start()
            rows_over.start()

    def small_rows(_):
        each = small_wide.shape[1]
        for seq in range(seqs):
            for n in range(2 * width // each):
                row = pl.ds(seq * (2 * width // each) + n, 1)
                small_wide[row, :] = grad_cond[seq, :, pl.ds(n * each, each)]
        small_wide[pl.ds(seqs * 2 * width // each, rest.shape[0]), :] = rest[...]
        small_own[...] = small_wide[...].astype(bf16)
        keep_small.start()

    def input_weight(_):
        in_weight[...] = tn(noisy[...], grad_first[...]).astype(bf16)

    def qkv_weight(index):
        if index == 0:
            waits(6)
        part = pl.ds(index * 256, 256)
        w_qkv[part, :] = tn(entry_attn[:, part], grad_joined[...]).astype(bf16)

    def out_weight(index):
        if index == 0:
            waits(5)
        part = pl.ds(index * 512, 512)
        w_out[part, :] = tn(mixed[:, part], grad_attn[...]).astype(bf16)

    steps = []
    for step, number in (
        (second_norm, seqs),
        (mixed_grads, width // 512),
        (heads_grads, width // 128),
        (entry_grads, width // 256),
        (first_norm, seqs),
        (embedding_rows, 1),
        (small_rows, 1),
        (input_weight, 1),
        (qkv_weight, width // 256),
        (out_weight, width // 512),
    ):
        steps += [partial(step, n) for n in range(number)]
    at_once = -(-len(steps) // (4 * lag))

    def work():
        for _ in range(at_once):
            if steps:
                steps.pop(0)()

    def nothing():
        pass

    to_core(0, 0)
    to_core(0, 1)
    for copy in far_copies:
        copy.start()
    stop(0, 0, work)
    for turn in range(1, chips + lag):
        if turn + 1 < chips:
            to_core(0, turn + 1)
        if turn == 1:
            for copy in head_loads + head_copies[:2]:
                copy.start()
        if turn == lag:
            to_core(1, 0)
        if lag <= turn and turn - lag + 1 < chips:
            to_core(1, turn - lag + 1)
        if turn < chips:
            stop(0, turn, work if turn < lag else nothing)
        if turn >= lag:
            stop(1, turn - lag, nothing)
        hop = turn - lag - 2
        if hop == 0:
            packets_ready()
        if 0 <= hop <= line:
            pass_packets(hop)
        if hop == line:
            for copy in across:
                copy.start()
        if turn == 3:
            head_over_cores()
        if turn == chips + lag - 2:
            head_over_sections()
    each = outs[4].shape[0]
    give = remote(last_total.at[pl.ds(each, each)], outs[4], cross_send, cross_recv, section_peer)

    @pl.when(me_section == 0)
    def _():
        give.start()
        outs[4][...] = last_total[pl.ds(0, each), :]

    for copy in across:
        copy.wait()
    for copy in head_copies:
        copy.wait_send()
    for turn in range(2):
        for hop in range(hops[turn]):
            for copy in packet_hops(turn, hop, 0):
                copy.wait_send()
    for index in range(5):
        for turn in range(2):
            for step in range(chips):
                core_copy(index, turn, step).wait_send()
                if 0 < step < chips - 1:
                    ring_copy(index, turn, step).wait_send()

    @pl.when(me_section == 0)
    def _():
        rows_over.wait_send()
        give.wait_send()

    @pl.when(me_section == 1)
    def _():
        give.wait_recv()


def tail_pass(scale, rest, factors, embedded, noisy, w_in, far, parts, head_part, collective_id):
    grad_middle = far[0]
    tokens, width = grad_middle.shape
    seqs = scale.shape[0]
    line = parts[0].shape[0]
    chips = 2 * line
    count = 4 * line
    emb_width = noisy.shape[1]
    vmem = pl.BlockSpec(memory_space=pltpu.VMEM)
    anywhere = pl.BlockSpec(memory_space=pl.ANY)
    dma = pltpu.SemaphoreType.DMA
    shapes = [part.shape[-2:] for part in parts]
    shapes += [
        (width // count, 3 * width),
        (width // count, width),
        (emb_width // count, width),
    ]
    each = shapes[4][0] // 2
    high = head_part.shape[0] // 4
    small = (seqs * 2 * width // emb_width + rest.shape[0], emb_width)
    exact = ((tokens, width), f32)
    low = ((tokens, width), bf16)
    three = ((tokens, 3 * width), bf16)
    rows = (tokens, emb_width)
    results = [(shape, bf16) for shape in shapes[:4]]
    results += [((each, width), f32), ((high, width), bf16)]
    results += [((line, 2, 2) + small, bf16), ((line, 2, 2) + rows, bf16)]
    room = [exact, exact, exact, exact, three, low, low]
    room += [((width, width), bf16), ((width, 3 * width), bf16)]
    room += [low, low, three, low, ((seqs, 1, 2 * width), f32), ((emb_width, width), bf16)]
    room += [(rows, bf16), (small, f32), (small, bf16)]
    room += [((2,) + shape, bf16) for shape in shapes[:2]]
    room += [((3,) + shape, bf16) for shape in shapes]
    room += [((chips - 1,) + shape, bf16) for shape in shapes]
    room += [((2, high, width), bf16), ((2, high, width), bf16), ((high, width), bf16)]
    room += [(shapes[4], f32)]
    scratch = [pltpu.VMEM(*item) for item in room]
    scratch += [dma((9,)), dma((2, 2, chips)), dma((5, 2, chips)), dma((5, 2, chips))]
    scratch += [dma((5, 2, chips - 1)), dma((5, 2, chips - 1)), pltpu.SemaphoreType.REGULAR((2,))]
    scratch += [dma((2,)), dma((2, 2, line)), dma((2, 2, line)), dma((2,)), dma((2,)), dma, dma]
    scratch += [dma((2,)), dma((3,)), dma((3,)), dma, dma]
    return pl.pallas_call(
        partial(tail_kernel, line, seqs, line),
        out_shape=[jax.ShapeDtypeStruct(*item) for item in results],
        in_specs=[vmem] * 7 + [anywhere] * 12,
        out_specs=[vmem] * 6 + [anywhere] * 2,
        scratch_shapes=scratch,
        compiler_params=pltpu.CompilerParams(
            collective_id=collective_id, has_side_effects=True, vmem_limit_bytes=62 * 2**20
        ),
        cost_estimate=pl.CostEstimate(flops=0, bytes_accessed=2**29, transcendentals=0),
    )(scale, rest, *factors, embedded, noisy, w_in, *far, *parts, head_part)


def finish_kernel(line, head_rows, *refs):
    ids, rows, *lows = refs[:7]
    *exacts, grad_embed, total = refs[7:]
    me_section = lax.axis_index("section")
    me_line = lax.axis_index("line")
    me_pair = lax.axis_index("pair")
    me_core = lax.axis_index("core")
    high = total.shape[0]
    base = (((me_section * line + me_line) * 2 + me_pair) * 2 + me_core) * grad_embed.shape[0]
    tile = 768
    for index in range(rows.shape[0] // tile):
        part = pl.ds(index * tile, tile)
        entry = lax.broadcasted_iota(jnp.int32, (high, tile), 0) + base
        place = jnp.where(entry == ids[:, part], 1.0, 0.0).astype(bf16)
        product = nn(place, rows[part, :])
        total[...] = product if index == 0 else total[...] + product
    grad_embed[...] = total[pl.ds(0, grad_embed.shape[0]), :]
    for low, exact in zip(lows, exacts):
        whole = exact.shape[0] // 16
        left = exact.shape[0] % 16

        @pl.loop(0, whole)
        def _(block):
            part = pl.ds(pl.multiple_of(block * 16, 16), 16)
            exact[part, :] = low[part, :].astype(f32)

        if left:
            value = low[pl.ds(whole * 16, 16), :].astype(f32)
            exact[pl.ds(whole * 16, left), :] = value[:left]


def finish(ids, rows, lows, line, head_rows, out_rows):
    vmem = pl.BlockSpec(memory_space=pltpu.VMEM)
    shapes = [low.shape for low in lows[:-1]] + [(head_rows, lows[-1].shape[1])]
    shapes.append((out_rows, rows.shape[1]))
    return pl.pallas_call(
        partial(finish_kernel, line, head_rows),
        out_shape=[jax.ShapeDtypeStruct(shape, f32) for shape in shapes],
        in_specs=[vmem] * 7,
        out_specs=[vmem] * 6,
        scratch_shapes=[pltpu.VMEM((-(-out_rows // 16) * 16, rows.shape[1]), f32)],
        compiler_params=pltpu.CompilerParams(vmem_limit_bytes=60 * 2**20),
        cost_estimate=pl.CostEstimate(
            flops=2 * out_rows * rows.size, bytes_accessed=2**24, transcendentals=0
        ),
    )(ids, rows, *lows)


def norm_rows(values):
    centred = values - jnp.mean(values, -1, keepdims=True)
    factor = lax.rsqrt(jnp.mean(centred * centred, -1, keepdims=True) + epsilon)
    return (centred * factor, factor)


def norm_back(gradient, normed, factor):
    return factor * (
        gradient
        - jnp.mean(gradient, -1, keepdims=True)
        - normed * jnp.mean(gradient * normed, -1, keepdims=True)
    )


def time_features(noise_level):
    half_width = TFEAT // 2
    rates = jnp.exp(jnp.arange(half_width, dtype=f32) * (math.log(1000.0) / half_width))
    angles = (jnp.log(noise_level) / 4.0)[:, None] * rates[None, :]
    return jnp.concatenate([jnp.cos(angles), jnp.sin(angles)], -1)


def levels_of(bins, table):
    hits = bins[:, None] == jnp.arange(table.shape[0])[None, :]
    return jnp.sum(jnp.where(hits, table[None, :], 0.0), -1)


def over_dp(part):
    part = part.reshape((part.shape[0] // 4, 2, 2) + part.shape[1:])
    part = lax.psum_scatter(part, "core", scatter_dimension=2)
    part = lax.psum_scatter(part, "pair", scatter_dimension=1)
    return lax.psum_scatter(part, "line", scatter_dimension=0)


def by_owner(part):
    line = lax.axis_size("line")
    return part.astype(bf16).reshape((line, 2, 2, part.shape[0] // (line * 4)) + part.shape[1:])


def mm(spec, left, right):
    return jnp.einsum(spec, left, right, preferred_element_type=f32)


def layer_forward(stream, scale_attn, scale_mlp, weights):
    w_qkv, w_out, w_up, b_hidden, w_down = weights
    seq_count, length, model_width = stream.shape
    normed_attn, factor_attn = norm_rows(stream)
    attn_entry = (normed_attn * scale_attn).astype(bf16)
    joined = mm("nsd,de->nse", attn_entry, w_qkv).astype(bf16)
    qkv_parts = joined.reshape(seq_count, length, 3, HEADS, HEAD_DIM)
    query_rows = qkv_parts[:, :, 0]
    key_rows = qkv_parts[:, :, 1]
    value_rows = qkv_parts[:, :, 2]
    scores = mm("nqhe,nkhe->nhqk", query_rows, key_rows) / math.sqrt(HEAD_DIM)
    exp_scores = jnp.exp(scores - jnp.max(scores, -1, keepdims=True))
    attn_probs = exp_scores / jnp.sum(exp_scores, -1, keepdims=True)
    probs_low = attn_probs.astype(bf16)
    attn_mixed = mm("nhqk,nkhe->nqhe", probs_low, value_rows).astype(bf16)
    attn_mixed = attn_mixed.reshape(seq_count, length, model_width)
    middle = stream + mm("nsd,de->nse", attn_mixed, w_out)
    normed_mlp, factor_mlp = norm_rows(middle)
    mlp_entry = (normed_mlp * scale_mlp).astype(bf16)
    up_proj = mm("nsd,df->nsf", mlp_entry, w_up) + b_hidden
    below = 0.5 + 0.5 * lax.erf(up_proj * math.sqrt(0.5))
    hidden = (up_proj * below).astype(bf16)
    density = jnp.exp(-0.5 * up_proj * up_proj) * (1.0 / math.sqrt(2.0 * math.pi))
    slope = (below + up_proj * density).astype(bf16)
    block_out = middle + mm("nsf,fd->nsd", hidden, w_down)
    kept = (
        normed_attn,
        factor_attn,
        attn_entry,
        query_rows,
        key_rows,
        value_rows,
        attn_probs,
        probs_low,
        attn_mixed,
        normed_mlp,
        factor_mlp,
        mlp_entry,
        slope,
        hidden,
    )
    return (block_out, kept)


def layer_backward(grad_out, kept, scale_attn, scale_mlp, weights, whole):
    w_qkv, w_out, w_up, b_hidden, w_down = weights
    (
        normed_attn,
        factor_attn,
        attn_entry,
        query_rows,
        key_rows,
        value_rows,
        attn_probs,
        probs_low,
        attn_mixed,
        normed_mlp,
        factor_mlp,
        mlp_entry,
        slope,
        hidden,
    ) = kept
    seq_count, length, model_width = grad_out.shape
    grads = {}
    grad_branch = grad_out.astype(bf16)
    if whole:
        grads["down"] = by_owner(mm("nsf,nsd->fd", hidden, grad_branch))
    grad_hidden = mm("nsd,fd->nsf", grad_branch, w_down)
    grad_up_proj = (grad_hidden * slope.astype(f32)).astype(bf16)
    if whole:
        grads["bias"] = jnp.sum(grad_up_proj.astype(f32), (0, 1))
        grads["up"] = by_owner(mm("nsd,nsf->df", mlp_entry, grad_up_proj))
    grad_entry = mm("nsf,df->nsd", grad_up_proj, w_up)
    grad_middle = grad_out + norm_back(grad_entry * scale_mlp, normed_mlp, factor_mlp)
    grad_attn = grad_middle.astype(bf16)
    if whole:
        grads["out"] = by_owner(mm("nsd,nse->de", attn_mixed, grad_attn))
    grad_mixed = mm("nse,de->nsd", grad_attn, w_out)
    grad_mixed = grad_mixed.astype(bf16).reshape(seq_count, length, HEADS, HEAD_DIM)
    grad_probs = mm("nqhe,nkhe->nhqk", grad_mixed, value_rows)
    grad_values = mm("nhqk,nqhe->nkhe", probs_low, grad_mixed)
    grad_scores = (
        attn_probs * (grad_probs - jnp.sum(grad_probs * attn_probs, -1, keepdims=True))
    ).astype(bf16)
    grad_query = mm("nhqk,nkhe->nqhe", grad_scores, key_rows) / math.sqrt(HEAD_DIM)
    grad_keys = mm("nhqk,nqhe->nkhe", grad_scores, query_rows) / math.sqrt(HEAD_DIM)
    grad_joined = jnp.stack([grad_query, grad_keys, grad_values], 2).astype(bf16)
    grad_joined = grad_joined.reshape(seq_count, length, 3 * model_width)
    if whole:
        grads["qkv"] = by_owner(mm("nsd,nse->de", attn_entry, grad_joined))
    grad_attn_entry = mm("nse,de->nsd", grad_joined, w_qkv)
    grad_stream = grad_middle + norm_back(grad_attn_entry * scale_attn, normed_attn, factor_attn)
    if whole:
        grads["cond"] = jnp.concatenate(
            [jnp.sum(grad_attn_entry * normed_attn, 1), jnp.sum(grad_entry * normed_mlp, 1)], -1
        )
    return (grad_stream, grads)


def local(
    token_ids,
    target_ids,
    time_bins,
    sigma_table,
    noise,
    embed,
    w_in,
    w_time,
    norm_gain,
    w_qkv,
    w_out,
    w_up,
    b_hidden,
    w_down,
    out_gain,
    head,
):
    section = lax.axis_index("section")
    line_at = lax.axis_index("line")
    pair_at = lax.axis_index("pair")
    core = lax.axis_index("core")
    sections = lax.axis_size("section")
    line = lax.axis_size("line")
    chip = line_at * 2 + pair_at
    chips = line * 2
    cores = 2
    dp_count = chips * cores
    dp_index = chip * cores + core
    is_first = section == 0
    seqs, length = token_ids.shape
    tokens = seqs * length
    half = tokens // sections
    model_width = w_out.shape[-1]
    emb_rows, emb_width = embed.shape
    head_rows = head.shape[0]
    straight = line <= 4 and half % 16 == 0 and model_width // dp_count % 16 == 0

    if straight:
        lanes = -(-half // 128) * 128
        blocks = [part.reshape(2, half) for part in (token_ids, target_ids)]
        blocks.append(jnp.pad(time_bins[None, :], ((0, 0), (0, half - seqs))))
        own_ids = jnp.pad(jnp.concatenate(blocks, 0), ((0, 3), (0, lanes - half)))
        head_own = jnp.pad(head, ((0, -head_rows % 512), (0, 0)))
        all_ids, embedded, head_early, head_core = start_pass(
            own_ids, embed, head_own, half, line, 0
        )
        all_ids = all_ids.reshape(dp_count, 8, lanes)
        all_tokens = all_ids[:, 0:2, :half].reshape(dp_count, tokens)
        all_targets = all_ids[:, 2:4, :half].reshape(dp_count, tokens)
        all_bins = all_ids[:, 4, :seqs].reshape(-1)
        embedded = embedded.swapaxes(1, 2)
    else:
        own_ids = jnp.concatenate([token_ids.reshape(-1), target_ids.reshape(-1), time_bins])
        all_ids = lax.all_gather(own_ids, DP)
        all_tokens = all_ids[:, :tokens]
        all_targets = all_ids[:, tokens : 2 * tokens]
        all_bins = all_ids[:, 2 * tokens :].reshape(-1)
        own_rows = dp_index * emb_rows + jnp.arange(emb_rows)
        half_tokens = lax.dynamic_slice_in_dim(all_tokens, section * half, half, 1)
        picked = (half_tokens.reshape(-1)[:, None] == own_rows[None, :]).astype(bf16)
        found = jnp.dot(picked, embed, preferred_element_type=f32).astype(bf16)
        embedded = lax.all_gather(over_dp(found.reshape(dp_count, half, emb_width)), "section")
    embedded = embedded.astype(f32).reshape(seqs, length, emb_width)

    swapped = [(0, 1), (1, 0)]
    if not straight:
        head_group = lax.all_gather(lax.all_gather(head, "core"), "section")
        head_group = head_group.reshape(-1, model_width)
        vocab_base = (
            (jnp.arange(sections)[:, None] * chips + chip) * cores + jnp.arange(cores)[None, :]
        ) * head_rows
        columns = (vocab_base[:, :, None] + jnp.arange(head_rows)[None, None, :]).reshape(-1)

    noise_level = levels_of(time_bins, sigma_table)
    unit_factor = lax.rsqrt(jnp.mean(embedded * embedded, -1, keepdims=True) + epsilon)
    level_col = noise_level[:, None, None]
    noise_scale = lax.rsqrt(level_col * level_col + 1.0)
    noisy_rows = ((embedded * unit_factor + level_col * noise) * noise_scale).astype(bf16)
    time_feats = time_features(noise_level)
    conditioned = jnp.dot(time_feats, w_time[0].astype(f32), precision=highest) + norm_gain[0]
    scale_attn = conditioned[:, None, :model_width]
    scale_mlp = conditioned[:, None, model_width:]
    scale = conditioned[:, None, :]
    weights = (w_qkv[0], w_out[0], w_up[0], b_hidden[0], w_down[0])
    stacked = (w_qkv, w_out, w_up, b_hidden, w_down)
    stream0 = mm("nse,ed->nsd", noisy_rows, w_in)
    flat = (tokens, model_width)
    if straight:
        block_out, final_rows, *kept, head_late, head_fourth = forward_pass(
            stream0.reshape(flat), scale, stacked, out_gain[None, :], head_own, head_early, 1
        )
        heads = [head_own, head_core, head_early, head_late, head_fourth]
    else:
        first_out = layer_forward(stream0, scale_attn, scale_mlp, weights)[0].astype(bf16)
        arrived = lax.ppermute(first_out, "section", swapped)
        stream = jnp.where(is_first, stream0, arrived.astype(f32))
        block_out, kept = layer_forward(stream, scale_attn, scale_mlp, weights)
        final_normed, final_factor = norm_rows(block_out.astype(bf16).astype(f32))
        final_rows = (final_normed * out_gain).astype(bf16).reshape(flat)

    targets_group = lax.dynamic_slice_in_dim(
        all_targets.reshape(chips, cores, tokens), core, 1, 1
    )[:, 0]
    targets_group = lax.dynamic_slice_in_dim(targets_group, section * half, half, 1)
    if straight:
        grad_final, grad_head, lse, picks = head_pass(
            final_rows, targets_group.reshape(line, 1, tokens), heads, line, head_rows, length, 3
        )
        ce_part = jnp.sum(lse) / chips - jnp.sum(picks)
    else:
        targets_group = targets_group.reshape(-1)
        handed = lax.ppermute(final_rows[:half], "section", [(1, 0), (0, 1)])
        own_final = jnp.where(is_first, handed, final_rows[half:])
        group_final = lax.all_gather(own_final, ("line", "pair"), tiled=True)
        logits = mm("td,vd->tv", group_final, head_group)
        local_top = jnp.max(logits, -1)
        local_total = jnp.sum(jnp.exp(logits - local_top[:, None]), -1)
        mark = columns[None, :] == targets_group[:, None]
        local_pick = jnp.sum(jnp.where(mark, logits, 0.0))
        stats = lax.all_gather(jnp.stack([local_top, local_total]), ("line", "pair"))
        all_top = jnp.max(stats[:, 0], 0)
        all_total = jnp.sum(stats[:, 1] * jnp.exp(stats[:, 0] - all_top), 0)
        log_total = all_top + jnp.log(all_total)
        soft_rows = jnp.exp(logits - log_total[:, None])
        logit_grads = ((soft_rows - jnp.where(mark, 1.0, 0.0)) / length).astype(bf16)
        grad_final = jnp.dot(logit_grads, head_group, preferred_element_type=f32).astype(bf16)
        grad_final = lax.psum_scatter(grad_final, ("line", "pair"), scatter_dimension=0, tiled=True)
        handed = lax.ppermute(grad_final, "section", swapped)
        grad_final = jnp.concatenate([handed, grad_final], 0)
        grad_head = mm("tv,td->vd", logit_grads, group_final).astype(bf16)
        grad_head = grad_head.reshape(sections, cores, head_rows, model_width)
        grad_head = lax.psum_scatter(grad_head, "core", scatter_dimension=1)
        grad_head = lax.psum_scatter(grad_head, "section", scatter_dimension=0).astype(f32)

        ce_part = jnp.sum(log_total) / chips - local_pick
    if straight:
        grad_second, grad_top, out_part = backward_pass(
            grad_final, block_out, out_gain[None, :], scale, kept, stacked
        )
        returned = lax.ppermute(grad_second, "section", swapped)
        out_part = out_part.reshape(-1)
        x, joined, mixed, middle, entry_attn, entry_mlp, slope, hidden = kept
        grad_middle, grad_entry, grad_bias, down_part, up_part = backward_begin(
            returned, grad_top, seqs, hidden, entry_mlp, slope, w_up, w_down
        )
        parts = [by_owner(down_part), by_owner(up_part)]
        grad_bias = grad_bias.reshape(-1)
    else:
        grad_final = grad_final.astype(f32).reshape(stream0.shape)
        out_part = jnp.sum(grad_final * final_normed, (0, 1))
        grad_top = norm_back(grad_final * out_gain, final_normed, final_factor)
        grad_second = layer_backward(grad_top, kept, scale_attn, scale_mlp, weights, False)[0]
        returned = lax.ppermute(grad_second.astype(bf16), "section", swapped)
        grad_cot = jnp.where(is_first, returned.astype(f32), grad_top)
        grad_stream, grads = layer_backward(grad_cot, kept, scale_attn, scale_mlp, weights, True)
        grad_first = grad_stream.astype(bf16)
    out_part = jnp.where(is_first, 0.0, out_part)

    ce_high = ce_part.astype(bf16).astype(f32)
    ce_mid = (ce_part - ce_high).astype(bf16).astype(f32)
    ce_low = ce_part - ce_high - ce_mid
    shared = jnp.concatenate([out_part, jnp.stack([ce_high, ce_mid, ce_low])])
    shared_rows = -(-shared.shape[0] // emb_width)
    shared = jnp.pad(shared, (0, shared_rows * emb_width - shared.shape[0]))
    shared = shared.reshape(-1, emb_width).astype(bf16)
    both = [shared, lax.ppermute(shared, "section", swapped)]

    cubed = unit_factor * unit_factor * unit_factor
    cond_rows = seqs * 2 * model_width // emb_width
    bias_rows = b_hidden.shape[1] // emb_width
    if straight:
        rest = jnp.concatenate([grad_bias.reshape(-1, emb_width)] + both, 0).astype(f32)
        rest = jnp.pad(rest, ((0, -(cond_rows + rest.shape[0]) % 16), (0, 0)))
        factors = [
            (value * noise_scale).reshape(tokens, 1) for value in (unit_factor, cubed)
        ]
        owned = noisy_rows.reshape(tokens, sections, dp_count, -1)
        owned = owned.swapaxes(1, 2).reshape(tokens, emb_width)
        far = [grad_middle, grad_entry, middle, x, joined, mixed, entry_attn, w_out, w_qkv]
        grad_down, grad_up, grad_qkv, grad_wout, grad_w_in, grad_head, smalls, rows_all = tail_pass(
            scale,
            rest,
            factors,
            embedded.reshape(tokens, emb_width),
            owned,
            w_in,
            far,
            parts,
            grad_head,
            2,
        )
        ids = all_tokens.reshape(1, -1)
        grad_down, grad_up, grad_qkv, grad_wout, grad_head, grad_embed = finish(
            ids,
            rows_all.reshape(-1, emb_width),
            [grad_down, grad_up, grad_qkv, grad_wout, grad_head],
            line,
            head_rows,
            emb_rows // sections,
        )
    else:
        in_part = mm("nse,nsd->ed", noisy_rows, grad_first).astype(bf16)
        in_part = in_part.reshape(sections, dp_count, -1, model_width).swapaxes(0, 1)
        in_sum = over_dp(in_part).astype(f32)
        in_handed = lax.ppermute(in_sum[1], "section", swapped)
        grad_w_in = jnp.where(is_first, in_sum[0], in_handed)
        grad_noisy = mm("nsd,ed->nse", grad_first, w_in)
        grad_unit = grad_noisy * noise_scale
        grad_embedded = unit_factor * grad_unit - cubed * embedded * jnp.mean(
            grad_unit * embedded, -1, keepdims=True
        )
        grad_flat = grad_embedded.reshape(tokens, emb_width).astype(bf16)
        handed = lax.ppermute(grad_flat, "section", swapped)
        rows_all = lax.all_gather(jnp.where(is_first, grad_flat, handed), DP)
        small = [grads["cond"].reshape(-1, emb_width), grads["bias"].reshape(-1, emb_width)]
        smalls = lax.all_gather(
            jnp.concatenate([value.astype(bf16) for value in small] + both, 0), DP
        )
        grad_down, grad_up, grad_qkv, grad_wout = [
            over_dp(part.reshape((dp_count,) + part.shape[3:])).astype(f32)
            for part in (grads["down"], grads["up"], grads["qkv"], grads["out"])
        ]
        grad_all = rows_all.reshape(-1, emb_width)
        out_rows = emb_rows // sections
        target_rows = (section * dp_count + dp_index) * out_rows + jnp.arange(out_rows)
        place = (target_rows[:, None] == all_tokens.reshape(-1)[None, :]).astype(bf16)
        grad_embed = jnp.dot(place, grad_all, preferred_element_type=f32)

    smalls = smalls.reshape(dp_count, -1, emb_width).astype(f32)
    cond_all = smalls[:, :cond_rows].reshape(dp_count * seqs, 2 * model_width)
    bias_all = smalls[:, cond_rows : cond_rows + bias_rows].reshape(dp_count, -1)
    hidden_rows = bias_all.shape[1] // dp_count
    grad_bias = jnp.sum(
        lax.dynamic_slice_in_dim(bias_all, dp_index * hidden_rows, hidden_rows, 1), 0
    )
    norm_cols = 2 * model_width // dp_count
    grad_gain = jnp.sum(lax.dynamic_slice_in_dim(cond_all, dp_index * norm_cols, norm_cols, 1), 0)
    feats_all = time_features(levels_of(all_bins, sigma_table))
    feat_rows = TFEAT // dp_count
    feats_own = lax.dynamic_slice_in_dim(feats_all, dp_index * feat_rows, feat_rows, 1)
    grad_time = jnp.dot(feats_own.T, cond_all, precision=highest)
    shared_first = cond_rows + bias_rows
    both = smalls[:, shared_first : shared_first + 2 * shared_rows]
    both = jnp.sum(both.reshape(dp_count, 2, -1), (0, 1))
    loss = jnp.sum(both[model_width : model_width + 3]) / (tokens * dp_count)
    gain_rows = model_width // dp_count
    grad_out_gain = lax.dynamic_slice_in_dim(both, dp_index * gain_rows, gain_rows)
    return (
        loss,
        grad_embed,
        grad_w_in,
        grad_time[None],
        grad_gain[None],
        grad_qkv[None],
        grad_wout[None],
        grad_up[None],
        grad_bias[None],
        grad_down[None],
        grad_out_gain,
        grad_head,
    )


def solution(mesh):
    sections, dp_count = mesh.shape["section"], mesh.shape["dp"]
    fine = Mesh(mesh.devices.reshape(sections, dp_count // 4, 2, 2), ("section",) + DP)
    everywhere = ("section",) + DP
    in_specs = (
        P(DP, None),
        P(DP, None),
        P(DP),
        P(),
        P(DP, None, None),
        P(DP, None),
        P(),
        P("section", None, None),
        P("section", None),
        P("section", None, None),
        P("section", None, None),
        P("section", None, None),
        P("section", None),
        P("section", None, None),
        P(),
        P(everywhere, None),
    )
    out_specs = (
        P(),
        P(everywhere, None),
        P(everywhere, None),
        P("section", DP, None),
        P("section", DP),
        P("section", DP, None),
        P("section", DP, None),
        P("section", DP, None),
        P("section", DP),
        P("section", DP, None),
        P(DP),
        P(everywhere, None),
    )
    return jax.shard_map(local, mesh=fine, in_specs=in_specs, out_specs=out_specs, check_vma=False)
```

```python
from functools import partial
import math

import jax
import jax.numpy as jnp
from jax import lax
from jax.experimental import pallas as pl
from jax.experimental.pallas import tpu as pltpu
from jax.sharding import Mesh, PartitionSpec as P

HEADS = 16
HEAD_DIM = 64
TFEAT = 256

epsilon = 1e-05
highest = lax.Precision.HIGHEST
f32 = jnp.float32
bf16 = jnp.bfloat16
DP = ("line", "pair", "core")


MESH = pl.DeviceIdType.MESH


def nt(left, right):
    return lax.dot_general(left, right, (((1,), (1,)), ((), ())), preferred_element_type=f32)


def tn(left, right):
    return lax.dot_general(left, right, (((0,), (0,)), ((), ())), preferred_element_type=f32)


def nn(left, right):
    return jnp.dot(left, right, preferred_element_type=f32)


def greet(peers):
    barrier = pltpu.get_barrier_semaphore()
    for peer in peers:
        pl.semaphore_signal(barrier, inc=1, device_id=peer, device_id_type=MESH)
    pl.semaphore_wait(barrier, len(peers))


def remote(source, target, send, recv, peer):
    return pltpu.make_async_remote_copy(
        src_ref=source,
        dst_ref=target,
        send_sem=send,
        recv_sem=recv,
        device_id=peer,
        device_id_type=MESH,
    )


def ring_place(position, line):
    turned = position // line
    return position * (1 - turned) + (2 * line - 1 - position) * turned, turned


def start_kernel(line, *refs):
    ids, embed, head, all_ids, out, head_early, head_core = refs[:7]
    table, found, own, from_core, from_pair, from_line = refs[7:13]
    ids_send, ids_recv, own_sem, core_send, core_recv, pair_send, pair_recv = refs[13:20]
    line_send, line_recv, swap_send, swap_recv, head_send, head_recv = refs[20:]
    me_section = lax.axis_index("section")
    me_line = lax.axis_index("line")
    me_pair = lax.axis_index("pair")
    me_core = lax.axis_index("core")
    section_peer = {"section": 1 - me_section}
    core_peer = {"core": 1 - me_core}
    pair_peer = {"pair": 1 - me_pair}
    peers = []
    for step in range(1, line * 4):
        peers.append(
            {
                "line": lax.rem(me_line + step // 4, line),
                "pair": lax.rem(me_pair + step // 2 % 2, 2),
                "core": lax.rem(me_core + step % 2, 2),
            }
        )
    greet(peers + [section_peer])
    each = head_early.shape[0]
    to_section = remote(
        head.at[pl.ds(0, each)], head_early, head_send.at[0], head_recv.at[0], section_peer
    )
    to_section.start()
    to_other_core = remote(head, head_core, head_send.at[1], head_recv.at[1], core_peer)
    place = all_ids.at[me_line, me_pair, me_core]
    copies = [remote(ids, place, ids_send.at[n], ids_recv.at[n], peer) for n, peer in enumerate(peers)]
    for copy in copies:
        copy.start()
    keep = pltpu.make_async_copy(ids, place, own_sem)
    keep.start()
    rows = embed.shape[0]
    high = table.shape[1]
    half = out.shape[-1]
    padded = jnp.concatenate(
        [embed[...].astype(f32), jnp.zeros((high - rows, embed.shape[1]), f32)], 0
    )
    table[...] = padded.T.astype(bf16)
    keep.wait()
    for copy in copies:
        copy.wait_recv()
    base = ((me_line * 2 + me_pair) * 2 + me_core) * rows

    def pick(spot, pair, core):
        wanted = all_ids[spot, pair, core, pl.ds(me_section, 1), :][:, :half]
        entry = lax.broadcasted_iota(jnp.int32, (high, half), 0)
        entry = jnp.where(entry < rows, entry + base, -1)
        hot = jnp.where(entry == wanted, 1.0, 0.0).astype(bf16)
        return nn(table[...], hot).astype(bf16)

    def core_copy(spot, pair, turn):
        return remote(
            found.at[turn, spot],
            from_core.at[turn, spot],
            core_send.at[turn, spot],
            core_recv.at[turn, spot],
            core_peer,
        )

    def pair_copy(spot):
        return remote(
            from_core.at[0, spot], from_pair.at[spot], pair_send.at[spot], pair_recv.at[spot], pair_peer
        )

    def line_copy(step):
        spot = lax.rem(me_line + step, line)
        return remote(
            from_core.at[1, spot],
            from_line.at[step - 1],
            line_send.at[step - 1],
            line_recv.at[step - 1],
            {"line": spot},
        )

    order = [lax.rem(me_line + step, line) for step in list(range(1, line)) + [0]]
    for turn, pair in enumerate((1 - me_pair, me_pair)):

        @pl.loop(0, line)
        def _(step):
            spot = lax.rem(me_line + 1 + step, line)
            found[turn, spot] = pick(spot, pair, 1 - me_core)
            core_copy(spot, pair, turn).start()
            own[turn, spot] = pick(spot, pair, me_core)

        if turn == 0:
            for spot in order:
                core_copy(spot, pair, 0).wait_recv()
                from_core[0, spot] = from_core[0, spot] + own[0, spot]
                pair_copy(spot).start()
    for step in list(range(1, line)) + [0]:
        spot = lax.rem(me_line + step, line)
        core_copy(spot, me_pair, 1).wait_recv()
        pair_copy(spot).wait_recv()
        from_core[1, spot] = from_core[1, spot] + own[1, spot] + from_pair[spot]
        if step:
            line_copy(step).start()
    to_other_core.start()
    total = from_core[1, me_line]
    for step in range(1, line):
        line_copy(step).wait_recv()
        total = total + from_line[step - 1]
    out[me_section] = total
    swap = remote(out.at[me_section], out.at[me_section], swap_send, swap_recv, section_peer)
    swap.start()
    for copy in copies:
        copy.wait_send()
    for spot in range(line):
        for turn in range(2):
            core_copy(spot, me_pair, turn).wait_send()
        pair_copy(spot).wait_send()
    for step in range(1, line):
        line_copy(step).wait_send()
    swap.wait()
    to_section.wait()
    to_other_core.wait()


def start_pass(ids, embed, head, half, line, collective_id):
    rows, width = embed.shape
    high = -(-rows // 256) * 256
    vmem = pl.BlockSpec(memory_space=pltpu.VMEM)
    anywhere = pl.BlockSpec(memory_space=pltpu.HBM)
    dma = pltpu.SemaphoreType.DMA
    block = (width, half)
    return pl.pallas_call(
        partial(start_kernel, line),
        out_shape=[
            jax.ShapeDtypeStruct((line, 2, 2) + ids.shape, ids.dtype),
            jax.ShapeDtypeStruct((2,) + block, bf16),
            jax.ShapeDtypeStruct((head.shape[0] // 8 * 5, head.shape[1]), bf16),
            jax.ShapeDtypeStruct(head.shape, bf16),
        ],
        in_specs=[vmem, vmem, anywhere],
        out_specs=[vmem, vmem, anywhere, anywhere],
        scratch_shapes=[
            pltpu.VMEM((width, high), bf16),
            pltpu.VMEM((2, line) + block, bf16),
            pltpu.VMEM((2, line) + block, bf16),
            pltpu.VMEM((2, line) + block, bf16),
            pltpu.VMEM((line,) + block, bf16),
            pltpu.VMEM((line - 1,) + block, bf16),
            dma((line * 4 - 1,)),
            dma((line * 4 - 1,)),
            dma,
            dma((2, line)),
            dma((2, line)),
            dma((line,)),
            dma((line,)),
            dma((line - 1,)),
            dma((line - 1,)),
            dma,
            dma,
            dma((2,)),
            dma((2,)),
        ],
        compiler_params=pltpu.CompilerParams(
            collective_id=collective_id, has_side_effects=True, vmem_limit_bytes=60 * 2**20
        ),
        cost_estimate=pl.CostEstimate(flops=0, bytes_accessed=2**27, transcendentals=0),
    )(ids, embed, head)


def head_kernel(line, head_rows, length, *refs):
    final, targets, *heads = refs[:7]
    out, grads, lse_out, pick_out = refs[7:11]
    (table, rows_all, logits, probs, acc, parts, from_pair, from_line, stats, done) = refs[11:21]
    (head_sem, own_sem, give_send, give_recv, along_send, along_recv, pair_send, pair_recv) = refs[21:29]
    (stat_send, stat_recv, sum_send, sum_recv, line_send, line_recv, back_send, back_recv) = refs[29:37]
    last_send, last_recv = refs[37:]
    half = final.shape[0] // 2
    width = 2 * half
    padded = heads[0].shape[0]
    me_section = lax.axis_index("section")
    me_line = lax.axis_index("line")
    me_pair = lax.axis_index("pair")
    me_core = lax.axis_index("core")
    section_peer = {"section": 1 - me_section}
    pair_peer = {"pair": 1 - me_pair}
    chip_peers = []
    for step in range(1, 2 * line):
        chip_peers.append(
            {"line": lax.rem(me_line + step // 2, line), "pair": lax.rem(me_pair + step % 2, 2)}
        )
    greet(chip_peers + [section_peer, {"core": 1 - me_core}])

    def side(pair):
        return pl.ds(pl.multiple_of(pair * half, 16), half)

    loads = []
    for n, part in enumerate(heads):
        first = sum(other.shape[0] for other in heads[:n])
        target = table.at[pl.ds(first, part.shape[0])]
        loads.append(pltpu.make_async_copy(part, target, head_sem.at[n]))
    late = heads[3]
    last = remote(
        late,
        table.at[pl.ds(4 * padded - late.shape[0], late.shape[0])],
        last_send,
        last_recv,
        {"core": 1 - me_core},
    )
    last.start()
    for load in loads:
        load.start()

    quarter = half // 2

    def token_rows(place, pair, chunk):
        first = place * width + pair * half + chunk * quarter
        return pl.ds(pl.multiple_of(first, 16), quarter)

    def group(place):
        return pl.ds(pl.multiple_of(place * width, 128), width)

    def column_block(place, chunk):
        return rows_all.at[token_rows(place, me_pair, chunk)]

    def give(chunk):
        return remote(
            final.at[pl.ds(chunk * quarter, quarter)],
            column_block(me_line, chunk),
            give_send.at[chunk],
            give_recv.at[chunk],
            section_peer,
        )

    def along(step, way, chunk):
        block = column_block(me_line - way * step, chunk)
        turn = (way + 1) // 2
        return remote(
            block,
            block,
            along_send.at[turn, step, chunk],
            along_recv.at[turn, step, chunk],
            {"line": me_line + way},
        )

    def inside(place):
        return (place >= 0) & (place < line)

    def sends_along(step, way):
        return inside(me_line - way * step) & inside(me_line + way)

    def sideways(place, chunk):
        block = column_block(place, chunk)
        return remote(
            block, block, pair_send.at[place, chunk], pair_recv.at[place, chunk], pair_peer
        )

    def arrived_sideways(place, chunk):
        block = rows_all.at[token_rows(place, 1 - me_pair, chunk)]
        return remote(
            block, block, pair_send.at[place, chunk], pair_recv.at[place, chunk], pair_peer
        )

    @pl.when(me_section == 1)
    def _():
        for chunk in range(2):
            give(chunk).start()
        for chunk in range(2):
            keep = pltpu.make_async_copy(
                final.at[pl.ds(half + chunk * quarter, quarter)],
                column_block(me_line, chunk),
                own_sem.at[chunk],
            )
            keep.start()
            keep.wait()

    for chunk in range(2):

        @pl.when(me_section == 0)
        def _():
            give(chunk).wait_recv()

        for way in (1, -1):

            @pl.when(sends_along(0, way))
            def _():
                along(0, way, chunk).start()

        sideways(me_line, chunk).start()

    def pass_on(step):
        for chunk in range(2):
            for way in (1, -1):
                place = me_line - way * step

                @pl.when(inside(place))
                def _():
                    block = column_block(place, chunk)
                    turn = (way + 1) // 2
                    remote(
                        block,
                        block,
                        along_send.at[turn, step - 1, chunk],
                        along_recv.at[turn, step - 1, chunk],
                        {"line": me_line - way},
                    ).wait_recv()

                    @pl.when(inside(me_line + way))
                    def _():
                        along(step, way, chunk).start()

                    sideways(place, chunk).start()

    nearest = []
    for own in range(line):
        near = [own]
        for step in range(1, line):
            near += [place for place in (own - step, own + step) if 0 <= place < line]
        nearest.append(near)

    def by_distance(turn):
        place = 0
        for own in range(line):
            for n in range(line):
                hit = ((me_line == own) & (turn == n)).astype(jnp.int32)
                place = place + hit * nearest[own][n]
        return place

    def vocabulary(tile, rows):
        shard = tile * rows // padded
        first = lax.rem(tile * rows, padded)
        shard_section = lax.rem(me_section + shard // 2, 2)
        shard_core = lax.rem(me_core + lax.rem(shard, 2), 2)
        base = (((shard_section * line + me_line) * 2 + me_pair) * 2 + shard_core) * head_rows
        row = lax.broadcasted_iota(jnp.int32, (rows, 1), 0) + first
        return jnp.where(row < head_rows, row + base, -1)

    tile_rows = 512
    tiles = 4 * padded // tile_rows
    lowest = -1e30

    def score(turn, tops):
        place = by_distance(turn) if turn < line else None
        before = by_distance(turn - 1) if turn > 0 else None
        wanted = None if place is None else targets[place]

        def one(tile, carry):
            rows = pl.ds(pl.multiple_of(tile * tile_rows, tile_rows), tile_rows)
            out = []
            if place is not None:
                top, pick = carry[:2]
                entry = vocabulary(tile, tile_rows)
                part = nt(table[rows, :], rows_all[group(place), :])
                part = jnp.where(entry >= 0, part, lowest)
                logits[turn % 2, rows, :] = part
                out.append(jnp.maximum(top, jnp.max(part, 0, keepdims=True)))
                out.append(
                    pick + jnp.sum(jnp.where(entry == wanted, part, 0.0), 0, keepdims=True)
                )
            if before is not None:
                value = jnp.exp(logits[(turn - 1) % 2, rows, :] - tops)
                probs[rows, group(before)] = value.astype(bf16)
                out.append(carry[-1] + jnp.sum(value, 0, keepdims=True))
            return tuple(out)

        none = jnp.zeros((1, width), f32)
        start = () if place is None else (jnp.full((1, width), lowest, f32), none)
        start += () if before is None else (none,)
        result = lax.fori_loop(0, tiles, one, start)
        if place is not None:
            pick_out[place] = result[1]
        if before is not None:
            own = stats.at[me_line, me_pair, before]
            own[:, 0:width] = tops
            own[:, width : 2 * width] = result[-1]
            for n in range(len(chip_peers)):
                stat_copy(n, before).start()
        return None if place is None else result[0]

    def stat_copy(n, place):
        own = stats.at[me_line, me_pair, place]
        return remote(own, own, stat_send.at[n, place], stat_recv.at[n, place], chip_peers[n])

    def stat_wait(n, place):
        peer = chip_peers[n]
        source_line = lax.rem(2 * me_line + line - peer["line"], line)
        source_pair = peer["pair"]
        block = stats.at[source_line, source_pair, place]
        remote(block, block, stat_send.at[n, place], stat_recv.at[n, place], peer).wait_recv()

    for load in loads:
        load.wait()
    last.wait()

    tops = None
    for turn in range(line + 1):
        if turn + 1 < line:
            pass_on(turn + 1)
        if turn < line:
            for chunk in range(2):
                arrived_sideways(by_distance(turn), chunk).wait_recv()
        tops = score(turn, tops)

    def part_rows(pair, chunk):
        return pl.ds(pl.multiple_of(pair * half + chunk * quarter, 16), quarter)

    def sum_copy(turn, chunk):
        place = lax.rem(me_line + turn + 1, line)
        return remote(
            parts.at[place, part_rows(1 - me_pair, chunk)],
            from_pair.at[turn, pl.ds(chunk * quarter, quarter)],
            sum_send.at[turn, chunk],
            sum_recv.at[turn, chunk],
            pair_peer,
        )

    def line_copy(turn, chunk):
        place = lax.rem(me_line + turn + 1, line)
        return remote(
            parts.at[place, part_rows(me_pair, chunk)],
            from_line.at[turn, pl.ds(chunk * quarter, quarter)],
            line_send.at[turn, chunk],
            line_recv.at[turn, chunk],
            {"line": place},
        )

    def finish(turn, chunk):
        place = lax.rem(me_line + turn + 1, line)
        sum_copy(turn, chunk).wait_recv()
        own = parts.at[place, part_rows(me_pair, chunk)]
        other = from_pair.at[turn, pl.ds(chunk * quarter, quarter)]

        @pl.loop(0, quarter // 16)
        def _(block):
            rows = pl.ds(pl.multiple_of(block * 16, 16), 16)
            own[rows, :] = (own[rows, :].astype(f32) + other[rows, :].astype(f32)).astype(bf16)

    @pl.loop(0, line)
    def _(turn):
        place = lax.rem(me_line + turn + 1, line)
        for n in range(len(chip_peers)):
            stat_wait(n, place)
        tops = [stats[a, b, place, :, 0:width] for a in range(line) for b in range(2)]
        totals = [
            stats[a, b, place, :, width : 2 * width] for a in range(line) for b in range(2)
        ]
        top = tops[0]
        for value in tops[1:]:
            top = jnp.maximum(top, value)
        total = jnp.zeros_like(top)
        for peak, part in zip(tops, totals):
            total = total + part * jnp.exp(peak - top)
        lse = top + jnp.log(total)
        lse_out[place] = lse
        factor = jnp.exp(stats[me_line, me_pair, place, :, 0:width] - lse) / length
        wanted = targets[place]

        def scaled(tile):
            rows = pl.ds(tile * padded, padded)
            entry = vocabulary(tile, padded)
            grad = probs[rows, group(place)].astype(f32) * factor
            grad = (grad - jnp.where(entry == wanted, 1.0 / length, 0.0)).astype(bf16)
            probs[rows, group(place)] = grad
            return grad

        grad = scaled(0)
        for tile in range(4):
            product = tn(grad, table[pl.ds(tile * padded, padded), :])
            if tile < 3:
                grad = scaled(tile + 1)
                acc[...] = product if tile == 0 else acc[...] + product
            else:
                parts[place] = (acc[...] + product).astype(bf16)

        for chunk in range(2):
            sum_copy(turn, chunk).start()

        @pl.when(turn > 0)
        def _():
            for chunk in range(2):
                finish(turn - 1, chunk)
                line_copy(turn - 1, chunk).start()

    gh_rows = 256
    gh_tiles = 4 * padded // gh_rows

    def head_grads(first, last):
        @pl.loop(first, last)
        def _(tile):
            rows = pl.ds(pl.multiple_of(tile * gh_rows, gh_rows), gh_rows)
            value = jnp.dot(probs[rows, :], rows_all[...], preferred_element_type=f32)
            grads[rows, :] = value.astype(bf16)

    def back(chunk):
        part = pl.ds(chunk * quarter, quarter)
        return remote(
            done.at[part], out.at[part], back_send.at[chunk], back_recv.at[chunk], section_peer
        )

    head_grads(0, gh_tiles // 2)
    for chunk in range(2):
        finish(line - 1, chunk)
        for turn in range(line - 1):
            line_copy(turn, chunk).wait_recv()
        own = parts.at[me_line, part_rows(me_pair, chunk)]

        @pl.loop(0, quarter // 16)
        def _(block):
            rows = pl.ds(pl.multiple_of(block * 16, 16), 16)
            chunk_rows = pl.ds(pl.multiple_of(chunk * quarter + block * 16, 16), 16)
            value = own[rows, :].astype(f32)
            for turn in range(line - 1):
                value = value + from_line[turn, chunk_rows, :].astype(f32)
            done[chunk_rows, :] = value.astype(bf16)

        @pl.when(me_section == 0)
        def _():
            back(chunk).start()

    @pl.when(me_section == 0)
    def _():
        out[...] = jnp.zeros_like(out)

    @pl.when(me_section == 1)
    def _():
        out[pl.ds(half, half), :] = done[...]

    head_grads(gh_tiles // 2, gh_tiles)
    for chunk in range(2):

        @pl.when(me_section == 0)
        def _():
            back(chunk).wait_send()

        @pl.when(me_section == 1)
        def _():
            back(chunk).wait_recv()
            give(chunk).wait_send()

        for way in (1, -1):
            for step in range(line - 1):

                @pl.when(sends_along(step, way))
                def _():
                    along(step, way, chunk).wait_send()

        for place in range(line):
            sideways(place, chunk).wait_send()
        for turn in range(line):
            sum_copy(turn, chunk).wait_send()
        for turn in range(line - 1):
            line_copy(turn, chunk).wait_send()
    for place in range(line):
        for n in range(len(chip_peers)):
            stat_copy(n, place).wait_send()


def head_pass(final, targets, heads, line, head_rows, length, collective_id):
    tokens, deep = final.shape
    half = tokens // 2
    padded = heads[0].shape[0]
    vmem = pl.BlockSpec(memory_space=pltpu.VMEM)
    anywhere = pl.BlockSpec(memory_space=pltpu.HBM)
    dma = pltpu.SemaphoreType.DMA
    peers = 2 * line - 1
    return pl.pallas_call(
        partial(head_kernel, line, head_rows, length),
        out_shape=[
            jax.ShapeDtypeStruct((tokens, deep), bf16),
            jax.ShapeDtypeStruct((4 * padded, deep), bf16),
            jax.ShapeDtypeStruct((line, 1, tokens), f32),
            jax.ShapeDtypeStruct((line, 1, tokens), f32),
        ],
        in_specs=[vmem, vmem] + [anywhere] * len(heads),
        out_specs=[vmem] * 4,
        scratch_shapes=[
            pltpu.VMEM((4 * padded, deep), bf16),
            pltpu.VMEM((line * tokens, deep), bf16),
            pltpu.VMEM((2, 4 * padded, tokens), f32),
            pltpu.VMEM((4 * padded, line * tokens), bf16),
            pltpu.VMEM((tokens, deep), f32),
            pltpu.VMEM((line, tokens, deep), bf16),
            pltpu.VMEM((line, half, deep), bf16),
            pltpu.VMEM((line - 1, half, deep), bf16),
            pltpu.VMEM((line, 2, line, 1, 2 * tokens), f32),
            pltpu.VMEM((half, deep), bf16),
            dma((len(heads),)),
            dma((2,)),
            dma((2,)),
            dma((2,)),
            dma((2, line, 2)),
            dma((2, line, 2)),
            dma((line, 2)),
            dma((line, 2)),
            dma((peers, line)),
            dma((peers, line)),
            dma((line, 2)),
            dma((line, 2)),
            dma((line, 2)),
            dma((line, 2)),
            dma((2,)),
            dma((2,)),
            dma,
            dma,
        ],
        compiler_params=pltpu.CompilerParams(
            collective_id=collective_id, has_side_effects=True, vmem_limit_bytes=60 * 2**20
        ),
        cost_estimate=pl.CostEstimate(
            flops=24 * line * padded * tokens * deep, bytes_accessed=2**28, transcendentals=0
        ),
    )(final, targets, *heads)


def row_stats(values):
    centred = values - jnp.mean(values, -1, keepdims=True)
    factor = lax.rsqrt(jnp.mean(centred * centred, -1, keepdims=True) + epsilon)
    return centred * factor, factor


def two_heads(block):
    first = lax.broadcasted_iota(jnp.int32, block.shape, 1) < HEAD_DIM
    zero = jnp.zeros_like(block)
    return jnp.concatenate([jnp.where(first, block, zero), jnp.where(first, zero, block)], 0)


def one_block(stacked):
    rows = stacked.shape[0] // 2
    first = lax.broadcasted_iota(jnp.int32, (rows, stacked.shape[1]), 1) < HEAD_DIM
    return jnp.where(first, stacked[:rows], stacked[rows:])


def attention_weights(queries, keys):
    scores = nt(keys, queries) * (1.0 / math.sqrt(HEAD_DIM))
    exped = jnp.exp(scores - jnp.max(scores, 0, keepdims=True))
    return exped * (1.0 / jnp.sum(exped, 0, keepdims=True))


def tile_of(index, size):
    return pl.ds(pl.multiple_of(index * size, size), size)


def forward_kernel(seqs, *refs):
    refs = list(refs)

    def take(number):
        return [refs.pop(0) for _ in range(number)]

    start, scale, bias, gain = take(4)
    weights = take(4)
    head, head_early = take(2)
    out, final, x, joined, mixed, middle, entry_attn, entry_mlp, slope, hidden = take(10)
    head_late, head_fourth = take(2)
    w_qkv, w_out, w_up, w_down, x_total, arrived, sems, relay_send, relay_recv = take(9)
    head_send, head_recv = refs
    width = start.shape[1]
    length = start.shape[0] // seqs
    me_section = lax.axis_index("section")
    section_peer = {"section": 1 - me_section}
    load_qkv, load_out, load_up, load_down = [
        pltpu.make_async_copy(source.at[0], target, sems.at[n])
        for n, (source, target) in enumerate(zip(weights, (w_qkv, w_out, w_up, w_down)))
    ]
    load_qkv.start()
    core_peer = {"core": 1 - lax.axis_index("core")}
    greet([section_peer, core_peer])
    each = head_early.shape[0]
    to_section = remote(
        head.at[pl.ds(each, head_late.shape[0])],
        head_late,
        head_send.at[0],
        head_recv.at[0],
        section_peer,
    )
    to_section.start()
    to_core = remote(head_early, head_fourth, head_send.at[1], head_recv.at[1], core_peer)
    to_core.start()

    def relay(seq):
        rows = pl.ds(seq * length, length)
        return remote(
            out.at[rows], arrived.at[rows], relay_send.at[seq], relay_recv.at[seq], section_peer
        )

    tile = 512

    def enter(seq):
        rows = pl.ds(seq * length, length)

        @pl.when(me_section == 0)
        def _():
            x[rows, :] = start[rows, :]

        @pl.when(me_section == 1)
        def _():
            relay(seq).wait_recv()
            x[rows, :] = arrived[rows, :].astype(f32)

        normed, _ = row_stats(x[rows, :])
        entry_attn[rows, :] = (normed * scale[seq, :, :width]).astype(bf16)

    def join(first, count):
        rows = pl.ds(first * length, count * length)

        @pl.loop(0, 3 * width // tile)
        def _(index):
            cols = tile_of(index, tile)
            joined[rows, cols] = nn(entry_attn[rows, :], w_qkv[:, cols]).astype(bf16)

    for seq in range(seqs - 1):
        enter(seq)
    load_qkv.wait()
    load_out.start()
    load_up.start()
    join(0, seqs - 1)
    enter(seqs - 1)
    join(seqs - 1, 1)
    load_out.wait()
    load_down.start()
    pairs = width // 128

    @pl.loop(0, pairs)
    def _(pair):
        cols = tile_of(pair, 128)
        for seq in range(seqs):
            rows = pl.ds(seq * length, length)
            queries = two_heads(joined[rows, cols])
            keys = joined[rows, tile_of(pair + pairs, 128)]
            values = joined[rows, tile_of(pair + 2 * pairs, 128)]
            probs = attention_weights(queries, keys).astype(bf16)
            mixed[rows, cols] = one_block(tn(probs, values)).astype(bf16)

    @pl.loop(0, width // tile)
    def _(index):
        cols = tile_of(index, tile)
        middle[:, cols] = x[:, cols] + nn(mixed[...], w_out[:, cols])

    for seq in range(seqs):
        rows = pl.ds(seq * length, length)
        normed, _ = row_stats(middle[rows, :])
        entry_mlp[rows, :] = (normed * scale[seq, :, width:]).astype(bf16)

    load_up.wait()
    load_down.wait()

    def gelu_of(up, rows, cols):
        below = 0.5 + 0.5 * lax.erf(up * math.sqrt(0.5))
        value = (up * below).astype(bf16)
        density = jnp.exp(-0.5 * up * up) * (1.0 / math.sqrt(2.0 * math.pi))
        slope[rows, cols] = (below + up * density).astype(bf16)
        hidden[rows, cols] = value
        return value

    def feed_forward(first, count):
        rows = pl.ds(first * length, count * length)

        def one(index, total):
            sides = [tile_of(2 * index + side, tile) for side in range(2)]
            ups = [nn(entry_mlp[rows, :], w_up[:, cols]) + bias[:, cols] for cols in sides]
            both = jnp.concatenate([gelu_of(up, rows, cols) for up, cols in zip(ups, sides)], 1)
            x_total[rows, :] += nn(both, w_down[tile_of(index, 2 * tile), :])
            return total

        x_total[rows, :] = middle[rows, :]
        lax.fori_loop(0, w_up.shape[1] // (2 * tile), one, 0)
        for seq in range(first, first + count):
            rows = pl.ds(seq * length, length)
            value = x_total[rows, :].astype(bf16)
            out[rows, :] = value

            @pl.when(me_section == 0)
            def _():
                relay(seq).start()

            normed, _ = row_stats(value.astype(f32))
            final[rows, :] = (normed * gain[...]).astype(bf16)

    feed_forward(0, seqs)

    to_section.wait()
    to_core.wait()

    @pl.when(me_section == 0)
    def _():
        for seq in range(seqs):
            relay(seq).wait_send()


def layer_scratch(width, hidden):
    return [
        pltpu.VMEM((width, 3 * width), bf16),
        pltpu.VMEM((width, width), bf16),
        pltpu.VMEM((width, hidden), bf16),
        pltpu.VMEM((hidden, width), bf16),
    ]


def forward_pass(start, scale, weights, gain, head, head_early, collective_id):
    w_qkv, w_out, w_up, b_hidden, w_down = weights
    tokens, width = start.shape
    wide = w_up.shape[-1]
    seqs = scale.shape[0]
    vmem = pl.BlockSpec(memory_space=pltpu.VMEM)
    anywhere = pl.BlockSpec(memory_space=pl.ANY)

    far = pl.BlockSpec(memory_space=pltpu.HBM)

    def low(columns):
        return (tokens, columns), bf16

    exact = ((tokens, width), f32)
    results = [low(width), low(width), exact, low(3 * width), low(width), exact, low(width)]
    results += [low(width), low(wide), low(wide)]
    results += [((head.shape[0] - head_early.shape[0], width), bf16), (head_early.shape, bf16)]
    scratch = layer_scratch(width, wide) + [pltpu.VMEM(*exact), pltpu.VMEM(*low(width))]
    dma = pltpu.SemaphoreType.DMA
    flops = 4 * tokens * (4 * width * width + 2 * width * wide)
    return pl.pallas_call(
        partial(forward_kernel, seqs),
        out_shape=[jax.ShapeDtypeStruct(*item) for item in results],
        in_specs=[vmem] * 4 + [anywhere] * 4 + [far] * 2,
        out_specs=[vmem] * (len(results) - 2) + [far] * 2,
        scratch_shapes=scratch + [dma((4,)), dma((seqs,)), dma((seqs,)), dma((2,)), dma((2,))],
        compiler_params=pltpu.CompilerParams(
            collective_id=collective_id, has_side_effects=True, vmem_limit_bytes=60 * 2**20
        ),
        cost_estimate=pl.CostEstimate(flops=2 * flops, bytes_accessed=2**25, transcendentals=0),
    )(start, scale, b_hidden, gain, w_qkv, w_out, w_up, w_down, head, head_early)


def norm_grads(source, total, grad_middle, scale, grad_cond, half, seq, store):
    width = total.shape[1]
    length = total.shape[0] // scale.shape[0]
    rows = pl.ds(seq * length, length)
    cols = pl.ds(half * width, width)
    normed, factor = row_stats(source[rows, :])
    gradient = total[rows, :]
    if grad_cond is not None:
        grad_cond[seq, :, cols] = jnp.sum(gradient * normed, 0, keepdims=True)
    scaled = gradient * scale[seq, :, cols]
    back = factor * (
        scaled
        - jnp.mean(scaled, -1, keepdims=True)
        - normed * jnp.mean(scaled * normed, -1, keepdims=True)
    )
    store(rows, grad_middle[rows, :] + back)


def attention_grads(joined, grad_mixed, grad_joined, pair, seqs):
    pairs = grad_mixed.shape[1] // 128
    length = grad_mixed.shape[0] // seqs
    shrink = 1.0 / math.sqrt(HEAD_DIM)
    cols = tile_of(pair, 128)
    key_cols = tile_of(pair + pairs, 128)
    value_cols = tile_of(pair + 2 * pairs, 128)
    for seq in range(seqs):
        rows = pl.ds(seq * length, length)
        queries = two_heads(joined[rows, cols])
        keys = joined[rows, key_cols]
        probs = attention_weights(queries, keys)
        grads = two_heads(grad_mixed[rows, cols])
        grad_probs = nt(joined[rows, value_cols], grads)
        inner = jnp.sum(grad_probs * probs, 0, keepdims=True)
        grad_scores = (probs * (grad_probs - inner)).astype(bf16)
        grad_joined[rows, cols] = (one_block(tn(grad_scores, keys)) * shrink).astype(bf16)
        grad_joined[rows, key_cols] = (nn(grad_scores, queries) * shrink).astype(bf16)
        grad_joined[rows, value_cols] = nn(probs.astype(bf16), grads).astype(bf16)


def backward_kernel(begin, seqs, *refs):
    refs = list(refs)

    def take(number):
        return [refs.pop(0) for _ in range(number)]

    if begin:
        incoming, other, hidden, entry = take(4)
        far = take(3)
        grad_middle, total, grad_bias, down_out, up_out = take(5)
        grad_low, grad_up, entry_turned, down_weight, up_weight, out_sem = take(6)
        near = take(3)
    else:
        scale, incoming, other, gain = take(4)
        far = take(8)
        out, grad_top, grad_gain = take(3)
        grad_low, grad_up, grad_attn, grad_joined = take(4)
        near = take(8)
        total, grad_middle, grad_mixed = take(3)
    (sems,) = refs
    if begin:
        slope, w_up, w_down = near
        load_slope = pltpu.make_async_copy(far[0], slope, sems.at[0])
        load_up = pltpu.make_async_copy(far[1].at[0], w_up, sems.at[1])
        load_down = pltpu.make_async_copy(far[2].at[0], w_down, sems.at[2])
    else:
        slope, w_up, w_down, x, middle, joined, w_qkv, w_out = near
        load_slope = pltpu.make_async_copy(far[0], slope, sems.at[0])
        load_up = pltpu.make_async_copy(far[1].at[0], w_up, sems.at[1])
        load_down = pltpu.make_async_copy(far[2].at[0], w_down, sems.at[2])
        load_x = pltpu.make_async_copy(far[3], x, sems.at[3])
        load_middle = pltpu.make_async_copy(far[4], middle, sems.at[4])
        load_joined = pltpu.make_async_copy(far[5], joined, sems.at[5])
        load_qkv = pltpu.make_async_copy(far[6].at[0], w_qkv, sems.at[6])
        load_out = pltpu.make_async_copy(far[7].at[0], w_out, sems.at[7])
    width = incoming.shape[1]
    length = incoming.shape[0] // seqs
    load_down.start()
    load_slope.start()
    if begin:
        entry_turned[...] = entry[...].T

    for seq in range(seqs):
        rows = pl.ds(seq * length, length)
        if begin:
            first = (lax.axis_index("section") == 0).astype(f32)
            value = incoming[rows, :].astype(f32) * first + other[rows, :] * (1.0 - first)
        else:
            normed, factor = row_stats(other[rows, :].astype(f32))
            gradient = incoming[rows, :].astype(f32)
            part = jnp.sum(gradient * normed, 0, keepdims=True)
            grad_gain[...] = part if seq == 0 else grad_gain[...] + part
            scaled = gradient * gain[...]
            value = factor * (
                scaled
                - jnp.mean(scaled, -1, keepdims=True)
                - normed * jnp.mean(scaled * normed, -1, keepdims=True)
            )
            grad_top[rows, :] = value
        grad_middle[rows, :] = value
        grad_low[rows, :] = value.astype(bf16)

    load_down.wait()
    load_slope.wait()
    load_up.start()
    if not begin:
        load_middle.start()
        load_out.start()
        load_joined.start()
    tile = 1024

    @pl.loop(0, w_up.shape[1] // tile)
    def _(index):
        cols = tile_of(index, tile)
        grad_hidden = nt(grad_low[...], w_down[cols, :])
        value = (grad_hidden * slope[:, cols].astype(f32)).astype(bf16)
        grad_up[:, cols] = value
        if begin:
            grad_bias[:, cols] = jnp.sum(value.astype(f32), 0, keepdims=True)
            down_weight[cols, :] = tn(hidden[:, cols], grad_low[...]).astype(bf16)
            pltpu.make_async_copy(
                down_weight.at[cols], down_out.at[cols], out_sem.at[0, index]
            ).start()
            up_weight[:, cols] = nn(entry_turned[...], value).astype(bf16)

    if begin:
        whole_up = pltpu.make_async_copy(up_weight, up_out, out_sem.at[1, 0])
        whole_up.start()
    load_up.wait()
    if not begin:
        load_middle.wait()
        load_out.wait()
        load_joined.wait()
        load_qkv.start()
        load_x.start()

    @pl.loop(0, width // 256)
    def _(index):
        total[:, tile_of(index, 256)] = nt(grad_up[...], w_up[tile_of(index, 256), :])

    if begin:
        for index in range(w_up.shape[1] // tile):
            cols = pl.ds(index * tile, tile)
            pltpu.make_async_copy(
                down_weight.at[cols], down_out.at[cols], out_sem.at[0, index]
            ).wait()
        whole_up.wait()
        return

    def store_middle(rows, value):
        grad_middle[rows, :] = value
        grad_attn[rows, :] = value.astype(bf16)

    for seq in range(seqs):
        norm_grads(middle, total, grad_middle, scale, None, 1, seq, store_middle)

    @pl.loop(0, width // 512)
    def _(index):
        part = tile_of(index, 512)
        grad_mixed[:, part] = nt(grad_attn[...], w_out[part, :]).astype(bf16)

    @pl.loop(0, width // 128)
    def _(pair):
        attention_grads(joined, grad_mixed, grad_joined, pair, seqs)

    load_qkv.wait()
    load_x.wait()

    @pl.loop(0, width // 256)
    def _(index):
        total[:, tile_of(index, 256)] = nt(grad_joined[...], w_qkv[tile_of(index, 256), :])

    def store_out(rows, value):
        out[rows, :] = value.astype(bf16)

    for seq in range(seqs):
        norm_grads(x, total, grad_middle, scale, None, 0, seq, store_out)


def backward_pass(grad_final, block_out, gain, scale, kept, weights):
    w_qkv, w_out, w_up, _, w_down = weights
    x, joined, _, middle, _, _, slope, _ = kept
    tokens, width = x.shape
    wide = w_up.shape[-1]
    vmem = pl.BlockSpec(memory_space=pltpu.VMEM)
    anywhere = pl.BlockSpec(memory_space=pl.ANY)
    exact = ((tokens, width), f32)
    low = ((tokens, width), bf16)
    lows = [low, ((tokens, wide), bf16), low, ((tokens, 3 * width), bf16)]
    near = [
        ((tokens, wide), bf16),
        ((width, wide), bf16),
        ((wide, width), bf16),
        exact,
        exact,
        ((tokens, 3 * width), bf16),
        ((width, 3 * width), bf16),
        ((width, width), bf16),
    ]
    flops = 4 * tokens * (4 * width * width + 2 * width * wide)
    return pl.pallas_call(
        partial(backward_kernel, False, scale.shape[0]),
        out_shape=[jax.ShapeDtypeStruct(*item) for item in [low, exact, ((1, width), f32)]],
        in_specs=[vmem] * 4 + [anywhere] * 8,
        out_specs=[vmem] * 3,
        scratch_shapes=[pltpu.VMEM(*item) for item in lows + near + [exact, exact, low]]
        + [pltpu.SemaphoreType.DMA((8,))],
        compiler_params=pltpu.CompilerParams(vmem_limit_bytes=60 * 2**20),
        cost_estimate=pl.CostEstimate(flops=flops, bytes_accessed=2**25, transcendentals=0),
    )(scale, grad_final, block_out, gain, slope, w_up, w_down, x, middle, joined, w_qkv, w_out)


def backward_begin(returned, grad_top, seqs, hidden, entry, slope, w_up, w_down):
    tokens, width = grad_top.shape
    wide = w_up.shape[-1]
    vmem = pl.BlockSpec(memory_space=pltpu.VMEM)
    anywhere = pl.BlockSpec(memory_space=pl.ANY)
    exact = ((tokens, width), f32)
    low = ((tokens, width), bf16)
    wide_low = ((tokens, wide), bf16)
    up, down = ((width, wide), bf16), ((wide, width), bf16)
    results = [exact, exact, ((1, wide), f32), down, up]
    inside = [low, wide_low, ((width, tokens), bf16), down, up]
    return pl.pallas_call(
        partial(backward_kernel, True, seqs),
        out_shape=[jax.ShapeDtypeStruct(*item) for item in results],
        in_specs=[vmem] * 4 + [anywhere] * 3,
        out_specs=[vmem] * 3 + [anywhere] * 2,
        scratch_shapes=[pltpu.VMEM(*item) for item in inside]
        + [pltpu.SemaphoreType.DMA((2, wide // 1024))]
        + [pltpu.VMEM(*item) for item in (wide_low, up, down)]
        + [pltpu.SemaphoreType.DMA((3,))],
        compiler_params=pltpu.CompilerParams(vmem_limit_bytes=60 * 2**20),
        cost_estimate=pl.CostEstimate(
            flops=16 * tokens * width * wide, bytes_accessed=2**25, transcendentals=0
        ),
    )(returned, grad_top, hidden, entry, slope, w_up, w_down)


def tail_kernel(line, seqs, lag, *refs):
    refs = list(refs)

    def take(number):
        return [refs.pop(0) for _ in range(number)]

    scale, bias_grad, rest, factor_one, factor_two, embedded, noisy, w_in = take(8)
    far = take(9)
    parts = take(2)
    (head_part,) = take(1)
    outs = take(5)
    head_out, smalls, rows_all = take(3)
    near = take(9)
    grad_attn, grad_mixed, grad_joined, grad_first, grad_cond, in_weight = take(6)
    rows_own, small_wide, small_own = take(3)
    own, from_core, slots = take(2), take(5), take(5)
    head_own, head_core, head_section, last_total = take(4)
    far_sem, load_sem, core_send, core_recv, ring_send, ring_recv, credit = take(7)
    keep_sem, packet_send, packet_recv, wide_send, wide_recv, rows_send, rows_recv = take(7)
    head_sem, head_send, head_recv, cross_send, cross_recv = take(5)
    grad_middle, grad_entry, middle, x, joined, mixed, entry_attn, w_out, w_qkv = near
    inside = [w_qkv, w_out, in_weight]
    groups = ((0, 1), (2, 3, 4))
    chips = 2 * line
    width = x.shape[1]
    me_section = lax.axis_index("section")
    me_line = lax.axis_index("line")
    me_pair = lax.axis_index("pair")
    me_core = lax.axis_index("core")
    position = me_line + me_pair * (chips - 1 - 2 * me_line)
    section_peer = {"section": 1 - me_section}
    core_peer = {"core": 1 - me_core}
    ways = (1, -1)
    ring_peers = []
    for way in ways:
        peer_line, peer_pair = ring_place(lax.rem(position + way + chips, chips), line)
        ring_peers.append({"line": peer_line, "pair": peer_pair})
    greet([core_peer, section_peer] + ring_peers)

    shapes = [ref.shape[-2:] for ref in from_core]

    def block_of(turn, step):
        ahead = lax.rem(position - ways[turn] * (1 + step) + 2 * chips, chips)
        return ring_place(ahead, line)

    def portion(index, turn):
        high, wide = shapes[index]
        if high % 32 == 0:
            return turn * (high // 2), high // 2, 0, wide
        return 0, high, turn * (wide // 2), wide // 2

    def half_of(index, turn):
        first, rows, col, cols = portion(index, turn)
        return pl.ds(first, rows), pl.ds(col, cols)

    def inside_rows(index, place, pair, core, first, rows):
        base = ((place * 2 + pair) * 2 + core) * shapes[index][0] + first
        return pl.ds(pl.multiple_of(base, 16), rows)

    def source(index, turn, step, core):
        place, pair = block_of(turn, step)
        rows, cols = half_of(index, turn)
        if index < 2:
            return parts[index].at[place, pair, core, rows, cols]
        first, high = portion(index, turn)[:2]
        return inside[index - 2].at[inside_rows(index, place, pair, core, first, high), cols]

    def load(index, turn, step):
        return pltpu.make_async_copy(
            source(index, turn, step, me_core),
            own[index].at[(step % 2, *half_of(index, turn))],
            load_sem.at[index, turn, step],
        )

    def core_copy(index, turn, step):
        return remote(
            source(index, turn, step, 1 - me_core),
            from_core[index].at[(step % 3, *half_of(index, turn))],
            core_send.at[index, turn, step],
            core_recv.at[index, turn, step],
            core_peer,
        )

    def ring_copy(index, turn, step):
        half = half_of(index, turn)
        passed = from_core[index].at[(0, *half)] if step == 0 else slots[index].at[(step - 1, *half)]
        return remote(
            passed,
            slots[index].at[(step, *half)],
            ring_send.at[index, turn, step],
            ring_recv.at[index, turn, step],
            ring_peers[turn],
        )

    def to_core(group, step):
        if step >= 3:
            pl.semaphore_wait(credit.at[group], 1)
        for index in groups[group]:
            for turn in range(2):
                if index < 2:
                    load(index, turn, step).start()
                core_copy(index, turn, step).start()

    def stop(group, step, between):
        first, last = step == 0, step == chips - 1
        for index in groups[group]:
            for turn in range(2):
                start, rows, left, wide = portion(index, turn)
                tile = min(wide, 512)
                if index < 2:
                    load(index, turn, step).wait()
                core_copy(index, turn, step).wait_recv()
                if not first:
                    ring_copy(index, turn, step - 1).wait_recv()
                place, pair = block_of(turn, step)

                @pl.loop(0, rows // 16)
                def _(block):
                    row = pl.ds(pl.multiple_of(start + block * 16, 16), 16)
                    if index >= 2:
                        own_row = inside_rows(index, place, pair, me_core, start + block * 16, 16)
                    for col in range(left, left + wide, tile):
                        cols = pl.ds(col, tile)
                        if index < 2:
                            mine = own[index][step % 2, row, cols]
                        else:
                            mine = inside[index - 2][own_row, cols]
                        total = from_core[index][step % 3, row, cols].astype(f32)
                        total = total + mine.astype(f32)
                        if not first:
                            total = total + slots[index][step - 1, row, cols].astype(f32)
                        if last and index == 4:
                            last_total[row, cols] = total
                        elif last:
                            outs[index][row, cols] = total.astype(bf16)
                        elif first:
                            from_core[index][0, row, cols] = total.astype(bf16)
                        else:
                            slots[index][step - 1, row, cols] = total.astype(bf16)

                if not last:
                    ring_copy(index, turn, step).start()
                between()
        if step == 1:
            for index in groups[group]:
                for turn in range(2):
                    ring_copy(index, turn, 0).wait_send()
        if 1 <= step <= 4:
            amount = 2 if step == 1 else 1
            pl.semaphore_signal(
                credit.at[group], inc=amount, device_id=core_peer, device_id_type=MESH
            )

    hops = (line, line - 1)

    def packet_blocks(place, pair):
        return [smalls.at[place, pair, me_core], rows_all.at[place, pair, me_core]]

    def packet_hops(turn, hop, away):
        place, pair = ring_place(
            lax.rem(position - ways[turn] * (hop + away) + 2 * chips, chips), line
        )
        return [
            remote(
                block,
                block,
                packet_send.at[n, turn, hop],
                packet_recv.at[n, turn, hop],
                ring_peers[turn],
            )
            for n, block in enumerate(packet_blocks(place, pair))
        ]

    def pass_packets(hop):
        for turn in range(2):
            if 0 < hop <= hops[turn]:
                for copy in packet_hops(turn, hop - 1, 1):
                    copy.wait_recv()
            if hop < hops[turn]:
                for copy in packet_hops(turn, hop, 0):
                    copy.start()

    small_slot, rows_slot = packet_blocks(me_line, me_pair)
    keep_small = pltpu.make_async_copy(small_own, small_slot, keep_sem.at[0])
    keep_rows = pltpu.make_async_copy(rows_own, rows_slot, keep_sem.at[1])
    rows_over = remote(rows_own, rows_slot, rows_send, rows_recv, section_peer)
    across = [
        remote(block, block, wide_send.at[n], wide_recv.at[n], core_peer)
        for n, block in enumerate([smalls.at[:, :, me_core], rows_all.at[:, :, me_core]])
    ]
    def packets_ready():
        keep_small.wait()

        @pl.when(me_section == 0)
        def _():
            keep_rows.wait()

        @pl.when(me_section == 1)
        def _():
            rows_over.wait_recv()

    high = head_part.shape[0] // 4

    def shard(n):
        return head_part.at[pl.ds(n * high, high)]

    head_loads = [
        pltpu.make_async_copy(shard(2 * n), head_own.at[n], head_sem.at[n]) for n in range(2)
    ]
    head_copies = [
        remote(shard(2 * n + 1), head_core.at[n], head_send.at[n], head_recv.at[n], core_peer)
        for n in range(2)
    ]
    head_copies.append(
        remote(head_core.at[1], head_section, head_send.at[2], head_recv.at[2], section_peer)
    )

    def head_over_cores():
        for copy in head_loads:
            copy.wait()
        for copy in head_copies[:2]:
            copy.wait_recv()

        @pl.loop(0, high // 16)
        def _(block):
            rows = pl.ds(pl.multiple_of(block * 16, 16), 16)
            value = head_core[1, rows, :].astype(f32) + head_own[1, rows, :].astype(f32)
            head_core[1, rows, :] = value.astype(bf16)

        head_copies[2].start()

    def head_over_sections():
        head_copies[2].wait_recv()

        @pl.loop(0, high // 16)
        def _(block):
            rows = pl.ds(pl.multiple_of(block * 16, 16), 16)
            value = head_core[0, rows, :].astype(f32) + head_own[0, rows, :].astype(f32)
            value = value + head_section[rows, :].astype(f32)
            head_out[rows, :] = value.astype(bf16)

    far_copies = []
    for n, (where, target) in enumerate(zip(far, near)):
        where = where.at[0] if n >= 7 else where
        far_copies.append(pltpu.make_async_copy(where, target, far_sem.at[n]))

    def waits(*numbers):
        for n in numbers:
            far_copies[n].wait()

    def store_middle(rows, value):
        grad_middle[rows, :] = value
        grad_attn[rows, :] = value.astype(bf16)

    def store_first(rows, value):
        grad_first[rows, :] = value.astype(bf16)

    def second_norm(seq):
        if seq == 0:
            waits(0, 1, 2)
        norm_grads(middle, grad_entry, grad_middle, scale, grad_cond, 1, seq, store_middle)

    def mixed_grads(index):
        if index == 0:
            waits(7)
        part = pl.ds(index * 512, 512)
        grad_mixed[:, part] = nt(grad_attn[...], w_out[part, :]).astype(bf16)

    def heads_grads(pair):
        if pair == 0:
            waits(4)
        attention_grads(joined, grad_mixed, grad_joined, pair, seqs)

    def entry_grads(index):
        if index == 0:
            waits(8)
        part = pl.ds(index * 256, 256)
        grad_entry[:, part] = nt(grad_joined[...], w_qkv[part, :])

    def first_norm(seq):
        if seq == 0:
            waits(3)
        norm_grads(x, grad_entry, grad_middle, scale, grad_cond, 0, seq, store_first)

    def embedding_rows(_):
        grad_noisy = nt(grad_first[...], w_in[...])
        inner = jnp.mean(grad_noisy * embedded[...], -1, keepdims=True)
        value = factor_one[...] * grad_noisy - factor_two[...] * embedded[...] * inner
        rows_own[...] = value.astype(bf16)

        @pl.when(me_section == 0)
        def _():
            keep_rows.start()
            rows_over.start()

    def small_rows(_):
        each = small_wide.shape[1]
        for seq in range(seqs):
            for n in range(2 * width // each):
                row = pl.ds(seq * (2 * width // each) + n, 1)
                small_wide[row, :] = grad_cond[seq, :, pl.ds(n * each, each)]
        first = seqs * 2 * width // each
        for n in range(bias_grad.shape[1] // each):
            small_wide[pl.ds(first + n, 1), :] = bias_grad[:, pl.ds(n * each, each)]
        first += bias_grad.shape[1] // each
        small_wide[pl.ds(first, rest.shape[0]), :] = rest[...]
        small_own[...] = small_wide[...].astype(bf16)
        keep_small.start()

    def input_weight(_):
        in_weight[...] = tn(noisy[...], grad_first[...]).astype(bf16)

    def qkv_weight(index):
        if index == 0:
            waits(6)
        part = pl.ds(index * 256, 256)
        w_qkv[part, :] = tn(entry_attn[:, part], grad_joined[...]).astype(bf16)

    def out_weight(index):
        if index == 0:
            waits(5)
        part = pl.ds(index * 512, 512)
        w_out[part, :] = tn(mixed[:, part], grad_attn[...]).astype(bf16)

    steps = []
    for step, number in (
        (second_norm, seqs),
        (mixed_grads, width // 512),
        (heads_grads, width // 128),
        (entry_grads, width // 256),
        (first_norm, seqs),
        (embedding_rows, 1),
        (small_rows, 1),
        (input_weight, 1),
        (qkv_weight, width // 256),
        (out_weight, width // 512),
    ):
        steps += [partial(step, n) for n in range(number)]
    at_once = -(-len(steps) // (4 * lag))

    def work():
        for _ in range(at_once):
            if steps:
                steps.pop(0)()

    def nothing():
        pass

    to_core(0, 0)
    for copy in far_copies[:3]:
        copy.start()
    to_core(0, 1)
    for n in (7, 4, 8, 3, 6, 5):
        far_copies[n].start()
    stop(0, 0, work)
    for turn in range(1, chips + lag):
        if turn + 1 < chips:
            to_core(0, turn + 1)
        if turn == 1:
            for copy in head_loads + head_copies[:2]:
                copy.start()
        if turn == lag:
            to_core(1, 0)
        if lag <= turn and turn - lag + 1 < chips:
            to_core(1, turn - lag + 1)
        if turn < chips:
            stop(0, turn, work if turn < lag else nothing)
        if turn >= lag:
            stop(1, turn - lag, nothing)
        hop = turn - lag - 2
        if hop == 0:
            packets_ready()
        if 0 <= hop <= line:
            pass_packets(hop)
        if hop == line:
            for copy in across:
                copy.start()
        if turn == 3:
            head_over_cores()
        if turn == chips + lag - 2:
            head_over_sections()
    each = outs[4].shape[0]
    give = remote(last_total.at[pl.ds(each, each)], outs[4], cross_send, cross_recv, section_peer)

    @pl.when(me_section == 0)
    def _():
        give.start()
        outs[4][...] = last_total[pl.ds(0, each), :]

    for copy in across:
        copy.wait()
    for copy in head_copies:
        copy.wait_send()
    for turn in range(2):
        for hop in range(hops[turn]):
            for copy in packet_hops(turn, hop, 0):
                copy.wait_send()
    for index in range(5):
        for turn in range(2):
            for step in range(chips):
                core_copy(index, turn, step).wait_send()
                if 0 < step < chips - 1:
                    ring_copy(index, turn, step).wait_send()

    @pl.when(me_section == 0)
    def _():
        rows_over.wait_send()
        give.wait_send()

    @pl.when(me_section == 1)
    def _():
        give.wait_recv()


def tail_pass(
    scale, bias_grad, rest, factors, embedded, noisy, w_in, far, parts, head_part, collective_id
):
    grad_middle = far[0]
    tokens, width = grad_middle.shape
    seqs = scale.shape[0]
    line = parts[0].shape[0]
    chips = 2 * line
    count = 4 * line
    emb_width = noisy.shape[1]
    vmem = pl.BlockSpec(memory_space=pltpu.VMEM)
    anywhere = pl.BlockSpec(memory_space=pl.ANY)
    dma = pltpu.SemaphoreType.DMA
    shapes = [part.shape[-2:] for part in parts]
    shapes += [
        (width // count, 3 * width),
        (width // count, width),
        (emb_width // count, width),
    ]
    each = shapes[4][0] // 2
    high = head_part.shape[0] // 4
    small = ((seqs * 2 * width + bias_grad.shape[1]) // emb_width + rest.shape[0], emb_width)
    exact = ((tokens, width), f32)
    low = ((tokens, width), bf16)
    three = ((tokens, 3 * width), bf16)
    rows = (tokens, emb_width)
    results = [(shape, bf16) for shape in shapes[:4]]
    results += [((each, width), f32), ((high, width), bf16)]
    results += [((line, 2, 2) + small, bf16), ((line, 2, 2) + rows, bf16)]
    room = [exact, exact, exact, exact, three, low, low]
    room += [((width, width), bf16), ((width, 3 * width), bf16)]
    room += [low, low, three, low, ((seqs, 1, 2 * width), f32), ((emb_width, width), bf16)]
    room += [(rows, bf16), (small, f32), (small, bf16)]
    room += [((2,) + shape, bf16) for shape in shapes[:2]]
    room += [((3,) + shape, bf16) for shape in shapes]
    room += [((chips - 1,) + shape, bf16) for shape in shapes]
    room += [((2, high, width), bf16), ((2, high, width), bf16), ((high, width), bf16)]
    room += [(shapes[4], f32)]
    scratch = [pltpu.VMEM(*item) for item in room]
    scratch += [dma((9,)), dma((2, 2, chips)), dma((5, 2, chips)), dma((5, 2, chips))]
    scratch += [dma((5, 2, chips - 1)), dma((5, 2, chips - 1)), pltpu.SemaphoreType.REGULAR((2,))]
    scratch += [dma((2,)), dma((2, 2, line)), dma((2, 2, line)), dma((2,)), dma((2,)), dma, dma]
    scratch += [dma((2,)), dma((3,)), dma((3,)), dma, dma]
    return pl.pallas_call(
        partial(tail_kernel, line, seqs, line),
        out_shape=[jax.ShapeDtypeStruct(*item) for item in results],
        in_specs=[vmem] * 8 + [anywhere] * 12,
        out_specs=[vmem] * 6 + [anywhere] * 2,
        scratch_shapes=scratch,
        compiler_params=pltpu.CompilerParams(
            collective_id=collective_id, has_side_effects=True, vmem_limit_bytes=62 * 2**20
        ),
        cost_estimate=pl.CostEstimate(flops=0, bytes_accessed=2**29, transcendentals=0),
    )(scale, bias_grad, rest, *factors, embedded, noisy, w_in, *far, *parts, head_part)


def finish_kernel(line, head_rows, *refs):
    ids, rows, *lows = refs[:7]
    *exacts, grad_embed, total = refs[7:]
    me_section = lax.axis_index("section")
    me_line = lax.axis_index("line")
    me_pair = lax.axis_index("pair")
    me_core = lax.axis_index("core")
    high = total.shape[0]
    base = (((me_section * line + me_line) * 2 + me_pair) * 2 + me_core) * grad_embed.shape[0]
    tile = 768
    for index in range(rows.shape[0] // tile):
        part = pl.ds(index * tile, tile)
        entry = lax.broadcasted_iota(jnp.int32, (high, tile), 0) + base
        place = jnp.where(entry == ids[:, part], 1.0, 0.0).astype(bf16)
        product = nn(place, rows[part, :])
        total[...] = product if index == 0 else total[...] + product
    grad_embed[...] = total[pl.ds(0, grad_embed.shape[0]), :]
    for low, exact in zip(lows, exacts):
        whole = exact.shape[0] // 16
        left = exact.shape[0] % 16

        @pl.loop(0, whole)
        def _(block):
            part = pl.ds(pl.multiple_of(block * 16, 16), 16)
            exact[part, :] = low[part, :].astype(f32)

        if left:
            value = low[pl.ds(whole * 16, 16), :].astype(f32)
            exact[pl.ds(whole * 16, left), :] = value[:left]


def finish(ids, rows, lows, line, head_rows, out_rows):
    vmem = pl.BlockSpec(memory_space=pltpu.VMEM)
    shapes = [low.shape for low in lows[:-1]] + [(head_rows, lows[-1].shape[1])]
    shapes.append((out_rows, rows.shape[1]))
    return pl.pallas_call(
        partial(finish_kernel, line, head_rows),
        out_shape=[jax.ShapeDtypeStruct(shape, f32) for shape in shapes],
        in_specs=[vmem] * 7,
        out_specs=[vmem] * 6,
        scratch_shapes=[pltpu.VMEM((-(-out_rows // 16) * 16, rows.shape[1]), f32)],
        compiler_params=pltpu.CompilerParams(vmem_limit_bytes=60 * 2**20),
        cost_estimate=pl.CostEstimate(
            flops=2 * out_rows * rows.size, bytes_accessed=2**24, transcendentals=0
        ),
    )(ids, rows, *lows)


def norm_rows(values):
    centred = values - jnp.mean(values, -1, keepdims=True)
    factor = lax.rsqrt(jnp.mean(centred * centred, -1, keepdims=True) + epsilon)
    return (centred * factor, factor)


def norm_back(gradient, normed, factor):
    return factor * (
        gradient
        - jnp.mean(gradient, -1, keepdims=True)
        - normed * jnp.mean(gradient * normed, -1, keepdims=True)
    )


def time_features(noise_level):
    half_width = TFEAT // 2
    rates = jnp.exp(jnp.arange(half_width, dtype=f32) * (math.log(1000.0) / half_width))
    angles = (jnp.log(noise_level) / 4.0)[:, None] * rates[None, :]
    return jnp.concatenate([jnp.cos(angles), jnp.sin(angles)], -1)


def levels_of(bins, table):
    hits = bins[:, None] == jnp.arange(table.shape[0])[None, :]
    return jnp.sum(jnp.where(hits, table[None, :], 0.0), -1)


def over_dp(part):
    part = part.reshape((part.shape[0] // 4, 2, 2) + part.shape[1:])
    part = lax.psum_scatter(part, "core", scatter_dimension=2)
    part = lax.psum_scatter(part, "pair", scatter_dimension=1)
    return lax.psum_scatter(part, "line", scatter_dimension=0)


def by_owner(part):
    line = lax.axis_size("line")
    return part.astype(bf16).reshape((line, 2, 2, part.shape[0] // (line * 4)) + part.shape[1:])


def mm(spec, left, right):
    return jnp.einsum(spec, left, right, preferred_element_type=f32)


def layer_forward(stream, scale_attn, scale_mlp, weights):
    w_qkv, w_out, w_up, b_hidden, w_down = weights
    seq_count, length, model_width = stream.shape
    normed_attn, factor_attn = norm_rows(stream)
    attn_entry = (normed_attn * scale_attn).astype(bf16)
    joined = mm("nsd,de->nse", attn_entry, w_qkv).astype(bf16)
    qkv_parts = joined.reshape(seq_count, length, 3, HEADS, HEAD_DIM)
    query_rows = qkv_parts[:, :, 0]
    key_rows = qkv_parts[:, :, 1]
    value_rows = qkv_parts[:, :, 2]
    scores = mm("nqhe,nkhe->nhqk", query_rows, key_rows) / math.sqrt(HEAD_DIM)
    exp_scores = jnp.exp(scores - jnp.max(scores, -1, keepdims=True))
    attn_probs = exp_scores / jnp.sum(exp_scores, -1, keepdims=True)
    probs_low = attn_probs.astype(bf16)
    attn_mixed = mm("nhqk,nkhe->nqhe", probs_low, value_rows).astype(bf16)
    attn_mixed = attn_mixed.reshape(seq_count, length, model_width)
    middle = stream + mm("nsd,de->nse", attn_mixed, w_out)
    normed_mlp, factor_mlp = norm_rows(middle)
    mlp_entry = (normed_mlp * scale_mlp).astype(bf16)
    up_proj = mm("nsd,df->nsf", mlp_entry, w_up) + b_hidden
    below = 0.5 + 0.5 * lax.erf(up_proj * math.sqrt(0.5))
    hidden = (up_proj * below).astype(bf16)
    density = jnp.exp(-0.5 * up_proj * up_proj) * (1.0 / math.sqrt(2.0 * math.pi))
    slope = (below + up_proj * density).astype(bf16)
    block_out = middle + mm("nsf,fd->nsd", hidden, w_down)
    kept = (
        normed_attn,
        factor_attn,
        attn_entry,
        query_rows,
        key_rows,
        value_rows,
        attn_probs,
        probs_low,
        attn_mixed,
        normed_mlp,
        factor_mlp,
        mlp_entry,
        slope,
        hidden,
    )
    return (block_out, kept)


def layer_backward(grad_out, kept, scale_attn, scale_mlp, weights, whole):
    w_qkv, w_out, w_up, b_hidden, w_down = weights
    (
        normed_attn,
        factor_attn,
        attn_entry,
        query_rows,
        key_rows,
        value_rows,
        attn_probs,
        probs_low,
        attn_mixed,
        normed_mlp,
        factor_mlp,
        mlp_entry,
        slope,
        hidden,
    ) = kept
    seq_count, length, model_width = grad_out.shape
    grads = {}
    grad_branch = grad_out.astype(bf16)
    if whole:
        grads["down"] = by_owner(mm("nsf,nsd->fd", hidden, grad_branch))
    grad_hidden = mm("nsd,fd->nsf", grad_branch, w_down)
    grad_up_proj = (grad_hidden * slope.astype(f32)).astype(bf16)
    if whole:
        grads["bias"] = jnp.sum(grad_up_proj.astype(f32), (0, 1))
        grads["up"] = by_owner(mm("nsd,nsf->df", mlp_entry, grad_up_proj))
    grad_entry = mm("nsf,df->nsd", grad_up_proj, w_up)
    grad_middle = grad_out + norm_back(grad_entry * scale_mlp, normed_mlp, factor_mlp)
    grad_attn = grad_middle.astype(bf16)
    if whole:
        grads["out"] = by_owner(mm("nsd,nse->de", attn_mixed, grad_attn))
    grad_mixed = mm("nse,de->nsd", grad_attn, w_out)
    grad_mixed = grad_mixed.astype(bf16).reshape(seq_count, length, HEADS, HEAD_DIM)
    grad_probs = mm("nqhe,nkhe->nhqk", grad_mixed, value_rows)
    grad_values = mm("nhqk,nqhe->nkhe", probs_low, grad_mixed)
    grad_scores = (
        attn_probs * (grad_probs - jnp.sum(grad_probs * attn_probs, -1, keepdims=True))
    ).astype(bf16)
    grad_query = mm("nhqk,nkhe->nqhe", grad_scores, key_rows) / math.sqrt(HEAD_DIM)
    grad_keys = mm("nhqk,nqhe->nkhe", grad_scores, query_rows) / math.sqrt(HEAD_DIM)
    grad_joined = jnp.stack([grad_query, grad_keys, grad_values], 2).astype(bf16)
    grad_joined = grad_joined.reshape(seq_count, length, 3 * model_width)
    if whole:
        grads["qkv"] = by_owner(mm("nsd,nse->de", attn_entry, grad_joined))
    grad_attn_entry = mm("nse,de->nsd", grad_joined, w_qkv)
    grad_stream = grad_middle + norm_back(grad_attn_entry * scale_attn, normed_attn, factor_attn)
    if whole:
        grads["cond"] = jnp.concatenate(
            [jnp.sum(grad_attn_entry * normed_attn, 1), jnp.sum(grad_entry * normed_mlp, 1)], -1
        )
    return (grad_stream, grads)


def local(
    token_ids,
    target_ids,
    time_bins,
    sigma_table,
    noise,
    embed,
    w_in,
    w_time,
    norm_gain,
    w_qkv,
    w_out,
    w_up,
    b_hidden,
    w_down,
    out_gain,
    head,
):
    section = lax.axis_index("section")
    line_at = lax.axis_index("line")
    pair_at = lax.axis_index("pair")
    core = lax.axis_index("core")
    sections = lax.axis_size("section")
    line = lax.axis_size("line")
    chip = line_at * 2 + pair_at
    chips = line * 2
    cores = 2
    dp_count = chips * cores
    dp_index = chip * cores + core
    is_first = section == 0
    seqs, length = token_ids.shape
    tokens = seqs * length
    half = tokens // sections
    model_width = w_out.shape[-1]
    emb_rows, emb_width = embed.shape
    head_rows = head.shape[0]
    straight = line <= 4 and half % 16 == 0 and model_width // dp_count % 16 == 0

    if straight:
        lanes = -(-half // 128) * 128
        blocks = [part.reshape(2, half) for part in (token_ids, target_ids)]
        blocks.append(jnp.pad(time_bins[None, :], ((0, 0), (0, half - seqs))))
        own_ids = jnp.pad(jnp.concatenate(blocks, 0), ((0, 3), (0, lanes - half)))
        head_own = jnp.pad(head, ((0, -head_rows % 512), (0, 0)))
        all_ids, embedded, head_early, head_core = start_pass(
            own_ids, embed, head_own, half, line, 0
        )
        all_ids = all_ids.reshape(dp_count, 8, lanes)
        all_tokens = all_ids[:, 0:2, :half].reshape(dp_count, tokens)
        all_targets = all_ids[:, 2:4, :half].reshape(dp_count, tokens)
        all_bins = all_ids[:, 4, :seqs].reshape(-1)
        embedded = embedded.swapaxes(1, 2)
    else:
        own_ids = jnp.concatenate([token_ids.reshape(-1), target_ids.reshape(-1), time_bins])
        all_ids = lax.all_gather(own_ids, DP)
        all_tokens = all_ids[:, :tokens]
        all_targets = all_ids[:, tokens : 2 * tokens]
        all_bins = all_ids[:, 2 * tokens :].reshape(-1)
        own_rows = dp_index * emb_rows + jnp.arange(emb_rows)
        half_tokens = lax.dynamic_slice_in_dim(all_tokens, section * half, half, 1)
        picked = (half_tokens.reshape(-1)[:, None] == own_rows[None, :]).astype(bf16)
        found = jnp.dot(picked, embed, preferred_element_type=f32).astype(bf16)
        embedded = lax.all_gather(over_dp(found.reshape(dp_count, half, emb_width)), "section")
    embedded = embedded.astype(f32).reshape(seqs, length, emb_width)

    swapped = [(0, 1), (1, 0)]
    if not straight:
        head_group = lax.all_gather(lax.all_gather(head, "core"), "section")
        head_group = head_group.reshape(-1, model_width)
        vocab_base = (
            (jnp.arange(sections)[:, None] * chips + chip) * cores + jnp.arange(cores)[None, :]
        ) * head_rows
        columns = (vocab_base[:, :, None] + jnp.arange(head_rows)[None, None, :]).reshape(-1)

    noise_level = levels_of(time_bins, sigma_table)
    unit_factor = lax.rsqrt(jnp.mean(embedded * embedded, -1, keepdims=True) + epsilon)
    level_col = noise_level[:, None, None]
    noise_scale = lax.rsqrt(level_col * level_col + 1.0)
    noisy_rows = ((embedded * unit_factor + level_col * noise) * noise_scale).astype(bf16)
    time_feats = time_features(noise_level)
    conditioned = jnp.dot(time_feats, w_time[0].astype(f32), precision=highest) + norm_gain[0]
    scale_attn = conditioned[:, None, :model_width]
    scale_mlp = conditioned[:, None, model_width:]
    scale = conditioned[:, None, :]
    weights = (w_qkv[0], w_out[0], w_up[0], b_hidden[0], w_down[0])
    stacked = (w_qkv, w_out, w_up, b_hidden, w_down)
    stream0 = mm("nse,ed->nsd", noisy_rows, w_in)
    flat = (tokens, model_width)
    if straight:
        block_out, final_rows, *kept, head_late, head_fourth = forward_pass(
            stream0.reshape(flat), scale, stacked, out_gain[None, :], head_own, head_early, 1
        )
        heads = [head_own, head_core, head_early, head_late, head_fourth]
    else:
        first_out = layer_forward(stream0, scale_attn, scale_mlp, weights)[0].astype(bf16)
        arrived = lax.ppermute(first_out, "section", swapped)
        stream = jnp.where(is_first, stream0, arrived.astype(f32))
        block_out, kept = layer_forward(stream, scale_attn, scale_mlp, weights)
        final_normed, final_factor = norm_rows(block_out.astype(bf16).astype(f32))
        final_rows = (final_normed * out_gain).astype(bf16).reshape(flat)

    targets_group = lax.dynamic_slice_in_dim(
        all_targets.reshape(chips, cores, tokens), core, 1, 1
    )[:, 0]
    targets_group = lax.dynamic_slice_in_dim(targets_group, section * half, half, 1)
    if straight:
        grad_final, grad_head, lse, picks = head_pass(
            final_rows, targets_group.reshape(line, 1, tokens), heads, line, head_rows, length, 3
        )
    else:
        targets_group = targets_group.reshape(-1)
        handed = lax.ppermute(final_rows[:half], "section", [(1, 0), (0, 1)])
        own_final = jnp.where(is_first, handed, final_rows[half:])
        group_final = lax.all_gather(own_final, ("line", "pair"), tiled=True)
        logits = mm("td,vd->tv", group_final, head_group)
        local_top = jnp.max(logits, -1)
        local_total = jnp.sum(jnp.exp(logits - local_top[:, None]), -1)
        mark = columns[None, :] == targets_group[:, None]
        local_pick = jnp.sum(jnp.where(mark, logits, 0.0))
        stats = lax.all_gather(jnp.stack([local_top, local_total]), ("line", "pair"))
        all_top = jnp.max(stats[:, 0], 0)
        all_total = jnp.sum(stats[:, 1] * jnp.exp(stats[:, 0] - all_top), 0)
        log_total = all_top + jnp.log(all_total)
        soft_rows = jnp.exp(logits - log_total[:, None])
        logit_grads = ((soft_rows - jnp.where(mark, 1.0, 0.0)) / length).astype(bf16)
        grad_final = jnp.dot(logit_grads, head_group, preferred_element_type=f32).astype(bf16)
        grad_final = lax.psum_scatter(grad_final, ("line", "pair"), scatter_dimension=0, tiled=True)
        handed = lax.ppermute(grad_final, "section", swapped)
        grad_final = jnp.concatenate([handed, grad_final], 0)
        grad_head = mm("tv,td->vd", logit_grads, group_final).astype(bf16)
        grad_head = grad_head.reshape(sections, cores, head_rows, model_width)
        grad_head = lax.psum_scatter(grad_head, "core", scatter_dimension=1)
        grad_head = lax.psum_scatter(grad_head, "section", scatter_dimension=0).astype(f32)

        ce_part = jnp.sum(log_total) / chips - local_pick
    if straight:
        grad_second, grad_top, out_part = backward_pass(
            grad_final, block_out, out_gain[None, :], scale, kept, stacked
        )
        returned = lax.ppermute(grad_second, "section", swapped)
        lse, picks, out_part = lax.optimization_barrier((lse, picks, out_part))
        ce_part = jnp.sum(lse) / chips - jnp.sum(picks)
        out_part = out_part.reshape(-1)
        x, joined, mixed, middle, entry_attn, entry_mlp, slope, hidden = kept
        grad_middle, grad_entry, grad_bias, down_part, up_part = backward_begin(
            returned, grad_top, seqs, hidden, entry_mlp, slope, w_up, w_down
        )
        parts = [by_owner(down_part), by_owner(up_part)]
    else:
        grad_final = grad_final.astype(f32).reshape(stream0.shape)
        out_part = jnp.sum(grad_final * final_normed, (0, 1))
        grad_top = norm_back(grad_final * out_gain, final_normed, final_factor)
        grad_second = layer_backward(grad_top, kept, scale_attn, scale_mlp, weights, False)[0]
        returned = lax.ppermute(grad_second.astype(bf16), "section", swapped)
        grad_cot = jnp.where(is_first, returned.astype(f32), grad_top)
        grad_stream, grads = layer_backward(grad_cot, kept, scale_attn, scale_mlp, weights, True)
        grad_first = grad_stream.astype(bf16)
    out_part = jnp.where(is_first, 0.0, out_part)

    ce_high = ce_part.astype(bf16).astype(f32)
    ce_mid = (ce_part - ce_high).astype(bf16).astype(f32)
    ce_low = ce_part - ce_high - ce_mid
    shared = jnp.concatenate([out_part, jnp.stack([ce_high, ce_mid, ce_low])])
    shared_rows = -(-shared.shape[0] // emb_width)
    shared = jnp.pad(shared, (0, shared_rows * emb_width - shared.shape[0]))
    shared = shared.reshape(-1, emb_width).astype(bf16)
    both = [shared, lax.ppermute(shared, "section", swapped)]

    cubed = unit_factor * unit_factor * unit_factor
    cond_rows = seqs * 2 * model_width // emb_width
    bias_rows = b_hidden.shape[1] // emb_width
    if straight:
        rest = jnp.concatenate(both, 0).astype(f32)
        rest = jnp.pad(rest, ((0, -(cond_rows + bias_rows + rest.shape[0]) % 16), (0, 0)))
        factors = [
            (value * noise_scale).reshape(tokens, 1) for value in (unit_factor, cubed)
        ]
        owned = noisy_rows.reshape(tokens, sections, dp_count, -1)
        owned = owned.swapaxes(1, 2).reshape(tokens, emb_width)
        far = [grad_middle, grad_entry, middle, x, joined, mixed, entry_attn, w_out, w_qkv]
        grad_down, grad_up, grad_qkv, grad_wout, grad_w_in, grad_head, smalls, rows_all = tail_pass(
            scale,
            grad_bias,
            rest,
            factors,
            embedded.reshape(tokens, emb_width),
            owned,
            w_in,
            far,
            parts,
            grad_head,
            2,
        )
        ids = all_tokens.reshape(1, -1)
        grad_down, grad_up, grad_qkv, grad_wout, grad_head, grad_embed = finish(
            ids,
            rows_all.reshape(-1, emb_width),
            [grad_down, grad_up, grad_qkv, grad_wout, grad_head],
            line,
            head_rows,
            emb_rows // sections,
        )
    else:
        in_part = mm("nse,nsd->ed", noisy_rows, grad_first).astype(bf16)
        in_part = in_part.reshape(sections, dp_count, -1, model_width).swapaxes(0, 1)
        in_sum = over_dp(in_part).astype(f32)
        in_handed = lax.ppermute(in_sum[1], "section", swapped)
        grad_w_in = jnp.where(is_first, in_sum[0], in_handed)
        grad_noisy = mm("nsd,ed->nse", grad_first, w_in)
        grad_unit = grad_noisy * noise_scale
        grad_embedded = unit_factor * grad_unit - cubed * embedded * jnp.mean(
            grad_unit * embedded, -1, keepdims=True
        )
        grad_flat = grad_embedded.reshape(tokens, emb_width).astype(bf16)
        handed = lax.ppermute(grad_flat, "section", swapped)
        rows_all = lax.all_gather(jnp.where(is_first, grad_flat, handed), DP)
        small = [grads["cond"].reshape(-1, emb_width), grads["bias"].reshape(-1, emb_width)]
        smalls = lax.all_gather(
            jnp.concatenate([value.astype(bf16) for value in small] + both, 0), DP
        )
        grad_down, grad_up, grad_qkv, grad_wout = [
            over_dp(part.reshape((dp_count,) + part.shape[3:])).astype(f32)
            for part in (grads["down"], grads["up"], grads["qkv"], grads["out"])
        ]
        grad_all = rows_all.reshape(-1, emb_width)
        out_rows = emb_rows // sections
        target_rows = (section * dp_count + dp_index) * out_rows + jnp.arange(out_rows)
        place = (target_rows[:, None] == all_tokens.reshape(-1)[None, :]).astype(bf16)
        grad_embed = jnp.dot(place, grad_all, preferred_element_type=f32)

    smalls = smalls.reshape(dp_count, -1, emb_width).astype(f32)
    cond_all = smalls[:, :cond_rows].reshape(dp_count * seqs, 2 * model_width)
    bias_all = smalls[:, cond_rows : cond_rows + bias_rows].reshape(dp_count, -1)
    hidden_rows = bias_all.shape[1] // dp_count
    grad_bias = jnp.sum(
        lax.dynamic_slice_in_dim(bias_all, dp_index * hidden_rows, hidden_rows, 1), 0
    )
    norm_cols = 2 * model_width // dp_count
    grad_gain = jnp.sum(lax.dynamic_slice_in_dim(cond_all, dp_index * norm_cols, norm_cols, 1), 0)
    feats_all = time_features(levels_of(all_bins, sigma_table))
    feat_rows = TFEAT // dp_count
    feats_own = lax.dynamic_slice_in_dim(feats_all, dp_index * feat_rows, feat_rows, 1)
    grad_time = jnp.dot(feats_own.T, cond_all, precision=highest)
    shared_first = cond_rows + bias_rows
    both = smalls[:, shared_first : shared_first + 2 * shared_rows]
    both = jnp.sum(both.reshape(dp_count, 2, -1), (0, 1))
    loss = jnp.sum(both[model_width : model_width + 3]) / (tokens * dp_count)
    gain_rows = model_width // dp_count
    grad_out_gain = lax.dynamic_slice_in_dim(both, dp_index * gain_rows, gain_rows)
    return (
        loss,
        grad_embed,
        grad_w_in,
        grad_time[None],
        grad_gain[None],
        grad_qkv[None],
        grad_wout[None],
        grad_up[None],
        grad_bias[None],
        grad_down[None],
        grad_out_gain,
        grad_head,
    )


def solution(mesh):
    sections, dp_count = mesh.shape["section"], mesh.shape["dp"]
    fine = Mesh(mesh.devices.reshape(sections, dp_count // 4, 2, 2), ("section",) + DP)
    everywhere = ("section",) + DP
    in_specs = (
        P(DP, None),
        P(DP, None),
        P(DP),
        P(),
        P(DP, None, None),
        P(DP, None),
        P(),
        P("section", None, None),
        P("section", None),
        P("section", None, None),
        P("section", None, None),
        P("section", None, None),
        P("section", None),
        P("section", None, None),
        P(),
        P(everywhere, None),
    )
    out_specs = (
        P(),
        P(everywhere, None),
        P(everywhere, None),
        P("section", DP, None),
        P("section", DP),
        P("section", DP, None),
        P("section", DP, None),
        P("section", DP, None),
        P("section", DP),
        P("section", DP, None),
        P(DP),
        P(everywhere, None),
    )
    return jax.shard_map(local, mesh=fine, in_specs=in_specs, out_specs=out_specs, check_vma=False)
```

```python
from functools import partial
import math

import jax
import jax.numpy as jnp
from jax import lax
from jax.experimental import pallas as pl
from jax.experimental.pallas import tpu as pltpu
from jax.sharding import Mesh, PartitionSpec as P

HEADS = 16
HEAD_DIM = 64
TFEAT = 256

epsilon = 1e-05
highest = lax.Precision.HIGHEST
f32 = jnp.float32
bf16 = jnp.bfloat16
DP = ("line", "pair", "core")


MESH = pl.DeviceIdType.MESH


def nt(left, right):
    return lax.dot_general(left, right, (((1,), (1,)), ((), ())), preferred_element_type=f32)


def tn(left, right):
    return lax.dot_general(left, right, (((0,), (0,)), ((), ())), preferred_element_type=f32)


def nn(left, right):
    return jnp.dot(left, right, preferred_element_type=f32)


def greet(peers):
    barrier = pltpu.get_barrier_semaphore()
    for peer in peers:
        pl.semaphore_signal(barrier, inc=1, device_id=peer, device_id_type=MESH)
    pl.semaphore_wait(barrier, len(peers))


def remote(source, target, send, recv, peer):
    return pltpu.make_async_remote_copy(
        src_ref=source,
        dst_ref=target,
        send_sem=send,
        recv_sem=recv,
        device_id=peer,
        device_id_type=MESH,
    )


def ring_place(position, line):
    turned = position // line
    return position * (1 - turned) + (2 * line - 1 - position) * turned, turned


def start_kernel(line, *refs):
    ids, embed, head, all_ids, out, head_early, head_core = refs[:7]
    table, found, own, from_core, from_pair, from_line = refs[7:13]
    ids_send, ids_recv, own_sem, core_send, core_recv, pair_send, pair_recv = refs[13:20]
    line_send, line_recv, swap_send, swap_recv, head_send, head_recv = refs[20:]
    me_section = lax.axis_index("section")
    me_line = lax.axis_index("line")
    me_pair = lax.axis_index("pair")
    me_core = lax.axis_index("core")
    section_peer = {"section": 1 - me_section}
    core_peer = {"core": 1 - me_core}
    pair_peer = {"pair": 1 - me_pair}
    peers = []
    for step in range(1, line * 4):
        peers.append(
            {
                "line": lax.rem(me_line + step // 4, line),
                "pair": lax.rem(me_pair + step // 2 % 2, 2),
                "core": lax.rem(me_core + step % 2, 2),
            }
        )
    greet(peers + [section_peer])
    each = head_early.shape[0]
    to_section = remote(
        head.at[pl.ds(0, each)], head_early, head_send.at[0], head_recv.at[0], section_peer
    )
    to_section.start()
    to_other_core = remote(head, head_core, head_send.at[1], head_recv.at[1], core_peer)
    to_other_core.start()
    place = all_ids.at[me_line, me_pair, me_core]
    copies = [remote(ids, place, ids_send.at[n], ids_recv.at[n], peer) for n, peer in enumerate(peers)]
    for copy in copies:
        copy.start()
    keep = pltpu.make_async_copy(ids, place, own_sem)
    keep.start()
    rows = embed.shape[0]
    high = table.shape[1]
    half = out.shape[-1]
    padded = jnp.concatenate(
        [embed[...].astype(f32), jnp.zeros((high - rows, embed.shape[1]), f32)], 0
    )
    table[...] = padded.T.astype(bf16)
    keep.wait()
    for copy in copies:
        copy.wait_recv()
    base = ((me_line * 2 + me_pair) * 2 + me_core) * rows

    def pick(spot, pair, core):
        wanted = all_ids[spot, pair, core, pl.ds(me_section, 1), :][:, :half]
        entry = lax.broadcasted_iota(jnp.int32, (high, half), 0)
        entry = jnp.where(entry < rows, entry + base, -1)
        hot = jnp.where(entry == wanted, 1.0, 0.0).astype(bf16)
        return nn(table[...], hot).astype(bf16)

    def core_copy(spot, pair, turn):
        return remote(
            found.at[turn, spot],
            from_core.at[turn, spot],
            core_send.at[turn, spot],
            core_recv.at[turn, spot],
            core_peer,
        )

    def pair_copy(spot):
        return remote(
            from_core.at[0, spot], from_pair.at[spot], pair_send.at[spot], pair_recv.at[spot], pair_peer
        )

    def line_copy(step):
        spot = lax.rem(me_line + step, line)
        return remote(
            from_core.at[1, spot],
            from_line.at[step - 1],
            line_send.at[step - 1],
            line_recv.at[step - 1],
            {"line": spot},
        )

    order = [lax.rem(me_line + step, line) for step in list(range(1, line)) + [0]]
    for turn, pair in enumerate((1 - me_pair, me_pair)):

        @pl.loop(0, line)
        def _(step):
            spot = lax.rem(me_line + 1 + step, line)
            found[turn, spot] = pick(spot, pair, 1 - me_core)
            core_copy(spot, pair, turn).start()
            own[turn, spot] = pick(spot, pair, me_core)

        if turn == 0:
            for spot in order:
                core_copy(spot, pair, 0).wait_recv()
                from_core[0, spot] = from_core[0, spot] + own[0, spot]
                pair_copy(spot).start()
    for step in list(range(1, line)) + [0]:
        spot = lax.rem(me_line + step, line)
        core_copy(spot, me_pair, 1).wait_recv()
        pair_copy(spot).wait_recv()
        from_core[1, spot] = from_core[1, spot] + own[1, spot] + from_pair[spot]
        if step:
            line_copy(step).start()
    total = from_core[1, me_line]
    for step in range(1, line):
        line_copy(step).wait_recv()
        total = total + from_line[step - 1]
    out[me_section] = total
    swap = remote(out.at[me_section], out.at[me_section], swap_send, swap_recv, section_peer)
    swap.start()
    for copy in copies:
        copy.wait_send()
    for spot in range(line):
        for turn in range(2):
            core_copy(spot, me_pair, turn).wait_send()
        pair_copy(spot).wait_send()
    for step in range(1, line):
        line_copy(step).wait_send()
    swap.wait()
    to_section.wait()
    to_other_core.wait()


def start_pass(ids, embed, head, half, line, collective_id):
    rows, width = embed.shape
    high = -(-rows // 256) * 256
    vmem = pl.BlockSpec(memory_space=pltpu.VMEM)
    anywhere = pl.BlockSpec(memory_space=pltpu.HBM)
    dma = pltpu.SemaphoreType.DMA
    block = (width, half)
    return pl.pallas_call(
        partial(start_kernel, line),
        out_shape=[
            jax.ShapeDtypeStruct((line, 2, 2) + ids.shape, ids.dtype),
            jax.ShapeDtypeStruct((2,) + block, bf16),
            jax.ShapeDtypeStruct((head.shape[0] // 16 * 7, head.shape[1]), bf16),
            jax.ShapeDtypeStruct(head.shape, bf16),
        ],
        in_specs=[vmem, vmem, anywhere],
        out_specs=[vmem, vmem, anywhere, anywhere],
        scratch_shapes=[
            pltpu.VMEM((width, high), bf16),
            pltpu.VMEM((2, line) + block, bf16),
            pltpu.VMEM((2, line) + block, bf16),
            pltpu.VMEM((2, line) + block, bf16),
            pltpu.VMEM((line,) + block, bf16),
            pltpu.VMEM((line - 1,) + block, bf16),
            dma((line * 4 - 1,)),
            dma((line * 4 - 1,)),
            dma,
            dma((2, line)),
            dma((2, line)),
            dma((line,)),
            dma((line,)),
            dma((line - 1,)),
            dma((line - 1,)),
            dma,
            dma,
            dma((2,)),
            dma((2,)),
        ],
        compiler_params=pltpu.CompilerParams(
            collective_id=collective_id, has_side_effects=True, vmem_limit_bytes=60 * 2**20
        ),
        cost_estimate=pl.CostEstimate(flops=0, bytes_accessed=2**27, transcendentals=0),
    )(ids, embed, head)


def head_kernel(line, head_rows, length, *refs):
    final, targets, *heads = refs[:7]
    out, grads, lse_out, pick_out = refs[7:11]
    (table, rows_all, logits, probs, acc, parts, from_pair, from_line, stats, done) = refs[11:21]
    (head_sem, own_sem, give_send, give_recv, along_send, along_recv, pair_send, pair_recv) = refs[21:29]
    (stat_send, stat_recv, sum_send, sum_recv, line_send, line_recv, back_send, back_recv) = refs[29:37]
    last_send, last_recv = refs[37:]
    half = final.shape[0] // 2
    width = 2 * half
    padded = heads[0].shape[0]
    me_section = lax.axis_index("section")
    me_line = lax.axis_index("line")
    me_pair = lax.axis_index("pair")
    me_core = lax.axis_index("core")
    section_peer = {"section": 1 - me_section}
    pair_peer = {"pair": 1 - me_pair}
    chip_peers = []
    for step in range(1, 2 * line):
        chip_peers.append(
            {"line": lax.rem(me_line + step // 2, line), "pair": lax.rem(me_pair + step % 2, 2)}
        )
    greet(chip_peers + [section_peer, {"core": 1 - me_core}])

    def side(pair):
        return pl.ds(pl.multiple_of(pair * half, 16), half)

    loads = []
    for n, part in enumerate(heads):
        first = sum(other.shape[0] for other in heads[:n])
        target = table.at[pl.ds(first, part.shape[0])]
        loads.append(pltpu.make_async_copy(part, target, head_sem.at[n]))
    late = heads[3]
    last = remote(
        late,
        table.at[pl.ds(4 * padded - late.shape[0], late.shape[0])],
        last_send,
        last_recv,
        {"core": 1 - me_core},
    )
    last.start()
    for load in loads:
        load.start()

    quarter = half // 2

    def token_rows(place, pair, chunk):
        first = place * width + pair * half + chunk * quarter
        return pl.ds(pl.multiple_of(first, 16), quarter)

    def group(place):
        return pl.ds(pl.multiple_of(place * width, 128), width)

    def column_block(place, chunk):
        return rows_all.at[token_rows(place, me_pair, chunk)]

    def give(chunk):
        return remote(
            final.at[pl.ds(chunk * quarter, quarter)],
            column_block(me_line, chunk),
            give_send.at[chunk],
            give_recv.at[chunk],
            section_peer,
        )

    def along(step, way, chunk):
        block = column_block(me_line - way * step, chunk)
        turn = (way + 1) // 2
        return remote(
            block,
            block,
            along_send.at[turn, step, chunk],
            along_recv.at[turn, step, chunk],
            {"line": me_line + way},
        )

    def inside(place):
        return (place >= 0) & (place < line)

    def sends_along(step, way):
        return inside(me_line - way * step) & inside(me_line + way)

    def sideways(place, chunk):
        block = column_block(place, chunk)
        return remote(
            block, block, pair_send.at[place, chunk], pair_recv.at[place, chunk], pair_peer
        )

    def arrived_sideways(place, chunk):
        block = rows_all.at[token_rows(place, 1 - me_pair, chunk)]
        return remote(
            block, block, pair_send.at[place, chunk], pair_recv.at[place, chunk], pair_peer
        )

    @pl.when(me_section == 1)
    def _():
        for chunk in range(2):
            give(chunk).start()
        for chunk in range(2):
            keep = pltpu.make_async_copy(
                final.at[pl.ds(half + chunk * quarter, quarter)],
                column_block(me_line, chunk),
                own_sem.at[chunk],
            )
            keep.start()
            keep.wait()

    for chunk in range(2):

        @pl.when(me_section == 0)
        def _():
            give(chunk).wait_recv()

        for way in (1, -1):

            @pl.when(sends_along(0, way))
            def _():
                along(0, way, chunk).start()

        sideways(me_line, chunk).start()

    def pass_on(step):
        for chunk in range(2):
            for way in (1, -1):
                place = me_line - way * step

                @pl.when(inside(place))
                def _():
                    block = column_block(place, chunk)
                    turn = (way + 1) // 2
                    remote(
                        block,
                        block,
                        along_send.at[turn, step - 1, chunk],
                        along_recv.at[turn, step - 1, chunk],
                        {"line": me_line - way},
                    ).wait_recv()

                    @pl.when(inside(me_line + way))
                    def _():
                        along(step, way, chunk).start()

                    sideways(place, chunk).start()

    nearest = []
    for own in range(line):
        near = [own]
        for step in range(1, line):
            near += [place for place in (own - step, own + step) if 0 <= place < line]
        nearest.append(near)

    def by_distance(turn):
        place = 0
        for own in range(line):
            for n in range(line):
                hit = ((me_line == own) & (turn == n)).astype(jnp.int32)
                place = place + hit * nearest[own][n]
        return place

    def vocabulary(tile, rows):
        shard = tile * rows // padded
        first = lax.rem(tile * rows, padded)
        shard_section = lax.rem(me_section + shard // 2, 2)
        shard_core = lax.rem(me_core + lax.rem(shard, 2), 2)
        base = (((shard_section * line + me_line) * 2 + me_pair) * 2 + shard_core) * head_rows
        row = lax.broadcasted_iota(jnp.int32, (rows, 1), 0) + first
        return jnp.where(row < head_rows, row + base, -1)

    tile_rows = 512
    tiles = 4 * padded // tile_rows
    lowest = -1e30

    def score(turn, tops):
        place = by_distance(turn) if turn < line else None
        before = by_distance(turn - 1) if turn > 0 else None
        wanted = None if place is None else targets[place]

        def one(tile, carry):
            rows = pl.ds(pl.multiple_of(tile * tile_rows, tile_rows), tile_rows)
            out = []
            if place is not None:
                top, pick = carry[:2]
                entry = vocabulary(tile, tile_rows)
                part = nt(table[rows, :], rows_all[group(place), :])
                part = jnp.where(entry >= 0, part, lowest)
                logits[turn % 2, rows, :] = part
                out.append(jnp.maximum(top, jnp.max(part, 0, keepdims=True)))
                out.append(
                    pick + jnp.sum(jnp.where(entry == wanted, part, 0.0), 0, keepdims=True)
                )
            if before is not None:
                value = jnp.exp(logits[(turn - 1) % 2, rows, :] - tops)
                probs[rows, group(before)] = value.astype(bf16)
                out.append(carry[-1] + jnp.sum(value, 0, keepdims=True))
            return tuple(out)

        none = jnp.zeros((1, width), f32)
        start = () if place is None else (jnp.full((1, width), lowest, f32), none)
        start += () if before is None else (none,)
        result = lax.fori_loop(0, tiles, one, start)
        if place is not None:
            pick_out[place] = result[1]
        if before is not None:
            own = stats.at[me_line, me_pair, before]
            own[:, 0:width] = tops
            own[:, width : 2 * width] = result[-1]
            for n in range(len(chip_peers)):
                stat_copy(n, before).start()
        return None if place is None else result[0]

    def stat_copy(n, place):
        own = stats.at[me_line, me_pair, place]
        return remote(own, own, stat_send.at[n, place], stat_recv.at[n, place], chip_peers[n])

    def stat_wait(n, place):
        peer = chip_peers[n]
        source_line = lax.rem(2 * me_line + line - peer["line"], line)
        source_pair = peer["pair"]
        block = stats.at[source_line, source_pair, place]
        remote(block, block, stat_send.at[n, place], stat_recv.at[n, place], peer).wait_recv()

    for load in loads:
        load.wait()
    last.wait()

    tops = None
    for turn in range(line + 1):
        if turn + 1 < line:
            pass_on(turn + 1)
        if turn < line:
            for chunk in range(2):
                arrived_sideways(by_distance(turn), chunk).wait_recv()
        tops = score(turn, tops)

    def part_rows(pair, chunk):
        return pl.ds(pl.multiple_of(pair * half + chunk * quarter, 16), quarter)

    def sum_copy(turn, chunk):
        place = lax.rem(me_line + turn + 1, line)
        return remote(
            parts.at[place, part_rows(1 - me_pair, chunk)],
            from_pair.at[turn, pl.ds(chunk * quarter, quarter)],
            sum_send.at[turn, chunk],
            sum_recv.at[turn, chunk],
            pair_peer,
        )

    def line_copy(turn, chunk):
        place = lax.rem(me_line + turn + 1, line)
        return remote(
            parts.at[place, part_rows(me_pair, chunk)],
            from_line.at[turn, pl.ds(chunk * quarter, quarter)],
            line_send.at[turn, chunk],
            line_recv.at[turn, chunk],
            {"line": place},
        )

    def finish(turn, chunk):
        place = lax.rem(me_line + turn + 1, line)
        sum_copy(turn, chunk).wait_recv()
        own = parts.at[place, part_rows(me_pair, chunk)]
        other = from_pair.at[turn, pl.ds(chunk * quarter, quarter)]

        @pl.loop(0, quarter // 16)
        def _(block):
            rows = pl.ds(pl.multiple_of(block * 16, 16), 16)
            own[rows, :] = (own[rows, :].astype(f32) + other[rows, :].astype(f32)).astype(bf16)

    @pl.loop(0, line)
    def _(turn):
        place = lax.rem(me_line + turn + 1, line)
        for n in range(len(chip_peers)):
            stat_wait(n, place)
        tops = [stats[a, b, place, :, 0:width] for a in range(line) for b in range(2)]
        totals = [
            stats[a, b, place, :, width : 2 * width] for a in range(line) for b in range(2)
        ]
        top = tops[0]
        for value in tops[1:]:
            top = jnp.maximum(top, value)
        total = jnp.zeros_like(top)
        for peak, part in zip(tops, totals):
            total = total + part * jnp.exp(peak - top)
        lse = top + jnp.log(total)
        lse_out[place] = lse
        factor = jnp.exp(stats[me_line, me_pair, place, :, 0:width] - lse) / length
        wanted = targets[place]

        def scaled(tile):
            rows = pl.ds(tile * padded, padded)
            entry = vocabulary(tile, padded)
            grad = probs[rows, group(place)].astype(f32) * factor
            grad = (grad - jnp.where(entry == wanted, 1.0 / length, 0.0)).astype(bf16)
            probs[rows, group(place)] = grad
            return grad

        grad = scaled(0)
        for tile in range(4):
            product = tn(grad, table[pl.ds(tile * padded, padded), :])
            if tile < 3:
                grad = scaled(tile + 1)
                acc[...] = product if tile == 0 else acc[...] + product
            else:
                parts[place] = (acc[...] + product).astype(bf16)

        for chunk in range(2):
            sum_copy(turn, chunk).start()

        @pl.when(turn > 0)
        def _():
            for chunk in range(2):
                finish(turn - 1, chunk)
                line_copy(turn - 1, chunk).start()

    gh_rows = 256
    gh_tiles = 4 * padded // gh_rows

    def head_grads(first, last):
        @pl.loop(first, last)
        def _(tile):
            rows = pl.ds(pl.multiple_of(tile * gh_rows, gh_rows), gh_rows)
            value = jnp.dot(probs[rows, :], rows_all[...], preferred_element_type=f32)
            grads[rows, :] = value.astype(bf16)

    def back(chunk):
        part = pl.ds(chunk * quarter, quarter)
        return remote(
            done.at[part], out.at[part], back_send.at[chunk], back_recv.at[chunk], section_peer
        )

    head_grads(0, gh_tiles // 2)
    for chunk in range(2):
        finish(line - 1, chunk)
        for turn in range(line - 1):
            line_copy(turn, chunk).wait_recv()
        own = parts.at[me_line, part_rows(me_pair, chunk)]

        @pl.loop(0, quarter // 16)
        def _(block):
            rows = pl.ds(pl.multiple_of(block * 16, 16), 16)
            chunk_rows = pl.ds(pl.multiple_of(chunk * quarter + block * 16, 16), 16)
            value = own[rows, :].astype(f32)
            for turn in range(line - 1):
                value = value + from_line[turn, chunk_rows, :].astype(f32)
            done[chunk_rows, :] = value.astype(bf16)

        @pl.when(me_section == 0)
        def _():
            back(chunk).start()

    @pl.when(me_section == 0)
    def _():
        out[...] = jnp.zeros_like(out)

    @pl.when(me_section == 1)
    def _():
        out[pl.ds(half, half), :] = done[...]

    head_grads(gh_tiles // 2, gh_tiles)
    for chunk in range(2):

        @pl.when(me_section == 0)
        def _():
            back(chunk).wait_send()

        @pl.when(me_section == 1)
        def _():
            back(chunk).wait_recv()
            give(chunk).wait_send()

        for way in (1, -1):
            for step in range(line - 1):

                @pl.when(sends_along(step, way))
                def _():
                    along(step, way, chunk).wait_send()

        for place in range(line):
            sideways(place, chunk).wait_send()
        for turn in range(line):
            sum_copy(turn, chunk).wait_send()
        for turn in range(line - 1):
            line_copy(turn, chunk).wait_send()
    for place in range(line):
        for n in range(len(chip_peers)):
            stat_copy(n, place).wait_send()


def head_pass(final, targets, heads, line, head_rows, length, collective_id):
    tokens, deep = final.shape
    half = tokens // 2
    padded = heads[0].shape[0]
    vmem = pl.BlockSpec(memory_space=pltpu.VMEM)
    anywhere = pl.BlockSpec(memory_space=pltpu.HBM)
    dma = pltpu.SemaphoreType.DMA
    peers = 2 * line - 1
    return pl.pallas_call(
        partial(head_kernel, line, head_rows, length),
        out_shape=[
            jax.ShapeDtypeStruct((tokens, deep), bf16),
            jax.ShapeDtypeStruct((4 * padded, deep), bf16),
            jax.ShapeDtypeStruct((line, 1, tokens), f32),
            jax.ShapeDtypeStruct((line, 1, tokens), f32),
        ],
        in_specs=[vmem, vmem] + [anywhere] * len(heads),
        out_specs=[vmem] * 4,
        scratch_shapes=[
            pltpu.VMEM((4 * padded, deep), bf16),
            pltpu.VMEM((line * tokens, deep), bf16),
            pltpu.VMEM((2, 4 * padded, tokens), f32),
            pltpu.VMEM((4 * padded, line * tokens), bf16),
            pltpu.VMEM((tokens, deep), f32),
            pltpu.VMEM((line, tokens, deep), bf16),
            pltpu.VMEM((line, half, deep), bf16),
            pltpu.VMEM((line - 1, half, deep), bf16),
            pltpu.VMEM((line, 2, line, 1, 2 * tokens), f32),
            pltpu.VMEM((half, deep), bf16),
            dma((len(heads),)),
            dma((2,)),
            dma((2,)),
            dma((2,)),
            dma((2, line, 2)),
            dma((2, line, 2)),
            dma((line, 2)),
            dma((line, 2)),
            dma((peers, line)),
            dma((peers, line)),
            dma((line, 2)),
            dma((line, 2)),
            dma((line, 2)),
            dma((line, 2)),
            dma((2,)),
            dma((2,)),
            dma,
            dma,
        ],
        compiler_params=pltpu.CompilerParams(
            collective_id=collective_id, has_side_effects=True, vmem_limit_bytes=60 * 2**20
        ),
        cost_estimate=pl.CostEstimate(
            flops=24 * line * padded * tokens * deep, bytes_accessed=2**28, transcendentals=0
        ),
    )(final, targets, *heads)


def row_stats(values):
    centred = values - jnp.mean(values, -1, keepdims=True)
    factor = lax.rsqrt(jnp.mean(centred * centred, -1, keepdims=True) + epsilon)
    return centred * factor, factor


def two_heads(block):
    first = lax.broadcasted_iota(jnp.int32, block.shape, 1) < HEAD_DIM
    zero = jnp.zeros_like(block)
    return jnp.concatenate([jnp.where(first, block, zero), jnp.where(first, zero, block)], 0)


def one_block(stacked):
    rows = stacked.shape[0] // 2
    first = lax.broadcasted_iota(jnp.int32, (rows, stacked.shape[1]), 1) < HEAD_DIM
    return jnp.where(first, stacked[:rows], stacked[rows:])


def attention_weights(queries, keys):
    scores = nt(keys, queries) * (1.0 / math.sqrt(HEAD_DIM))
    exped = jnp.exp(scores - jnp.max(scores, 0, keepdims=True))
    return exped * (1.0 / jnp.sum(exped, 0, keepdims=True))


def tile_of(index, size):
    return pl.ds(pl.multiple_of(index * size, size), size)


def forward_kernel(seqs, *refs):
    refs = list(refs)

    def take(number):
        return [refs.pop(0) for _ in range(number)]

    start, scale, bias, gain = take(4)
    weights = take(4)
    head, head_early = take(2)
    out, final, x, joined, mixed, middle, entry_attn, entry_mlp, slope, hidden = take(10)
    head_late, head_fourth = take(2)
    w_qkv, w_out, w_up, w_down, x_total, arrived, sems, relay_send, relay_recv = take(9)
    head_send, head_recv = refs
    width = start.shape[1]
    length = start.shape[0] // seqs
    me_section = lax.axis_index("section")
    section_peer = {"section": 1 - me_section}
    load_qkv, load_out, load_up, load_down = [
        pltpu.make_async_copy(source.at[0], target, sems.at[n])
        for n, (source, target) in enumerate(zip(weights, (w_qkv, w_out, w_up, w_down)))
    ]
    load_qkv.start()
    core_peer = {"core": 1 - lax.axis_index("core")}
    greet([section_peer, core_peer])
    each = head_early.shape[0]
    to_section = remote(
        head.at[pl.ds(each, head_late.shape[0])],
        head_late,
        head_send.at[0],
        head_recv.at[0],
        section_peer,
    )
    to_section.start()
    to_core = remote(head_early, head_fourth, head_send.at[1], head_recv.at[1], core_peer)
    to_core.start()

    def relay(seq):
        rows = pl.ds(seq * length, length)
        return remote(
            out.at[rows], arrived.at[rows], relay_send.at[seq], relay_recv.at[seq], section_peer
        )

    tile = 512

    def enter(seq):
        rows = pl.ds(seq * length, length)

        @pl.when(me_section == 0)
        def _():
            x[rows, :] = start[rows, :]

        @pl.when(me_section == 1)
        def _():
            relay(seq).wait_recv()
            x[rows, :] = arrived[rows, :].astype(f32)

        normed, _ = row_stats(x[rows, :])
        entry_attn[rows, :] = (normed * scale[seq, :, :width]).astype(bf16)

    def join(first, count):
        rows = pl.ds(first * length, count * length)

        @pl.loop(0, 3 * width // tile)
        def _(index):
            cols = tile_of(index, tile)
            joined[rows, cols] = nn(entry_attn[rows, :], w_qkv[:, cols]).astype(bf16)

    for seq in range(seqs - 1):
        enter(seq)
    load_qkv.wait()
    load_out.start()
    load_up.start()
    join(0, seqs - 1)
    enter(seqs - 1)
    join(seqs - 1, 1)
    load_out.wait()
    load_down.start()
    pairs = width // 128

    @pl.loop(0, pairs)
    def _(pair):
        cols = tile_of(pair, 128)
        for seq in range(seqs):
            rows = pl.ds(seq * length, length)
            queries = two_heads(joined[rows, cols])
            keys = joined[rows, tile_of(pair + pairs, 128)]
            values = joined[rows, tile_of(pair + 2 * pairs, 128)]
            probs = attention_weights(queries, keys).astype(bf16)
            mixed[rows, cols] = one_block(tn(probs, values)).astype(bf16)

    @pl.loop(0, width // tile)
    def _(index):
        cols = tile_of(index, tile)
        middle[:, cols] = x[:, cols] + nn(mixed[...], w_out[:, cols])

    for seq in range(seqs):
        rows = pl.ds(seq * length, length)
        normed, _ = row_stats(middle[rows, :])
        entry_mlp[rows, :] = (normed * scale[seq, :, width:]).astype(bf16)

    load_up.wait()
    load_down.wait()

    def gelu_of(up, rows, cols):
        below = 0.5 + 0.5 * lax.erf(up * math.sqrt(0.5))
        value = (up * below).astype(bf16)
        density = jnp.exp(-0.5 * up * up) * (1.0 / math.sqrt(2.0 * math.pi))
        slope[rows, cols] = (below + up * density).astype(bf16)
        hidden[rows, cols] = value
        return value

    def feed_forward(first, count):
        rows = pl.ds(first * length, count * length)

        def one(index, total):
            sides = [tile_of(2 * index + side, tile) for side in range(2)]
            ups = [nn(entry_mlp[rows, :], w_up[:, cols]) + bias[:, cols] for cols in sides]
            both = jnp.concatenate([gelu_of(up, rows, cols) for up, cols in zip(ups, sides)], 1)
            x_total[rows, :] += nn(both, w_down[tile_of(index, 2 * tile), :])
            return total

        x_total[rows, :] = middle[rows, :]
        lax.fori_loop(0, w_up.shape[1] // (2 * tile), one, 0)
        for seq in range(first, first + count):
            rows = pl.ds(seq * length, length)
            value = x_total[rows, :].astype(bf16)
            out[rows, :] = value

            @pl.when(me_section == 0)
            def _():
                relay(seq).start()

            normed, _ = row_stats(value.astype(f32))
            final[rows, :] = (normed * gain[...]).astype(bf16)

    feed_forward(0, seqs)

    to_section.wait()
    to_core.wait()

    @pl.when(me_section == 0)
    def _():
        for seq in range(seqs):
            relay(seq).wait_send()


def layer_scratch(width, hidden):
    return [
        pltpu.VMEM((width, 3 * width), bf16),
        pltpu.VMEM((width, width), bf16),
        pltpu.VMEM((width, hidden), bf16),
        pltpu.VMEM((hidden, width), bf16),
    ]


def forward_pass(start, scale, weights, gain, head, head_early, collective_id):
    w_qkv, w_out, w_up, b_hidden, w_down = weights
    tokens, width = start.shape
    wide = w_up.shape[-1]
    seqs = scale.shape[0]
    vmem = pl.BlockSpec(memory_space=pltpu.VMEM)
    anywhere = pl.BlockSpec(memory_space=pl.ANY)

    far = pl.BlockSpec(memory_space=pltpu.HBM)

    def low(columns):
        return (tokens, columns), bf16

    exact = ((tokens, width), f32)
    results = [low(width), low(width), exact, low(3 * width), low(width), exact, low(width)]
    results += [low(width), low(wide), low(wide)]
    results += [((head.shape[0] - head_early.shape[0], width), bf16), (head_early.shape, bf16)]
    scratch = layer_scratch(width, wide) + [pltpu.VMEM(*exact), pltpu.VMEM(*low(width))]
    dma = pltpu.SemaphoreType.DMA
    flops = 4 * tokens * (4 * width * width + 2 * width * wide)
    return pl.pallas_call(
        partial(forward_kernel, seqs),
        out_shape=[jax.ShapeDtypeStruct(*item) for item in results],
        in_specs=[vmem] * 4 + [anywhere] * 4 + [far] * 2,
        out_specs=[vmem] * (len(results) - 2) + [far] * 2,
        scratch_shapes=scratch + [dma((4,)), dma((seqs,)), dma((seqs,)), dma((2,)), dma((2,))],
        compiler_params=pltpu.CompilerParams(
            collective_id=collective_id, has_side_effects=True, vmem_limit_bytes=60 * 2**20
        ),
        cost_estimate=pl.CostEstimate(flops=2 * flops, bytes_accessed=2**25, transcendentals=0),
    )(start, scale, b_hidden, gain, w_qkv, w_out, w_up, w_down, head, head_early)


def norm_grads(source, total, grad_middle, scale, grad_cond, half, seq, store):
    width = total.shape[1]
    length = total.shape[0] // scale.shape[0]
    rows = pl.ds(seq * length, length)
    cols = pl.ds(half * width, width)
    normed, factor = row_stats(source[rows, :])
    gradient = total[rows, :]
    if grad_cond is not None:
        grad_cond[seq, :, cols] = jnp.sum(gradient * normed, 0, keepdims=True)
    scaled = gradient * scale[seq, :, cols]
    back = factor * (
        scaled
        - jnp.mean(scaled, -1, keepdims=True)
        - normed * jnp.mean(scaled * normed, -1, keepdims=True)
    )
    store(rows, grad_middle[rows, :] + back)


def attention_grads(joined, grad_mixed, grad_joined, pair, seqs):
    pairs = grad_mixed.shape[1] // 128
    length = grad_mixed.shape[0] // seqs
    shrink = 1.0 / math.sqrt(HEAD_DIM)
    cols = tile_of(pair, 128)
    key_cols = tile_of(pair + pairs, 128)
    value_cols = tile_of(pair + 2 * pairs, 128)
    for seq in range(seqs):
        rows = pl.ds(seq * length, length)
        queries = two_heads(joined[rows, cols])
        keys = joined[rows, key_cols]
        probs = attention_weights(queries, keys)
        grads = two_heads(grad_mixed[rows, cols])
        grad_probs = nt(joined[rows, value_cols], grads)
        inner = jnp.sum(grad_probs * probs, 0, keepdims=True)
        grad_scores = (probs * (grad_probs - inner)).astype(bf16)
        grad_joined[rows, cols] = (one_block(tn(grad_scores, keys)) * shrink).astype(bf16)
        grad_joined[rows, key_cols] = (nn(grad_scores, queries) * shrink).astype(bf16)
        grad_joined[rows, value_cols] = nn(probs.astype(bf16), grads).astype(bf16)


def backward_kernel(begin, seqs, *refs):
    refs = list(refs)

    def take(number):
        return [refs.pop(0) for _ in range(number)]

    if begin:
        incoming, other, hidden, entry = take(4)
        far = take(3)
        grad_middle, total, grad_bias, down_out, up_out = take(5)
        grad_low, grad_up, entry_turned, down_weight, up_weight, out_sem = take(6)
        near = take(3)
    else:
        scale, incoming, other, gain = take(4)
        far = take(8)
        out, grad_top, grad_gain = take(3)
        grad_low, grad_up, grad_attn, grad_joined = take(4)
        near = take(8)
        total, grad_middle, grad_mixed = take(3)
    (sems,) = refs
    if begin:
        slope, w_up, w_down = near
        load_slope = pltpu.make_async_copy(far[0], slope, sems.at[0])
        load_up = pltpu.make_async_copy(far[1].at[0], w_up, sems.at[1])
        load_down = pltpu.make_async_copy(far[2].at[0], w_down, sems.at[2])
    else:
        slope, w_up, w_down, x, middle, joined, w_qkv, w_out = near
        load_slope = pltpu.make_async_copy(far[0], slope, sems.at[0])
        load_up = pltpu.make_async_copy(far[1].at[0], w_up, sems.at[1])
        load_down = pltpu.make_async_copy(far[2].at[0], w_down, sems.at[2])
        load_x = pltpu.make_async_copy(far[3], x, sems.at[3])
        load_middle = pltpu.make_async_copy(far[4], middle, sems.at[4])
        load_joined = pltpu.make_async_copy(far[5], joined, sems.at[5])
        load_qkv = pltpu.make_async_copy(far[6].at[0], w_qkv, sems.at[6])
        load_out = pltpu.make_async_copy(far[7].at[0], w_out, sems.at[7])
    width = incoming.shape[1]
    length = incoming.shape[0] // seqs
    load_down.start()
    load_slope.start()
    if begin:
        entry_turned[...] = entry[...].T

    for seq in range(seqs):
        rows = pl.ds(seq * length, length)
        if begin:
            first = (lax.axis_index("section") == 0).astype(f32)
            value = incoming[rows, :].astype(f32) * first + other[rows, :] * (1.0 - first)
        else:
            normed, factor = row_stats(other[rows, :].astype(f32))
            gradient = incoming[rows, :].astype(f32)
            part = jnp.sum(gradient * normed, 0, keepdims=True)
            grad_gain[...] = part if seq == 0 else grad_gain[...] + part
            scaled = gradient * gain[...]
            value = factor * (
                scaled
                - jnp.mean(scaled, -1, keepdims=True)
                - normed * jnp.mean(scaled * normed, -1, keepdims=True)
            )
            grad_top[rows, :] = value
        grad_middle[rows, :] = value
        grad_low[rows, :] = value.astype(bf16)

    load_down.wait()
    load_slope.wait()
    load_up.start()
    if not begin:
        load_middle.start()
        load_out.start()
        load_joined.start()
    tile = 1024

    @pl.loop(0, w_up.shape[1] // tile)
    def _(index):
        cols = tile_of(index, tile)
        grad_hidden = nt(grad_low[...], w_down[cols, :])
        value = (grad_hidden * slope[:, cols].astype(f32)).astype(bf16)
        grad_up[:, cols] = value
        if begin:
            grad_bias[:, cols] = jnp.sum(value.astype(f32), 0, keepdims=True)
            down_weight[cols, :] = tn(hidden[:, cols], grad_low[...]).astype(bf16)
            pltpu.make_async_copy(
                down_weight.at[cols], down_out.at[cols], out_sem.at[0, index]
            ).start()
            up_weight[:, cols] = nn(entry_turned[...], value).astype(bf16)

    if begin:
        whole_up = pltpu.make_async_copy(up_weight, up_out, out_sem.at[1, 0])
        whole_up.start()
    load_up.wait()
    if not begin:
        load_middle.wait()
        load_out.wait()
        load_joined.wait()
        load_qkv.start()
        load_x.start()

    @pl.loop(0, width // 256)
    def _(index):
        total[:, tile_of(index, 256)] = nt(grad_up[...], w_up[tile_of(index, 256), :])

    if begin:
        for index in range(w_up.shape[1] // tile):
            cols = pl.ds(index * tile, tile)
            pltpu.make_async_copy(
                down_weight.at[cols], down_out.at[cols], out_sem.at[0, index]
            ).wait()
        whole_up.wait()
        return

    def store_middle(rows, value):
        grad_middle[rows, :] = value
        grad_attn[rows, :] = value.astype(bf16)

    for seq in range(seqs):
        norm_grads(middle, total, grad_middle, scale, None, 1, seq, store_middle)

    @pl.loop(0, width // 512)
    def _(index):
        part = tile_of(index, 512)
        grad_mixed[:, part] = nt(grad_attn[...], w_out[part, :]).astype(bf16)

    @pl.loop(0, width // 128)
    def _(pair):
        attention_grads(joined, grad_mixed, grad_joined, pair, seqs)

    load_qkv.wait()
    load_x.wait()

    @pl.loop(0, width // 256)
    def _(index):
        total[:, tile_of(index, 256)] = nt(grad_joined[...], w_qkv[tile_of(index, 256), :])

    def store_out(rows, value):
        out[rows, :] = value.astype(bf16)

    for seq in range(seqs):
        norm_grads(x, total, grad_middle, scale, None, 0, seq, store_out)


def backward_pass(grad_final, block_out, gain, scale, kept, weights):
    w_qkv, w_out, w_up, _, w_down = weights
    x, joined, _, middle, _, _, slope, _ = kept
    tokens, width = x.shape
    wide = w_up.shape[-1]
    vmem = pl.BlockSpec(memory_space=pltpu.VMEM)
    anywhere = pl.BlockSpec(memory_space=pl.ANY)
    exact = ((tokens, width), f32)
    low = ((tokens, width), bf16)
    lows = [low, ((tokens, wide), bf16), low, ((tokens, 3 * width), bf16)]
    near = [
        ((tokens, wide), bf16),
        ((width, wide), bf16),
        ((wide, width), bf16),
        exact,
        exact,
        ((tokens, 3 * width), bf16),
        ((width, 3 * width), bf16),
        ((width, width), bf16),
    ]
    flops = 4 * tokens * (4 * width * width + 2 * width * wide)
    return pl.pallas_call(
        partial(backward_kernel, False, scale.shape[0]),
        out_shape=[jax.ShapeDtypeStruct(*item) for item in [low, exact, ((1, width), f32)]],
        in_specs=[vmem] * 4 + [anywhere] * 8,
        out_specs=[vmem] * 3,
        scratch_shapes=[pltpu.VMEM(*item) for item in lows + near + [exact, exact, low]]
        + [pltpu.SemaphoreType.DMA((8,))],
        compiler_params=pltpu.CompilerParams(vmem_limit_bytes=60 * 2**20),
        cost_estimate=pl.CostEstimate(flops=flops, bytes_accessed=2**25, transcendentals=0),
    )(scale, grad_final, block_out, gain, slope, w_up, w_down, x, middle, joined, w_qkv, w_out)


def backward_begin(returned, grad_top, seqs, hidden, entry, slope, w_up, w_down):
    tokens, width = grad_top.shape
    wide = w_up.shape[-1]
    vmem = pl.BlockSpec(memory_space=pltpu.VMEM)
    anywhere = pl.BlockSpec(memory_space=pl.ANY)
    exact = ((tokens, width), f32)
    low = ((tokens, width), bf16)
    wide_low = ((tokens, wide), bf16)
    up, down = ((width, wide), bf16), ((wide, width), bf16)
    results = [exact, exact, ((1, wide), f32), down, up]
    inside = [low, wide_low, ((width, tokens), bf16), down, up]
    return pl.pallas_call(
        partial(backward_kernel, True, seqs),
        out_shape=[jax.ShapeDtypeStruct(*item) for item in results],
        in_specs=[vmem] * 4 + [anywhere] * 3,
        out_specs=[vmem] * 3 + [anywhere] * 2,
        scratch_shapes=[pltpu.VMEM(*item) for item in inside]
        + [pltpu.SemaphoreType.DMA((2, wide // 1024))]
        + [pltpu.VMEM(*item) for item in (wide_low, up, down)]
        + [pltpu.SemaphoreType.DMA((3,))],
        compiler_params=pltpu.CompilerParams(vmem_limit_bytes=60 * 2**20),
        cost_estimate=pl.CostEstimate(
            flops=16 * tokens * width * wide, bytes_accessed=2**25, transcendentals=0
        ),
    )(returned, grad_top, hidden, entry, slope, w_up, w_down)


def tail_kernel(line, seqs, lag, *refs):
    refs = list(refs)

    def take(number):
        return [refs.pop(0) for _ in range(number)]

    scale, bias_grad, rest, factor_one, factor_two, embedded, noisy, w_in = take(8)
    far = take(9)
    parts = take(2)
    (head_part,) = take(1)
    outs = take(5)
    head_out, smalls, rows_all = take(3)
    near = take(9)
    grad_attn, grad_mixed, grad_joined, grad_first, grad_cond, in_weight = take(6)
    rows_own, small_wide, small_own = take(3)
    own, from_core, slots = take(2), take(5), take(5)
    head_own, head_core, head_section, last_total = take(4)
    far_sem, load_sem, core_send, core_recv, ring_send, ring_recv, credit = take(7)
    keep_sem, packet_send, packet_recv, wide_send, wide_recv, rows_send, rows_recv = take(7)
    head_sem, head_send, head_recv, cross_send, cross_recv = take(5)
    grad_middle, grad_entry, middle, x, joined, mixed, entry_attn, w_out, w_qkv = near
    inside = [w_qkv, w_out, in_weight]
    groups = ((0, 1), (2, 3, 4))
    chips = 2 * line
    width = x.shape[1]
    me_section = lax.axis_index("section")
    me_line = lax.axis_index("line")
    me_pair = lax.axis_index("pair")
    me_core = lax.axis_index("core")
    position = me_line + me_pair * (chips - 1 - 2 * me_line)
    section_peer = {"section": 1 - me_section}
    core_peer = {"core": 1 - me_core}
    ways = (1, -1)
    ring_peers = []
    for way in ways:
        peer_line, peer_pair = ring_place(lax.rem(position + way + chips, chips), line)
        ring_peers.append({"line": peer_line, "pair": peer_pair})
    greet([core_peer, section_peer] + ring_peers)

    shapes = [ref.shape[-2:] for ref in from_core]

    def block_of(turn, step):
        ahead = lax.rem(position - ways[turn] * (1 + step) + 2 * chips, chips)
        return ring_place(ahead, line)

    def portion(index, turn):
        high, wide = shapes[index]
        if high % 32 == 0:
            return turn * (high // 2), high // 2, 0, wide
        return 0, high, turn * (wide // 2), wide // 2

    def half_of(index, turn):
        first, rows, col, cols = portion(index, turn)
        return pl.ds(first, rows), pl.ds(col, cols)

    def inside_rows(index, place, pair, core, first, rows):
        base = ((place * 2 + pair) * 2 + core) * shapes[index][0] + first
        return pl.ds(pl.multiple_of(base, 16), rows)

    def source(index, turn, step, core):
        place, pair = block_of(turn, step)
        rows, cols = half_of(index, turn)
        if index < 2:
            return parts[index].at[place, pair, core, rows, cols]
        first, high = portion(index, turn)[:2]
        return inside[index - 2].at[inside_rows(index, place, pair, core, first, high), cols]

    def load(index, turn, step):
        return pltpu.make_async_copy(
            source(index, turn, step, me_core),
            own[index].at[(step % 2, *half_of(index, turn))],
            load_sem.at[index, turn, step],
        )

    def core_copy(index, turn, step):
        return remote(
            source(index, turn, step, 1 - me_core),
            from_core[index].at[(step % 3, *half_of(index, turn))],
            core_send.at[index, turn, step],
            core_recv.at[index, turn, step],
            core_peer,
        )

    def ring_copy(index, turn, step):
        half = half_of(index, turn)
        passed = from_core[index].at[(0, *half)] if step == 0 else slots[index].at[(step - 1, *half)]
        return remote(
            passed,
            slots[index].at[(step, *half)],
            ring_send.at[index, turn, step],
            ring_recv.at[index, turn, step],
            ring_peers[turn],
        )

    def to_core(group, step):
        if step >= 3:
            pl.semaphore_wait(credit.at[group], 1)
        for index in groups[group]:
            for turn in range(2):
                if index < 2:
                    load(index, turn, step).start()
                core_copy(index, turn, step).start()

    def stop(group, step, between):
        first, last = step == 0, step == chips - 1
        for index in groups[group]:
            for turn in range(2):
                start, rows, left, wide = portion(index, turn)
                tile = min(wide, 512)
                if index < 2:
                    load(index, turn, step).wait()
                core_copy(index, turn, step).wait_recv()
                if not first:
                    ring_copy(index, turn, step - 1).wait_recv()
                place, pair = block_of(turn, step)

                @pl.loop(0, rows // 16)
                def _(block):
                    row = pl.ds(pl.multiple_of(start + block * 16, 16), 16)
                    if index >= 2:
                        own_row = inside_rows(index, place, pair, me_core, start + block * 16, 16)
                    for col in range(left, left + wide, tile):
                        cols = pl.ds(col, tile)
                        if index < 2:
                            mine = own[index][step % 2, row, cols]
                        else:
                            mine = inside[index - 2][own_row, cols]
                        total = from_core[index][step % 3, row, cols].astype(f32)
                        total = total + mine.astype(f32)
                        if not first:
                            total = total + slots[index][step - 1, row, cols].astype(f32)
                        if last and index == 4:
                            last_total[row, cols] = total
                        elif last:
                            outs[index][row, cols] = total.astype(bf16)
                        elif first:
                            from_core[index][0, row, cols] = total.astype(bf16)
                        else:
                            slots[index][step - 1, row, cols] = total.astype(bf16)

                if not last:
                    ring_copy(index, turn, step).start()
                between()
        if step == 1:
            for index in groups[group]:
                for turn in range(2):
                    ring_copy(index, turn, 0).wait_send()
        if 1 <= step <= 4:
            amount = 2 if step == 1 else 1
            pl.semaphore_signal(
                credit.at[group], inc=amount, device_id=core_peer, device_id_type=MESH
            )

    hops = (line, line - 1)

    def packet_blocks(place, pair):
        return [smalls.at[place, pair, me_core], rows_all.at[place, pair, me_core]]

    def packet_hops(turn, hop, away):
        place, pair = ring_place(
            lax.rem(position - ways[turn] * (hop + away) + 2 * chips, chips), line
        )
        return [
            remote(
                block,
                block,
                packet_send.at[n, turn, hop],
                packet_recv.at[n, turn, hop],
                ring_peers[turn],
            )
            for n, block in enumerate(packet_blocks(place, pair))
        ]

    def pass_packets(hop):
        for turn in range(2):
            if 0 < hop <= hops[turn]:
                for copy in packet_hops(turn, hop - 1, 1):
                    copy.wait_recv()
            if hop < hops[turn]:
                for copy in packet_hops(turn, hop, 0):
                    copy.start()

    small_slot, rows_slot = packet_blocks(me_line, me_pair)
    keep_small = pltpu.make_async_copy(small_own, small_slot, keep_sem.at[0])
    keep_rows = pltpu.make_async_copy(rows_own, rows_slot, keep_sem.at[1])
    rows_over = remote(rows_own, rows_slot, rows_send, rows_recv, section_peer)
    across = [
        remote(block, block, wide_send.at[n], wide_recv.at[n], core_peer)
        for n, block in enumerate([smalls.at[:, :, me_core], rows_all.at[:, :, me_core]])
    ]
    def packets_ready():
        keep_small.wait()

        @pl.when(me_section == 0)
        def _():
            keep_rows.wait()

        @pl.when(me_section == 1)
        def _():
            rows_over.wait_recv()

    high = head_part.shape[0] // 4

    def shard(n):
        return head_part.at[pl.ds(n * high, high)]

    head_loads = [
        pltpu.make_async_copy(shard(2 * n), head_own.at[n], head_sem.at[n]) for n in range(2)
    ]
    head_copies = [
        remote(shard(2 * n + 1), head_core.at[n], head_send.at[n], head_recv.at[n], core_peer)
        for n in range(2)
    ]
    head_copies.append(
        remote(head_core.at[1], head_section, head_send.at[2], head_recv.at[2], section_peer)
    )

    def head_over_cores():
        for copy in head_loads:
            copy.wait()
        for copy in head_copies[:2]:
            copy.wait_recv()

        @pl.loop(0, high // 16)
        def _(block):
            rows = pl.ds(pl.multiple_of(block * 16, 16), 16)
            value = head_core[1, rows, :].astype(f32) + head_own[1, rows, :].astype(f32)
            head_core[1, rows, :] = value.astype(bf16)

        head_copies[2].start()

    def head_over_sections():
        head_copies[2].wait_recv()

        @pl.loop(0, high // 16)
        def _(block):
            rows = pl.ds(pl.multiple_of(block * 16, 16), 16)
            value = head_core[0, rows, :].astype(f32) + head_own[0, rows, :].astype(f32)
            value = value + head_section[rows, :].astype(f32)
            head_out[rows, :] = value.astype(bf16)

    far_copies = []
    for n, (where, target) in enumerate(zip(far, near)):
        where = where.at[0] if n >= 7 else where
        far_copies.append(pltpu.make_async_copy(where, target, far_sem.at[n]))

    def waits(*numbers):
        for n in numbers:
            far_copies[n].wait()

    def store_middle(rows, value):
        grad_middle[rows, :] = value
        grad_attn[rows, :] = value.astype(bf16)

    def store_first(rows, value):
        grad_first[rows, :] = value.astype(bf16)

    def second_norm(seq):
        if seq == 0:
            waits(0, 1, 2)
        norm_grads(middle, grad_entry, grad_middle, scale, grad_cond, 1, seq, store_middle)

    def mixed_grads(index):
        if index == 0:
            waits(7)
        part = pl.ds(index * 512, 512)
        grad_mixed[:, part] = nt(grad_attn[...], w_out[part, :]).astype(bf16)

    def heads_grads(pair):
        if pair == 0:
            waits(4)
        attention_grads(joined, grad_mixed, grad_joined, pair, seqs)

    def entry_grads(index):
        if index == 0:
            waits(8)
        part = pl.ds(index * 256, 256)
        grad_entry[:, part] = nt(grad_joined[...], w_qkv[part, :])

    def first_norm(seq):
        if seq == 0:
            waits(3)
        norm_grads(x, grad_entry, grad_middle, scale, grad_cond, 0, seq, store_first)

    def embedding_rows(_):
        grad_noisy = nt(grad_first[...], w_in[...])
        inner = jnp.mean(grad_noisy * embedded[...], -1, keepdims=True)
        value = factor_one[...] * grad_noisy - factor_two[...] * embedded[...] * inner
        rows_own[...] = value.astype(bf16)

        @pl.when(me_section == 0)
        def _():
            keep_rows.start()
            rows_over.start()

    def small_rows(_):
        each = small_wide.shape[1]
        for seq in range(seqs):
            for n in range(2 * width // each):
                row = pl.ds(seq * (2 * width // each) + n, 1)
                small_wide[row, :] = grad_cond[seq, :, pl.ds(n * each, each)]
        first = seqs * 2 * width // each
        for n in range(bias_grad.shape[1] // each):
            small_wide[pl.ds(first + n, 1), :] = bias_grad[:, pl.ds(n * each, each)]
        first += bias_grad.shape[1] // each
        small_wide[pl.ds(first, rest.shape[0]), :] = rest[...]
        small_own[...] = small_wide[...].astype(bf16)
        keep_small.start()

    def input_weight(_):
        in_weight[...] = tn(noisy[...], grad_first[...]).astype(bf16)

    def qkv_weight(index):
        if index == 0:
            waits(6)
        part = pl.ds(index * 256, 256)
        w_qkv[part, :] = tn(entry_attn[:, part], grad_joined[...]).astype(bf16)

    def out_weight(index):
        if index == 0:
            waits(5)
        part = pl.ds(index * 512, 512)
        w_out[part, :] = tn(mixed[:, part], grad_attn[...]).astype(bf16)

    steps = []
    for step, number in (
        (second_norm, seqs),
        (mixed_grads, width // 512),
        (heads_grads, width // 128),
        (entry_grads, width // 256),
        (first_norm, seqs),
        (embedding_rows, 1),
        (small_rows, 1),
        (input_weight, 1),
        (qkv_weight, width // 256),
        (out_weight, width // 512),
    ):
        steps += [partial(step, n) for n in range(number)]
    at_once = -(-len(steps) // (4 * lag))

    def work():
        for _ in range(at_once):
            if steps:
                steps.pop(0)()

    def nothing():
        pass

    to_core(0, 0)
    for copy in far_copies[:3]:
        copy.start()
    to_core(0, 1)
    for n in (7, 4, 8, 3, 6, 5):
        far_copies[n].start()
    stop(0, 0, work)
    for turn in range(1, chips + lag):
        if turn + 1 < chips:
            to_core(0, turn + 1)
        if turn == 1:
            for copy in head_loads + head_copies[:2]:
                copy.start()
        if turn == lag:
            to_core(1, 0)
        if lag <= turn and turn - lag + 1 < chips:
            to_core(1, turn - lag + 1)
        if turn < chips:
            stop(0, turn, work if turn < lag else nothing)
        if turn >= lag:
            stop(1, turn - lag, nothing)
        hop = turn - lag - 2
        if hop == 0:
            packets_ready()
        if 0 <= hop <= line:
            pass_packets(hop)
        if hop == line:
            for copy in across:
                copy.start()
        if turn == 3:
            head_over_cores()
        if turn == chips + lag - 2:
            head_over_sections()
    each = outs[4].shape[0]
    give = remote(last_total.at[pl.ds(each, each)], outs[4], cross_send, cross_recv, section_peer)

    @pl.when(me_section == 0)
    def _():
        give.start()
        outs[4][...] = last_total[pl.ds(0, each), :]

    for copy in across:
        copy.wait()
    for copy in head_copies:
        copy.wait_send()
    for turn in range(2):
        for hop in range(hops[turn]):
            for copy in packet_hops(turn, hop, 0):
                copy.wait_send()
    for index in range(5):
        for turn in range(2):
            for step in range(chips):
                core_copy(index, turn, step).wait_send()
                if 0 < step < chips - 1:
                    ring_copy(index, turn, step).wait_send()

    @pl.when(me_section == 0)
    def _():
        rows_over.wait_send()
        give.wait_send()

    @pl.when(me_section == 1)
    def _():
        give.wait_recv()


def tail_pass(
    scale, bias_grad, rest, factors, embedded, noisy, w_in, far, parts, head_part, collective_id
):
    grad_middle = far[0]
    tokens, width = grad_middle.shape
    seqs = scale.shape[0]
    line = parts[0].shape[0]
    chips = 2 * line
    count = 4 * line
    emb_width = noisy.shape[1]
    vmem = pl.BlockSpec(memory_space=pltpu.VMEM)
    anywhere = pl.BlockSpec(memory_space=pl.ANY)
    dma = pltpu.SemaphoreType.DMA
    shapes = [part.shape[-2:] for part in parts]
    shapes += [
        (width // count, 3 * width),
        (width // count, width),
        (emb_width // count, width),
    ]
    each = shapes[4][0] // 2
    high = head_part.shape[0] // 4
    small = ((seqs * 2 * width + bias_grad.shape[1]) // emb_width + rest.shape[0], emb_width)
    exact = ((tokens, width), f32)
    low = ((tokens, width), bf16)
    three = ((tokens, 3 * width), bf16)
    rows = (tokens, emb_width)
    results = [(shape, bf16) for shape in shapes[:4]]
    results += [((each, width), f32), ((high, width), bf16)]
    results += [((line, 2, 2) + small, bf16), ((line, 2, 2) + rows, bf16)]
    room = [exact, exact, exact, exact, three, low, low]
    room += [((width, width), bf16), ((width, 3 * width), bf16)]
    room += [low, low, three, low, ((seqs, 1, 2 * width), f32), ((emb_width, width), bf16)]
    room += [(rows, bf16), (small, f32), (small, bf16)]
    room += [((2,) + shape, bf16) for shape in shapes[:2]]
    room += [((3,) + shape, bf16) for shape in shapes]
    room += [((chips - 1,) + shape, bf16) for shape in shapes]
    room += [((2, high, width), bf16), ((2, high, width), bf16), ((high, width), bf16)]
    room += [(shapes[4], f32)]
    scratch = [pltpu.VMEM(*item) for item in room]
    scratch += [dma((9,)), dma((2, 2, chips)), dma((5, 2, chips)), dma((5, 2, chips))]
    scratch += [dma((5, 2, chips - 1)), dma((5, 2, chips - 1)), pltpu.SemaphoreType.REGULAR((2,))]
    scratch += [dma((2,)), dma((2, 2, line)), dma((2, 2, line)), dma((2,)), dma((2,)), dma, dma]
    scratch += [dma((2,)), dma((3,)), dma((3,)), dma, dma]
    return pl.pallas_call(
        partial(tail_kernel, line, seqs, line),
        out_shape=[jax.ShapeDtypeStruct(*item) for item in results],
        in_specs=[vmem] * 8 + [anywhere] * 12,
        out_specs=[vmem] * 6 + [anywhere] * 2,
        scratch_shapes=scratch,
        compiler_params=pltpu.CompilerParams(
            collective_id=collective_id, has_side_effects=True, vmem_limit_bytes=62 * 2**20
        ),
        cost_estimate=pl.CostEstimate(flops=0, bytes_accessed=2**29, transcendentals=0),
    )(scale, bias_grad, rest, *factors, embedded, noisy, w_in, *far, *parts, head_part)


def finish_kernel(line, head_rows, *refs):
    ids, rows, *lows = refs[:7]
    *exacts, grad_embed, total = refs[7:]
    me_section = lax.axis_index("section")
    me_line = lax.axis_index("line")
    me_pair = lax.axis_index("pair")
    me_core = lax.axis_index("core")
    high = total.shape[0]
    base = (((me_section * line + me_line) * 2 + me_pair) * 2 + me_core) * grad_embed.shape[0]
    tile = 768
    for index in range(rows.shape[0] // tile):
        part = pl.ds(index * tile, tile)
        entry = lax.broadcasted_iota(jnp.int32, (high, tile), 0) + base
        place = jnp.where(entry == ids[:, part], 1.0, 0.0).astype(bf16)
        product = nn(place, rows[part, :])
        total[...] = product if index == 0 else total[...] + product
    grad_embed[...] = total[pl.ds(0, grad_embed.shape[0]), :]
    for low, exact in zip(lows, exacts):
        whole = exact.shape[0] // 16
        left = exact.shape[0] % 16

        @pl.loop(0, whole)
        def _(block):
            part = pl.ds(pl.multiple_of(block * 16, 16), 16)
            exact[part, :] = low[part, :].astype(f32)

        if left:
            value = low[pl.ds(whole * 16, 16), :].astype(f32)
            exact[pl.ds(whole * 16, left), :] = value[:left]


def finish(ids, rows, lows, line, head_rows, out_rows):
    vmem = pl.BlockSpec(memory_space=pltpu.VMEM)
    shapes = [low.shape for low in lows[:-1]] + [(head_rows, lows[-1].shape[1])]
    shapes.append((out_rows, rows.shape[1]))
    return pl.pallas_call(
        partial(finish_kernel, line, head_rows),
        out_shape=[jax.ShapeDtypeStruct(shape, f32) for shape in shapes],
        in_specs=[vmem] * 7,
        out_specs=[vmem] * 6,
        scratch_shapes=[pltpu.VMEM((-(-out_rows // 16) * 16, rows.shape[1]), f32)],
        compiler_params=pltpu.CompilerParams(vmem_limit_bytes=60 * 2**20),
        cost_estimate=pl.CostEstimate(
            flops=2 * out_rows * rows.size, bytes_accessed=2**24, transcendentals=0
        ),
    )(ids, rows, *lows)


def norm_rows(values):
    centred = values - jnp.mean(values, -1, keepdims=True)
    factor = lax.rsqrt(jnp.mean(centred * centred, -1, keepdims=True) + epsilon)
    return (centred * factor, factor)


def norm_back(gradient, normed, factor):
    return factor * (
        gradient
        - jnp.mean(gradient, -1, keepdims=True)
        - normed * jnp.mean(gradient * normed, -1, keepdims=True)
    )


def time_features(noise_level):
    half_width = TFEAT // 2
    rates = jnp.exp(jnp.arange(half_width, dtype=f32) * (math.log(1000.0) / half_width))
    angles = (jnp.log(noise_level) / 4.0)[:, None] * rates[None, :]
    return jnp.concatenate([jnp.cos(angles), jnp.sin(angles)], -1)


def levels_of(bins, table):
    hits = bins[:, None] == jnp.arange(table.shape[0])[None, :]
    return jnp.sum(jnp.where(hits, table[None, :], 0.0), -1)


def over_dp(part):
    part = part.reshape((part.shape[0] // 4, 2, 2) + part.shape[1:])
    part = lax.psum_scatter(part, "core", scatter_dimension=2)
    part = lax.psum_scatter(part, "pair", scatter_dimension=1)
    return lax.psum_scatter(part, "line", scatter_dimension=0)


def by_owner(part):
    line = lax.axis_size("line")
    return part.astype(bf16).reshape((line, 2, 2, part.shape[0] // (line * 4)) + part.shape[1:])


def mm(spec, left, right):
    return jnp.einsum(spec, left, right, preferred_element_type=f32)


def layer_forward(stream, scale_attn, scale_mlp, weights):
    w_qkv, w_out, w_up, b_hidden, w_down = weights
    seq_count, length, model_width = stream.shape
    normed_attn, factor_attn = norm_rows(stream)
    attn_entry = (normed_attn * scale_attn).astype(bf16)
    joined = mm("nsd,de->nse", attn_entry, w_qkv).astype(bf16)
    qkv_parts = joined.reshape(seq_count, length, 3, HEADS, HEAD_DIM)
    query_rows = qkv_parts[:, :, 0]
    key_rows = qkv_parts[:, :, 1]
    value_rows = qkv_parts[:, :, 2]
    scores = mm("nqhe,nkhe->nhqk", query_rows, key_rows) / math.sqrt(HEAD_DIM)
    exp_scores = jnp.exp(scores - jnp.max(scores, -1, keepdims=True))
    attn_probs = exp_scores / jnp.sum(exp_scores, -1, keepdims=True)
    probs_low = attn_probs.astype(bf16)
    attn_mixed = mm("nhqk,nkhe->nqhe", probs_low, value_rows).astype(bf16)
    attn_mixed = attn_mixed.reshape(seq_count, length, model_width)
    middle = stream + mm("nsd,de->nse", attn_mixed, w_out)
    normed_mlp, factor_mlp = norm_rows(middle)
    mlp_entry = (normed_mlp * scale_mlp).astype(bf16)
    up_proj = mm("nsd,df->nsf", mlp_entry, w_up) + b_hidden
    below = 0.5 + 0.5 * lax.erf(up_proj * math.sqrt(0.5))
    hidden = (up_proj * below).astype(bf16)
    density = jnp.exp(-0.5 * up_proj * up_proj) * (1.0 / math.sqrt(2.0 * math.pi))
    slope = (below + up_proj * density).astype(bf16)
    block_out = middle + mm("nsf,fd->nsd", hidden, w_down)
    kept = (
        normed_attn,
        factor_attn,
        attn_entry,
        query_rows,
        key_rows,
        value_rows,
        attn_probs,
        probs_low,
        attn_mixed,
        normed_mlp,
        factor_mlp,
        mlp_entry,
        slope,
        hidden,
    )
    return (block_out, kept)


def layer_backward(grad_out, kept, scale_attn, scale_mlp, weights, whole):
    w_qkv, w_out, w_up, b_hidden, w_down = weights
    (
        normed_attn,
        factor_attn,
        attn_entry,
        query_rows,
        key_rows,
        value_rows,
        attn_probs,
        probs_low,
        attn_mixed,
        normed_mlp,
        factor_mlp,
        mlp_entry,
        slope,
        hidden,
    ) = kept
    seq_count, length, model_width = grad_out.shape
    grads = {}
    grad_branch = grad_out.astype(bf16)
    if whole:
        grads["down"] = by_owner(mm("nsf,nsd->fd", hidden, grad_branch))
    grad_hidden = mm("nsd,fd->nsf", grad_branch, w_down)
    grad_up_proj = (grad_hidden * slope.astype(f32)).astype(bf16)
    if whole:
        grads["bias"] = jnp.sum(grad_up_proj.astype(f32), (0, 1))
        grads["up"] = by_owner(mm("nsd,nsf->df", mlp_entry, grad_up_proj))
    grad_entry = mm("nsf,df->nsd", grad_up_proj, w_up)
    grad_middle = grad_out + norm_back(grad_entry * scale_mlp, normed_mlp, factor_mlp)
    grad_attn = grad_middle.astype(bf16)
    if whole:
        grads["out"] = by_owner(mm("nsd,nse->de", attn_mixed, grad_attn))
    grad_mixed = mm("nse,de->nsd", grad_attn, w_out)
    grad_mixed = grad_mixed.astype(bf16).reshape(seq_count, length, HEADS, HEAD_DIM)
    grad_probs = mm("nqhe,nkhe->nhqk", grad_mixed, value_rows)
    grad_values = mm("nhqk,nqhe->nkhe", probs_low, grad_mixed)
    grad_scores = (
        attn_probs * (grad_probs - jnp.sum(grad_probs * attn_probs, -1, keepdims=True))
    ).astype(bf16)
    grad_query = mm("nhqk,nkhe->nqhe", grad_scores, key_rows) / math.sqrt(HEAD_DIM)
    grad_keys = mm("nhqk,nqhe->nkhe", grad_scores, query_rows) / math.sqrt(HEAD_DIM)
    grad_joined = jnp.stack([grad_query, grad_keys, grad_values], 2).astype(bf16)
    grad_joined = grad_joined.reshape(seq_count, length, 3 * model_width)
    if whole:
        grads["qkv"] = by_owner(mm("nsd,nse->de", attn_entry, grad_joined))
    grad_attn_entry = mm("nse,de->nsd", grad_joined, w_qkv)
    grad_stream = grad_middle + norm_back(grad_attn_entry * scale_attn, normed_attn, factor_attn)
    if whole:
        grads["cond"] = jnp.concatenate(
            [jnp.sum(grad_attn_entry * normed_attn, 1), jnp.sum(grad_entry * normed_mlp, 1)], -1
        )
    return (grad_stream, grads)


def local(
    token_ids,
    target_ids,
    time_bins,
    sigma_table,
    noise,
    embed,
    w_in,
    w_time,
    norm_gain,
    w_qkv,
    w_out,
    w_up,
    b_hidden,
    w_down,
    out_gain,
    head,
):
    section = lax.axis_index("section")
    line_at = lax.axis_index("line")
    pair_at = lax.axis_index("pair")
    core = lax.axis_index("core")
    sections = lax.axis_size("section")
    line = lax.axis_size("line")
    chip = line_at * 2 + pair_at
    chips = line * 2
    cores = 2
    dp_count = chips * cores
    dp_index = chip * cores + core
    is_first = section == 0
    seqs, length = token_ids.shape
    tokens = seqs * length
    half = tokens // sections
    model_width = w_out.shape[-1]
    emb_rows, emb_width = embed.shape
    head_rows = head.shape[0]
    straight = line <= 4 and half % 16 == 0 and model_width // dp_count % 16 == 0

    if straight:
        lanes = -(-half // 128) * 128
        blocks = [part.reshape(2, half) for part in (token_ids, target_ids)]
        blocks.append(jnp.pad(time_bins[None, :], ((0, 0), (0, half - seqs))))
        own_ids = jnp.pad(jnp.concatenate(blocks, 0), ((0, 3), (0, lanes - half)))
        head_own = jnp.pad(head, ((0, -head_rows % 512), (0, 0)))
        all_ids, embedded, head_early, head_core = start_pass(
            own_ids, embed, head_own, half, line, 0
        )
        all_ids = all_ids.reshape(dp_count, 8, lanes)
        all_tokens = all_ids[:, 0:2, :half].reshape(dp_count, tokens)
        all_targets = all_ids[:, 2:4, :half].reshape(dp_count, tokens)
        all_bins = all_ids[:, 4, :seqs].reshape(-1)
        embedded = embedded.swapaxes(1, 2)
    else:
        own_ids = jnp.concatenate([token_ids.reshape(-1), target_ids.reshape(-1), time_bins])
        all_ids = lax.all_gather(own_ids, DP)
        all_tokens = all_ids[:, :tokens]
        all_targets = all_ids[:, tokens : 2 * tokens]
        all_bins = all_ids[:, 2 * tokens :].reshape(-1)
        own_rows = dp_index * emb_rows + jnp.arange(emb_rows)
        half_tokens = lax.dynamic_slice_in_dim(all_tokens, section * half, half, 1)
        picked = (half_tokens.reshape(-1)[:, None] == own_rows[None, :]).astype(bf16)
        found = jnp.dot(picked, embed, preferred_element_type=f32).astype(bf16)
        embedded = lax.all_gather(over_dp(found.reshape(dp_count, half, emb_width)), "section")
    embedded = embedded.astype(f32).reshape(seqs, length, emb_width)

    swapped = [(0, 1), (1, 0)]
    if not straight:
        head_group = lax.all_gather(lax.all_gather(head, "core"), "section")
        head_group = head_group.reshape(-1, model_width)
        vocab_base = (
            (jnp.arange(sections)[:, None] * chips + chip) * cores + jnp.arange(cores)[None, :]
        ) * head_rows
        columns = (vocab_base[:, :, None] + jnp.arange(head_rows)[None, None, :]).reshape(-1)

    noise_level = levels_of(time_bins, sigma_table)
    unit_factor = lax.rsqrt(jnp.mean(embedded * embedded, -1, keepdims=True) + epsilon)
    level_col = noise_level[:, None, None]
    noise_scale = lax.rsqrt(level_col * level_col + 1.0)
    noisy_rows = ((embedded * unit_factor + level_col * noise) * noise_scale).astype(bf16)
    time_feats = time_features(noise_level)
    conditioned = jnp.dot(time_feats, w_time[0].astype(f32), precision=highest) + norm_gain[0]
    scale_attn = conditioned[:, None, :model_width]
    scale_mlp = conditioned[:, None, model_width:]
    scale = conditioned[:, None, :]
    weights = (w_qkv[0], w_out[0], w_up[0], b_hidden[0], w_down[0])
    stacked = (w_qkv, w_out, w_up, b_hidden, w_down)
    stream0 = mm("nse,ed->nsd", noisy_rows, w_in)
    flat = (tokens, model_width)
    if straight:
        block_out, final_rows, *kept, head_late, head_fourth = forward_pass(
            stream0.reshape(flat), scale, stacked, out_gain[None, :], head_own, head_early, 1
        )
        heads = [head_own, head_core, head_early, head_late, head_fourth]
    else:
        first_out = layer_forward(stream0, scale_attn, scale_mlp, weights)[0].astype(bf16)
        arrived = lax.ppermute(first_out, "section", swapped)
        stream = jnp.where(is_first, stream0, arrived.astype(f32))
        block_out, kept = layer_forward(stream, scale_attn, scale_mlp, weights)
        final_normed, final_factor = norm_rows(block_out.astype(bf16).astype(f32))
        final_rows = (final_normed * out_gain).astype(bf16).reshape(flat)

    targets_group = lax.dynamic_slice_in_dim(
        all_targets.reshape(chips, cores, tokens), core, 1, 1
    )[:, 0]
    targets_group = lax.dynamic_slice_in_dim(targets_group, section * half, half, 1)
    if straight:
        grad_final, grad_head, lse, picks = head_pass(
            final_rows, targets_group.reshape(line, 1, tokens), heads, line, head_rows, length, 3
        )
    else:
        targets_group = targets_group.reshape(-1)
        handed = lax.ppermute(final_rows[:half], "section", [(1, 0), (0, 1)])
        own_final = jnp.where(is_first, handed, final_rows[half:])
        group_final = lax.all_gather(own_final, ("line", "pair"), tiled=True)
        logits = mm("td,vd->tv", group_final, head_group)
        local_top = jnp.max(logits, -1)
        local_total = jnp.sum(jnp.exp(logits - local_top[:, None]), -1)
        mark = columns[None, :] == targets_group[:, None]
        local_pick = jnp.sum(jnp.where(mark, logits, 0.0))
        stats = lax.all_gather(jnp.stack([local_top, local_total]), ("line", "pair"))
        all_top = jnp.max(stats[:, 0], 0)
        all_total = jnp.sum(stats[:, 1] * jnp.exp(stats[:, 0] - all_top), 0)
        log_total = all_top + jnp.log(all_total)
        soft_rows = jnp.exp(logits - log_total[:, None])
        logit_grads = ((soft_rows - jnp.where(mark, 1.0, 0.0)) / length).astype(bf16)
        grad_final = jnp.dot(logit_grads, head_group, preferred_element_type=f32).astype(bf16)
        grad_final = lax.psum_scatter(grad_final, ("line", "pair"), scatter_dimension=0, tiled=True)
        handed = lax.ppermute(grad_final, "section", swapped)
        grad_final = jnp.concatenate([handed, grad_final], 0)
        grad_head = mm("tv,td->vd", logit_grads, group_final).astype(bf16)
        grad_head = grad_head.reshape(sections, cores, head_rows, model_width)
        grad_head = lax.psum_scatter(grad_head, "core", scatter_dimension=1)
        grad_head = lax.psum_scatter(grad_head, "section", scatter_dimension=0).astype(f32)

        ce_part = jnp.sum(log_total) / chips - local_pick
    if straight:
        grad_second, grad_top, out_part = backward_pass(
            grad_final, block_out, out_gain[None, :], scale, kept, stacked
        )
        returned = lax.ppermute(grad_second, "section", swapped)
        lse, picks, out_part = lax.optimization_barrier((lse, picks, out_part))
        ce_part = jnp.sum(lse) / chips - jnp.sum(picks)
        out_part = out_part.reshape(-1)
        x, joined, mixed, middle, entry_attn, entry_mlp, slope, hidden = kept
        grad_middle, grad_entry, grad_bias, down_part, up_part = backward_begin(
            returned, grad_top, seqs, hidden, entry_mlp, slope, w_up, w_down
        )
        parts = [by_owner(down_part), by_owner(up_part)]
    else:
        grad_final = grad_final.astype(f32).reshape(stream0.shape)
        out_part = jnp.sum(grad_final * final_normed, (0, 1))
        grad_top = norm_back(grad_final * out_gain, final_normed, final_factor)
        grad_second = layer_backward(grad_top, kept, scale_attn, scale_mlp, weights, False)[0]
        returned = lax.ppermute(grad_second.astype(bf16), "section", swapped)
        grad_cot = jnp.where(is_first, returned.astype(f32), grad_top)
        grad_stream, grads = layer_backward(grad_cot, kept, scale_attn, scale_mlp, weights, True)
        grad_first = grad_stream.astype(bf16)
    out_part = jnp.where(is_first, 0.0, out_part)

    ce_high = ce_part.astype(bf16).astype(f32)
    ce_mid = (ce_part - ce_high).astype(bf16).astype(f32)
    ce_low = ce_part - ce_high - ce_mid
    shared = jnp.concatenate([out_part, jnp.stack([ce_high, ce_mid, ce_low])])
    shared_rows = -(-shared.shape[0] // emb_width)
    shared = jnp.pad(shared, (0, shared_rows * emb_width - shared.shape[0]))
    shared = shared.reshape(-1, emb_width).astype(bf16)
    both = [shared, lax.ppermute(shared, "section", swapped)]

    cubed = unit_factor * unit_factor * unit_factor
    cond_rows = seqs * 2 * model_width // emb_width
    bias_rows = b_hidden.shape[1] // emb_width
    if straight:
        rest = jnp.concatenate(both, 0).astype(f32)
        rest = jnp.pad(rest, ((0, -(cond_rows + bias_rows + rest.shape[0]) % 16), (0, 0)))
        factors = [
            (value * noise_scale).reshape(tokens, 1) for value in (unit_factor, cubed)
        ]
        owned = noisy_rows.reshape(tokens, sections, dp_count, -1)
        owned = owned.swapaxes(1, 2).reshape(tokens, emb_width)
        far = [grad_middle, grad_entry, middle, x, joined, mixed, entry_attn, w_out, w_qkv]
        grad_down, grad_up, grad_qkv, grad_wout, grad_w_in, grad_head, smalls, rows_all = tail_pass(
            scale,
            grad_bias,
            rest,
            factors,
            embedded.reshape(tokens, emb_width),
            owned,
            w_in,
            far,
            parts,
            grad_head,
            2,
        )
        ids = all_tokens.reshape(1, -1)
        grad_down, grad_up, grad_qkv, grad_wout, grad_head, grad_embed = finish(
            ids,
            rows_all.reshape(-1, emb_width),
            [grad_down, grad_up, grad_qkv, grad_wout, grad_head],
            line,
            head_rows,
            emb_rows // sections,
        )
    else:
        in_part = mm("nse,nsd->ed", noisy_rows, grad_first).astype(bf16)
        in_part = in_part.reshape(sections, dp_count, -1, model_width).swapaxes(0, 1)
        in_sum = over_dp(in_part).astype(f32)
        in_handed = lax.ppermute(in_sum[1], "section", swapped)
        grad_w_in = jnp.where(is_first, in_sum[0], in_handed)
        grad_noisy = mm("nsd,ed->nse", grad_first, w_in)
        grad_unit = grad_noisy * noise_scale
        grad_embedded = unit_factor * grad_unit - cubed * embedded * jnp.mean(
            grad_unit * embedded, -1, keepdims=True
        )
        grad_flat = grad_embedded.reshape(tokens, emb_width).astype(bf16)
        handed = lax.ppermute(grad_flat, "section", swapped)
        rows_all = lax.all_gather(jnp.where(is_first, grad_flat, handed), DP)
        small = [grads["cond"].reshape(-1, emb_width), grads["bias"].reshape(-1, emb_width)]
        smalls = lax.all_gather(
            jnp.concatenate([value.astype(bf16) for value in small] + both, 0), DP
        )
        grad_down, grad_up, grad_qkv, grad_wout = [
            over_dp(part.reshape((dp_count,) + part.shape[3:])).astype(f32)
            for part in (grads["down"], grads["up"], grads["qkv"], grads["out"])
        ]
        grad_all = rows_all.reshape(-1, emb_width)
        out_rows = emb_rows // sections
        target_rows = (section * dp_count + dp_index) * out_rows + jnp.arange(out_rows)
        place = (target_rows[:, None] == all_tokens.reshape(-1)[None, :]).astype(bf16)
        grad_embed = jnp.dot(place, grad_all, preferred_element_type=f32)

    smalls = smalls.reshape(dp_count, -1, emb_width).astype(f32)
    cond_all = smalls[:, :cond_rows].reshape(dp_count * seqs, 2 * model_width)
    bias_all = smalls[:, cond_rows : cond_rows + bias_rows].reshape(dp_count, -1)
    hidden_rows = bias_all.shape[1] // dp_count
    grad_bias = jnp.sum(
        lax.dynamic_slice_in_dim(bias_all, dp_index * hidden_rows, hidden_rows, 1), 0
    )
    norm_cols = 2 * model_width // dp_count
    grad_gain = jnp.sum(lax.dynamic_slice_in_dim(cond_all, dp_index * norm_cols, norm_cols, 1), 0)
    feats_all = time_features(levels_of(all_bins, sigma_table))
    feat_rows = TFEAT // dp_count
    feats_own = lax.dynamic_slice_in_dim(feats_all, dp_index * feat_rows, feat_rows, 1)
    grad_time = jnp.dot(feats_own.T, cond_all, precision=highest)
    shared_first = cond_rows + bias_rows
    both = smalls[:, shared_first : shared_first + 2 * shared_rows]
    both = jnp.sum(both.reshape(dp_count, 2, -1), (0, 1))
    loss = jnp.sum(both[model_width : model_width + 3]) / (tokens * dp_count)
    gain_rows = model_width // dp_count
    grad_out_gain = lax.dynamic_slice_in_dim(both, dp_index * gain_rows, gain_rows)
    return (
        loss,
        grad_embed,
        grad_w_in,
        grad_time[None],
        grad_gain[None],
        grad_qkv[None],
        grad_wout[None],
        grad_up[None],
        grad_bias[None],
        grad_down[None],
        grad_out_gain,
        grad_head,
    )


def solution(mesh):
    sections, dp_count = mesh.shape["section"], mesh.shape["dp"]
    fine = Mesh(mesh.devices.reshape(sections, dp_count // 4, 2, 2), ("section",) + DP)
    everywhere = ("section",) + DP
    in_specs = (
        P(DP, None),
        P(DP, None),
        P(DP),
        P(),
        P(DP, None, None),
        P(DP, None),
        P(),
        P("section", None, None),
        P("section", None),
        P("section", None, None),
        P("section", None, None),
        P("section", None, None),
        P("section", None),
        P("section", None, None),
        P(),
        P(everywhere, None),
    )
    out_specs = (
        P(),
        P(everywhere, None),
        P(everywhere, None),
        P("section", DP, None),
        P("section", DP),
        P("section", DP, None),
        P("section", DP, None),
        P("section", DP, None),
        P("section", DP),
        P("section", DP, None),
        P(DP),
        P(everywhere, None),
    )
    return jax.shard_map(local, mesh=fine, in_specs=in_specs, out_specs=out_specs, check_vma=False)
```
